32 devices in a mesh: slab: 8 (over z, x), mp: 4 (over y, core).
Axes of the slice: x: 2, y: 2, z: 4, core: 2. Of those that a mesh axis runs over, the one named last changes fastest.
Arguments:
- feats: float32 [56, 28, 7, 384], P('slab', 'mp'), may hold values from -6 to 6
- labels: int32 [56, 28, 7], P('slab', 'mp'), may hold values from 0 to 13
- valid: int32 [56, 28, 7], P('slab', 'mp'), may hold values from 0 to 1, as said below
- params: float32 [872558], replicated
- moment_one: float32 [872558], replicated, may hold values from -1.5258789e-05 to 1.5258789e-05
- moment_two: float32 [872558], replicated, may hold values from 1.1460556e-13 to 4.5842225e-13
Outputs:
- loss_sum: float32 [], replicated
- valid_count: float32 [], replicated
- grad_norm: float32 [], replicated
- new_params: float32 [872558], replicated
- new_first: float32 [872558], replicated
- new_second: float32 [872558], replicated
The draws below stay inside these ranges and needn't reach their ends.
Inputs may be any that keep to these rules, and one draw needn't show every extreme that they name: valid is 0 or 1; the share of ones rises with depth.
All inputs are finite; a program needn't handle non-finite values.
Results may differ from the reference program's by a relative error of at most 0.0003.
Values sent between devices are 32-bit elements; how exact they have to be, the bound alone decides.
No kernel may reach another device: no remote copies, remote signals or barrier semaphores. Data moves between devices by JAX's collectives and lax.ppermute only.
A program may use at most 192 MiB of HBM per device.

```python
import math
from functools import partial
import jax
import jax.numpy as jnp
from jax import lax

EMB = 96
HEADS = 6
HDIM = 16
HID = 384
MERGE = 384
CLASSES = 14
WIN = 7
SHIFT = 3
LAYERS = 3
STEP = 10
DEPTH = 56
HH = 28
WW = 7
NPARAM = 872558


def layout_drawn():
    table = [('merge_gain', (MERGE,), 0, 1), ('merge_bias', (MERGE,), 1, 1), ('merge_weight', (MERGE, EMB), 2, MERGE)]
    for layer in range(LAYERS):
        tag = str(layer)
        table += [('first_gain' + tag, (EMB,), 0, 1), ('first_bias' + tag, (EMB,), 1, 1), ('second_gain' + tag, (EMB,), 0, 1), ('second_bias' + tag, (EMB,), 1, 1), ('qkv_weight' + tag, (EMB, 3 * EMB), 2, EMB), ('qkv_bias' + tag, (3 * EMB,), 1, 1), ('proj_weight' + tag, (EMB, EMB), 2, EMB // 4), ('proj_bias' + tag, (EMB,), 1, 1), ('hidden_weight' + tag, (EMB, HID), 2, EMB), ('hidden_bias' + tag, (HID,), 1, 1), ('output_weight' + tag, (HID, EMB), 2, HID), ('output_bias' + tag, (EMB,), 1, 1)]
    table += [('conv_weight0', (3, 3, 3, EMB, EMB), 2, 27 * EMB), ('conv_bias0', (EMB,), 1, 1), ('conv_weight1', (3, 3, 3, EMB, EMB), 2, 27 * EMB), ('conv_bias1', (EMB,), 1, 1)]
    table += [('inorm_gain', (EMB,), 0, 1), ('inorm_bias', (EMB,), 1, 1), ('head_weight', (EMB, CLASSES), 2, EMB), ('head_bias', (CLASSES,), 1, 1)]
    return table


def draw_params(key, part):
    key = jax.random.fold_in(key, 7)
    noise = jax.random.normal(key, (NPARAM,), jnp.float32)
    pieces = []
    offset = 0
    for name, shape, kind, fan in layout_drawn():
        count = math.prod(shape)
        segment = noise[offset:offset + count]
        if kind == 0:
            pieces.append(1.0 + 0.1 * segment)
        elif kind == 1:
            pieces.append(0.1 * segment)
        else:
            pieces.append(segment * fan ** (-0.5))
        offset += count
    return jnp.concatenate(pieces)


def draw_valid(key, part):
    key = jax.random.fold_in(key, 11)
    score = jax.random.randint(key, (DEPTH, HH, WW), 0, 1000)
    planes = jnp.arange(DEPTH, dtype=jnp.int32)[:, None, None]
    limit = 250 + 700 * planes // DEPTH
    return (score < limit).astype(jnp.int32)


def with_ends(array, rng, smallest, top_value):
    place = [jax.random.randint(jax.random.fold_in(rng, axis), (), 0, length) for axis, length in enumerate(array.shape)]
    main_axis = array.shape.index(max(array.shape))
    beside = place[:main_axis] + [(place[main_axis] + 1) % array.shape[main_axis]] + place[main_axis + 1:]
    return array.at[tuple(place)].set(smallest).at[tuple(beside)].set(top_value)


def block_scale(own_key, extent, shards, least, high):
    def one(position, blocks):
        heights = jax.random.uniform(jax.random.fold_in(jax.random.fold_in(own_key, 6), position), (blocks,), jnp.float32, least / len(shards), high / len(shards))
        return jnp.repeat(jnp.exp(heights), extent[position] // blocks).reshape((-1,) + (1,) * (len(extent) - position - 1))

    factor_of = one(*shards[0])
    for cut in shards[1:]:
        factor_of = factor_of * one(*cut)
    return factor_of


def bell_draw(key, shape, scale, reach, cuts=(), kind=jnp.bfloat16):
    result = jax.random.normal(key, shape, jnp.float32) * scale
    if len(cuts) > 0:
        result = block_scale(key, shape, cuts, -0.22, 0.18) * result
    return jnp.clip(result, min=-reach, max=reach).astype(kind)


def setup_inputs(seed: int = 0) -> dict:
    splits = jax.random.split(jax.random.key(seed), 7)
    return {
        "feats": bell_draw(splits[0], (DEPTH, HH, WW, MERGE), 1.0, 6.0, ((0, 8), (1, 4)), jnp.float32),
        "labels": with_ends(jax.random.randint(splits[1], (DEPTH, HH, WW), 0, CLASSES), jax.random.fold_in(splits[1], 1), 0, CLASSES - 1).astype(jnp.int32),
        "valid": draw_valid(jax.random.fold_in(splits[6], 71), 0),
        "params": draw_params(jax.random.fold_in(splits[6], 71), 0),
        "moment_one": bell_draw(splits[4], (NPARAM,), (0.0011 / NPARAM ** 0.5), 1.52587890625e-05, (), jnp.float32),
        "moment_two": jnp.clip(jnp.exp(jax.random.uniform(splits[5], (NPARAM,), jnp.float32, math.log(1.1460556353752593e-13), math.log(4.584222541501037e-13))), 1.1460556353752593e-13, 4.584222541501037e-13),
    }


HIGH = lax.Precision.HIGHEST
eps_norm = 1e-05
beta_one = 0.9
beta_two = 0.999
adam_eps = 1e-08
learn_rate = 0.05
decay_rate = 0.05
clip_norm = 0.01

def layout():
    table = [('merge_gain', (MERGE,), 0, 1), ('merge_bias', (MERGE,), 1, 1), ('merge_weight', (MERGE, EMB), 2, MERGE)]
    for layer in range(LAYERS):
        tag = str(layer)
        table += [('first_gain' + tag, (EMB,), 0, 1), ('first_bias' + tag, (EMB,), 1, 1), ('second_gain' + tag, (EMB,), 0, 1), ('second_bias' + tag, (EMB,), 1, 1), ('qkv_weight' + tag, (EMB, 3 * EMB), 2, EMB), ('qkv_bias' + tag, (3 * EMB,), 1, 1), ('proj_weight' + tag, (EMB, EMB), 2, EMB // 4), ('proj_bias' + tag, (EMB,), 1, 1), ('hidden_weight' + tag, (EMB, HID), 2, EMB), ('hidden_bias' + tag, (HID,), 1, 1), ('output_weight' + tag, (HID, EMB), 2, HID), ('output_bias' + tag, (EMB,), 1, 1)]
    table += [('conv_weight0', (3, 3, 3, EMB, EMB), 2, 27 * EMB), ('conv_bias0', (EMB,), 1, 1), ('conv_weight1', (3, 3, 3, EMB, EMB), 2, 27 * EMB), ('conv_bias1', (EMB,), 1, 1)]
    table += [('inorm_gain', (EMB,), 0, 1), ('inorm_bias', (EMB,), 1, 1), ('head_weight', (EMB, CLASSES), 2, EMB), ('head_bias', (CLASSES,), 1, 1)]
    return table

def carve(flat):
    parts = {}
    offset = 0
    for name, shape, kind, fan in layout():
        count = math.prod(shape)
        parts[name] = flat[offset:offset + count].reshape(shape)
        offset += count
    return parts

def norm_rows(tokens, gain_row, bias_row):
    average = lax.optimization_barrier(jnp.mean(tokens, -1, keepdims=True))
    centred = tokens - average
    spread = lax.optimization_barrier(jnp.mean(centred * centred, -1, keepdims=True))
    return centred * lax.rsqrt(spread + eps_norm) * gain_row + bias_row

def matmul(tokens, weight):
    return jnp.einsum('...c,cd->...d', tokens, weight, precision=HIGH)

def embed(parts, feats):
    return matmul(norm_rows(feats, parts['merge_gain'], parts['merge_bias']), parts['merge_weight'])

def conv_valid(padded, weight):
    planes, height, breadth = (padded.shape[0] - 2, padded.shape[1] - 2, padded.shape[2] - 2)
    total = jnp.zeros((planes, height, breadth, weight.shape[-1]), jnp.float32)
    for first in range(3):
        for second in range(3):
            for third in range(3):
                total = total + matmul(padded[first:first + planes, second:second + height, third:third + breadth], weight[first, second, third])
    return total

def pad_all(volume):
    return jnp.pad(volume, ((1, 1), (1, 1), (1, 1), (0, 0)))

def conv_block(parts, tokens):
    inner = jax.nn.gelu(conv_valid(pad_all(tokens), parts['conv_weight0']) + parts['conv_bias0'], approximate=False)
    return tokens + conv_valid(pad_all(inner), parts['conv_weight1']) + parts['conv_bias1']

def partition(volume):
    planes, height, breadth, channels = volume.shape
    grid = volume.reshape(planes, height // WIN, WIN, breadth // WIN, WIN, channels).transpose(1, 3, 0, 2, 4, 5)
    return grid.reshape(height // WIN * (breadth // WIN), planes * WIN * WIN, channels)

def unpartition(windows, shape):
    planes, height, breadth, channels = shape
    grid = windows.reshape(height // WIN, breadth // WIN, planes, WIN, WIN, channels).transpose(2, 0, 3, 1, 4, 5)
    return grid.reshape(shape)

def region_ids(depth_pos, height_pos, breadth_pos, depth_len, height_len, breadth_len):

    def part_of(places, length):
        return jnp.where(places < length - WIN, 0, jnp.where(places < length - SHIFT, 1, 2))
    return (part_of(depth_pos, depth_len)[:, None, None] * 9 + part_of(height_pos, height_len)[None, :, None] * 3 + part_of(breadth_pos, breadth_len)[None, None, :]).astype(jnp.int32)

def window_attention(parts, layer, volume, region):
    tag = str(layer)
    window = partition(volume)
    count, length, channels = window.shape
    qkv = matmul(window, parts['qkv_weight' + tag]) + parts['qkv_bias' + tag]
    qkv = qkv.reshape(count, length, 3, HEADS, HDIM)
    queries, key_rows, value_rows = (qkv[:, :, 0], qkv[:, :, 1], qkv[:, :, 2])
    scores = jnp.einsum('nqhd,nkhd->nhqk', queries, key_rows, precision=HIGH) * HDIM ** (-0.5)
    if region is not None:
        labels_win = partition(region[..., None])[..., 0]
        same = labels_win[:, None, :, None] == labels_win[:, None, None, :]
        scores = scores + jnp.where(same, 0.0, -100.0)
    weights = jax.nn.softmax(scores, -1)
    mixed_rows = jnp.einsum('nhqk,nkhd->nqhd', weights, value_rows, precision=HIGH).reshape(count, length, channels)
    output = matmul(mixed_rows, parts['proj_weight' + tag]) + parts['proj_bias' + tag]
    return unpartition(output, volume.shape)

def pre_norm(parts, layer, tokens):
    tag = str(layer)
    return norm_rows(tokens, parts['first_gain' + tag], parts['first_bias' + tag])

def mlp_block(parts, layer, tokens, attended):
    tag = str(layer)
    middle = tokens + attended
    normed = norm_rows(middle, parts['second_gain' + tag], parts['second_bias' + tag])
    hidden = jax.nn.gelu(matmul(normed, parts['hidden_weight' + tag]) + parts['hidden_bias' + tag], approximate=False)
    return middle + matmul(hidden, parts['output_weight' + tag]) + parts['output_bias' + tag]

def head_loss(parts, tokens, first_sum, second_sum, voxels, labels, valid):
    average = first_sum / voxels
    spread = second_sum / voxels - average * average
    normed = (tokens - average) * lax.rsqrt(spread + eps_norm) * parts['inorm_gain'] + parts['inorm_bias']
    logits = matmul(jax.nn.gelu(normed, approximate=False), parts['head_weight']) + parts['head_bias']
    logp = jax.nn.log_softmax(logits, -1)
    picked = lax.optimization_barrier(jnp.sum(jnp.where(labels[..., None] == jnp.arange(CLASSES, dtype=jnp.int32), logp, 0.0), -1))
    return -picked * valid.astype(logp.dtype)

def by_blocks(func, *arrays):
    count = arrays[0].shape[0] // WIN
    stacked = tuple((item.reshape((count, WIN) + item.shape[1:]) for item in arrays))
    output = lax.map(lambda group: jax.checkpoint(func)(*group), stacked)
    return output.reshape((count * WIN,) + output.shape[2:])

def layer_step(parts, tokens, region, layer):
    shifted = layer % 2 == 1
    normed = pre_norm(parts, layer, tokens)
    if shifted:
        normed = jnp.roll(normed, (-SHIFT, -SHIFT, -SHIFT), (0, 1, 2))
        attended = by_blocks(lambda piece, ids: window_attention(parts, layer, piece, ids), normed, region)
        attended = jnp.roll(attended, (SHIFT, SHIFT, SHIFT), (0, 1, 2))
    else:
        attended = by_blocks(lambda piece: window_attention(parts, layer, piece, None), normed)
    return by_blocks(lambda piece, extra: mlp_block(parts, layer, piece, extra), tokens, attended)

def forward(flat, feats, labels, valid):
    parts = carve(flat)
    tokens = by_blocks(lambda piece: embed(parts, piece), feats)
    depth_len, height_len, breadth_len = tokens.shape[:3]
    region = region_ids(jnp.arange(depth_len), jnp.arange(height_len), jnp.arange(breadth_len), depth_len, height_len, breadth_len)
    for layer in range(LAYERS):
        tokens = jax.checkpoint(partial(layer_step, layer=layer))(parts, tokens, region)
    tokens = jax.checkpoint(conv_block)(parts, tokens)
    first_sum = lax.optimization_barrier(jnp.sum(tokens, (0, 1, 2)))
    second_sum = lax.optimization_barrier(jnp.sum(tokens * tokens, (0, 1, 2)))
    voxels = depth_len * height_len * breadth_len
    losses = by_blocks(lambda piece, lab, val: head_loss(parts, piece, first_sum, second_sum, voxels, lab, val), tokens, labels, valid)
    return jnp.sum(losses)

def adamw(param, grad, first, second, scale):
    grad = grad * scale
    first = beta_one * first + (1.0 - beta_one) * grad
    second = beta_two * second + (1.0 - beta_two) * grad * grad
    first_hat = first / (1.0 - beta_one ** STEP)
    second_hat = second / (1.0 - beta_two ** STEP)
    param = param - learn_rate * (first_hat / (jnp.sqrt(second_hat) + adam_eps) + decay_rate * param)
    return (param, first, second)

def reference(feats, labels, valid, params, moment_one, moment_two):
    valid_count = jnp.sum(valid).astype(params.dtype)
    loss_sum, backward = jax.vjp(lambda flat: forward(flat, feats, labels, valid), params)
    gradient, = backward(1.0 / valid_count)
    grad_norm = jnp.sqrt(jnp.sum(gradient * gradient))
    scale = jnp.minimum(1.0, clip_norm / (grad_norm + 1e-06))
    new_params, new_first, new_second = adamw(params, gradient, moment_one, moment_two, scale)
    return (loss_sum, valid_count, grad_norm, new_params, new_first, new_second)
```

```python
import functools

import jax
import jax.numpy as jnp
from jax import lax
from jax.experimental import pallas as pl
from jax.experimental.pallas import tpu as pltpu
from jax.sharding import PartitionSpec as P

EMB = 96
HEADS = 6
HDIM = 16
HID = 384
MERGE = 384
CLASSES = 14
WIN = 7
SHIFT = 3
LAYERS = 3
STEP = 10

F32 = jnp.float32
BF16 = jnp.bfloat16
eps_norm = 1e-05
beta_one = 0.9
beta_two = 0.999
adam_eps = 1e-08
learn_rate = 0.05
decay_rate = 0.05
clip_norm = 0.01

VOX = WIN * WIN * WIN
ROWS = 384
BLK = 128
WIDE = 128
PLANE = WIN * WIN
FAR = WIN - SHIFT
ROWS_A = SHIFT * FAR * WIN
ROWS_B = FAR * SHIFT * WIN
ROWS_C = SHIFT * SHIFT * WIN

MERGE_ROWS = 392
LAYER_ROWS = 1165
TAP_ROWS = 27 * EMB
GROUPS = 2280
NPARAM = 872558
FLAT_ROWS = GROUPS * 3
LAYER_BASE = (98, 389, 680)
CONV_BASE = (971, 1620)
CUTS = (0, 392, 688, 976, 2280)

R_QKV, R_QKVB, R_PROJ, R_PROJB = 4, 292, 295, 391
R_HID, R_HIDB, R_OUT, R_OUTB = 392, 776, 780, 1164

VMEM = 56 * 1024 * 1024


def iota(shape, dim):
    return lax.broadcasted_iota(jnp.int32, shape, dim)


def split(x):
    hi = x.astype(BF16)
    return hi, (x - hi.astype(F32)).astype(BF16)


def pair(x):
    return jnp.concatenate(split(x), 1)


def fold(y):
    half = y.shape[1] // 2
    return y[:, :half] + y[:, half:]


def fold_rows(y):
    half = y.shape[0] // 2
    return y[:half] + y[half:]


def dot(a, b):
    return jnp.dot(a, b, preferred_element_type=F32)


def dot_nt(a, b):
    return lax.dot_general(a, b, (((1,), (1,)), ((), ())), preferred_element_type=F32)


def weight_nn(w):
    top = pair(w)
    return jnp.concatenate([top, top], 0)


def weight_nt(w):
    hi, lo = split(w)
    return jnp.concatenate(
        [jnp.concatenate([hi, hi], 1), jnp.concatenate([lo, lo], 1)], 0
    )


def mm(x, w):
    return fold(dot(pair(x), weight_nn(w)))


def mm_nt(x, w):
    return fold(dot_nt(pair(x), weight_nt(w)))


def rows_t(x):
    return jnp.concatenate(split(x.T), 0)


def mm_tn(xt, y):
    return fold_rows(fold(dot(xt, pair(y))))


def deep(w):
    return jnp.concatenate([w, jnp.zeros((WIDE - EMB, w.shape[1]), F32)], 0)


def roll(x, shift, axis):
    return pltpu.roll(x, shift, axis)


def four_to_three(y):
    lane = iota(y[0].shape, 1)
    a = jnp.where(lane < 96, y[0], roll(y[1], 96, 1))
    b = jnp.where(lane < 64, roll(y[1], 96, 1), roll(y[2], 64, 1))
    c = jnp.where(lane < 32, roll(y[2], 64, 1), roll(y[3], 32, 1))
    return a, b, c


def three_to_four(x):
    lane = iota(x[0].shape, 1)
    live = lane < EMB
    a = x[0]
    b = jnp.where(lane < 32, roll(x[0], 32, 1), roll(x[1], 32, 1))
    c = jnp.where(lane < 64, roll(x[1], 64, 1), roll(x[2], 64, 1))
    d = roll(x[2], 96, 1)
    return tuple(jnp.where(live, v, 0.0) for v in (a, b, c, d))


def hidden_rows(ref, start, count):
    return jnp.concatenate(
        four_to_three([ref[pl.ds(start + c, count, stride=4), :] for c in range(4)]), 1
    )


def put_hidden_rows(ref, start, count, x):
    parts = three_to_four([x[:, i * WIDE : (i + 1) * WIDE] for i in range(3)])
    for c in range(4):
        ref[pl.ds(start + c, count, stride=4), :] = parts[c]


def flatten(ref, start, groups, out):
    parts = four_to_three([ref[pl.ds(start + c, groups, stride=4), :] for c in range(4)])
    for c in range(3):
        out[pl.ds(c, groups, stride=3), :] = parts[c]


def norm_stats(x):
    live = iota(x.shape, 1) < EMB
    mean = jnp.sum(x, 1, keepdims=True) * (1.0 / EMB)
    centred = jnp.where(live, x - mean, 0.0)
    var = jnp.sum(centred * centred, 1, keepdims=True) * (1.0 / EMB)
    inv = lax.rsqrt(var + eps_norm)
    return centred * inv, inv


def norm(x, gain, bias):
    hat, _ = norm_stats(x)
    return hat * gain + bias


def norm_back(hat, inv, gain, grad):
    up = grad * gain
    one = jnp.sum(up, 1, keepdims=True) * (1.0 / EMB)
    two = jnp.sum(up * hat, 1, keepdims=True) * (1.0 / EMB)
    live = iota(hat.shape, 1) < EMB
    return jnp.where(live, inv * (up - one - hat * two), 0.0)


def colsum(x):
    return jnp.sum(x, 0, keepdims=True)


def gelu(x):
    return 0.5 * x * (1.0 + lax.erf(x * (0.5**0.5)))


def gelu_both(x):
    cdf = 0.5 * (1.0 + lax.erf(x * (0.5**0.5)))
    slope = cdf + x * (jnp.exp(x * x * -0.5) * 0.3989422804014327)
    return x * cdf, slope


def head_groups(x):
    lane = iota(x.shape, 1)
    swapped = roll(x, 64, 1)
    return jnp.where(lane < 64, x, swapped), jnp.where(lane < 64, swapped, x)


def as_left(x):
    both = []
    low = iota(x.shape, 1) < 64
    for part in head_groups(x):
        hi = part.astype(BF16).astype(F32)
        one = jnp.where(low, hi, part - hi).astype(BF16)
        both.append(jnp.concatenate([one, one], 1))
    return both


def as_right(x):
    return [pair(part) for part in head_groups(x)]


def head_mask(h, width):
    lane = iota((1, width), 1)
    lane = jnp.bitwise_and(lane, 63)
    low = jnp.bitwise_and(h, 3) * HDIM
    return jnp.where((lane >= low) & (lane < low + HDIM), 1.0, 0.0)


def own_lanes(h):
    lane = iota((1, WIDE), 1)
    return jnp.where((lane >= h * HDIM) & (lane < (h + 1) * HDIM), 1.0, 0.0)


def scores(q, k, h, rows, region):
    left = q * head_mask(h, 2 * WIDE).astype(BF16)
    s = dot_nt(left, k)
    if region is not None:
        region_rows, region_lanes = region
        here = region_rows[rows, 0:1]
        s = s + jnp.where(here == region_lanes[0:1, :], 0.0, -100.0)
    return jnp.where(iota(s.shape, 1) < VOX, s, -1e30)


def attention(normed, layer, save, lse, mixed, left, right, values, region=None):
    x = pair(normed)
    qkv = []
    for i in range(3):
        w = deep(layer[pl.ds(R_QKV + i, EMB, stride=3), :])
        y = fold(dot(x, weight_nn(w))) + layer[R_QKVB + i : R_QKVB + i + 1, :]
        if i == 0:
            y = y * HDIM**-0.5
        save[:, i * WIDE : (i + 1) * WIDE] = y
        qkv.append(y)
    for g, part in enumerate(as_left(qkv[0])):
        left[g] = part
    for g, part in enumerate(as_right(qkv[1])):
        right[g] = part
    v = pair(qkv[2])
    values[0:ROWS, :] = v
    values[ROWS : 2 * ROWS, :] = v
    mixed[...] = jnp.zeros_like(mixed)
    lse[...] = jnp.zeros_like(lse)

    def per_head(h, carry):
        g = lax.div(h, 4)
        lanes = own_lanes(h)
        at_h = jnp.where(iota((1, WIDE), 1) == h, 1.0, 0.0)
        for b in range(ROWS // BLK):
            rows = slice(b * BLK, (b + 1) * BLK)
            s = scores(left[g, rows, :], right[g], h, rows, region)
            top = jnp.max(s, 1, keepdims=True)
            e = jnp.exp(s - top)
            total = jnp.sum(e, 1, keepdims=True)
            o = fold(dot(pair(e), values[...]))
            mixed[rows, :] += o * (lanes / total)
            lse[rows, :] += (top + jnp.log(total)) * at_h
        return carry

    lax.fori_loop(0, HEADS, per_head, 0)
    proj = deep(layer[R_PROJ : R_PROJ + EMB, :])
    return mm(mixed[...], proj) + layer[R_PROJB : R_PROJB + 1, :]


def attention_back(grad, normed, layer, save, lse, mixed, sc, grads, at, region=None):
    left, right, gleft, vright, keys, dq, dkv_t, weights, slopes, q_t, do_t, dmix = sc
    proj = deep(layer[R_PROJ : R_PROJ + EMB, :])
    grads[at + R_PROJ : at + R_PROJ + EMB, :] = mm_tn(rows_t(mixed[...]), grad)[:EMB]
    grads[at + R_PROJB : at + R_PROJB + 1, :] = colsum(grad)
    d_mixed = mm_nt(grad, proj)
    dmix[...] = d_mixed
    q, k, v = (save[:, i * WIDE : (i + 1) * WIDE] for i in range(3))
    for g, part in enumerate(as_left(q)):
        left[g] = part
    for g, part in enumerate(as_right(k)):
        right[g] = part
    for g, part in enumerate(as_left(d_mixed)):
        gleft[g] = part
    for g, part in enumerate(as_right(v)):
        vright[g] = part
    kk = pair(k)
    keys[0:ROWS, :] = kk
    keys[ROWS : 2 * ROWS, :] = kk
    for ref, x in ((q_t, q), (do_t, d_mixed)):
        hi, lo = split(x.T)
        ref[0] = hi
        ref[1] = lo
    dq[...] = jnp.zeros_like(dq)
    dkv_t[...] = jnp.zeros_like(dkv_t)

    def per_head(h, carry):
        g = lax.div(h, 4)
        lanes = own_lanes(h)
        at_h = jnp.where(iota((1, WIDE), 1) == h, 1.0, 0.0)
        mask = head_mask(h, 2 * WIDE).astype(BF16)
        for b in range(ROWS // BLK):
            rows = slice(b * BLK, (b + 1) * BLK)
            s = scores(left[g, rows, :], right[g], h, rows, region)
            level = jnp.sum(lse[rows, :] * at_h, 1, keepdims=True)
            p = jnp.exp(s - level)
            dp = dot_nt(gleft[g, rows, :] * mask, vright[g])
            delta = jnp.sum(dmix[rows, :] * mixed[rows, :] * lanes, 1, keepdims=True)
            ds = p * (dp - delta)
            both = pair(ds)
            weights[rows, :] = pair(p)
            slopes[rows, :] = both
            dq[rows, :] += fold(dot(both, keys[...])) * lanes
        here = pl.multiple_of(h * HDIM, HDIM)
        for i, (t, m) in enumerate(((q_t, slopes), (do_t, weights))):
            lhs = jnp.concatenate([t[0, pl.ds(here, HDIM), :], t[1, pl.ds(here, HDIM), :]], 0)
            out = fold_rows(fold(dot(lhs, m[...])))
            dkv_t[i, pl.ds(here, HDIM), :] = out
        return carry

    lax.fori_loop(0, HEADS, per_head, 0)
    d_q = dq[...] * HDIM**-0.5
    d_k = dkv_t[0].T
    d_v = dkv_t[1].T
    x_t = rows_t(normed)
    d_normed = None
    for i, d in enumerate((d_q, d_k, d_v)):
        grads[pl.ds(at + R_QKV + i, EMB, stride=3), :] = mm_tn(x_t, d)[:EMB]
        grads[at + R_QKVB + i : at + R_QKVB + i + 1, :] = colsum(d)
        part = mm_nt(d, deep(layer[pl.ds(R_QKV + i, EMB, stride=3), :]))
        d_normed = part if d_normed is None else d_normed + part
    return d_normed


def mlp(middle, layer, hpre):
    normed = norm(middle, layer[2:3, :], layer[3:4, :])
    w = deep(hidden_rows(layer, R_HID, EMB))
    pre = mm(normed, w) + hidden_rows(layer, R_HIDB, 1)
    hpre[...] = pre
    out = mm(gelu(pre), layer[R_OUT : R_OUT + HID, :])
    return middle + out + layer[R_OUTB : R_OUTB + 1, :]


def mlp_back(grad, middle, hpre, layer, grads, at):
    hat, inv = norm_stats(middle)
    normed = hat * layer[2:3, :] + layer[3:4, :]
    act, slope = gelu_both(hpre[...])
    grads[at + R_OUTB : at + R_OUTB + 1, :] = colsum(grad)
    grads[at + R_OUT : at + R_OUT + HID, :] = mm_tn(rows_t(grad), act).T
    d_pre = mm_nt(grad, layer[R_OUT : R_OUT + HID, :]) * slope
    put_hidden_rows(grads, at + R_HIDB, 1, colsum(d_pre))
    put_hidden_rows(grads, at + R_HID, EMB, mm_tn(rows_t(normed), d_pre)[:EMB])
    d_normed = mm_nt(d_pre, deep(hidden_rows(layer, R_HID, EMB)))
    grads[at + 2 : at + 3, :] = colsum(d_normed * hat)
    grads[at + 3 : at + 4, :] = colsum(d_normed)
    return grad + norm_back(hat, inv, layer[2:3, :], d_normed)


def pre_norm_back(grad, tokens, layer, grads, at):
    hat, inv = norm_stats(tokens)
    grads[at : at + 1, :] = colsum(grad * hat)
    grads[at + 1 : at + 2, :] = colsum(grad)
    return norm_back(hat, inv, layer[0:1, :], grad)


def send_parts(ref, a, b, c):
    far = FAR * WIN
    near = SHIFT * WIN
    for d in range(SHIFT):
        base = d * PLANE
        c[d * near : (d + 1) * near, :] = ref[base : base + near, :]
        a[d * far : (d + 1) * far, :] = ref[base + near : base + PLANE, :]
    for d in range(FAR):
        base = (d + SHIFT) * PLANE
        b[d * near : (d + 1) * near, :] = ref[base : base + near, :]


def take_parts(own, a, b, c, out):
    far = FAR * WIN
    near = SHIFT * WIN
    for d in range(WIN):
        base = d * PLANE
        if d < SHIFT:
            out[base : base + near, :] = c[d * near : (d + 1) * near, :]
            out[base + near : base + PLANE, :] = a[d * far : (d + 1) * far, :]
        else:
            e = d - SHIFT
            out[base : base + near, :] = b[e * near : (e + 1) * near, :]
            out[base + near : base + PLANE, :] = own[base + near : base + PLANE, :]
    out[VOX:, :] = jnp.zeros((ROWS - VOX, WIDE), F32)


def prep_kernel(flat, merge, lay0, lay1, lay2, conv0, conv1):
    spans = [(0, 98)] + [(g, g + 292) for g in LAYER_BASE]
    spans += [(CONV_BASE[0], CONV_BASE[0] + 649), (CONV_BASE[1], GROUPS)]
    for out, (low, high) in zip((merge, lay0, lay1, lay2, conv0, conv1), spans):
        count = high - low
        parts = three_to_four(
            [flat[pl.ds(3 * low + c, count, stride=3), :] for c in range(3)]
        )
        for c in range(4):
            out[pl.ds(c, count, stride=4), :] = parts[c]


def offset(ref, at):
    return ref.at[pl.ds(at, ref.shape[0] - at), :]


class Rows:
    def __init__(self, ref, at):
        self.ref, self.at = ref, at

    def __getitem__(self, key):
        rows, lanes = key
        if isinstance(rows, slice):
            rows = slice(rows.start + self.at, rows.stop + self.at)
        else:
            rows = pl.ds(rows.start + self.at, rows.size, stride=rows.stride)
        return self.ref[rows, lanes]


def merged_norm(x):
    mean = jnp.sum(x, 1, keepdims=True) * (1.0 / MERGE)
    centred = x - mean
    var = jnp.sum(centred * centred, 1, keepdims=True) * (1.0 / MERGE)
    return centred * lax.rsqrt(var + eps_norm)


def first_kernel(
    feats, merge, lay0, lay1,
    dense, tok0, save, lse, mixed, middle, hpre, tok1, ahead, pa, pb, pc,
    left, right, values,
):
    dense[VOX:, :] = jnp.zeros((ROWS - VOX, MERGE), F32)
    for line in range(PLANE):
        dense[line * WIN : (line + 1) * WIN, :] = feats[line]
    hat = merged_norm(dense[...])
    normed = hat * hidden_rows(merge, 0, 1) + hidden_rows(merge, 4, 1)
    tokens = mm(normed, merge[8 : 8 + MERGE, :])
    tok0[...] = tokens
    layer = Rows(lay0, 0)
    normed = norm(tokens, layer[0:1, :], layer[1:2, :])
    attended = attention(normed, layer, save, lse, mixed, left, right, values)
    mid = tokens + attended
    middle[...] = mid
    tokens = mlp(mid, layer, hpre)
    tok1[...] = tokens
    ahead[...] = norm(tokens, lay1[1:2, :], lay1[2:3, :])
    send_parts(ahead, pa, pb, pc)


def shifted_kernel(
    own, pa, pb, pc, lay1, region_rows, region_lanes,
    window, save, lse, mixed, out, qa, qb, qc,
    left, right, values,
):
    take_parts(own, pa, pb, pc, window)
    out[...] = attention(
        window[...], Rows(lay1, 1), save, lse, mixed, left, right, values,
        (region_rows, region_lanes),
    )
    send_parts(out, qa, qb, qc)


def to_lines(ref, out):
    for line in range(PLANE):
        out[line, 0:WIN, :] = ref[line * WIN : (line + 1) * WIN, :]
        out[line, WIN:8, :] = jnp.zeros((8 - WIN, WIDE), F32)


def from_lines(ref, out):
    out[VOX:, :] = jnp.zeros((ROWS - VOX, WIDE), F32)
    for line in range(PLANE):
        out[line * WIN : (line + 1) * WIN, :] = ref[line, 0:WIN, :]


def second_kernel(
    tok1, own, qa, qb, qc, lay1, lay2,
    mid1, hpre1, tok2, save, lse, mixed, mid2, hpre2, lines,
    attended, left, right, values,
):
    take_parts(own, qa, qb, qc, attended)
    mid = tok1[...] + attended[...]
    mid1[...] = mid
    tokens = mlp(mid, Rows(lay1, 1), hpre1)
    tok2[...] = tokens
    layer = Rows(lay2, 2)
    normed = norm(tokens, layer[0:1, :], layer[1:2, :])
    mid = tokens + attention(normed, layer, save, lse, mixed, left, right, values)
    mid2[...] = mid
    attended[...] = mlp(mid, layer, hpre2)
    to_lines(attended, lines)


def grown_lines(own, low_d, high_d, low_h, high_h, out):
    out[...] = jnp.zeros_like(out)
    for d in range(WIN):
        out[d + 2, 2 : 2 + WIN] = own[d * WIN : (d + 1) * WIN]
    for d in range(2):
        out[d, 2 : 2 + WIN] = low_d[d * WIN : (d + 1) * WIN]
        out[d + 9, 2 : 2 + WIN] = high_d[d * WIN : (d + 1) * WIN]
    for d in range(11):
        out[d, 0:2] = low_h[2 * d : 2 * d + 2]
        out[d, 9:11] = high_h[2 * d : 2 * d + 2]


def taps(source, first_plane, planes, first_line, lines, out):
    def per_plane(d, carry):
        for c in range(3):
            for b in range(3):
                x = source[d + first_plane, first_line + b : first_line + b + lines]
                if c != 1:
                    x = roll(x, 1 if c == 0 else 7, 1)
                x = pair(x.reshape(lines * 8, WIDE))
                at = pl.multiple_of(d * (lines * 8), lines * 8)
                t = b * 3 + c
                out[pl.ds(at, lines * 8), t * 256 : (t + 1) * 256] = x
        return carry

    lax.fori_loop(0, planes, per_plane, 0)


def tap_weights(ref, at, out):
    def per_tap(i, carry):
        w = deep(ref[pl.ds(i * EMB + at, EMB), :])
        out[pl.ds(pl.multiple_of(i * 256, 256), 256), :] = weight_nn(w)
        return carry

    lax.fori_loop(0, 27, per_tap, 0)


def tap_weights_back(ref, at, out):
    def per_tap(i, carry):
        w = deep(ref[pl.ds((26 - i) * EMB + at, EMB), :]).T
        out[pl.ds(pl.multiple_of(i * 256, 256), 256), :] = weight_nn(w)
        return carry

    lax.fori_loop(0, 27, per_tap, 0)


def conv(side, weights, planes, pitch, at_once, put):
    rows = at_once * pitch
    for start in range(0, planes, at_once):
        total = None
        for a in range(3):
            low = (start + a) * pitch
            part = dot(side[low : low + rows, :], weights[a * 2304 : (a + 1) * 2304, :])
            total = part if total is None else total + part
        put(start, fold(total))


def conv_weight_grad(side, grad_rows, pitch, out, at):
    rows = 512
    g = jnp.concatenate([grad_rows, jnp.zeros((rows - grad_rows.shape[0], WIDE), F32)], 0)
    left = rows_t(g)
    for a in range(3):
        for bc in range(9):
            y = dot(left, side[a * pitch : a * pitch + rows, bc * 256 : (bc + 1) * 256])
            y = fold_rows(fold(y)).T
            t = a * 9 + bc
            out[at + t * EMB : at + (t + 1) * EMB, :] = y[:EMB]


def volume_mask(ends, planes, lines, reach, real_lines):
    shape = (planes, lines, 8, WIDE)
    d, h, w = iota(shape, 0), iota(shape, 1), iota(shape, 2)
    low_d = jnp.where(ends[0] == 1, reach, 0)
    high_d = jnp.where(ends[1] == 1, planes - reach, planes)
    low_h = jnp.where(ends[2] == 1, reach, 0)
    high_h = jnp.where(ends[3] == 1, real_lines - reach, real_lines)
    inside = (d >= low_d) & (d < high_d) & (h >= low_h) & (h < high_h) & (w < WIN)
    return jnp.where(inside, 1.0, 0.0)


def conv_kernel(
    ends, own, low_d, high_d, low_h, high_h, marks, conv0, conv1,
    grown, pre, tok, stats,
    act, side, side_own, weights,
):
    grown_lines(own, low_d, high_d, low_h, high_h, grown)
    tap_weights(conv0, 3, weights)
    taps(grown, 0, 11, 0, 10, side)
    bias0 = conv0[3 + TAP_ROWS : 4 + TAP_ROWS, :]
    inside = volume_mask(ends, 9, 10, 1, 9)

    def put(start, y):
        z = (y + bias0).reshape(3, 10, 8, WIDE)
        pre[start : start + 3] = z
        act[start : start + 3] = gelu(z) * inside[start : start + 3]

    conv(side, weights, 9, 80, 3, put)
    tap_weights(conv1, 0, weights)
    taps(act, 0, 9, 0, 8, side_own)
    bias1 = conv1[TAP_ROWS : TAP_ROWS + 1, :]
    sums = []

    def put_own(start, y):
        y = (y + bias1).reshape(WIN, 8, 8, WIDE)[:, 0:WIN]
        y = y + own[...].reshape(WIN, WIN, 8, WIDE)
        y = jnp.where(iota(y.shape, 2) < WIN, y, 0.0).reshape(PLANE, 8, WIDE)
        tok[...] = y + marks[...]
        flat = y.reshape(PLANE * 8, WIDE)
        sums.append(colsum(flat))
        sums.append(colsum(flat * flat))

    conv(side_own, weights, WIN, 64, WIN, put_own)
    count = jnp.sum(marks[...].reshape(PLANE * 8, WIDE))
    row = iota((8, WIDE), 0)
    stats[...] = (
        jnp.where(row == 0, sums[0], 0.0)
        + jnp.where(row == 1, sums[1], 0.0)
        + jnp.where(row == 2, count, 0.0)
    )


def head_kernel(
    own, low_d, high_d, low_h, high_h, sums, conv1, head_w, head_b, voxels,
    grown, slope_out, stats, d_head, d_rows,
):
    grown_lines(own, low_d, high_d, low_h, high_h, grown)
    rows = 11 * 12 * 8
    both = grown[...].reshape(rows, WIDE)
    lane = iota((rows, WIDE), 1)
    tokens = jnp.where(lane < EMB, both, 0.0)
    target = jnp.where(lane < CLASSES, roll(both, WIDE - EMB, 1), 0.0)
    live = jnp.sum(target, 1, keepdims=True)
    count = voxels[0]
    average = sums[0:1, :] / count
    spread = sums[1:2, :] / count - average * average
    inv = lax.rsqrt(spread + eps_norm)
    gain = conv1[TAP_ROWS + 1 : TAP_ROWS + 2, :]
    bias = conv1[TAP_ROWS + 2 : TAP_ROWS + 3, :]
    hat = (tokens - average) * inv
    act, slope = gelu_both(hat * gain + bias)
    w = head_w[...]
    logits = mm(act, w) + head_b[0:1, :]
    logits = jnp.where(lane < CLASSES, logits, -1e30)
    top = jnp.max(logits, 1, keepdims=True)
    e = jnp.exp(logits - top)
    total = jnp.sum(e, 1, keepdims=True)
    logp = logits - top - jnp.log(total)
    scale = 1.0 / sums[2:3, 0:1]
    d_logits = (e / total * live - target) * scale
    d_normed = mm_nt(d_logits, w) * slope
    d_tokens = d_normed * gain * inv
    slope_out[...] = d_tokens.reshape(11, 12, 8, WIDE)

    def own_rows(x):
        x = x.reshape(11, 12, 8, WIDE)[2:9, 2:9]
        x = jnp.where(iota(x.shape, 2) < WIN, x, 0.0)
        return x.reshape(PLANE * 8, WIDE)

    loss = -jnp.sum(own_rows(target * jnp.where(lane < CLASSES, logp, 0.0)))
    own_d = own_rows(d_logits)
    own_n = own_rows(d_normed)
    own_hat = own_rows(hat)
    zeros = jnp.zeros((512 - PLANE * 8, WIDE), F32)
    left = rows_t(jnp.concatenate([own_d, zeros], 0))
    d_head[...] = mm_tn(left, jnp.concatenate([own_rows(act), zeros], 0)).T
    d_gain = colsum(own_n * own_hat)
    d_bias = colsum(own_n)
    d_average = -d_bias * gain * inv
    d_spread = d_gain * gain * inv * inv * -0.5
    d_two = d_spread / count
    d_one = (d_average - 2.0 * average * d_spread) / count
    row = iota((8, WIDE), 0)
    live_lane = iota((8, WIDE), 1) < EMB
    stats[...] = (
        jnp.where((row == 0) & live_lane, d_one, 0.0)
        + jnp.where((row == 1) & live_lane, d_two, 0.0)
        + jnp.where(row == 2, loss, 0.0)
    )
    d_rows[...] = (
        jnp.where(row == 0, d_gain, 0.0)
        + jnp.where(row == 1, d_bias, 0.0)
        + jnp.where(row == 2, colsum(own_d), 0.0)
    )


def conv_back_kernel(
    ends, tok, slope, sums, grown, pre, conv0, conv1, d_rows, d_head,
    d_own, flat, carry,
    grads, dgrown, act, side, side_own, weights,
):
    lane = iota((11, 12, 8, WIDE), 3)
    inside = volume_mask(ends, 11, 12, 2, 11)
    steady = sums[0:1, :].reshape(1, 1, 1, WIDE)
    rising = 2.0 * sums[1:2, :].reshape(1, 1, 1, WIDE)
    d_tok = slope[...] + jnp.where(lane < EMB, (steady + tok[...] * rising) * inside, 0.0)
    dgrown[...] = d_tok
    grads[5208:, :] = jnp.zeros((28, WIDE), F32)
    grads[0:8, :] = jnp.zeros((8, WIDE), F32)
    grads[5189:5191, :] = d_rows[0:2, :]
    grads[5191:5208, :] = d_head[0:17, :]
    own = dgrown[2:9, 2:10]
    line = iota(own.shape, 1)
    own = jnp.where(line < WIN, own, 0.0).reshape(WIN * 64, WIDE)
    grads[5188:5189, :] = colsum(own)

    near = volume_mask(ends, 9, 10, 1, 9)
    act[0:9] = gelu(pre[...]) * near
    act[9:10] = jnp.zeros((1, 10, 8, WIDE), F32)
    taps(act, 0, 10, 0, 8, side_own)
    conv_weight_grad(side_own, own, 64, grads, 2596)
    tap_weights_back(conv1, 0, weights)
    taps(dgrown, 0, 11, 0, 10, side)

    def put(start, y):
        _, s = gelu_both(pre[start : start + 3])
        z = y.reshape(3, 10, 8, WIDE) * s * near[start : start + 3]
        act[start : start + 3] = z

    conv(side, weights, 9, 80, 3, put)

    own = act[1:8, 1:9]
    line = iota(own.shape, 1)
    own = jnp.where(line < WIN, own, 0.0).reshape(WIN * 64, WIDE)
    grads[2595:2596, :] = colsum(own)
    taps(grown, 1, 10, 1, 8, side_own)
    conv_weight_grad(side_own, own, 64, grads, 3)
    carry[...] = grads[0:24, :]
    flatten(grads, 20, GROUPS - CUTS[3], flat)
    tap_weights_back(conv0, 3, weights)
    taps(act, 0, 9, 0, 8, side_own)

    def put_own(start, y):
        y = y.reshape(WIN, 8, 8, WIDE)[:, 0:WIN] + dgrown[2:9, 2:9]
        y = jnp.where(iota(y.shape, 2) < WIN, y, 0.0)
        d_own[...] = y.reshape(PLANE, 8, WIDE)

    conv(side_own, weights, WIN, 64, WIN, put_own)


def back_two_kernel(
    d_own, carry, lay1, lay2, tok2, save, lse, mixed, mid2, hpre2, mid1, hpre1,
    d_mid, grads1, flat, carry2, pa, pb, pc,
    grads, dense, *sc,
):
    from_lines(d_own, dense)
    layer = Rows(lay2, 2)
    grads[0:8, :] = jnp.zeros((8, WIDE), F32)
    d = mlp_back(dense[...], mid2[...], hpre2, layer, grads, 2)
    tokens = tok2[...]
    normed = norm(tokens, layer[0:1, :], layer[1:2, :])
    d_normed = attention_back(d, normed, layer, save, lse, mixed, sc, grads, 2)
    d = d + pre_norm_back(d_normed, tokens, layer, grads, 2)
    grads[1167:1184, :] = carry[3:20, :]
    flatten(grads, 32, CUTS[3] - CUTS[2], flat)
    carry2[...] = grads[0:32, :]
    layer = Rows(lay1, 1)
    d = mlp_back(d, mid1[...], hpre1, layer, grads1, 1)
    d_mid[...] = d
    send_parts(d_mid, pa, pb, pc)


def back_shifted_kernel(
    own, pa, pb, pc, lay1, region_rows, region_lanes, window, save, lse, mixed, grads1, carry2,
    d_window, flat, carry1, qa, qb, qc,
    grads, grad, *sc,
):
    take_parts(own, pa, pb, pc, grad)
    grads[0:1168, :] = grads1[...]
    grads[0:3, :] = jnp.zeros((3, WIDE), F32)
    d_window[...] = attention_back(
        grad[...], window[...], Rows(lay1, 1), save, lse, mixed, sc, grads, 1,
        (region_rows, region_lanes),
    )
    send_parts(d_window, qa, qb, qc)
    grads[1166:1196, :] = carry2[2:32, :]
    flatten(grads, 12, CUTS[2] - CUTS[1], flat)
    carry1[...] = grads[0:16, :]


def back_first_kernel(
    d_mid, own, qa, qb, qc, tok1, lay0, lay1, merge, dense, tok0, save, lse, mixed, middle, hpre, carry1,
    flat,
    grads, grad, *sc,
):
    take_parts(own, qa, qb, qc, grad)
    grads[1556:1572, :] = carry1[...]
    d = d_mid[...] + pre_norm_back(grad[...], tok1[...], Rows(lay1, 1), grads, 1557)
    layer = Rows(lay0, 0)
    at = MERGE_ROWS
    d = mlp_back(d, middle[...], hpre, layer, grads, at)
    tokens = tok0[...]
    normed = norm(tokens, layer[0:1, :], layer[1:2, :])
    d_normed = attention_back(d, normed, layer, save, lse, mixed, sc, grads, at)
    d = d + pre_norm_back(d_normed, tokens, layer, grads, at)
    live = iota((ROWS, WIDE), 0) < VOX
    d = jnp.where(live, d, 0.0)
    hat = merged_norm(dense[...])
    gain = hidden_rows(merge, 0, 1)
    bias = hidden_rows(merge, 4, 1)
    w = merge[8 : 8 + MERGE, :]
    put_hidden_rows(grads, 8 - 8, 1, jnp.zeros((1, MERGE), F32))
    grads[8 : 8 + MERGE, :] = mm_tn(rows_t(d), hat * gain + bias).T
    d_hat = mm_nt(d, w)
    put_hidden_rows(grads, 0, 1, colsum(d_hat * hat))
    put_hidden_rows(grads, 4, 1, colsum(d_hat))
    flatten(grads, 0, CUTS[1], flat)


def arr(*shape):
    return jax.ShapeDtypeStruct(shape, F32)


def call(kernel, outs, scratch, *args, scalars=0, name=None):
    smem = pl.BlockSpec(memory_space=pltpu.SMEM)
    vmem = pl.BlockSpec(memory_space=pltpu.VMEM)
    specs = [smem if a.size <= 8 and a.ndim == 1 else vmem for a in args]
    return pl.pallas_call(
        kernel,
        out_shape=list(outs),
        in_specs=specs,
        out_specs=[vmem] * len(outs),
        scratch_shapes=list(scratch),
        compiler_params=pltpu.CompilerParams(vmem_limit_bytes=VMEM),
        name=name,
    )(*args)


SQUARE = arr(ROWS, WIDE)
SAVE = arr(ROWS, 3 * WIDE)
FORWARD = [
    pltpu.VMEM((2, ROWS, 2 * WIDE), BF16),
    pltpu.VMEM((2, ROWS, 2 * WIDE), BF16),
    pltpu.VMEM((2 * ROWS, 2 * WIDE), BF16),
]
BACKWARD = [
    pltpu.VMEM((2, ROWS, 2 * WIDE), BF16),
    pltpu.VMEM((2, ROWS, 2 * WIDE), BF16),
    pltpu.VMEM((2, ROWS, 2 * WIDE), BF16),
    pltpu.VMEM((2, ROWS, 2 * WIDE), BF16),
    pltpu.VMEM((2 * ROWS, 2 * WIDE), BF16),
    pltpu.VMEM((ROWS, WIDE), F32),
    pltpu.VMEM((2, WIDE, ROWS), F32),
    pltpu.VMEM((ROWS, 2 * ROWS), BF16),
    pltpu.VMEM((ROWS, 2 * ROWS), BF16),
    pltpu.VMEM((2, WIDE, ROWS), BF16),
    pltpu.VMEM((2, WIDE, ROWS), BF16),
    pltpu.VMEM((ROWS, WIDE), F32),
]
PARTS = [arr(ROWS_A, WIDE), arr(ROWS_B, WIDE), arr(ROWS_C, WIDE)]


def passed(parts, steps, sizes):
    slabs, rows = sizes
    moved = []
    for part, (ds, dm) in zip(parts, ((1, 0), (0, 1), (1, 1))):
        pairs = []
        for s in range(slabs):
            for m in range(rows):
                target = ((s + steps * ds) % slabs) * rows + (m + steps * dm) % rows
                pairs.append((s * rows + m, target))
        moved.append(lax.ppermute(part, ("slab", "mp"), pairs))
    return moved


def beside(lines, sizes):
    slabs, rows = sizes
    up = [(i, i + 1) for i in range(slabs - 1)]
    down = [(i + 1, i) for i in range(slabs - 1)]
    low_d = lax.ppermute(lines[(WIN - 2) * WIN :], "slab", up)
    high_d = lax.ppermute(lines[: 2 * WIN], "slab", down)
    column = jnp.concatenate([low_d, lines, high_d], 0).reshape(11, WIN, 8, WIDE)
    first = column[:, 0:2].reshape(22, 8, WIDE)
    last = column[:, WIN - 2 :].reshape(22, 8, WIDE)
    up = [(i, i + 1) for i in range(rows - 1)]
    down = [(i + 1, i) for i in range(rows - 1)]
    low_h = lax.ppermute(last, "mp", up)
    high_h = lax.ppermute(first, "mp", down)
    return low_d, high_d, low_h, high_h


def window_regions(slab, row, sizes):
    def part_of(places, length):
        return jnp.where(places < length - WIN, 0, jnp.where(places < length - SHIFT, 1, 2))

    turned = (jnp.arange(WIN, dtype=jnp.int32) + FAR) % WIN
    depth = part_of(slab * WIN + turned, WIN * sizes[0])
    height = part_of(row * WIN + turned, WIN * sizes[1])
    breadth = part_of(turned, WIN)
    ids = depth[:, None, None] * 9 + height[None, :, None] * 3 + breadth[None, None, :]
    ids = jnp.pad(ids.reshape(VOX).astype(F32), (0, ROWS - VOX))
    return jnp.broadcast_to(ids[:, None], (ROWS, WIDE)), jnp.broadcast_to(ids[None], (8, ROWS))


def adamw(param, grad, first, second, scale):
    grad = grad * scale
    first = beta_one * first + (1.0 - beta_one) * grad
    second = beta_two * second + (1.0 - beta_two) * grad * grad
    first_hat = first / (1.0 - beta_one**STEP)
    second_hat = second / (1.0 - beta_two**STEP)
    param = param - learn_rate * (
        first_hat / (jnp.sqrt(second_hat) + adam_eps) + decay_rate * param
    )
    return (param, first, second)


def on_device(sizes, feats, labels, valid, params, moment_one, moment_two):
    slabs, rows = sizes
    slab, row = lax.axis_index("slab"), lax.axis_index("mp")
    both = ("slab", "mp")
    ends = jnp.stack([slab == 0, slab == slabs - 1, row == 0, row == rows - 1]).astype(jnp.int32)
    region = window_regions(slab, row, sizes)
    voxels = jnp.full((1,), WIN * slabs * WIN * rows * WIN, F32)

    flat = jnp.pad(params, (0, FLAT_ROWS * WIDE - NPARAM)).reshape(FLAT_ROWS, WIDE)
    merge, lay0, lay1, lay2, conv0, conv1 = call(
        prep_kernel,
        [arr(MERGE_ROWS, WIDE)] + [arr(1168, WIDE)] * 3 + [arr(2596, WIDE), arr(2640, WIDE)],
        [],
        flat,
        name="prep",
    )
    head = params[NPARAM - CLASSES * (EMB + 1) :]
    head_w = jnp.pad(
        head[: EMB * CLASSES].reshape(EMB, CLASSES), ((0, WIDE - EMB), (0, WIDE - CLASSES))
    )
    head_b = jnp.broadcast_to(jnp.pad(head[EMB * CLASSES :], (0, WIDE - CLASSES)), (8, WIDE))
    classes = jnp.arange(WIDE, dtype=jnp.int32) - EMB
    marks = (labels[..., None] == classes).astype(F32) * valid.astype(F32)[..., None]
    marks = jnp.pad(marks, ((0, 0), (0, 0), (0, 1), (0, 0))).reshape(PLANE, 8, WIDE)

    dense, tok0, save0, lse0, mixed0, mid0, hpre0, tok1, ahead, *parts = call(
        first_kernel,
        [arr(ROWS, MERGE), SQUARE, SAVE, SQUARE, SQUARE, SQUARE, arr(ROWS, HID), SQUARE, SQUARE]
        + PARTS,
        FORWARD,
        feats.reshape(PLANE, WIN, MERGE), merge, lay0, lay1,
        name="first",
    )
    parts = passed(parts, -1, sizes)
    window, save1, lse1, mixed1, out1, *parts = call(
        shifted_kernel,
        [SQUARE, SAVE, SQUARE, SQUARE, SQUARE] + PARTS,
        FORWARD,
        ahead, *parts, lay1, *region,
        name="shifted",
    )
    parts = passed(parts, 1, sizes)
    mid1, hpre1, tok2, save2, lse2, mixed2, mid2, hpre2, lines = call(
        second_kernel,
        [SQUARE, arr(ROWS, HID), SQUARE, SAVE, SQUARE, SQUARE, SQUARE, arr(ROWS, HID)]
        + [arr(PLANE, 8, WIDE)],
        [pltpu.VMEM((ROWS, WIDE), F32)] + FORWARD,
        tok1, out1, *parts, lay1, lay2,
        name="second",
    )
    near = beside(lines, sizes)
    grown, pre, tok3, stats = call(
        conv_kernel,
        [arr(11, 12, 8, WIDE), arr(9, 10, 8, WIDE), arr(PLANE, 8, WIDE), arr(8, WIDE)],
        [
            pltpu.VMEM((9, 10, 8, WIDE), F32),
            pltpu.VMEM((880, 2304), BF16),
            pltpu.VMEM((576, 2304), BF16),
            pltpu.VMEM((27 * 256, 256), BF16),
        ],
        ends, lines, *near, marks, conv0, conv1,
        name="conv",
    )
    near = beside(tok3, sizes)
    stats = lax.psum(stats, both)
    tok3, slope, tail, d_head, d_rows = call(
        head_kernel,
        [arr(11, 12, 8, WIDE), arr(11, 12, 8, WIDE), arr(8, WIDE), arr(WIDE, WIDE), arr(8, WIDE)],
        [],
        tok3, *near, stats, conv1, head_w, head_b, voxels,
        name="head",
    )
    d_head = jnp.concatenate([d_head[:EMB, :CLASSES].reshape(-1), d_rows[2, :CLASSES]])
    d_head = jnp.pad(d_head, (0, 24 * EMB - CLASSES * (EMB + 1))).reshape(24, EMB)
    d_head = jnp.pad(d_head, ((0, 0), (0, WIDE - EMB)))
    tail = lax.psum(tail, both)
    d_own, flat3, carry3 = call(
        conv_back_kernel,
        [arr(PLANE, 8, WIDE), arr(3 * (CUTS[4] - CUTS[3]), WIDE), arr(24, WIDE)],
        [
            pltpu.VMEM((5236, WIDE), F32),
            pltpu.VMEM((11, 12, 8, WIDE), F32),
            pltpu.VMEM((10, 10, 8, WIDE), F32),
            pltpu.VMEM((880, 2304), BF16),
            pltpu.VMEM((640, 2304), BF16),
            pltpu.VMEM((27 * 256, 256), BF16),
        ],
        ends, tok3, slope, tail, grown, pre, conv0, conv1, d_rows, d_head,
        name="conv_back",
    )
    flat3 = lax.psum(flat3.reshape(-1), both)
    d_mid, grads1, flat2, carry2, *parts = call(
        back_two_kernel,
        [SQUARE, arr(1168, WIDE), arr(3 * (CUTS[3] - CUTS[2]), WIDE), arr(32, WIDE)] + PARTS,
        [pltpu.VMEM((1184, WIDE), F32), pltpu.VMEM((ROWS, WIDE), F32)] + BACKWARD,
        d_own, carry3, lay1, lay2, tok2, save2, lse2, mixed2, mid2, hpre2, mid1, hpre1,
        name="back_two",
    )
    flat2 = lax.psum(flat2.reshape(-1), both)
    parts = passed(parts, -1, sizes)
    d_window, flat1, carry1, *parts = call(
        back_shifted_kernel,
        [SQUARE, arr(3 * (CUTS[2] - CUTS[1]), WIDE), arr(16, WIDE)] + PARTS,
        [pltpu.VMEM((1200, WIDE), F32), pltpu.VMEM((ROWS, WIDE), F32)] + BACKWARD,
        d_mid, *parts, lay1, *region, window, save1, lse1, mixed1, grads1, carry2,
        name="back_shifted",
    )
    flat1 = lax.psum(flat1.reshape(-1), both)
    parts = passed(parts, 1, sizes)
    (flat0,) = call(
        back_first_kernel,
        [arr(3 * (CUTS[1] - CUTS[0]), WIDE)],
        [pltpu.VMEM((1572, WIDE), F32), pltpu.VMEM((ROWS, WIDE), F32)] + BACKWARD,
        d_mid, d_window, *parts, tok1, lay0, lay1, merge, dense, tok0, save0, lse0, mixed0, mid0,
        hpre0, carry1,
        name="back_first",
    )
    flat0 = lax.psum(flat0.reshape(-1), both)
    gradient = jnp.concatenate([flat0, flat1, flat2, flat3])[:NPARAM]
    grad_norm = jnp.sqrt(jnp.sum(gradient * gradient))
    scale = jnp.minimum(1.0, clip_norm / (grad_norm + 1e-06))
    new_params, new_first, new_second = adamw(params, gradient, moment_one, moment_two, scale)
    return (tail[2, 0], stats[2, 0], grad_norm, new_params, new_first, new_second)


def solution(mesh):
    placed = (
        P("slab", "mp", None, None),
        P("slab", "mp", None),
        P("slab", "mp", None),
        P(),
        P(),
        P(),
    )
    sizes = (mesh.shape["slab"], mesh.shape["mp"])
    return jax.shard_map(
        functools.partial(on_device, sizes),
        mesh=mesh,
        in_specs=placed,
        out_specs=(P(), P(), P(), P(), P(), P()),
        check_vma=False,
    )
```

```python
import functools

import jax
import jax.numpy as jnp
from jax import lax
from jax.experimental import pallas as pl
from jax.experimental.pallas import tpu as pltpu
from jax.sharding import PartitionSpec as P

EMB = 96
HEADS = 6
HDIM = 16
HID = 384
MERGE = 384
CLASSES = 14
WIN = 7
SHIFT = 3
LAYERS = 3
STEP = 10

F32 = jnp.float32
BF16 = jnp.bfloat16
eps_norm = 1e-05
beta_one = 0.9
beta_two = 0.999
adam_eps = 1e-08
learn_rate = 0.05
decay_rate = 0.05
clip_norm = 0.01

VOX = WIN * WIN * WIN
ROWS = 384
BLK = 128
WIDE = 128
PLANE = WIN * WIN
FAR = WIN - SHIFT
ROWS_A = SHIFT * FAR * WIN
ROWS_B = FAR * SHIFT * WIN
ROWS_C = SHIFT * SHIFT * WIN

MERGE_ROWS = 392
LAYER_ROWS = 1165
TAP_ROWS = 27 * EMB
GROUPS = 2280
NPARAM = 872558
FLAT_ROWS = GROUPS * 3
LAYER_BASE = (98, 389, 680)
CONV_BASE = (971, 1620)
CUTS = (0, 392, 688, 976, 2280)

R_QKV, R_QKVB, R_PROJ, R_PROJB = 4, 292, 295, 391
R_HID, R_HIDB, R_OUT, R_OUTB = 392, 776, 780, 1164

VMEM = 56 * 1024 * 1024


def iota(shape, dim):
    return lax.broadcasted_iota(jnp.int32, shape, dim)


def split(x):
    hi = x.astype(BF16)
    return hi, (x - hi.astype(F32)).astype(BF16)


def pair(x):
    return jnp.concatenate(split(x), 1)


def fold(y):
    half = y.shape[1] // 2
    return y[:, :half] + y[:, half:]


def fold_rows(y):
    half = y.shape[0] // 2
    return y[:half] + y[half:]


def dot(a, b):
    return jnp.dot(a, b, preferred_element_type=F32)


def dot_nt(a, b):
    return lax.dot_general(a, b, (((1,), (1,)), ((), ())), preferred_element_type=F32)


def weight_nn(w):
    top = pair(w)
    return jnp.concatenate([top, top], 0)


def weight_nt(w):
    hi, lo = split(w)
    return jnp.concatenate(
        [jnp.concatenate([hi, hi], 1), jnp.concatenate([lo, lo], 1)], 0
    )


def mm(x, w):
    return fold(dot(pair(x), weight_nn(w)))


def mm_nt(x, w):
    return fold(dot_nt(pair(x), weight_nt(w)))


def rows_t(x):
    return jnp.concatenate(split(x.T), 0)


def mm_tn(xt, y):
    return fold_rows(fold(dot(xt, pair(y))))


def deep(w):
    return jnp.concatenate([w, jnp.zeros((WIDE - EMB, w.shape[1]), F32)], 0)


def roll(x, shift, axis):
    return pltpu.roll(x, shift, axis)


def four_to_three(y):
    lane = iota(y[0].shape, 1)
    a = jnp.where(lane < 96, y[0], roll(y[1], 96, 1))
    b = jnp.where(lane < 64, roll(y[1], 96, 1), roll(y[2], 64, 1))
    c = jnp.where(lane < 32, roll(y[2], 64, 1), roll(y[3], 32, 1))
    return a, b, c


def three_to_four(x):
    lane = iota(x[0].shape, 1)
    live = lane < EMB
    a = x[0]
    b = jnp.where(lane < 32, roll(x[0], 32, 1), roll(x[1], 32, 1))
    c = jnp.where(lane < 64, roll(x[1], 64, 1), roll(x[2], 64, 1))
    d = roll(x[2], 96, 1)
    return tuple(jnp.where(live, v, 0.0) for v in (a, b, c, d))


def hidden_rows(ref, start, count):
    return jnp.concatenate(
        four_to_three([ref[pl.ds(start + c, count, stride=4), :] for c in range(4)]), 1
    )


def put_hidden_rows(ref, start, count, x):
    parts = three_to_four([x[:, i * WIDE : (i + 1) * WIDE] for i in range(3)])
    for c in range(4):
        ref[pl.ds(start + c, count, stride=4), :] = parts[c]


def flatten(ref, start, groups, out):
    parts = four_to_three([ref[pl.ds(start + c, groups, stride=4), :] for c in range(4)])
    for c in range(3):
        out[pl.ds(c, groups, stride=3), :] = parts[c]


def norm_stats(x):
    live = iota(x.shape, 1) < EMB
    mean = jnp.sum(x, 1, keepdims=True) * (1.0 / EMB)
    centred = jnp.where(live, x - mean, 0.0)
    var = jnp.sum(centred * centred, 1, keepdims=True) * (1.0 / EMB)
    inv = lax.rsqrt(var + eps_norm)
    return centred * inv, inv


def norm(x, gain, bias):
    hat, _ = norm_stats(x)
    return hat * gain + bias


def norm_back(hat, inv, gain, grad):
    up = grad * gain
    one = jnp.sum(up, 1, keepdims=True) * (1.0 / EMB)
    two = jnp.sum(up * hat, 1, keepdims=True) * (1.0 / EMB)
    live = iota(hat.shape, 1) < EMB
    return jnp.where(live, inv * (up - one - hat * two), 0.0)


def colsum(x):
    return jnp.sum(x, 0, keepdims=True)


def gelu(x):
    return 0.5 * x * (1.0 + lax.erf(x * (0.5**0.5)))


def gelu_both(x):
    cdf = 0.5 * (1.0 + lax.erf(x * (0.5**0.5)))
    slope = cdf + x * (jnp.exp(x * x * -0.5) * 0.3989422804014327)
    return x * cdf, slope


def head_groups(x):
    lane = iota(x.shape, 1)
    swapped = roll(x, 64, 1)
    return jnp.where(lane < 64, x, swapped), jnp.where(lane < 64, swapped, x)


def as_left(x):
    both = []
    low = iota(x.shape, 1) < 64
    for part in head_groups(x):
        hi = part.astype(BF16).astype(F32)
        one = jnp.where(low, hi, part - hi).astype(BF16)
        both.append(jnp.concatenate([one, one], 1))
    return both


def as_right(x):
    return [pair(part) for part in head_groups(x)]


def head_mask(h, width):
    lane = iota((1, width), 1)
    lane = jnp.bitwise_and(lane, 63)
    low = jnp.bitwise_and(h, 3) * HDIM
    return jnp.where((lane >= low) & (lane < low + HDIM), 1.0, 0.0)


def own_lanes(h):
    lane = iota((1, WIDE), 1)
    return jnp.where((lane >= h * HDIM) & (lane < (h + 1) * HDIM), 1.0, 0.0)


def scores(q, k, h, rows, region):
    left = q * head_mask(h, 2 * WIDE).astype(BF16)
    s = dot_nt(left, k)
    if region is not None:
        region_rows, region_lanes = region
        here = region_rows[rows, 0:1]
        s = s + jnp.where(here == region_lanes[0:1, :], 0.0, -100.0)
    return jnp.where(iota(s.shape, 1) < VOX, s, -1e30)


def attention(normed, layer, save, lse, mixed, left, right, values, region=None):
    x = pair(normed)
    qkv = []
    for i in range(3):
        w = deep(layer[pl.ds(R_QKV + i, EMB, stride=3), :])
        y = fold(dot(x, weight_nn(w))) + layer[R_QKVB + i : R_QKVB + i + 1, :]
        if i == 0:
            y = y * HDIM**-0.5
        save[:, i * WIDE : (i + 1) * WIDE] = y
        qkv.append(y)
    for g, part in enumerate(as_left(qkv[0])):
        left[g] = part
    for g, part in enumerate(as_right(qkv[1])):
        right[g] = part
    v = pair(qkv[2])
    values[0:ROWS, :] = v
    values[ROWS : 2 * ROWS, :] = v
    mixed[...] = jnp.zeros_like(mixed)
    lse[...] = jnp.zeros_like(lse)

    def per_head(h, carry):
        g = lax.div(h, 4)
        lanes = own_lanes(h)
        at_h = jnp.where(iota((1, WIDE), 1) == h, 1.0, 0.0)
        for b in range(ROWS // BLK):
            rows = slice(b * BLK, (b + 1) * BLK)
            s = scores(left[g, rows, :], right[g], h, rows, region)
            top = jnp.max(s, 1, keepdims=True)
            e = jnp.exp(s - top)
            total = jnp.sum(e, 1, keepdims=True)
            o = fold(dot(pair(e), values[...]))
            mixed[rows, :] += o * (lanes / total)
            lse[rows, :] += (top + jnp.log(total)) * at_h
        return carry

    lax.fori_loop(0, HEADS, per_head, 0)
    proj = deep(layer[R_PROJ : R_PROJ + EMB, :])
    return mm(mixed[...], proj) + layer[R_PROJB : R_PROJB + 1, :]


def attention_back(grad, normed, layer, save, lse, mixed, sc, grads, at, region=None):
    left, right, gleft, vright, keys, dq, dkv_t, weights, slopes, q_t, do_t, dmix = sc
    proj = deep(layer[R_PROJ : R_PROJ + EMB, :])
    grads[at + R_PROJ : at + R_PROJ + EMB, :] = mm_tn(rows_t(mixed[...]), grad)[:EMB]
    grads[at + R_PROJB : at + R_PROJB + 1, :] = colsum(grad)
    d_mixed = mm_nt(grad, proj)
    dmix[...] = d_mixed
    q, k, v = (save[:, i * WIDE : (i + 1) * WIDE] for i in range(3))
    for g, part in enumerate(as_left(q)):
        left[g] = part
    for g, part in enumerate(as_right(k)):
        right[g] = part
    for g, part in enumerate(as_left(d_mixed)):
        gleft[g] = part
    for g, part in enumerate(as_right(v)):
        vright[g] = part
    kk = pair(k)
    keys[0:ROWS, :] = kk
    keys[ROWS : 2 * ROWS, :] = kk
    for ref, x in ((q_t, q), (do_t, d_mixed)):
        hi, lo = split(x.T)
        ref[0] = hi
        ref[1] = lo
    dq[...] = jnp.zeros_like(dq)
    dkv_t[...] = jnp.zeros_like(dkv_t)

    def per_head(h, carry):
        g = lax.div(h, 4)
        lanes = own_lanes(h)
        at_h = jnp.where(iota((1, WIDE), 1) == h, 1.0, 0.0)
        mask = head_mask(h, 2 * WIDE).astype(BF16)
        for b in range(ROWS // BLK):
            rows = slice(b * BLK, (b + 1) * BLK)
            s = scores(left[g, rows, :], right[g], h, rows, region)
            level = jnp.sum(lse[rows, :] * at_h, 1, keepdims=True)
            p = jnp.exp(s - level)
            dp = dot_nt(gleft[g, rows, :] * mask, vright[g])
            delta = jnp.sum(dmix[rows, :] * mixed[rows, :] * lanes, 1, keepdims=True)
            ds = p * (dp - delta)
            both = pair(ds)
            weights[rows, :] = pair(p)
            slopes[rows, :] = both
            dq[rows, :] += fold(dot(both, keys[...])) * lanes
        here = pl.multiple_of(h * HDIM, HDIM)
        for i, (t, m) in enumerate(((q_t, slopes), (do_t, weights))):
            lhs = jnp.concatenate([t[0, pl.ds(here, HDIM), :], t[1, pl.ds(here, HDIM), :]], 0)
            out = fold_rows(fold(dot(lhs, m[...])))
            dkv_t[i, pl.ds(here, HDIM), :] = out
        return carry

    lax.fori_loop(0, HEADS, per_head, 0)
    d_q = dq[...] * HDIM**-0.5
    d_k = dkv_t[0].T
    d_v = dkv_t[1].T
    x_t = rows_t(normed)
    d_normed = None
    for i, d in enumerate((d_q, d_k, d_v)):
        grads[pl.ds(at + R_QKV + i, EMB, stride=3), :] = mm_tn(x_t, d)[:EMB]
        grads[at + R_QKVB + i : at + R_QKVB + i + 1, :] = colsum(d)
        part = mm_nt(d, deep(layer[pl.ds(R_QKV + i, EMB, stride=3), :]))
        d_normed = part if d_normed is None else d_normed + part
    return d_normed


def mlp(middle, layer, hpre):
    normed = norm(middle, layer[2:3, :], layer[3:4, :])
    w = deep(hidden_rows(layer, R_HID, EMB))
    pre = mm(normed, w) + hidden_rows(layer, R_HIDB, 1)
    hpre[...] = pre
    out = mm(gelu(pre), layer[R_OUT : R_OUT + HID, :])
    return middle + out + layer[R_OUTB : R_OUTB + 1, :]


def mlp_back(grad, middle, hpre, layer, grads, at):
    hat, inv = norm_stats(middle)
    normed = hat * layer[2:3, :] + layer[3:4, :]
    act, slope = gelu_both(hpre[...])
    grads[at + R_OUTB : at + R_OUTB + 1, :] = colsum(grad)
    grads[at + R_OUT : at + R_OUT + HID, :] = mm_tn(rows_t(grad), act).T
    d_pre = mm_nt(grad, layer[R_OUT : R_OUT + HID, :]) * slope
    put_hidden_rows(grads, at + R_HIDB, 1, colsum(d_pre))
    put_hidden_rows(grads, at + R_HID, EMB, mm_tn(rows_t(normed), d_pre)[:EMB])
    d_normed = mm_nt(d_pre, deep(hidden_rows(layer, R_HID, EMB)))
    grads[at + 2 : at + 3, :] = colsum(d_normed * hat)
    grads[at + 3 : at + 4, :] = colsum(d_normed)
    return grad + norm_back(hat, inv, layer[2:3, :], d_normed)


def pre_norm_back(grad, tokens, layer, grads, at):
    hat, inv = norm_stats(tokens)
    grads[at : at + 1, :] = colsum(grad * hat)
    grads[at + 1 : at + 2, :] = colsum(grad)
    return norm_back(hat, inv, layer[0:1, :], grad)


def send_parts(ref, a, b, c):
    far = FAR * WIN
    near = SHIFT * WIN
    for d in range(SHIFT):
        base = d * PLANE
        c[d * near : (d + 1) * near, :] = ref[base : base + near, :]
        a[d * far : (d + 1) * far, :] = ref[base + near : base + PLANE, :]
    for d in range(FAR):
        base = (d + SHIFT) * PLANE
        b[d * near : (d + 1) * near, :] = ref[base : base + near, :]


def take_parts(own, a, b, c, out):
    far = FAR * WIN
    near = SHIFT * WIN
    for d in range(WIN):
        base = d * PLANE
        if d < SHIFT:
            out[base : base + near, :] = c[d * near : (d + 1) * near, :]
            out[base + near : base + PLANE, :] = a[d * far : (d + 1) * far, :]
        else:
            e = d - SHIFT
            out[base : base + near, :] = b[e * near : (e + 1) * near, :]
            out[base + near : base + PLANE, :] = own[base + near : base + PLANE, :]
    out[VOX:, :] = jnp.zeros((ROWS - VOX, WIDE), F32)


def prep_kernel(flat, merge, lay0, lay1, lay2, conv0, conv1):
    spans = [(0, 98)] + [(g, g + 292) for g in LAYER_BASE]
    spans += [(CONV_BASE[0], CONV_BASE[0] + 649), (CONV_BASE[1], GROUPS)]
    for out, (low, high) in zip((merge, lay0, lay1, lay2, conv0, conv1), spans):
        count = high - low
        parts = three_to_four(
            [flat[pl.ds(3 * low + c, count, stride=3), :] for c in range(3)]
        )
        for c in range(4):
            out[pl.ds(c, count, stride=4), :] = parts[c]


def offset(ref, at):
    return ref.at[pl.ds(at, ref.shape[0] - at), :]


class Rows:
    def __init__(self, ref, at):
        self.ref, self.at = ref, at

    def __getitem__(self, key):
        rows, lanes = key
        if isinstance(rows, slice):
            rows = slice(rows.start + self.at, rows.stop + self.at)
        else:
            rows = pl.ds(rows.start + self.at, rows.size, stride=rows.stride)
        return self.ref[rows, lanes]


def merged_norm(x):
    mean = jnp.sum(x, 1, keepdims=True) * (1.0 / MERGE)
    centred = x - mean
    var = jnp.sum(centred * centred, 1, keepdims=True) * (1.0 / MERGE)
    return centred * lax.rsqrt(var + eps_norm)


def first_kernel(
    feats, merge, lay0, lay1,
    dense, tok0, save, lse, mixed, middle, hpre, tok1, ahead, pa, pb, pc,
    left, right, values,
):
    dense[VOX:, :] = jnp.zeros((ROWS - VOX, MERGE), F32)
    for line in range(PLANE):
        dense[line * WIN : (line + 1) * WIN, :] = feats[line]
    hat = merged_norm(dense[...])
    normed = hat * hidden_rows(merge, 0, 1) + hidden_rows(merge, 4, 1)
    tokens = mm(normed, merge[8 : 8 + MERGE, :])
    tok0[...] = tokens
    layer = Rows(lay0, 0)
    normed = norm(tokens, layer[0:1, :], layer[1:2, :])
    attended = attention(normed, layer, save, lse, mixed, left, right, values)
    mid = tokens + attended
    middle[...] = mid
    tokens = mlp(mid, layer, hpre)
    tok1[...] = tokens
    ahead[...] = norm(tokens, lay1[1:2, :], lay1[2:3, :])
    send_parts(ahead, pa, pb, pc)


def shifted_kernel(
    own, pa, pb, pc, lay1, region_rows, region_lanes,
    window, save, lse, mixed, out, qa, qb, qc,
    left, right, values,
):
    take_parts(own, pa, pb, pc, window)
    out[...] = attention(
        window[...], Rows(lay1, 1), save, lse, mixed, left, right, values,
        (region_rows, region_lanes),
    )
    send_parts(out, qa, qb, qc)


def to_lines(ref, out):
    for line in range(PLANE):
        out[line, 0:WIN, :] = ref[line * WIN : (line + 1) * WIN, :]
        out[line, WIN:8, :] = jnp.zeros((8 - WIN, WIDE), F32)


def from_lines(ref, out):
    out[VOX:, :] = jnp.zeros((ROWS - VOX, WIDE), F32)
    for line in range(PLANE):
        out[line * WIN : (line + 1) * WIN, :] = ref[line, 0:WIN, :]


def second_kernel(
    tok1, own, qa, qb, qc, lay1, lay2,
    mid1, hpre1, tok2, save, lse, mixed, mid2, hpre2, lines,
    attended, left, right, values,
):
    take_parts(own, qa, qb, qc, attended)
    mid = tok1[...] + attended[...]
    mid1[...] = mid
    tokens = mlp(mid, Rows(lay1, 1), hpre1)
    tok2[...] = tokens
    layer = Rows(lay2, 2)
    normed = norm(tokens, layer[0:1, :], layer[1:2, :])
    mid = tokens + attention(normed, layer, save, lse, mixed, left, right, values)
    mid2[...] = mid
    attended[...] = mlp(mid, layer, hpre2)
    to_lines(attended, lines)


def grown_lines(own, low_d, high_d, low_h, high_h, out):
    out[...] = jnp.zeros_like(out)
    for d in range(WIN):
        out[d + 2, 2 : 2 + WIN] = own[d * WIN : (d + 1) * WIN]
    for d in range(2):
        out[d, 2 : 2 + WIN] = low_d[d * WIN : (d + 1) * WIN]
        out[d + 9, 2 : 2 + WIN] = high_d[d * WIN : (d + 1) * WIN]
    for d in range(11):
        out[d, 0:2] = low_h[2 * d : 2 * d + 2]
        out[d, 9:11] = high_h[2 * d : 2 * d + 2]


def taps(source, first_plane, planes, first_line, lines, out):
    def per_plane(d, carry):
        for c in range(3):
            for b in range(3):
                x = source[d + first_plane, first_line + b : first_line + b + lines]
                if c != 1:
                    x = roll(x, 1 if c == 0 else 7, 1)
                x = pair(x.reshape(lines * 8, WIDE))
                at = pl.multiple_of(d * (lines * 8), lines * 8)
                t = b * 3 + c
                out[pl.ds(at, lines * 8), t * 256 : (t + 1) * 256] = x
        return carry

    lax.fori_loop(0, planes, per_plane, 0)


def tap_weights(ref, at, out):
    def per_tap(i, carry):
        w = deep(ref[pl.ds(i * EMB + at, EMB), :])
        out[pl.ds(pl.multiple_of(i * 256, 256), 256), :] = weight_nn(w)
        return carry

    lax.fori_loop(0, 27, per_tap, 0)


def tap_weights_back(ref, at, out):
    def per_tap(i, carry):
        w = deep(ref[pl.ds((26 - i) * EMB + at, EMB), :]).T
        out[pl.ds(pl.multiple_of(i * 256, 256), 256), :] = weight_nn(w)
        return carry

    lax.fori_loop(0, 27, per_tap, 0)


def conv(side, weights, planes, pitch, at_once, put):
    rows = at_once * pitch
    for start in range(0, planes, at_once):
        total = None
        for a in range(3):
            low = (start + a) * pitch
            part = dot(side[low : low + rows, :], weights[a * 2304 : (a + 1) * 2304, :])
            total = part if total is None else total + part
        put(start, fold(total))


def conv_weight_grad(side, grad_rows, pitch, out, at):
    rows = 512
    g = jnp.concatenate([grad_rows, jnp.zeros((rows - grad_rows.shape[0], WIDE), F32)], 0)
    left = rows_t(g)
    for a in range(3):
        for bc in range(9):
            y = dot(left, side[a * pitch : a * pitch + rows, bc * 256 : (bc + 1) * 256])
            y = fold_rows(fold(y)).T
            t = a * 9 + bc
            out[at + t * EMB : at + (t + 1) * EMB, :] = y[:EMB]


def volume_mask(ends, planes, lines, reach, real_lines):
    shape = (planes, lines, 8, WIDE)
    d, h, w = iota(shape, 0), iota(shape, 1), iota(shape, 2)
    low_d = jnp.where(ends[0] == 1, reach, 0)
    high_d = jnp.where(ends[1] == 1, planes - reach, planes)
    low_h = jnp.where(ends[2] == 1, reach, 0)
    high_h = jnp.where(ends[3] == 1, real_lines - reach, real_lines)
    inside = (d >= low_d) & (d < high_d) & (h >= low_h) & (h < high_h) & (w < WIN)
    return jnp.where(inside, 1.0, 0.0)


def conv_kernel(
    ends, own, low_d, high_d, low_h, high_h, marks, conv0, conv1,
    grown, pre, tok, stats,
    act, side, side_own, weights,
):
    grown_lines(own, low_d, high_d, low_h, high_h, grown)
    tap_weights(conv0, 3, weights)
    taps(grown, 0, 11, 0, 10, side)
    bias0 = conv0[3 + TAP_ROWS : 4 + TAP_ROWS, :]
    inside = volume_mask(ends, 9, 10, 1, 9)

    def put(start, y):
        z = (y + bias0).reshape(3, 10, 8, WIDE)
        pre[start : start + 3] = z
        act[start : start + 3] = gelu(z) * inside[start : start + 3]

    conv(side, weights, 9, 80, 3, put)
    tap_weights(conv1, 0, weights)
    taps(act, 0, 9, 0, 8, side_own)
    bias1 = conv1[TAP_ROWS : TAP_ROWS + 1, :]
    sums = []

    def put_own(start, y):
        y = (y + bias1).reshape(WIN, 8, 8, WIDE)[:, 0:WIN]
        y = y + own[...].reshape(WIN, WIN, 8, WIDE)
        y = jnp.where(iota(y.shape, 2) < WIN, y, 0.0).reshape(PLANE, 8, WIDE)
        tok[...] = y + marks[...]
        flat = y.reshape(PLANE * 8, WIDE)
        sums.append(colsum(flat))
        sums.append(colsum(flat * flat))

    conv(side_own, weights, WIN, 64, WIN, put_own)
    count = jnp.sum(marks[...].reshape(PLANE * 8, WIDE))
    row = iota((8, WIDE), 0)
    stats[...] = (
        jnp.where(row == 0, sums[0], 0.0)
        + jnp.where(row == 1, sums[1], 0.0)
        + jnp.where(row == 2, count, 0.0)
    )


def head_kernel(
    own, low_d, high_d, low_h, high_h, all_sums, conv1, head_w, head_b, voxels,
    grown, slope_out, stats, d_head, d_rows, sums,
):
    sums[...] = jnp.sum(all_sums[...].reshape(-1, 8, WIDE), 0)
    grown_lines(own, low_d, high_d, low_h, high_h, grown)
    rows = 11 * 12 * 8
    both = grown[...].reshape(rows, WIDE)
    lane = iota((rows, WIDE), 1)
    tokens = jnp.where(lane < EMB, both, 0.0)
    target = jnp.where(lane < CLASSES, roll(both, WIDE - EMB, 1), 0.0)
    live = jnp.sum(target, 1, keepdims=True)
    count = voxels[0]
    average = sums[0:1, :] / count
    spread = sums[1:2, :] / count - average * average
    inv = lax.rsqrt(spread + eps_norm)
    gain = conv1[TAP_ROWS + 1 : TAP_ROWS + 2, :]
    bias = conv1[TAP_ROWS + 2 : TAP_ROWS + 3, :]
    hat = (tokens - average) * inv
    act, slope = gelu_both(hat * gain + bias)
    w = head_w[...]
    logits = mm(act, w) + head_b[0:1, :]
    logits = jnp.where(lane < CLASSES, logits, -1e30)
    top = jnp.max(logits, 1, keepdims=True)
    e = jnp.exp(logits - top)
    total = jnp.sum(e, 1, keepdims=True)
    logp = logits - top - jnp.log(total)
    scale = 1.0 / sums[2:3, 0:1]
    d_logits = (e / total * live - target) * scale
    d_normed = mm_nt(d_logits, w) * slope
    d_tokens = d_normed * gain * inv
    slope_out[...] = d_tokens.reshape(11, 12, 8, WIDE)

    def own_rows(x):
        x = x.reshape(11, 12, 8, WIDE)[2:9, 2:9]
        x = jnp.where(iota(x.shape, 2) < WIN, x, 0.0)
        return x.reshape(PLANE * 8, WIDE)

    loss = -jnp.sum(own_rows(target * jnp.where(lane < CLASSES, logp, 0.0)))
    own_d = own_rows(d_logits)
    own_n = own_rows(d_normed)
    own_hat = own_rows(hat)
    zeros = jnp.zeros((512 - PLANE * 8, WIDE), F32)
    left = rows_t(jnp.concatenate([own_d, zeros], 0))
    d_head[...] = mm_tn(left, jnp.concatenate([own_rows(act), zeros], 0)).T
    d_gain = colsum(own_n * own_hat)
    d_bias = colsum(own_n)
    d_average = -d_bias * gain * inv
    d_spread = d_gain * gain * inv * inv * -0.5
    d_two = d_spread / count
    d_one = (d_average - 2.0 * average * d_spread) / count
    row = iota((8, WIDE), 0)
    live_lane = iota((8, WIDE), 1) < EMB
    stats[...] = (
        jnp.where((row == 0) & live_lane, d_one, 0.0)
        + jnp.where((row == 1) & live_lane, d_two, 0.0)
        + jnp.where(row == 2, loss, 0.0)
    )
    d_rows[...] = (
        jnp.where(row == 0, d_gain, 0.0)
        + jnp.where(row == 1, d_bias, 0.0)
        + jnp.where(row == 2, colsum(own_d), 0.0)
    )


def conv_back_kernel(
    ends, tok, slope, sums, grown, pre, conv0, conv1, d_rows, d_head,
    d_own, flat, carry,
    grads, dgrown, act, side, side_own, weights,
):
    lane = iota((11, 12, 8, WIDE), 3)
    inside = volume_mask(ends, 11, 12, 2, 11)
    steady = sums[0:1, :].reshape(1, 1, 1, WIDE)
    rising = 2.0 * sums[1:2, :].reshape(1, 1, 1, WIDE)
    d_tok = slope[...] + jnp.where(lane < EMB, (steady + tok[...] * rising) * inside, 0.0)
    dgrown[...] = d_tok
    grads[5208:, :] = jnp.zeros((28, WIDE), F32)
    grads[0:8, :] = jnp.zeros((8, WIDE), F32)
    grads[5189:5191, :] = d_rows[0:2, :]
    grads[5191:5208, :] = d_head[0:17, :]
    own = dgrown[2:9, 2:10]
    line = iota(own.shape, 1)
    own = jnp.where(line < WIN, own, 0.0).reshape(WIN * 64, WIDE)
    grads[5188:5189, :] = colsum(own)

    near = volume_mask(ends, 9, 10, 1, 9)
    act[0:9] = gelu(pre[...]) * near
    act[9:10] = jnp.zeros((1, 10, 8, WIDE), F32)
    taps(act, 0, 10, 0, 8, side_own)
    conv_weight_grad(side_own, own, 64, grads, 2596)
    tap_weights_back(conv1, 0, weights)
    taps(dgrown, 0, 11, 0, 10, side)

    def put(start, y):
        _, s = gelu_both(pre[start : start + 3])
        z = y.reshape(3, 10, 8, WIDE) * s * near[start : start + 3]
        act[start : start + 3] = z

    conv(side, weights, 9, 80, 3, put)

    own = act[1:8, 1:9]
    line = iota(own.shape, 1)
    own = jnp.where(line < WIN, own, 0.0).reshape(WIN * 64, WIDE)
    grads[2595:2596, :] = colsum(own)
    taps(grown, 1, 10, 1, 8, side_own)
    conv_weight_grad(side_own, own, 64, grads, 3)
    carry[...] = grads[0:24, :]
    flatten(grads, 20, GROUPS - CUTS[3], flat)
    flat[3912:, :] = jnp.zeros((4096 - 3912, WIDE), F32)
    tap_weights_back(conv0, 3, weights)
    taps(act, 0, 9, 0, 8, side_own)

    def put_own(start, y):
        y = y.reshape(WIN, 8, 8, WIDE)[:, 0:WIN] + dgrown[2:9, 2:9]
        y = jnp.where(iota(y.shape, 2) < WIN, y, 0.0)
        d_own[...] = y.reshape(PLANE, 8, WIDE)

    conv(side_own, weights, WIN, 64, WIN, put_own)


def back_two_kernel(
    d_own, carry, lay1, lay2, tok2, save, lse, mixed, mid2, hpre2, mid1, hpre1,
    d_mid, grads1, flat, carry2, pa, pb, pc,
    grads, dense, *sc,
):
    from_lines(d_own, dense)
    layer = Rows(lay2, 2)
    grads[0:8, :] = jnp.zeros((8, WIDE), F32)
    d = mlp_back(dense[...], mid2[...], hpre2, layer, grads, 2)
    tokens = tok2[...]
    normed = norm(tokens, layer[0:1, :], layer[1:2, :])
    d_normed = attention_back(d, normed, layer, save, lse, mixed, sc, grads, 2)
    d = d + pre_norm_back(d_normed, tokens, layer, grads, 2)
    grads[1167:1184, :] = carry[3:20, :]
    flatten(grads, 32, CUTS[3] - CUTS[2], flat)
    carry2[...] = grads[0:32, :]
    layer = Rows(lay1, 1)
    d = mlp_back(d, mid1[...], hpre1, layer, grads1, 1)
    d_mid[...] = d
    send_parts(d_mid, pa, pb, pc)


def back_shifted_kernel(
    own, pa, pb, pc, lay1, region_rows, region_lanes, window, save, lse, mixed, grads1, carry2,
    d_window, flat, carry1, qa, qb, qc,
    grads, grad, *sc,
):
    take_parts(own, pa, pb, pc, grad)
    grads[0:1168, :] = grads1[...]
    grads[0:3, :] = jnp.zeros((3, WIDE), F32)
    d_window[...] = attention_back(
        grad[...], window[...], Rows(lay1, 1), save, lse, mixed, sc, grads, 1,
        (region_rows, region_lanes),
    )
    send_parts(d_window, qa, qb, qc)
    grads[1166:1196, :] = carry2[2:32, :]
    flatten(grads, 12, CUTS[2] - CUTS[1], flat)
    carry1[...] = grads[0:16, :]


def back_first_kernel(
    d_mid, own, qa, qb, qc, tok1, lay0, lay1, merge, dense, tok0, save, lse, mixed, middle, hpre, carry1,
    flat,
    grads, grad, *sc,
):
    take_parts(own, qa, qb, qc, grad)
    grads[1556:1572, :] = carry1[...]
    d = d_mid[...] + pre_norm_back(grad[...], tok1[...], Rows(lay1, 1), grads, 1557)
    layer = Rows(lay0, 0)
    at = MERGE_ROWS
    d = mlp_back(d, middle[...], hpre, layer, grads, at)
    tokens = tok0[...]
    normed = norm(tokens, layer[0:1, :], layer[1:2, :])
    d_normed = attention_back(d, normed, layer, save, lse, mixed, sc, grads, at)
    d = d + pre_norm_back(d_normed, tokens, layer, grads, at)
    live = iota((ROWS, WIDE), 0) < VOX
    d = jnp.where(live, d, 0.0)
    hat = merged_norm(dense[...])
    gain = hidden_rows(merge, 0, 1)
    bias = hidden_rows(merge, 4, 1)
    w = merge[8 : 8 + MERGE, :]
    put_hidden_rows(grads, 8 - 8, 1, jnp.zeros((1, MERGE), F32))
    grads[8 : 8 + MERGE, :] = mm_tn(rows_t(d), hat * gain + bias).T
    d_hat = mm_nt(d, w)
    put_hidden_rows(grads, 0, 1, colsum(d_hat * hat))
    put_hidden_rows(grads, 4, 1, colsum(d_hat))
    flatten(grads, 0, CUTS[1], flat)
    flat[1176:, :] = jnp.zeros((8, WIDE), F32)


def arr(*shape):
    return jax.ShapeDtypeStruct(shape, F32)


def call(kernel, outs, scratch, *args, scalars=0, name=None):
    smem = pl.BlockSpec(memory_space=pltpu.SMEM)
    vmem = pl.BlockSpec(memory_space=pltpu.VMEM)
    specs = [smem if a.size <= 8 and a.ndim == 1 else vmem for a in args]
    return pl.pallas_call(
        kernel,
        out_shape=list(outs),
        in_specs=specs,
        out_specs=[vmem] * len(outs),
        scratch_shapes=list(scratch),
        compiler_params=pltpu.CompilerParams(vmem_limit_bytes=VMEM),
        name=name,
    )(*args)


SQUARE = arr(ROWS, WIDE)
SAVE = arr(ROWS, 3 * WIDE)
FORWARD = [
    pltpu.VMEM((2, ROWS, 2 * WIDE), BF16),
    pltpu.VMEM((2, ROWS, 2 * WIDE), BF16),
    pltpu.VMEM((2 * ROWS, 2 * WIDE), BF16),
]
BACKWARD = [
    pltpu.VMEM((2, ROWS, 2 * WIDE), BF16),
    pltpu.VMEM((2, ROWS, 2 * WIDE), BF16),
    pltpu.VMEM((2, ROWS, 2 * WIDE), BF16),
    pltpu.VMEM((2, ROWS, 2 * WIDE), BF16),
    pltpu.VMEM((2 * ROWS, 2 * WIDE), BF16),
    pltpu.VMEM((ROWS, WIDE), F32),
    pltpu.VMEM((2, WIDE, ROWS), F32),
    pltpu.VMEM((ROWS, 2 * ROWS), BF16),
    pltpu.VMEM((ROWS, 2 * ROWS), BF16),
    pltpu.VMEM((2, WIDE, ROWS), BF16),
    pltpu.VMEM((2, WIDE, ROWS), BF16),
    pltpu.VMEM((ROWS, WIDE), F32),
]
PARTS = [arr(ROWS_A, WIDE), arr(ROWS_B, WIDE), arr(ROWS_C, WIDE)]


def passed(parts, steps, sizes):
    slabs, rows = sizes
    moved = []
    for part, (ds, dm) in zip(parts, ((1, 0), (0, 1), (1, 1))):
        pairs = []
        for s in range(slabs):
            for m in range(rows):
                target = ((s + steps * ds) % slabs) * rows + (m + steps * dm) % rows
                pairs.append((s * rows + m, target))
        moved.append(lax.ppermute(part, ("slab", "mp"), pairs))
    return moved


def beside(lines, sizes):
    slabs, rows = sizes
    up = [(i, i + 1) for i in range(slabs - 1)]
    down = [(i + 1, i) for i in range(slabs - 1)]
    low_d = lax.ppermute(lines[(WIN - 2) * WIN :], "slab", up)
    high_d = lax.ppermute(lines[: 2 * WIN], "slab", down)
    column = jnp.concatenate([low_d, lines, high_d], 0).reshape(11, WIN, 8, WIDE)
    first = column[:, 0:2].reshape(22, 8, WIDE)
    last = column[:, WIN - 2 :].reshape(22, 8, WIDE)
    up = [(i, i + 1) for i in range(rows - 1)]
    down = [(i + 1, i) for i in range(rows - 1)]
    low_h = lax.ppermute(last, "mp", up)
    high_h = lax.ppermute(first, "mp", down)
    return low_d, high_d, low_h, high_h


def window_regions(slab, row, sizes):
    def part_of(places, length):
        return jnp.where(places < length - WIN, 0, jnp.where(places < length - SHIFT, 1, 2))

    turned = (jnp.arange(WIN, dtype=jnp.int32) + FAR) % WIN
    depth = part_of(slab * WIN + turned, WIN * sizes[0])
    height = part_of(row * WIN + turned, WIN * sizes[1])
    breadth = part_of(turned, WIN)
    ids = depth[:, None, None] * 9 + height[None, :, None] * 3 + breadth[None, None, :]
    ids = jnp.pad(ids.reshape(VOX).astype(F32), (0, ROWS - VOX))
    return jnp.broadcast_to(ids[:, None], (ROWS, WIDE)), jnp.broadcast_to(ids[None], (8, ROWS))


def exchanged_sum(value, axis, size):
    step = 1
    while step < size:
        radix = 4 if size // step >= 4 else 2
        got = [value]
        for k in range(1, radix):
            pairs = [(i, i ^ (k * step)) for i in range(size)]
            got.append(lax.ppermute(value, axis, pairs))
        while len(got) > 1:
            got = [got[i] + got[i + 1] for i in range(0, len(got), 2)]
        value = got[0]
        step *= radix
    return value


def adamw(param, grad, first, second, scale):
    grad = grad * scale
    first = beta_one * first + (1.0 - beta_one) * grad
    second = beta_two * second + (1.0 - beta_two) * grad * grad
    first_hat = first / (1.0 - beta_one**STEP)
    second_hat = second / (1.0 - beta_two**STEP)
    param = param - learn_rate * (
        first_hat / (jnp.sqrt(second_hat) + adam_eps) + decay_rate * param
    )
    return (param, first, second)


def on_device(sizes, feats, labels, valid, params, moment_one, moment_two):
    slabs, rows = sizes
    slab, row = lax.axis_index("slab"), lax.axis_index("mp")
    both = ("slab", "mp")
    ends = jnp.stack([slab == 0, slab == slabs - 1, row == 0, row == rows - 1]).astype(jnp.int32)
    region = window_regions(slab, row, sizes)
    voxels = jnp.full((1,), WIN * slabs * WIN * rows * WIN, F32)

    flat = jnp.pad(params, (0, FLAT_ROWS * WIDE - NPARAM)).reshape(FLAT_ROWS, WIDE)
    merge, lay0, lay1, lay2, conv0, conv1 = call(
        prep_kernel,
        [arr(MERGE_ROWS, WIDE)] + [arr(1168, WIDE)] * 3 + [arr(2596, WIDE), arr(2640, WIDE)],
        [],
        flat,
        name="prep",
    )
    head = params[NPARAM - CLASSES * (EMB + 1) :]
    head_w = jnp.pad(
        head[: EMB * CLASSES].reshape(EMB, CLASSES), ((0, WIDE - EMB), (0, WIDE - CLASSES))
    )
    head_b = jnp.broadcast_to(jnp.pad(head[EMB * CLASSES :], (0, WIDE - CLASSES)), (8, WIDE))
    classes = jnp.arange(WIDE, dtype=jnp.int32) - EMB
    marks = (labels[..., None] == classes).astype(F32) * valid.astype(F32)[..., None]
    marks = jnp.pad(marks, ((0, 0), (0, 0), (0, 1), (0, 0))).reshape(PLANE, 8, WIDE)

    dense, tok0, save0, lse0, mixed0, mid0, hpre0, tok1, ahead, *parts = call(
        first_kernel,
        [arr(ROWS, MERGE), SQUARE, SAVE, SQUARE, SQUARE, SQUARE, arr(ROWS, HID), SQUARE, SQUARE]
        + PARTS,
        FORWARD,
        feats.reshape(PLANE, WIN, MERGE), merge, lay0, lay1,
        name="first",
    )
    parts = passed(parts, -1, sizes)
    window, save1, lse1, mixed1, out1, *parts = call(
        shifted_kernel,
        [SQUARE, SAVE, SQUARE, SQUARE, SQUARE] + PARTS,
        FORWARD,
        ahead, *parts, lay1, *region,
        name="shifted",
    )
    parts = passed(parts, 1, sizes)
    mid1, hpre1, tok2, save2, lse2, mixed2, mid2, hpre2, lines = call(
        second_kernel,
        [SQUARE, arr(ROWS, HID), SQUARE, SAVE, SQUARE, SQUARE, SQUARE, arr(ROWS, HID)]
        + [arr(PLANE, 8, WIDE)],
        [pltpu.VMEM((ROWS, WIDE), F32)] + FORWARD,
        tok1, out1, *parts, lay1, lay2,
        name="second",
    )
    near = beside(lines, sizes)
    grown, pre, tok3, stats = call(
        conv_kernel,
        [arr(11, 12, 8, WIDE), arr(9, 10, 8, WIDE), arr(PLANE, 8, WIDE), arr(8, WIDE)],
        [
            pltpu.VMEM((9, 10, 8, WIDE), F32),
            pltpu.VMEM((880, 2304), BF16),
            pltpu.VMEM((576, 2304), BF16),
            pltpu.VMEM((27 * 256, 256), BF16),
        ],
        ends, lines, *near, marks, conv0, conv1,
        name="conv",
    )
    near = beside(tok3, sizes)
    stats = lax.all_gather(stats, both, axis=0, tiled=True)
    tok3, slope, tail, d_head, d_rows, stats = call(
        head_kernel,
        [arr(11, 12, 8, WIDE), arr(11, 12, 8, WIDE), arr(8, WIDE), arr(WIDE, WIDE), arr(8, WIDE)]
        + [arr(8, WIDE)],
        [],
        tok3, *near, stats, conv1, head_w, head_b, voxels,
        name="head",
    )
    d_head = jnp.concatenate([d_head[:EMB, :CLASSES].reshape(-1), d_rows[2, :CLASSES]])
    d_head = jnp.pad(d_head, (0, 24 * EMB - CLASSES * (EMB + 1))).reshape(24, EMB)
    d_head = jnp.pad(d_head, ((0, 0), (0, WIDE - EMB)))
    tail = exchanged_sum(exchanged_sum(tail, "mp", rows), "slab", slabs)
    d_own, flat3, carry3 = call(
        conv_back_kernel,
        [arr(PLANE, 8, WIDE), arr(4096, WIDE), arr(24, WIDE)],
        [
            pltpu.VMEM((5236, WIDE), F32),
            pltpu.VMEM((11, 12, 8, WIDE), F32),
            pltpu.VMEM((10, 10, 8, WIDE), F32),
            pltpu.VMEM((880, 2304), BF16),
            pltpu.VMEM((640, 2304), BF16),
            pltpu.VMEM((27 * 256, 256), BF16),
        ],
        ends, tok3, slope, tail, grown, pre, conv0, conv1, d_rows, d_head,
        name="conv_back",
    )
    flat3 = lax.psum_scatter(flat3, both, scatter_dimension=0, tiled=True)
    flat3 = lax.all_gather(flat3, both, axis=0, tiled=True)
    d_mid, grads1, flat2, carry2, *parts = call(
        back_two_kernel,
        [SQUARE, arr(1168, WIDE), arr(3 * (CUTS[3] - CUTS[2]), WIDE), arr(32, WIDE)] + PARTS,
        [pltpu.VMEM((1184, WIDE), F32), pltpu.VMEM((ROWS, WIDE), F32)] + BACKWARD,
        d_own, carry3, lay1, lay2, tok2, save2, lse2, mixed2, mid2, hpre2, mid1, hpre1,
        name="back_two",
    )
    flat2 = lax.psum(flat2, both)
    parts = passed(parts, -1, sizes)
    d_window, flat1, carry1, *parts = call(
        back_shifted_kernel,
        [SQUARE, arr(3 * (CUTS[2] - CUTS[1]), WIDE), arr(16, WIDE)] + PARTS,
        [pltpu.VMEM((1200, WIDE), F32), pltpu.VMEM((ROWS, WIDE), F32)] + BACKWARD,
        d_mid, *parts, lay1, *region, window, save1, lse1, mixed1, grads1, carry2,
        name="back_shifted",
    )
    flat1 = lax.psum(flat1, both)
    parts = passed(parts, 1, sizes)
    (flat0,) = call(
        back_first_kernel,
        [arr(1184, WIDE)],
        [pltpu.VMEM((1572, WIDE), F32), pltpu.VMEM((ROWS, WIDE), F32)] + BACKWARD,
        d_mid, d_window, *parts, tok1, lay0, lay1, merge, dense, tok0, save0, lse0, mixed0, mid0,
        hpre0, carry1,
        name="back_first",
    )
    flat0 = lax.psum_scatter(flat0, "mp", scatter_dimension=0, tiled=True)
    flat0 = lax.psum(flat0, "slab")
    flat0 = lax.all_gather(flat0, "mp", axis=0, tiled=True)
    gradient = jnp.concatenate([flat0[:1176], flat1, flat2, flat3[:3912]], 0)
    gradient = gradient.reshape(-1)[:NPARAM]
    grad_norm = jnp.sqrt(jnp.sum(gradient * gradient))
    scale = jnp.minimum(1.0, clip_norm / (grad_norm + 1e-06))
    new_params, new_first, new_second = adamw(params, gradient, moment_one, moment_two, scale)
    return (tail[2, 0], stats[2, 0], grad_norm, new_params, new_first, new_second)


def solution(mesh):
    placed = (
        P("slab", "mp", None, None),
        P("slab", "mp", None),
        P("slab", "mp", None),
        P(),
        P(),
        P(),
    )
    sizes = (mesh.shape["slab"], mesh.shape["mp"])
    return jax.shard_map(
        functools.partial(on_device, sizes),
        mesh=mesh,
        in_specs=placed,
        out_specs=(P(), P(), P(), P(), P(), P()),
        check_vma=False,
    )
```

```python
import functools

import jax
import jax.numpy as jnp
from jax import lax
from jax.experimental import pallas as pl
from jax.experimental.pallas import tpu as pltpu
from jax.sharding import PartitionSpec as P

EMB = 96
HEADS = 6
HDIM = 16
HID = 384
MERGE = 384
CLASSES = 14
WIN = 7
SHIFT = 3
LAYERS = 3
STEP = 10

F32 = jnp.float32
BF16 = jnp.bfloat16
eps_norm = 1e-05
beta_one = 0.9
beta_two = 0.999
adam_eps = 1e-08
learn_rate = 0.05
decay_rate = 0.05
clip_norm = 0.01

VOX = WIN * WIN * WIN
ROWS = 384
BLK = 128
WIDE = 128
PLANE = WIN * WIN
FAR = WIN - SHIFT
ROWS_A = SHIFT * FAR * WIN
ROWS_B = FAR * SHIFT * WIN
ROWS_C = SHIFT * SHIFT * WIN

MERGE_ROWS = 392
LAYER_ROWS = 1165
TAP_ROWS = 27 * EMB
GROUPS = 2280
NPARAM = 872558
HEAD_ROW = 6806
HEAD_ROWS = 11
HEAD_LANE = 32
LATE_ROWS = 3072
EARLY_ROWS = 3840
LAYER_BASE = (98, 389, 680)
CONV_BASE = (971, 1620)
CUTS = (0, 392, 688, 976, 2280)

R_QKV, R_QKVB, R_PROJ, R_PROJB = 4, 292, 295, 391
R_HID, R_HIDB, R_OUT, R_OUTB = 392, 776, 780, 1164

VMEM = 56 * 1024 * 1024


def iota(shape, dim):
    return lax.broadcasted_iota(jnp.int32, shape, dim)


def split(x):
    hi = x.astype(BF16)
    return hi, (x - hi.astype(F32)).astype(BF16)


def pair(x):
    return jnp.concatenate(split(x), 1)


def fold(y):
    half = y.shape[1] // 2
    return y[:, :half] + y[:, half:]


def fold_rows(y):
    half = y.shape[0] // 2
    return y[:half] + y[half:]


def dot(a, b):
    return jnp.dot(a, b, preferred_element_type=F32)


def dot_nt(a, b):
    return lax.dot_general(a, b, (((1,), (1,)), ((), ())), preferred_element_type=F32)


def weight_nn(w):
    top = pair(w)
    return jnp.concatenate([top, top], 0)


def weight_nt(w):
    hi, lo = split(w)
    return jnp.concatenate(
        [jnp.concatenate([hi, hi], 1), jnp.concatenate([lo, lo], 1)], 0
    )


def mm(x, w):
    return fold(dot(pair(x), weight_nn(w)))


def mm_nt(x, w):
    return fold(dot_nt(pair(x), weight_nt(w)))


def rows_t(x):
    return jnp.concatenate(split(x.T), 0)


def mm_tn(xt, y):
    return fold_rows(fold(dot(xt, pair(y))))


def deep(w):
    return jnp.concatenate([w, jnp.zeros((WIDE - EMB, w.shape[1]), F32)], 0)


def roll(x, shift, axis):
    return pltpu.roll(x, shift, axis)


def four_to_three(y):
    lane = iota(y[0].shape, 1)
    a = jnp.where(lane < 96, y[0], roll(y[1], 96, 1))
    b = jnp.where(lane < 64, roll(y[1], 96, 1), roll(y[2], 64, 1))
    c = jnp.where(lane < 32, roll(y[2], 64, 1), roll(y[3], 32, 1))
    return a, b, c


def three_to_four(x):
    lane = iota(x[0].shape, 1)
    live = lane < EMB
    a = x[0]
    b = jnp.where(lane < 32, roll(x[0], 32, 1), roll(x[1], 32, 1))
    c = jnp.where(lane < 64, roll(x[1], 64, 1), roll(x[2], 64, 1))
    d = roll(x[2], 96, 1)
    return tuple(jnp.where(live, v, 0.0) for v in (a, b, c, d))


def hidden_rows(ref, start, count):
    return jnp.concatenate(
        four_to_three([ref[pl.ds(start + c, count, stride=4), :] for c in range(4)]), 1
    )


def put_hidden_rows(ref, start, count, x):
    parts = three_to_four([x[:, i * WIDE : (i + 1) * WIDE] for i in range(3)])
    for c in range(4):
        ref[pl.ds(start + c, count, stride=4), :] = parts[c]


def flatten(ref, start, groups, out):
    parts = four_to_three([ref[pl.ds(start + c, groups, stride=4), :] for c in range(4)])
    for c in range(3):
        out[pl.ds(c, groups, stride=3), :] = parts[c]


def norm_stats(x):
    live = iota(x.shape, 1) < EMB
    mean = jnp.sum(x, 1, keepdims=True) * (1.0 / EMB)
    centred = jnp.where(live, x - mean, 0.0)
    var = jnp.sum(centred * centred, 1, keepdims=True) * (1.0 / EMB)
    inv = lax.rsqrt(var + eps_norm)
    return centred * inv, inv


def norm(x, gain, bias):
    hat, _ = norm_stats(x)
    return hat * gain + bias


def norm_back(hat, inv, gain, grad):
    up = grad * gain
    one = jnp.sum(up, 1, keepdims=True) * (1.0 / EMB)
    two = jnp.sum(up * hat, 1, keepdims=True) * (1.0 / EMB)
    live = iota(hat.shape, 1) < EMB
    return jnp.where(live, inv * (up - one - hat * two), 0.0)


def colsum(x):
    return jnp.sum(x, 0, keepdims=True)


def gelu(x):
    return 0.5 * x * (1.0 + lax.erf(x * (0.5**0.5)))


def gelu_both(x):
    cdf = 0.5 * (1.0 + lax.erf(x * (0.5**0.5)))
    slope = cdf + x * (jnp.exp(x * x * -0.5) * 0.3989422804014327)
    return x * cdf, slope


def head_groups(x):
    lane = iota(x.shape, 1)
    swapped = roll(x, 64, 1)
    return jnp.where(lane < 64, x, swapped), jnp.where(lane < 64, swapped, x)


def as_left(x):
    both = []
    low = iota(x.shape, 1) < 64
    for part in head_groups(x):
        hi = part.astype(BF16).astype(F32)
        one = jnp.where(low, hi, part - hi).astype(BF16)
        both.append(jnp.concatenate([one, one], 1))
    return both


def as_right(x):
    return [pair(part) for part in head_groups(x)]


def head_mask(h, width):
    lane = iota((1, width), 1)
    lane = jnp.bitwise_and(lane, 63)
    low = jnp.bitwise_and(h, 3) * HDIM
    return jnp.where((lane >= low) & (lane < low + HDIM), 1.0, 0.0)


def own_lanes(h):
    lane = iota((1, WIDE), 1)
    return jnp.where((lane >= h * HDIM) & (lane < (h + 1) * HDIM), 1.0, 0.0)


def scores(q, k, h, rows, region):
    left = q * head_mask(h, 2 * WIDE).astype(BF16)
    s = dot_nt(left, k)
    if region is not None:
        region_rows, region_lanes = region
        here = region_rows[rows, 0:1]
        s = s + jnp.where(here == region_lanes[0:1, :], 0.0, -100.0)
    return jnp.where(iota(s.shape, 1) < VOX, s, -1e30)


def attention(normed, layer, save, lse, mixed, left, right, values, region=None):
    x = pair(normed)
    qkv = []
    for i in range(3):
        w = deep(layer[pl.ds(R_QKV + i, EMB, stride=3), :])
        y = fold(dot(x, weight_nn(w))) + layer[R_QKVB + i : R_QKVB + i + 1, :]
        if i == 0:
            y = y * HDIM**-0.5
        save[:, i * WIDE : (i + 1) * WIDE] = y
        qkv.append(y)
    for g, part in enumerate(as_left(qkv[0])):
        left[g] = part
    for g, part in enumerate(as_right(qkv[1])):
        right[g] = part
    v = pair(qkv[2])
    values[0:ROWS, :] = v
    values[ROWS : 2 * ROWS, :] = v
    mixed[...] = jnp.zeros_like(mixed)
    lse[...] = jnp.zeros_like(lse)

    def per_head(h, carry):
        g = lax.div(h, 4)
        lanes = own_lanes(h)
        at_h = jnp.where(iota((1, WIDE), 1) == h, 1.0, 0.0)
        for b in range(ROWS // BLK):
            rows = slice(b * BLK, (b + 1) * BLK)
            s = scores(left[g, rows, :], right[g], h, rows, region)
            top = jnp.max(s, 1, keepdims=True)
            e = jnp.exp(s - top)
            total = jnp.sum(e, 1, keepdims=True)
            o = fold(dot(pair(e), values[...]))
            mixed[rows, :] += o * (lanes / total)
            lse[rows, :] += (top + jnp.log(total)) * at_h
        return carry

    lax.fori_loop(0, HEADS, per_head, 0)
    proj = deep(layer[R_PROJ : R_PROJ + EMB, :])
    return mm(mixed[...], proj) + layer[R_PROJB : R_PROJB + 1, :]


def attention_back(grad, normed, layer, save, lse, mixed, sc, grads, at, region=None):
    left, right, gleft, vright, keys, dq, dkv_t, weights, slopes, q_t, do_t, dmix = sc
    proj = deep(layer[R_PROJ : R_PROJ + EMB, :])
    grads[at + R_PROJ : at + R_PROJ + EMB, :] = mm_tn(rows_t(mixed[...]), grad)[:EMB]
    grads[at + R_PROJB : at + R_PROJB + 1, :] = colsum(grad)
    d_mixed = mm_nt(grad, proj)
    dmix[...] = d_mixed
    q, k, v = (save[:, i * WIDE : (i + 1) * WIDE] for i in range(3))
    for g, part in enumerate(as_left(q)):
        left[g] = part
    for g, part in enumerate(as_right(k)):
        right[g] = part
    for g, part in enumerate(as_left(d_mixed)):
        gleft[g] = part
    for g, part in enumerate(as_right(v)):
        vright[g] = part
    kk = pair(k)
    keys[0:ROWS, :] = kk
    keys[ROWS : 2 * ROWS, :] = kk
    for ref, x in ((q_t, q), (do_t, d_mixed)):
        hi, lo = split(x.T)
        ref[0] = hi
        ref[1] = lo
    dq[...] = jnp.zeros_like(dq)
    dkv_t[...] = jnp.zeros_like(dkv_t)

    def per_head(h, carry):
        g = lax.div(h, 4)
        lanes = own_lanes(h)
        at_h = jnp.where(iota((1, WIDE), 1) == h, 1.0, 0.0)
        mask = head_mask(h, 2 * WIDE).astype(BF16)
        for b in range(ROWS // BLK):
            rows = slice(b * BLK, (b + 1) * BLK)
            s = scores(left[g, rows, :], right[g], h, rows, region)
            level = jnp.sum(lse[rows, :] * at_h, 1, keepdims=True)
            p = jnp.exp(s - level)
            dp = dot_nt(gleft[g, rows, :] * mask, vright[g])
            delta = jnp.sum(dmix[rows, :] * mixed[rows, :] * lanes, 1, keepdims=True)
            ds = p * (dp - delta)
            both = pair(ds)
            weights[rows, :] = pair(p)
            slopes[rows, :] = both
            dq[rows, :] += fold(dot(both, keys[...])) * lanes
        here = pl.multiple_of(h * HDIM, HDIM)
        for i, (t, m) in enumerate(((q_t, slopes), (do_t, weights))):
            lhs = jnp.concatenate([t[0, pl.ds(here, HDIM), :], t[1, pl.ds(here, HDIM), :]], 0)
            out = fold_rows(fold(dot(lhs, m[...])))
            dkv_t[i, pl.ds(here, HDIM), :] = out
        return carry

    lax.fori_loop(0, HEADS, per_head, 0)
    d_q = dq[...] * HDIM**-0.5
    d_k = dkv_t[0].T
    d_v = dkv_t[1].T
    x_t = rows_t(normed)
    d_normed = None
    for i, d in enumerate((d_q, d_k, d_v)):
        grads[pl.ds(at + R_QKV + i, EMB, stride=3), :] = mm_tn(x_t, d)[:EMB]
        grads[at + R_QKVB + i : at + R_QKVB + i + 1, :] = colsum(d)
        part = mm_nt(d, deep(layer[pl.ds(R_QKV + i, EMB, stride=3), :]))
        d_normed = part if d_normed is None else d_normed + part
    return d_normed


def mlp(middle, layer, hpre):
    normed = norm(middle, layer[2:3, :], layer[3:4, :])
    w = deep(hidden_rows(layer, R_HID, EMB))
    pre = mm(normed, w) + hidden_rows(layer, R_HIDB, 1)
    hpre[...] = pre
    out = mm(gelu(pre), layer[R_OUT : R_OUT + HID, :])
    return middle + out + layer[R_OUTB : R_OUTB + 1, :]


def mlp_back(grad, middle, hpre, layer, grads, at):
    hat, inv = norm_stats(middle)
    normed = hat * layer[2:3, :] + layer[3:4, :]
    act, slope = gelu_both(hpre[...])
    grads[at + R_OUTB : at + R_OUTB + 1, :] = colsum(grad)
    grads[at + R_OUT : at + R_OUT + HID, :] = mm_tn(rows_t(grad), act).T
    d_pre = mm_nt(grad, layer[R_OUT : R_OUT + HID, :]) * slope
    put_hidden_rows(grads, at + R_HIDB, 1, colsum(d_pre))
    put_hidden_rows(grads, at + R_HID, EMB, mm_tn(rows_t(normed), d_pre)[:EMB])
    d_normed = mm_nt(d_pre, deep(hidden_rows(layer, R_HID, EMB)))
    grads[at + 2 : at + 3, :] = colsum(d_normed * hat)
    grads[at + 3 : at + 4, :] = colsum(d_normed)
    return grad + norm_back(hat, inv, layer[2:3, :], d_normed)


def pre_norm_back(grad, tokens, layer, grads, at):
    hat, inv = norm_stats(tokens)
    grads[at : at + 1, :] = colsum(grad * hat)
    grads[at + 1 : at + 2, :] = colsum(grad)
    return norm_back(hat, inv, layer[0:1, :], grad)


def region_of(rows, sizes):
    d = lax.shift_right_logical(rows * 1338, 16)
    line = lax.shift_right_logical(rows * 9363, 16)
    places = (d, line - d * WIN, rows - line * WIN)
    starts = (lax.axis_index("slab") * WIN, lax.axis_index("mp") * WIN, 0)
    total = None
    for place, start, blocks in zip(places, starts, sizes + (1,)):
        turned = jnp.where(place < SHIFT, place + FAR, place - SHIFT) + start
        length = WIN * blocks
        part = jnp.where(turned < length - WIN, 0, jnp.where(turned < length - SHIFT, 1, 2))
        total = part if total is None else total * 3 + part
    return total


def put_regions(region, sizes):
    region_rows, region_lanes = region
    region_rows[...] = region_of(iota((ROWS, WIDE), 0), sizes).astype(F32)
    region_lanes[...] = region_of(iota((8, ROWS), 1), sizes).astype(F32)


def send_parts(ref, a, b, c):
    far = FAR * WIN
    near = SHIFT * WIN
    for d in range(SHIFT):
        base = d * PLANE
        c[d * near : (d + 1) * near, :] = ref[base : base + near, :]
        a[d * far : (d + 1) * far, :] = ref[base + near : base + PLANE, :]
    for d in range(FAR):
        base = (d + SHIFT) * PLANE
        b[d * near : (d + 1) * near, :] = ref[base : base + near, :]


def take_parts(own, a, b, c, out):
    far = FAR * WIN
    near = SHIFT * WIN
    for d in range(WIN):
        base = d * PLANE
        if d < SHIFT:
            out[base : base + near, :] = c[d * near : (d + 1) * near, :]
            out[base + near : base + PLANE, :] = a[d * far : (d + 1) * far, :]
        else:
            e = d - SHIFT
            out[base : base + near, :] = b[e * near : (e + 1) * near, :]
            out[base + near : base + PLANE, :] = own[base + near : base + PLANE, :]
    out[VOX:, :] = jnp.zeros((ROWS - VOX, WIDE), F32)


def relay(params, groups, out, square):
    low, high = groups
    first = 3 * low // 8 * 8
    count = min(3 * high, NPARAM // WIDE) - first
    whole = count // 8 * 8
    square[0:whole, :] = params[first * WIDE : (first + whole) * WIDE].reshape(whole, WIDE)
    if 3 * high > NPARAM // WIDE:
        rest = NPARAM - (first + whole) * WIDE
        square[whole : whole + 16, :] = jnp.zeros((16, WIDE), F32)
        for r in range(0, rest, WIDE):
            n = min(WIDE, rest - r)
            low_at = (first + whole) * WIDE + r
            square[whole + r // WIDE : whole + r // WIDE + 1, 0:n] = params[
                low_at : low_at + n
            ].reshape(1, n)
    elif whole < count:
        last = first + whole
        square[whole : whole + 8, :] = params[last * WIDE : (last + 8) * WIDE].reshape(8, WIDE)
    skip = 3 * low - first
    n = high - low
    parts = three_to_four([square[pl.ds(skip + c, n, stride=3), :] for c in range(3)])
    for c in range(4):
        out[pl.ds(c, n, stride=4), :] = parts[c]


def prep_first_kernel(params, merge, lay0, square):
    relay(params, (0, 98), merge, square)
    relay(params, (LAYER_BASE[0], LAYER_BASE[0] + 292), lay0, square)


def prep_layers_kernel(params, lay1, lay2, square):
    relay(params, (LAYER_BASE[1], LAYER_BASE[1] + 292), lay1, square)
    relay(params, (LAYER_BASE[2], LAYER_BASE[2] + 292), lay2, square)


def head_picks():
    width = HEAD_ROWS * WIDE
    place = iota((WIDE, width), 1) - HEAD_LANE
    row = iota((WIDE, width), 0)
    here = (place >= row * CLASSES) & (place < (row + 1) * CLASSES) & (row <= EMB)
    place = iota((width, WIDE), 0) - HEAD_LANE
    col = iota((width, WIDE), 1)
    row = lax.shift_right_logical(place * 4682, 16)
    there = (place - row * CLASSES == col) & (place >= 0)
    return jnp.where(here, 1.0, 0.0), jnp.where(there, 1.0, 0.0).astype(BF16)


def prep_conv_kernel(params, conv0, conv1, head, square):
    relay(params, (CONV_BASE[0], CONV_BASE[0] + 649), conv0, square)
    relay(params, (CONV_BASE[1], GROUPS), conv1, square)
    first = 3 * CONV_BASE[1] // 8 * 8
    row = jnp.concatenate(
        [square[HEAD_ROW + i - first : HEAD_ROW + i - first + 1, :] for i in range(HEAD_ROWS)], 1
    )
    here, there = head_picks()
    hi, lo = split(here * row)
    head[...] = dot(hi, there) + dot(lo, there)


def head_rows(d_head, out, at):
    here, there = head_picks()
    hi, lo = split(d_head)
    spread = (dot_nt(hi, there) + dot_nt(lo, there)) * here
    row = colsum(spread)
    for i in range(HEAD_ROWS):
        out[at + i : at + i + 1, :] += row[:, i * WIDE : (i + 1) * WIDE]


class Rows:
    def __init__(self, ref, at):
        self.ref, self.at = ref, at

    def __getitem__(self, key):
        rows, lanes = key
        if isinstance(rows, slice):
            rows = slice(rows.start + self.at, rows.stop + self.at)
        else:
            rows = pl.ds(rows.start + self.at, rows.size, stride=rows.stride)
        return self.ref[rows, lanes]


def merged_norm(x):
    mean = jnp.sum(x, 1, keepdims=True) * (1.0 / MERGE)
    centred = x - mean
    var = jnp.sum(centred * centred, 1, keepdims=True) * (1.0 / MERGE)
    return centred * lax.rsqrt(var + eps_norm)


def first_kernel(
    feats, merge, lay0, lay1,
    dense, tok0, save, lse, mixed, middle, hpre, tok1, ahead, pa, pb, pc,
    left, right, values,
):
    dense[VOX:, :] = jnp.zeros((ROWS - VOX, MERGE), F32)
    for line in range(PLANE):
        dense[line * WIN : (line + 1) * WIN, :] = feats[line]
    hat = merged_norm(dense[...])
    normed = hat * hidden_rows(merge, 0, 1) + hidden_rows(merge, 4, 1)
    tokens = mm(normed, merge[8 : 8 + MERGE, :])
    tok0[...] = tokens
    layer = Rows(lay0, 0)
    normed = norm(tokens, layer[0:1, :], layer[1:2, :])
    attended = attention(normed, layer, save, lse, mixed, left, right, values)
    mid = tokens + attended
    middle[...] = mid
    tokens = mlp(mid, layer, hpre)
    tok1[...] = tokens
    ahead[...] = norm(tokens, lay1[1:2, :], lay1[2:3, :])
    send_parts(ahead, pa, pb, pc)


def shifted_kernel(
    sizes,
    own, pa, pb, pc, lay1,
    window, save, lse, mixed, out, qa, qb, qc,
    region_rows, region_lanes, left, right, values,
):
    put_regions((region_rows, region_lanes), sizes)
    take_parts(own, pa, pb, pc, window)
    out[...] = attention(
        window[...], Rows(lay1, 1), save, lse, mixed, left, right, values,
        (region_rows, region_lanes),
    )
    send_parts(out, qa, qb, qc)


def to_lines(ref, out):
    for line in range(PLANE):
        out[line, 0:WIN, :] = ref[line * WIN : (line + 1) * WIN, :]
        out[line, WIN:8, :] = jnp.zeros((8 - WIN, WIDE), F32)


def from_lines(ref, out):
    out[VOX:, :] = jnp.zeros((ROWS - VOX, WIDE), F32)
    for line in range(PLANE):
        out[line * WIN : (line + 1) * WIN, :] = ref[line, 0:WIN, :]


def send_sides(lines, sides):
    low_d, high_d, low_h, high_h, corners = sides[0], sides[1], sides[2], sides[3], sides[4:]
    low_d[...] = lines[0 : 2 * WIN]
    high_d[...] = lines[(WIN - 2) * WIN :]
    for d in range(WIN):
        low_h[2 * d : 2 * d + 2] = lines[d * WIN : d * WIN + 2]
        high_h[2 * d : 2 * d + 2] = lines[d * WIN + WIN - 2 : (d + 1) * WIN]
    for i, corner in enumerate(corners):
        first = (WIN - 2 if i & 2 else 0) * WIN + (WIN - 2 if i & 1 else 0)
        for d in range(2):
            corner[2 * d : 2 * d + 2] = lines[first + d * WIN : first + d * WIN + 2]


def second_kernel(
    tok1, own, qa, qb, qc, lay1, lay2,
    mid1, hpre1, tok2, save, lse, mixed, mid2, hpre2, lines,
    s0, s1, s2, s3, s4, s5, s6, s7,
    attended, left, right, values,
):
    take_parts(own, qa, qb, qc, attended)
    mid = tok1[...] + attended[...]
    mid1[...] = mid
    tokens = mlp(mid, Rows(lay1, 1), hpre1)
    tok2[...] = tokens
    layer = Rows(lay2, 2)
    normed = norm(tokens, layer[0:1, :], layer[1:2, :])
    mid = tokens + attention(normed, layer, save, lse, mixed, left, right, values)
    mid2[...] = mid
    attended[...] = mlp(mid, layer, hpre2)
    to_lines(attended, lines)
    send_sides(lines, (s0, s1, s2, s3, s4, s5, s6, s7))


def grown_lines(own, sides, out):
    out[...] = jnp.zeros_like(out)
    for d in range(WIN):
        out[d + 2, 2 : 2 + WIN] = own[d * WIN : (d + 1) * WIN]
        out[d + 2, 0:2] = sides[2][2 * d : 2 * d + 2]
        out[d + 2, 9:11] = sides[3][2 * d : 2 * d + 2]
    for d in range(2):
        out[d, 2 : 2 + WIN] = sides[0][d * WIN : (d + 1) * WIN]
        out[d + 9, 2 : 2 + WIN] = sides[1][d * WIN : (d + 1) * WIN]
    for i, corner in enumerate(sides[4:]):
        d, h = (9 if i & 2 else 0), (9 if i & 1 else 0)
        for e in range(2):
            out[d + e, h : h + 2] = corner[2 * e : 2 * e + 2]


def put_marks(labels, valid, out):
    across = iota((8, WIN), 1) == iota((8, WIN), 0)
    classes = iota((8, WIDE), 1) - EMB
    for d in range(WIN):
        code = jnp.where(valid[d] == 1, labels[d], -1 - EMB - WIDE)
        code = code.astype(F32)
        for h in range(WIN):
            line = jnp.where(across, code[h : h + 1, :], 0.0)
            column = jnp.sum(line, 1, keepdims=True)
            mark = jnp.where(column == classes.astype(F32), 1.0, 0.0)
            out[d * WIN + h] = jnp.where(iota((8, WIDE), 0) < WIN, mark, 0.0)


def taps(source, first_plane, planes, first_line, lines, out):
    def per_plane(d, carry):
        for c in range(3):
            for b in range(3):
                x = source[d + first_plane, first_line + b : first_line + b + lines]
                if c != 1:
                    x = roll(x, 1 if c == 0 else 7, 1)
                x = pair(x.reshape(lines * 8, WIDE))
                at = pl.multiple_of(d * (lines * 8), lines * 8)
                t = b * 3 + c
                out[pl.ds(at, lines * 8), t * 256 : (t + 1) * 256] = x
        return carry

    lax.fori_loop(0, planes, per_plane, 0)


def tap_weights(ref, at, out):
    def per_tap(i, carry):
        w = deep(ref[pl.ds(i * EMB + at, EMB), :])
        out[pl.ds(pl.multiple_of(i * 256, 256), 256), :] = weight_nn(w)
        return carry

    lax.fori_loop(0, 27, per_tap, 0)


def tap_weights_back(ref, at, out):
    def per_tap(i, carry):
        w = deep(ref[pl.ds((26 - i) * EMB + at, EMB), :]).T
        out[pl.ds(pl.multiple_of(i * 256, 256), 256), :] = weight_nn(w)
        return carry

    lax.fori_loop(0, 27, per_tap, 0)


def conv(side, weights, planes, pitch, at_once, put):
    rows = at_once * pitch
    for start in range(0, planes, at_once):
        total = None
        for a in range(3):
            low = (start + a) * pitch
            part = dot(side[low : low + rows, :], weights[a * 2304 : (a + 1) * 2304, :])
            total = part if total is None else total + part
        put(start, fold(total))


def conv_weight_grad(side, grad_rows, pitch, out, at):
    rows = 512
    g = jnp.concatenate([grad_rows, jnp.zeros((rows - grad_rows.shape[0], WIDE), F32)], 0)
    left = rows_t(g)
    for a in range(3):
        for bc in range(9):
            y = dot(left, side[a * pitch : a * pitch + rows, bc * 256 : (bc + 1) * 256])
            y = fold_rows(fold(y)).T
            t = a * 9 + bc
            out[at + t * EMB : at + (t + 1) * EMB, :] = y[:EMB]


def volume_mask(sizes, planes, lines, reach, real_lines):
    slab, row = lax.axis_index("slab"), lax.axis_index("mp")
    ends = (slab == 0, slab == sizes[0] - 1, row == 0, row == sizes[1] - 1)
    shape = (planes, lines, 8, WIDE)
    d, h, w = iota(shape, 0), iota(shape, 1), iota(shape, 2)
    low_d = jnp.where(ends[0], reach, 0)
    high_d = jnp.where(ends[1], planes - reach, planes)
    low_h = jnp.where(ends[2], reach, 0)
    high_h = jnp.where(ends[3], real_lines - reach, real_lines)
    inside = (d >= low_d) & (d < high_d) & (h >= low_h) & (h < high_h) & (w < WIN)
    return jnp.where(inside, 1.0, 0.0)


def conv_kernel(
    sizes,
    own, s0, s1, s2, s3, s4, s5, s6, s7, labels, valid, conv0, conv1,
    grown, pre, tok, stats, t0, t1, t2, t3, t4, t5, t6, t7,
    act, side, side_own, weights, marks,
):
    grown_lines(own, (s0, s1, s2, s3, s4, s5, s6, s7), grown)
    put_marks(labels, valid, marks)
    tap_weights(conv0, 3, weights)
    taps(grown, 0, 11, 0, 10, side)
    bias0 = conv0[3 + TAP_ROWS : 4 + TAP_ROWS, :]
    inside = volume_mask(sizes, 9, 10, 1, 9)

    def put(start, y):
        z = (y + bias0).reshape(3, 10, 8, WIDE)
        pre[start : start + 3] = z
        act[start : start + 3] = gelu(z) * inside[start : start + 3]

    conv(side, weights, 9, 80, 3, put)
    tap_weights(conv1, 0, weights)
    taps(act, 0, 9, 0, 8, side_own)
    bias1 = conv1[TAP_ROWS : TAP_ROWS + 1, :]
    sums = []

    def put_own(start, y):
        y = (y + bias1).reshape(WIN, 8, 8, WIDE)[:, 0:WIN]
        y = y + own[...].reshape(WIN, WIN, 8, WIDE)
        y = jnp.where(iota(y.shape, 2) < WIN, y, 0.0).reshape(PLANE, 8, WIDE)
        tok[...] = y + marks[...]
        send_sides(tok, (t0, t1, t2, t3, t4, t5, t6, t7))
        flat = y.reshape(PLANE * 8, WIDE)
        sums.append(colsum(flat))
        sums.append(colsum(flat * flat))

    conv(side_own, weights, WIN, 64, WIN, put_own)
    count = jnp.sum(marks[...].reshape(PLANE * 8, WIDE))
    row = iota((8, WIDE), 0)
    stats[...] = (
        jnp.where(row == 0, sums[0], 0.0)
        + jnp.where(row == 1, sums[1], 0.0)
        + jnp.where(row == 2, count, 0.0)
    )


def head_kernel(
    voxels,
    own, s0, s1, s2, s3, s4, s5, s6, s7, sums, conv1, head_w,
    grown, slope_out, stats, d_head, d_rows,
):
    grown_lines(own, (s0, s1, s2, s3, s4, s5, s6, s7), grown)
    rows = 11 * 12 * 8
    both = grown[...].reshape(rows, WIDE)
    lane = iota((rows, WIDE), 1)
    tokens = jnp.where(lane < EMB, both, 0.0)
    target = jnp.where(lane < CLASSES, roll(both, WIDE - EMB, 1), 0.0)
    live = jnp.sum(target, 1, keepdims=True)
    count = F32(voxels)
    average = sums[0:1, :] / count
    spread = sums[1:2, :] / count - average * average
    inv = lax.rsqrt(spread + eps_norm)
    gain = conv1[TAP_ROWS + 1 : TAP_ROWS + 2, :]
    bias = conv1[TAP_ROWS + 2 : TAP_ROWS + 3, :]
    hat = (tokens - average) * inv
    act, slope = gelu_both(hat * gain + bias)
    act = jnp.where(lane == EMB, 1.0, act)
    w = head_w[...]
    logits = mm(act, w)
    logits = jnp.where(lane < CLASSES, logits, -1e30)
    top = jnp.max(logits, 1, keepdims=True)
    e = jnp.exp(logits - top)
    total = jnp.sum(e, 1, keepdims=True)
    logp = logits - top - jnp.log(total)
    scale = 1.0 / sums[2:3, 0:1]
    d_logits = (e / total * live - target) * scale
    d_normed = jnp.where(lane < EMB, mm_nt(d_logits, w) * slope, 0.0)
    d_tokens = d_normed * gain * inv
    slope_out[...] = d_tokens.reshape(11, 12, 8, WIDE)

    def own_rows(x):
        x = x.reshape(11, 12, 8, WIDE)[2:9, 2:9]
        x = jnp.where(iota(x.shape, 2) < WIN, x, 0.0)
        return x.reshape(PLANE * 8, WIDE)

    loss = -jnp.sum(own_rows(target * jnp.where(lane < CLASSES, logp, 0.0)))
    own_d = own_rows(d_logits)
    own_n = own_rows(d_normed)
    own_hat = own_rows(hat)
    zeros = jnp.zeros((512 - PLANE * 8, WIDE), F32)
    left = rows_t(jnp.concatenate([own_d, zeros], 0))
    d_head[...] = mm_tn(left, jnp.concatenate([own_rows(act), zeros], 0)).T
    d_gain = colsum(own_n * own_hat)
    d_bias = colsum(own_n)
    d_average = -d_bias * gain * inv
    d_spread = d_gain * gain * inv * inv * -0.5
    d_two = d_spread / count
    d_one = (d_average - 2.0 * average * d_spread) / count
    row = iota((8, WIDE), 0)
    live_lane = iota((8, WIDE), 1) < EMB
    stats[...] = (
        jnp.where((row == 0) & live_lane, d_one, 0.0)
        + jnp.where((row == 1) & live_lane, d_two, 0.0)
        + jnp.where(row == 2, loss, 0.0)
    )
    d_rows[...] = (
        jnp.where(row == 0, d_gain, 0.0)
        + jnp.where(row == 1, d_bias, 0.0)
    )


def conv_back_kernel(
    sizes,
    tok, slope, sums, grown, pre, conv0, conv1, d_rows, d_head,
    d_own, keep, send, carry, seam,
    grads, dgrown, act, side, side_own, weights, flat,
):
    lane = iota((11, 12, 8, WIDE), 3)
    inside = volume_mask(sizes, 11, 12, 2, 11)
    steady = sums[0:1, :].reshape(1, 1, 1, WIDE)
    rising = 2.0 * sums[1:2, :].reshape(1, 1, 1, WIDE)
    d_tok = slope[...] + jnp.where(lane < EMB, (steady + tok[...] * rising) * inside, 0.0)
    dgrown[...] = d_tok
    grads[5191:, :] = jnp.zeros((45, WIDE), F32)
    grads[0:8, :] = jnp.zeros((8, WIDE), F32)
    grads[5189:5191, :] = d_rows[0:2, :]
    own = dgrown[2:9, 2:10]
    line = iota(own.shape, 1)
    own = jnp.where(line < WIN, own, 0.0).reshape(WIN * 64, WIDE)
    grads[5188:5189, :] = colsum(own)

    near = volume_mask(sizes, 9, 10, 1, 9)
    act[0:9] = gelu(pre[...]) * near
    act[9:10] = jnp.zeros((1, 10, 8, WIDE), F32)
    taps(act, 0, 10, 0, 8, side_own)
    conv_weight_grad(side_own, own, 64, grads, 2596)
    tap_weights_back(conv1, 0, weights)
    taps(dgrown, 0, 11, 0, 10, side)

    def put(start, y):
        _, s = gelu_both(pre[start : start + 3])
        z = y.reshape(3, 10, 8, WIDE) * s * near[start : start + 3]
        act[start : start + 3] = z

    conv(side, weights, 9, 80, 3, put)

    own = act[1:8, 1:9]
    line = iota(own.shape, 1)
    own = jnp.where(line < WIN, own, 0.0).reshape(WIN * 64, WIDE)
    grads[2595:2596, :] = colsum(own)
    taps(grown, 1, 10, 1, 8, side_own)
    conv_weight_grad(side_own, own, 64, grads, 3)
    carry[...] = grads[0:24, :]
    flat[3 * (GROUPS - CUTS[3]) :, :] = jnp.zeros((flat.shape[0] - 3912, WIDE), F32)
    flatten(grads, 20, GROUPS - CUTS[3], flat)
    start = 3 * CUTS[3]
    head_rows(d_head[...], flat, HEAD_ROW - start)
    seam[...] = flat[0 : LATE_ROWS - start, :]
    scatter(sizes, flat, LATE_ROWS - start, keep, send)
    tap_weights_back(conv0, 3, weights)
    taps(act, 0, 9, 0, 8, side_own)

    def put_own(start, y):
        y = y.reshape(WIN, 8, 8, WIDE)[:, 0:WIN] + dgrown[2:9, 2:9]
        y = jnp.where(iota(y.shape, 2) < WIN, y, 0.0)
        d_own[...] = y.reshape(PLANE, 8, WIDE)

    conv(side_own, weights, WIN, 64, WIN, put_own)


def back_two_kernel(
    d_own, carry, lay1, lay2, tok2, save, lse, mixed, mid2, hpre2, mid1, hpre1,
    d_mid, grads1, flat, carry2, pa, pb, pc,
    grads, dense, *sc,
):
    from_lines(d_own, dense)
    layer = Rows(lay2, 2)
    grads[0:8, :] = jnp.zeros((8, WIDE), F32)
    d = mlp_back(dense[...], mid2[...], hpre2, layer, grads, 2)
    tokens = tok2[...]
    normed = norm(tokens, layer[0:1, :], layer[1:2, :])
    d_normed = attention_back(d, normed, layer, save, lse, mixed, sc, grads, 2)
    d = d + pre_norm_back(d_normed, tokens, layer, grads, 2)
    grads[1167:1184, :] = carry[3:20, :]
    flatten(grads, 32, CUTS[3] - CUTS[2], flat)
    carry2[...] = grads[0:32, :]
    layer = Rows(lay1, 1)
    d = mlp_back(d, mid1[...], hpre1, layer, grads1, 1)
    d_mid[...] = d
    send_parts(d_mid, pa, pb, pc)


def back_shifted_kernel(
    sizes,
    own, pa, pb, pc, lay1, window, save, lse, mixed, grads1, carry2,
    d_window, flat, carry1, qa, qb, qc,
    region_rows, region_lanes, grads, grad, *sc,
):
    put_regions((region_rows, region_lanes), sizes)
    take_parts(own, pa, pb, pc, grad)
    grads[0:1168, :] = grads1[...]
    grads[0:3, :] = jnp.zeros((3, WIDE), F32)
    d_window[...] = attention_back(
        grad[...], window[...], Rows(lay1, 1), save, lse, mixed, sc, grads, 1,
        (region_rows, region_lanes),
    )
    send_parts(d_window, qa, qb, qc)
    grads[1166:1196, :] = carry2[2:32, :]
    flatten(grads, 12, CUTS[2] - CUTS[1], flat)
    carry1[...] = grads[0:16, :]


def back_first_kernel(
    sizes,
    d_mid, own, qa, qb, qc, tok1, lay0, lay1, merge, dense, tok0, save, lse, mixed, middle, hpre,
    carry1, flat1, flat2, seam,
    keep, send,
    flat, grads, grad, *sc,
):
    take_parts(own, qa, qb, qc, grad)
    grads[1556:1572, :] = carry1[...]
    d = d_mid[...] + pre_norm_back(grad[...], tok1[...], Rows(lay1, 1), grads, 1557)
    layer = Rows(lay0, 0)
    at = MERGE_ROWS
    d = mlp_back(d, middle[...], hpre, layer, grads, at)
    tokens = tok0[...]
    normed = norm(tokens, layer[0:1, :], layer[1:2, :])
    d_normed = attention_back(d, normed, layer, save, lse, mixed, sc, grads, at)
    d = d + pre_norm_back(d_normed, tokens, layer, grads, at)
    live = iota((ROWS, WIDE), 0) < VOX
    d = jnp.where(live, d, 0.0)
    hat = merged_norm(dense[...])
    gain = hidden_rows(merge, 0, 1)
    bias = hidden_rows(merge, 4, 1)
    w = merge[8 : 8 + MERGE, :]
    put_hidden_rows(grads, 8 - 8, 1, jnp.zeros((1, MERGE), F32))
    grads[8 : 8 + MERGE, :] = mm_tn(rows_t(d), hat * gain + bias).T
    d_hat = mm_nt(d, w)
    put_hidden_rows(grads, 0, 1, colsum(d_hat * hat))
    put_hidden_rows(grads, 4, 1, colsum(d_hat))
    flatten(grads, 0, CUTS[1], flat)
    at = 0
    for cut, part in ((CUTS[1], flat1), (CUTS[2], flat2), (CUTS[3], seam)):
        at = 3 * cut
        flat[at : at + part.shape[0], :] = part[...]
    at += seam.shape[0]
    if flat.shape[0] > at:
        flat[at:, :] = jnp.zeros((flat.shape[0] - at, WIDE), F32)
    scatter(sizes, flat, 0, keep, send)


def radices(count):
    steps = [2]
    left = count // 2
    while left > 1:
        steps.append(4 if left >= 4 else 2)
        left //= steps[-1]
    return steps


def block_rows(rows, count):
    return -(-rows // (8 * count)) * 8


def own_number(sizes):
    return lax.axis_index("slab") * sizes[1] + lax.axis_index("mp")


def place_in_half(distance, count):
    place = 0
    shift = 1
    for radix in radices(count)[1:]:
        digit = jnp.bitwise_and(lax.shift_right_logical(distance, shift), radix - 1)
        place = place * radix + digit
        shift += radix.bit_length() - 1
    return place


def scatter(sizes, source, first, keep, send):
    count = sizes[0] * sizes[1]
    rows = keep.shape[0] * 2 // count
    me = own_number(sizes)
    odd = jnp.bitwise_and(me, 1)

    def per_pair(t, carry):
        for block, out in ((2 * t + odd, keep), (2 * t + 1 - odd, send)):
            place = place_in_half(jnp.bitwise_xor(block, me), count)
            at = pl.multiple_of(first + block * rows, 8)
            to = pl.multiple_of(place * rows, 8)
            out[pl.ds(to, rows), :] = source[pl.ds(at, rows), :]
        return carry

    lax.fori_loop(0, count // 2, per_pair, 0)


def add_kernel(count, *refs):
    total = refs[0][...]
    for ref in refs[1:count]:
        total = total + ref[...]
    outs = refs[count:]
    rows = total.shape[0] // len(outs)
    for i, out in enumerate(outs):
        out[...] = total[i * rows : (i + 1) * rows]


def join_kernel(*refs):
    out = refs[-1]
    rows = refs[0].shape[0]
    for i, ref in enumerate(refs[:-1]):
        out[i * rows : (i + 1) * rows, :] = ref[...]


def traded(value, distance, count):
    pairs = [(i, i ^ distance) for i in range(count)]
    return lax.ppermute(value, ("slab", "mp"), pairs)


def summing(keep, send, count):
    steps = radices(count)
    got = [keep, traded(send, 1, count)]
    shift = 1
    after = yield None
    for radix in steps[1:]:
        rows = got[0].shape[0] // radix
        parts = call(
            functools.partial(add_kernel, len(got)), [arr(rows, WIDE)] * radix, [], *got,
            name="add", us=0.7, after=after,
        )
        got = [parts[0]] + [traded(parts[k], k << shift, count) for k in range(1, radix)]
        shift += radix.bit_length() - 1
        after = yield parts[0]
    (own,) = call(
        functools.partial(add_kernel, len(got)), [arr(*got[0].shape)], [], *got,
        name="add", us=0.5, after=after,
    )
    for radix in reversed(steps[1:]):
        shift -= radix.bit_length() - 1
        got = [own] + [traded(own, k << shift, count) for k in range(1, radix)]
        after = yield own
        (own,) = call(
            join_kernel, [arr(own.shape[0] * radix, WIDE)], [], *got,
            name="join", us=0.7, after=after,
        )
    other = traded(own, 1, count)
    yield own
    yield own, other


def finished(chain):
    last = None
    while not isinstance(last, tuple):
        last = chain.send(())
    return last


def exchanged_sum(value, count):
    shift = 0
    for radix in radices(count):
        got = [value] + [traded(value, k << shift, count) for k in range(1, radix)]
        while len(got) > 1:
            got = [got[i] + got[i + 1] for i in range(0, len(got), 2)]
        value = got[0]
        shift += radix.bit_length() - 1
    return value


def adamw_kernel(
    sizes,
    late, late_other, early, early_other, params, first, second, tail, sums,
    new_params, new_first, new_second, loss, valid, norm_out,
):
    count = sizes[0] * sizes[1]
    me = own_number(sizes)
    total = jnp.zeros((8, WIDE), F32)
    for ref in (late, late_other, early, early_other):
        x = ref[...]
        total = total + jnp.sum((x * x).reshape(-1, 8, WIDE), 0)
    norm = jnp.sqrt(jnp.sum(total))
    loss[0] = jnp.sum(tail[2:3, 0:1])
    valid[0] = jnp.sum(sums[2:3, 0:1])
    norm_out[0] = norm
    scale = jnp.minimum(1.0, clip_norm / (norm + 1e-06))

    def update(own, other, rows, base, block, size):
        distance = jnp.bitwise_xor(block, me)
        at = pl.ds(pl.multiple_of(place_in_half(distance, count) * rows, 8), rows)
        near = jnp.bitwise_and(distance, 1) == 0
        grad = jnp.where(near, own[at, :], other[at, :]).reshape(rows * WIDE) * scale
        if size < rows * WIDE:
            grad = grad[:size]
        here = pl.ds(pl.multiple_of(base + block * (rows * WIDE), 1024), size)
        one = beta_one * first[here] + (1.0 - beta_one) * grad
        two = beta_two * second[here] + (1.0 - beta_two) * grad * grad
        new_first[here] = one
        new_second[here] = two
        one = one * (1.0 / (1.0 - beta_one**STEP))
        two = two * (1.0 / (1.0 - beta_two**STEP))
        old = params[here]
        new_params[here] = old - learn_rate * (one / (jnp.sqrt(two) + adam_eps) + decay_rate * old)

    base = 0
    for own, other, size in (
        (late, late_other, LATE_ROWS * WIDE),
        (early, early_other, NPARAM - LATE_ROWS * WIDE),
    ):
        rows = own.shape[0] * 2 // count
        whole = size // (rows * WIDE)

        def per_block(block, carry, own=own, other=other, rows=rows, base=base):
            update(own, other, rows, base, block, rows * WIDE)
            return carry

        lax.fori_loop(0, whole, per_block, 0)
        if size % (rows * WIDE):
            update(own, other, rows, base, whole, size % (rows * WIDE))
        base += size


def arr(*shape):
    return jax.ShapeDtypeStruct(shape, F32)


def call(kernel, outs, scratch, *args, name=None, us=1.0, after=()):
    if len(after):
        inner, first, skip = kernel, len(args), len(after)

        def kernel(*refs):
            inner(*refs[:first], *refs[first + skip :])

    smem = pl.BlockSpec(memory_space=pltpu.SMEM)
    vmem = pl.BlockSpec(memory_space=pltpu.VMEM)
    return pl.pallas_call(
        kernel,
        out_shape=list(outs),
        in_specs=[vmem] * len(args) + [pl.BlockSpec(memory_space=pl.ANY)] * len(after),
        out_specs=[smem if o.shape == (1,) else vmem for o in outs],
        scratch_shapes=list(scratch),
        compiler_params=pltpu.CompilerParams(vmem_limit_bytes=VMEM),
        cost_estimate=pl.CostEstimate(
            flops=int(us * 1.15e9), bytes_accessed=0, transcendentals=0
        ),
        name=name,
    )(*args, *after)


SQUARE = arr(ROWS, WIDE)
SAVE = arr(ROWS, 3 * WIDE)
FORWARD = [
    pltpu.VMEM((2, ROWS, 2 * WIDE), BF16),
    pltpu.VMEM((2, ROWS, 2 * WIDE), BF16),
    pltpu.VMEM((2 * ROWS, 2 * WIDE), BF16),
]
BACKWARD = [
    pltpu.VMEM((2, ROWS, 2 * WIDE), BF16),
    pltpu.VMEM((2, ROWS, 2 * WIDE), BF16),
    pltpu.VMEM((2, ROWS, 2 * WIDE), BF16),
    pltpu.VMEM((2, ROWS, 2 * WIDE), BF16),
    pltpu.VMEM((2 * ROWS, 2 * WIDE), BF16),
    pltpu.VMEM((ROWS, WIDE), F32),
    pltpu.VMEM((2, WIDE, ROWS), F32),
    pltpu.VMEM((ROWS, 2 * ROWS), BF16),
    pltpu.VMEM((ROWS, 2 * ROWS), BF16),
    pltpu.VMEM((2, WIDE, ROWS), BF16),
    pltpu.VMEM((2, WIDE, ROWS), BF16),
    pltpu.VMEM((ROWS, WIDE), F32),
]
PARTS = [arr(ROWS_A, WIDE), arr(ROWS_B, WIDE), arr(ROWS_C, WIDE)]


def passed(parts, steps, sizes):
    slabs, rows = sizes
    moved = []
    for part, (ds, dm) in zip(parts, ((1, 0), (0, 1), (1, 1))):
        pairs = []
        for s in range(slabs):
            for m in range(rows):
                target = ((s + steps * ds) % slabs) * rows + (m + steps * dm) % rows
                pairs.append((s * rows + m, target))
        moved.append(lax.ppermute(part, ("slab", "mp"), pairs))
    return moved


SIDES = [arr(2 * WIN, 8, WIDE)] * 4 + [arr(4, 8, WIDE)] * 4


def beside(sides, sizes):
    slabs, rows = sizes
    steps = [(1, 0), (-1, 0), (0, 1), (0, -1)]
    steps += [(1, 1), (1, -1), (-1, 1), (-1, -1)]
    source = (1, 0, 3, 2, 7, 6, 5, 4)
    got = []
    for (ds, dm), side in zip(steps, source):
        pairs = []
        for s in range(slabs):
            for m in range(rows):
                if 0 <= s + ds < slabs and 0 <= m + dm < rows:
                    pairs.append((s * rows + m, (s + ds) * rows + m + dm))
        got.append(lax.ppermute(sides[side], ("slab", "mp"), pairs))
    return got


REGION = [pltpu.VMEM((ROWS, WIDE), F32), pltpu.VMEM((8, ROWS), F32)]


def on_device(sizes, feats, labels, valid, params, moment_one, moment_two):
    slabs, rows = sizes
    count = slabs * rows
    square = [pltpu.VMEM((2048, WIDE), F32)]
    merge, lay0 = call(
        prep_first_kernel, [arr(MERGE_ROWS, WIDE), arr(1168, WIDE)], square, params,
        name="prep_first", us=2.0,
    )
    lay1, lay2 = call(
        prep_layers_kernel, [arr(1168, WIDE)] * 2, square, params, name="prep_layers", us=2.0
    )
    conv0, conv1, head_w = call(
        prep_conv_kernel, [arr(2596, WIDE), arr(2640, WIDE), arr(WIDE, WIDE)], square, params,
        name="prep_conv", us=3.0,
    )

    dense, tok0, save0, lse0, mixed0, mid0, hpre0, tok1, ahead, *parts = call(
        first_kernel,
        [arr(ROWS, MERGE), SQUARE, SAVE, SQUARE, SQUARE, SQUARE, arr(ROWS, HID), SQUARE, SQUARE]
        + PARTS,
        FORWARD,
        feats.reshape(PLANE, WIN, MERGE), merge, lay0, lay1,
        name="first", us=9.5,
    )
    parts = passed(parts, -1, sizes)
    window, save1, lse1, mixed1, out1, *parts = call(
        functools.partial(shifted_kernel, sizes),
        [SQUARE, SAVE, SQUARE, SQUARE, SQUARE] + PARTS,
        REGION + FORWARD,
        ahead, *parts, lay1,
        name="shifted", us=7.5,
    )
    parts = passed(parts, 1, sizes)
    mid1, hpre1, tok2, save2, lse2, mixed2, mid2, hpre2, lines, *sides = call(
        second_kernel,
        [SQUARE, arr(ROWS, HID), SQUARE, SAVE, SQUARE, SQUARE, SQUARE, arr(ROWS, HID)]
        + [arr(PLANE, 8, WIDE)] + SIDES,
        [pltpu.VMEM((ROWS, WIDE), F32)] + FORWARD,
        tok1, out1, *parts, lay1, lay2,
        name="second", us=9.5,
    )
    sides = beside(sides, sizes)
    grown, pre, tok3, sums, *tok_sides = call(
        functools.partial(conv_kernel, sizes),
        [arr(11, 12, 8, WIDE), arr(9, 10, 8, WIDE), arr(PLANE, 8, WIDE), arr(8, WIDE)] + SIDES,
        [
            pltpu.VMEM((9, 10, 8, WIDE), F32),
            pltpu.VMEM((880, 2304), BF16),
            pltpu.VMEM((576, 2304), BF16),
            pltpu.VMEM((27 * 256, 256), BF16),
            pltpu.VMEM((PLANE, 8, WIDE), F32),
        ],
        lines, *sides, labels, valid, conv0, conv1,
        name="conv", us=10.5,
    )
    tok_sides = beside(tok_sides, sizes)
    sums = exchanged_sum(sums, count)
    voxels = WIN * slabs * WIN * rows * WIN
    tok3, slope, tail, d_head, d_rows = call(
        functools.partial(head_kernel, voxels),
        [arr(11, 12, 8, WIDE), arr(11, 12, 8, WIDE), arr(8, WIDE), arr(WIDE, WIDE), arr(8, WIDE)],
        [],
        tok3, *tok_sides, sums, conv1, head_w,
        name="head", us=3.5,
    )
    tail = exchanged_sum(tail, count)
    late_rows = block_rows(LATE_ROWS, count) * count
    early_rows = block_rows(EARLY_ROWS, count) * count
    seam_rows = LATE_ROWS - 3 * CUTS[3]
    d_own, keep, send, carry3, seam = call(
        functools.partial(conv_back_kernel, sizes),
        [arr(PLANE, 8, WIDE)] + [arr(early_rows // 2, WIDE)] * 2
        + [arr(24, WIDE), arr(seam_rows, WIDE)],
        [
            pltpu.VMEM((5236, WIDE), F32),
            pltpu.VMEM((11, 12, 8, WIDE), F32),
            pltpu.VMEM((10, 10, 8, WIDE), F32),
            pltpu.VMEM((880, 2304), BF16),
            pltpu.VMEM((640, 2304), BF16),
            pltpu.VMEM((27 * 256, 256), BF16),
            pltpu.VMEM((seam_rows + early_rows, WIDE), F32),
        ],
        tok3, slope, tail, grown, pre, conv0, conv1, d_rows, d_head,
        name="conv_back", us=21.0,
    )
    early = summing(keep, send, count)
    next(early)
    d_mid, grads1, flat2, carry2, *parts = call(
        back_two_kernel,
        [SQUARE, arr(1168, WIDE), arr(3 * (CUTS[3] - CUTS[2]), WIDE), arr(32, WIDE)] + PARTS,
        [pltpu.VMEM((1184, WIDE), F32), pltpu.VMEM((ROWS, WIDE), F32)] + BACKWARD,
        d_own, carry3, lay1, lay2, tok2, save2, lse2, mixed2, mid2, hpre2, mid1, hpre1,
        name="back_two", us=14.0,
    )
    early.send((d_mid,))
    parts = passed(parts, -1, sizes)
    step = early.send(())
    d_window, flat1, carry1, *parts = call(
        functools.partial(back_shifted_kernel, sizes),
        [SQUARE, arr(3 * (CUTS[2] - CUTS[1]), WIDE), arr(16, WIDE)] + PARTS,
        REGION + [pltpu.VMEM((1200, WIDE), F32), pltpu.VMEM((ROWS, WIDE), F32)] + BACKWARD,
        d_mid, *parts, lay1, window, save1, lse1, mixed1, grads1, carry2,
        name="back_shifted", us=10.5, after=(step,),
    )
    early.send((d_window,))
    parts = passed(parts, 1, sizes)
    step = early.send(())
    late = call(
        functools.partial(back_first_kernel, sizes),
        [arr(late_rows // 2, WIDE)] * 2,
        [
            pltpu.VMEM((late_rows, WIDE), F32),
            pltpu.VMEM((1572, WIDE), F32),
            pltpu.VMEM((ROWS, WIDE), F32),
        ]
        + BACKWARD,
        d_mid, d_window, *parts, tok1, lay0, lay1, merge, dense, tok0, save0, lse0, mixed0, mid0,
        hpre0, carry1, flat1, flat2, seam,
        name="back_first", us=13.5, after=(step,),
    )
    early.send((late[0],))
    late = summing(*late, count)
    next(late)
    late = finished(late)
    early = finished(early)
    new_params, new_first, new_second, loss, valid_count, norm = call(
        functools.partial(adamw_kernel, sizes),
        [arr(NPARAM)] * 3 + [arr(1)] * 3,
        [],
        *late, *early, params, moment_one, moment_two, tail, sums,
        name="adamw", us=8.0,
    )
    return (
        loss.reshape(()), valid_count.reshape(()), norm.reshape(()),
        new_params, new_first, new_second,
    )


def solution(mesh):
    placed = (
        P("slab", "mp", None, None),
        P("slab", "mp", None),
        P("slab", "mp", None),
        P(),
        P(),
        P(),
    )
    sizes = (mesh.shape["slab"], mesh.shape["mp"])
    return jax.shard_map(
        functools.partial(on_device, sizes),
        mesh=mesh,
        in_specs=placed,
        out_specs=(P(), P(), P(), P(), P(), P()),
        check_vma=False,
    )
```

```python
import functools
import math

import jax
import jax.numpy as jnp
from jax import lax
from jax.experimental import pallas as pl
from jax.experimental.pallas import tpu as pltpu
from jax.sharding import PartitionSpec as P

EMB = 96
HEADS = 6
HDIM = 16
HID = 384
MERGE = 384
CLASSES = 14
WIN = 7
SHIFT = 3
LAYERS = 3
STEP = 10

F32 = jnp.float32
BF16 = jnp.bfloat16
eps_norm = 1e-05
beta_one = 0.9
beta_two = 0.999
adam_eps = 1e-08
learn_rate = 0.05
decay_rate = 0.05
clip_norm = 0.01

VOX = WIN * WIN * WIN
ROWS = 384
BLK = 128
WIDE = 128
PLANE = WIN * WIN
FAR = WIN - SHIFT
ROWS_A = SHIFT * FAR * WIN
ROWS_B = FAR * SHIFT * WIN
ROWS_C = SHIFT * SHIFT * WIN

MERGE_ROWS = 392
LAYER_ROWS = 1165
TAP_ROWS = 27 * EMB
GROUPS = 2280
NPARAM = 872558
HEAD_ROW = 6806
HEAD_ROWS = 11
HEAD_LANE = 32
LATE_ROWS = 3072
EARLY_ROWS = 3840
LAYER_BASE = (98, 389, 680)
CONV_BASE = (971, 1620)
CUTS = (0, 392, 688, 976, 2280)

R_QKV, R_QKVB, R_PROJ, R_PROJB = 4, 292, 295, 391
R_HID, R_HIDB, R_OUT, R_OUTB = 392, 776, 780, 1164

VMEM = 56 * 1024 * 1024


def iota(shape, dim):
    return lax.broadcasted_iota(jnp.int32, shape, dim)


def split(x):
    hi = x.astype(BF16)
    return hi, (x - hi.astype(F32)).astype(BF16)


def pair(x):
    return jnp.concatenate(split(x), 1)


def fold(y):
    half = y.shape[1] // 2
    return y[:, :half] + y[:, half:]


def fold_rows(y):
    half = y.shape[0] // 2
    return y[:half] + y[half:]


def dot(a, b):
    return jnp.dot(a, b, preferred_element_type=F32)


def dot_nt(a, b):
    return lax.dot_general(a, b, (((1,), (1,)), ((), ())), preferred_element_type=F32)


def weight_nn(w):
    top = pair(w)
    return jnp.concatenate([top, top], 0)


def weight_nt(w):
    hi, lo = split(w)
    return jnp.concatenate(
        [jnp.concatenate([hi, hi], 1), jnp.concatenate([lo, lo], 1)], 0
    )


def mm(x, w):
    return fold(dot(pair(x), weight_nn(w)))


def mm_nt(x, w):
    return fold(dot_nt(pair(x), weight_nt(w)))


def rows_t(x):
    return jnp.concatenate(split(x.T), 0)


def mm_tn(xt, y):
    return fold_rows(fold(dot(xt, pair(y))))


def deep(w):
    return jnp.concatenate([w, jnp.zeros((WIDE - EMB, w.shape[1]), F32)], 0)


def roll(x, shift, axis):
    return pltpu.roll(x, shift, axis)


def four_to_three(y):
    lane = iota(y[0].shape, 1)
    a = jnp.where(lane < 96, y[0], roll(y[1], 96, 1))
    b = jnp.where(lane < 64, roll(y[1], 96, 1), roll(y[2], 64, 1))
    c = jnp.where(lane < 32, roll(y[2], 64, 1), roll(y[3], 32, 1))
    return a, b, c


def three_to_four(x):
    lane = iota(x[0].shape, 1)
    live = lane < EMB
    a = x[0]
    b = jnp.where(lane < 32, roll(x[0], 32, 1), roll(x[1], 32, 1))
    c = jnp.where(lane < 64, roll(x[1], 64, 1), roll(x[2], 64, 1))
    d = roll(x[2], 96, 1)
    return tuple(jnp.where(live, v, 0.0) for v in (a, b, c, d))


def hidden_rows(ref, start, count):
    return jnp.concatenate(
        four_to_three([ref[pl.ds(start + c, count, stride=4), :] for c in range(4)]), 1
    )


def put_hidden_rows(ref, start, count, x):
    parts = three_to_four([x[:, i * WIDE : (i + 1) * WIDE] for i in range(3)])
    for c in range(4):
        ref[pl.ds(start + c, count, stride=4), :] = parts[c]


def flatten(ref, start, groups, out):
    parts = four_to_three([ref[pl.ds(start + c, groups, stride=4), :] for c in range(4)])
    for c in range(3):
        out[pl.ds(c, groups, stride=3), :] = parts[c]


def norm_stats(x):
    live = iota(x.shape, 1) < EMB
    mean = jnp.sum(x, 1, keepdims=True) * (1.0 / EMB)
    centred = jnp.where(live, x - mean, 0.0)
    var = jnp.sum(centred * centred, 1, keepdims=True) * (1.0 / EMB)
    inv = lax.rsqrt(var + eps_norm)
    return centred * inv, inv


def norm(x, gain, bias):
    hat, _ = norm_stats(x)
    return hat * gain + bias


def norm_back(hat, inv, gain, grad):
    up = grad * gain
    one = jnp.sum(up, 1, keepdims=True) * (1.0 / EMB)
    two = jnp.sum(up * hat, 1, keepdims=True) * (1.0 / EMB)
    live = iota(hat.shape, 1) < EMB
    return jnp.where(live, inv * (up - one - hat * two), 0.0)


def colsum(x):
    return jnp.sum(x, 0, keepdims=True)


def gelu(x):
    return 0.5 * x * (1.0 + lax.erf(x * (0.5**0.5)))


def gelu_both(x):
    cdf = 0.5 * (1.0 + lax.erf(x * (0.5**0.5)))
    slope = cdf + x * (jnp.exp(x * x * -0.5) * 0.3989422804014327)
    return x * cdf, slope


def head_groups(x):
    lane = iota(x.shape, 1)
    swapped = roll(x, 64, 1)
    return jnp.where(lane < 64, x, swapped), jnp.where(lane < 64, swapped, x)


def as_left(x):
    both = []
    low = iota(x.shape, 1) < 64
    for part in head_groups(x):
        hi = part.astype(BF16).astype(F32)
        one = jnp.where(low, hi, part - hi).astype(BF16)
        both.append(jnp.concatenate([one, one], 1))
    return both


def as_right(x):
    return [pair(part) for part in head_groups(x)]


def head_mask(h, width):
    lane = iota((1, width), 1)
    lane = jnp.bitwise_and(lane, 63)
    low = jnp.bitwise_and(h, 3) * HDIM
    return jnp.where((lane >= low) & (lane < low + HDIM), 1.0, 0.0)


def own_lanes(h):
    lane = iota((1, WIDE), 1)
    return jnp.where((lane >= h * HDIM) & (lane < (h + 1) * HDIM), 1.0, 0.0)


def scores(q, k, h, rows, region):
    left = q * head_mask(h, 2 * WIDE).astype(BF16)
    s = dot_nt(left, k)
    if region is not None:
        region_rows, region_lanes = region
        here = region_rows[rows, 0:1]
        s = s + jnp.where(here == region_lanes[0:1, :], 0.0, -100.0)
    return jnp.where(iota(s.shape, 1) < VOX, s, -1e30)


def attention(normed, layer, save, lse, mixed, left, right, values, region=None):
    x = pair(normed)
    qkv = []
    for i in range(3):
        w = deep(layer[pl.ds(R_QKV + i, EMB, stride=3), :])
        y = fold(dot(x, weight_nn(w))) + layer[R_QKVB + i : R_QKVB + i + 1, :]
        if i == 0:
            y = y * HDIM**-0.5
        save[:, i * WIDE : (i + 1) * WIDE] = y
        qkv.append(y)
    for g, part in enumerate(as_left(qkv[0])):
        left[g] = part
    for g, part in enumerate(as_right(qkv[1])):
        right[g] = part
    v = pair(qkv[2])
    values[0:ROWS, :] = v
    values[ROWS : 2 * ROWS, :] = v
    mixed[...] = jnp.zeros_like(mixed)
    lse[...] = jnp.zeros_like(lse)

    def per_head(h, carry):
        g = lax.div(h, 4)
        lanes = own_lanes(h)
        at_h = jnp.where(iota((1, WIDE), 1) == h, 1.0, 0.0)
        for b in range(ROWS // BLK):
            rows = slice(b * BLK, (b + 1) * BLK)
            s = scores(left[g, rows, :], right[g], h, rows, region)
            top = jnp.max(s, 1, keepdims=True)
            e = jnp.exp(s - top)
            total = jnp.sum(e, 1, keepdims=True)
            o = fold(dot(pair(e), values[...]))
            mixed[rows, :] += o * (lanes / total)
            lse[rows, :] += (top + jnp.log(total)) * at_h
        return carry

    lax.fori_loop(0, HEADS, per_head, 0)
    proj = deep(layer[R_PROJ : R_PROJ + EMB, :])
    return mm(mixed[...], proj) + layer[R_PROJB : R_PROJB + 1, :]


def attention_back(grad, normed, layer, save, lse, mixed, sc, grads, at, region=None):
    left, right, gleft, vright, keys, dq, dkv_t, weights, slopes, q_t, do_t, dmix = sc
    proj = deep(layer[R_PROJ : R_PROJ + EMB, :])
    grads[at + R_PROJ : at + R_PROJ + EMB, :] = mm_tn(rows_t(mixed[...]), grad)[:EMB]
    grads[at + R_PROJB : at + R_PROJB + 1, :] = colsum(grad)
    d_mixed = mm_nt(grad, proj)
    dmix[...] = d_mixed
    q, k, v = (save[:, i * WIDE : (i + 1) * WIDE] for i in range(3))
    for g, part in enumerate(as_left(q)):
        left[g] = part
    for g, part in enumerate(as_right(k)):
        right[g] = part
    for g, part in enumerate(as_left(d_mixed)):
        gleft[g] = part
    for g, part in enumerate(as_right(v)):
        vright[g] = part
    kk = pair(k)
    keys[0:ROWS, :] = kk
    keys[ROWS : 2 * ROWS, :] = kk
    for ref, x in ((q_t, q), (do_t, d_mixed)):
        hi, lo = split(x.T)
        ref[0] = hi
        ref[1] = lo
    dq[...] = jnp.zeros_like(dq)
    dkv_t[...] = jnp.zeros_like(dkv_t)

    def per_head(h, carry):
        g = lax.div(h, 4)
        lanes = own_lanes(h)
        at_h = jnp.where(iota((1, WIDE), 1) == h, 1.0, 0.0)
        mask = head_mask(h, 2 * WIDE).astype(BF16)
        for b in range(ROWS // BLK):
            rows = slice(b * BLK, (b + 1) * BLK)
            s = scores(left[g, rows, :], right[g], h, rows, region)
            level = jnp.sum(lse[rows, :] * at_h, 1, keepdims=True)
            p = jnp.exp(s - level)
            dp = dot_nt(gleft[g, rows, :] * mask, vright[g])
            delta = jnp.sum(dmix[rows, :] * mixed[rows, :] * lanes, 1, keepdims=True)
            ds = p * (dp - delta)
            both = pair(ds)
            weights[rows, :] = pair(p)
            slopes[rows, :] = both
            dq[rows, :] += fold(dot(both, keys[...])) * lanes
        here = pl.multiple_of(h * HDIM, HDIM)
        for i, (t, m) in enumerate(((q_t, slopes), (do_t, weights))):
            lhs = jnp.concatenate([t[0, pl.ds(here, HDIM), :], t[1, pl.ds(here, HDIM), :]], 0)
            out = fold_rows(fold(dot(lhs, m[...])))
            dkv_t[i, pl.ds(here, HDIM), :] = out
        return carry

    lax.fori_loop(0, HEADS, per_head, 0)
    d_q = dq[...] * HDIM**-0.5
    d_k = dkv_t[0].T
    d_v = dkv_t[1].T
    x_t = rows_t(normed)
    d_normed = None
    for i, d in enumerate((d_q, d_k, d_v)):
        grads[pl.ds(at + R_QKV + i, EMB, stride=3), :] = mm_tn(x_t, d)[:EMB]
        grads[at + R_QKVB + i : at + R_QKVB + i + 1, :] = colsum(d)
        part = mm_nt(d, deep(layer[pl.ds(R_QKV + i, EMB, stride=3), :]))
        d_normed = part if d_normed is None else d_normed + part
    return d_normed


def mlp(middle, layer, hpre):
    normed = norm(middle, layer[2:3, :], layer[3:4, :])
    w = deep(hidden_rows(layer, R_HID, EMB))
    pre = mm(normed, w) + hidden_rows(layer, R_HIDB, 1)
    hpre[...] = pre
    out = mm(gelu(pre), layer[R_OUT : R_OUT + HID, :])
    return middle + out + layer[R_OUTB : R_OUTB + 1, :]


def mlp_back(grad, middle, hpre, layer, grads, at):
    hat, inv = norm_stats(middle)
    normed = hat * layer[2:3, :] + layer[3:4, :]
    act, slope = gelu_both(hpre[...])
    grads[at + R_OUTB : at + R_OUTB + 1, :] = colsum(grad)
    grads[at + R_OUT : at + R_OUT + HID, :] = mm_tn(rows_t(grad), act).T
    d_pre = mm_nt(grad, layer[R_OUT : R_OUT + HID, :]) * slope
    put_hidden_rows(grads, at + R_HIDB, 1, colsum(d_pre))
    put_hidden_rows(grads, at + R_HID, EMB, mm_tn(rows_t(normed), d_pre)[:EMB])
    d_normed = mm_nt(d_pre, deep(hidden_rows(layer, R_HID, EMB)))
    grads[at + 2 : at + 3, :] = colsum(d_normed * hat)
    grads[at + 3 : at + 4, :] = colsum(d_normed)
    return grad + norm_back(hat, inv, layer[2:3, :], d_normed)


def pre_norm_back(grad, tokens, layer, grads, at):
    hat, inv = norm_stats(tokens)
    grads[at : at + 1, :] = colsum(grad * hat)
    grads[at + 1 : at + 2, :] = colsum(grad)
    return norm_back(hat, inv, layer[0:1, :], grad)


def region_of(rows, sizes):
    d = lax.shift_right_logical(rows * 1338, 16)
    line = lax.shift_right_logical(rows * 9363, 16)
    places = (d, line - d * WIN, rows - line * WIN)
    starts = (lax.axis_index("slab") * WIN, lax.axis_index("mp") * WIN, 0)
    total = None
    for place, start, blocks in zip(places, starts, sizes + (1,)):
        turned = jnp.where(place < SHIFT, place + FAR, place - SHIFT) + start
        length = WIN * blocks
        part = jnp.where(turned < length - WIN, 0, jnp.where(turned < length - SHIFT, 1, 2))
        total = part if total is None else total * 3 + part
    return total


def put_regions(region, sizes):
    region_rows, region_lanes = region
    region_rows[...] = region_of(iota((ROWS, WIDE), 0), sizes).astype(F32)
    region_lanes[...] = region_of(iota((8, ROWS), 1), sizes).astype(F32)


def send_parts(ref, a, b, c):
    far = FAR * WIN
    near = SHIFT * WIN
    for d in range(SHIFT):
        base = d * PLANE
        c[d * near : (d + 1) * near, :] = ref[base : base + near, :]
        a[d * far : (d + 1) * far, :] = ref[base + near : base + PLANE, :]
    for d in range(FAR):
        base = (d + SHIFT) * PLANE
        b[d * near : (d + 1) * near, :] = ref[base : base + near, :]


def take_parts(own, a, b, c, out):
    far = FAR * WIN
    near = SHIFT * WIN
    for d in range(WIN):
        base = d * PLANE
        if d < SHIFT:
            out[base : base + near, :] = c[d * near : (d + 1) * near, :]
            out[base + near : base + PLANE, :] = a[d * far : (d + 1) * far, :]
        else:
            e = d - SHIFT
            out[base : base + near, :] = b[e * near : (e + 1) * near, :]
            out[base + near : base + PLANE, :] = own[base + near : base + PLANE, :]
    out[VOX:, :] = jnp.zeros((ROWS - VOX, WIDE), F32)


def span_of(groups):
    low, high = groups
    first = 3 * low // 8 * 8
    last = -(-3 * high // 8) * 8
    return first, min(last, NPARAM // WIDE // 8 * 8) - first


def copied(params, groups, flat, sem):
    first, rows = span_of(groups)
    size = rows * WIDE
    return pltpu.make_async_copy(
        params.at[pl.ds(first * WIDE, size)], flat.at[pl.ds(0, size)], sem
    )


def relay(groups, flat, out, square, last=None):
    low, high = groups
    first, rows = span_of(groups)
    square[0:rows, :] = flat[0 : rows * WIDE].reshape(rows, WIDE)
    if last is not None:
        square[rows : rows + 24, :] = jnp.zeros((24, WIDE), F32)
        square[rows : rows + 1, 0 : last.shape[0]] = last[...].reshape(1, last.shape[0])
    skip = 3 * low - first
    n = high - low
    parts = three_to_four([square[pl.ds(skip + c, n, stride=3), :] for c in range(3)])
    for c in range(4):
        out[pl.ds(c, n, stride=4), :] = parts[c]


FIRST_SPANS = ((0, 98), (98, 392))
LAYER_SPANS = ((389, 681), (680, 972))
CONV_SPANS = ((971, 1620), (1620, GROUPS))


def prep_kernel(spans, params, *refs, last=None):
    outs, (flats, square, sems) = refs[: len(spans)], refs[-3:]
    for i, groups in enumerate(spans):
        copied(params, groups, flats[i], sems.at[i]).start()
    for i, groups in enumerate(spans):
        copied(params, groups, flats[i], sems.at[i]).wait()
        relay(groups, flats[i], outs[i], square, last if i == len(spans) - 1 else None)


def head_picks():
    width = HEAD_ROWS * WIDE
    place = iota((WIDE, width), 1) - HEAD_LANE
    row = iota((WIDE, width), 0)
    here = (place >= row * CLASSES) & (place < (row + 1) * CLASSES) & (row <= EMB)
    place = iota((width, WIDE), 0) - HEAD_LANE
    col = iota((width, WIDE), 1)
    row = lax.shift_right_logical(place * 4682, 16)
    there = (place - row * CLASSES == col) & (place >= 0)
    return jnp.where(here, 1.0, 0.0), jnp.where(there, 1.0, 0.0).astype(BF16)


def prep_conv_kernel(last, params, conv0, conv1, head, *scratch):
    prep_kernel(CONV_SPANS, params, conv0, conv1, *scratch, last=last)
    square = scratch[1]
    first, _ = span_of(CONV_SPANS[1])
    row = jnp.concatenate(
        [square[HEAD_ROW + i - first : HEAD_ROW + i - first + 1, :] for i in range(HEAD_ROWS)], 1
    )
    here, there = head_picks()
    hi, lo = split(here * row)
    head[...] = dot(hi, there) + dot(lo, there)


def head_rows(d_head, out, at):
    here, there = head_picks()
    hi, lo = split(d_head)
    spread = (dot_nt(hi, there) + dot_nt(lo, there)) * here
    row = colsum(spread)
    for i in range(HEAD_ROWS):
        out[at + i : at + i + 1, :] += row[:, i * WIDE : (i + 1) * WIDE]


class Rows:
    def __init__(self, ref, at):
        self.ref, self.at = ref, at

    def __getitem__(self, key):
        rows, lanes = key
        if isinstance(rows, slice):
            rows = slice(rows.start + self.at, rows.stop + self.at)
        else:
            rows = pl.ds(rows.start + self.at, rows.size, stride=rows.stride)
        return self.ref[rows, lanes]


def merged_norm(x):
    mean = jnp.sum(x, 1, keepdims=True) * (1.0 / MERGE)
    centred = x - mean
    var = jnp.sum(centred * centred, 1, keepdims=True) * (1.0 / MERGE)
    return centred * lax.rsqrt(var + eps_norm)


def first_kernel(
    feats, merge, lay0,
    dense, tok0, save, lse, mixed, middle, hpre, tok1, ahead, pa, pb, pc,
    left, right, values,
):
    dense[VOX:, :] = jnp.zeros((ROWS - VOX, MERGE), F32)
    for line in range(PLANE):
        dense[line * WIN : (line + 1) * WIN, :] = feats[line]
    hat = merged_norm(dense[...])
    normed = hat * hidden_rows(merge, 0, 1) + hidden_rows(merge, 4, 1)
    tokens = mm(normed, merge[8 : 8 + MERGE, :])
    tok0[...] = tokens
    layer = Rows(lay0, 0)
    normed = norm(tokens, layer[0:1, :], layer[1:2, :])
    attended = attention(normed, layer, save, lse, mixed, left, right, values)
    mid = tokens + attended
    middle[...] = mid
    tokens = mlp(mid, layer, hpre)
    tok1[...] = tokens
    ahead[...] = norm(tokens, layer[1165:1166, :], layer[1166:1167, :])
    send_parts(ahead, pa, pb, pc)


def shifted_kernel(
    sizes,
    own, pa, pb, pc, lay1,
    window, save, lse, mixed, out, qa, qb, qc,
    region_rows, region_lanes, left, right, values,
):
    put_regions((region_rows, region_lanes), sizes)
    take_parts(own, pa, pb, pc, window)
    out[...] = attention(
        window[...], Rows(lay1, 1), save, lse, mixed, left, right, values,
        (region_rows, region_lanes),
    )
    send_parts(out, qa, qb, qc)


def to_lines(ref, out):
    for line in range(PLANE):
        out[line, 0:WIN, :] = ref[line * WIN : (line + 1) * WIN, :]
        out[line, WIN:8, :] = jnp.zeros((8 - WIN, WIDE), F32)


def from_lines(ref, out):
    out[VOX:, :] = jnp.zeros((ROWS - VOX, WIDE), F32)
    for line in range(PLANE):
        out[line * WIN : (line + 1) * WIN, :] = ref[line, 0:WIN, :]


def send_sides(lines, low_d, high_d, low_h, high_h):
    low_d[...] = lines[0 : 2 * WIN]
    high_d[...] = lines[(WIN - 2) * WIN :]
    for d in range(WIN):
        low_h[2 * d : 2 * d + 2] = lines[d * WIN : d * WIN + 2]
        high_h[2 * d : 2 * d + 2] = lines[d * WIN + WIN - 2 : (d + 1) * WIN]


def second_kernel(
    tok1, own, qa, qb, qc, lay1, lay2,
    mid1, hpre1, tok2, save, lse, mixed, mid2, hpre2, lines,
    s0, s1, s2, s3,
    attended, left, right, values,
):
    take_parts(own, qa, qb, qc, attended)
    mid = tok1[...] + attended[...]
    mid1[...] = mid
    tokens = mlp(mid, Rows(lay1, 1), hpre1)
    tok2[...] = tokens
    layer = Rows(lay2, 2)
    normed = norm(tokens, layer[0:1, :], layer[1:2, :])
    mid = tokens + attention(normed, layer, save, lse, mixed, left, right, values)
    mid2[...] = mid
    attended[...] = mlp(mid, layer, hpre2)
    to_lines(attended, lines)
    send_sides(lines, s0, s1, s2, s3)


def grown_lines(own, low_d, high_d, low_h, high_h, out):
    out[...] = jnp.zeros_like(out)
    for d in range(WIN):
        out[d + 2, 2 : 2 + WIN] = own[d * WIN : (d + 1) * WIN]
    for d in range(2):
        out[d, 2 : 2 + WIN] = low_d[d * WIN : (d + 1) * WIN]
        out[d + 9, 2 : 2 + WIN] = high_d[d * WIN : (d + 1) * WIN]
    for d in range(11):
        out[d, 0:2] = low_h[2 * d : 2 * d + 2]
        out[d, 9:11] = high_h[2 * d : 2 * d + 2]


def put_marks(labels, valid, out):
    across = iota((8, WIN), 1) == iota((8, WIN), 0)
    classes = iota((8, WIDE), 1) - EMB
    for d in range(WIN):
        code = jnp.where(valid[d] == 1, labels[d], -1 - EMB - WIDE)
        code = code.astype(F32)
        for h in range(WIN):
            line = jnp.where(across, code[h : h + 1, :], 0.0)
            column = jnp.sum(line, 1, keepdims=True)
            mark = jnp.where(column == classes.astype(F32), 1.0, 0.0)
            out[d * WIN + h] = jnp.where(iota((8, WIDE), 0) < WIN, mark, 0.0)


def taps(source, first_plane, planes, first_line, lines, out):
    def per_plane(d, carry):
        for c in range(3):
            for b in range(3):
                x = source[d + first_plane, first_line + b : first_line + b + lines]
                if c != 1:
                    x = roll(x, 1 if c == 0 else 7, 1)
                x = pair(x.reshape(lines * 8, WIDE))
                at = pl.multiple_of(d * (lines * 8), lines * 8)
                t = b * 3 + c
                out[pl.ds(at, lines * 8), t * 256 : (t + 1) * 256] = x
        return carry

    lax.fori_loop(0, planes, per_plane, 0)


def tap_weights(ref, at, out):
    def per_tap(i, carry):
        w = deep(ref[pl.ds(i * EMB + at, EMB), :])
        out[pl.ds(pl.multiple_of(i * 256, 256), 256), :] = weight_nn(w)
        return carry

    lax.fori_loop(0, 27, per_tap, 0)


def tap_weights_back(ref, at, out):
    def per_tap(i, carry):
        w = deep(ref[pl.ds((26 - i) * EMB + at, EMB), :]).T
        out[pl.ds(pl.multiple_of(i * 256, 256), 256), :] = weight_nn(w)
        return carry

    lax.fori_loop(0, 27, per_tap, 0)


def conv(side, weights, planes, pitch, at_once, put):
    rows = at_once * pitch
    for start in range(0, planes, at_once):
        total = None
        for a in range(3):
            low = (start + a) * pitch
            part = dot(side[low : low + rows, :], weights[a * 2304 : (a + 1) * 2304, :])
            total = part if total is None else total + part
        put(start, fold(total))


def conv_weight_grad(side, grad_rows, pitch, out, at):
    rows = 512
    g = jnp.concatenate([grad_rows, jnp.zeros((rows - grad_rows.shape[0], WIDE), F32)], 0)
    left = rows_t(g)
    for a in range(3):
        for bc in range(9):
            y = dot(left, side[a * pitch : a * pitch + rows, bc * 256 : (bc + 1) * 256])
            y = fold_rows(fold(y)).T
            t = a * 9 + bc
            out[at + t * EMB : at + (t + 1) * EMB, :] = y[:EMB]


def volume_mask(sizes, planes, lines, reach, real_lines):
    slab, row = lax.axis_index("slab"), lax.axis_index("mp")
    ends = (slab == 0, slab == sizes[0] - 1, row == 0, row == sizes[1] - 1)
    shape = (planes, lines, 8, WIDE)
    d, h, w = iota(shape, 0), iota(shape, 1), iota(shape, 2)
    low_d = jnp.where(ends[0], reach, 0)
    high_d = jnp.where(ends[1], planes - reach, planes)
    low_h = jnp.where(ends[2], reach, 0)
    high_h = jnp.where(ends[3], real_lines - reach, real_lines)
    inside = (d >= low_d) & (d < high_d) & (h >= low_h) & (h < high_h) & (w < WIN)
    return jnp.where(inside, 1.0, 0.0)


def conv_kernel(
    sizes,
    own, s0, s1, s2, s3, labels, valid, conv0, conv1,
    grown, pre, tok, stats, t0, t1, t2, t3,
    act, side, side_own, weights, marks,
):
    grown_lines(own, s0, s1, s2, s3, grown)
    put_marks(labels, valid, marks)
    tap_weights(conv0, 3, weights)
    taps(grown, 0, 11, 0, 10, side)
    bias0 = conv0[3 + TAP_ROWS : 4 + TAP_ROWS, :]
    inside = volume_mask(sizes, 9, 10, 1, 9)

    def put(start, y):
        z = (y + bias0).reshape(3, 10, 8, WIDE)
        pre[start : start + 3] = z
        act[start : start + 3] = gelu(z) * inside[start : start + 3]

    conv(side, weights, 9, 80, 3, put)
    tap_weights(conv1, 0, weights)
    taps(act, 0, 9, 0, 8, side_own)
    bias1 = conv1[TAP_ROWS : TAP_ROWS + 1, :]
    sums = []

    def put_own(start, y):
        y = (y + bias1).reshape(WIN, 8, 8, WIDE)[:, 0:WIN]
        y = y + own[...].reshape(WIN, WIN, 8, WIDE)
        y = jnp.where(iota(y.shape, 2) < WIN, y, 0.0).reshape(PLANE, 8, WIDE)
        tok[...] = y + marks[...]
        send_sides(tok, t0, t1, t2, t3)
        flat = y.reshape(PLANE * 8, WIDE)
        sums.append(colsum(flat))
        sums.append(colsum(flat * flat))

    conv(side_own, weights, WIN, 64, WIN, put_own)
    count = jnp.sum(marks[...].reshape(PLANE * 8, WIDE))
    row = iota((8, WIDE), 0)
    stats[...] = (
        jnp.where(row == 0, sums[0], 0.0)
        + jnp.where(row == 1, sums[1], 0.0)
        + jnp.where(row == 2, count, 0.0)
    )


def head_kernel(
    voxels,
    own, s0, s1, s2, s3, sums, conv1, head_w,
    grown, slope_out, stats, d_head, d_rows,
):
    grown_lines(own, s0, s1, s2, s3, grown)
    rows = 11 * 12 * 8
    both = grown[...].reshape(rows, WIDE)
    lane = iota((rows, WIDE), 1)
    tokens = jnp.where(lane < EMB, both, 0.0)
    target = jnp.where(lane < CLASSES, roll(both, WIDE - EMB, 1), 0.0)
    live = jnp.sum(target, 1, keepdims=True)
    count = F32(voxels)
    average = sums[0:1, :] / count
    spread = sums[1:2, :] / count - average * average
    inv = lax.rsqrt(spread + eps_norm)
    gain = conv1[TAP_ROWS + 1 : TAP_ROWS + 2, :]
    bias = conv1[TAP_ROWS + 2 : TAP_ROWS + 3, :]
    hat = (tokens - average) * inv
    act, slope = gelu_both(hat * gain + bias)
    act = jnp.where(lane == EMB, 1.0, act)
    w = head_w[...]
    logits = mm(act, w)
    logits = jnp.where(lane < CLASSES, logits, -1e30)
    top = jnp.max(logits, 1, keepdims=True)
    e = jnp.exp(logits - top)
    total = jnp.sum(e, 1, keepdims=True)
    logp = logits - top - jnp.log(total)
    scale = 1.0 / sums[2:3, 0:1]
    d_logits = (e / total * live - target) * scale
    d_normed = jnp.where(lane < EMB, mm_nt(d_logits, w) * slope, 0.0)
    d_tokens = d_normed * gain * inv
    slope_out[...] = d_tokens.reshape(11, 12, 8, WIDE)

    def own_rows(x):
        x = x.reshape(11, 12, 8, WIDE)[2:9, 2:9]
        x = jnp.where(iota(x.shape, 2) < WIN, x, 0.0)
        return x.reshape(PLANE * 8, WIDE)

    loss = -jnp.sum(own_rows(target * jnp.where(lane < CLASSES, logp, 0.0)))
    own_d = own_rows(d_logits)
    own_n = own_rows(d_normed)
    own_hat = own_rows(hat)
    zeros = jnp.zeros((512 - PLANE * 8, WIDE), F32)
    left = rows_t(jnp.concatenate([own_d, zeros], 0))
    d_head[...] = mm_tn(left, jnp.concatenate([own_rows(act), zeros], 0)).T
    d_gain = colsum(own_n * own_hat)
    d_bias = colsum(own_n)
    d_average = -d_bias * gain * inv
    d_spread = d_gain * gain * inv * inv * -0.5
    d_two = d_spread / count
    d_one = (d_average - 2.0 * average * d_spread) / count
    row = iota((8, WIDE), 0)
    live_lane = iota((8, WIDE), 1) < EMB
    stats[...] = (
        jnp.where((row == 0) & live_lane, d_one, 0.0)
        + jnp.where((row == 1) & live_lane, d_two, 0.0)
        + jnp.where(row == 2, loss, 0.0)
    )
    d_rows[...] = (
        jnp.where(row == 0, d_gain, 0.0)
        + jnp.where(row == 1, d_bias, 0.0)
    )


def conv_back_kernel(
    sizes,
    tok, slope, sums, grown, pre, conv0, conv1, d_rows, d_head,
    d_own, keep, send, carry, seam,
    grads, dgrown, act, side, side_own, weights, flat,
):
    lane = iota((11, 12, 8, WIDE), 3)
    inside = volume_mask(sizes, 11, 12, 2, 11)
    steady = sums[0:1, :].reshape(1, 1, 1, WIDE)
    rising = 2.0 * sums[1:2, :].reshape(1, 1, 1, WIDE)
    d_tok = slope[...] + jnp.where(lane < EMB, (steady + tok[...] * rising) * inside, 0.0)
    dgrown[...] = d_tok
    grads[5191:, :] = jnp.zeros((45, WIDE), F32)
    grads[0:8, :] = jnp.zeros((8, WIDE), F32)
    grads[5189:5191, :] = d_rows[0:2, :]
    own = dgrown[2:9, 2:10]
    line = iota(own.shape, 1)
    own = jnp.where(line < WIN, own, 0.0).reshape(WIN * 64, WIDE)
    grads[5188:5189, :] = colsum(own)

    near = volume_mask(sizes, 9, 10, 1, 9)
    act[0:9] = gelu(pre[...]) * near
    act[9:10] = jnp.zeros((1, 10, 8, WIDE), F32)
    taps(act, 0, 10, 0, 8, side_own)
    conv_weight_grad(side_own, own, 64, grads, 2596)
    tap_weights_back(conv1, 0, weights)
    taps(dgrown, 0, 11, 0, 10, side)

    def put(start, y):
        _, s = gelu_both(pre[start : start + 3])
        z = y.reshape(3, 10, 8, WIDE) * s * near[start : start + 3]
        act[start : start + 3] = z

    conv(side, weights, 9, 80, 3, put)

    own = act[1:8, 1:9]
    line = iota(own.shape, 1)
    own = jnp.where(line < WIN, own, 0.0).reshape(WIN * 64, WIDE)
    grads[2595:2596, :] = colsum(own)
    taps(grown, 1, 10, 1, 8, side_own)
    conv_weight_grad(side_own, own, 64, grads, 3)
    carry[...] = grads[0:24, :]
    flat[3 * (GROUPS - CUTS[3]) :, :] = jnp.zeros((flat.shape[0] - 3912, WIDE), F32)
    flatten(grads, 20, GROUPS - CUTS[3], flat)
    start = 3 * CUTS[3]
    head_rows(d_head[...], flat, HEAD_ROW - start)
    seam[...] = flat[0 : LATE_ROWS - start, :]
    core = jnp.bitwise_and(lax.axis_index("mp"), 1)
    for out, half in ((keep, core), (send, 1 - core)):
        n = keep.shape[0]
        at = pl.multiple_of(LATE_ROWS - start + half * n, 8)
        out[...] = flat[pl.ds(at, n), :]
    tap_weights_back(conv0, 3, weights)
    taps(act, 0, 9, 0, 8, side_own)

    def put_own(start, y):
        y = y.reshape(WIN, 8, 8, WIDE)[:, 0:WIN] + dgrown[2:9, 2:9]
        y = jnp.where(iota(y.shape, 2) < WIN, y, 0.0)
        d_own[...] = y.reshape(PLANE, 8, WIDE)

    conv(side_own, weights, WIN, 64, WIN, put_own)


def back_two_kernel(
    d_own, carry, lay1, lay2, tok2, save, lse, mixed, mid2, hpre2, mid1, hpre1,
    d_mid, grads1, flat, carry2, pa, pb, pc,
    grads, dense, *sc,
):
    from_lines(d_own, dense)
    layer = Rows(lay2, 2)
    grads[0:8, :] = jnp.zeros((8, WIDE), F32)
    d = mlp_back(dense[...], mid2[...], hpre2, layer, grads, 2)
    tokens = tok2[...]
    normed = norm(tokens, layer[0:1, :], layer[1:2, :])
    d_normed = attention_back(d, normed, layer, save, lse, mixed, sc, grads, 2)
    d = d + pre_norm_back(d_normed, tokens, layer, grads, 2)
    grads[1167:1184, :] = carry[3:20, :]
    flatten(grads, 32, CUTS[3] - CUTS[2], flat)
    carry2[...] = grads[0:32, :]
    layer = Rows(lay1, 1)
    d = mlp_back(d, mid1[...], hpre1, layer, grads1, 1)
    d_mid[...] = d
    send_parts(d_mid, pa, pb, pc)


def back_shifted_kernel(
    sizes,
    own, pa, pb, pc, lay1, window, save, lse, mixed, grads1, carry2,
    d_window, flat, carry1, qa, qb, qc,
    region_rows, region_lanes, grads, grad, *sc,
):
    put_regions((region_rows, region_lanes), sizes)
    take_parts(own, pa, pb, pc, grad)
    grads[0:1168, :] = grads1[...]
    grads[0:3, :] = jnp.zeros((3, WIDE), F32)
    d_window[...] = attention_back(
        grad[...], window[...], Rows(lay1, 1), save, lse, mixed, sc, grads, 1,
        (region_rows, region_lanes),
    )
    send_parts(d_window, qa, qb, qc)
    grads[1166:1196, :] = carry2[2:32, :]
    flatten(grads, 12, CUTS[2] - CUTS[1], flat)
    carry1[...] = grads[0:16, :]


def back_first_kernel(
    sizes,
    d_mid, own, qa, qb, qc, tok1, lay0, lay1, merge, dense, tok0, save, lse, mixed, middle, hpre,
    carry1, flat1, flat2, seam,
    keep, send,
    flat, grads, grad, *sc,
):
    take_parts(own, qa, qb, qc, grad)
    grads[1556:1572, :] = carry1[...]
    d = d_mid[...] + pre_norm_back(grad[...], tok1[...], Rows(lay1, 1), grads, 1557)
    layer = Rows(lay0, 0)
    at = MERGE_ROWS
    d = mlp_back(d, middle[...], hpre, layer, grads, at)
    tokens = tok0[...]
    normed = norm(tokens, layer[0:1, :], layer[1:2, :])
    d_normed = attention_back(d, normed, layer, save, lse, mixed, sc, grads, at)
    d = d + pre_norm_back(d_normed, tokens, layer, grads, at)
    live = iota((ROWS, WIDE), 0) < VOX
    d = jnp.where(live, d, 0.0)
    hat = merged_norm(dense[...])
    gain = hidden_rows(merge, 0, 1)
    bias = hidden_rows(merge, 4, 1)
    w = merge[8 : 8 + MERGE, :]
    put_hidden_rows(grads, 8 - 8, 1, jnp.zeros((1, MERGE), F32))
    grads[8 : 8 + MERGE, :] = mm_tn(rows_t(d), hat * gain + bias).T
    d_hat = mm_nt(d, w)
    put_hidden_rows(grads, 0, 1, colsum(d_hat * hat))
    put_hidden_rows(grads, 4, 1, colsum(d_hat))
    flatten(grads, 0, CUTS[1], flat)
    at = 0
    for cut, part in ((CUTS[1], flat1), (CUTS[2], flat2), (CUTS[3], seam)):
        at = 3 * cut
        flat[at : at + part.shape[0], :] = part[...]
    at += seam.shape[0]
    if flat.shape[0] > at:
        flat[at:, :] = jnp.zeros((flat.shape[0] - at, WIDE), F32)
    scatter(sizes, flat, 0, keep, send)


def radices(count):
    steps = [2]
    left = count // 2
    while left > 1:
        steps.append(4 if left >= 4 else 2)
        left //= steps[-1]
    return steps


def block_rows(rows, count):
    return -(-rows // (8 * count)) * 8


def own_number(sizes):
    return lax.axis_index("slab") * sizes[1] + lax.axis_index("mp")


def place_in_half(distance, count):
    place = 0
    shift = 1
    for radix in radices(count)[1:]:
        digit = jnp.bitwise_and(lax.shift_right_logical(distance, shift), radix - 1)
        place = place * radix + digit
        shift += radix.bit_length() - 1
    return place


def scatter(sizes, source, first, keep, send):
    count = sizes[0] * sizes[1]
    rows = keep.shape[0] * 2 // count
    me = own_number(sizes)
    odd = jnp.bitwise_and(me, 1)

    def per_pair(t, carry):
        for block, out in ((2 * t + odd, keep), (2 * t + 1 - odd, send)):
            place = place_in_half(jnp.bitwise_xor(block, me), count)
            at = pl.multiple_of(first + block * rows, 8)
            to = pl.multiple_of(place * rows, 8)
            out[pl.ds(to, rows), :] = source[pl.ds(at, rows), :]
        return carry

    lax.fori_loop(0, count // 2, per_pair, 0)


def traded(value, distance, count):
    pairs = [(i, i ^ distance) for i in range(count)]
    return lax.ppermute(value, ("slab", "mp"), pairs)


def summed_blocks(keep, send, count):
    steps = radices(count)
    got = [keep, traded(send, 1, count)]
    shift = 1
    for radix in steps[1:]:
        total = sum(got[1:], got[0])
        rows = total.shape[0] // radix
        parts = [total[k * rows : (k + 1) * rows] for k in range(radix)]
        got = parts[:1] + [traded(parts[k], k << shift, count) for k in range(1, radix)]
        shift += radix.bit_length() - 1
    own = sum(got[1:], got[0])
    for radix in reversed(steps[1:]):
        shift -= radix.bit_length() - 1
        got = [own] + [traded(own, k << shift, count) for k in range(1, radix)]
        own = jnp.concatenate(got, 0)
    return own, traded(own, 1, count)


def summed_halves(keep, send, count):
    groups = [[i for i in range(count) if i % 2 == core] for core in range(2)]
    own = keep + traded(send, 1, count)
    own = lax.psum(own, ("slab", "mp"), axis_index_groups=groups)
    return own, traded(own, 1, count)


def grouped_sum(value, sizes):
    value = lax.psum(value, "mp")
    size = sizes[0]
    low = 2
    while low <= size:
        radix = 2 if low == 2 else min(4, size // (low // 2))
        step = low // 2
        groups = [
            [base + k * step for k in range(radix)]
            for base in range(size)
            if (base // step) % radix == 0
        ]
        value = lax.psum(value, "slab", axis_index_groups=groups)
        low *= radix
    return value


def exchanged_sum(value, count):
    shift = 0
    for radix in radices(count):
        got = [value] + [traded(value, k << shift, count) for k in range(1, radix)]
        while len(got) > 1:
            got = [got[i] + got[i + 1] for i in range(0, len(got), 2)]
        value = got[0]
        shift += radix.bit_length() - 1
    return value


PIECE = 65536


def adamw_kernel(
    sizes,
    late, late_other, early, early_other, tail, sums, params, first, second,
    new_params, new_first, new_second, loss, valid, norm_out,
    grad, scale_ref,
):
    count = sizes[0] * sizes[1]
    step = pl.program_id(0)

    @pl.when(step == 0)
    def gather():
        me = own_number(sizes)
        odd = jnp.bitwise_and(me, 1)
        total = jnp.zeros((8, WIDE), F32)
        for ref in (late, late_other, early, early_other):
            x = ref[...]
            total = total + jnp.sum((x * x).reshape(-1, 8, WIDE), 0)
        norm = jnp.sqrt(jnp.sum(total))
        loss[0] = jnp.sum(tail[2:3, 0:1])
        valid[0] = jnp.sum(sums[2:3, 0:1])
        norm_out[0] = norm
        scale_ref[0] = jnp.minimum(1.0, clip_norm / (norm + 1e-06))
        rows = late.shape[0] * 2 // count

        def late_block(block, carry):
            distance = jnp.bitwise_xor(block, me)
            at = pl.ds(pl.multiple_of(place_in_half(distance, count) * rows, 8), rows)
            near = jnp.bitwise_and(distance, 1) == 0
            to = pl.ds(pl.multiple_of(block * rows, 8), rows)
            grad[to, :] = jnp.where(near, late[at, :], late_other[at, :])
            return carry

        lax.fori_loop(0, LATE_ROWS // rows, late_block, 0)
        half = early.shape[0]
        part = math.gcd(half, 128)

        def early_block(i, carry):
            at = pl.ds(pl.multiple_of(i * part, 8), part)
            for k in range(2):
                x = jnp.where(odd == k, early[at, :], early_other[at, :])
                to = pl.multiple_of(LATE_ROWS + k * half + i * part, 8)
                grad[pl.ds(to, part), :] = x
            return carry

        lax.fori_loop(0, half // part, early_block, 0)

    rows = PIECE // WIDE
    g = grad[pl.ds(pl.multiple_of(step * rows, 8), rows), :].reshape(PIECE) * scale_ref[0]
    one = beta_one * first[...] + (1.0 - beta_one) * g
    two = beta_two * second[...] + (1.0 - beta_two) * g * g
    new_first[...] = one
    new_second[...] = two
    one = one * (1.0 / (1.0 - beta_one**STEP))
    two = two * (1.0 / (1.0 - beta_two**STEP))
    old = params[...]
    new_params[...] = old - learn_rate * (one / (jnp.sqrt(two) + adam_eps) + decay_rate * old)


def adamw(sizes, parts, arrays):
    pieces = -(-NPARAM // PIECE)
    piece = pl.BlockSpec((PIECE,), lambda i: (i,))
    smem = pl.BlockSpec(memory_space=pltpu.SMEM)
    return pl.pallas_call(
        functools.partial(adamw_kernel, sizes),
        grid=(pieces,),
        out_shape=[arr(NPARAM)] * 3 + [arr(1)] * 3,
        in_specs=[pl.BlockSpec(p.shape, lambda i: (0, 0)) for p in parts] + [piece] * 3,
        out_specs=[piece] * 3 + [smem] * 3,
        scratch_shapes=[
            pltpu.VMEM((pieces * PIECE // WIDE, WIDE), F32),
            pltpu.SMEM((1,), F32),
        ],
        compiler_params=pltpu.CompilerParams(vmem_limit_bytes=VMEM),
        cost_estimate=pl.CostEstimate(
            flops=8 * 10**9, bytes_accessed=0, transcendentals=0
        ),
        name="adamw",
    )(*parts, *arrays)


def arr(*shape):
    return jax.ShapeDtypeStruct(shape, F32)


def call(kernel, outs, scratch, *args, name=None, us=1.0, far=()):
    vmem = pl.BlockSpec(memory_space=pltpu.VMEM)
    return pl.pallas_call(
        kernel,
        out_shape=list(outs),
        in_specs=[vmem] * len(args) + [pl.BlockSpec(memory_space=pl.ANY)] * len(far),
        out_specs=[vmem] * len(outs),
        scratch_shapes=list(scratch),
        compiler_params=pltpu.CompilerParams(vmem_limit_bytes=VMEM),
        cost_estimate=pl.CostEstimate(
            flops=int(us * 1.15e9), bytes_accessed=0, transcendentals=0
        ),
        name=name,
    )(*args, *far)


SQUARE = arr(ROWS, WIDE)
SAVE = arr(ROWS, 3 * WIDE)
FORWARD = [
    pltpu.VMEM((2, ROWS, 2 * WIDE), BF16),
    pltpu.VMEM((2, ROWS, 2 * WIDE), BF16),
    pltpu.VMEM((2 * ROWS, 2 * WIDE), BF16),
]
BACKWARD = [
    pltpu.VMEM((2, ROWS, 2 * WIDE), BF16),
    pltpu.VMEM((2, ROWS, 2 * WIDE), BF16),
    pltpu.VMEM((2, ROWS, 2 * WIDE), BF16),
    pltpu.VMEM((2, ROWS, 2 * WIDE), BF16),
    pltpu.VMEM((2 * ROWS, 2 * WIDE), BF16),
    pltpu.VMEM((ROWS, WIDE), F32),
    pltpu.VMEM((2, WIDE, ROWS), F32),
    pltpu.VMEM((ROWS, 2 * ROWS), BF16),
    pltpu.VMEM((ROWS, 2 * ROWS), BF16),
    pltpu.VMEM((2, WIDE, ROWS), BF16),
    pltpu.VMEM((2, WIDE, ROWS), BF16),
    pltpu.VMEM((ROWS, WIDE), F32),
]
PARTS = [arr(ROWS_A, WIDE), arr(ROWS_B, WIDE), arr(ROWS_C, WIDE)]


def passed(parts, steps, sizes):
    slabs, rows = sizes
    moved = []
    for part, (ds, dm) in zip(parts, ((1, 0), (0, 1), (1, 1))):
        pairs = []
        for s in range(slabs):
            for m in range(rows):
                target = ((s + steps * ds) % slabs) * rows + (m + steps * dm) % rows
                pairs.append((s * rows + m, target))
        moved.append(lax.ppermute(part, ("slab", "mp"), pairs))
    return moved


SIDES = [arr(2 * WIN, 8, WIDE)] * 4


def beside(sides, sizes):
    slabs, rows = sizes
    low_d, high_d, low_h, high_h = sides
    up = [(i, i + 1) for i in range(slabs - 1)]
    down = [(i + 1, i) for i in range(slabs - 1)]
    before = lax.ppermute(high_d, "slab", up)
    after = lax.ppermute(low_d, "slab", down)

    def column(own, start):
        ends = [
            x.reshape(2, WIN, 8, WIDE)[:, start : start + 2].reshape(4, 8, WIDE)
            for x in (before, after)
        ]
        return jnp.concatenate([ends[0], own, ends[1]], 0)

    up = [(i, i + 1) for i in range(rows - 1)]
    down = [(i + 1, i) for i in range(rows - 1)]
    left = lax.ppermute(column(high_h, WIN - 2), "mp", up)
    right = lax.ppermute(column(low_h, 0), "mp", down)
    return before, after, left, right


REGION = [pltpu.VMEM((ROWS, WIDE), F32), pltpu.VMEM((8, ROWS), F32)]


def on_device(sizes, feats, labels, valid, params, moment_one, moment_two):
    slabs, rows = sizes
    count = slabs * rows

    def room(spans):
        sizes = [(span_of(groups)[1] + 8) * WIDE for groups in spans]
        return [
            [pltpu.VMEM((size,), F32) for size in sizes],
            pltpu.VMEM((2048, WIDE), F32),
            pltpu.SemaphoreType.DMA((len(spans),)),
        ]

    merge, lay0 = call(
        functools.partial(prep_kernel, FIRST_SPANS),
        [arr(MERGE_ROWS, WIDE), arr(1176, WIDE)],
        room(FIRST_SPANS),
        name="prep_first", us=2.0, far=(params,),
    )
    lay1, lay2 = call(
        functools.partial(prep_kernel, LAYER_SPANS),
        [arr(1168, WIDE)] * 2,
        room(LAYER_SPANS),
        name="prep_layers", us=2.0, far=(params,),
    )
    conv0, conv1, head_w = call(
        prep_conv_kernel,
        [arr(2596, WIDE), arr(2640, WIDE), arr(WIDE, WIDE)],
        room(CONV_SPANS),
        params[NPARAM // WIDE * WIDE :],
        name="prep_conv", us=3.0, far=(params,),
    )

    dense, tok0, save0, lse0, mixed0, mid0, hpre0, tok1, ahead, *parts = call(
        first_kernel,
        [arr(ROWS, MERGE), SQUARE, SAVE, SQUARE, SQUARE, SQUARE, arr(ROWS, HID), SQUARE, SQUARE]
        + PARTS,
        FORWARD,
        feats.reshape(PLANE, WIN, MERGE), merge, lay0,
        name="first", us=9.5,
    )
    parts = passed(parts, -1, sizes)
    window, save1, lse1, mixed1, out1, *parts = call(
        functools.partial(shifted_kernel, sizes),
        [SQUARE, SAVE, SQUARE, SQUARE, SQUARE] + PARTS,
        REGION + FORWARD,
        ahead, *parts, lay1,
        name="shifted", us=7.5,
    )
    parts = passed(parts, 1, sizes)
    mid1, hpre1, tok2, save2, lse2, mixed2, mid2, hpre2, lines, *sides = call(
        second_kernel,
        [SQUARE, arr(ROWS, HID), SQUARE, SAVE, SQUARE, SQUARE, SQUARE, arr(ROWS, HID)]
        + [arr(PLANE, 8, WIDE)] + SIDES,
        [pltpu.VMEM((ROWS, WIDE), F32)] + FORWARD,
        tok1, out1, *parts, lay1, lay2,
        name="second", us=9.5,
    )
    sides = beside(sides, sizes)
    grown, pre, tok3, sums, *tok_sides = call(
        functools.partial(conv_kernel, sizes),
        [arr(11, 12, 8, WIDE), arr(9, 10, 8, WIDE), arr(PLANE, 8, WIDE), arr(8, WIDE)] + SIDES,
        [
            pltpu.VMEM((9, 10, 8, WIDE), F32),
            pltpu.VMEM((880, 2304), BF16),
            pltpu.VMEM((576, 2304), BF16),
            pltpu.VMEM((27 * 256, 256), BF16),
            pltpu.VMEM((PLANE, 8, WIDE), F32),
        ],
        lines, *sides, labels, valid, conv0, conv1,
        name="conv", us=10.5,
    )
    tok_sides = beside(tok_sides, sizes)
    sums = grouped_sum(sums, sizes)
    voxels = WIN * slabs * WIN * rows * WIN
    tok3, slope, tail, d_head, d_rows = call(
        functools.partial(head_kernel, voxels),
        [arr(11, 12, 8, WIDE), arr(11, 12, 8, WIDE), arr(8, WIDE), arr(WIDE, WIDE), arr(8, WIDE)],
        [],
        tok3, *tok_sides, sums, conv1, head_w,
        name="head", us=3.5,
    )
    tail = exchanged_sum(tail, count)
    late_rows = block_rows(LATE_ROWS, count) * count
    early_rows = EARLY_ROWS
    seam_rows = LATE_ROWS - 3 * CUTS[3]
    d_own, keep, send, carry3, seam = call(
        functools.partial(conv_back_kernel, sizes),
        [arr(PLANE, 8, WIDE)] + [arr(early_rows // 2, WIDE)] * 2
        + [arr(24, WIDE), arr(seam_rows, WIDE)],
        [
            pltpu.VMEM((5236, WIDE), F32),
            pltpu.VMEM((11, 12, 8, WIDE), F32),
            pltpu.VMEM((10, 10, 8, WIDE), F32),
            pltpu.VMEM((880, 2304), BF16),
            pltpu.VMEM((640, 2304), BF16),
            pltpu.VMEM((27 * 256, 256), BF16),
            pltpu.VMEM((seam_rows + early_rows, WIDE), F32),
        ],
        tok3, slope, tail, grown, pre, conv0, conv1, d_rows, d_head,
        name="conv_back", us=21.0,
    )
    early = summed_halves(keep, send, count)
    d_mid, grads1, flat2, carry2, *parts = call(
        back_two_kernel,
        [SQUARE, arr(1168, WIDE), arr(3 * (CUTS[3] - CUTS[2]), WIDE), arr(32, WIDE)] + PARTS,
        [pltpu.VMEM((1184, WIDE), F32), pltpu.VMEM((ROWS, WIDE), F32)] + BACKWARD,
        d_own, carry3, lay1, lay2, tok2, save2, lse2, mixed2, mid2, hpre2, mid1, hpre1,
        name="back_two", us=14.0,
    )
    parts = passed(parts, -1, sizes)
    d_window, flat1, carry1, *parts = call(
        functools.partial(back_shifted_kernel, sizes),
        [SQUARE, arr(3 * (CUTS[2] - CUTS[1]), WIDE), arr(16, WIDE)] + PARTS,
        REGION + [pltpu.VMEM((1200, WIDE), F32), pltpu.VMEM((ROWS, WIDE), F32)] + BACKWARD,
        d_mid, *parts, lay1, window, save1, lse1, mixed1, grads1, carry2,
        name="back_shifted", us=10.5,
    )
    parts = passed(parts, 1, sizes)
    late = call(
        functools.partial(back_first_kernel, sizes),
        [arr(late_rows // 2, WIDE)] * 2,
        [
            pltpu.VMEM((late_rows, WIDE), F32),
            pltpu.VMEM((1572, WIDE), F32),
            pltpu.VMEM((ROWS, WIDE), F32),
        ]
        + BACKWARD,
        d_mid, d_window, *parts, tok1, lay0, lay1, merge, dense, tok0, save0, lse0, mixed0, mid0,
        hpre0, carry1, flat1, flat2, seam,
        name="back_first", us=13.5,
    )
    late = summed_blocks(*late, count)
    new_params, new_first, new_second, loss, valid_count, norm = adamw(
        sizes, (*late, *early, tail, sums), (params, moment_one, moment_two)
    )
    return (
        loss.reshape(()), valid_count.reshape(()), norm.reshape(()),
        new_params, new_first, new_second,
    )


def solution(mesh):
    placed = (
        P("slab", "mp", None, None),
        P("slab", "mp", None),
        P("slab", "mp", None),
        P(),
        P(),
        P(),
    )
    sizes = (mesh.shape["slab"], mesh.shape["mp"])
    return jax.shard_map(
        functools.partial(on_device, sizes),
        mesh=mesh,
        in_specs=placed,
        out_specs=(P(), P(), P(), P(), P(), P()),
        check_vma=False,
    )
```

```python
import functools

import jax
import jax.numpy as jnp
from jax import lax
from jax.experimental import pallas as pl
from jax.experimental.pallas import tpu as pltpu
from jax.sharding import PartitionSpec as P

EMB = 96
HEADS = 6
HDIM = 16
HID = 384
MERGE = 384
CLASSES = 14
WIN = 7
SHIFT = 3
LAYERS = 3
STEP = 10

F32 = jnp.float32
BF16 = jnp.bfloat16
eps_norm = 1e-05
beta_one = 0.9
beta_two = 0.999
adam_eps = 1e-08
learn_rate = 0.05
decay_rate = 0.05
clip_norm = 0.01

VOX = WIN * WIN * WIN
ROWS = 384
BLK = 128
WIDE = 128
PLANE = WIN * WIN
FAR = WIN - SHIFT
ROWS_A = SHIFT * FAR * WIN
ROWS_B = FAR * SHIFT * WIN
ROWS_C = SHIFT * SHIFT * WIN

MERGE_ROWS = 392
LAYER_ROWS = 1165
TAP_ROWS = 27 * EMB
GROUPS = 2280
NPARAM = 872558
HEAD_ROW = 6806
HEAD_ROWS = 11
HEAD_LANE = 32
LATE_ROWS = 3072
EARLY_ROWS = 3840
LAYER_BASE = (98, 389, 680)
CONV_BASE = (971, 1620)
CUTS = (0, 392, 688, 976, 2280)

R_QKV, R_QKVB, R_PROJ, R_PROJB = 4, 292, 295, 391
R_HID, R_HIDB, R_OUT, R_OUTB = 392, 776, 780, 1164


def iota(shape, dim):
    return lax.broadcasted_iota(jnp.int32, shape, dim)


def split(x):
    hi = x.astype(BF16)
    return hi, (x - hi.astype(F32)).astype(BF16)


def pair(x):
    return jnp.concatenate(split(x), 1)


def fold(y):
    half = y.shape[1] // 2
    return y[:, :half] + y[:, half:]


def fold_rows(y):
    half = y.shape[0] // 2
    return y[:half] + y[half:]


def dot(a, b):
    return jnp.dot(a, b, preferred_element_type=F32)


def dot_nt(a, b):
    return lax.dot_general(a, b, (((1,), (1,)), ((), ())), preferred_element_type=F32)


def weight_nn(w):
    top = pair(w)
    return jnp.concatenate([top, top], 0)


def weight_nt(w):
    hi, lo = split(w)
    return jnp.concatenate(
        [jnp.concatenate([hi, hi], 1), jnp.concatenate([lo, lo], 1)], 0
    )


def mm(x, w):
    return fold(dot(pair(x), weight_nn(w)))


def mm_nt(x, w):
    return fold(dot_nt(pair(x), weight_nt(w)))


def rows_t(x):
    return jnp.concatenate(split(x.T), 0)


def mm_tn(xt, y):
    return fold_rows(fold(dot(xt, pair(y))))


def deep(w):
    return jnp.concatenate([w, jnp.zeros((WIDE - EMB, w.shape[1]), F32)], 0)


def roll(x, shift, axis):
    return pltpu.roll(x, shift, axis)


def four_to_three(y):
    lane = iota(y[0].shape, 1)
    a = jnp.where(lane < 96, y[0], roll(y[1], 96, 1))
    b = jnp.where(lane < 64, roll(y[1], 96, 1), roll(y[2], 64, 1))
    c = jnp.where(lane < 32, roll(y[2], 64, 1), roll(y[3], 32, 1))
    return a, b, c


def three_to_four(x):
    lane = iota(x[0].shape, 1)
    live = lane < EMB
    a = x[0]
    b = jnp.where(lane < 32, roll(x[0], 32, 1), roll(x[1], 32, 1))
    c = jnp.where(lane < 64, roll(x[1], 64, 1), roll(x[2], 64, 1))
    d = roll(x[2], 96, 1)
    return tuple(jnp.where(live, v, 0.0) for v in (a, b, c, d))


def hidden_rows(ref, start, count):
    return jnp.concatenate(
        four_to_three([ref[pl.ds(start + c, count, stride=4), :] for c in range(4)]), 1
    )


def put_hidden_rows(ref, start, count, x):
    parts = three_to_four([x[:, i * WIDE : (i + 1) * WIDE] for i in range(3)])
    for c in range(4):
        ref[pl.ds(start + c, count, stride=4), :] = parts[c]


def flatten(ref, start, groups, out):
    parts = four_to_three([ref[pl.ds(start + c, groups, stride=4), :] for c in range(4)])
    for c in range(3):
        out[pl.ds(c, groups, stride=3), :] = parts[c]


def norm_stats(x):
    live = iota(x.shape, 1) < EMB
    mean = jnp.sum(x, 1, keepdims=True) * (1.0 / EMB)
    centred = jnp.where(live, x - mean, 0.0)
    var = jnp.sum(centred * centred, 1, keepdims=True) * (1.0 / EMB)
    inv = lax.rsqrt(var + eps_norm)
    return centred * inv, inv


def norm(x, gain, bias):
    hat, _ = norm_stats(x)
    return hat * gain + bias


def norm_back(hat, inv, gain, grad):
    up = grad * gain
    one = jnp.sum(up, 1, keepdims=True) * (1.0 / EMB)
    two = jnp.sum(up * hat, 1, keepdims=True) * (1.0 / EMB)
    live = iota(hat.shape, 1) < EMB
    return jnp.where(live, inv * (up - one - hat * two), 0.0)


def colsum(x):
    return jnp.sum(x, 0, keepdims=True)


def gelu(x):
    return 0.5 * x * (1.0 + lax.erf(x * (0.5**0.5)))


def gelu_both(x):
    cdf = 0.5 * (1.0 + lax.erf(x * (0.5**0.5)))
    slope = cdf + x * (jnp.exp(x * x * -0.5) * 0.3989422804014327)
    return x * cdf, slope


def head_groups(x):
    lane = iota(x.shape, 1)
    swapped = roll(x, 64, 1)
    return jnp.where(lane < 64, x, swapped), jnp.where(lane < 64, swapped, x)


def as_left(x):
    both = []
    low = iota(x.shape, 1) < 64
    for part in head_groups(x):
        hi = part.astype(BF16).astype(F32)
        one = jnp.where(low, hi, part - hi).astype(BF16)
        both.append(jnp.concatenate([one, one], 1))
    return both


def as_right(x):
    return [pair(part) for part in head_groups(x)]


def head_mask(h, width):
    lane = iota((1, width), 1)
    lane = jnp.bitwise_and(lane, 63)
    low = jnp.bitwise_and(h, 3) * HDIM
    return jnp.where((lane >= low) & (lane < low + HDIM), 1.0, 0.0)


def own_lanes(h):
    lane = iota((1, WIDE), 1)
    return jnp.where((lane >= h * HDIM) & (lane < (h + 1) * HDIM), 1.0, 0.0)


def scores(q, k, h, rows, region):
    left = q * head_mask(h, 2 * WIDE).astype(BF16)
    s = dot_nt(left, k)
    if region is not None:
        region_rows, region_lanes = region
        here = region_rows[rows, 0:1]
        s = s + jnp.where(here == region_lanes[0:1, :], 0.0, -100.0)
    return jnp.where(iota(s.shape, 1) < VOX, s, -1e30)


def attention(normed, layer, save, lse, mixed, left, right, values, region=None):
    x = pair(normed)
    qkv = []
    for i in range(3):
        w = deep(layer[pl.ds(R_QKV + i, EMB, stride=3), :])
        y = fold(dot(x, weight_nn(w))) + layer[R_QKVB + i : R_QKVB + i + 1, :]
        if i == 0:
            y = y * HDIM**-0.5
        save[:, i * WIDE : (i + 1) * WIDE] = y
        qkv.append(y)
    for g, part in enumerate(as_left(qkv[0])):
        left[g] = part
    for g, part in enumerate(as_right(qkv[1])):
        right[g] = part
    v = pair(qkv[2])
    values[0:ROWS, :] = v
    values[ROWS : 2 * ROWS, :] = v
    mixed[...] = jnp.zeros_like(mixed)
    lse[...] = jnp.zeros_like(lse)

    def per_head(h, carry):
        g = lax.div(h, 4)
        lanes = own_lanes(h)
        at_h = jnp.where(iota((1, WIDE), 1) == h, 1.0, 0.0)
        for b in range(ROWS // BLK):
            rows = slice(b * BLK, (b + 1) * BLK)
            s = scores(left[g, rows, :], right[g], h, rows, region)
            top = jnp.max(s, 1, keepdims=True)
            e = jnp.exp(s - top)
            total = jnp.sum(e, 1, keepdims=True)
            o = fold(dot(pair(e), values[...]))
            mixed[rows, :] += o * (lanes / total)
            lse[rows, :] += (top + jnp.log(total)) * at_h
        return carry

    lax.fori_loop(0, HEADS, per_head, 0)
    proj = deep(layer[R_PROJ : R_PROJ + EMB, :])
    return mm(mixed[...], proj) + layer[R_PROJB : R_PROJB + 1, :]


def attention_back(grad, normed, layer, save, lse, mixed, sc, grads, at, region=None):
    left, right, gleft, vright, keys, dq, dkv_t, weights, slopes, q_t, do_t, dmix = sc
    proj = deep(layer[R_PROJ : R_PROJ + EMB, :])
    grads[at + R_PROJ : at + R_PROJ + EMB, :] = mm_tn(rows_t(mixed[...]), grad)[:EMB]
    grads[at + R_PROJB : at + R_PROJB + 1, :] = colsum(grad)
    d_mixed = mm_nt(grad, proj)
    dmix[...] = d_mixed
    q, k, v = (save[:, i * WIDE : (i + 1) * WIDE] for i in range(3))
    for g, part in enumerate(as_left(q)):
        left[g] = part
    for g, part in enumerate(as_right(k)):
        right[g] = part
    for g, part in enumerate(as_left(d_mixed)):
        gleft[g] = part
    for g, part in enumerate(as_right(v)):
        vright[g] = part
    kk = pair(k)
    keys[0:ROWS, :] = kk
    keys[ROWS : 2 * ROWS, :] = kk
    for ref, x in ((q_t, q), (do_t, d_mixed)):
        hi, lo = split(x.T)
        ref[0] = hi
        ref[1] = lo
    dq[...] = jnp.zeros_like(dq)
    dkv_t[...] = jnp.zeros_like(dkv_t)

    def per_head(h, carry):
        g = lax.div(h, 4)
        lanes = own_lanes(h)
        at_h = jnp.where(iota((1, WIDE), 1) == h, 1.0, 0.0)
        mask = head_mask(h, 2 * WIDE).astype(BF16)
        for b in range(ROWS // BLK):
            rows = slice(b * BLK, (b + 1) * BLK)
            s = scores(left[g, rows, :], right[g], h, rows, region)
            level = jnp.sum(lse[rows, :] * at_h, 1, keepdims=True)
            p = jnp.exp(s - level)
            dp = dot_nt(gleft[g, rows, :] * mask, vright[g])
            delta = jnp.sum(dmix[rows, :] * mixed[rows, :] * lanes, 1, keepdims=True)
            ds = p * (dp - delta)
            both = pair(ds)
            weights[rows, :] = pair(p)
            slopes[rows, :] = both
            dq[rows, :] += fold(dot(both, keys[...])) * lanes
        here = pl.multiple_of(h * HDIM, HDIM)
        for i, (t, m) in enumerate(((q_t, slopes), (do_t, weights))):
            lhs = jnp.concatenate([t[0, pl.ds(here, HDIM), :], t[1, pl.ds(here, HDIM), :]], 0)
            out = fold_rows(fold(dot(lhs, m[...])))
            dkv_t[i, pl.ds(here, HDIM), :] = out
        return carry

    lax.fori_loop(0, HEADS, per_head, 0)
    d_q = dq[...] * HDIM**-0.5
    d_k = dkv_t[0].T
    d_v = dkv_t[1].T
    x_t = rows_t(normed)
    d_normed = None
    for i, d in enumerate((d_q, d_k, d_v)):
        grads[pl.ds(at + R_QKV + i, EMB, stride=3), :] = mm_tn(x_t, d)[:EMB]
        grads[at + R_QKVB + i : at + R_QKVB + i + 1, :] = colsum(d)
        part = mm_nt(d, deep(layer[pl.ds(R_QKV + i, EMB, stride=3), :]))
        d_normed = part if d_normed is None else d_normed + part
    return d_normed


def mlp(middle, layer, hpre):
    normed = norm(middle, layer[2:3, :], layer[3:4, :])
    w = deep(hidden_rows(layer, R_HID, EMB))
    pre = mm(normed, w) + hidden_rows(layer, R_HIDB, 1)
    hpre[...] = pre
    out = mm(gelu(pre), layer[R_OUT : R_OUT + HID, :])
    return middle + out + layer[R_OUTB : R_OUTB + 1, :]


def mlp_back(grad, middle, hpre, layer, grads, at):
    hat, inv = norm_stats(middle)
    normed = hat * layer[2:3, :] + layer[3:4, :]
    act, slope = gelu_both(hpre[...])
    grads[at + R_OUTB : at + R_OUTB + 1, :] = colsum(grad)
    grads[at + R_OUT : at + R_OUT + HID, :] = mm_tn(rows_t(grad), act).T
    d_pre = mm_nt(grad, layer[R_OUT : R_OUT + HID, :]) * slope
    put_hidden_rows(grads, at + R_HIDB, 1, colsum(d_pre))
    put_hidden_rows(grads, at + R_HID, EMB, mm_tn(rows_t(normed), d_pre)[:EMB])
    d_normed = mm_nt(d_pre, deep(hidden_rows(layer, R_HID, EMB)))
    grads[at + 2 : at + 3, :] = colsum(d_normed * hat)
    grads[at + 3 : at + 4, :] = colsum(d_normed)
    return grad + norm_back(hat, inv, layer[2:3, :], d_normed)


def pre_norm_back(grad, tokens, layer, grads, at):
    hat, inv = norm_stats(tokens)
    grads[at : at + 1, :] = colsum(grad * hat)
    grads[at + 1 : at + 2, :] = colsum(grad)
    return norm_back(hat, inv, layer[0:1, :], grad)


def region_of(rows, sizes):
    d = lax.shift_right_logical(rows * 1338, 16)
    line = lax.shift_right_logical(rows * 9363, 16)
    places = (d, line - d * WIN, rows - line * WIN)
    starts = (lax.axis_index("slab") * WIN, lax.axis_index("mp") * WIN, 0)
    total = None
    for place, start, blocks in zip(places, starts, sizes + (1,)):
        turned = jnp.where(place < SHIFT, place + FAR, place - SHIFT) + start
        length = WIN * blocks
        part = jnp.where(turned < length - WIN, 0, jnp.where(turned < length - SHIFT, 1, 2))
        total = part if total is None else total * 3 + part
    return total


def put_regions(region, sizes):
    region_rows, region_lanes = region
    region_rows[...] = region_of(iota((ROWS, WIDE), 0), sizes).astype(F32)
    region_lanes[...] = region_of(iota((8, ROWS), 1), sizes).astype(F32)


def send_parts(ref, a, b, c):
    far = FAR * WIN
    near = SHIFT * WIN
    for d in range(SHIFT):
        base = d * PLANE
        c[d * near : (d + 1) * near, :] = ref[base : base + near, :]
        a[d * far : (d + 1) * far, :] = ref[base + near : base + PLANE, :]
    for d in range(FAR):
        base = (d + SHIFT) * PLANE
        b[d * near : (d + 1) * near, :] = ref[base : base + near, :]


def take_parts(own, a, b, c, out):
    far = FAR * WIN
    near = SHIFT * WIN
    for d in range(WIN):
        base = d * PLANE
        if d < SHIFT:
            out[base : base + near, :] = c[d * near : (d + 1) * near, :]
            out[base + near : base + PLANE, :] = a[d * far : (d + 1) * far, :]
        else:
            e = d - SHIFT
            out[base : base + near, :] = b[e * near : (e + 1) * near, :]
            out[base + near : base + PLANE, :] = own[base + near : base + PLANE, :]
    out[VOX:, :] = jnp.zeros((ROWS - VOX, WIDE), F32)


def span_of(groups):
    low, high = groups
    first = 3 * low // 8 * 8
    last = -(-3 * high // 8) * 8
    return first, min(last, NPARAM // WIDE // 8 * 8) - first


def copied(params, groups, flat, sem):
    first, rows = span_of(groups)
    size = rows * WIDE
    return pltpu.make_async_copy(
        params.at[pl.ds(first * WIDE, size)], flat.at[pl.ds(0, size)], sem
    )


def relay(groups, flat, out, square, last=None):
    low, high = groups
    first, rows = span_of(groups)
    square[0:rows, :] = flat[0 : rows * WIDE].reshape(rows, WIDE)
    if last is not None:
        square[rows : rows + 24, :] = jnp.zeros((24, WIDE), F32)
        square[rows : rows + 1, 0 : last.shape[0]] = last[...].reshape(1, last.shape[0])
    skip = 3 * low - first
    n = high - low
    parts = three_to_four([square[pl.ds(skip + c, n, stride=3), :] for c in range(3)])
    for c in range(4):
        out[pl.ds(c, n, stride=4), :] = parts[c]


FIRST_SPANS = ((0, 98), (98, 392))
LAYER_SPANS = ((389, 681), (680, 972))
CONV_SPANS = ((971, 1620), (1620, GROUPS))


def prep_kernel(spans, params, *refs, last=None):
    outs, (flats, square, sems) = refs[: len(spans)], refs[-3:]
    for i, groups in enumerate(spans):
        copied(params, groups, flats[i], sems.at[i]).start()
    for i, groups in enumerate(spans):
        copied(params, groups, flats[i], sems.at[i]).wait()
        relay(groups, flats[i], outs[i], square, last if i == len(spans) - 1 else None)


def head_picks():
    width = HEAD_ROWS * WIDE
    place = iota((WIDE, width), 1) - HEAD_LANE
    row = iota((WIDE, width), 0)
    here = (place >= row * CLASSES) & (place < (row + 1) * CLASSES) & (row <= EMB)
    place = iota((width, WIDE), 0) - HEAD_LANE
    col = iota((width, WIDE), 1)
    row = lax.shift_right_logical(place * 4682, 16)
    there = (place - row * CLASSES == col) & (place >= 0)
    return jnp.where(here, 1.0, 0.0), jnp.where(there, 1.0, 0.0).astype(BF16)


def prep_conv_kernel(last, params, conv0, conv1, head, *scratch):
    prep_kernel(CONV_SPANS, params, conv0, conv1, *scratch, last=last)
    square = scratch[1]
    first, _ = span_of(CONV_SPANS[1])
    row = jnp.concatenate(
        [square[HEAD_ROW + i - first : HEAD_ROW + i - first + 1, :] for i in range(HEAD_ROWS)], 1
    )
    here, there = head_picks()
    hi, lo = split(here * row)
    head[...] = dot(hi, there) + dot(lo, there)


def head_rows(d_head, out, at):
    here, there = head_picks()
    hi, lo = split(d_head)
    spread = (dot_nt(hi, there) + dot_nt(lo, there)) * here
    row = colsum(spread)
    for i in range(HEAD_ROWS):
        out[at + i : at + i + 1, :] += row[:, i * WIDE : (i + 1) * WIDE]


class Rows:
    def __init__(self, ref, at):
        self.ref, self.at = ref, at

    def __getitem__(self, key):
        rows, lanes = key
        if isinstance(rows, slice):
            rows = slice(rows.start + self.at, rows.stop + self.at)
        else:
            rows = pl.ds(rows.start + self.at, rows.size, stride=rows.stride)
        return self.ref[rows, lanes]


def merged_norm(x):
    mean = jnp.sum(x, 1, keepdims=True) * (1.0 / MERGE)
    centred = x - mean
    var = jnp.sum(centred * centred, 1, keepdims=True) * (1.0 / MERGE)
    return centred * lax.rsqrt(var + eps_norm)


def first_kernel(
    feats, merge, lay0,
    dense, tok0, save, lse, mixed, middle, hpre, tok1, ahead, pa, pb, pc,
    left, right, values,
):
    dense[VOX:, :] = jnp.zeros((ROWS - VOX, MERGE), F32)
    for line in range(PLANE):
        dense[line * WIN : (line + 1) * WIN, :] = feats[line]
    hat = merged_norm(dense[...])
    normed = hat * hidden_rows(merge, 0, 1) + hidden_rows(merge, 4, 1)
    tokens = mm(normed, merge[8 : 8 + MERGE, :])
    tok0[...] = tokens
    layer = Rows(lay0, 0)
    normed = norm(tokens, layer[0:1, :], layer[1:2, :])
    attended = attention(normed, layer, save, lse, mixed, left, right, values)
    mid = tokens + attended
    middle[...] = mid
    tokens = mlp(mid, layer, hpre)
    tok1[...] = tokens
    ahead[...] = norm(tokens, layer[1165:1166, :], layer[1166:1167, :])
    send_parts(ahead, pa, pb, pc)


def shifted_kernel(
    sizes,
    own, pa, pb, pc, lay1,
    window, save, lse, mixed, out, qa, qb, qc,
    region_rows, region_lanes, left, right, values,
):
    put_regions((region_rows, region_lanes), sizes)
    take_parts(own, pa, pb, pc, window)
    out[...] = attention(
        window[...], Rows(lay1, 1), save, lse, mixed, left, right, values,
        (region_rows, region_lanes),
    )
    send_parts(out, qa, qb, qc)


def to_lines(ref, out):
    for line in range(PLANE):
        out[line, 0:WIN, :] = ref[line * WIN : (line + 1) * WIN, :]
        out[line, WIN:8, :] = jnp.zeros((8 - WIN, WIDE), F32)


def from_lines(ref, out):
    out[VOX:, :] = jnp.zeros((ROWS - VOX, WIDE), F32)
    for line in range(PLANE):
        out[line * WIN : (line + 1) * WIN, :] = ref[line, 0:WIN, :]


def send_sides(lines, low_d, high_d, low_h, high_h):
    low_d[...] = lines[0 : 2 * WIN]
    high_d[...] = lines[(WIN - 2) * WIN :]
    for d in range(WIN):
        low_h[2 * d : 2 * d + 2] = lines[d * WIN : d * WIN + 2]
        high_h[2 * d : 2 * d + 2] = lines[d * WIN + WIN - 2 : (d + 1) * WIN]


def second_kernel(
    tok1, own, qa, qb, qc, lay1, lay2,
    mid1, hpre1, tok2, save, lse, mixed, mid2, hpre2, lines,
    s0, s1, s2, s3,
    attended, left, right, values,
):
    take_parts(own, qa, qb, qc, attended)
    mid = tok1[...] + attended[...]
    mid1[...] = mid
    tokens = mlp(mid, Rows(lay1, 1), hpre1)
    tok2[...] = tokens
    layer = Rows(lay2, 2)
    normed = norm(tokens, layer[0:1, :], layer[1:2, :])
    mid = tokens + attention(normed, layer, save, lse, mixed, left, right, values)
    mid2[...] = mid
    attended[...] = mlp(mid, layer, hpre2)
    to_lines(attended, lines)
    send_sides(lines, s0, s1, s2, s3)


def grown_lines(own, low_d, high_d, low_h, high_h, out):
    out[...] = jnp.zeros_like(out)
    for d in range(WIN):
        out[d + 2, 2 : 2 + WIN] = own[d * WIN : (d + 1) * WIN]
    for d in range(2):
        out[d, 2 : 2 + WIN] = low_d[d * WIN : (d + 1) * WIN]
        out[d + 9, 2 : 2 + WIN] = high_d[d * WIN : (d + 1) * WIN]
    for d in range(11):
        out[d, 0:2] = low_h[2 * d : 2 * d + 2]
        out[d, 9:11] = high_h[2 * d : 2 * d + 2]


def put_marks(labels, valid, out):
    across = iota((8, WIN), 1) == iota((8, WIN), 0)
    classes = iota((8, WIDE), 1) - EMB
    for d in range(WIN):
        code = jnp.where(valid[d] == 1, labels[d], -1 - EMB - WIDE)
        code = code.astype(F32)
        for h in range(WIN):
            line = jnp.where(across, code[h : h + 1, :], 0.0)
            column = jnp.sum(line, 1, keepdims=True)
            mark = jnp.where(column == classes.astype(F32), 1.0, 0.0)
            out[d * WIN + h] = jnp.where(iota((8, WIDE), 0) < WIN, mark, 0.0)


def taps(source, first_plane, planes, first_line, lines, out):
    def per_plane(d, carry):
        for c in range(3):
            for b in range(3):
                x = source[d + first_plane, first_line + b : first_line + b + lines]
                if c != 1:
                    x = roll(x, 1 if c == 0 else 7, 1)
                x = pair(x.reshape(lines * 8, WIDE))
                at = pl.multiple_of(d * (lines * 8), lines * 8)
                t = b * 3 + c
                out[pl.ds(at, lines * 8), t * 256 : (t + 1) * 256] = x
        return carry

    lax.fori_loop(0, planes, per_plane, 0)


def tap_weights(ref, at, out):
    def per_tap(i, carry):
        w = deep(ref[pl.ds(i * EMB + at, EMB), :])
        out[pl.ds(pl.multiple_of(i * 256, 256), 256), :] = weight_nn(w)
        return carry

    lax.fori_loop(0, 27, per_tap, 0)


def tap_weights_back(ref, at, out):
    def per_tap(i, carry):
        w = deep(ref[pl.ds((26 - i) * EMB + at, EMB), :]).T
        out[pl.ds(pl.multiple_of(i * 256, 256), 256), :] = weight_nn(w)
        return carry

    lax.fori_loop(0, 27, per_tap, 0)


def conv(side, weights, planes, pitch, at_once, put):
    rows = at_once * pitch
    for start in range(0, planes, at_once):
        total = None
        for a in range(3):
            low = (start + a) * pitch
            part = dot(side[low : low + rows, :], weights[a * 2304 : (a + 1) * 2304, :])
            total = part if total is None else total + part
        put(start, fold(total))


def conv_weight_grad(side, grad_rows, pitch, out, at):
    rows = 512
    g = jnp.concatenate([grad_rows, jnp.zeros((rows - grad_rows.shape[0], WIDE), F32)], 0)
    left = rows_t(g)
    for a in range(3):
        for bc in range(9):
            y = dot(left, side[a * pitch : a * pitch + rows, bc * 256 : (bc + 1) * 256])
            y = fold_rows(fold(y)).T
            t = a * 9 + bc
            out[at + t * EMB : at + (t + 1) * EMB, :] = y[:EMB]


def volume_mask(sizes, planes, lines, reach, real_lines):
    slab, row = lax.axis_index("slab"), lax.axis_index("mp")
    ends = (slab == 0, slab == sizes[0] - 1, row == 0, row == sizes[1] - 1)
    shape = (planes, lines, 8, WIDE)
    d, h, w = iota(shape, 0), iota(shape, 1), iota(shape, 2)
    low_d = jnp.where(ends[0], reach, 0)
    high_d = jnp.where(ends[1], planes - reach, planes)
    low_h = jnp.where(ends[2], reach, 0)
    high_h = jnp.where(ends[3], real_lines - reach, real_lines)
    inside = (d >= low_d) & (d < high_d) & (h >= low_h) & (h < high_h) & (w < WIN)
    return jnp.where(inside, 1.0, 0.0)


def conv_kernel(
    sizes,
    own, s0, s1, s2, s3, labels, valid, conv0, conv1,
    grown, pre, tok, stats, t0, t1, t2, t3,
    act, side, side_own, weights, marks,
):
    grown_lines(own, s0, s1, s2, s3, grown)
    put_marks(labels, valid, marks)
    tap_weights(conv0, 3, weights)
    taps(grown, 0, 11, 0, 10, side)
    bias0 = conv0[3 + TAP_ROWS : 4 + TAP_ROWS, :]
    inside = volume_mask(sizes, 9, 10, 1, 9)

    def put(start, y):
        z = (y + bias0).reshape(3, 10, 8, WIDE)
        pre[start : start + 3] = z
        act[start : start + 3] = gelu(z) * inside[start : start + 3]

    conv(side, weights, 9, 80, 3, put)
    tap_weights(conv1, 0, weights)
    taps(act, 0, 9, 0, 8, side_own)
    bias1 = conv1[TAP_ROWS : TAP_ROWS + 1, :]
    sums = []

    def put_own(start, y):
        y = (y + bias1).reshape(WIN, 8, 8, WIDE)[:, 0:WIN]
        y = y + own[...].reshape(WIN, WIN, 8, WIDE)
        y = jnp.where(iota(y.shape, 2) < WIN, y, 0.0).reshape(PLANE, 8, WIDE)
        tok[...] = y + marks[...]
        send_sides(tok, t0, t1, t2, t3)
        flat = y.reshape(PLANE * 8, WIDE)
        sums.append(colsum(flat))
        sums.append(colsum(flat * flat))

    conv(side_own, weights, WIN, 64, WIN, put_own)
    count = jnp.sum(marks[...].reshape(PLANE * 8, WIDE))
    row = iota((8, WIDE), 0)
    stats[...] = (
        jnp.where(row == 0, sums[0], 0.0)
        + jnp.where(row == 1, sums[1], 0.0)
        + jnp.where(row == 2, count, 0.0)
    )


def head_kernel(
    voxels,
    own, s0, s1, s2, s3, sums, conv1, head_w,
    grown, slope_out, stats, d_head, d_rows,
):
    grown_lines(own, s0, s1, s2, s3, grown)
    rows = 11 * 12 * 8
    both = grown[...].reshape(rows, WIDE)
    lane = iota((rows, WIDE), 1)
    tokens = jnp.where(lane < EMB, both, 0.0)
    target = jnp.where(lane < CLASSES, roll(both, WIDE - EMB, 1), 0.0)
    live = jnp.sum(target, 1, keepdims=True)
    count = F32(voxels)
    average = sums[0:1, :] / count
    spread = sums[1:2, :] / count - average * average
    inv = lax.rsqrt(spread + eps_norm)
    gain = conv1[TAP_ROWS + 1 : TAP_ROWS + 2, :]
    bias = conv1[TAP_ROWS + 2 : TAP_ROWS + 3, :]
    hat = (tokens - average) * inv
    act, slope = gelu_both(hat * gain + bias)
    act = jnp.where(lane == EMB, 1.0, act)
    w = head_w[...]
    logits = mm(act, w)
    logits = jnp.where(lane < CLASSES, logits, -1e30)
    top = jnp.max(logits, 1, keepdims=True)
    e = jnp.exp(logits - top)
    total = jnp.sum(e, 1, keepdims=True)
    logp = logits - top - jnp.log(total)
    scale = 1.0 / sums[2:3, 0:1]
    d_logits = (e / total * live - target) * scale
    d_normed = jnp.where(lane < EMB, mm_nt(d_logits, w) * slope, 0.0)
    d_tokens = d_normed * gain * inv
    slope_out[...] = d_tokens.reshape(11, 12, 8, WIDE)

    def own_rows(x):
        x = x.reshape(11, 12, 8, WIDE)[2:9, 2:9]
        x = jnp.where(iota(x.shape, 2) < WIN, x, 0.0)
        return x.reshape(PLANE * 8, WIDE)

    loss = -jnp.sum(own_rows(target * jnp.where(lane < CLASSES, logp, 0.0)))
    own_d = own_rows(d_logits)
    own_n = own_rows(d_normed)
    own_hat = own_rows(hat)
    zeros = jnp.zeros((512 - PLANE * 8, WIDE), F32)
    left = rows_t(jnp.concatenate([own_d, zeros], 0))
    d_head[...] = mm_tn(left, jnp.concatenate([own_rows(act), zeros], 0)).T
    d_gain = colsum(own_n * own_hat)
    d_bias = colsum(own_n)
    d_average = -d_bias * gain * inv
    d_spread = d_gain * gain * inv * inv * -0.5
    d_two = d_spread / count
    d_one = (d_average - 2.0 * average * d_spread) / count
    row = iota((8, WIDE), 0)
    live_lane = iota((8, WIDE), 1) < EMB
    stats[...] = (
        jnp.where((row == 0) & live_lane, d_one, 0.0)
        + jnp.where((row == 1) & live_lane, d_two, 0.0)
        + jnp.where(row == 2, loss, 0.0)
    )
    d_rows[...] = (
        jnp.where(row == 0, d_gain, 0.0)
        + jnp.where(row == 1, d_bias, 0.0)
    )


def conv_back_kernel(
    sizes,
    tok, slope, sums, grown, pre, conv0, conv1, d_rows, d_head,
    d_own, keep, send, carry, seam,
    grads, dgrown, act, side, side_own, weights, flat,
):
    lane = iota((11, 12, 8, WIDE), 3)
    inside = volume_mask(sizes, 11, 12, 2, 11)
    steady = sums[0:1, :].reshape(1, 1, 1, WIDE)
    rising = 2.0 * sums[1:2, :].reshape(1, 1, 1, WIDE)
    d_tok = slope[...] + jnp.where(lane < EMB, (steady + tok[...] * rising) * inside, 0.0)
    dgrown[...] = d_tok
    grads[5191:, :] = jnp.zeros((45, WIDE), F32)
    grads[0:8, :] = jnp.zeros((8, WIDE), F32)
    grads[5189:5191, :] = d_rows[0:2, :]
    own = dgrown[2:9, 2:10]
    line = iota(own.shape, 1)
    own = jnp.where(line < WIN, own, 0.0).reshape(WIN * 64, WIDE)
    grads[5188:5189, :] = colsum(own)

    near = volume_mask(sizes, 9, 10, 1, 9)
    act[0:9] = gelu(pre[...]) * near
    act[9:10] = jnp.zeros((1, 10, 8, WIDE), F32)
    taps(act, 0, 10, 0, 8, side_own)
    conv_weight_grad(side_own, own, 64, grads, 2596)
    tap_weights_back(conv1, 0, weights)
    taps(dgrown, 0, 11, 0, 10, side)

    def put(start, y):
        _, s = gelu_both(pre[start : start + 3])
        z = y.reshape(3, 10, 8, WIDE) * s * near[start : start + 3]
        act[start : start + 3] = z

    conv(side, weights, 9, 80, 3, put)

    own = act[1:8, 1:9]
    line = iota(own.shape, 1)
    own = jnp.where(line < WIN, own, 0.0).reshape(WIN * 64, WIDE)
    grads[2595:2596, :] = colsum(own)
    taps(grown, 1, 10, 1, 8, side_own)
    conv_weight_grad(side_own, own, 64, grads, 3)
    carry[...] = grads[0:24, :]
    flat[3 * (GROUPS - CUTS[3]) :, :] = jnp.zeros((flat.shape[0] - 3912, WIDE), F32)
    flatten(grads, 20, GROUPS - CUTS[3], flat)
    start = 3 * CUTS[3]
    head_rows(d_head[...], flat, HEAD_ROW - start)
    seam[...] = flat[0 : LATE_ROWS - start, :]
    scatter(sizes, flat, LATE_ROWS - start, keep, send)
    tap_weights_back(conv0, 3, weights)
    taps(act, 0, 9, 0, 8, side_own)

    def put_own(start, y):
        y = y.reshape(WIN, 8, 8, WIDE)[:, 0:WIN] + dgrown[2:9, 2:9]
        y = jnp.where(iota(y.shape, 2) < WIN, y, 0.0)
        d_own[...] = y.reshape(PLANE, 8, WIDE)

    conv(side_own, weights, WIN, 64, WIN, put_own)


def back_two_kernel(
    d_own, carry, lay1, lay2, tok2, save, lse, mixed, mid2, hpre2, mid1, hpre1,
    d_mid, grads1, flat, carry2, pa, pb, pc,
    grads, dense, *sc,
):
    from_lines(d_own, dense)
    layer = Rows(lay2, 2)
    grads[0:8, :] = jnp.zeros((8, WIDE), F32)
    d = mlp_back(dense[...], mid2[...], hpre2, layer, grads, 2)
    tokens = tok2[...]
    normed = norm(tokens, layer[0:1, :], layer[1:2, :])
    d_normed = attention_back(d, normed, layer, save, lse, mixed, sc, grads, 2)
    d = d + pre_norm_back(d_normed, tokens, layer, grads, 2)
    grads[1167:1184, :] = carry[3:20, :]
    flatten(grads, 32, CUTS[3] - CUTS[2], flat)
    carry2[...] = grads[0:32, :]
    layer = Rows(lay1, 1)
    d = mlp_back(d, mid1[...], hpre1, layer, grads1, 1)
    d_mid[...] = d
    send_parts(d_mid, pa, pb, pc)


def back_shifted_kernel(
    sizes,
    own, pa, pb, pc, lay1, window, save, lse, mixed, grads1, carry2, _,
    d_window, flat, carry1, qa, qb, qc,
    region_rows, region_lanes, grads, grad, *sc,
):
    put_regions((region_rows, region_lanes), sizes)
    take_parts(own, pa, pb, pc, grad)
    grads[0:1168, :] = grads1[...]
    grads[0:3, :] = jnp.zeros((3, WIDE), F32)
    d_window[...] = attention_back(
        grad[...], window[...], Rows(lay1, 1), save, lse, mixed, sc, grads, 1,
        (region_rows, region_lanes),
    )
    send_parts(d_window, qa, qb, qc)
    grads[1166:1196, :] = carry2[2:32, :]
    flatten(grads, 12, CUTS[2] - CUTS[1], flat)
    carry1[...] = grads[0:16, :]


def back_first_kernel(
    sizes,
    d_mid, own, qa, qb, qc, tok1, lay0, lay1, merge, dense, tok0, save, lse, mixed, middle, hpre,
    carry1, flat1, flat2, seam, _,
    keep, send,
    flat, grads, grad, *sc,
):
    take_parts(own, qa, qb, qc, grad)
    grads[1556:1572, :] = carry1[...]
    d = d_mid[...] + pre_norm_back(grad[...], tok1[...], Rows(lay1, 1), grads, 1557)
    layer = Rows(lay0, 0)
    at = MERGE_ROWS
    d = mlp_back(d, middle[...], hpre, layer, grads, at)
    tokens = tok0[...]
    normed = norm(tokens, layer[0:1, :], layer[1:2, :])
    d_normed = attention_back(d, normed, layer, save, lse, mixed, sc, grads, at)
    d = d + pre_norm_back(d_normed, tokens, layer, grads, at)
    live = iota((ROWS, WIDE), 0) < VOX
    d = jnp.where(live, d, 0.0)
    hat = merged_norm(dense[...])
    gain = hidden_rows(merge, 0, 1)
    bias = hidden_rows(merge, 4, 1)
    w = merge[8 : 8 + MERGE, :]
    put_hidden_rows(grads, 8 - 8, 1, jnp.zeros((1, MERGE), F32))
    grads[8 : 8 + MERGE, :] = mm_tn(rows_t(d), hat * gain + bias).T
    d_hat = mm_nt(d, w)
    put_hidden_rows(grads, 0, 1, colsum(d_hat * hat))
    put_hidden_rows(grads, 4, 1, colsum(d_hat))
    flatten(grads, 0, CUTS[1], flat)
    at = 0
    for cut, part in ((CUTS[1], flat1), (CUTS[2], flat2), (CUTS[3], seam)):
        at = 3 * cut
        flat[at : at + part.shape[0], :] = part[...]
    at += seam.shape[0]
    if flat.shape[0] > at:
        flat[at:, :] = jnp.zeros((flat.shape[0] - at, WIDE), F32)
    scatter(sizes, flat, 0, keep, send)


def radices(count):
    steps = [2]
    left = count // 2
    while left > 1:
        steps.append(4 if left >= 4 else 2)
        left //= steps[-1]
    return steps


def block_rows(rows, count):
    return -(-rows // (8 * count)) * 8


def own_number(sizes):
    return lax.axis_index("slab") * sizes[1] + lax.axis_index("mp")


def place_in_half(distance, count):
    place = 0
    shift = 1
    for radix in radices(count)[1:]:
        digit = jnp.bitwise_and(lax.shift_right_logical(distance, shift), radix - 1)
        place = place * radix + digit
        shift += radix.bit_length() - 1
    return place


def scatter(sizes, source, first, keep, send):
    count = sizes[0] * sizes[1]
    rows = keep.shape[0] * 2 // count
    me = own_number(sizes)
    odd = jnp.bitwise_and(me, 1)

    def per_pair(t, carry):
        for block, out in ((2 * t + odd, keep), (2 * t + 1 - odd, send)):
            place = place_in_half(jnp.bitwise_xor(block, me), count)
            at = pl.multiple_of(first + block * rows, 8)
            to = pl.multiple_of(place * rows, 8)
            out[pl.ds(to, rows), :] = source[pl.ds(at, rows), :]
        return carry

    lax.fori_loop(0, count // 2, per_pair, 0)


def traded(value, distance, count):
    pairs = [(i, i ^ distance) for i in range(count)]
    return lax.ppermute(value, ("slab", "mp"), pairs)


def summing(keep, send, count):
    def later(got, after):
        return got if after is None else list(lax.optimization_barrier((*got, after)))[:-1]

    steps = radices(count)
    got = [keep, traded(send, 1, count)]
    shift = 1
    after = yield None
    for radix in steps[1:]:
        got = later(got, after)
        total = sum(got[1:], got[0])
        rows = total.shape[0] // radix
        parts = [total[k * rows : (k + 1) * rows] for k in range(radix)]
        got = parts[:1] + [traded(parts[k], k << shift, count) for k in range(1, radix)]
        shift += radix.bit_length() - 1
        after = yield parts[0]
    got = later(got, after)
    own = sum(got[1:], got[0])
    for radix in reversed(steps[1:]):
        shift -= radix.bit_length() - 1
        got = [own] + [traded(own, k << shift, count) for k in range(1, radix)]
        after = yield own
        own = jnp.concatenate(later(got, after), 0)
    yield own, traded(own, 1, count)


def finished(chain, after=None):
    last = next(chain) if after is None else chain.send(after)
    while not isinstance(last, tuple):
        last = next(chain)
    return last


def exchanged_sum(value, count):
    shift = 0
    for radix in radices(count):
        got = [value] + [traded(value, k << shift, count) for k in range(1, radix)]
        while len(got) > 1:
            got = [got[i] + got[i + 1] for i in range(0, len(got), 2)]
        value = got[0]
        shift += radix.bit_length() - 1
    return value


def gather_kernel(
    sizes, late, late_other, early, early_other, tail, sums, grad, loss, valid, norm
):
    count = sizes[0] * sizes[1]
    me = own_number(sizes)
    total = jnp.zeros((8, WIDE), F32)
    for ref in (late, late_other, early, early_other):
        x = ref[...]
        total = total + jnp.sum((x * x).reshape(-1, 8, WIDE), 0)
    norm[0] = jnp.sqrt(jnp.sum(total))
    loss[0] = jnp.sum(tail[2:3, 0:1])
    valid[0] = jnp.sum(sums[2:3, 0:1])
    first = 0
    for own, other, size in ((late, late_other, LATE_ROWS), (early, early_other, EARLY_ROWS)):
        rows = own.shape[0] * 2 // count

        def per_block(block, carry, own=own, other=other, rows=rows, first=first):
            distance = jnp.bitwise_xor(block, me)
            at = pl.ds(pl.multiple_of(place_in_half(distance, count) * rows, 8), rows)
            near = jnp.bitwise_and(distance, 1) == 0
            to = pl.ds(pl.multiple_of(first + block * rows, 8), rows)
            grad[to, :] = jnp.where(near, own[at, :], other[at, :])
            return carry

        lax.fori_loop(0, size // rows, per_block, 0)
        first += size


def adamw(param, grad, first, second, scale):
    grad = grad * scale
    first = beta_one * first + (1.0 - beta_one) * grad
    second = beta_two * second + (1.0 - beta_two) * grad * grad
    first_hat = first / (1.0 - beta_one**STEP)
    second_hat = second / (1.0 - beta_two**STEP)
    param = param - learn_rate * (
        first_hat / (jnp.sqrt(second_hat) + adam_eps) + decay_rate * param
    )
    return (param, first, second)


def arr(*shape):
    return jax.ShapeDtypeStruct(shape, F32)


def call(kernel, outs, scratch, *args, name=None, us=1.0, far=(), mib=24):
    vmem = pl.BlockSpec(memory_space=pltpu.VMEM)
    smem = pl.BlockSpec(memory_space=pltpu.SMEM)
    return pl.pallas_call(
        kernel,
        out_shape=list(outs),
        in_specs=[vmem] * len(args) + [pl.BlockSpec(memory_space=pl.ANY)] * len(far),
        out_specs=[smem if o.shape == (1,) else vmem for o in outs],
        scratch_shapes=list(scratch),
        compiler_params=pltpu.CompilerParams(vmem_limit_bytes=mib * 1024 * 1024),
        cost_estimate=pl.CostEstimate(
            flops=int(us * 1.15e9), bytes_accessed=0, transcendentals=0
        ),
        name=name,
    )(*args, *far)


SQUARE = arr(ROWS, WIDE)
SAVE = arr(ROWS, 3 * WIDE)
FORWARD = [
    pltpu.VMEM((2, ROWS, 2 * WIDE), BF16),
    pltpu.VMEM((2, ROWS, 2 * WIDE), BF16),
    pltpu.VMEM((2 * ROWS, 2 * WIDE), BF16),
]
BACKWARD = [
    pltpu.VMEM((2, ROWS, 2 * WIDE), BF16),
    pltpu.VMEM((2, ROWS, 2 * WIDE), BF16),
    pltpu.VMEM((2, ROWS, 2 * WIDE), BF16),
    pltpu.VMEM((2, ROWS, 2 * WIDE), BF16),
    pltpu.VMEM((2 * ROWS, 2 * WIDE), BF16),
    pltpu.VMEM((ROWS, WIDE), F32),
    pltpu.VMEM((2, WIDE, ROWS), F32),
    pltpu.VMEM((ROWS, 2 * ROWS), BF16),
    pltpu.VMEM((ROWS, 2 * ROWS), BF16),
    pltpu.VMEM((2, WIDE, ROWS), BF16),
    pltpu.VMEM((2, WIDE, ROWS), BF16),
    pltpu.VMEM((ROWS, WIDE), F32),
]
PARTS = [arr(ROWS_A, WIDE), arr(ROWS_B, WIDE), arr(ROWS_C, WIDE)]


def passed(parts, steps, sizes):
    slabs, rows = sizes
    moved = []
    for part, (ds, dm) in zip(parts, ((1, 0), (0, 1), (1, 1))):
        pairs = []
        for s in range(slabs):
            for m in range(rows):
                target = ((s + steps * ds) % slabs) * rows + (m + steps * dm) % rows
                pairs.append((s * rows + m, target))
        moved.append(lax.ppermute(part, ("slab", "mp"), pairs))
    return moved


SIDES = [arr(2 * WIN, 8, WIDE)] * 4


def beside(sides, sizes):
    slabs, rows = sizes
    low_d, high_d, low_h, high_h = sides
    up = [(i, i + 1) for i in range(slabs - 1)]
    down = [(i + 1, i) for i in range(slabs - 1)]
    before = lax.ppermute(high_d, "slab", up)
    after = lax.ppermute(low_d, "slab", down)

    def column(own, start):
        ends = [
            x.reshape(2, WIN, 8, WIDE)[:, start : start + 2].reshape(4, 8, WIDE)
            for x in (before, after)
        ]
        return jnp.concatenate([ends[0], own, ends[1]], 0)

    up = [(i, i + 1) for i in range(rows - 1)]
    down = [(i + 1, i) for i in range(rows - 1)]
    left = lax.ppermute(column(high_h, WIN - 2), "mp", up)
    right = lax.ppermute(column(low_h, 0), "mp", down)
    return before, after, left, right


REGION = [pltpu.VMEM((ROWS, WIDE), F32), pltpu.VMEM((8, ROWS), F32)]


def on_device(sizes, feats, labels, valid, params, moment_one, moment_two):
    slabs, rows = sizes
    count = slabs * rows

    def room(spans):
        sizes = [(span_of(groups)[1] + 8) * WIDE for groups in spans]
        return [
            [pltpu.VMEM((size,), F32) for size in sizes],
            pltpu.VMEM((2048, WIDE), F32),
            pltpu.SemaphoreType.DMA((len(spans),)),
        ]

    merge, lay0 = call(
        functools.partial(prep_kernel, FIRST_SPANS),
        [arr(MERGE_ROWS, WIDE), arr(1176, WIDE)],
        room(FIRST_SPANS),
        name="prep_first", us=2.0, far=(params,),
    )
    lay1, lay2 = call(
        functools.partial(prep_kernel, LAYER_SPANS),
        [arr(1168, WIDE)] * 2,
        room(LAYER_SPANS),
        name="prep_layers", us=2.0, far=(params,),
    )
    conv0, conv1, head_w = call(
        prep_conv_kernel,
        [arr(2596, WIDE), arr(2640, WIDE), arr(WIDE, WIDE)],
        room(CONV_SPANS),
        params[NPARAM // WIDE * WIDE :],
        name="prep_conv", us=3.0, far=(params,),
    )

    dense, tok0, save0, lse0, mixed0, mid0, hpre0, tok1, ahead, *parts = call(
        first_kernel,
        [arr(ROWS, MERGE), SQUARE, SAVE, SQUARE, SQUARE, SQUARE, arr(ROWS, HID), SQUARE, SQUARE]
        + PARTS,
        FORWARD,
        feats.reshape(PLANE, WIN, MERGE), merge, lay0,
        name="first", us=9.5,
    )
    parts = passed(parts, -1, sizes)
    window, save1, lse1, mixed1, out1, *parts = call(
        functools.partial(shifted_kernel, sizes),
        [SQUARE, SAVE, SQUARE, SQUARE, SQUARE] + PARTS,
        REGION + FORWARD,
        ahead, *parts, lay1,
        name="shifted", us=7.5,
    )
    parts = passed(parts, 1, sizes)
    mid1, hpre1, tok2, save2, lse2, mixed2, mid2, hpre2, lines, *sides = call(
        second_kernel,
        [SQUARE, arr(ROWS, HID), SQUARE, SAVE, SQUARE, SQUARE, SQUARE, arr(ROWS, HID)]
        + [arr(PLANE, 8, WIDE)] + SIDES,
        [pltpu.VMEM((ROWS, WIDE), F32)] + FORWARD,
        tok1, out1, *parts, lay1, lay2,
        name="second", us=9.5,
    )
    sides = beside(sides, sizes)
    grown, pre, tok3, sums, *tok_sides = call(
        functools.partial(conv_kernel, sizes),
        [arr(11, 12, 8, WIDE), arr(9, 10, 8, WIDE), arr(PLANE, 8, WIDE), arr(8, WIDE)] + SIDES,
        [
            pltpu.VMEM((9, 10, 8, WIDE), F32),
            pltpu.VMEM((880, 2304), BF16),
            pltpu.VMEM((576, 2304), BF16),
            pltpu.VMEM((27 * 256, 256), BF16),
            pltpu.VMEM((PLANE, 8, WIDE), F32),
        ],
        lines, *sides, labels, valid, conv0, conv1,
        name="conv", us=10.5, mib=32,
    )
    tok_sides = beside(tok_sides, sizes)
    sums = exchanged_sum(sums, count)
    voxels = WIN * slabs * WIN * rows * WIN
    tok3, slope, tail, d_head, d_rows = call(
        functools.partial(head_kernel, voxels),
        [arr(11, 12, 8, WIDE), arr(11, 12, 8, WIDE), arr(8, WIDE), arr(WIDE, WIDE), arr(8, WIDE)],
        [],
        tok3, *tok_sides, sums, conv1, head_w,
        name="head", us=3.5,
    )
    tail = exchanged_sum(tail, count)
    late_rows = block_rows(LATE_ROWS, count) * count
    early_rows = block_rows(EARLY_ROWS, count) * count
    seam_rows = LATE_ROWS - 3 * CUTS[3]
    d_own, keep, send, carry3, seam = call(
        functools.partial(conv_back_kernel, sizes),
        [arr(PLANE, 8, WIDE)] + [arr(early_rows // 2, WIDE)] * 2
        + [arr(24, WIDE), arr(seam_rows, WIDE)],
        [
            pltpu.VMEM((5236, WIDE), F32),
            pltpu.VMEM((11, 12, 8, WIDE), F32),
            pltpu.VMEM((10, 10, 8, WIDE), F32),
            pltpu.VMEM((880, 2304), BF16),
            pltpu.VMEM((640, 2304), BF16),
            pltpu.VMEM((27 * 256, 256), BF16),
            pltpu.VMEM((seam_rows + early_rows, WIDE), F32),
        ],
        tok3, slope, tail, grown, pre, conv0, conv1, d_rows, d_head,
        name="conv_back", us=21.0, mib=40,
    )
    early = summing(keep, send, count)
    next(early)
    d_mid, grads1, flat2, carry2, *parts = call(
        back_two_kernel,
        [SQUARE, arr(1168, WIDE), arr(3 * (CUTS[3] - CUTS[2]), WIDE), arr(32, WIDE)] + PARTS,
        [pltpu.VMEM((1184, WIDE), F32), pltpu.VMEM((ROWS, WIDE), F32)] + BACKWARD,
        d_own, carry3, lay1, lay2, tok2, save2, lse2, mixed2, mid2, hpre2, mid1, hpre1,
        name="back_two", us=14.0,
    )
    early.send(d_mid)
    parts = passed(parts, -1, sizes)
    step = next(early)
    d_window, flat1, carry1, *parts = call(
        functools.partial(back_shifted_kernel, sizes),
        [SQUARE, arr(3 * (CUTS[2] - CUTS[1]), WIDE), arr(16, WIDE)] + PARTS,
        REGION + [pltpu.VMEM((1200, WIDE), F32), pltpu.VMEM((ROWS, WIDE), F32)] + BACKWARD,
        d_mid, *parts, lay1, window, save1, lse1, mixed1, grads1, carry2,
        name="back_shifted", us=10.5, far=(step,),
    )
    early.send(d_window)
    parts = passed(parts, 1, sizes)
    step = next(early)
    late = call(
        functools.partial(back_first_kernel, sizes),
        [arr(late_rows // 2, WIDE)] * 2,
        [
            pltpu.VMEM((late_rows, WIDE), F32),
            pltpu.VMEM((1572, WIDE), F32),
            pltpu.VMEM((ROWS, WIDE), F32),
        ]
        + BACKWARD,
        d_mid, d_window, *parts, tok1, lay0, lay1, merge, dense, tok0, save0, lse0, mixed0, mid0,
        hpre0, carry1, flat1, flat2, seam,
        name="back_first", us=13.5, far=(step,),
    )
    late_sum = finished(summing(*late, count))
    early = finished(early, late[0])
    gradient, loss, valid_count, norm = call(
        functools.partial(gather_kernel, sizes),
        [arr(LATE_ROWS + EARLY_ROWS, WIDE)] + [arr(1)] * 3,
        [],
        *late_sum, *early, tail, sums,
        name="gather", us=2.5,
    )
    gradient = gradient.reshape(-1)[:NPARAM]
    norm = norm.reshape(())
    scale = jnp.minimum(1.0, clip_norm / (norm + 1e-06))
    new_params, new_first, new_second = adamw(params, gradient, moment_one, moment_two, scale)
    return (
        loss.reshape(()), valid_count.reshape(()), norm,
        new_params, new_first, new_second,
    )


def solution(mesh):
    placed = (
        P("slab", "mp", None, None),
        P("slab", "mp", None),
        P("slab", "mp", None),
        P(),
        P(),
        P(),
    )
    sizes = (mesh.shape["slab"], mesh.shape["mp"])
    return jax.shard_map(
        functools.partial(on_device, sizes),
        mesh=mesh,
        in_specs=placed,
        out_specs=(P(), P(), P(), P(), P(), P()),
        check_vma=False,
    )
```

```python
import functools

import jax
import jax.numpy as jnp
from jax import lax
from jax.experimental import pallas as pl
from jax.experimental.pallas import tpu as pltpu
from jax.sharding import PartitionSpec as P

EMB = 96
HEADS = 6
HDIM = 16
HID = 384
MERGE = 384
CLASSES = 14
WIN = 7
SHIFT = 3
LAYERS = 3
STEP = 10

F32 = jnp.float32
BF16 = jnp.bfloat16
eps_norm = 1e-05
beta_one = 0.9
beta_two = 0.999
adam_eps = 1e-08
learn_rate = 0.05
decay_rate = 0.05
clip_norm = 0.01

VOX = WIN * WIN * WIN
ROWS = 384
BLK = 128
WIDE = 128
PLANE = WIN * WIN
FAR = WIN - SHIFT
ROWS_A = SHIFT * FAR * WIN
ROWS_B = FAR * SHIFT * WIN
ROWS_C = SHIFT * SHIFT * WIN

MERGE_ROWS = 392
LAYER_ROWS = 1165
TAP_ROWS = 27 * EMB
GROUPS = 2280
NPARAM = 872558
HEAD_ROW = 6806
HEAD_ROWS = 11
HEAD_LANE = 32
LATE_ROWS = 3072
EARLY_ROWS = 3840
LAYER_BASE = (98, 389, 680)
CONV_BASE = (971, 1620)
CUTS = (0, 392, 688, 976, 2280)

R_QKV, R_QKVB, R_PROJ, R_PROJB = 4, 292, 295, 391
R_HID, R_HIDB, R_OUT, R_OUTB = 392, 776, 780, 1164


def iota(shape, dim):
    return lax.broadcasted_iota(jnp.int32, shape, dim)


def split(x):
    hi = x.astype(BF16)
    return hi, (x - hi.astype(F32)).astype(BF16)


def pair(x):
    return jnp.concatenate(split(x), 1)


def fold(y):
    half = y.shape[1] // 2
    return y[:, :half] + y[:, half:]


def fold_rows(y):
    half = y.shape[0] // 2
    return y[:half] + y[half:]


def dot(a, b):
    return jnp.dot(a, b, preferred_element_type=F32)


def dot_nt(a, b):
    return lax.dot_general(a, b, (((1,), (1,)), ((), ())), preferred_element_type=F32)


def weight_nn(w):
    top = pair(w)
    return jnp.concatenate([top, top], 0)


def weight_nt(w):
    hi, lo = split(w)
    return jnp.concatenate(
        [jnp.concatenate([hi, hi], 1), jnp.concatenate([lo, lo], 1)], 0
    )


def mm(x, w):
    return fold(dot(pair(x), weight_nn(w)))


def mm_nt(x, w):
    return fold(dot_nt(pair(x), weight_nt(w)))


def rows_t(x):
    return jnp.concatenate(split(x.T), 0)


def mm_tn(xt, y):
    return fold_rows(fold(dot(xt, pair(y))))


def deep(w):
    return jnp.concatenate([w, jnp.zeros((WIDE - EMB, w.shape[1]), F32)], 0)


def roll(x, shift, axis):
    return pltpu.roll(x, shift, axis)


def four_to_three(y):
    lane = iota(y[0].shape, 1)
    a = jnp.where(lane < 96, y[0], roll(y[1], 96, 1))
    b = jnp.where(lane < 64, roll(y[1], 96, 1), roll(y[2], 64, 1))
    c = jnp.where(lane < 32, roll(y[2], 64, 1), roll(y[3], 32, 1))
    return a, b, c


def three_to_four(x):
    lane = iota(x[0].shape, 1)
    live = lane < EMB
    a = x[0]
    b = jnp.where(lane < 32, roll(x[0], 32, 1), roll(x[1], 32, 1))
    c = jnp.where(lane < 64, roll(x[1], 64, 1), roll(x[2], 64, 1))
    d = roll(x[2], 96, 1)
    return tuple(jnp.where(live, v, 0.0) for v in (a, b, c, d))


def hidden_rows(ref, start, count):
    return jnp.concatenate(
        four_to_three([ref[pl.ds(start + c, count, stride=4), :] for c in range(4)]), 1
    )


def put_hidden_rows(ref, start, count, x):
    parts = three_to_four([x[:, i * WIDE : (i + 1) * WIDE] for i in range(3)])
    for c in range(4):
        ref[pl.ds(start + c, count, stride=4), :] = parts[c]


def flatten(ref, start, groups, out):
    parts = four_to_three([ref[pl.ds(start + c, groups, stride=4), :] for c in range(4)])
    for c in range(3):
        out[pl.ds(c, groups, stride=3), :] = parts[c]


def norm_stats(x):
    live = iota(x.shape, 1) < EMB
    mean = jnp.sum(x, 1, keepdims=True) * (1.0 / EMB)
    centred = jnp.where(live, x - mean, 0.0)
    var = jnp.sum(centred * centred, 1, keepdims=True) * (1.0 / EMB)
    inv = lax.rsqrt(var + eps_norm)
    return centred * inv, inv


def norm(x, gain, bias):
    hat, _ = norm_stats(x)
    return hat * gain + bias


def norm_back(hat, inv, gain, grad):
    up = grad * gain
    one = jnp.sum(up, 1, keepdims=True) * (1.0 / EMB)
    two = jnp.sum(up * hat, 1, keepdims=True) * (1.0 / EMB)
    live = iota(hat.shape, 1) < EMB
    return jnp.where(live, inv * (up - one - hat * two), 0.0)


def colsum(x):
    return jnp.sum(x, 0, keepdims=True)


def gelu(x):
    return 0.5 * x * (1.0 + lax.erf(x * (0.5**0.5)))


def gelu_both(x):
    cdf = 0.5 * (1.0 + lax.erf(x * (0.5**0.5)))
    slope = cdf + x * (jnp.exp(x * x * -0.5) * 0.3989422804014327)
    return x * cdf, slope


def head_groups(x):
    lane = iota(x.shape, 1)
    swapped = roll(x, 64, 1)
    return jnp.where(lane < 64, x, swapped), jnp.where(lane < 64, swapped, x)


def as_left(x):
    both = []
    low = iota(x.shape, 1) < 64
    for part in head_groups(x):
        hi = part.astype(BF16).astype(F32)
        one = jnp.where(low, hi, part - hi).astype(BF16)
        both.append(jnp.concatenate([one, one], 1))
    return both


def as_right(x):
    return [pair(part) for part in head_groups(x)]


def head_mask(h, width):
    lane = iota((1, width), 1)
    lane = jnp.bitwise_and(lane, 63)
    low = jnp.bitwise_and(h, 3) * HDIM
    return jnp.where((lane >= low) & (lane < low + HDIM), 1.0, 0.0)


def own_lanes(h):
    lane = iota((1, WIDE), 1)
    return jnp.where((lane >= h * HDIM) & (lane < (h + 1) * HDIM), 1.0, 0.0)


def scores(q, k, h, rows, region):
    left = q * head_mask(h, 2 * WIDE).astype(BF16)
    s = dot_nt(left, k)
    if region is not None:
        region_rows, region_lanes = region
        here = region_rows[rows, 0:1]
        s = s + jnp.where(here == region_lanes[0:1, :], 0.0, -100.0)
    return jnp.where(iota(s.shape, 1) < VOX, s, -1e30)


def attention(normed, layer, save, lse, mixed, left, right, values, region=None):
    x = pair(normed)
    qkv = []
    for i in range(3):
        w = deep(layer[pl.ds(R_QKV + i, EMB, stride=3), :])
        y = fold(dot(x, weight_nn(w))) + layer[R_QKVB + i : R_QKVB + i + 1, :]
        if i == 0:
            y = y * HDIM**-0.5
        save[:, i * WIDE : (i + 1) * WIDE] = y
        qkv.append(y)
    for g, part in enumerate(as_left(qkv[0])):
        left[g] = part
    for g, part in enumerate(as_right(qkv[1])):
        right[g] = part
    v = pair(qkv[2])
    values[0:ROWS, :] = v
    values[ROWS : 2 * ROWS, :] = v
    mixed[...] = jnp.zeros_like(mixed)
    lse[...] = jnp.zeros_like(lse)

    def per_head(h, carry):
        g = lax.div(h, 4)
        lanes = own_lanes(h)
        at_h = jnp.where(iota((1, WIDE), 1) == h, 1.0, 0.0)
        for b in range(ROWS // BLK):
            rows = slice(b * BLK, (b + 1) * BLK)
            s = scores(left[g, rows, :], right[g], h, rows, region)
            top = jnp.max(s, 1, keepdims=True)
            e = jnp.exp(s - top)
            total = jnp.sum(e, 1, keepdims=True)
            o = fold(dot(pair(e), values[...]))
            mixed[rows, :] += o * (lanes / total)
            lse[rows, :] += (top + jnp.log(total)) * at_h
        return carry

    lax.fori_loop(0, HEADS, per_head, 0)
    proj = deep(layer[R_PROJ : R_PROJ + EMB, :])
    return mm(mixed[...], proj) + layer[R_PROJB : R_PROJB + 1, :]


def attention_back(grad, normed, layer, save, lse, mixed, sc, grads, at, region=None):
    left, right, gleft, vright, keys, dq, dkv_t, weights, slopes, q_t, do_t, dmix = sc
    proj = deep(layer[R_PROJ : R_PROJ + EMB, :])
    grads[at + R_PROJ : at + R_PROJ + EMB, :] = mm_tn(rows_t(mixed[...]), grad)[:EMB]
    grads[at + R_PROJB : at + R_PROJB + 1, :] = colsum(grad)
    d_mixed = mm_nt(grad, proj)
    dmix[...] = d_mixed
    q, k, v = (save[:, i * WIDE : (i + 1) * WIDE] for i in range(3))
    for g, part in enumerate(as_left(q)):
        left[g] = part
    for g, part in enumerate(as_right(k)):
        right[g] = part
    for g, part in enumerate(as_left(d_mixed)):
        gleft[g] = part
    for g, part in enumerate(as_right(v)):
        vright[g] = part
    kk = pair(k)
    keys[0:ROWS, :] = kk
    keys[ROWS : 2 * ROWS, :] = kk
    for ref, x in ((q_t, q), (do_t, d_mixed)):
        hi, lo = split(x.T)
        ref[0] = hi
        ref[1] = lo
    dq[...] = jnp.zeros_like(dq)
    dkv_t[...] = jnp.zeros_like(dkv_t)

    def per_head(h, carry):
        g = lax.div(h, 4)
        lanes = own_lanes(h)
        at_h = jnp.where(iota((1, WIDE), 1) == h, 1.0, 0.0)
        mask = head_mask(h, 2 * WIDE).astype(BF16)
        for b in range(ROWS // BLK):
            rows = slice(b * BLK, (b + 1) * BLK)
            s = scores(left[g, rows, :], right[g], h, rows, region)
            level = jnp.sum(lse[rows, :] * at_h, 1, keepdims=True)
            p = jnp.exp(s - level)
            dp = dot_nt(gleft[g, rows, :] * mask, vright[g])
            delta = jnp.sum(dmix[rows, :] * mixed[rows, :] * lanes, 1, keepdims=True)
            ds = p * (dp - delta)
            both = pair(ds)
            weights[rows, :] = pair(p)
            slopes[rows, :] = both
            dq[rows, :] += fold(dot(both, keys[...])) * lanes
        here = pl.multiple_of(h * HDIM, HDIM)
        for i, (t, m) in enumerate(((q_t, slopes), (do_t, weights))):
            lhs = jnp.concatenate([t[0, pl.ds(here, HDIM), :], t[1, pl.ds(here, HDIM), :]], 0)
            out = fold_rows(fold(dot(lhs, m[...])))
            dkv_t[i, pl.ds(here, HDIM), :] = out
        return carry

    lax.fori_loop(0, HEADS, per_head, 0)
    d_q = dq[...] * HDIM**-0.5
    d_k = dkv_t[0].T
    d_v = dkv_t[1].T
    x_t = rows_t(normed)
    d_normed = None
    for i, d in enumerate((d_q, d_k, d_v)):
        grads[pl.ds(at + R_QKV + i, EMB, stride=3), :] = mm_tn(x_t, d)[:EMB]
        grads[at + R_QKVB + i : at + R_QKVB + i + 1, :] = colsum(d)
        part = mm_nt(d, deep(layer[pl.ds(R_QKV + i, EMB, stride=3), :]))
        d_normed = part if d_normed is None else d_normed + part
    return d_normed


def mlp(middle, layer, hpre):
    normed = norm(middle, layer[2:3, :], layer[3:4, :])
    w = deep(hidden_rows(layer, R_HID, EMB))
    pre = mm(normed, w) + hidden_rows(layer, R_HIDB, 1)
    hpre[...] = pre
    out = mm(gelu(pre), layer[R_OUT : R_OUT + HID, :])
    return middle + out + layer[R_OUTB : R_OUTB + 1, :]


def mlp_back(grad, middle, hpre, layer, grads, at):
    hat, inv = norm_stats(middle)
    normed = hat * layer[2:3, :] + layer[3:4, :]
    act, slope = gelu_both(hpre[...])
    grads[at + R_OUTB : at + R_OUTB + 1, :] = colsum(grad)
    grads[at + R_OUT : at + R_OUT + HID, :] = mm_tn(rows_t(grad), act).T
    d_pre = mm_nt(grad, layer[R_OUT : R_OUT + HID, :]) * slope
    put_hidden_rows(grads, at + R_HIDB, 1, colsum(d_pre))
    put_hidden_rows(grads, at + R_HID, EMB, mm_tn(rows_t(normed), d_pre)[:EMB])
    d_normed = mm_nt(d_pre, deep(hidden_rows(layer, R_HID, EMB)))
    grads[at + 2 : at + 3, :] = colsum(d_normed * hat)
    grads[at + 3 : at + 4, :] = colsum(d_normed)
    return grad + norm_back(hat, inv, layer[2:3, :], d_normed)


def pre_norm_back(grad, tokens, layer, grads, at):
    hat, inv = norm_stats(tokens)
    grads[at : at + 1, :] = colsum(grad * hat)
    grads[at + 1 : at + 2, :] = colsum(grad)
    return norm_back(hat, inv, layer[0:1, :], grad)


def region_of(rows, sizes):
    d = lax.shift_right_logical(rows * 1338, 16)
    line = lax.shift_right_logical(rows * 9363, 16)
    places = (d, line - d * WIN, rows - line * WIN)
    starts = (lax.axis_index("slab") * WIN, lax.axis_index("mp") * WIN, 0)
    total = None
    for place, start, blocks in zip(places, starts, sizes + (1,)):
        turned = jnp.where(place < SHIFT, place + FAR, place - SHIFT) + start
        length = WIN * blocks
        part = jnp.where(turned < length - WIN, 0, jnp.where(turned < length - SHIFT, 1, 2))
        total = part if total is None else total * 3 + part
    return total


def put_regions(region, sizes):
    region_rows, region_lanes = region
    region_rows[...] = region_of(iota((ROWS, WIDE), 0), sizes).astype(F32)
    region_lanes[...] = region_of(iota((8, ROWS), 1), sizes).astype(F32)


def send_parts(ref, a, b, c):
    far = FAR * WIN
    near = SHIFT * WIN
    for d in range(SHIFT):
        base = d * PLANE
        c[d * near : (d + 1) * near, :] = ref[base : base + near, :]
        a[d * far : (d + 1) * far, :] = ref[base + near : base + PLANE, :]
    for d in range(FAR):
        base = (d + SHIFT) * PLANE
        b[d * near : (d + 1) * near, :] = ref[base : base + near, :]


def take_parts(own, a, b, c, out):
    far = FAR * WIN
    near = SHIFT * WIN
    for d in range(WIN):
        base = d * PLANE
        if d < SHIFT:
            out[base : base + near, :] = c[d * near : (d + 1) * near, :]
            out[base + near : base + PLANE, :] = a[d * far : (d + 1) * far, :]
        else:
            e = d - SHIFT
            out[base : base + near, :] = b[e * near : (e + 1) * near, :]
            out[base + near : base + PLANE, :] = own[base + near : base + PLANE, :]
    out[VOX:, :] = jnp.zeros((ROWS - VOX, WIDE), F32)


def span_of(groups):
    low, high = groups
    first = 3 * low // 8 * 8
    last = -(-3 * high // 8) * 8
    return first, min(last, NPARAM // WIDE // 8 * 8) - first


def copied(params, groups, flat, sem):
    first, rows = span_of(groups)
    size = rows * WIDE
    return pltpu.make_async_copy(
        params.at[pl.ds(first * WIDE, size)], flat.at[pl.ds(0, size)], sem
    )


def relay(groups, flat, out, square, last=None):
    low, high = groups
    first, rows = span_of(groups)
    square[0:rows, :] = flat[0 : rows * WIDE].reshape(rows, WIDE)
    if last is not None:
        square[rows : rows + 24, :] = jnp.zeros((24, WIDE), F32)
        square[rows : rows + 1, 0 : last.shape[0]] = last[...].reshape(1, last.shape[0])
    skip = 3 * low - first
    n = high - low
    parts = three_to_four([square[pl.ds(skip + c, n, stride=3), :] for c in range(3)])
    for c in range(4):
        out[pl.ds(c, n, stride=4), :] = parts[c]


FIRST_SPANS = ((0, 98), (98, 392))
LAYER_SPANS = ((389, 681), (680, 972))
CONV_SPANS = ((971, 1620), (1620, GROUPS))


def prep_kernel(spans, params, *refs, last=None):
    outs, (flats, square, sems) = refs[: len(spans)], refs[-3:]
    for i, groups in enumerate(spans):
        copied(params, groups, flats[i], sems.at[i]).start()
    for i, groups in enumerate(spans):
        copied(params, groups, flats[i], sems.at[i]).wait()
        relay(groups, flats[i], outs[i], square, last if i == len(spans) - 1 else None)


def head_picks():
    width = HEAD_ROWS * WIDE
    place = iota((WIDE, width), 1) - HEAD_LANE
    row = iota((WIDE, width), 0)
    here = (place >= row * CLASSES) & (place < (row + 1) * CLASSES) & (row <= EMB)
    place = iota((width, WIDE), 0) - HEAD_LANE
    col = iota((width, WIDE), 1)
    row = lax.shift_right_logical(place * 4682, 16)
    there = (place - row * CLASSES == col) & (place >= 0)
    return jnp.where(here, 1.0, 0.0), jnp.where(there, 1.0, 0.0).astype(BF16)


def prep_conv_kernel(last, params, conv0, conv1, head, *scratch):
    prep_kernel(CONV_SPANS, params, conv0, conv1, *scratch, last=last)
    square = scratch[1]
    first, _ = span_of(CONV_SPANS[1])
    row = jnp.concatenate(
        [square[HEAD_ROW + i - first : HEAD_ROW + i - first + 1, :] for i in range(HEAD_ROWS)], 1
    )
    here, there = head_picks()
    hi, lo = split(here * row)
    head[...] = dot(hi, there) + dot(lo, there)


def head_rows(d_head, out, at):
    here, there = head_picks()
    hi, lo = split(d_head)
    spread = (dot_nt(hi, there) + dot_nt(lo, there)) * here
    row = colsum(spread)
    for i in range(HEAD_ROWS):
        out[at + i : at + i + 1, :] += row[:, i * WIDE : (i + 1) * WIDE]


class Rows:
    def __init__(self, ref, at):
        self.ref, self.at = ref, at

    def __getitem__(self, key):
        rows, lanes = key
        if isinstance(rows, slice):
            rows = slice(rows.start + self.at, rows.stop + self.at)
        else:
            rows = pl.ds(rows.start + self.at, rows.size, stride=rows.stride)
        return self.ref[rows, lanes]


def merged_norm(x):
    mean = jnp.sum(x, 1, keepdims=True) * (1.0 / MERGE)
    centred = x - mean
    var = jnp.sum(centred * centred, 1, keepdims=True) * (1.0 / MERGE)
    return centred * lax.rsqrt(var + eps_norm)


def first_kernel(
    feats, merge, lay0,
    dense, tok0, save, lse, mixed, middle, hpre, tok1, ahead, pa, pb, pc,
    left, right, values,
):
    dense[VOX:, :] = jnp.zeros((ROWS - VOX, MERGE), F32)
    for line in range(PLANE):
        dense[line * WIN : (line + 1) * WIN, :] = feats[line]
    hat = merged_norm(dense[...])
    normed = hat * hidden_rows(merge, 0, 1) + hidden_rows(merge, 4, 1)
    tokens = mm(normed, merge[8 : 8 + MERGE, :])
    tok0[...] = tokens
    layer = Rows(lay0, 0)
    normed = norm(tokens, layer[0:1, :], layer[1:2, :])
    attended = attention(normed, layer, save, lse, mixed, left, right, values)
    mid = tokens + attended
    middle[...] = mid
    tokens = mlp(mid, layer, hpre)
    tok1[...] = tokens
    ahead[...] = norm(tokens, layer[1165:1166, :], layer[1166:1167, :])
    send_parts(ahead, pa, pb, pc)


def shifted_kernel(
    sizes,
    own, pa, pb, pc, lay1,
    window, save, lse, mixed, out, qa, qb, qc,
    region_rows, region_lanes, left, right, values,
):
    put_regions((region_rows, region_lanes), sizes)
    take_parts(own, pa, pb, pc, window)
    out[...] = attention(
        window[...], Rows(lay1, 1), save, lse, mixed, left, right, values,
        (region_rows, region_lanes),
    )
    send_parts(out, qa, qb, qc)


def to_lines(ref, out):
    for line in range(PLANE):
        out[line, 0:WIN, :] = ref[line * WIN : (line + 1) * WIN, :]
        out[line, WIN:8, :] = jnp.zeros((8 - WIN, WIDE), F32)


def from_lines(ref, out):
    out[VOX:, :] = jnp.zeros((ROWS - VOX, WIDE), F32)
    for line in range(PLANE):
        out[line * WIN : (line + 1) * WIN, :] = ref[line, 0:WIN, :]


def send_sides(lines, low_d, high_d, low_h, high_h):
    low_d[...] = lines[0 : 2 * WIN]
    high_d[...] = lines[(WIN - 2) * WIN :]
    for d in range(WIN):
        low_h[2 * d : 2 * d + 2] = lines[d * WIN : d * WIN + 2]
        high_h[2 * d : 2 * d + 2] = lines[d * WIN + WIN - 2 : (d + 1) * WIN]


def second_kernel(
    tok1, own, qa, qb, qc, lay1, lay2,
    mid1, hpre1, tok2, save, lse, mixed, mid2, hpre2, lines,
    s0, s1, s2, s3,
    attended, left, right, values,
):
    take_parts(own, qa, qb, qc, attended)
    mid = tok1[...] + attended[...]
    mid1[...] = mid
    tokens = mlp(mid, Rows(lay1, 1), hpre1)
    tok2[...] = tokens
    layer = Rows(lay2, 2)
    normed = norm(tokens, layer[0:1, :], layer[1:2, :])
    mid = tokens + attention(normed, layer, save, lse, mixed, left, right, values)
    mid2[...] = mid
    attended[...] = mlp(mid, layer, hpre2)
    to_lines(attended, lines)
    send_sides(lines, s0, s1, s2, s3)


def grown_lines(own, low_d, high_d, low_h, high_h, out):
    out[...] = jnp.zeros_like(out)
    for d in range(WIN):
        out[d + 2, 2 : 2 + WIN] = own[d * WIN : (d + 1) * WIN]
    for d in range(2):
        out[d, 2 : 2 + WIN] = low_d[d * WIN : (d + 1) * WIN]
        out[d + 9, 2 : 2 + WIN] = high_d[d * WIN : (d + 1) * WIN]
    for d in range(11):
        out[d, 0:2] = low_h[2 * d : 2 * d + 2]
        out[d, 9:11] = high_h[2 * d : 2 * d + 2]


def put_marks(labels, valid, out):
    across = iota((8, WIN), 1) == iota((8, WIN), 0)
    classes = iota((8, WIDE), 1) - EMB
    for d in range(WIN):
        code = jnp.where(valid[d] == 1, labels[d], -1 - EMB - WIDE)
        code = code.astype(F32)
        for h in range(WIN):
            line = jnp.where(across, code[h : h + 1, :], 0.0)
            column = jnp.sum(line, 1, keepdims=True)
            mark = jnp.where(column == classes.astype(F32), 1.0, 0.0)
            out[d * WIN + h] = jnp.where(iota((8, WIDE), 0) < WIN, mark, 0.0)


def taps(source, first_plane, planes, first_line, lines, out):
    def per_plane(d, carry):
        for c in range(3):
            for b in range(3):
                x = source[d + first_plane, first_line + b : first_line + b + lines]
                if c != 1:
                    x = roll(x, 1 if c == 0 else 7, 1)
                x = pair(x.reshape(lines * 8, WIDE))
                at = pl.multiple_of(d * (lines * 8), lines * 8)
                t = b * 3 + c
                out[pl.ds(at, lines * 8), t * 256 : (t + 1) * 256] = x
        return carry

    lax.fori_loop(0, planes, per_plane, 0)


def tap_weights(ref, at, out):
    def per_tap(i, carry):
        w = deep(ref[pl.ds(i * EMB + at, EMB), :])
        out[pl.ds(pl.multiple_of(i * 256, 256), 256), :] = weight_nn(w)
        return carry

    lax.fori_loop(0, 27, per_tap, 0)


def tap_weights_back(ref, at, out):
    def per_tap(i, carry):
        w = deep(ref[pl.ds((26 - i) * EMB + at, EMB), :]).T
        out[pl.ds(pl.multiple_of(i * 256, 256), 256), :] = weight_nn(w)
        return carry

    lax.fori_loop(0, 27, per_tap, 0)


def conv(side, weights, planes, pitch, at_once, put):
    rows = at_once * pitch
    for start in range(0, planes, at_once):
        total = None
        for a in range(3):
            low = (start + a) * pitch
            part = dot(side[low : low + rows, :], weights[a * 2304 : (a + 1) * 2304, :])
            total = part if total is None else total + part
        put(start, fold(total))


def conv_weight_grad(side, grad_rows, pitch, out, at):
    rows = 512
    g = jnp.concatenate([grad_rows, jnp.zeros((rows - grad_rows.shape[0], WIDE), F32)], 0)
    left = rows_t(g)
    for a in range(3):
        for bc in range(9):
            y = dot(left, side[a * pitch : a * pitch + rows, bc * 256 : (bc + 1) * 256])
            y = fold_rows(fold(y)).T
            t = a * 9 + bc
            out[at + t * EMB : at + (t + 1) * EMB, :] = y[:EMB]


def volume_mask(sizes, planes, lines, reach, real_lines):
    slab, row = lax.axis_index("slab"), lax.axis_index("mp")
    ends = (slab == 0, slab == sizes[0] - 1, row == 0, row == sizes[1] - 1)
    shape = (planes, lines, 8, WIDE)
    d, h, w = iota(shape, 0), iota(shape, 1), iota(shape, 2)
    low_d = jnp.where(ends[0], reach, 0)
    high_d = jnp.where(ends[1], planes - reach, planes)
    low_h = jnp.where(ends[2], reach, 0)
    high_h = jnp.where(ends[3], real_lines - reach, real_lines)
    inside = (d >= low_d) & (d < high_d) & (h >= low_h) & (h < high_h) & (w < WIN)
    return jnp.where(inside, 1.0, 0.0)


def conv_kernel(
    sizes,
    own, s0, s1, s2, s3, labels, valid, conv0, conv1,
    grown, pre, tok, stats, t0, t1, t2, t3,
    act, side, side_own, weights, marks,
):
    grown_lines(own, s0, s1, s2, s3, grown)
    put_marks(labels, valid, marks)
    tap_weights(conv0, 3, weights)
    taps(grown, 0, 11, 0, 10, side)
    bias0 = conv0[3 + TAP_ROWS : 4 + TAP_ROWS, :]
    inside = volume_mask(sizes, 9, 10, 1, 9)

    def put(start, y):
        z = (y + bias0).reshape(3, 10, 8, WIDE)
        pre[start : start + 3] = z
        act[start : start + 3] = gelu(z) * inside[start : start + 3]

    conv(side, weights, 9, 80, 3, put)
    tap_weights(conv1, 0, weights)
    taps(act, 0, 9, 0, 8, side_own)
    bias1 = conv1[TAP_ROWS : TAP_ROWS + 1, :]
    sums = []

    def put_own(start, y):
        y = (y + bias1).reshape(WIN, 8, 8, WIDE)[:, 0:WIN]
        y = y + own[...].reshape(WIN, WIN, 8, WIDE)
        y = jnp.where(iota(y.shape, 2) < WIN, y, 0.0).reshape(PLANE, 8, WIDE)
        tok[...] = y + marks[...]
        send_sides(tok, t0, t1, t2, t3)
        flat = y.reshape(PLANE * 8, WIDE)
        sums.append(colsum(flat))
        sums.append(colsum(flat * flat))

    conv(side_own, weights, WIN, 64, WIN, put_own)
    count = jnp.sum(marks[...].reshape(PLANE * 8, WIDE))
    row = iota((8, WIDE), 0)
    stats[...] = (
        jnp.where(row == 0, sums[0], 0.0)
        + jnp.where(row == 1, sums[1], 0.0)
        + jnp.where(row == 2, count, 0.0)
    )


def head_kernel(
    voxels,
    own, s0, s1, s2, s3, all_sums, conv1, head_w,
    grown, slope_out, stats, d_head, d_rows, sums,
):
    sums[...] = jnp.sum(all_sums[...].reshape(-1, 8, WIDE), 0)
    grown_lines(own, s0, s1, s2, s3, grown)
    rows = 11 * 12 * 8
    both = grown[...].reshape(rows, WIDE)
    lane = iota((rows, WIDE), 1)
    tokens = jnp.where(lane < EMB, both, 0.0)
    target = jnp.where(lane < CLASSES, roll(both, WIDE - EMB, 1), 0.0)
    live = jnp.sum(target, 1, keepdims=True)
    count = F32(voxels)
    average = sums[0:1, :] / count
    spread = sums[1:2, :] / count - average * average
    inv = lax.rsqrt(spread + eps_norm)
    gain = conv1[TAP_ROWS + 1 : TAP_ROWS + 2, :]
    bias = conv1[TAP_ROWS + 2 : TAP_ROWS + 3, :]
    hat = (tokens - average) * inv
    act, slope = gelu_both(hat * gain + bias)
    act = jnp.where(lane == EMB, 1.0, act)
    w = head_w[...]
    logits = mm(act, w)
    logits = jnp.where(lane < CLASSES, logits, -1e30)
    top = jnp.max(logits, 1, keepdims=True)
    e = jnp.exp(logits - top)
    total = jnp.sum(e, 1, keepdims=True)
    logp = logits - top - jnp.log(total)
    scale = 1.0 / sums[2:3, 0:1]
    d_logits = (e / total * live - target) * scale
    d_normed = jnp.where(lane < EMB, mm_nt(d_logits, w) * slope, 0.0)
    d_tokens = d_normed * gain * inv
    slope_out[...] = d_tokens.reshape(11, 12, 8, WIDE)

    def own_rows(x):
        x = x.reshape(11, 12, 8, WIDE)[2:9, 2:9]
        x = jnp.where(iota(x.shape, 2) < WIN, x, 0.0)
        return x.reshape(PLANE * 8, WIDE)

    loss = -jnp.sum(own_rows(target * jnp.where(lane < CLASSES, logp, 0.0)))
    own_d = own_rows(d_logits)
    own_n = own_rows(d_normed)
    own_hat = own_rows(hat)
    zeros = jnp.zeros((512 - PLANE * 8, WIDE), F32)
    left = rows_t(jnp.concatenate([own_d, zeros], 0))
    d_head[...] = mm_tn(left, jnp.concatenate([own_rows(act), zeros], 0)).T
    d_gain = colsum(own_n * own_hat)
    d_bias = colsum(own_n)
    d_average = -d_bias * gain * inv
    d_spread = d_gain * gain * inv * inv * -0.5
    d_two = d_spread / count
    d_one = (d_average - 2.0 * average * d_spread) / count
    row = iota((8, WIDE), 0)
    live_lane = iota((8, WIDE), 1) < EMB
    stats[...] = (
        jnp.where((row == 0) & live_lane, d_one, 0.0)
        + jnp.where((row == 1) & live_lane, d_two, 0.0)
        + jnp.where(row == 2, loss, 0.0)
    )
    d_rows[...] = (
        jnp.where(row == 0, d_gain, 0.0)
        + jnp.where(row == 1, d_bias, 0.0)
    )


def conv_back_kernel(
    sizes,
    tok, slope, all_sums, grown, pre, conv0, conv1, d_rows, d_head,
    d_own, keep, send, carry, seam, sums,
    grads, dgrown, act, side, side_own, weights, flat,
):
    sums[...] = jnp.sum(all_sums[...].reshape(-1, 8, WIDE), 0)
    lane = iota((11, 12, 8, WIDE), 3)
    inside = volume_mask(sizes, 11, 12, 2, 11)
    steady = sums[0:1, :].reshape(1, 1, 1, WIDE)
    rising = 2.0 * sums[1:2, :].reshape(1, 1, 1, WIDE)
    d_tok = slope[...] + jnp.where(lane < EMB, (steady + tok[...] * rising) * inside, 0.0)
    dgrown[...] = d_tok
    grads[5191:, :] = jnp.zeros((45, WIDE), F32)
    grads[0:8, :] = jnp.zeros((8, WIDE), F32)
    grads[5189:5191, :] = d_rows[0:2, :]
    own = dgrown[2:9, 2:10]
    line = iota(own.shape, 1)
    own = jnp.where(line < WIN, own, 0.0).reshape(WIN * 64, WIDE)
    grads[5188:5189, :] = colsum(own)

    near = volume_mask(sizes, 9, 10, 1, 9)
    act[0:9] = gelu(pre[...]) * near
    act[9:10] = jnp.zeros((1, 10, 8, WIDE), F32)
    taps(act, 0, 10, 0, 8, side_own)
    conv_weight_grad(side_own, own, 64, grads, 2596)
    tap_weights_back(conv1, 0, weights)
    taps(dgrown, 0, 11, 0, 10, side)

    def put(start, y):
        _, s = gelu_both(pre[start : start + 3])
        z = y.reshape(3, 10, 8, WIDE) * s * near[start : start + 3]
        act[start : start + 3] = z

    conv(side, weights, 9, 80, 3, put)

    own = act[1:8, 1:9]
    line = iota(own.shape, 1)
    own = jnp.where(line < WIN, own, 0.0).reshape(WIN * 64, WIDE)
    grads[2595:2596, :] = colsum(own)
    taps(grown, 1, 10, 1, 8, side_own)
    conv_weight_grad(side_own, own, 64, grads, 3)
    carry[...] = grads[0:24, :]
    flat[3 * (GROUPS - CUTS[3]) :, :] = jnp.zeros((flat.shape[0] - 3912, WIDE), F32)
    flatten(grads, 20, GROUPS - CUTS[3], flat)
    start = 3 * CUTS[3]
    head_rows(d_head[...], flat, HEAD_ROW - start)
    seam[...] = flat[0 : LATE_ROWS - start, :]
    scatter(sizes, flat, LATE_ROWS - start, keep, send)
    tap_weights_back(conv0, 3, weights)
    taps(act, 0, 9, 0, 8, side_own)

    def put_own(start, y):
        y = y.reshape(WIN, 8, 8, WIDE)[:, 0:WIN] + dgrown[2:9, 2:9]
        y = jnp.where(iota(y.shape, 2) < WIN, y, 0.0)
        d_own[...] = y.reshape(PLANE, 8, WIDE)

    conv(side_own, weights, WIN, 64, WIN, put_own)


def back_mlp_kernel(d_own, lay2, mid2, hpre2, d_mid, grads, dense):
    from_lines(d_own, dense)
    grads[...] = jnp.zeros_like(grads)
    d_mid[...] = mlp_back(dense[...], mid2[...], hpre2, Rows(lay2, 2), grads, 2)


def back_two_kernel(
    d_mid2, grads2, carry, lay1, lay2, tok2, save, lse, mixed, mid1, hpre1,
    d_mid, grads1, flat, carry2, pa, pb, pc,
    grads, *sc,
):
    layer = Rows(lay2, 2)
    grads[0:1168, :] = grads2[...]
    d = d_mid2[...]
    tokens = tok2[...]
    normed = norm(tokens, layer[0:1, :], layer[1:2, :])
    d_normed = attention_back(d, normed, layer, save, lse, mixed, sc, grads, 2)
    d = d + pre_norm_back(d_normed, tokens, layer, grads, 2)
    grads[1167:1184, :] = carry[3:20, :]
    flatten(grads, 32, CUTS[3] - CUTS[2], flat)
    carry2[...] = grads[0:32, :]
    layer = Rows(lay1, 1)
    d = mlp_back(d, mid1[...], hpre1, layer, grads1, 1)
    d_mid[...] = d
    send_parts(d_mid, pa, pb, pc)


def back_shifted_kernel(
    sizes,
    own, pa, pb, pc, lay1, window, save, lse, mixed, grads1, carry2, _,
    d_window, flat, carry1, qa, qb, qc,
    region_rows, region_lanes, grads, grad, *sc,
):
    put_regions((region_rows, region_lanes), sizes)
    take_parts(own, pa, pb, pc, grad)
    grads[0:1168, :] = grads1[...]
    grads[0:3, :] = jnp.zeros((3, WIDE), F32)
    d_window[...] = attention_back(
        grad[...], window[...], Rows(lay1, 1), save, lse, mixed, sc, grads, 1,
        (region_rows, region_lanes),
    )
    send_parts(d_window, qa, qb, qc)
    grads[1166:1196, :] = carry2[2:32, :]
    flatten(grads, 12, CUTS[2] - CUTS[1], flat)
    carry1[...] = grads[0:16, :]


def back_first_kernel(
    sizes,
    d_mid, own, qa, qb, qc, tok1, lay0, lay1, merge, dense, tok0, save, lse, mixed, middle, hpre,
    carry1, flat1, flat2, seam, _,
    keep, send,
    flat, grads, grad, *sc,
):
    take_parts(own, qa, qb, qc, grad)
    grads[1556:1572, :] = carry1[...]
    d = d_mid[...] + pre_norm_back(grad[...], tok1[...], Rows(lay1, 1), grads, 1557)
    layer = Rows(lay0, 0)
    at = MERGE_ROWS
    d = mlp_back(d, middle[...], hpre, layer, grads, at)
    tokens = tok0[...]
    normed = norm(tokens, layer[0:1, :], layer[1:2, :])
    d_normed = attention_back(d, normed, layer, save, lse, mixed, sc, grads, at)
    d = d + pre_norm_back(d_normed, tokens, layer, grads, at)
    live = iota((ROWS, WIDE), 0) < VOX
    d = jnp.where(live, d, 0.0)
    hat = merged_norm(dense[...])
    gain = hidden_rows(merge, 0, 1)
    bias = hidden_rows(merge, 4, 1)
    w = merge[8 : 8 + MERGE, :]
    put_hidden_rows(grads, 8 - 8, 1, jnp.zeros((1, MERGE), F32))
    grads[8 : 8 + MERGE, :] = mm_tn(rows_t(d), hat * gain + bias).T
    d_hat = mm_nt(d, w)
    put_hidden_rows(grads, 0, 1, colsum(d_hat * hat))
    put_hidden_rows(grads, 4, 1, colsum(d_hat))
    flatten(grads, 0, CUTS[1], flat)
    at = 0
    for cut, part in ((CUTS[1], flat1), (CUTS[2], flat2), (CUTS[3], seam)):
        at = 3 * cut
        flat[at : at + part.shape[0], :] = part[...]
    at += seam.shape[0]
    if flat.shape[0] > at:
        flat[at:, :] = jnp.zeros((flat.shape[0] - at, WIDE), F32)
    scatter(sizes, flat, 0, keep, send, fixed=True)


def radices(count):
    steps = [2]
    left = count // 2
    while left > 1:
        steps.append(4 if left >= 4 else 2)
        left //= steps[-1]
    return steps


def block_rows(rows, count):
    return -(-rows // (8 * count)) * 8


def own_number(sizes):
    return lax.axis_index("slab") * sizes[1] + lax.axis_index("mp")


def place_in_half(distance, count):
    place = 0
    shift = 1
    for radix in radices(count)[1:]:
        digit = jnp.bitwise_and(lax.shift_right_logical(distance, shift), radix - 1)
        place = place * radix + digit
        shift += radix.bit_length() - 1
    return place


def scatter(sizes, source, first, keep, send, fixed=False):
    count = sizes[0] * sizes[1]
    rows = keep.shape[0] * 2 // count
    me = own_number(sizes)
    odd = jnp.bitwise_and(me, 1)

    def per_pair(t, carry):
        for block, out in ((2 * t + odd, keep), (2 * t + 1 - odd, send)):
            place = place_in_half(block if fixed else jnp.bitwise_xor(block, me), count)
            at = pl.multiple_of(first + block * rows, 8)
            to = pl.multiple_of(place * rows, 8)
            out[pl.ds(to, rows), :] = source[pl.ds(at, rows), :]
        return carry

    lax.fori_loop(0, count // 2, per_pair, 0)


def traded(value, distance, count):
    pairs = [(i, i ^ distance) for i in range(count)]
    return lax.ppermute(value, ("slab", "mp"), pairs)


def groups_of(count, shift, radix):
    return [
        [base + (k << shift) for k in range(radix)]
        for base in range(count)
        if (base >> shift) & (radix - 1) == 0
    ]


def later(got, after):
    return got if after is None else list(lax.optimization_barrier((*got, after)))[:-1]


def summing(keep, send, count):
    steps = radices(count)
    got = [keep, traded(send, 1, count)]
    shift = 1
    after = yield None
    for radix in steps[1:]:
        got = later(got, after)
        total = sum(got[1:], got[0])
        rows = total.shape[0] // radix
        parts = [total[k * rows : (k + 1) * rows] for k in range(radix)]
        got = parts[:1] + [traded(parts[k], k << shift, count) for k in range(1, radix)]
        shift += radix.bit_length() - 1
        after = yield parts[0]
    got = later(got, after)
    own = sum(got[1:], got[0])
    for radix in reversed(steps[1:]):
        shift -= radix.bit_length() - 1
        got = [own] + [traded(own, k << shift, count) for k in range(1, radix)]
        after = yield own
        own = jnp.concatenate(later(got, after), 0)
        yield own
    yield own, traded(own, 1, count)


def summed_at_once(keep, send, count):
    steps = radices(count)
    own = keep + traded(send, 1, count)
    shift = 1
    for radix in steps[1:]:
        own = lax.all_to_all(
            own, ("slab", "mp"), 0, 0, axis_index_groups=groups_of(count, shift, radix), tiled=True
        )
        own = own.reshape(radix, -1, WIDE)
        own = sum([own[k] for k in range(1, radix)], own[0])
        shift += radix.bit_length() - 1
    for radix in reversed(steps[1:]):
        shift -= radix.bit_length() - 1
        got = [own] + [traded(own, k << shift, count) for k in range(1, radix)]
        own = jnp.concatenate(got, 0)
    return own, traded(own, 1, count)


def finished(chain, after=None):
    last = next(chain) if after is None else chain.send(after)
    while not isinstance(last, tuple):
        last = next(chain)
    return last


def exchanged(value, axes, count):
    value = jnp.broadcast_to(value, (count, *value.shape)).reshape(-1, WIDE)
    return lax.all_to_all(value, axes, 0, 0, tiled=True)


def gather_kernel(
    sizes, late, late_other, early, early_other, tail, sums, grad, loss, valid, norm
):
    count = sizes[0] * sizes[1]
    me = own_number(sizes)
    total = jnp.zeros((8, WIDE), F32)
    for ref in (late, late_other, early, early_other):
        x = ref[...]
        total = total + jnp.sum((x * x).reshape(-1, 8, WIDE), 0)
    norm[0] = jnp.sqrt(jnp.sum(total))
    loss[0] = jnp.sum(tail[2:3, 0:1])
    valid[0] = jnp.sum(sums[2:3, 0:1])
    first = 0
    for own, other, size in ((late, late_other, LATE_ROWS), (early, early_other, EARLY_ROWS)):
        rows = own.shape[0] * 2 // count

        def per_block(block, carry, own=own, other=other, rows=rows, first=first):
            distance = jnp.bitwise_xor(block, me)
            at = pl.ds(pl.multiple_of(place_in_half(distance, count) * rows, 8), rows)
            near = jnp.bitwise_and(distance, 1) == 0
            to = pl.ds(pl.multiple_of(first + block * rows, 8), rows)
            grad[to, :] = jnp.where(near, own[at, :], other[at, :])
            return carry

        lax.fori_loop(0, size // rows, per_block, 0)
        first += size


def adamw(param, grad, first, second, scale):
    grad = grad * scale
    first = beta_one * first + (1.0 - beta_one) * grad
    second = beta_two * second + (1.0 - beta_two) * grad * grad
    first_hat = first / (1.0 - beta_one**STEP)
    second_hat = second / (1.0 - beta_two**STEP)
    param = param - learn_rate * (
        first_hat / (jnp.sqrt(second_hat) + adam_eps) + decay_rate * param
    )
    return (param, first, second)


def arr(*shape):
    return jax.ShapeDtypeStruct(shape, F32)


def call(kernel, outs, scratch, *args, name=None, us=1.0, far=(), mib=24):
    vmem = pl.BlockSpec(memory_space=pltpu.VMEM)
    smem = pl.BlockSpec(memory_space=pltpu.SMEM)
    return pl.pallas_call(
        kernel,
        out_shape=list(outs),
        in_specs=[vmem] * len(args) + [pl.BlockSpec(memory_space=pl.ANY)] * len(far),
        out_specs=[smem if o.shape == (1,) else vmem for o in outs],
        scratch_shapes=list(scratch),
        compiler_params=pltpu.CompilerParams(vmem_limit_bytes=mib * 1024 * 1024),
        cost_estimate=pl.CostEstimate(
            flops=int(us * 1.15e9), bytes_accessed=0, transcendentals=0
        ),
        name=name,
    )(*args, *far)


SQUARE = arr(ROWS, WIDE)
SAVE = arr(ROWS, 3 * WIDE)
FORWARD = [
    pltpu.VMEM((2, ROWS, 2 * WIDE), BF16),
    pltpu.VMEM((2, ROWS, 2 * WIDE), BF16),
    pltpu.VMEM((2 * ROWS, 2 * WIDE), BF16),
]
BACKWARD = [
    pltpu.VMEM((2, ROWS, 2 * WIDE), BF16),
    pltpu.VMEM((2, ROWS, 2 * WIDE), BF16),
    pltpu.VMEM((2, ROWS, 2 * WIDE), BF16),
    pltpu.VMEM((2, ROWS, 2 * WIDE), BF16),
    pltpu.VMEM((2 * ROWS, 2 * WIDE), BF16),
    pltpu.VMEM((ROWS, WIDE), F32),
    pltpu.VMEM((2, WIDE, ROWS), F32),
    pltpu.VMEM((ROWS, 2 * ROWS), BF16),
    pltpu.VMEM((ROWS, 2 * ROWS), BF16),
    pltpu.VMEM((2, WIDE, ROWS), BF16),
    pltpu.VMEM((2, WIDE, ROWS), BF16),
    pltpu.VMEM((ROWS, WIDE), F32),
]
PARTS = [arr(ROWS_A, WIDE), arr(ROWS_B, WIDE), arr(ROWS_C, WIDE)]


def passed(parts, steps, sizes):
    slabs, rows = sizes
    moved = []
    for part, (ds, dm) in zip(parts, ((1, 0), (0, 1), (1, 1))):
        pairs = []
        for s in range(slabs):
            for m in range(rows):
                target = ((s + steps * ds) % slabs) * rows + (m + steps * dm) % rows
                pairs.append((s * rows + m, target))
        moved.append(lax.ppermute(part, ("slab", "mp"), pairs))
    return moved


SIDES = [arr(2 * WIN, 8, WIDE)] * 4


def beside(sides, sizes):
    slabs, rows = sizes
    low_d, high_d, low_h, high_h = sides
    up = [(i, i + 1) for i in range(slabs - 1)]
    down = [(i + 1, i) for i in range(slabs - 1)]
    before = lax.ppermute(high_d, "slab", up)
    after = lax.ppermute(low_d, "slab", down)

    def column(own, start):
        ends = [
            x.reshape(2, WIN, 8, WIDE)[:, start : start + 2].reshape(4, 8, WIDE)
            for x in (before, after)
        ]
        return jnp.concatenate([ends[0], own, ends[1]], 0)

    up = [(i, i + 1) for i in range(rows - 1)]
    down = [(i + 1, i) for i in range(rows - 1)]
    left = lax.ppermute(column(high_h, WIN - 2), "mp", up)
    right = lax.ppermute(column(low_h, 0), "mp", down)
    return before, after, left, right


REGION = [pltpu.VMEM((ROWS, WIDE), F32), pltpu.VMEM((8, ROWS), F32)]


def on_device(sizes, feats, labels, valid, params, moment_one, moment_two):
    slabs, rows = sizes
    count = slabs * rows

    def room(spans):
        sizes = [(span_of(groups)[1] + 8) * WIDE for groups in spans]
        return [
            [pltpu.VMEM((size,), F32) for size in sizes],
            pltpu.VMEM((2048, WIDE), F32),
            pltpu.SemaphoreType.DMA((len(spans),)),
        ]

    merge, lay0 = call(
        functools.partial(prep_kernel, FIRST_SPANS),
        [arr(MERGE_ROWS, WIDE), arr(1176, WIDE)],
        room(FIRST_SPANS),
        name="prep_first", us=2.0, far=(params,),
    )
    lay1, lay2 = call(
        functools.partial(prep_kernel, LAYER_SPANS),
        [arr(1168, WIDE)] * 2,
        room(LAYER_SPANS),
        name="prep_layers", us=2.0, far=(params,),
    )
    conv0, conv1, head_w = call(
        prep_conv_kernel,
        [arr(2596, WIDE), arr(2640, WIDE), arr(WIDE, WIDE)],
        room(CONV_SPANS),
        params[NPARAM // WIDE * WIDE :],
        name="prep_conv", us=3.0, far=(params,),
    )

    dense, tok0, save0, lse0, mixed0, mid0, hpre0, tok1, ahead, *parts = call(
        first_kernel,
        [arr(ROWS, MERGE), SQUARE, SAVE, SQUARE, SQUARE, SQUARE, arr(ROWS, HID), SQUARE, SQUARE]
        + PARTS,
        FORWARD,
        feats.reshape(PLANE, WIN, MERGE), merge, lay0,
        name="first", us=9.5,
    )
    parts = passed(parts, -1, sizes)
    window, save1, lse1, mixed1, out1, *parts = call(
        functools.partial(shifted_kernel, sizes),
        [SQUARE, SAVE, SQUARE, SQUARE, SQUARE] + PARTS,
        REGION + FORWARD,
        ahead, *parts, lay1,
        name="shifted", us=7.5,
    )
    parts = passed(parts, 1, sizes)
    mid1, hpre1, tok2, save2, lse2, mixed2, mid2, hpre2, lines, *sides = call(
        second_kernel,
        [SQUARE, arr(ROWS, HID), SQUARE, SAVE, SQUARE, SQUARE, SQUARE, arr(ROWS, HID)]
        + [arr(PLANE, 8, WIDE)] + SIDES,
        [pltpu.VMEM((ROWS, WIDE), F32)] + FORWARD,
        tok1, out1, *parts, lay1, lay2,
        name="second", us=9.5,
    )
    sides = beside(sides, sizes)
    grown, pre, tok3, sums, *tok_sides = call(
        functools.partial(conv_kernel, sizes),
        [arr(11, 12, 8, WIDE), arr(9, 10, 8, WIDE), arr(PLANE, 8, WIDE), arr(8, WIDE)] + SIDES,
        [
            pltpu.VMEM((9, 10, 8, WIDE), F32),
            pltpu.VMEM((880, 2304), BF16),
            pltpu.VMEM((576, 2304), BF16),
            pltpu.VMEM((27 * 256, 256), BF16),
            pltpu.VMEM((PLANE, 8, WIDE), F32),
        ],
        lines, *sides, labels, valid, conv0, conv1,
        name="conv", us=10.5, mib=32,
    )
    tok_sides = beside(tok_sides, sizes)
    sums = exchanged(sums, ("slab", "mp"), count)
    voxels = WIN * slabs * WIN * rows * WIN
    tok3, slope, tail, d_head, d_rows, sums = call(
        functools.partial(head_kernel, voxels),
        [arr(11, 12, 8, WIDE), arr(11, 12, 8, WIDE), arr(8, WIDE), arr(WIDE, WIDE), arr(8, WIDE)]
        + [arr(8, WIDE)],
        [],
        tok3, *tok_sides, sums, conv1, head_w,
        name="head", us=3.5,
    )
    tail = exchanged(tail, "mp", rows)
    tail = tail.reshape(rows, 8, WIDE)
    tail = exchanged((tail[0] + tail[1]) + (tail[2] + tail[3]), "slab", slabs)
    late_rows = block_rows(LATE_ROWS, count) * count
    early_rows = block_rows(EARLY_ROWS, count) * count
    seam_rows = LATE_ROWS - 3 * CUTS[3]
    d_own, keep, send, carry3, seam, tail = call(
        functools.partial(conv_back_kernel, sizes),
        [arr(PLANE, 8, WIDE)] + [arr(early_rows // 2, WIDE)] * 2
        + [arr(24, WIDE), arr(seam_rows, WIDE), arr(8, WIDE)],
        [
            pltpu.VMEM((5236, WIDE), F32),
            pltpu.VMEM((11, 12, 8, WIDE), F32),
            pltpu.VMEM((10, 10, 8, WIDE), F32),
            pltpu.VMEM((880, 2304), BF16),
            pltpu.VMEM((640, 2304), BF16),
            pltpu.VMEM((27 * 256, 256), BF16),
            pltpu.VMEM((seam_rows + early_rows, WIDE), F32),
        ],
        tok3, slope, tail, grown, pre, conv0, conv1, d_rows, d_head,
        name="conv_back", us=21.0, mib=40,
    )
    early = summing(keep, send, count)
    next(early)
    d_mid2, grads2 = call(
        back_mlp_kernel,
        [SQUARE, arr(1168, WIDE)],
        [pltpu.VMEM((ROWS, WIDE), F32)],
        d_own, lay2, mid2, hpre2,
        name="back_mlp", us=3.0,
    )
    step = early.send(d_mid2)
    d_mid, grads1, flat2, carry2, *parts = call(
        back_two_kernel,
        [SQUARE, arr(1168, WIDE), arr(3 * (CUTS[3] - CUTS[2]), WIDE), arr(32, WIDE)] + PARTS,
        [pltpu.VMEM((1184, WIDE), F32)] + BACKWARD,
        d_mid2, grads2, carry3, lay1, lay2, tok2, save2, lse2, mixed2, mid1, hpre1,
        name="back_two", us=9.0,
    )
    parts = passed(parts, -1, sizes)
    step = early.send(d_mid)
    d_window, flat1, carry1, *parts = call(
        functools.partial(back_shifted_kernel, sizes),
        [SQUARE, arr(3 * (CUTS[2] - CUTS[1]), WIDE), arr(16, WIDE)] + PARTS,
        REGION + [pltpu.VMEM((1200, WIDE), F32), pltpu.VMEM((ROWS, WIDE), F32)] + BACKWARD,
        d_mid, *parts, lay1, window, save1, lse1, mixed1, grads1, carry2,
        name="back_shifted", us=10.5, far=(step,),
    )
    step = next(early)
    parts = passed(parts, 1, sizes)
    next(early)
    step = next(early)
    late = call(
        functools.partial(back_first_kernel, sizes),
        [arr(late_rows // 2, WIDE)] * 2,
        [
            pltpu.VMEM((late_rows, WIDE), F32),
            pltpu.VMEM((1572, WIDE), F32),
            pltpu.VMEM((ROWS, WIDE), F32),
        ]
        + BACKWARD,
        d_mid, d_window, *parts, tok1, lay0, lay1, merge, dense, tok0, save0, lse0, mixed0, mid0,
        hpre0, carry1, flat1, flat2, seam,
        name="back_first", us=13.5, far=(step,),
    )
    step = early.send(late[0])
    keep, send = later(list(late), step)
    late_sum = summed_at_once(keep, send, count)
    early = finished(early)
    gradient, loss, valid_count, norm = call(
        functools.partial(gather_kernel, sizes),
        [arr(LATE_ROWS + EARLY_ROWS, WIDE)] + [arr(1)] * 3,
        [],
        *late_sum, *early, tail, sums,
        name="gather", us=2.5,
    )
    gradient = gradient.reshape(-1)[:NPARAM]
    norm = norm.reshape(())
    scale = jnp.minimum(1.0, clip_norm / (norm + 1e-06))
    new_params, new_first, new_second = adamw(params, gradient, moment_one, moment_two, scale)
    return (
        loss.reshape(()), valid_count.reshape(()), norm,
        new_params, new_first, new_second,
    )


def solution(mesh):
    placed = (
        P("slab", "mp", None, None),
        P("slab", "mp", None),
        P("slab", "mp", None),
        P(),
        P(),
        P(),
    )
    sizes = (mesh.shape["slab"], mesh.shape["mp"])
    return jax.shard_map(
        functools.partial(on_device, sizes),
        mesh=mesh,
        in_specs=placed,
        out_specs=(P(), P(), P(), P(), P(), P()),
        check_vma=False,
    )
```

```python
import functools

import jax
import jax.numpy as jnp
from jax import lax
from jax.experimental import pallas as pl
from jax.experimental.pallas import tpu as pltpu
from jax.sharding import PartitionSpec as P

EMB = 96
HEADS = 6
HDIM = 16
HID = 384
MERGE = 384
CLASSES = 14
WIN = 7
SHIFT = 3
LAYERS = 3
STEP = 10

F32 = jnp.float32
BF16 = jnp.bfloat16
eps_norm = 1e-05
beta_one = 0.9
beta_two = 0.999
adam_eps = 1e-08
learn_rate = 0.05
decay_rate = 0.05
clip_norm = 0.01
LOG2E = 1.4426950408889634

VOX = WIN * WIN * WIN
ROWS = 384
BLK = 128
WIDE = 128
PLANE = WIN * WIN
FAR = WIN - SHIFT
ROWS_A = SHIFT * FAR * WIN
ROWS_B = FAR * SHIFT * WIN
ROWS_C = SHIFT * SHIFT * WIN

MERGE_ROWS = 392
LAYER_ROWS = 1165
TAP_ROWS = 27 * EMB
GROUPS = 2280
NPARAM = 872558
HEAD_ROW = 6806
HEAD_ROWS = 11
HEAD_LANE = 32
LATE_ROWS = 3072
EARLY_ROWS = 3840
LAYER_BASE = (98, 389, 680)
CONV_BASE = (971, 1620)
CUTS = (0, 392, 688, 976, 2280)

R_QKV, R_QKVB, R_PROJ, R_PROJB = 4, 292, 295, 391
R_HID, R_HIDB, R_OUT, R_OUTB = 392, 776, 780, 1164


def iota(shape, dim):
    return lax.broadcasted_iota(jnp.int32, shape, dim)


def split(x):
    hi = x.astype(BF16)
    return hi, (x - hi.astype(F32)).astype(BF16)


def pair(x):
    return jnp.concatenate(split(x), 1)


def fold(y):
    half = y.shape[1] // 2
    return y[:, :half] + y[:, half:]


def fold_rows(y):
    half = y.shape[0] // 2
    return y[:half] + y[half:]


def dot(a, b):
    return jnp.dot(a, b, preferred_element_type=F32)


def dot_nt(a, b):
    return lax.dot_general(a, b, (((1,), (1,)), ((), ())), preferred_element_type=F32)


def weight_nn(w):
    top = pair(w)
    return jnp.concatenate([top, top], 0)


def weight_nt(w):
    hi, lo = split(w)
    return jnp.concatenate(
        [jnp.concatenate([hi, hi], 1), jnp.concatenate([lo, lo], 1)], 0
    )


def mm(x, w):
    return fold(dot(pair(x), weight_nn(w)))


def mm_nt(x, w):
    return fold(dot_nt(pair(x), weight_nt(w)))


def rows_t(x):
    return jnp.concatenate(split(x.T), 0)


def mm_tn(xt, y):
    return fold_rows(fold(dot(xt, pair(y))))


def deep(w):
    return jnp.concatenate([w, jnp.zeros((WIDE - EMB, w.shape[1]), F32)], 0)


def roll(x, shift, axis):
    return pltpu.roll(x, shift, axis)


def four_to_three(y):
    lane = iota(y[0].shape, 1)
    a = jnp.where(lane < 96, y[0], roll(y[1], 96, 1))
    b = jnp.where(lane < 64, roll(y[1], 96, 1), roll(y[2], 64, 1))
    c = jnp.where(lane < 32, roll(y[2], 64, 1), roll(y[3], 32, 1))
    return a, b, c


def three_to_four(x):
    lane = iota(x[0].shape, 1)
    live = lane < EMB
    a = x[0]
    b = jnp.where(lane < 32, roll(x[0], 32, 1), roll(x[1], 32, 1))
    c = jnp.where(lane < 64, roll(x[1], 64, 1), roll(x[2], 64, 1))
    d = roll(x[2], 96, 1)
    return tuple(jnp.where(live, v, 0.0) for v in (a, b, c, d))


def hidden_rows(ref, start, count):
    return jnp.concatenate(
        four_to_three([ref[pl.ds(start + c, count, stride=4), :] for c in range(4)]), 1
    )


def put_hidden_rows(ref, start, count, x):
    parts = three_to_four([x[:, i * WIDE : (i + 1) * WIDE] for i in range(3)])
    for c in range(4):
        ref[pl.ds(start + c, count, stride=4), :] = parts[c]


def flatten(ref, start, groups, out):
    parts = four_to_three([ref[pl.ds(start + c, groups, stride=4), :] for c in range(4)])
    for c in range(3):
        out[pl.ds(c, groups, stride=3), :] = parts[c]


def norm_stats(x):
    live = iota(x.shape, 1) < EMB
    mean = jnp.sum(x, 1, keepdims=True) * (1.0 / EMB)
    centred = jnp.where(live, x - mean, 0.0)
    var = jnp.sum(centred * centred, 1, keepdims=True) * (1.0 / EMB)
    inv = lax.rsqrt(var + eps_norm)
    return centred * inv, inv


def norm(x, gain, bias):
    hat, _ = norm_stats(x)
    return hat * gain + bias


def norm_back(hat, inv, gain, grad):
    up = grad * gain
    one = jnp.sum(up, 1, keepdims=True) * (1.0 / EMB)
    two = jnp.sum(up * hat, 1, keepdims=True) * (1.0 / EMB)
    live = iota(hat.shape, 1) < EMB
    return jnp.where(live, inv * (up - one - hat * two), 0.0)


def colsum(x):
    return jnp.sum(x, 0, keepdims=True)


def gelu(x):
    return 0.5 * x * (1.0 + lax.erf(x * (0.5**0.5)))


def gelu_both(x):
    cdf = 0.5 * (1.0 + lax.erf(x * (0.5**0.5)))
    slope = cdf + x * (jnp.exp(x * x * -0.5) * 0.3989422804014327)
    return x * cdf, slope


def head_groups(x):
    lane = iota(x.shape, 1)
    swapped = roll(x, 64, 1)
    return jnp.where(lane < 64, x, swapped), jnp.where(lane < 64, swapped, x)


def as_left(x):
    both = []
    low = iota(x.shape, 1) < 64
    for part in head_groups(x):
        hi = part.astype(BF16).astype(F32)
        one = jnp.where(low, hi, part - hi).astype(BF16)
        both.append(jnp.concatenate([one, one], 1))
    return both


def as_right(x):
    return [pair(part) for part in head_groups(x)]


def head_mask(h, width):
    lane = iota((1, width), 1)
    lane = jnp.bitwise_and(lane, 63)
    low = jnp.bitwise_and(h, 3) * HDIM
    return jnp.where((lane >= low) & (lane < low + HDIM), 1.0, 0.0)


def own_lanes(h):
    lane = iota((1, WIDE), 1)
    return jnp.where((lane >= h * HDIM) & (lane < (h + 1) * HDIM), 1.0, 0.0)


def score_tiles(s, rows, region):
    tiles = [s[rows, i * WIDE : (i + 1) * WIDE] for i in range(3)]
    if region is not None:
        return [t + region[rows, i * WIDE : (i + 1) * WIDE] for i, t in enumerate(tiles)]
    pad = jnp.where(iota((1, WIDE), 1) < VOX - 2 * WIDE, 0.0, -1e30)
    return tiles[:2] + [tiles[2] + pad]


def put_split(ref, rows, i, x):
    hi, lo = split(x)
    ref[rows, i * WIDE : (i + 1) * WIDE] = hi
    ref[rows, ROWS + i * WIDE : ROWS + (i + 1) * WIDE] = lo


def attention(normed, layer, save, lse, mixed, sc, region=None):
    left, right, values, s, weights = sc
    x = pair(normed)
    qkv = []
    for i in range(3):
        w = deep(layer[pl.ds(R_QKV + i, EMB, stride=3), :])
        y = fold(dot(x, weight_nn(w))) + layer[R_QKVB + i : R_QKVB + i + 1, :]
        if i == 0:
            y = y * (HDIM**-0.5 * LOG2E)
        save[:, i * WIDE : (i + 1) * WIDE] = y
        qkv.append(y)
    for g, part in enumerate(as_left(qkv[0])):
        left[g] = part
    for g, part in enumerate(as_right(qkv[1])):
        right[g] = part
    v = pair(jnp.where(iota((ROWS, WIDE), 1) == EMB, 1.0, qkv[2]))
    values[0:ROWS, :] = v
    values[ROWS : 2 * ROWS, :] = v
    mixed[...] = jnp.zeros_like(mixed)
    lse[...] = jnp.zeros_like(lse)

    def per_head(h, carry):
        g = lax.div(h, 4)
        lanes = own_lanes(h)
        at_h = jnp.where(iota((1, WIDE), 1) == h, 1.0, 0.0)
        s[...] = dot_nt(left[g] * head_mask(h, 2 * WIDE).astype(BF16), right[g])
        tops = []
        for b in range(ROWS // BLK):
            rows = slice(b * BLK, (b + 1) * BLK)
            tiles = score_tiles(s, rows, region)
            top = jnp.maximum(jnp.maximum(tiles[0], tiles[1]), tiles[2])
            top = jnp.max(top, 1, keepdims=True)
            tops.append(top)
            for i, t in enumerate(tiles):
                put_split(weights, rows, i, jnp.exp2(t - top))
        o = fold(dot(weights[...], values[...]))
        total = o[:, EMB : EMB + 1]
        mixed[...] += o * (lanes / total)
        lse[...] += (jnp.concatenate(tops, 0) + jnp.log(total) * LOG2E) * at_h
        return carry

    lax.fori_loop(0, HEADS, per_head, 0)
    proj = deep(layer[R_PROJ : R_PROJ + EMB, :])
    return mm(mixed[...], proj) + layer[R_PROJB : R_PROJB + 1, :]


def attention_back(grad, normed, layer, save, lse, mixed, sc, grads, at, region=None):
    left, right, gleft, vright, keys, dq, dkv_t, weights, slopes, q_t, do_t, dmix, s, dp = sc
    proj = deep(layer[R_PROJ : R_PROJ + EMB, :])
    grads[at + R_PROJ : at + R_PROJ + EMB, :] = mm_tn(rows_t(mixed[...]), grad)[:EMB]
    grads[at + R_PROJB : at + R_PROJB + 1, :] = colsum(grad)
    d_mixed = mm_nt(grad, proj)
    dmix[...] = d_mixed * mixed[...]
    q, k, v = (save[:, i * WIDE : (i + 1) * WIDE] for i in range(3))
    for g, part in enumerate(as_left(q)):
        left[g] = part
    for g, part in enumerate(as_right(k)):
        right[g] = part
    for g, part in enumerate(as_left(d_mixed)):
        gleft[g] = part
    for g, part in enumerate(as_right(v)):
        vright[g] = part
    kk = pair(k)
    keys[0:ROWS, :] = kk
    keys[ROWS : 2 * ROWS, :] = kk
    for ref, x in ((q_t, q), (do_t, d_mixed)):
        hi, lo = split(x.T)
        ref[0] = hi
        ref[1] = lo
    dq[...] = jnp.zeros_like(dq)
    dkv_t[...] = jnp.zeros_like(dkv_t)

    def per_head(h, carry):
        g = lax.div(h, 4)
        lanes = own_lanes(h)
        at_h = jnp.where(iota((1, WIDE), 1) == h, 1.0, 0.0)
        mask = head_mask(h, 2 * WIDE).astype(BF16)
        s[...] = dot_nt(left[g] * mask, right[g])
        dp[...] = dot_nt(gleft[g] * mask, vright[g])
        for b in range(ROWS // BLK):
            rows = slice(b * BLK, (b + 1) * BLK)
            level = jnp.sum(lse[rows, :] * at_h, 1, keepdims=True)
            delta = jnp.sum(dmix[rows, :] * lanes, 1, keepdims=True)
            for i, t in enumerate(score_tiles(s, rows, region)):
                p = jnp.exp2(t - level)
                put_split(weights, rows, i, p)
                put_split(slopes, rows, i, p * (dp[rows, i * WIDE : (i + 1) * WIDE] - delta))
        dq[...] += fold(dot(slopes[...], keys[...])) * lanes
        here = pl.multiple_of(h * HDIM, HDIM)
        for i, (t, m) in enumerate(((q_t, slopes), (do_t, weights))):
            lhs = jnp.concatenate([t[0, pl.ds(here, HDIM), :], t[1, pl.ds(here, HDIM), :]], 0)
            out = fold_rows(fold(dot(lhs, m[...])))
            dkv_t[i, pl.ds(here, HDIM), :] = out
        return carry

    lax.fori_loop(0, HEADS, per_head, 0)
    d_q = dq[...] * HDIM**-0.5
    d_k = dkv_t[0].T * (1.0 / LOG2E)
    d_v = dkv_t[1].T
    x_t = rows_t(normed)
    d_normed = None
    for i, d in enumerate((d_q, d_k, d_v)):
        grads[pl.ds(at + R_QKV + i, EMB, stride=3), :] = mm_tn(x_t, d)[:EMB]
        grads[at + R_QKVB + i : at + R_QKVB + i + 1, :] = colsum(d)
        part = mm_nt(d, deep(layer[pl.ds(R_QKV + i, EMB, stride=3), :]))
        d_normed = part if d_normed is None else d_normed + part
    return d_normed


def mlp(middle, layer, hpre):
    normed = norm(middle, layer[2:3, :], layer[3:4, :])
    w = deep(hidden_rows(layer, R_HID, EMB))
    pre = mm(normed, w) + hidden_rows(layer, R_HIDB, 1)
    hpre[...] = pre
    out = mm(gelu(pre), layer[R_OUT : R_OUT + HID, :])
    return middle + out + layer[R_OUTB : R_OUTB + 1, :]


def mlp_back(grad, middle, hpre, layer, grads, at):
    hat, inv = norm_stats(middle)
    normed = hat * layer[2:3, :] + layer[3:4, :]
    act, slope = gelu_both(hpre[...])
    grads[at + R_OUTB : at + R_OUTB + 1, :] = colsum(grad)
    grads[at + R_OUT : at + R_OUT + HID, :] = mm_tn(rows_t(grad), act).T
    d_pre = mm_nt(grad, layer[R_OUT : R_OUT + HID, :]) * slope
    put_hidden_rows(grads, at + R_HIDB, 1, colsum(d_pre))
    put_hidden_rows(grads, at + R_HID, EMB, mm_tn(rows_t(normed), d_pre)[:EMB])
    d_normed = mm_nt(d_pre, deep(hidden_rows(layer, R_HID, EMB)))
    grads[at + 2 : at + 3, :] = colsum(d_normed * hat)
    grads[at + 3 : at + 4, :] = colsum(d_normed)
    return grad + norm_back(hat, inv, layer[2:3, :], d_normed)


def pre_norm_back(grad, tokens, layer, grads, at):
    hat, inv = norm_stats(tokens)
    grads[at : at + 1, :] = colsum(grad * hat)
    grads[at + 1 : at + 2, :] = colsum(grad)
    return norm_back(hat, inv, layer[0:1, :], grad)


def region_of(rows, sizes):
    d = lax.shift_right_logical(rows * 1338, 16)
    line = lax.shift_right_logical(rows * 9363, 16)
    places = (d, line - d * WIN, rows - line * WIN)
    starts = (lax.axis_index("slab") * WIN, lax.axis_index("mp") * WIN, 0)
    total = None
    for place, start, blocks in zip(places, starts, sizes + (1,)):
        turned = jnp.where(place < SHIFT, place + FAR, place - SHIFT) + start
        length = WIN * blocks
        part = jnp.where(turned < length - WIN, 0, jnp.where(turned < length - SHIFT, 1, 2))
        total = part if total is None else total * 3 + part
    return total


def put_region(region, sizes):
    rows = region_of(iota((ROWS, WIDE), 0), sizes)[:, 0:1]
    lanes = region_of(iota((8, ROWS), 1), sizes)[0:1, :]
    apart = jnp.where(rows == lanes, 0.0, -100.0 * LOG2E)
    region[...] = jnp.where(iota((ROWS, ROWS), 1) < VOX, apart, -1e30)


def send_parts(ref, a, b, c):
    far = FAR * WIN
    near = SHIFT * WIN
    for d in range(SHIFT):
        base = d * PLANE
        c[d * near : (d + 1) * near, :] = ref[base : base + near, :]
        a[d * far : (d + 1) * far, :] = ref[base + near : base + PLANE, :]
    for d in range(FAR):
        base = (d + SHIFT) * PLANE
        b[d * near : (d + 1) * near, :] = ref[base : base + near, :]


def take_parts(own, a, b, c, out):
    far = FAR * WIN
    near = SHIFT * WIN
    for d in range(WIN):
        base = d * PLANE
        if d < SHIFT:
            out[base : base + near, :] = c[d * near : (d + 1) * near, :]
            out[base + near : base + PLANE, :] = a[d * far : (d + 1) * far, :]
        else:
            e = d - SHIFT
            out[base : base + near, :] = b[e * near : (e + 1) * near, :]
            out[base + near : base + PLANE, :] = own[base + near : base + PLANE, :]
    out[VOX:, :] = jnp.zeros((ROWS - VOX, WIDE), F32)


def span_of(groups):
    low, high = groups
    first = 3 * low // 8 * 8
    last = -(-3 * high // 8) * 8
    return first, min(last, NPARAM // WIDE // 8 * 8) - first


def copied(params, groups, flat, sem):
    first, rows = span_of(groups)
    size = rows * WIDE
    return pltpu.make_async_copy(
        params.at[pl.ds(first * WIDE, size)], flat.at[pl.ds(0, size)], sem
    )


def relay(groups, flat, out, square, last=None):
    low, high = groups
    first, rows = span_of(groups)
    square[0:rows, :] = flat[0 : rows * WIDE].reshape(rows, WIDE)
    if last is not None:
        square[rows : rows + 24, :] = jnp.zeros((24, WIDE), F32)
        square[rows : rows + 1, 0 : last.shape[0]] = last[...].reshape(1, last.shape[0])
    skip = 3 * low - first
    n = high - low
    parts = three_to_four([square[pl.ds(skip + c, n, stride=3), :] for c in range(3)])
    for c in range(4):
        out[pl.ds(c, n, stride=4), :] = parts[c]


FIRST_SPANS = ((0, 98), (98, 392))
LAYER_SPANS = ((389, 681), (680, 972))
CONV_SPANS = ((971, 1620), (1620, GROUPS))


def prep_kernel(spans, params, *refs, last=None):
    outs, (flats, square, sems) = refs[: len(spans)], refs[-3:]
    for i, groups in enumerate(spans):
        copied(params, groups, flats[i], sems.at[i]).start()
    for i, groups in enumerate(spans):
        copied(params, groups, flats[i], sems.at[i]).wait()
        relay(groups, flats[i], outs[i], square, last if i == len(spans) - 1 else None)


def head_picks():
    width = HEAD_ROWS * WIDE
    place = iota((WIDE, width), 1) - HEAD_LANE
    row = iota((WIDE, width), 0)
    here = (place >= row * CLASSES) & (place < (row + 1) * CLASSES) & (row <= EMB)
    place = iota((width, WIDE), 0) - HEAD_LANE
    col = iota((width, WIDE), 1)
    row = lax.shift_right_logical(place * 4682, 16)
    there = (place - row * CLASSES == col) & (place >= 0)
    return jnp.where(here, 1.0, 0.0), jnp.where(there, 1.0, 0.0).astype(BF16)


def prep_conv_kernel(last, params, conv0, conv1, head, *scratch):
    prep_kernel(CONV_SPANS, params, conv0, conv1, *scratch, last=last)
    square = scratch[1]
    first, _ = span_of(CONV_SPANS[1])
    row = jnp.concatenate(
        [square[HEAD_ROW + i - first : HEAD_ROW + i - first + 1, :] for i in range(HEAD_ROWS)], 1
    )
    here, there = head_picks()
    hi, lo = split(here * row)
    head[...] = dot(hi, there) + dot(lo, there)


def head_rows(d_head, out, at):
    here, there = head_picks()
    hi, lo = split(d_head)
    spread = (dot_nt(hi, there) + dot_nt(lo, there)) * here
    row = colsum(spread)
    for i in range(HEAD_ROWS):
        out[at + i : at + i + 1, :] += row[:, i * WIDE : (i + 1) * WIDE]


class Rows:
    def __init__(self, ref, at):
        self.ref, self.at = ref, at

    def __getitem__(self, key):
        rows, lanes = key
        if isinstance(rows, slice):
            rows = slice(rows.start + self.at, rows.stop + self.at)
        else:
            rows = pl.ds(rows.start + self.at, rows.size, stride=rows.stride)
        return self.ref[rows, lanes]


def merged_norm(x):
    mean = jnp.sum(x, 1, keepdims=True) * (1.0 / MERGE)
    centred = x - mean
    var = jnp.sum(centred * centred, 1, keepdims=True) * (1.0 / MERGE)
    return centred * lax.rsqrt(var + eps_norm)


def first_kernel(
    feats, merge, lay0,
    dense, tok0, save, lse, mixed, middle, hpre, tok1, ahead, pa, pb, pc,
    *sc,
):
    dense[VOX:, :] = jnp.zeros((ROWS - VOX, MERGE), F32)
    for line in range(PLANE):
        dense[line * WIN : (line + 1) * WIN, :] = feats[line]
    hat = merged_norm(dense[...])
    normed = hat * hidden_rows(merge, 0, 1) + hidden_rows(merge, 4, 1)
    tokens = mm(normed, merge[8 : 8 + MERGE, :])
    tok0[...] = tokens
    layer = Rows(lay0, 0)
    normed = norm(tokens, layer[0:1, :], layer[1:2, :])
    attended = attention(normed, layer, save, lse, mixed, sc)
    mid = tokens + attended
    middle[...] = mid
    tokens = mlp(mid, layer, hpre)
    tok1[...] = tokens
    ahead[...] = norm(tokens, layer[1165:1166, :], layer[1166:1167, :])
    send_parts(ahead, pa, pb, pc)


def shifted_kernel(
    sizes,
    own, pa, pb, pc, lay1,
    window, save, lse, mixed, out, qa, qb, qc,
    region, *sc,
):
    put_region(region, sizes)
    take_parts(own, pa, pb, pc, window)
    out[...] = attention(
        window[...], Rows(lay1, 1), save, lse, mixed, sc, region
    )
    send_parts(out, qa, qb, qc)


def to_lines(ref, out):
    for line in range(PLANE):
        out[line, 0:WIN, :] = ref[line * WIN : (line + 1) * WIN, :]
        out[line, WIN:8, :] = jnp.zeros((8 - WIN, WIDE), F32)


def from_lines(ref, out):
    out[VOX:, :] = jnp.zeros((ROWS - VOX, WIDE), F32)
    for line in range(PLANE):
        out[line * WIN : (line + 1) * WIN, :] = ref[line, 0:WIN, :]


def send_sides(lines, low_d, high_d, low_h, high_h):
    low_d[...] = lines[0 : 2 * WIN]
    high_d[...] = lines[(WIN - 2) * WIN :]
    for d in range(WIN):
        low_h[2 * d : 2 * d + 2] = lines[d * WIN : d * WIN + 2]
        high_h[2 * d : 2 * d + 2] = lines[d * WIN + WIN - 2 : (d + 1) * WIN]


def second_kernel(
    tok1, own, qa, qb, qc, lay1, lay2,
    mid1, hpre1, tok2, save, lse, mixed, mid2, hpre2, lines,
    s0, s1, s2, s3,
    attended, *sc,
):
    take_parts(own, qa, qb, qc, attended)
    mid = tok1[...] + attended[...]
    mid1[...] = mid
    tokens = mlp(mid, Rows(lay1, 1), hpre1)
    tok2[...] = tokens
    layer = Rows(lay2, 2)
    normed = norm(tokens, layer[0:1, :], layer[1:2, :])
    mid = tokens + attention(normed, layer, save, lse, mixed, sc)
    mid2[...] = mid
    attended[...] = mlp(mid, layer, hpre2)
    to_lines(attended, lines)
    send_sides(lines, s0, s1, s2, s3)


def grown_lines(own, low_d, high_d, low_h, high_h, out):
    out[...] = jnp.zeros_like(out)
    for d in range(WIN):
        out[d + 2, 2 : 2 + WIN] = own[d * WIN : (d + 1) * WIN]
    for d in range(2):
        out[d, 2 : 2 + WIN] = low_d[d * WIN : (d + 1) * WIN]
        out[d + 9, 2 : 2 + WIN] = high_d[d * WIN : (d + 1) * WIN]
    for d in range(11):
        out[d, 0:2] = low_h[2 * d : 2 * d + 2]
        out[d, 9:11] = high_h[2 * d : 2 * d + 2]


def put_marks(labels, valid, out):
    across = iota((8, WIN), 1) == iota((8, WIN), 0)
    classes = iota((8, WIDE), 1) - EMB
    for d in range(WIN):
        code = jnp.where(valid[d] == 1, labels[d], -1 - EMB - WIDE)
        code = code.astype(F32)
        for h in range(WIN):
            line = jnp.where(across, code[h : h + 1, :], 0.0)
            column = jnp.sum(line, 1, keepdims=True)
            mark = jnp.where(column == classes.astype(F32), 1.0, 0.0)
            out[d * WIN + h] = jnp.where(iota((8, WIDE), 0) < WIN, mark, 0.0)


def taps(source, first_plane, planes, first_line, lines, out):
    def per_plane(d, carry):
        for c in range(3):
            for b in range(3):
                x = source[d + first_plane, first_line + b : first_line + b + lines]
                if c != 1:
                    x = roll(x, 1 if c == 0 else 7, 1)
                x = pair(x.reshape(lines * 8, WIDE))
                at = pl.multiple_of(d * (lines * 8), lines * 8)
                t = b * 3 + c
                out[pl.ds(at, lines * 8), t * 256 : (t + 1) * 256] = x
        return carry

    lax.fori_loop(0, planes, per_plane, 0)


def tap_weights(ref, at, out):
    def per_tap(i, carry):
        w = deep(ref[pl.ds(i * EMB + at, EMB), :])
        out[pl.ds(pl.multiple_of(i * 256, 256), 256), :] = weight_nn(w)
        return carry

    lax.fori_loop(0, 27, per_tap, 0)


def tap_weights_back(ref, at, out):
    for i in range(27):
        w = deep(ref[(26 - i) * EMB + at : (27 - i) * EMB + at, :])
        out[:, i * 256 : (i + 1) * 256] = weight_nt(w)


def conv(side, weights, planes, pitch, back=False):
    rows = planes * pitch
    total = None
    for a in range(3):
        x = side[a * pitch : a * pitch + rows, :]
        if back:
            part = dot_nt(x, weights[:, a * 2304 : (a + 1) * 2304])
        else:
            part = dot(x, weights[a * 2304 : (a + 1) * 2304, :])
        total = part if total is None else total + part
    return fold(total)


def conv_weight_grad(side, grad_rows, pitch, out, at):
    rows = 512
    g = jnp.concatenate([grad_rows, jnp.zeros((rows - grad_rows.shape[0], WIDE), F32)], 0)
    left = rows_t(g)
    for a in range(3):
        for bc in range(9):
            y = dot(left, side[a * pitch : a * pitch + rows, bc * 256 : (bc + 1) * 256])
            y = fold_rows(fold(y)).T
            t = a * 9 + bc
            out[at + t * EMB : at + (t + 1) * EMB, :] = y[:EMB]


def volume_mask(sizes, planes, lines, reach, real_lines):
    slab, row = lax.axis_index("slab"), lax.axis_index("mp")
    ends = (slab == 0, slab == sizes[0] - 1, row == 0, row == sizes[1] - 1)
    shape = (planes, lines, 8, WIDE)
    d, h, w = iota(shape, 0), iota(shape, 1), iota(shape, 2)
    low_d = jnp.where(ends[0], reach, 0)
    high_d = jnp.where(ends[1], planes - reach, planes)
    low_h = jnp.where(ends[2], reach, 0)
    high_h = jnp.where(ends[3], real_lines - reach, real_lines)
    inside = (d >= low_d) & (d < high_d) & (h >= low_h) & (h < high_h) & (w < WIN)
    return jnp.where(inside, 1.0, 0.0)


def conv_kernel(
    sizes,
    own, s0, s1, s2, s3, labels, valid, conv0, conv1,
    grown, pre, tok, stats, t0, t1, t2, t3,
    act, side, side_own, weights, marks,
):
    grown_lines(own, s0, s1, s2, s3, grown)
    put_marks(labels, valid, marks)
    tap_weights(conv0, 3, weights)
    taps(grown, 0, 11, 0, 10, side)
    bias0 = conv0[3 + TAP_ROWS : 4 + TAP_ROWS, :]
    inside = volume_mask(sizes, 9, 10, 1, 9)

    z = (conv(side, weights, 9, 80) + bias0).reshape(9, 10, 8, WIDE)
    pre[...] = z
    act[...] = gelu(z) * inside
    tap_weights(conv1, 0, weights)
    taps(act, 0, 9, 0, 8, side_own)
    bias1 = conv1[TAP_ROWS : TAP_ROWS + 1, :]
    y = (conv(side_own, weights, WIN, 64) + bias1).reshape(WIN, 8, 8, WIDE)[:, 0:WIN]
    y = y + own[...].reshape(WIN, WIN, 8, WIDE)
    y = jnp.where(iota(y.shape, 2) < WIN, y, 0.0).reshape(PLANE, 8, WIDE)
    tok[...] = y + marks[...]
    send_sides(tok, t0, t1, t2, t3)
    flat = y.reshape(PLANE * 8, WIDE)
    count = jnp.sum(marks[...].reshape(PLANE * 8, WIDE))
    row = iota((8, WIDE), 0)
    stats[...] = (
        jnp.where(row == 0, colsum(flat), 0.0)
        + jnp.where(row == 1, colsum(flat * flat), 0.0)
        + jnp.where(row == 2, count, 0.0)
    )


def head_kernel(
    voxels,
    own, s0, s1, s2, s3, sums, conv1, head_w,
    grown, slope_out, stats, d_head, d_rows,
):
    grown_lines(own, s0, s1, s2, s3, grown)
    rows = 11 * 12 * 8
    both = grown[...].reshape(rows, WIDE)
    lane = iota((rows, WIDE), 1)
    tokens = jnp.where(lane < EMB, both, 0.0)
    target = jnp.where(lane < CLASSES, roll(both, WIDE - EMB, 1), 0.0)
    live = jnp.sum(target, 1, keepdims=True)
    count = F32(voxels)
    average = sums[0:1, :] / count
    spread = sums[1:2, :] / count - average * average
    inv = lax.rsqrt(spread + eps_norm)
    gain = conv1[TAP_ROWS + 1 : TAP_ROWS + 2, :]
    bias = conv1[TAP_ROWS + 2 : TAP_ROWS + 3, :]
    hat = (tokens - average) * inv
    act, slope = gelu_both(hat * gain + bias)
    act = jnp.where(lane == EMB, 1.0, act)
    w = head_w[...]
    logits = mm(act, w)
    logits = jnp.where(lane < CLASSES, logits, -1e30)
    top = jnp.max(logits, 1, keepdims=True)
    e = jnp.exp(logits - top)
    total = jnp.sum(e, 1, keepdims=True)
    logp = logits - top - jnp.log(total)
    scale = 1.0 / sums[2:3, 0:1]
    d_logits = (e / total * live - target) * scale
    d_normed = jnp.where(lane < EMB, mm_nt(d_logits, w) * slope, 0.0)
    d_tokens = d_normed * gain * inv
    slope_out[...] = d_tokens.reshape(11, 12, 8, WIDE)

    def own_rows(x):
        x = x.reshape(11, 12, 8, WIDE)[2:9, 2:9]
        x = jnp.where(iota(x.shape, 2) < WIN, x, 0.0)
        return x.reshape(PLANE * 8, WIDE)

    loss = -jnp.sum(own_rows(target * jnp.where(lane < CLASSES, logp, 0.0)))
    own_d = own_rows(d_logits)
    own_n = own_rows(d_normed)
    own_hat = own_rows(hat)
    zeros = jnp.zeros((512 - PLANE * 8, WIDE), F32)
    left = rows_t(jnp.concatenate([own_d, zeros], 0))
    d_head[...] = mm_tn(left, jnp.concatenate([own_rows(act), zeros], 0)).T
    d_gain = colsum(own_n * own_hat)
    d_bias = colsum(own_n)
    d_average = -d_bias * gain * inv
    d_spread = d_gain * gain * inv * inv * -0.5
    d_two = d_spread / count
    d_one = (d_average - 2.0 * average * d_spread) / count
    row = iota((8, WIDE), 0)
    live_lane = iota((8, WIDE), 1) < EMB
    stats[...] = (
        jnp.where((row == 0) & live_lane, d_one, 0.0)
        + jnp.where((row == 1) & live_lane, d_two, 0.0)
        + jnp.where(row == 2, loss, 0.0)
    )
    d_rows[...] = (
        jnp.where(row == 0, d_gain, 0.0)
        + jnp.where(row == 1, d_bias, 0.0)
    )


def conv_back_kernel(
    sizes,
    tok, slope, sums, grown, pre, conv0, conv1, d_rows, d_head,
    d_own, keep, send, carry, seam,
    grads, dgrown, act, side, side_own, weights, flat,
):
    lane = iota((11, 12, 8, WIDE), 3)
    inside = volume_mask(sizes, 11, 12, 2, 11)
    steady = sums[0:1, :].reshape(1, 1, 1, WIDE)
    rising = 2.0 * sums[1:2, :].reshape(1, 1, 1, WIDE)
    d_tok = slope[...] + jnp.where(lane < EMB, (steady + tok[...] * rising) * inside, 0.0)
    dgrown[...] = d_tok
    grads[5191:, :] = jnp.zeros((45, WIDE), F32)
    grads[0:8, :] = jnp.zeros((8, WIDE), F32)
    grads[5189:5191, :] = d_rows[0:2, :]
    own = dgrown[2:9, 2:10]
    line = iota(own.shape, 1)
    own = jnp.where(line < WIN, own, 0.0).reshape(WIN * 64, WIDE)
    grads[5188:5189, :] = colsum(own)

    near = volume_mask(sizes, 9, 10, 1, 9)
    act[0:9] = gelu(pre[...]) * near
    act[9:10] = jnp.zeros((1, 10, 8, WIDE), F32)
    taps(act, 0, 10, 0, 8, side_own)
    conv_weight_grad(side_own, own, 64, grads, 2596)
    tap_weights_back(conv1, 0, weights)
    taps(dgrown, 0, 11, 0, 10, side)

    y = conv(side, weights, 9, 80, back=True).reshape(9, 10, 8, WIDE)
    act[0:9] = y * gelu_both(pre[...])[1] * near

    own = act[1:8, 1:9]
    line = iota(own.shape, 1)
    own = jnp.where(line < WIN, own, 0.0).reshape(WIN * 64, WIDE)
    grads[2595:2596, :] = colsum(own)
    taps(grown, 1, 10, 1, 8, side_own)
    conv_weight_grad(side_own, own, 64, grads, 3)
    carry[...] = grads[0:24, :]
    flat[3 * (GROUPS - CUTS[3]) :, :] = jnp.zeros((flat.shape[0] - 3912, WIDE), F32)
    flatten(grads, 20, GROUPS - CUTS[3], flat)
    start = 3 * CUTS[3]
    head_rows(d_head[...], flat, HEAD_ROW - start)
    seam[...] = flat[0 : LATE_ROWS - start, :]
    scatter(sizes, flat, LATE_ROWS - start, keep, send)
    tap_weights_back(conv0, 3, weights)
    taps(act, 0, 9, 0, 8, side_own)

    y = conv(side_own, weights, WIN, 64, back=True).reshape(WIN, 8, 8, WIDE)[:, 0:WIN]
    y = y + dgrown[2:9, 2:9]
    y = jnp.where(iota(y.shape, 2) < WIN, y, 0.0)
    d_own[...] = y.reshape(PLANE, 8, WIDE)


def back_mlp_kernel(d_own, lay2, mid2, hpre2, d_mid, grads, dense):
    from_lines(d_own, dense)
    grads[...] = jnp.zeros_like(grads)
    d_mid[...] = mlp_back(dense[...], mid2[...], hpre2, Rows(lay2, 2), grads, 2)


def back_two_kernel(
    d_mid2, grads2, carry, lay1, lay2, tok2, save, lse, mixed, mid1, hpre1,
    d_mid, grads1, flat, carry2, pa, pb, pc,
    grads, *sc,
):
    layer = Rows(lay2, 2)
    grads[0:1168, :] = grads2[...]
    d = d_mid2[...]
    tokens = tok2[...]
    normed = norm(tokens, layer[0:1, :], layer[1:2, :])
    d_normed = attention_back(d, normed, layer, save, lse, mixed, sc, grads, 2)
    d = d + pre_norm_back(d_normed, tokens, layer, grads, 2)
    grads[1167:1184, :] = carry[3:20, :]
    flatten(grads, 32, CUTS[3] - CUTS[2], flat)
    carry2[...] = grads[0:32, :]
    layer = Rows(lay1, 1)
    d = mlp_back(d, mid1[...], hpre1, layer, grads1, 1)
    d_mid[...] = d
    send_parts(d_mid, pa, pb, pc)


def back_shifted_kernel(
    sizes,
    own, pa, pb, pc, lay1, window, save, lse, mixed, grads1, carry2, _,
    d_window, flat, carry1, qa, qb, qc,
    region, grads, grad, *sc,
):
    put_region(region, sizes)
    take_parts(own, pa, pb, pc, grad)
    grads[0:1168, :] = grads1[...]
    grads[0:3, :] = jnp.zeros((3, WIDE), F32)
    d_window[...] = attention_back(
        grad[...], window[...], Rows(lay1, 1), save, lse, mixed, sc, grads, 1,
        region,
    )
    send_parts(d_window, qa, qb, qc)
    grads[1166:1196, :] = carry2[2:32, :]
    flatten(grads, 12, CUTS[2] - CUTS[1], flat)
    carry1[...] = grads[0:16, :]


def back_first_kernel(
    sizes,
    d_mid, own, qa, qb, qc, tok1, lay0, lay1, merge, dense, tok0, save, lse, mixed, middle, hpre,
    carry1, flat1, flat2, seam, _,
    keep, send,
    flat, grads, grad, *sc,
):
    take_parts(own, qa, qb, qc, grad)
    grads[1556:1572, :] = carry1[...]
    d = d_mid[...] + pre_norm_back(grad[...], tok1[...], Rows(lay1, 1), grads, 1557)
    layer = Rows(lay0, 0)
    at = MERGE_ROWS
    d = mlp_back(d, middle[...], hpre, layer, grads, at)
    tokens = tok0[...]
    normed = norm(tokens, layer[0:1, :], layer[1:2, :])
    d_normed = attention_back(d, normed, layer, save, lse, mixed, sc, grads, at)
    d = d + pre_norm_back(d_normed, tokens, layer, grads, at)
    live = iota((ROWS, WIDE), 0) < VOX
    d = jnp.where(live, d, 0.0)
    hat = merged_norm(dense[...])
    gain = hidden_rows(merge, 0, 1)
    bias = hidden_rows(merge, 4, 1)
    w = merge[8 : 8 + MERGE, :]
    put_hidden_rows(grads, 8 - 8, 1, jnp.zeros((1, MERGE), F32))
    grads[8 : 8 + MERGE, :] = mm_tn(rows_t(d), hat * gain + bias).T
    d_hat = mm_nt(d, w)
    put_hidden_rows(grads, 0, 1, colsum(d_hat * hat))
    put_hidden_rows(grads, 4, 1, colsum(d_hat))
    flatten(grads, 0, CUTS[1], flat)
    at = 0
    for cut, part in ((CUTS[1], flat1), (CUTS[2], flat2), (CUTS[3], seam)):
        at = 3 * cut
        flat[at : at + part.shape[0], :] = part[...]
    at += seam.shape[0]
    if flat.shape[0] > at:
        flat[at:, :] = jnp.zeros((flat.shape[0] - at, WIDE), F32)
    scatter(sizes, flat, 0, keep, send)


def radices(count):
    steps = [2]
    left = count // 2
    while left > 1:
        steps.append(4 if left >= 4 else 2)
        left //= steps[-1]
    return steps


def block_rows(rows, count):
    return -(-rows // (8 * count)) * 8


def own_number(sizes):
    return lax.axis_index("slab") * sizes[1] + lax.axis_index("mp")


def place_in_half(distance, count):
    place = 0
    shift = 1
    for radix in radices(count)[1:]:
        digit = jnp.bitwise_and(lax.shift_right_logical(distance, shift), radix - 1)
        place = place * radix + digit
        shift += radix.bit_length() - 1
    return place


def scatter(sizes, source, first, keep, send):
    count = sizes[0] * sizes[1]
    rows = keep.shape[0] * 2 // count
    me = own_number(sizes)
    odd = jnp.bitwise_and(me, 1)

    def per_pair(t, carry):
        for block, out in ((2 * t + odd, keep), (2 * t + 1 - odd, send)):
            place = place_in_half(jnp.bitwise_xor(block, me), count)
            at = pl.multiple_of(first + block * rows, 8)
            to = pl.multiple_of(place * rows, 8)
            out[pl.ds(to, rows), :] = source[pl.ds(at, rows), :]
        return carry

    lax.fori_loop(0, count // 2, per_pair, 0)


def traded(value, distance, count):
    pairs = [(i, i ^ distance) for i in range(count)]
    return lax.ppermute(value, ("slab", "mp"), pairs)


def later(got, after):
    return got if after is None else list(lax.optimization_barrier((*got, after)))[:-1]


def summing(keep, send, count):
    steps = radices(count)
    got = [keep, traded(send, 1, count)]
    shift = 1
    after = yield None
    for radix in steps[1:]:
        got = later(got, after)
        total = sum(got[1:], got[0])
        rows = total.shape[0] // radix
        parts = [total[k * rows : (k + 1) * rows] for k in range(radix)]
        got = parts[:1] + [traded(parts[k], k << shift, count) for k in range(1, radix)]
        shift += radix.bit_length() - 1
        after = yield parts[0]
    got = later(got, after)
    own = sum(got[1:], got[0])
    for radix in reversed(steps[1:]):
        shift -= radix.bit_length() - 1
        got = [own] + [traded(own, k << shift, count) for k in range(1, radix)]
        after = yield own
        own = jnp.concatenate(later(got, after), 0)
        yield own
    yield own, traded(own, 1, count)


def finished(chain, after=None):
    last = next(chain) if after is None else chain.send(after)
    while not isinstance(last, tuple):
        last = next(chain)
    return last


def exchanged_sum(value, count):
    shift = 0
    for radix in radices(count):
        got = [value] + [traded(value, k << shift, count) for k in range(1, radix)]
        while len(got) > 1:
            got = [got[i] + got[i + 1] for i in range(0, len(got), 2)]
        value = got[0]
        shift += radix.bit_length() - 1
    return value


PIECE = 131072


def adamw_kernel(
    sizes,
    late, late_other, early, early_other, tail, sums, params, first, second,
    new_params, new_first, new_second, loss, valid, norm_out,
    grad, scale_ref,
):
    count = sizes[0] * sizes[1]
    step = pl.program_id(0)

    @pl.when(step == 0)
    def gather():
        me = own_number(sizes)
        total = jnp.zeros((8, WIDE), F32)
        for ref in (late, late_other, early, early_other):
            x = ref[...]
            total = total + jnp.sum((x * x).reshape(-1, 8, WIDE), 0)
        norm = jnp.sqrt(jnp.sum(total))
        loss[0] = jnp.sum(tail[2:3, 0:1])
        valid[0] = jnp.sum(sums[2:3, 0:1])
        norm_out[0] = norm
        scale_ref[0] = jnp.minimum(1.0, clip_norm / (norm + 1e-06))
        start = 0
        for own, other, size in ((late, late_other, LATE_ROWS), (early, early_other, EARLY_ROWS)):
            rows = own.shape[0] * 2 // count

            def per_block(block, carry, own=own, other=other, rows=rows, start=start):
                distance = jnp.bitwise_xor(block, me)
                at = pl.ds(pl.multiple_of(place_in_half(distance, count) * rows, 8), rows)
                near = jnp.bitwise_and(distance, 1) == 0
                to = pl.ds(pl.multiple_of(start + block * rows, 8), rows)
                grad[to, :] = jnp.where(near, own[at, :], other[at, :])
                return carry

            lax.fori_loop(0, size // rows, per_block, 0)
            start += size

    def update(base, low, size):
        rows = -(-size // 1024) * 8
        at = pl.ds(pl.multiple_of(base // WIDE + low // WIDE, 8), rows)
        g = grad[at, :].reshape(rows * WIDE)[:size] * scale_ref[0]
        here = pl.ds(pl.multiple_of(base + low, 1024), size)
        one = beta_one * first[here] + (1.0 - beta_one) * g
        two = beta_two * second[here] + (1.0 - beta_two) * g * g
        there = pl.ds(low, size)
        new_first[there] = one
        new_second[there] = two
        one = one * (1.0 / (1.0 - beta_one**STEP))
        two = two * (1.0 / (1.0 - beta_two**STEP))
        old = params[here]
        new_params[there] = old - learn_rate * (
            one / (jnp.sqrt(two) + adam_eps) + decay_rate * old
        )

    whole = NPARAM // PIECE

    @pl.when(step < whole)
    def full():
        def part(i, carry):
            low = pl.multiple_of(i * 16384, 16384)
            update(step * PIECE, low, 16384)
            return carry

        lax.fori_loop(0, PIECE // 16384, part, 0)

    @pl.when(step == whole)
    def last():
        rest = NPARAM - whole * PIECE
        main = rest // 1024 * 1024
        for low in range(0, main, 16384):
            update(whole * PIECE, low, min(16384, main - low))
        update(whole * PIECE, main, rest - main)


def adamw(sizes, parts, arrays):
    pieces = -(-NPARAM // PIECE)
    piece = pl.BlockSpec((PIECE,), lambda i: (i,))
    vmem = pl.BlockSpec(memory_space=pltpu.VMEM)
    smem = pl.BlockSpec(memory_space=pltpu.SMEM)
    return pl.pallas_call(
        functools.partial(adamw_kernel, sizes),
        grid=(pieces,),
        out_shape=[arr(NPARAM)] * 3 + [arr(1)] * 3,
        in_specs=[vmem] * (len(parts) + len(arrays)),
        out_specs=[piece] * 3 + [smem] * 3,
        scratch_shapes=[pltpu.VMEM((LATE_ROWS + EARLY_ROWS, WIDE), F32), pltpu.SMEM((1,), F32)],
        compiler_params=pltpu.CompilerParams(vmem_limit_bytes=24 * 1024 * 1024),
        cost_estimate=pl.CostEstimate(flops=6 * 10**9, bytes_accessed=0, transcendentals=0),
        name="adamw",
    )(*parts, *arrays)


def arr(*shape):
    return jax.ShapeDtypeStruct(shape, F32)


def call(kernel, outs, scratch, *args, name=None, us=1.0, far=(), mib=24):
    vmem = pl.BlockSpec(memory_space=pltpu.VMEM)
    smem = pl.BlockSpec(memory_space=pltpu.SMEM)
    return pl.pallas_call(
        kernel,
        out_shape=list(outs),
        in_specs=[vmem] * len(args) + [pl.BlockSpec(memory_space=pl.ANY)] * len(far),
        out_specs=[smem if o.shape == (1,) else vmem for o in outs],
        scratch_shapes=list(scratch),
        compiler_params=pltpu.CompilerParams(vmem_limit_bytes=mib * 1024 * 1024),
        cost_estimate=pl.CostEstimate(
            flops=int(us * 1.15e9), bytes_accessed=0, transcendentals=0
        ),
        name=name,
    )(*args, *far)


SQUARE = arr(ROWS, WIDE)
SAVE = arr(ROWS, 3 * WIDE)
FORWARD = [
    pltpu.VMEM((2, ROWS, 2 * WIDE), BF16),
    pltpu.VMEM((2, ROWS, 2 * WIDE), BF16),
    pltpu.VMEM((2 * ROWS, 2 * WIDE), BF16),
    pltpu.VMEM((ROWS, ROWS), F32),
    pltpu.VMEM((ROWS, 2 * ROWS), BF16),
]
BACKWARD = [
    pltpu.VMEM((2, ROWS, 2 * WIDE), BF16),
    pltpu.VMEM((2, ROWS, 2 * WIDE), BF16),
    pltpu.VMEM((2, ROWS, 2 * WIDE), BF16),
    pltpu.VMEM((2, ROWS, 2 * WIDE), BF16),
    pltpu.VMEM((2 * ROWS, 2 * WIDE), BF16),
    pltpu.VMEM((ROWS, WIDE), F32),
    pltpu.VMEM((2, WIDE, ROWS), F32),
    pltpu.VMEM((ROWS, 2 * ROWS), BF16),
    pltpu.VMEM((ROWS, 2 * ROWS), BF16),
    pltpu.VMEM((2, WIDE, ROWS), BF16),
    pltpu.VMEM((2, WIDE, ROWS), BF16),
    pltpu.VMEM((ROWS, WIDE), F32),
    pltpu.VMEM((ROWS, ROWS), F32),
    pltpu.VMEM((ROWS, ROWS), F32),
]
PARTS = [arr(ROWS_A, WIDE), arr(ROWS_B, WIDE), arr(ROWS_C, WIDE)]


def passed(parts, steps, sizes):
    slabs, rows = sizes
    moved = []
    for part, (ds, dm) in zip(parts, ((1, 0), (0, 1), (1, 1))):
        pairs = []
        for s in range(slabs):
            for m in range(rows):
                target = ((s + steps * ds) % slabs) * rows + (m + steps * dm) % rows
                pairs.append((s * rows + m, target))
        moved.append(lax.ppermute(part, ("slab", "mp"), pairs))
    return moved


SIDES = [arr(2 * WIN, 8, WIDE)] * 4


def beside(sides, sizes):
    slabs, rows = sizes
    low_d, high_d, low_h, high_h = sides
    up = [(i, i + 1) for i in range(slabs - 1)]
    down = [(i + 1, i) for i in range(slabs - 1)]
    before = lax.ppermute(high_d, "slab", up)
    after = lax.ppermute(low_d, "slab", down)

    def column(own, start):
        ends = [
            x.reshape(2, WIN, 8, WIDE)[:, start : start + 2].reshape(4, 8, WIDE)
            for x in (before, after)
        ]
        return jnp.concatenate([ends[0], own, ends[1]], 0)

    up = [(i, i + 1) for i in range(rows - 1)]
    down = [(i + 1, i) for i in range(rows - 1)]
    left = lax.ppermute(column(high_h, WIN - 2), "mp", up)
    right = lax.ppermute(column(low_h, 0), "mp", down)
    return before, after, left, right


REGION = [pltpu.VMEM((ROWS, ROWS), F32)]


def on_device(sizes, feats, labels, valid, params, moment_one, moment_two):
    slabs, rows = sizes
    count = slabs * rows

    def room(spans):
        sizes = [(span_of(groups)[1] + 8) * WIDE for groups in spans]
        return [
            [pltpu.VMEM((size,), F32) for size in sizes],
            pltpu.VMEM((2048, WIDE), F32),
            pltpu.SemaphoreType.DMA((len(spans),)),
        ]

    merge, lay0 = call(
        functools.partial(prep_kernel, FIRST_SPANS),
        [arr(MERGE_ROWS, WIDE), arr(1176, WIDE)],
        room(FIRST_SPANS),
        name="prep_first", us=2.0, far=(params,), mib=60,
    )
    lay1, lay2 = call(
        functools.partial(prep_kernel, LAYER_SPANS),
        [arr(1168, WIDE)] * 2,
        room(LAYER_SPANS),
        name="prep_layers", us=2.0, far=(params,),
    )
    conv0, conv1, head_w = call(
        prep_conv_kernel,
        [arr(2596, WIDE), arr(2640, WIDE), arr(WIDE, WIDE)],
        room(CONV_SPANS),
        params[NPARAM // WIDE * WIDE :],
        name="prep_conv", us=3.0, far=(params,),
    )

    dense, tok0, save0, lse0, mixed0, mid0, hpre0, tok1, ahead, *parts = call(
        first_kernel,
        [arr(ROWS, MERGE), SQUARE, SAVE, SQUARE, SQUARE, SQUARE, arr(ROWS, HID), SQUARE, SQUARE]
        + PARTS,
        FORWARD,
        feats.reshape(PLANE, WIN, MERGE), merge, lay0,
        name="first", us=9.5,
    )
    parts = passed(parts, -1, sizes)
    window, save1, lse1, mixed1, out1, *parts = call(
        functools.partial(shifted_kernel, sizes),
        [SQUARE, SAVE, SQUARE, SQUARE, SQUARE] + PARTS,
        REGION + FORWARD,
        ahead, *parts, lay1,
        name="shifted", us=7.5,
    )
    parts = passed(parts, 1, sizes)
    mid1, hpre1, tok2, save2, lse2, mixed2, mid2, hpre2, lines, *sides = call(
        second_kernel,
        [SQUARE, arr(ROWS, HID), SQUARE, SAVE, SQUARE, SQUARE, SQUARE, arr(ROWS, HID)]
        + [arr(PLANE, 8, WIDE)] + SIDES,
        [pltpu.VMEM((ROWS, WIDE), F32)] + FORWARD,
        tok1, out1, *parts, lay1, lay2,
        name="second", us=9.5,
    )
    sides = beside(sides, sizes)
    grown, pre, tok3, sums, *tok_sides = call(
        functools.partial(conv_kernel, sizes),
        [arr(11, 12, 8, WIDE), arr(9, 10, 8, WIDE), arr(PLANE, 8, WIDE), arr(8, WIDE)] + SIDES,
        [
            pltpu.VMEM((9, 10, 8, WIDE), F32),
            pltpu.VMEM((880, 2304), BF16),
            pltpu.VMEM((576, 2304), BF16),
            pltpu.VMEM((27 * 256, 256), BF16),
            pltpu.VMEM((PLANE, 8, WIDE), F32),
        ],
        lines, *sides, labels, valid, conv0, conv1,
        name="conv", us=10.5, mib=32,
    )
    tok_sides = beside(tok_sides, sizes)
    sums = exchanged_sum(sums, count)
    voxels = WIN * slabs * WIN * rows * WIN
    tok3, slope, tail, d_head, d_rows = call(
        functools.partial(head_kernel, voxels),
        [arr(11, 12, 8, WIDE), arr(11, 12, 8, WIDE), arr(8, WIDE), arr(WIDE, WIDE), arr(8, WIDE)],
        [],
        tok3, *tok_sides, sums, conv1, head_w,
        name="head", us=3.5,
    )
    tail = exchanged_sum(tail, count)
    late_rows = block_rows(LATE_ROWS, count) * count
    early_rows = block_rows(EARLY_ROWS, count) * count
    seam_rows = LATE_ROWS - 3 * CUTS[3]
    d_own, keep, send, carry3, seam = call(
        functools.partial(conv_back_kernel, sizes),
        [arr(PLANE, 8, WIDE)] + [arr(early_rows // 2, WIDE)] * 2
        + [arr(24, WIDE), arr(seam_rows, WIDE)],
        [
            pltpu.VMEM((5236, WIDE), F32),
            pltpu.VMEM((11, 12, 8, WIDE), F32),
            pltpu.VMEM((10, 10, 8, WIDE), F32),
            pltpu.VMEM((880, 2304), BF16),
            pltpu.VMEM((640, 2304), BF16),
            pltpu.VMEM((256, 27 * 256), BF16),
            pltpu.VMEM((seam_rows + early_rows, WIDE), F32),
        ],
        tok3, slope, tail, grown, pre, conv0, conv1, d_rows, d_head,
        name="conv_back", us=21.0, mib=40,
    )
    early = summing(keep, send, count)
    next(early)
    d_mid2, grads2 = call(
        back_mlp_kernel,
        [SQUARE, arr(1168, WIDE)],
        [pltpu.VMEM((ROWS, WIDE), F32)],
        d_own, lay2, mid2, hpre2,
        name="back_mlp", us=3.0,
    )
    step = early.send(d_mid2)
    d_mid, grads1, flat2, carry2, *parts = call(
        back_two_kernel,
        [SQUARE, arr(1168, WIDE), arr(3 * (CUTS[3] - CUTS[2]), WIDE), arr(32, WIDE)] + PARTS,
        [pltpu.VMEM((1184, WIDE), F32)] + BACKWARD,
        d_mid2, grads2, carry3, lay1, lay2, tok2, save2, lse2, mixed2, mid1, hpre1,
        name="back_two", us=9.0,
    )
    parts = passed(parts, -1, sizes)
    step = early.send(d_mid)
    d_window, flat1, carry1, *parts = call(
        functools.partial(back_shifted_kernel, sizes),
        [SQUARE, arr(3 * (CUTS[2] - CUTS[1]), WIDE), arr(16, WIDE)] + PARTS,
        REGION + [pltpu.VMEM((1200, WIDE), F32), pltpu.VMEM((ROWS, WIDE), F32)] + BACKWARD,
        d_mid, *parts, lay1, window, save1, lse1, mixed1, grads1, carry2,
        name="back_shifted", us=10.5, far=(step,),
    )
    step = next(early)
    parts = passed(parts, 1, sizes)
    next(early)
    step = next(early)
    late = call(
        functools.partial(back_first_kernel, sizes),
        [arr(late_rows // 2, WIDE)] * 2,
        [
            pltpu.VMEM((late_rows, WIDE), F32),
            pltpu.VMEM((1572, WIDE), F32),
            pltpu.VMEM((ROWS, WIDE), F32),
        ]
        + BACKWARD,
        d_mid, d_window, *parts, tok1, lay0, lay1, merge, dense, tok0, save0, lse0, mixed0, mid0,
        hpre0, carry1, flat1, flat2, seam,
        name="back_first", us=13.5, far=(step,),
    )
    step = early.send(late[0])
    keep, send = later(list(late), step)
    late_sum = finished(summing(keep, send, count))
    early = finished(early)
    new_params, new_first, new_second, loss, valid_count, norm = adamw(
        sizes, (*late_sum, *early, tail, sums), (params, moment_one, moment_two)
    )
    return (
        loss.reshape(()), valid_count.reshape(()), norm.reshape(()),
        new_params, new_first, new_second,
    )


def solution(mesh):
    placed = (
        P("slab", "mp", None, None),
        P("slab", "mp", None),
        P("slab", "mp", None),
        P(),
        P(),
        P(),
    )
    sizes = (mesh.shape["slab"], mesh.shape["mp"])
    return jax.shard_map(
        functools.partial(on_device, sizes),
        mesh=mesh,
        in_specs=placed,
        out_specs=(P(), P(), P(), P(), P(), P()),
        check_vma=False,
    )
```

```python
import functools

import jax
import jax.numpy as jnp
from jax import lax
from jax.experimental import pallas as pl
from jax.experimental.pallas import tpu as pltpu
from jax.sharding import PartitionSpec as P

EMB = 96
HEADS = 6
HDIM = 16
HID = 384
MERGE = 384
CLASSES = 14
WIN = 7
SHIFT = 3
LAYERS = 3
STEP = 10

F32 = jnp.float32
BF16 = jnp.bfloat16
eps_norm = 1e-05
beta_one = 0.9
beta_two = 0.999
adam_eps = 1e-08
learn_rate = 0.05
decay_rate = 0.05
clip_norm = 0.01
LOG2E = 1.4426950408889634

VOX = WIN * WIN * WIN
ROWS = 384
BLK = 128
WIDE = 128
PLANE = WIN * WIN
FAR = WIN - SHIFT
ROWS_A = SHIFT * FAR * WIN
ROWS_B = FAR * SHIFT * WIN
ROWS_C = SHIFT * SHIFT * WIN

MERGE_ROWS = 392
LAYER_ROWS = 1165
TAP_ROWS = 27 * EMB
GROUPS = 2280
NPARAM = 872558
HEAD_ROW = 6806
HEAD_ROWS = 11
HEAD_LANE = 32
LATE_ROWS = 3072
EARLY_ROWS = 3840
LAYER_BASE = (98, 389, 680)
CONV_BASE = (971, 1620)
CUTS = (0, 392, 688, 976, 2280)

R_QKV, R_QKVB, R_PROJ, R_PROJB = 4, 292, 295, 391
R_HID, R_HIDB, R_OUT, R_OUTB = 392, 776, 780, 1164


def iota(shape, dim):
    return lax.broadcasted_iota(jnp.int32, shape, dim)


def split(x):
    hi = x.astype(BF16)
    return hi, (x - hi.astype(F32)).astype(BF16)


def pair(x):
    return jnp.concatenate(split(x), 1)


def fold(y):
    half = y.shape[1] // 2
    return y[:, :half] + y[:, half:]


def fold_rows(y):
    half = y.shape[0] // 2
    return y[:half] + y[half:]


def dot(a, b):
    return jnp.dot(a, b, preferred_element_type=F32)


def dot_nt(a, b):
    return lax.dot_general(a, b, (((1,), (1,)), ((), ())), preferred_element_type=F32)


def weight_nn(w):
    top = pair(w)
    return jnp.concatenate([top, top], 0)


def weight_nt(w):
    hi, lo = split(w)
    return jnp.concatenate(
        [jnp.concatenate([hi, hi], 1), jnp.concatenate([lo, lo], 1)], 0
    )


def mm(x, w):
    return fold(dot(pair(x), weight_nn(w)))


def mm_nt(x, w):
    return fold(dot_nt(pair(x), weight_nt(w)))


def rows_t(x):
    return jnp.concatenate(split(x.T), 0)


def mm_tn(xt, y):
    return fold_rows(fold(dot(xt, pair(y))))


def deep(w):
    return jnp.concatenate([w, jnp.zeros((WIDE - EMB, w.shape[1]), F32)], 0)


def roll(x, shift, axis):
    return pltpu.roll(x, shift, axis)


def four_to_three(y):
    lane = iota(y[0].shape, 1)
    a = jnp.where(lane < 96, y[0], roll(y[1], 96, 1))
    b = jnp.where(lane < 64, roll(y[1], 96, 1), roll(y[2], 64, 1))
    c = jnp.where(lane < 32, roll(y[2], 64, 1), roll(y[3], 32, 1))
    return a, b, c


def three_to_four(x):
    lane = iota(x[0].shape, 1)
    live = lane < EMB
    a = x[0]
    b = jnp.where(lane < 32, roll(x[0], 32, 1), roll(x[1], 32, 1))
    c = jnp.where(lane < 64, roll(x[1], 64, 1), roll(x[2], 64, 1))
    d = roll(x[2], 96, 1)
    return tuple(jnp.where(live, v, 0.0) for v in (a, b, c, d))


def hidden_rows(ref, start, count):
    return jnp.concatenate(
        four_to_three([ref[pl.ds(start + c, count, stride=4), :] for c in range(4)]), 1
    )


def put_hidden_rows(ref, start, count, x):
    parts = three_to_four([x[:, i * WIDE : (i + 1) * WIDE] for i in range(3)])
    for c in range(4):
        ref[pl.ds(start + c, count, stride=4), :] = parts[c]


def flatten(ref, start, groups, out):
    parts = four_to_three([ref[pl.ds(start + c, groups, stride=4), :] for c in range(4)])
    for c in range(3):
        out[pl.ds(c, groups, stride=3), :] = parts[c]


def norm_stats(x):
    live = iota(x.shape, 1) < EMB
    mean = jnp.sum(x, 1, keepdims=True) * (1.0 / EMB)
    centred = jnp.where(live, x - mean, 0.0)
    var = jnp.sum(centred * centred, 1, keepdims=True) * (1.0 / EMB)
    inv = lax.rsqrt(var + eps_norm)
    return centred * inv, inv


def norm(x, gain, bias):
    hat, _ = norm_stats(x)
    return hat * gain + bias


def norm_back(hat, inv, gain, grad):
    up = grad * gain
    one = jnp.sum(up, 1, keepdims=True) * (1.0 / EMB)
    two = jnp.sum(up * hat, 1, keepdims=True) * (1.0 / EMB)
    live = iota(hat.shape, 1) < EMB
    return jnp.where(live, inv * (up - one - hat * two), 0.0)


def colsum(x):
    return jnp.sum(x, 0, keepdims=True)


def gelu(x):
    return 0.5 * x * (1.0 + lax.erf(x * (0.5**0.5)))


def gelu_both(x):
    cdf = 0.5 * (1.0 + lax.erf(x * (0.5**0.5)))
    slope = cdf + x * (jnp.exp(x * x * -0.5) * 0.3989422804014327)
    return x * cdf, slope


def head_groups(x):
    lane = iota(x.shape, 1)
    swapped = roll(x, 64, 1)
    return jnp.where(lane < 64, x, swapped), jnp.where(lane < 64, swapped, x)


def as_left(x):
    both = []
    low = iota(x.shape, 1) < 64
    for part in head_groups(x):
        hi = part.astype(BF16).astype(F32)
        one = jnp.where(low, hi, part - hi).astype(BF16)
        both.append(jnp.concatenate([one, one], 1))
    return both


def as_right(x):
    return [pair(part) for part in head_groups(x)]


def head_mask(h, width):
    lane = iota((1, width), 1)
    lane = jnp.bitwise_and(lane, 63)
    low = jnp.bitwise_and(h, 3) * HDIM
    return jnp.where((lane >= low) & (lane < low + HDIM), 1.0, 0.0)


def own_lanes(h):
    lane = iota((1, WIDE), 1)
    return jnp.where((lane >= h * HDIM) & (lane < (h + 1) * HDIM), 1.0, 0.0)


def score_tiles(s, rows, region):
    tiles = [s[:, i * WIDE : (i + 1) * WIDE] for i in range(3)]
    if region is not None:
        return [t + region[rows, i * WIDE : (i + 1) * WIDE] for i, t in enumerate(tiles)]
    pad = jnp.where(iota((1, WIDE), 1) < VOX - 2 * WIDE, 0.0, -1e30)
    return tiles[:2] + [tiles[2] + pad]


def put_split(ref, rows, i, x):
    hi, lo = split(x)
    ref[rows, i * WIDE : (i + 1) * WIDE] = hi
    ref[rows, ROWS + i * WIDE : ROWS + (i + 1) * WIDE] = lo


def attention(normed, layer, save, lse, mixed, sc, region=None):
    left, right, values = sc
    x = pair(normed)
    qkv = []
    for i in range(3):
        w = deep(layer[pl.ds(R_QKV + i, EMB, stride=3), :])
        y = fold(dot(x, weight_nn(w))) + layer[R_QKVB + i : R_QKVB + i + 1, :]
        if i == 0:
            y = y * (HDIM**-0.5 * LOG2E)
        save[:, i * WIDE : (i + 1) * WIDE] = y
        qkv.append(y)
    for g, part in enumerate(as_left(qkv[0])):
        left[g] = part
    for g, part in enumerate(as_right(qkv[1])):
        right[g] = part
    v = pair(jnp.where(iota((ROWS, WIDE), 1) == EMB, 1.0, qkv[2]))
    values[0:ROWS, :] = v
    values[ROWS : 2 * ROWS, :] = v
    mixed[...] = jnp.zeros_like(mixed)
    lse[...] = jnp.zeros_like(lse)

    def per_pair(pair_of, carry):
        heads = [2 * pair_of, 2 * pair_of + 1]
        masks = [head_mask(h, 2 * WIDE).astype(BF16) for h in heads]
        lanes = [own_lanes(h) for h in heads]
        spots = [jnp.where(iota((1, WIDE), 1) == h, 1.0, 0.0) for h in heads]
        g = lax.div(pair_of, 2)
        for b in range(ROWS // BLK):
            rows = slice(b * BLK, (b + 1) * BLK)
            out = level = 0.0
            for k in range(2):
                s = dot_nt(left[g, rows, :] * masks[k], right[g])
                tiles = score_tiles(s, rows, region)
                top = jnp.maximum(jnp.maximum(tiles[0], tiles[1]), tiles[2])
                top = jnp.max(top, 1, keepdims=True)
                parts = [split(jnp.exp2(t - top)) for t in tiles]
                e = jnp.concatenate([p[0] for p in parts] + [p[1] for p in parts], 1)
                o = fold(dot(e, values[...]))
                total = o[:, EMB : EMB + 1]
                out = out + o * (lanes[k] / total)
                level = level + (top + jnp.log(total) * LOG2E) * spots[k]
            mixed[rows, :] += out
            lse[rows, :] += level
        return carry

    lax.fori_loop(0, HEADS // 2, per_pair, 0)
    proj = deep(layer[R_PROJ : R_PROJ + EMB, :])
    return mm(mixed[...], proj) + layer[R_PROJB : R_PROJB + 1, :]


def attention_back(grad, normed, layer, save, lse, mixed, sc, grads, at, region=None):
    left, right, gleft, vright, keys, dq, dkv_t, weights, slopes, q_t, do_t, dmix, s, dp = sc
    proj = deep(layer[R_PROJ : R_PROJ + EMB, :])
    grads[at + R_PROJ : at + R_PROJ + EMB, :] = mm_tn(rows_t(mixed[...]), grad)[:EMB]
    grads[at + R_PROJB : at + R_PROJB + 1, :] = colsum(grad)
    d_mixed = mm_nt(grad, proj)
    dmix[...] = d_mixed * mixed[...]
    q, k, v = (save[:, i * WIDE : (i + 1) * WIDE] for i in range(3))
    for g, part in enumerate(as_left(q)):
        left[g] = part
    for g, part in enumerate(as_right(k)):
        right[g] = part
    for g, part in enumerate(as_left(d_mixed)):
        gleft[g] = part
    for g, part in enumerate(as_right(v)):
        vright[g] = part
    kk = pair(k)
    keys[0:ROWS, :] = kk
    keys[ROWS : 2 * ROWS, :] = kk
    for ref, x in ((q_t, q), (do_t, d_mixed)):
        hi, lo = split(x.T)
        ref[0] = hi
        ref[1] = lo
    dq[...] = jnp.zeros_like(dq)
    dkv_t[...] = jnp.zeros_like(dkv_t)

    def per_pair(pair_of, carry):
        g = lax.div(pair_of, 2)
        for k in range(2):
            h = 2 * pair_of + k
            mask = head_mask(h, 2 * WIDE).astype(BF16)
            s[k] = dot_nt(left[g] * mask, right[g])
            dp[k] = dot_nt(gleft[g] * mask, vright[g])
        for k in range(2):
            h = 2 * pair_of + k
            lanes = own_lanes(h)
            at_h = jnp.where(iota((1, WIDE), 1) == h, 1.0, 0.0)
            for b in range(ROWS // BLK):
                rows = slice(b * BLK, (b + 1) * BLK)
                level = jnp.sum(lse[rows, :] * at_h, 1, keepdims=True)
                delta = jnp.sum(dmix[rows, :] * lanes, 1, keepdims=True)
                for i, t in enumerate(score_tiles(s[k, rows, :], rows, region)):
                    p = jnp.exp2(t - level)
                    put_split(weights.at[k], rows, i, p)
                    p = p * (dp[k, rows, i * WIDE : (i + 1) * WIDE] - delta)
                    put_split(slopes.at[k], rows, i, p)
        total = 0.0
        for k in range(2):
            total = total + fold(dot(slopes[k], keys[...])) * own_lanes(2 * pair_of + k)
        dq[...] += total
        for k in range(2):
            here = pl.ds(pl.multiple_of((2 * pair_of + k) * HDIM, HDIM), HDIM)
            for i, (t, m) in enumerate(((q_t, slopes), (do_t, weights))):
                lhs = jnp.concatenate([t[0, here, :], t[1, here, :]], 0)
                dkv_t[i, here, :] = fold_rows(fold(dot(lhs, m[k])))
        return carry

    lax.fori_loop(0, HEADS // 2, per_pair, 0)
    d_q = dq[...] * HDIM**-0.5
    d_k = dkv_t[0].T * (1.0 / LOG2E)
    d_v = dkv_t[1].T
    x_t = rows_t(normed)
    d_normed = None
    for i, d in enumerate((d_q, d_k, d_v)):
        grads[pl.ds(at + R_QKV + i, EMB, stride=3), :] = mm_tn(x_t, d)[:EMB]
        grads[at + R_QKVB + i : at + R_QKVB + i + 1, :] = colsum(d)
        part = mm_nt(d, deep(layer[pl.ds(R_QKV + i, EMB, stride=3), :]))
        d_normed = part if d_normed is None else d_normed + part
    return d_normed


def mlp(middle, layer, hpre):
    normed = norm(middle, layer[2:3, :], layer[3:4, :])
    w = deep(hidden_rows(layer, R_HID, EMB))
    pre = mm(normed, w) + hidden_rows(layer, R_HIDB, 1)
    hpre[...] = pre
    out = mm(gelu(pre), layer[R_OUT : R_OUT + HID, :])
    return middle + out + layer[R_OUTB : R_OUTB + 1, :]


def mlp_back(grad, middle, hpre, layer, grads, at):
    hat, inv = norm_stats(middle)
    normed = hat * layer[2:3, :] + layer[3:4, :]
    act, slope = gelu_both(hpre[...])
    grads[at + R_OUTB : at + R_OUTB + 1, :] = colsum(grad)
    grads[at + R_OUT : at + R_OUT + HID, :] = mm_tn(rows_t(grad), act).T
    d_pre = mm_nt(grad, layer[R_OUT : R_OUT + HID, :]) * slope
    put_hidden_rows(grads, at + R_HIDB, 1, colsum(d_pre))
    put_hidden_rows(grads, at + R_HID, EMB, mm_tn(rows_t(normed), d_pre)[:EMB])
    d_normed = mm_nt(d_pre, deep(hidden_rows(layer, R_HID, EMB)))
    grads[at + 2 : at + 3, :] = colsum(d_normed * hat)
    grads[at + 3 : at + 4, :] = colsum(d_normed)
    return grad + norm_back(hat, inv, layer[2:3, :], d_normed)


def pre_norm_back(grad, tokens, layer, grads, at):
    hat, inv = norm_stats(tokens)
    grads[at : at + 1, :] = colsum(grad * hat)
    grads[at + 1 : at + 2, :] = colsum(grad)
    return norm_back(hat, inv, layer[0:1, :], grad)


def region_of(rows, sizes):
    d = lax.shift_right_logical(rows * 1338, 16)
    line = lax.shift_right_logical(rows * 9363, 16)
    places = (d, line - d * WIN, rows - line * WIN)
    starts = (lax.axis_index("slab") * WIN, lax.axis_index("mp") * WIN, 0)
    total = None
    for place, start, blocks in zip(places, starts, sizes + (1,)):
        turned = jnp.where(place < SHIFT, place + FAR, place - SHIFT) + start
        length = WIN * blocks
        part = jnp.where(turned < length - WIN, 0, jnp.where(turned < length - SHIFT, 1, 2))
        total = part if total is None else total * 3 + part
    return total


def put_region(region, sizes):
    rows = region_of(iota((ROWS, WIDE), 0), sizes)[:, 0:1]
    lanes = region_of(iota((8, ROWS), 1), sizes)[0:1, :]
    apart = jnp.where(rows == lanes, 0.0, -100.0 * LOG2E)
    region[...] = jnp.where(iota((ROWS, ROWS), 1) < VOX, apart, -1e30)


def send_parts(ref, a, b, c):
    far = FAR * WIN
    near = SHIFT * WIN
    for d in range(SHIFT):
        base = d * PLANE
        c[d * near : (d + 1) * near, :] = ref[base : base + near, :]
        a[d * far : (d + 1) * far, :] = ref[base + near : base + PLANE, :]
    for d in range(FAR):
        base = (d + SHIFT) * PLANE
        b[d * near : (d + 1) * near, :] = ref[base : base + near, :]


def take_parts(own, a, b, c, out):
    far = FAR * WIN
    near = SHIFT * WIN
    for d in range(WIN):
        base = d * PLANE
        if d < SHIFT:
            out[base : base + near, :] = c[d * near : (d + 1) * near, :]
            out[base + near : base + PLANE, :] = a[d * far : (d + 1) * far, :]
        else:
            e = d - SHIFT
            out[base : base + near, :] = b[e * near : (e + 1) * near, :]
            out[base + near : base + PLANE, :] = own[base + near : base + PLANE, :]
    out[VOX:, :] = jnp.zeros((ROWS - VOX, WIDE), F32)


def span_of(groups):
    low, high = groups
    first = 3 * low // 8 * 8
    last = -(-3 * high // 8) * 8
    return first, min(last, NPARAM // WIDE // 8 * 8) - first


def copied(params, groups, flat, sem):
    first, rows = span_of(groups)
    size = rows * WIDE
    return pltpu.make_async_copy(
        params.at[pl.ds(first * WIDE, size)], flat.at[pl.ds(0, size)], sem
    )


def relay(groups, flat, out, square, last=None):
    low, high = groups
    first, rows = span_of(groups)
    square[0:rows, :] = flat[0 : rows * WIDE].reshape(rows, WIDE)
    if last is not None:
        square[rows : rows + 24, :] = jnp.zeros((24, WIDE), F32)
        square[rows : rows + 1, 0 : last.shape[0]] = last[...].reshape(1, last.shape[0])
    skip = 3 * low - first
    n = high - low
    parts = three_to_four([square[pl.ds(skip + c, n, stride=3), :] for c in range(3)])
    for c in range(4):
        out[pl.ds(c, n, stride=4), :] = parts[c]


FIRST_SPANS = ((0, 98), (98, 392))
LAYER_SPANS = ((389, 681), (680, 972))
CONV_SPANS = ((971, 1620), (1620, GROUPS))


def prep_kernel(spans, params, *refs, last=None):
    outs, (flats, square, sems) = refs[: len(spans)], refs[-3:]
    for i, groups in enumerate(spans):
        copied(params, groups, flats[i], sems.at[i]).start()
    for i, groups in enumerate(spans):
        copied(params, groups, flats[i], sems.at[i]).wait()
        relay(groups, flats[i], outs[i], square, last if i == len(spans) - 1 else None)


def head_picks():
    width = HEAD_ROWS * WIDE
    place = iota((WIDE, width), 1) - HEAD_LANE
    row = iota((WIDE, width), 0)
    here = (place >= row * CLASSES) & (place < (row + 1) * CLASSES) & (row <= EMB)
    place = iota((width, WIDE), 0) - HEAD_LANE
    col = iota((width, WIDE), 1)
    row = lax.shift_right_logical(place * 4682, 16)
    there = (place - row * CLASSES == col) & (place >= 0)
    return jnp.where(here, 1.0, 0.0), jnp.where(there, 1.0, 0.0).astype(BF16)


def prep_conv_kernel(
    last, params, conv0, conv1, head, weights0, weights1, vectors, *scratch
):
    prep_kernel(CONV_SPANS, params, conv0, conv1, *scratch, last=last)
    tap_weights(conv0, 3, weights0)
    tap_weights(conv1, 0, weights1)
    vectors[0:1, :] = conv0[3 + TAP_ROWS : 4 + TAP_ROWS, :]
    vectors[1:4, :] = conv1[TAP_ROWS : TAP_ROWS + 3, :]
    vectors[4:8, :] = jnp.zeros((4, WIDE), F32)
    square = scratch[1]
    first, _ = span_of(CONV_SPANS[1])
    row = jnp.concatenate(
        [square[HEAD_ROW + i - first : HEAD_ROW + i - first + 1, :] for i in range(HEAD_ROWS)], 1
    )
    here, there = head_picks()
    hi, lo = split(here * row)
    head[...] = dot(hi, there) + dot(lo, there)


def head_rows(d_head, out, at):
    here, there = head_picks()
    hi, lo = split(d_head)
    spread = (dot_nt(hi, there) + dot_nt(lo, there)) * here
    row = colsum(spread)
    for i in range(HEAD_ROWS):
        out[at + i : at + i + 1, :] += row[:, i * WIDE : (i + 1) * WIDE]


class Rows:
    def __init__(self, ref, at):
        self.ref, self.at = ref, at

    def __getitem__(self, key):
        rows, lanes = key
        if isinstance(rows, slice):
            rows = slice(rows.start + self.at, rows.stop + self.at)
        else:
            rows = pl.ds(rows.start + self.at, rows.size, stride=rows.stride)
        return self.ref[rows, lanes]


def merged_norm(x):
    mean = jnp.sum(x, 1, keepdims=True) * (1.0 / MERGE)
    centred = x - mean
    var = jnp.sum(centred * centred, 1, keepdims=True) * (1.0 / MERGE)
    return centred * lax.rsqrt(var + eps_norm)


def first_kernel(
    feats, merge, lay0,
    dense, tok0, save, lse, mixed, middle, hpre, tok1, ahead, pa, pb, pc,
    *sc,
):
    dense[VOX:, :] = jnp.zeros((ROWS - VOX, MERGE), F32)
    for line in range(PLANE):
        dense[line * WIN : (line + 1) * WIN, :] = feats[line]
    hat = merged_norm(dense[...])
    normed = hat * hidden_rows(merge, 0, 1) + hidden_rows(merge, 4, 1)
    tokens = mm(normed, merge[8 : 8 + MERGE, :])
    tok0[...] = tokens
    layer = Rows(lay0, 0)
    normed = norm(tokens, layer[0:1, :], layer[1:2, :])
    attended = attention(normed, layer, save, lse, mixed, sc)
    mid = tokens + attended
    middle[...] = mid
    tokens = mlp(mid, layer, hpre)
    tok1[...] = tokens
    ahead[...] = norm(tokens, layer[1165:1166, :], layer[1166:1167, :])
    send_parts(ahead, pa, pb, pc)


def shifted_kernel(
    sizes,
    own, pa, pb, pc, lay1,
    window, save, lse, mixed, out, qa, qb, qc,
    region, *sc,
):
    put_region(region, sizes)
    take_parts(own, pa, pb, pc, window)
    out[...] = attention(
        window[...], Rows(lay1, 1), save, lse, mixed, sc, region
    )
    send_parts(out, qa, qb, qc)


def to_lines(ref, out):
    for line in range(PLANE):
        out[line, 0:WIN, :] = ref[line * WIN : (line + 1) * WIN, :]
        out[line, WIN:8, :] = jnp.zeros((8 - WIN, WIDE), F32)


def from_lines(ref, out):
    out[VOX:, :] = jnp.zeros((ROWS - VOX, WIDE), F32)
    for line in range(PLANE):
        out[line * WIN : (line + 1) * WIN, :] = ref[line, 0:WIN, :]


def send_sides(lines, low_d, high_d, low_h, high_h):
    low_d[...] = lines[0 : 2 * WIN]
    high_d[...] = lines[(WIN - 2) * WIN :]
    for d in range(WIN):
        low_h[2 * d : 2 * d + 2] = lines[d * WIN : d * WIN + 2]
        high_h[2 * d : 2 * d + 2] = lines[d * WIN + WIN - 2 : (d + 1) * WIN]


def second_kernel(
    tok1, own, qa, qb, qc, lay1, lay2,
    mid1, hpre1, tok2, save, lse, mixed, mid2, hpre2, lines,
    s0, s1, s2, s3,
    attended, *sc,
):
    take_parts(own, qa, qb, qc, attended)
    mid = tok1[...] + attended[...]
    mid1[...] = mid
    tokens = mlp(mid, Rows(lay1, 1), hpre1)
    tok2[...] = tokens
    layer = Rows(lay2, 2)
    normed = norm(tokens, layer[0:1, :], layer[1:2, :])
    mid = tokens + attention(normed, layer, save, lse, mixed, sc)
    mid2[...] = mid
    attended[...] = mlp(mid, layer, hpre2)
    to_lines(attended, lines)
    send_sides(lines, s0, s1, s2, s3)


def grown_lines(own, low_d, high_d, low_h, high_h, out):
    out[...] = jnp.zeros_like(out)
    for d in range(WIN):
        out[d + 2, 2 : 2 + WIN] = own[d * WIN : (d + 1) * WIN]
    for d in range(2):
        out[d, 2 : 2 + WIN] = low_d[d * WIN : (d + 1) * WIN]
        out[d + 9, 2 : 2 + WIN] = high_d[d * WIN : (d + 1) * WIN]
    for d in range(11):
        out[d, 0:2] = low_h[2 * d : 2 * d + 2]
        out[d, 9:11] = high_h[2 * d : 2 * d + 2]


def put_marks(labels, valid, out):
    across = iota((8, WIN), 1) == iota((8, WIN), 0)
    classes = iota((8, WIDE), 1) - EMB
    for d in range(WIN):
        code = jnp.where(valid[d] == 1, labels[d], -1 - EMB - WIDE)
        code = code.astype(F32)
        for h in range(WIN):
            line = jnp.where(across, code[h : h + 1, :], 0.0)
            column = jnp.sum(line, 1, keepdims=True)
            mark = jnp.where(column == classes.astype(F32), 1.0, 0.0)
            out[d * WIN + h] = jnp.where(iota((8, WIDE), 0) < WIN, mark, 0.0)


def taps(source, first_plane, planes, first_line, lines, out):
    def per_plane(d, carry):
        for c in range(3):
            for b in range(3):
                x = source[d + first_plane, first_line + b : first_line + b + lines]
                if c != 1:
                    x = roll(x, 1 if c == 0 else 7, 1)
                x = pair(x.reshape(lines * 8, WIDE))
                at = pl.multiple_of(d * (lines * 8), lines * 8)
                t = b * 3 + c
                out[pl.ds(at, lines * 8), t * 256 : (t + 1) * 256] = x
        return carry

    lax.fori_loop(0, planes, per_plane, 0)


def tap_weights(ref, at, out):
    def per_tap(i, carry):
        w = deep(ref[pl.ds(i * EMB + at, EMB), :])
        out[pl.ds(pl.multiple_of(i * 256, 256), 256), :] = weight_nn(w)
        return carry

    lax.fori_loop(0, 27, per_tap, 0)


def tap_weights_back(ref, at, out):
    for i in range(27):
        w = deep(ref[(26 - i) * EMB + at : (27 - i) * EMB + at, :])
        out[:, i * 256 : (i + 1) * 256] = weight_nt(w)


def conv(side, weights, planes, pitch, at_once, put, back=False):
    rows = at_once * pitch
    for start in range(0, planes, at_once):
        total = None
        for a in range(3):
            low = (start + a) * pitch
            x = side[low : low + rows, :]
            if back:
                part = dot_nt(x, weights[:, a * 2304 : (a + 1) * 2304])
            else:
                part = dot(x, weights[a * 2304 : (a + 1) * 2304, :])
            total = part if total is None else total + part
        put(start, fold(total))


def conv_weight_grad(side, grad_rows, pitch, out, at):
    rows = 512
    g = jnp.concatenate([grad_rows, jnp.zeros((rows - grad_rows.shape[0], WIDE), F32)], 0)
    left = jnp.concatenate(split(g.T[:EMB]), 0)
    for a in range(3):
        for bc in range(9):
            y = dot(left, side[a * pitch : a * pitch + rows, bc * 256 : (bc + 1) * 256])
            y = deep(fold_rows(fold(y))).T
            t = a * 9 + bc
            out[at + t * EMB : at + (t + 1) * EMB, :] = y[:EMB]


def volume_mask(sizes, planes, lines, reach, real_lines):
    slab, row = lax.axis_index("slab"), lax.axis_index("mp")
    ends = (slab == 0, slab == sizes[0] - 1, row == 0, row == sizes[1] - 1)
    shape = (planes, lines, 8, WIDE)
    d, h, w = iota(shape, 0), iota(shape, 1), iota(shape, 2)
    low_d = jnp.where(ends[0], reach, 0)
    high_d = jnp.where(ends[1], planes - reach, planes)
    low_h = jnp.where(ends[2], reach, 0)
    high_h = jnp.where(ends[3], real_lines - reach, real_lines)
    inside = (d >= low_d) & (d < high_d) & (h >= low_h) & (h < high_h) & (w < WIN)
    return jnp.where(inside, 1.0, 0.0)


def conv_kernel(
    sizes,
    own, s0, s1, s2, s3, labels, valid, weights0, weights1, vectors,
    grown, pre, tok, stats, t0, t1, t2, t3,
    act, side, side_own, marks,
):
    grown_lines(own, s0, s1, s2, s3, grown)
    put_marks(labels, valid, marks)
    taps(grown, 0, 11, 0, 10, side)
    bias0 = vectors[0:1, :]
    inside = volume_mask(sizes, 9, 10, 1, 9)


    def put(start, y):
        z = (y + bias0).reshape(3, 10, 8, WIDE)
        pre[start : start + 3] = z
        act[start : start + 3] = gelu(z) * inside[start : start + 3]

    conv(side, weights0, 9, 80, 3, put)
    taps(act, 0, 9, 0, 8, side_own)
    bias1 = vectors[1:2, :]
    sums = []

    def put_own(start, y):
        y = (y + bias1).reshape(WIN, 8, 8, WIDE)[:, 0:WIN]
        y = y + own[...].reshape(WIN, WIN, 8, WIDE)
        y = jnp.where(iota(y.shape, 2) < WIN, y, 0.0).reshape(PLANE, 8, WIDE)
        tok[...] = y + marks[...]
        send_sides(tok, t0, t1, t2, t3)
        flat = y.reshape(PLANE * 8, WIDE)
        sums.append(colsum(flat))
        sums.append(colsum(flat * flat))

    conv(side_own, weights1, WIN, 64, WIN, put_own)
    count = jnp.sum(marks[...].reshape(PLANE * 8, WIDE))
    row = iota((8, WIDE), 0)
    stats[...] = (
        jnp.where(row == 0, sums[0], 0.0)
        + jnp.where(row == 1, sums[1], 0.0)
        + jnp.where(row == 2, count, 0.0)
    )


def head_kernel(
    voxels,
    own, s0, s1, s2, s3, sums, vectors, head_w,
    grown, slope_out, stats, d_head, d_rows,
):
    grown_lines(own, s0, s1, s2, s3, grown)
    rows = 11 * 12 * 8
    both = grown[...].reshape(rows, WIDE)
    lane = iota((rows, WIDE), 1)
    tokens = jnp.where(lane < EMB, both, 0.0)
    target = jnp.where(lane < CLASSES, roll(both, WIDE - EMB, 1), 0.0)
    live = jnp.sum(target, 1, keepdims=True)
    count = F32(voxels)
    average = sums[0:1, :] / count
    spread = sums[1:2, :] / count - average * average
    inv = lax.rsqrt(spread + eps_norm)
    gain = vectors[2:3, :]
    bias = vectors[3:4, :]
    hat = (tokens - average) * inv
    act, slope = gelu_both(hat * gain + bias)
    act = jnp.where(lane == EMB, 1.0, act)
    w = head_w[...]
    logits = mm(act, w)
    logits = jnp.where(lane < CLASSES, logits, -1e30)
    top = jnp.max(logits, 1, keepdims=True)
    e = jnp.exp(logits - top)
    total = jnp.sum(e, 1, keepdims=True)
    logp = logits - top - jnp.log(total)
    scale = 1.0 / sums[2:3, 0:1]
    d_logits = (e / total * live - target) * scale
    d_normed = jnp.where(lane < EMB, mm_nt(d_logits, w) * slope, 0.0)
    d_tokens = d_normed * gain * inv
    slope_out[...] = d_tokens.reshape(11, 12, 8, WIDE)

    def own_rows(x):
        x = x.reshape(11, 12, 8, WIDE)[2:9, 2:9]
        x = jnp.where(iota(x.shape, 2) < WIN, x, 0.0)
        return x.reshape(PLANE * 8, WIDE)

    loss = -jnp.sum(own_rows(target * jnp.where(lane < CLASSES, logp, 0.0)))
    own_d = own_rows(d_logits)
    own_n = own_rows(d_normed)
    own_hat = own_rows(hat)
    zeros = jnp.zeros((512 - PLANE * 8, WIDE), F32)
    left = rows_t(jnp.concatenate([own_d, zeros], 0))
    d_head[...] = mm_tn(left, jnp.concatenate([own_rows(act), zeros], 0)).T
    d_gain = colsum(own_n * own_hat)
    d_bias = colsum(own_n)
    d_average = -d_bias * gain * inv
    d_spread = d_gain * gain * inv * inv * -0.5
    d_two = d_spread / count
    d_one = (d_average - 2.0 * average * d_spread) / count
    row = iota((8, WIDE), 0)
    live_lane = iota((8, WIDE), 1) < EMB
    stats[...] = (
        jnp.where((row == 0) & live_lane, d_one, 0.0)
        + jnp.where((row == 1) & live_lane, d_two, 0.0)
        + jnp.where(row == 2, loss, 0.0)
    )
    d_rows[...] = (
        jnp.where(row == 0, d_gain, 0.0)
        + jnp.where(row == 1, d_bias, 0.0)
    )


def sides_back_kernel(sizes, grown, pre, side_act, side_grown, act):
    act[0:9] = gelu(pre[...]) * volume_mask(sizes, 9, 10, 1, 9)
    act[9:10] = jnp.zeros((1, 10, 8, WIDE), F32)
    taps(act, 0, 10, 0, 8, side_act)
    taps(grown, 1, 10, 1, 8, side_grown)


def weights_back_kernel(conv0, conv1, weights0, weights1):
    tap_weights_back(conv0, 3, weights0)
    tap_weights_back(conv1, 0, weights1)


def conv_back_kernel(
    sizes,
    tok, slope, sums, pre, side_act, side_grown, weights0, weights1, d_rows, d_head,
    d_own, keep, send, carry, seam,
    grads, dgrown, act, side, side_own, flat,
):
    lane = iota((11, 12, 8, WIDE), 3)
    inside = volume_mask(sizes, 11, 12, 2, 11)
    steady = sums[0:1, :].reshape(1, 1, 1, WIDE)
    rising = 2.0 * sums[1:2, :].reshape(1, 1, 1, WIDE)
    d_tok = slope[...] + jnp.where(lane < EMB, (steady + tok[...] * rising) * inside, 0.0)
    dgrown[...] = d_tok
    grads[5191:, :] = jnp.zeros((45, WIDE), F32)
    grads[0:8, :] = jnp.zeros((8, WIDE), F32)
    grads[5189:5191, :] = d_rows[0:2, :]
    own = dgrown[2:9, 2:10]
    line = iota(own.shape, 1)
    own = jnp.where(line < WIN, own, 0.0).reshape(WIN * 64, WIDE)
    grads[5188:5189, :] = colsum(own)

    near = volume_mask(sizes, 9, 10, 1, 9)
    conv_weight_grad(side_act, own, 64, grads, 2596)
    taps(dgrown, 0, 11, 0, 10, side)


    def put(start, y):
        _, s = gelu_both(pre[start : start + 3])
        act[start : start + 3] = y.reshape(3, 10, 8, WIDE) * s * near[start : start + 3]

    conv(side, weights1, 9, 80, 3, put, back=True)

    own = act[1:8, 1:9]
    line = iota(own.shape, 1)
    own = jnp.where(line < WIN, own, 0.0).reshape(WIN * 64, WIDE)
    grads[2595:2596, :] = colsum(own)
    conv_weight_grad(side_grown, own, 64, grads, 3)
    carry[...] = grads[0:24, :]
    flat[3 * (GROUPS - CUTS[3]) :, :] = jnp.zeros((flat.shape[0] - 3912, WIDE), F32)
    flatten(grads, 20, GROUPS - CUTS[3], flat)
    start = 3 * CUTS[3]
    head_rows(d_head[...], flat, HEAD_ROW - start)
    seam[...] = flat[0 : LATE_ROWS - start, :]
    scatter(sizes, flat, LATE_ROWS - start, keep, send)
    taps(act, 0, 9, 0, 8, side_own)

    def put_own(start, y):
        y = y.reshape(WIN, 8, 8, WIDE)[:, 0:WIN] + dgrown[2:9, 2:9]
        y = jnp.where(iota(y.shape, 2) < WIN, y, 0.0)
        d_own[...] = y.reshape(PLANE, 8, WIDE)

    conv(side_own, weights0, WIN, 64, WIN, put_own, back=True)


def back_mlp_kernel(d_own, lay2, mid2, hpre2, d_mid, grads, dense):
    from_lines(d_own, dense)
    grads[...] = jnp.zeros_like(grads)
    d_mid[...] = mlp_back(dense[...], mid2[...], hpre2, Rows(lay2, 2), grads, 2)


def back_two_kernel(
    d_mid2, grads2, carry, lay1, lay2, tok2, save, lse, mixed, mid1, hpre1,
    d_mid, grads1, flat, carry2, pa, pb, pc,
    grads, *sc,
):
    layer = Rows(lay2, 2)
    grads[0:1168, :] = grads2[...]
    d = d_mid2[...]
    tokens = tok2[...]
    normed = norm(tokens, layer[0:1, :], layer[1:2, :])
    d_normed = attention_back(d, normed, layer, save, lse, mixed, sc, grads, 2)
    d = d + pre_norm_back(d_normed, tokens, layer, grads, 2)
    grads[1167:1184, :] = carry[3:20, :]
    flatten(grads, 32, CUTS[3] - CUTS[2], flat)
    carry2[...] = grads[0:32, :]
    layer = Rows(lay1, 1)
    d = mlp_back(d, mid1[...], hpre1, layer, grads1, 1)
    d_mid[...] = d
    send_parts(d_mid, pa, pb, pc)


def back_shifted_kernel(
    sizes,
    own, pa, pb, pc, lay1, window, save, lse, mixed, grads1, carry2, _,
    d_window, flat, carry1, qa, qb, qc,
    region, grads, grad, *sc,
):
    put_region(region, sizes)
    take_parts(own, pa, pb, pc, grad)
    grads[0:1168, :] = grads1[...]
    grads[0:3, :] = jnp.zeros((3, WIDE), F32)
    d_window[...] = attention_back(
        grad[...], window[...], Rows(lay1, 1), save, lse, mixed, sc, grads, 1,
        region,
    )
    send_parts(d_window, qa, qb, qc)
    grads[1166:1196, :] = carry2[2:32, :]
    flatten(grads, 12, CUTS[2] - CUTS[1], flat)
    carry1[...] = grads[0:16, :]


def back_first_kernel(
    sizes,
    d_mid, own, qa, qb, qc, tok1, lay0, lay1, merge, dense, tok0, save, lse, mixed, middle, hpre,
    carry1, flat1, flat2, seam, _,
    keep, send,
    flat, grads, grad, *sc,
):
    take_parts(own, qa, qb, qc, grad)
    grads[1556:1572, :] = carry1[...]
    d = d_mid[...] + pre_norm_back(grad[...], tok1[...], Rows(lay1, 1), grads, 1557)
    layer = Rows(lay0, 0)
    at = MERGE_ROWS
    d = mlp_back(d, middle[...], hpre, layer, grads, at)
    tokens = tok0[...]
    normed = norm(tokens, layer[0:1, :], layer[1:2, :])
    d_normed = attention_back(d, normed, layer, save, lse, mixed, sc, grads, at)
    d = d + pre_norm_back(d_normed, tokens, layer, grads, at)
    live = iota((ROWS, WIDE), 0) < VOX
    d = jnp.where(live, d, 0.0)
    hat = merged_norm(dense[...])
    gain = hidden_rows(merge, 0, 1)
    bias = hidden_rows(merge, 4, 1)
    w = merge[8 : 8 + MERGE, :]
    put_hidden_rows(grads, 8 - 8, 1, jnp.zeros((1, MERGE), F32))
    grads[8 : 8 + MERGE, :] = mm_tn(rows_t(d), hat * gain + bias).T
    d_hat = mm_nt(d, w)
    put_hidden_rows(grads, 0, 1, colsum(d_hat * hat))
    put_hidden_rows(grads, 4, 1, colsum(d_hat))
    flatten(grads, 0, CUTS[1], flat)
    at = 0
    for cut, part in ((CUTS[1], flat1), (CUTS[2], flat2), (CUTS[3], seam)):
        at = 3 * cut
        flat[at : at + part.shape[0], :] = part[...]
    at += seam.shape[0]
    if flat.shape[0] > at:
        flat[at:, :] = jnp.zeros((flat.shape[0] - at, WIDE), F32)
    scatter(sizes, flat, 0, keep, send)


def radices(count):
    steps = [2]
    left = count // 2
    while left > 1:
        steps.append(4 if left >= 4 else 2)
        left //= steps[-1]
    return steps


def block_rows(rows, count):
    return -(-rows // (8 * count)) * 8


def own_number(sizes):
    return lax.axis_index("slab") * sizes[1] + lax.axis_index("mp")


def place_in_half(distance, count):
    place = 0
    shift = 1
    for radix in radices(count)[1:]:
        digit = jnp.bitwise_and(lax.shift_right_logical(distance, shift), radix - 1)
        place = place * radix + digit
        shift += radix.bit_length() - 1
    return place


def scatter(sizes, source, first, keep, send):
    count = sizes[0] * sizes[1]
    rows = keep.shape[0] * 2 // count
    me = own_number(sizes)
    odd = jnp.bitwise_and(me, 1)

    def per_pair(t, carry):
        for block, out in ((2 * t + odd, keep), (2 * t + 1 - odd, send)):
            place = place_in_half(jnp.bitwise_xor(block, me), count)
            at = pl.multiple_of(first + block * rows, 8)
            to = pl.multiple_of(place * rows, 8)
            out[pl.ds(to, rows), :] = source[pl.ds(at, rows), :]
        return carry

    lax.fori_loop(0, count // 2, per_pair, 0)


def traded(value, distance, count):
    pairs = [(i, i ^ distance) for i in range(count)]
    return lax.ppermute(value, ("slab", "mp"), pairs)


def later(got, after):
    return got if after is None else list(lax.optimization_barrier((*got, after)))[:-1]


def summing(keep, send, count):
    steps = radices(count)
    got = [keep, traded(send, 1, count)]
    shift = 1
    after = yield None
    for radix in steps[1:]:
        got = later(got, after)
        total = sum(got[1:], got[0])
        rows = total.shape[0] // radix
        parts = [total[k * rows : (k + 1) * rows] for k in range(radix)]
        got = parts[:1] + [traded(parts[k], k << shift, count) for k in range(1, radix)]
        shift += radix.bit_length() - 1
        after = yield parts[0]
    got = later(got, after)
    own = sum(got[1:], got[0])
    for radix in reversed(steps[1:]):
        shift -= radix.bit_length() - 1
        got = [own] + [traded(own, k << shift, count) for k in range(1, radix)]
        after = yield own
        own = jnp.concatenate(later(got, after), 0)
        yield own
    yield own, traded(own, 1, count)


def finished(chain, after=None):
    last = next(chain) if after is None else chain.send(after)
    while not isinstance(last, tuple):
        last = next(chain)
    return last


def exchanged_sum(value, count):
    shift = 0
    for radix in radices(count):
        got = [value] + [traded(value, k << shift, count) for k in range(1, radix)]
        while len(got) > 1:
            got = [got[i] + got[i + 1] for i in range(0, len(got), 2)]
        value = got[0]
        shift += radix.bit_length() - 1
    return value


PIECE = 131072


def adamw_kernel(
    sizes,
    late, late_other, early, early_other, tail, sums, params, first, second,
    new_params, new_first, new_second, loss, valid, norm_out,
    grad, scale_ref,
):
    count = sizes[0] * sizes[1]
    step = pl.program_id(0)

    @pl.when(step == 0)
    def gather():
        me = own_number(sizes)
        total = jnp.zeros((8, WIDE), F32)
        for ref in (late, late_other, early, early_other):
            x = ref[...]
            total = total + jnp.sum((x * x).reshape(-1, 8, WIDE), 0)
        norm = jnp.sqrt(jnp.sum(total))
        loss[0] = jnp.sum(tail[2:3, 0:1])
        valid[0] = jnp.sum(sums[2:3, 0:1])
        norm_out[0] = norm
        scale_ref[0] = jnp.minimum(1.0, clip_norm / (norm + 1e-06))
        start = 0
        for own, other, size in ((late, late_other, LATE_ROWS), (early, early_other, EARLY_ROWS)):
            rows = own.shape[0] * 2 // count

            def per_block(block, carry, own=own, other=other, rows=rows, start=start):
                distance = jnp.bitwise_xor(block, me)
                at = pl.ds(pl.multiple_of(place_in_half(distance, count) * rows, 8), rows)
                near = jnp.bitwise_and(distance, 1) == 0
                to = pl.ds(pl.multiple_of(start + block * rows, 8), rows)
                grad[to, :] = jnp.where(near, own[at, :], other[at, :])
                return carry

            lax.fori_loop(0, size // rows, per_block, 0)
            start += size

    def update(base, low, size):
        rows = -(-size // 1024) * 8
        at = pl.ds(pl.multiple_of(base // WIDE + low // WIDE, 8), rows)
        g = grad[at, :].reshape(rows * WIDE)[:size] * scale_ref[0]
        here = pl.ds(pl.multiple_of(base + low, 1024), size)
        one = beta_one * first[here] + (1.0 - beta_one) * g
        two = beta_two * second[here] + (1.0 - beta_two) * g * g
        there = pl.ds(low, size)
        new_first[there] = one
        new_second[there] = two
        one = one * (1.0 / (1.0 - beta_one**STEP))
        two = two * (1.0 / (1.0 - beta_two**STEP))
        old = params[here]
        new_params[there] = old - learn_rate * (
            one / (jnp.sqrt(two) + adam_eps) + decay_rate * old
        )

    whole = NPARAM // PIECE

    @pl.when(step < whole)
    def full():
        def part(i, carry):
            low = pl.multiple_of(i * 16384, 16384)
            update(step * PIECE, low, 16384)
            return carry

        lax.fori_loop(0, PIECE // 16384, part, 0)

    @pl.when(step == whole)
    def last():
        rest = NPARAM - whole * PIECE
        main = rest // 1024 * 1024
        for low in range(0, main, 16384):
            update(whole * PIECE, low, min(16384, main - low))
        update(whole * PIECE, main, rest - main)


def adamw(sizes, parts, arrays):
    pieces = -(-NPARAM // PIECE)
    piece = pl.BlockSpec((PIECE,), lambda i: (i,))
    vmem = pl.BlockSpec(memory_space=pltpu.VMEM)
    smem = pl.BlockSpec(memory_space=pltpu.SMEM)
    return pl.pallas_call(
        functools.partial(adamw_kernel, sizes),
        grid=(pieces,),
        out_shape=[arr(NPARAM)] * 3 + [arr(1)] * 3,
        in_specs=[vmem] * (len(parts) + len(arrays)),
        out_specs=[piece] * 3 + [smem] * 3,
        scratch_shapes=[pltpu.VMEM((LATE_ROWS + EARLY_ROWS, WIDE), F32), pltpu.SMEM((1,), F32)],
        compiler_params=pltpu.CompilerParams(vmem_limit_bytes=16 * 1024 * 1024),
        cost_estimate=pl.CostEstimate(flops=6 * 10**9, bytes_accessed=0, transcendentals=0),
        name="adamw",
    )(*parts, *arrays)


def arr(*shape):
    return jax.ShapeDtypeStruct(shape, F32)


def call(kernel, outs, scratch, *args, name=None, us=1.0, far=(), mib=16):
    vmem = pl.BlockSpec(memory_space=pltpu.VMEM)
    smem = pl.BlockSpec(memory_space=pltpu.SMEM)
    return pl.pallas_call(
        kernel,
        out_shape=list(outs),
        in_specs=[vmem] * len(args) + [pl.BlockSpec(memory_space=pl.ANY)] * len(far),
        out_specs=[smem if o.shape == (1,) else vmem for o in outs],
        scratch_shapes=list(scratch),
        compiler_params=pltpu.CompilerParams(vmem_limit_bytes=mib * 1024 * 1024),
        cost_estimate=pl.CostEstimate(
            flops=int(us * 1.15e9), bytes_accessed=0, transcendentals=0
        ),
        name=name,
    )(*args, *far)


SQUARE = arr(ROWS, WIDE)
SAVE = arr(ROWS, 3 * WIDE)
FORWARD = [
    pltpu.VMEM((2, ROWS, 2 * WIDE), BF16),
    pltpu.VMEM((2, ROWS, 2 * WIDE), BF16),
    pltpu.VMEM((2 * ROWS, 2 * WIDE), BF16),
]
BACKWARD = [
    pltpu.VMEM((2, ROWS, 2 * WIDE), BF16),
    pltpu.VMEM((2, ROWS, 2 * WIDE), BF16),
    pltpu.VMEM((2, ROWS, 2 * WIDE), BF16),
    pltpu.VMEM((2, ROWS, 2 * WIDE), BF16),
    pltpu.VMEM((2 * ROWS, 2 * WIDE), BF16),
    pltpu.VMEM((ROWS, WIDE), F32),
    pltpu.VMEM((2, WIDE, ROWS), F32),
    pltpu.VMEM((2, ROWS, 2 * ROWS), BF16),
    pltpu.VMEM((2, ROWS, 2 * ROWS), BF16),
    pltpu.VMEM((2, WIDE, ROWS), BF16),
    pltpu.VMEM((2, WIDE, ROWS), BF16),
    pltpu.VMEM((ROWS, WIDE), F32),
    pltpu.VMEM((2, ROWS, ROWS), F32),
    pltpu.VMEM((2, ROWS, ROWS), F32),
]
PARTS = [arr(ROWS_A, WIDE), arr(ROWS_B, WIDE), arr(ROWS_C, WIDE)]


def passed(parts, steps, sizes):
    slabs, rows = sizes
    moved = []
    for part, (ds, dm) in zip(parts, ((1, 0), (0, 1), (1, 1))):
        pairs = []
        for s in range(slabs):
            for m in range(rows):
                target = ((s + steps * ds) % slabs) * rows + (m + steps * dm) % rows
                pairs.append((s * rows + m, target))
        moved.append(lax.ppermute(part, ("slab", "mp"), pairs))
    return moved


SIDES = [arr(2 * WIN, 8, WIDE)] * 4


def beside(sides, sizes):
    slabs, rows = sizes
    low_d, high_d, low_h, high_h = sides
    up = [(i, i + 1) for i in range(slabs - 1)]
    down = [(i + 1, i) for i in range(slabs - 1)]
    before = lax.ppermute(high_d, "slab", up)
    after = lax.ppermute(low_d, "slab", down)

    def column(own, start):
        ends = [
            x.reshape(2, WIN, 8, WIDE)[:, start : start + 2].reshape(4, 8, WIDE)
            for x in (before, after)
        ]
        return jnp.concatenate([ends[0], own, ends[1]], 0)

    up = [(i, i + 1) for i in range(rows - 1)]
    down = [(i + 1, i) for i in range(rows - 1)]
    left = lax.ppermute(column(high_h, WIN - 2), "mp", up)
    right = lax.ppermute(column(low_h, 0), "mp", down)
    return before, after, left, right


REGION = [pltpu.VMEM((ROWS, ROWS), F32)]


def on_device(sizes, feats, labels, valid, params, moment_one, moment_two):
    slabs, rows = sizes
    count = slabs * rows

    def room(spans):
        sizes = [(span_of(groups)[1] + 8) * WIDE for groups in spans]
        return [
            [pltpu.VMEM((size,), F32) for size in sizes],
            pltpu.VMEM((2048, WIDE), F32),
            pltpu.SemaphoreType.DMA((len(spans),)),
        ]

    first_size = FIRST_SPANS[-1][1] * 384
    merge, lay0 = call(
        functools.partial(prep_kernel, FIRST_SPANS),
        [arr(MERGE_ROWS, WIDE), arr(1176, WIDE)],
        room(FIRST_SPANS),
        name="prep_first", us=2.0, far=(params[:first_size],),
    )
    lay1, lay2 = call(
        functools.partial(prep_kernel, LAYER_SPANS),
        [arr(1168, WIDE)] * 2,
        room(LAYER_SPANS),
        name="prep_layers", us=2.0, far=(params,),
    )
    conv0, conv1, head_w, weights0, weights1, vectors = call(
        prep_conv_kernel,
        [arr(2596, WIDE), arr(2640, WIDE), arr(WIDE, WIDE)]
        + [jax.ShapeDtypeStruct((27 * 256, 256), BF16)] * 2
        + [arr(8, WIDE)],
        room(CONV_SPANS),
        params[NPARAM // WIDE * WIDE :],
        name="prep_conv", us=4.0, far=(params,),
    )

    dense, tok0, save0, lse0, mixed0, mid0, hpre0, tok1, ahead, *parts = call(
        first_kernel,
        [arr(ROWS, MERGE), SQUARE, SAVE, SQUARE, SQUARE, SQUARE, arr(ROWS, HID), SQUARE, SQUARE]
        + PARTS,
        FORWARD,
        feats.reshape(PLANE, WIN, MERGE), merge, lay0,
        name="first", us=9.5,
    )
    parts = passed(parts, -1, sizes)
    window, save1, lse1, mixed1, out1, *parts = call(
        functools.partial(shifted_kernel, sizes),
        [SQUARE, SAVE, SQUARE, SQUARE, SQUARE] + PARTS,
        REGION + FORWARD,
        ahead, *parts, lay1,
        name="shifted", us=7.5,
    )
    parts = passed(parts, 1, sizes)
    mid1, hpre1, tok2, save2, lse2, mixed2, mid2, hpre2, lines, *sides = call(
        second_kernel,
        [SQUARE, arr(ROWS, HID), SQUARE, SAVE, SQUARE, SQUARE, SQUARE, arr(ROWS, HID)]
        + [arr(PLANE, 8, WIDE)] + SIDES,
        [pltpu.VMEM((ROWS, WIDE), F32)] + FORWARD,
        tok1, out1, *parts, lay1, lay2,
        name="second", us=9.5,
    )
    sides = beside(sides, sizes)
    grown, pre, tok3, sums, *tok_sides = call(
        functools.partial(conv_kernel, sizes),
        [arr(11, 12, 8, WIDE), arr(9, 10, 8, WIDE), arr(PLANE, 8, WIDE), arr(8, WIDE)] + SIDES,
        [
            pltpu.VMEM((9, 10, 8, WIDE), F32),
            pltpu.VMEM((880, 2304), BF16),
            pltpu.VMEM((576, 2304), BF16),
            pltpu.VMEM((PLANE, 8, WIDE), F32),
        ],
        lines, *sides, labels, valid, weights0, weights1, vectors,
        name="conv", us=8.0, mib=20,
    )
    tok_sides = beside(tok_sides, sizes)
    side_act, side_grown = call(
        functools.partial(sides_back_kernel, sizes),
        [jax.ShapeDtypeStruct((640, 2304), BF16)] * 2,
        [pltpu.VMEM((10, 10, 8, WIDE), F32)],
        grown, pre,
        name="sides_back", us=2.0,
    )
    weights0, weights1 = call(
        weights_back_kernel,
        [jax.ShapeDtypeStruct((256, 27 * 256), BF16)] * 2,
        [],
        conv0, conv1,
        name="weights_back", us=1.5,
    )
    sums = exchanged_sum(sums, count)
    voxels = WIN * slabs * WIN * rows * WIN
    tok3, slope, tail, d_head, d_rows = call(
        functools.partial(head_kernel, voxels),
        [arr(11, 12, 8, WIDE), arr(11, 12, 8, WIDE), arr(8, WIDE), arr(WIDE, WIDE), arr(8, WIDE)],
        [],
        tok3, *tok_sides, sums, vectors, head_w,
        name="head", us=3.5,
    )
    tail = exchanged_sum(tail, count)
    late_rows = block_rows(LATE_ROWS, count) * count
    early_rows = block_rows(EARLY_ROWS, count) * count
    seam_rows = LATE_ROWS - 3 * CUTS[3]
    d_own, keep, send, carry3, seam = call(
        functools.partial(conv_back_kernel, sizes),
        [arr(PLANE, 8, WIDE)] + [arr(early_rows // 2, WIDE)] * 2
        + [arr(24, WIDE), arr(seam_rows, WIDE)],
        [
            pltpu.VMEM((5236, WIDE), F32),
            pltpu.VMEM((11, 12, 8, WIDE), F32),
            pltpu.VMEM((10, 10, 8, WIDE), F32),
            pltpu.VMEM((880, 2304), BF16),
            pltpu.VMEM((576, 2304), BF16),
            pltpu.VMEM((seam_rows + early_rows, WIDE), F32),
        ],
        tok3, slope, tail, pre, side_act, side_grown, weights0, weights1, d_rows, d_head,
        name="conv_back", us=14.0, mib=28,
    )
    early = summing(keep, send, count)
    next(early)
    d_mid2, grads2 = call(
        back_mlp_kernel,
        [SQUARE, arr(1168, WIDE)],
        [pltpu.VMEM((ROWS, WIDE), F32)],
        d_own, lay2, mid2, hpre2,
        name="back_mlp", us=3.0,
    )
    step = early.send(d_mid2)
    d_mid, grads1, flat2, carry2, *parts = call(
        back_two_kernel,
        [SQUARE, arr(1168, WIDE), arr(3 * (CUTS[3] - CUTS[2]), WIDE), arr(32, WIDE)] + PARTS,
        [pltpu.VMEM((1184, WIDE), F32)] + BACKWARD,
        d_mid2, grads2, carry3, lay1, lay2, tok2, save2, lse2, mixed2, mid1, hpre1,
        name="back_two", us=9.0,
    )
    parts = passed(parts, -1, sizes)
    step = early.send(d_mid)
    d_window, flat1, carry1, *parts = call(
        functools.partial(back_shifted_kernel, sizes),
        [SQUARE, arr(3 * (CUTS[2] - CUTS[1]), WIDE), arr(16, WIDE)] + PARTS,
        REGION + [pltpu.VMEM((1200, WIDE), F32), pltpu.VMEM((ROWS, WIDE), F32)] + BACKWARD,
        d_mid, *parts, lay1, window, save1, lse1, mixed1, grads1, carry2,
        name="back_shifted", us=10.5, far=(step,),
    )
    early.send(d_window)
    parts = passed(parts, 1, sizes)
    next(early)
    step = next(early)
    late = call(
        functools.partial(back_first_kernel, sizes),
        [arr(late_rows // 2, WIDE)] * 2,
        [
            pltpu.VMEM((late_rows, WIDE), F32),
            pltpu.VMEM((1572, WIDE), F32),
            pltpu.VMEM((ROWS, WIDE), F32),
        ]
        + BACKWARD,
        d_mid, d_window, *parts, tok1, lay0, lay1, merge, dense, tok0, save0, lse0, mixed0, mid0,
        hpre0, carry1, flat1, flat2, seam,
        name="back_first", us=13.5, far=(step,),
    )
    step = early.send(late[0])
    keep, send = later(list(late), step)
    late_sum = finished(summing(keep, send, count))
    early = finished(early)
    new_params, new_first, new_second, loss, valid_count, norm = adamw(
        sizes, (*late_sum, *early, tail, sums), (params, moment_one, moment_two)
    )
    return (
        loss.reshape(()), valid_count.reshape(()), norm.reshape(()),
        new_params, new_first, new_second,
    )


def solution(mesh):
    placed = (
        P("slab", "mp", None, None),
        P("slab", "mp", None),
        P("slab", "mp", None),
        P(),
        P(),
        P(),
    )
    sizes = (mesh.shape["slab"], mesh.shape["mp"])
    return jax.shard_map(
        functools.partial(on_device, sizes),
        mesh=mesh,
        in_specs=placed,
        out_specs=(P(), P(), P(), P(), P(), P()),
        check_vma=False,
    )
```

```python
import functools
import math

import jax
import jax.numpy as jnp
from jax import lax
from jax.experimental import pallas as pl
from jax.experimental.pallas import tpu as pltpu
from jax.sharding import PartitionSpec as P

EMB = 96
HEADS = 6
HDIM = 16
HID = 384
MERGE = 384
CLASSES = 14
WIN = 7
SHIFT = 3
LAYERS = 3
STEP = 10

F32 = jnp.float32
BF16 = jnp.bfloat16
eps_norm = 1e-05
beta_one = 0.9
beta_two = 0.999
adam_eps = 1e-08
learn_rate = 0.05
decay_rate = 0.05
clip_norm = 0.01
LOG2E = 1.4426950408889634

VOX = WIN * WIN * WIN
ROWS = 384
BLK = 128
WIDE = 128
PLANE = WIN * WIN
FAR = WIN - SHIFT
ROWS_A = SHIFT * FAR * WIN
ROWS_B = FAR * SHIFT * WIN
ROWS_C = SHIFT * SHIFT * WIN

MERGE_ROWS = 392
LAYER_ROWS = 1165
TAP_ROWS = 27 * EMB
GROUPS = 2280
NPARAM = 872558
HEAD_ROW = 6806
HEAD_ROWS = 11
HEAD_LANE = 32
LATE_ROWS = 3072
EARLY_ROWS = 3840
EARLY_BLOCKS = 8
LAYER_BASE = (98, 389, 680)
CONV_BASE = (971, 1620)
CUTS = (0, 392, 688, 976, 2280)

R_QKV, R_QKVB, R_PROJ, R_PROJB = 4, 292, 295, 391
R_HID, R_HIDB, R_OUT, R_OUTB = 392, 776, 780, 1164


def iota(shape, dim):
    return lax.broadcasted_iota(jnp.int32, shape, dim)


def split(x):
    hi = x.astype(BF16)
    return hi, (x - hi.astype(F32)).astype(BF16)


def pair(x):
    return jnp.concatenate(split(x), 1)


def fold(y):
    half = y.shape[1] // 2
    return y[:, :half] + y[:, half:]


def fold_rows(y):
    half = y.shape[0] // 2
    return y[:half] + y[half:]


def dot(a, b):
    return jnp.dot(a, b, preferred_element_type=F32)


def dot_nt(a, b):
    return lax.dot_general(a, b, (((1,), (1,)), ((), ())), preferred_element_type=F32)


def weight_nn(w):
    top = pair(w)
    return jnp.concatenate([top, top], 0)


def weight_nt(w):
    hi, lo = split(w)
    return jnp.concatenate(
        [jnp.concatenate([hi, hi], 1), jnp.concatenate([lo, lo], 1)], 0
    )


def mm(x, w):
    return fold(dot(pair(x), weight_nn(w)))


def mm_nt(x, w):
    return fold(dot_nt(pair(x), weight_nt(w)))


def rows_t(x):
    return jnp.concatenate(split(x.T), 0)


def mm_tn(xt, y):
    return fold_rows(fold(dot(xt, pair(y))))


def deep(w):
    return jnp.concatenate([w, jnp.zeros((WIDE - EMB, w.shape[1]), F32)], 0)


def roll(x, shift, axis):
    return pltpu.roll(x, shift, axis)


def four_to_three(y):
    lane = iota(y[0].shape, 1)
    a = jnp.where(lane < 96, y[0], roll(y[1], 96, 1))
    b = jnp.where(lane < 64, roll(y[1], 96, 1), roll(y[2], 64, 1))
    c = jnp.where(lane < 32, roll(y[2], 64, 1), roll(y[3], 32, 1))
    return a, b, c


def three_to_four(x):
    lane = iota(x[0].shape, 1)
    live = lane < EMB
    a = x[0]
    b = jnp.where(lane < 32, roll(x[0], 32, 1), roll(x[1], 32, 1))
    c = jnp.where(lane < 64, roll(x[1], 64, 1), roll(x[2], 64, 1))
    d = roll(x[2], 96, 1)
    return tuple(jnp.where(live, v, 0.0) for v in (a, b, c, d))


def hidden_rows(ref, start, count):
    return jnp.concatenate(
        four_to_three([ref[pl.ds(start + c, count, stride=4), :] for c in range(4)]), 1
    )


def put_hidden_rows(ref, start, count, x):
    parts = three_to_four([x[:, i * WIDE : (i + 1) * WIDE] for i in range(3)])
    for c in range(4):
        ref[pl.ds(start + c, count, stride=4), :] = parts[c]


def flatten(ref, start, groups, out):
    parts = four_to_three([ref[pl.ds(start + c, groups, stride=4), :] for c in range(4)])
    for c in range(3):
        out[pl.ds(c, groups, stride=3), :] = parts[c]


def norm_stats(x):
    live = iota(x.shape, 1) < EMB
    mean = jnp.sum(x, 1, keepdims=True) * (1.0 / EMB)
    centred = jnp.where(live, x - mean, 0.0)
    var = jnp.sum(centred * centred, 1, keepdims=True) * (1.0 / EMB)
    inv = lax.rsqrt(var + eps_norm)
    return centred * inv, inv


def norm(x, gain, bias):
    hat, _ = norm_stats(x)
    return hat * gain + bias


def norm_back(hat, inv, gain, grad):
    up = grad * gain
    one = jnp.sum(up, 1, keepdims=True) * (1.0 / EMB)
    two = jnp.sum(up * hat, 1, keepdims=True) * (1.0 / EMB)
    live = iota(hat.shape, 1) < EMB
    return jnp.where(live, inv * (up - one - hat * two), 0.0)


def colsum(x):
    return jnp.sum(x, 0, keepdims=True)


def gelu(x):
    return 0.5 * x * (1.0 + lax.erf(x * (0.5**0.5)))


def gelu_both(x):
    cdf = 0.5 * (1.0 + lax.erf(x * (0.5**0.5)))
    slope = cdf + x * (jnp.exp(x * x * -0.5) * 0.3989422804014327)
    return x * cdf, slope


def head_groups(x):
    lane = iota(x.shape, 1)
    swapped = roll(x, 64, 1)
    return jnp.where(lane < 64, x, swapped), jnp.where(lane < 64, swapped, x)


def as_left(x):
    both = []
    low = iota(x.shape, 1) < 64
    for part in head_groups(x):
        hi = part.astype(BF16).astype(F32)
        one = jnp.where(low, hi, part - hi).astype(BF16)
        both.append(jnp.concatenate([one, one], 1))
    return both


def as_right(x):
    return [pair(part) for part in head_groups(x)]


def head_mask(h, width):
    lane = iota((1, width), 1)
    lane = jnp.bitwise_and(lane, 63)
    low = jnp.bitwise_and(h, 3) * HDIM
    return jnp.where((lane >= low) & (lane < low + HDIM), 1.0, 0.0)


def own_lanes(h):
    lane = iota((1, WIDE), 1)
    return jnp.where((lane >= h * HDIM) & (lane < (h + 1) * HDIM), 1.0, 0.0)


def both_heads(right, heads, out):
    for k, h in enumerate(heads):
        out[k * ROWS : (k + 1) * ROWS, :] = right * head_mask(h, 2 * WIDE).astype(BF16)


def score_tiles(s, rows, region):
    tiles = [s[:, i * WIDE : (i + 1) * WIDE] for i in range(3)]
    if region is not None:
        return [t + region[rows, i * WIDE : (i + 1) * WIDE] for i, t in enumerate(tiles)]
    pad = jnp.where(iota((1, WIDE), 1) < VOX - 2 * WIDE, 0.0, -1e30)
    return tiles[:2] + [tiles[2] + pad]


def put_split(ref, rows, i, x):
    hi, lo = split(x)
    ref[rows, i * WIDE : (i + 1) * WIDE] = hi
    ref[rows, ROWS + i * WIDE : ROWS + (i + 1) * WIDE] = lo


def attention(normed, layer, save, lse, mixed, sc, region=None):
    left, right, values, keys = sc
    x = pair(normed)
    qkv = []
    for i in range(3):
        w = deep(layer[pl.ds(R_QKV + i, EMB, stride=3), :])
        y = fold(dot(x, weight_nn(w))) + layer[R_QKVB + i : R_QKVB + i + 1, :]
        if i == 0:
            y = y * (HDIM**-0.5 * LOG2E)
        save[:, i * WIDE : (i + 1) * WIDE] = y
        qkv.append(y)
    for g, part in enumerate(as_left(qkv[0])):
        left[g] = part
    for g, part in enumerate(as_right(qkv[1])):
        right[g] = part
    v = pair(jnp.where(iota((ROWS, WIDE), 1) == EMB, 1.0, qkv[2]))
    values[0:ROWS, :] = v
    values[ROWS : 2 * ROWS, :] = v
    mixed[...] = jnp.zeros_like(mixed)
    lse[...] = jnp.zeros_like(lse)

    def per_pair(pair_of, carry):
        heads = [2 * pair_of, 2 * pair_of + 1]
        lanes = [own_lanes(h) for h in heads]
        spots = [jnp.where(iota((1, WIDE), 1) == h, 1.0, 0.0) for h in heads]
        g = lax.div(pair_of, 2)
        both_heads(right[g], heads, keys)
        for b in range(ROWS // BLK):
            rows = slice(b * BLK, (b + 1) * BLK)
            out = level = 0.0
            s = dot_nt(left[g, rows, :], keys[...])
            for k in range(2):
                tiles = score_tiles(s[:, k * ROWS : (k + 1) * ROWS], rows, region)
                top = jnp.maximum(jnp.maximum(tiles[0], tiles[1]), tiles[2])
                top = jnp.max(top, 1, keepdims=True)
                parts = [split(jnp.exp2(t - top)) for t in tiles]
                e = jnp.concatenate([p[0] for p in parts] + [p[1] for p in parts], 1)
                o = fold(dot(e, values[...]))
                total = o[:, EMB : EMB + 1]
                out = out + o * (lanes[k] / total)
                level = level + (top + jnp.log(total) * LOG2E) * spots[k]
            mixed[rows, :] += out
            lse[rows, :] += level
        return carry

    lax.fori_loop(0, HEADS // 2, per_pair, 0)
    proj = deep(layer[R_PROJ : R_PROJ + EMB, :])
    return mm(mixed[...], proj) + layer[R_PROJB : R_PROJB + 1, :]


def attention_back(grad, normed, layer, save, lse, mixed, sc, grads, at, region=None):
    left, right, gleft, vright, keys, dq, dkv_t, weights, slopes = sc[:9]
    q_t, do_t, dmix, s, dp, two_keys, two_values = sc[9:]
    proj = deep(layer[R_PROJ : R_PROJ + EMB, :])
    grads[at + R_PROJ : at + R_PROJ + EMB, :] = mm_tn(rows_t(mixed[...]), grad)[:EMB]
    grads[at + R_PROJB : at + R_PROJB + 1, :] = colsum(grad)
    d_mixed = mm_nt(grad, proj)
    dmix[...] = d_mixed * mixed[...]
    q, k, v = (save[:, i * WIDE : (i + 1) * WIDE] for i in range(3))
    for g, part in enumerate(as_left(q)):
        left[g] = part
    for g, part in enumerate(as_right(k)):
        right[g] = part
    for g, part in enumerate(as_left(d_mixed)):
        gleft[g] = part
    for g, part in enumerate(as_right(v)):
        vright[g] = part
    kk = pair(k)
    keys[0:ROWS, :] = kk
    keys[ROWS : 2 * ROWS, :] = kk
    for ref, x in ((q_t, q), (do_t, d_mixed)):
        hi, lo = split(x.T)
        ref[0] = hi
        ref[1] = lo
    dq[...] = jnp.zeros_like(dq)
    dkv_t[...] = jnp.zeros_like(dkv_t)

    def per_pair(pair_of, carry):
        g = lax.div(pair_of, 2)
        heads = [2 * pair_of, 2 * pair_of + 1]
        both_heads(right[g], heads, two_keys)
        both_heads(vright[g], heads, two_values)
        s[...] = dot_nt(left[g], two_keys[...])
        dp[...] = dot_nt(gleft[g], two_values[...])
        for k in range(2):
            h = 2 * pair_of + k
            lanes = own_lanes(h)
            at_h = jnp.where(iota((1, WIDE), 1) == h, 1.0, 0.0)
            for b in range(ROWS // BLK):
                rows = slice(b * BLK, (b + 1) * BLK)
                level = jnp.sum(lse[rows, :] * at_h, 1, keepdims=True)
                delta = jnp.sum(dmix[rows, :] * lanes, 1, keepdims=True)
                at_k = k * ROWS
                tiles = score_tiles(s[rows, at_k : at_k + ROWS], rows, region)
                for i, t in enumerate(tiles):
                    p = jnp.exp2(t - level)
                    put_split(weights.at[k], rows, i, p)
                    low = at_k + i * WIDE
                    p = p * (dp[rows, low : low + WIDE] - delta)
                    put_split(slopes.at[k], rows, i, p)
        total = 0.0
        for k in range(2):
            total = total + fold(dot(slopes[k], keys[...])) * own_lanes(2 * pair_of + k)
        dq[...] += total
        for k in range(2):
            here = pl.ds(pl.multiple_of((2 * pair_of + k) * HDIM, HDIM), HDIM)
            for i, (t, m) in enumerate(((q_t, slopes), (do_t, weights))):
                lhs = jnp.concatenate([t[0, here, :], t[1, here, :]], 0)
                dkv_t[i, here, :] = fold_rows(fold(dot(lhs, m[k])))
        return carry

    lax.fori_loop(0, HEADS // 2, per_pair, 0)
    d_q = dq[...] * HDIM**-0.5
    d_k = dkv_t[0].T * (1.0 / LOG2E)
    d_v = dkv_t[1].T
    x_t = rows_t(normed)
    d_normed = None
    for i, d in enumerate((d_q, d_k, d_v)):
        grads[pl.ds(at + R_QKV + i, EMB, stride=3), :] = mm_tn(x_t, d)[:EMB]
        grads[at + R_QKVB + i : at + R_QKVB + i + 1, :] = colsum(d)
        part = mm_nt(d, deep(layer[pl.ds(R_QKV + i, EMB, stride=3), :]))
        d_normed = part if d_normed is None else d_normed + part
    return d_normed


def mlp(middle, layer, hpre):
    normed = norm(middle, layer[2:3, :], layer[3:4, :])
    w = deep(hidden_rows(layer, R_HID, EMB))
    pre = mm(normed, w) + hidden_rows(layer, R_HIDB, 1)
    hpre[...] = pre
    out = mm(gelu(pre), layer[R_OUT : R_OUT + HID, :])
    return middle + out + layer[R_OUTB : R_OUTB + 1, :]


def mlp_back(grad, middle, hpre, layer, grads, at):
    hat, inv = norm_stats(middle)
    normed = hat * layer[2:3, :] + layer[3:4, :]
    act, slope = gelu_both(hpre[...])
    grads[at + R_OUTB : at + R_OUTB + 1, :] = colsum(grad)
    grads[at + R_OUT : at + R_OUT + HID, :] = mm_tn(rows_t(grad), act).T
    d_pre = mm_nt(grad, layer[R_OUT : R_OUT + HID, :]) * slope
    put_hidden_rows(grads, at + R_HIDB, 1, colsum(d_pre))
    put_hidden_rows(grads, at + R_HID, EMB, mm_tn(rows_t(normed), d_pre)[:EMB])
    d_normed = mm_nt(d_pre, deep(hidden_rows(layer, R_HID, EMB)))
    grads[at + 2 : at + 3, :] = colsum(d_normed * hat)
    grads[at + 3 : at + 4, :] = colsum(d_normed)
    return grad + norm_back(hat, inv, layer[2:3, :], d_normed)


def pre_norm_back(grad, tokens, layer, grads, at):
    hat, inv = norm_stats(tokens)
    grads[at : at + 1, :] = colsum(grad * hat)
    grads[at + 1 : at + 2, :] = colsum(grad)
    return norm_back(hat, inv, layer[0:1, :], grad)


def region_of(rows, sizes):
    d = lax.shift_right_logical(rows * 1338, 16)
    line = lax.shift_right_logical(rows * 9363, 16)
    places = (d, line - d * WIN, rows - line * WIN)
    starts = (lax.axis_index("slab") * WIN, lax.axis_index("mp") * WIN, 0)
    total = None
    for place, start, blocks in zip(places, starts, sizes + (1,)):
        turned = jnp.where(place < SHIFT, place + FAR, place - SHIFT) + start
        length = WIN * blocks
        part = jnp.where(turned < length - WIN, 0, jnp.where(turned < length - SHIFT, 1, 2))
        total = part if total is None else total * 3 + part
    return total


def put_region(region, sizes):
    rows = region_of(iota((ROWS, WIDE), 0), sizes)[:, 0:1]
    lanes = region_of(iota((8, ROWS), 1), sizes)[0:1, :]
    apart = jnp.where(rows == lanes, 0.0, -100.0 * LOG2E)
    region[...] = jnp.where(iota((ROWS, ROWS), 1) < VOX, apart, -1e30)


def send_parts(ref, a, b, c):
    far = FAR * WIN
    near = SHIFT * WIN
    for d in range(SHIFT):
        base = d * PLANE
        c[d * near : (d + 1) * near, :] = ref[base : base + near, :]
        a[d * far : (d + 1) * far, :] = ref[base + near : base + PLANE, :]
    for d in range(FAR):
        base = (d + SHIFT) * PLANE
        b[d * near : (d + 1) * near, :] = ref[base : base + near, :]


def take_parts(own, a, b, c, out):
    far = FAR * WIN
    near = SHIFT * WIN
    for d in range(WIN):
        base = d * PLANE
        if d < SHIFT:
            out[base : base + near, :] = c[d * near : (d + 1) * near, :]
            out[base + near : base + PLANE, :] = a[d * far : (d + 1) * far, :]
        else:
            e = d - SHIFT
            out[base : base + near, :] = b[e * near : (e + 1) * near, :]
            out[base + near : base + PLANE, :] = own[base + near : base + PLANE, :]
    out[VOX:, :] = jnp.zeros((ROWS - VOX, WIDE), F32)


def span_of(groups):
    low, high = groups
    first = 3 * low // 8 * 8
    last = -(-3 * high // 8) * 8
    return first, min(last, NPARAM // WIDE // 8 * 8) - first


def copied(params, groups, flat, sem):
    first, rows = span_of(groups)
    size = rows * WIDE
    return pltpu.make_async_copy(
        params.at[pl.ds(first * WIDE, size)], flat.at[pl.ds(0, size)], sem
    )


def relay(groups, flat, out, square, last=None):
    low, high = groups
    first, rows = span_of(groups)
    square[0:rows, :] = flat[0 : rows * WIDE].reshape(rows, WIDE)
    if last is not None:
        square[rows : rows + 24, :] = jnp.zeros((24, WIDE), F32)
        square[rows : rows + 1, 0 : last.shape[0]] = last[...].reshape(1, last.shape[0])
    skip = 3 * low - first
    n = high - low
    parts = three_to_four([square[pl.ds(skip + c, n, stride=3), :] for c in range(3)])
    for c in range(4):
        out[pl.ds(c, n, stride=4), :] = parts[c]


FIRST_SPANS = ((0, 98), (98, 392))
LAYER_SPANS = ((389, 681), (680, 972))
CONV_SPANS = ((971, 1620), (1620, GROUPS))


def prep_kernel(spans, params, *refs, last=None):
    outs, (flats, square, sems) = refs[: len(spans)], refs[-3:]
    for i, groups in enumerate(spans):
        copied(params, groups, flats[i], sems.at[i]).start()
    for i, groups in enumerate(spans):
        copied(params, groups, flats[i], sems.at[i]).wait()
        relay(groups, flats[i], outs[i], square, last if i == len(spans) - 1 else None)


def head_picks():
    width = HEAD_ROWS * WIDE
    place = iota((WIDE, width), 1) - HEAD_LANE
    row = iota((WIDE, width), 0)
    here = (place >= row * CLASSES) & (place < (row + 1) * CLASSES) & (row <= EMB)
    place = iota((width, WIDE), 0) - HEAD_LANE
    col = iota((width, WIDE), 1)
    row = lax.shift_right_logical(place * 4682, 16)
    there = (place - row * CLASSES == col) & (place >= 0)
    return jnp.where(here, 1.0, 0.0), jnp.where(there, 1.0, 0.0).astype(BF16)


def prep_conv_kernel(
    last, params, conv0, conv1, head, weights0, weights1, vectors, *scratch
):
    prep_kernel(CONV_SPANS, params, conv0, conv1, *scratch, last=last)
    tap_weights(conv0, 3, weights0)
    tap_weights(conv1, 0, weights1)
    vectors[0:1, :] = conv0[3 + TAP_ROWS : 4 + TAP_ROWS, :]
    vectors[1:4, :] = conv1[TAP_ROWS : TAP_ROWS + 3, :]
    vectors[4:8, :] = jnp.zeros((4, WIDE), F32)
    square = scratch[1]
    first, _ = span_of(CONV_SPANS[1])
    row = jnp.concatenate(
        [square[HEAD_ROW + i - first : HEAD_ROW + i - first + 1, :] for i in range(HEAD_ROWS)], 1
    )
    here, there = head_picks()
    hi, lo = split(here * row)
    head[...] = dot(hi, there) + dot(lo, there)


def head_rows(d_head, out, at):
    here, there = head_picks()
    hi, lo = split(d_head)
    spread = (dot_nt(hi, there) + dot_nt(lo, there)) * here
    row = colsum(spread)
    for i in range(HEAD_ROWS):
        out[at + i : at + i + 1, :] += row[:, i * WIDE : (i + 1) * WIDE]


class Rows:
    def __init__(self, ref, at):
        self.ref, self.at = ref, at

    def __getitem__(self, key):
        rows, lanes = key
        if isinstance(rows, slice):
            rows = slice(rows.start + self.at, rows.stop + self.at)
        else:
            rows = pl.ds(rows.start + self.at, rows.size, stride=rows.stride)
        return self.ref[rows, lanes]


def merged_norm(x):
    mean = jnp.sum(x, 1, keepdims=True) * (1.0 / MERGE)
    centred = x - mean
    var = jnp.sum(centred * centred, 1, keepdims=True) * (1.0 / MERGE)
    return centred * lax.rsqrt(var + eps_norm)


def first_kernel(
    feats, merge, lay0,
    dense, tok0, save, lse, mixed, middle, hpre, tok1, ahead, pa, pb, pc,
    *sc,
):
    dense[VOX:, :] = jnp.zeros((ROWS - VOX, MERGE), F32)
    for line in range(PLANE):
        dense[line * WIN : (line + 1) * WIN, :] = feats[line]
    hat = merged_norm(dense[...])
    normed = hat * hidden_rows(merge, 0, 1) + hidden_rows(merge, 4, 1)
    tokens = mm(normed, merge[8 : 8 + MERGE, :])
    tok0[...] = tokens
    layer = Rows(lay0, 0)
    normed = norm(tokens, layer[0:1, :], layer[1:2, :])
    attended = attention(normed, layer, save, lse, mixed, sc)
    mid = tokens + attended
    middle[...] = mid
    tokens = mlp(mid, layer, hpre)
    tok1[...] = tokens
    ahead[...] = norm(tokens, layer[1165:1166, :], layer[1166:1167, :])
    send_parts(ahead, pa, pb, pc)


def shifted_kernel(
    sizes,
    own, pa, pb, pc, lay1,
    window, save, lse, mixed, out, qa, qb, qc,
    region, *sc,
):
    put_region(region, sizes)
    take_parts(own, pa, pb, pc, window)
    out[...] = attention(
        window[...], Rows(lay1, 1), save, lse, mixed, sc, region
    )
    send_parts(out, qa, qb, qc)


def to_lines(ref, out):
    for line in range(PLANE):
        out[line, 0:WIN, :] = ref[line * WIN : (line + 1) * WIN, :]
        out[line, WIN:8, :] = jnp.zeros((8 - WIN, WIDE), F32)


def from_lines(ref, out):
    out[VOX:, :] = jnp.zeros((ROWS - VOX, WIDE), F32)
    for line in range(PLANE):
        out[line * WIN : (line + 1) * WIN, :] = ref[line, 0:WIN, :]


def send_sides(lines, low_d, high_d, low_h, high_h):
    low_d[...] = lines[0 : 2 * WIN]
    high_d[...] = lines[(WIN - 2) * WIN :]
    for d in range(WIN):
        low_h[2 * d : 2 * d + 2] = lines[d * WIN : d * WIN + 2]
        high_h[2 * d : 2 * d + 2] = lines[d * WIN + WIN - 2 : (d + 1) * WIN]


def second_kernel(
    tok1, own, qa, qb, qc, lay1, lay2, _,
    mid1, hpre1, tok2, save, lse, mixed, mid2, hpre2, lines,
    s0, s1, s2, s3,
    attended, *sc,
):
    take_parts(own, qa, qb, qc, attended)
    mid = tok1[...] + attended[...]
    mid1[...] = mid
    tokens = mlp(mid, Rows(lay1, 1), hpre1)
    tok2[...] = tokens
    layer = Rows(lay2, 2)
    normed = norm(tokens, layer[0:1, :], layer[1:2, :])
    mid = tokens + attention(normed, layer, save, lse, mixed, sc)
    mid2[...] = mid
    attended[...] = mlp(mid, layer, hpre2)
    to_lines(attended, lines)
    send_sides(lines, s0, s1, s2, s3)


def grown_lines(own, low_d, high_d, low_h, high_h, out):
    out[...] = jnp.zeros_like(out)
    for d in range(WIN):
        out[d + 2, 2 : 2 + WIN] = own[d * WIN : (d + 1) * WIN]
    for d in range(2):
        out[d, 2 : 2 + WIN] = low_d[d * WIN : (d + 1) * WIN]
        out[d + 9, 2 : 2 + WIN] = high_d[d * WIN : (d + 1) * WIN]
    for d in range(11):
        out[d, 0:2] = low_h[2 * d : 2 * d + 2]
        out[d, 9:11] = high_h[2 * d : 2 * d + 2]


def put_marks(labels, valid, out):
    across = iota((8, WIN), 1) == iota((8, WIN), 0)
    classes = iota((8, WIDE), 1) - EMB
    for d in range(WIN):
        code = jnp.where(valid[d] == 1, labels[d], -1 - EMB - WIDE)
        code = code.astype(F32)
        for h in range(WIN):
            line = jnp.where(across, code[h : h + 1, :], 0.0)
            column = jnp.sum(line, 1, keepdims=True)
            mark = jnp.where(column == classes.astype(F32), 1.0, 0.0)
            out[d * WIN + h] = jnp.where(iota((8, WIDE), 0) < WIN, mark, 0.0)


def taps(source, first_plane, planes, first_line, lines, out):
    def per_plane(d, carry):
        for c in range(3):
            for b in range(3):
                x = source[d + first_plane, first_line + b : first_line + b + lines]
                if c != 1:
                    x = roll(x, 1 if c == 0 else 7, 1)
                x = pair(x.reshape(lines * 8, WIDE))
                at = pl.multiple_of(d * (lines * 8), lines * 8)
                t = b * 3 + c
                out[pl.ds(at, lines * 8), t * 256 : (t + 1) * 256] = x
        return carry

    lax.fori_loop(0, planes, per_plane, 0)


def tap_weights(ref, at, out):
    def per_tap(i, carry):
        w = deep(ref[pl.ds(i * EMB + at, EMB), :])
        out[pl.ds(pl.multiple_of(i * 256, 256), 256), :] = weight_nn(w)
        return carry

    lax.fori_loop(0, 27, per_tap, 0)


def tap_weights_back(ref, at, out):
    for i in range(27):
        w = deep(ref[(26 - i) * EMB + at : (27 - i) * EMB + at, :])
        out[:, i * 256 : (i + 1) * 256] = weight_nt(w)


def conv(side, weights, planes, pitch, at_once, put, back=False):
    rows = at_once * pitch
    for start in range(0, planes, at_once):
        total = None
        for a in range(3):
            low = (start + a) * pitch
            x = side[low : low + rows, :]
            if back:
                part = dot_nt(x, weights[:, a * 2304 : (a + 1) * 2304])
            else:
                part = dot(x, weights[a * 2304 : (a + 1) * 2304, :])
            total = part if total is None else total + part
        put(start, fold(total))


def conv_weight_grad(side, grad_rows, pitch, out, at):
    rows = 512
    g = jnp.concatenate([grad_rows, jnp.zeros((rows - grad_rows.shape[0], WIDE), F32)], 0)
    left = jnp.concatenate(split(g.T[:EMB]), 0)
    for a in range(3):
        for bc in range(9):
            y = dot(left, side[a * pitch : a * pitch + rows, bc * 256 : (bc + 1) * 256])
            y = deep(fold_rows(fold(y))).T
            t = a * 9 + bc
            out[at + t * EMB : at + (t + 1) * EMB, :] = y[:EMB]


def volume_mask(sizes, planes, lines, reach, real_lines):
    slab, row = lax.axis_index("slab"), lax.axis_index("mp")
    ends = (slab == 0, slab == sizes[0] - 1, row == 0, row == sizes[1] - 1)
    shape = (planes, lines, 8, WIDE)
    d, h, w = iota(shape, 0), iota(shape, 1), iota(shape, 2)
    low_d = jnp.where(ends[0], reach, 0)
    high_d = jnp.where(ends[1], planes - reach, planes)
    low_h = jnp.where(ends[2], reach, 0)
    high_h = jnp.where(ends[3], real_lines - reach, real_lines)
    inside = (d >= low_d) & (d < high_d) & (h >= low_h) & (h < high_h) & (w < WIN)
    return jnp.where(inside, 1.0, 0.0)


def conv_kernel(
    sizes,
    own, s0, s1, s2, s3, labels, valid, weights0, weights1, vectors,
    grown, pre, tok, stats, t0, t1, t2, t3,
    act, side, side_own, marks,
):
    grown_lines(own, s0, s1, s2, s3, grown)
    put_marks(labels, valid, marks)
    taps(grown, 0, 11, 0, 10, side)
    bias0 = vectors[0:1, :]
    inside = volume_mask(sizes, 9, 10, 1, 9)


    def put(start, y):
        z = (y + bias0).reshape(3, 10, 8, WIDE)
        pre[start : start + 3] = z
        act[start : start + 3] = gelu(z) * inside[start : start + 3]

    conv(side, weights0, 9, 80, 3, put)
    taps(act, 0, 9, 0, 8, side_own)
    bias1 = vectors[1:2, :]
    sums = []

    def put_own(start, y):
        y = (y + bias1).reshape(WIN, 8, 8, WIDE)[:, 0:WIN]
        y = y + own[...].reshape(WIN, WIN, 8, WIDE)
        y = jnp.where(iota(y.shape, 2) < WIN, y, 0.0).reshape(PLANE, 8, WIDE)
        tok[...] = y + marks[...]
        send_sides(tok, t0, t1, t2, t3)
        flat = y.reshape(PLANE * 8, WIDE)
        sums.append(colsum(flat))
        sums.append(colsum(flat * flat))

    conv(side_own, weights1, WIN, 64, WIN, put_own)
    count = jnp.sum(marks[...].reshape(PLANE * 8, WIDE))
    row = iota((8, WIDE), 0)
    stats[...] = (
        jnp.where(row == 0, sums[0], 0.0)
        + jnp.where(row == 1, sums[1], 0.0)
        + jnp.where(row == 2, count, 0.0)
    )


def head_kernel(
    voxels,
    own, s0, s1, s2, s3, sums, vectors, head_w,
    grown, slope_out, stats, d_head, d_rows,
):
    grown_lines(own, s0, s1, s2, s3, grown)
    rows = 11 * 12 * 8
    both = grown[...].reshape(rows, WIDE)
    lane = iota((rows, WIDE), 1)
    tokens = jnp.where(lane < EMB, both, 0.0)
    target = jnp.where(lane < CLASSES, roll(both, WIDE - EMB, 1), 0.0)
    live = jnp.sum(target, 1, keepdims=True)
    count = F32(voxels)
    average = sums[0:1, :] / count
    spread = sums[1:2, :] / count - average * average
    inv = lax.rsqrt(spread + eps_norm)
    gain = vectors[2:3, :]
    bias = vectors[3:4, :]
    hat = (tokens - average) * inv
    act, slope = gelu_both(hat * gain + bias)
    act = jnp.where(lane == EMB, 1.0, act)
    w = head_w[...]
    logits = mm(act, w)
    logits = jnp.where(lane < CLASSES, logits, -1e30)
    top = jnp.max(logits, 1, keepdims=True)
    e = jnp.exp(logits - top)
    total = jnp.sum(e, 1, keepdims=True)
    logp = logits - top - jnp.log(total)
    scale = 1.0 / sums[2:3, 0:1]
    d_logits = (e / total * live - target) * scale
    d_normed = jnp.where(lane < EMB, mm_nt(d_logits, w) * slope, 0.0)
    d_tokens = d_normed * gain * inv
    slope_out[...] = d_tokens.reshape(11, 12, 8, WIDE)

    def own_rows(x):
        x = x.reshape(11, 12, 8, WIDE)[2:9, 2:9]
        x = jnp.where(iota(x.shape, 2) < WIN, x, 0.0)
        return x.reshape(PLANE * 8, WIDE)

    loss = -jnp.sum(own_rows(target * jnp.where(lane < CLASSES, logp, 0.0)))
    own_d = own_rows(d_logits)
    own_n = own_rows(d_normed)
    own_hat = own_rows(hat)
    zeros = jnp.zeros((512 - PLANE * 8, WIDE), F32)
    left = rows_t(jnp.concatenate([own_d, zeros], 0))
    d_head[...] = mm_tn(left, jnp.concatenate([own_rows(act), zeros], 0)).T
    d_gain = colsum(own_n * own_hat)
    d_bias = colsum(own_n)
    d_average = -d_bias * gain * inv
    d_spread = d_gain * gain * inv * inv * -0.5
    d_two = d_spread / count
    d_one = (d_average - 2.0 * average * d_spread) / count
    row = iota((8, WIDE), 0)
    live_lane = iota((8, WIDE), 1) < EMB
    stats[...] = (
        jnp.where((row == 0) & live_lane, d_one, 0.0)
        + jnp.where((row == 1) & live_lane, d_two, 0.0)
        + jnp.where(row == 2, loss, 0.0)
    )
    d_rows[...] = (
        jnp.where(row == 0, d_gain, 0.0)
        + jnp.where(row == 1, d_bias, 0.0)
    )


def sides_back_kernel(sizes, grown, pre, side_act, side_grown, act):
    act[0:9] = gelu(pre[...]) * volume_mask(sizes, 9, 10, 1, 9)
    act[9:10] = jnp.zeros((1, 10, 8, WIDE), F32)
    taps(act, 0, 10, 0, 8, side_act)
    taps(grown, 1, 10, 1, 8, side_grown)


def weights_back_kernel(conv0, conv1, weights0, weights1):
    tap_weights_back(conv0, 3, weights0)
    tap_weights_back(conv1, 0, weights1)


def conv_back_kernel(
    sizes,
    tok, slope, sums, pre, side_act, side_grown, weights0, weights1, d_rows, d_head,
    d_own, keep, send, carry, seam,
    grads, dgrown, act, side, side_own, flat,
):
    lane = iota((11, 12, 8, WIDE), 3)
    inside = volume_mask(sizes, 11, 12, 2, 11)
    steady = sums[0:1, :].reshape(1, 1, 1, WIDE)
    rising = 2.0 * sums[1:2, :].reshape(1, 1, 1, WIDE)
    d_tok = slope[...] + jnp.where(lane < EMB, (steady + tok[...] * rising) * inside, 0.0)
    dgrown[...] = d_tok
    grads[5191:, :] = jnp.zeros((45, WIDE), F32)
    grads[0:8, :] = jnp.zeros((8, WIDE), F32)
    grads[5189:5191, :] = d_rows[0:2, :]
    own = dgrown[2:9, 2:10]
    line = iota(own.shape, 1)
    own = jnp.where(line < WIN, own, 0.0).reshape(WIN * 64, WIDE)
    grads[5188:5189, :] = colsum(own)

    near = volume_mask(sizes, 9, 10, 1, 9)
    conv_weight_grad(side_act, own, 64, grads, 2596)
    taps(dgrown, 0, 11, 0, 10, side)


    def put(start, y):
        _, s = gelu_both(pre[start : start + 3])
        act[start : start + 3] = y.reshape(3, 10, 8, WIDE) * s * near[start : start + 3]

    conv(side, weights1, 9, 80, 3, put, back=True)

    own = act[1:8, 1:9]
    line = iota(own.shape, 1)
    own = jnp.where(line < WIN, own, 0.0).reshape(WIN * 64, WIDE)
    grads[2595:2596, :] = colsum(own)
    conv_weight_grad(side_grown, own, 64, grads, 3)
    carry[...] = grads[0:24, :]
    flat[3 * (GROUPS - CUTS[3]) :, :] = jnp.zeros((flat.shape[0] - 3912, WIDE), F32)
    flatten(grads, 20, GROUPS - CUTS[3], flat)
    start = 3 * CUTS[3]
    head_rows(d_head[...], flat, HEAD_ROW - start)
    seam[...] = flat[0 : LATE_ROWS - start, :]
    scatter(sizes, flat, LATE_ROWS - start, keep, send, EARLY_BLOCKS)
    taps(act, 0, 9, 0, 8, side_own)

    def put_own(start, y):
        y = y.reshape(WIN, 8, 8, WIDE)[:, 0:WIN] + dgrown[2:9, 2:9]
        y = jnp.where(iota(y.shape, 2) < WIN, y, 0.0)
        d_own[...] = y.reshape(PLANE, 8, WIDE)

    conv(side_own, weights0, WIN, 64, WIN, put_own, back=True)


def back_mlp_kernel(d_own, lay2, mid2, hpre2, d_mid, grads, dense):
    from_lines(d_own, dense)
    grads[...] = jnp.zeros_like(grads)
    d_mid[...] = mlp_back(dense[...], mid2[...], hpre2, Rows(lay2, 2), grads, 2)


def back_two_kernel(
    d_mid2, grads2, carry, lay1, lay2, tok2, save, lse, mixed, mid1, hpre1,
    d_mid, grads1, flat, carry2, pa, pb, pc,
    grads, *sc,
):
    layer = Rows(lay2, 2)
    grads[0:1168, :] = grads2[...]
    d = d_mid2[...]
    tokens = tok2[...]
    normed = norm(tokens, layer[0:1, :], layer[1:2, :])
    d_normed = attention_back(d, normed, layer, save, lse, mixed, sc, grads, 2)
    d = d + pre_norm_back(d_normed, tokens, layer, grads, 2)
    grads[1167:1184, :] = carry[3:20, :]
    flatten(grads, 32, CUTS[3] - CUTS[2], flat)
    carry2[...] = grads[0:32, :]
    layer = Rows(lay1, 1)
    d = mlp_back(d, mid1[...], hpre1, layer, grads1, 1)
    d_mid[...] = d
    send_parts(d_mid, pa, pb, pc)


def back_shifted_kernel(
    sizes,
    own, pa, pb, pc, lay1, window, save, lse, mixed, grads1, carry2,
    d_window, flat, carry1, qa, qb, qc,
    region, grads, grad, *sc,
):
    put_region(region, sizes)
    take_parts(own, pa, pb, pc, grad)
    grads[0:1168, :] = grads1[...]
    grads[0:3, :] = jnp.zeros((3, WIDE), F32)
    d_window[...] = attention_back(
        grad[...], window[...], Rows(lay1, 1), save, lse, mixed, sc, grads, 1,
        region,
    )
    send_parts(d_window, qa, qb, qc)
    grads[1166:1196, :] = carry2[2:32, :]
    flatten(grads, 12, CUTS[2] - CUTS[1], flat)
    carry1[...] = grads[0:16, :]


def back_first_kernel(
    sizes,
    d_mid, own, qa, qb, qc, tok1, lay0, lay1, merge, dense, tok0, save, lse, mixed, middle, hpre,
    carry1, flat1, flat2, seam, _,
    keep, send,
    flat, grads, grad, *sc,
):
    take_parts(own, qa, qb, qc, grad)
    grads[1556:1572, :] = carry1[...]
    d = d_mid[...] + pre_norm_back(grad[...], tok1[...], Rows(lay1, 1), grads, 1557)
    layer = Rows(lay0, 0)
    at = MERGE_ROWS
    d = mlp_back(d, middle[...], hpre, layer, grads, at)
    tokens = tok0[...]
    normed = norm(tokens, layer[0:1, :], layer[1:2, :])
    d_normed = attention_back(d, normed, layer, save, lse, mixed, sc, grads, at)
    d = d + pre_norm_back(d_normed, tokens, layer, grads, at)
    live = iota((ROWS, WIDE), 0) < VOX
    d = jnp.where(live, d, 0.0)
    hat = merged_norm(dense[...])
    gain = hidden_rows(merge, 0, 1)
    bias = hidden_rows(merge, 4, 1)
    w = merge[8 : 8 + MERGE, :]
    put_hidden_rows(grads, 8 - 8, 1, jnp.zeros((1, MERGE), F32))
    grads[8 : 8 + MERGE, :] = mm_tn(rows_t(d), hat * gain + bias).T
    d_hat = mm_nt(d, w)
    put_hidden_rows(grads, 0, 1, colsum(d_hat * hat))
    put_hidden_rows(grads, 4, 1, colsum(d_hat))
    flatten(grads, 0, CUTS[1], flat)
    at = 0
    for cut, part in ((CUTS[1], flat1), (CUTS[2], flat2), (CUTS[3], seam)):
        at = 3 * cut
        flat[at : at + part.shape[0], :] = part[...]
    at += seam.shape[0]
    if flat.shape[0] > at:
        flat[at:, :] = jnp.zeros((flat.shape[0] - at, WIDE), F32)
    scatter(sizes, flat, 0, keep, send, sizes[0] * sizes[1])


def radices(count):
    steps = [2]
    left = count // 2
    while left > 1:
        steps.append(4 if left >= 4 else 2)
        left //= steps[-1]
    return steps


def block_rows(rows, count):
    return -(-rows // (8 * count)) * 8


def own_number(sizes):
    return lax.axis_index("slab") * sizes[1] + lax.axis_index("mp")


def place_in_half(distance, count):
    place = 0
    shift = 1
    for radix in radices(count)[1:]:
        digit = jnp.bitwise_and(lax.shift_right_logical(distance, shift), radix - 1)
        place = place * radix + digit
        shift += radix.bit_length() - 1
    return place


def scatter(sizes, source, first, keep, send, count):
    rows = keep.shape[0] * 2 // count
    me = jnp.bitwise_and(own_number(sizes), count - 1)
    odd = jnp.bitwise_and(me, 1)

    def per_pair(t, carry):
        for block, out in ((2 * t + odd, keep), (2 * t + 1 - odd, send)):
            place = place_in_half(jnp.bitwise_xor(block, me), count)
            at = pl.multiple_of(first + block * rows, 8)
            to = pl.multiple_of(place * rows, 8)
            out[pl.ds(to, rows), :] = source[pl.ds(at, rows), :]
        return carry

    lax.fori_loop(0, count // 2, per_pair, 0)


def traded(value, distance, count):
    pairs = [(i, i ^ distance) for i in range(count)]
    return lax.ppermute(value, ("slab", "mp"), pairs)


def later(got, after):
    return got if after is None else list(lax.optimization_barrier((*got, after)))[:-1]


def summing(keep, send, count, blocks):
    steps = radices(blocks)
    got = [keep, traded(send, 1, count)]
    shift = 1
    after = yield None
    for radix in steps[1:]:
        got = later(got, after)
        total = sum(got[1:], got[0])
        rows = total.shape[0] // radix
        parts = [total[k * rows : (k + 1) * rows] for k in range(radix)]
        got = parts[:1] + [traded(parts[k], k << shift, count) for k in range(1, radix)]
        shift += radix.bit_length() - 1
        after = yield parts[0]
    top = shift
    while 1 << top < count:
        radix = 4 if count >> top >= 4 else 2
        got = later(got, after)
        own = sum(got[1:], got[0])
        got = [own] + [traded(own, k << top, count) for k in range(1, radix)]
        if radix == 4:
            got = [got[0] + got[1], got[2] + got[3]]
        top += radix.bit_length() - 1
        after = yield own
    got = later(got, after)
    own = sum(got[1:], got[0])
    for radix in reversed(steps[1:]):
        shift -= radix.bit_length() - 1
        got = [own] + [traded(own, k << shift, count) for k in range(1, radix)]
        after = yield own
        own = jnp.concatenate(later(got, after), 0)
        yield own
    yield own, traded(own, 1, count)


def finished(chain, after=None):
    last = next(chain) if after is None else chain.send(after)
    while not isinstance(last, tuple):
        last = next(chain)
    return last


def exchanged_sum(value, count):
    distance = 1
    while distance < count:
        value = value + traded(value, distance, count)
        distance *= 2
    return value


PIECE = 262144


def adamw_kernel(
    sizes,
    late, late_other, early, early_other, tail, sums, params, first, second,
    new_params, new_first, new_second, loss, valid, norm_out,
    grad, scale_ref,
):
    count = sizes[0] * sizes[1]
    step = pl.program_id(0)

    @pl.when(step == 0)
    def gather():
        me = own_number(sizes)
        total = jnp.zeros((8, WIDE), F32)
        for ref in (late, late_other, early, early_other):
            x = ref[...]
            total = total + jnp.sum((x * x).reshape(-1, 8, WIDE), 0)
        norm = jnp.sqrt(jnp.sum(total))
        loss[0] = jnp.sum(tail[2:3, 0:1])
        valid[0] = jnp.sum(sums[2:3, 0:1])
        norm_out[0] = norm
        scale_ref[0] = jnp.minimum(1.0, clip_norm / (norm + 1e-06))
        start = 0
        for own, other, size, blocks in (
            (late, late_other, LATE_ROWS, count),
            (early, early_other, EARLY_ROWS, EARLY_BLOCKS),
        ):
            rows = own.shape[0] * 2 // blocks
            here = jnp.bitwise_and(me, blocks - 1)

            def per_block(block, carry, own=own, other=other, rows=rows, start=start, blocks=blocks, here=here):
                distance = jnp.bitwise_xor(block, here)
                place = place_in_half(distance, blocks)
                near = jnp.bitwise_and(distance, 1) == 0
                part = math.gcd(rows, 96)
                for low in range(0, rows, part):
                    at = pl.ds(pl.multiple_of(place * rows + low, 8), part)
                    to = pl.ds(pl.multiple_of(start + block * rows + low, 8), part)
                    grad[to, :] = jnp.where(near, own[at, :], other[at, :])
                return carry

            lax.fori_loop(0, size // rows, per_block, 0)
            start += size

    def update(base, low, size):
        rows = -(-size // 1024) * 8
        at = pl.ds(pl.multiple_of(base // WIDE + low // WIDE, 8), rows)
        g = grad[at, :].reshape(rows * WIDE)[:size] * scale_ref[0]
        here = pl.ds(pl.multiple_of(base + low, 1024), size)
        one = beta_one * first[here] + (1.0 - beta_one) * g
        two = beta_two * second[here] + (1.0 - beta_two) * g * g
        there = pl.ds(low, size)
        new_first[there] = one
        new_second[there] = two
        two = two * (1.0 / (1.0 - beta_two**STEP))
        low_by = two * lax.rsqrt(jnp.maximum(two, 1e-37)) + adam_eps
        inverse = pl.reciprocal(low_by, approx=True)
        inverse = inverse * (2.0 - low_by * inverse)
        new_params[there] = params[here] * (1.0 - learn_rate * decay_rate) - (
            one * (learn_rate / (1.0 - beta_one**STEP))
        ) * inverse

    whole = NPARAM // PIECE

    @pl.when(step < whole)
    def full():
        def part(i, carry):
            low = pl.multiple_of(i * 16384, 16384)
            update(step * PIECE, low, 16384)
            return carry

        lax.fori_loop(0, PIECE // 16384, part, 0)

    @pl.when(step == whole)
    def last():
        rest = NPARAM - whole * PIECE
        main = rest // 1024 * 1024
        for low in range(0, main, 16384):
            update(whole * PIECE, low, min(16384, main - low))
        update(whole * PIECE, main, rest - main)


def adamw(sizes, parts, arrays):
    pieces = -(-NPARAM // PIECE)
    piece = pl.BlockSpec((PIECE,), lambda i: (i,))
    vmem = pl.BlockSpec(memory_space=pltpu.VMEM)
    smem = pl.BlockSpec(memory_space=pltpu.SMEM)
    return pl.pallas_call(
        functools.partial(adamw_kernel, sizes),
        grid=(pieces,),
        out_shape=[arr(NPARAM)] * 3 + [arr(1)] * 3,
        in_specs=[vmem] * (len(parts) + len(arrays)),
        out_specs=[piece] * 3 + [smem] * 3,
        scratch_shapes=[pltpu.VMEM((LATE_ROWS + EARLY_ROWS, WIDE), F32), pltpu.SMEM((1,), F32)],
        compiler_params=pltpu.CompilerParams(vmem_limit_bytes=16 * 1024 * 1024),
        cost_estimate=pl.CostEstimate(flops=6 * 10**9, bytes_accessed=0, transcendentals=0),
        name="adamw",
    )(*parts, *arrays)


def arr(*shape):
    return jax.ShapeDtypeStruct(shape, F32)


def call(kernel, outs, scratch, *args, name=None, us=1.0, far=(), mib=16):
    vmem = pl.BlockSpec(memory_space=pltpu.VMEM)
    smem = pl.BlockSpec(memory_space=pltpu.SMEM)
    return pl.pallas_call(
        kernel,
        out_shape=list(outs),
        in_specs=[vmem] * len(args) + [pl.BlockSpec(memory_space=pl.ANY)] * len(far),
        out_specs=[smem if o.shape == (1,) else vmem for o in outs],
        scratch_shapes=list(scratch),
        compiler_params=pltpu.CompilerParams(vmem_limit_bytes=mib * 1024 * 1024),
        cost_estimate=pl.CostEstimate(
            flops=int(us * 1.15e9), bytes_accessed=0, transcendentals=0
        ),
        name=name,
    )(*args, *far)


SQUARE = arr(ROWS, WIDE)
SAVE = arr(ROWS, 3 * WIDE)
FORWARD = [
    pltpu.VMEM((2, ROWS, 2 * WIDE), BF16),
    pltpu.VMEM((2, ROWS, 2 * WIDE), BF16),
    pltpu.VMEM((2 * ROWS, 2 * WIDE), BF16),
    pltpu.VMEM((2 * ROWS, 2 * WIDE), BF16),
]
BACKWARD = [
    pltpu.VMEM((2, ROWS, 2 * WIDE), BF16),
    pltpu.VMEM((2, ROWS, 2 * WIDE), BF16),
    pltpu.VMEM((2, ROWS, 2 * WIDE), BF16),
    pltpu.VMEM((2, ROWS, 2 * WIDE), BF16),
    pltpu.VMEM((2 * ROWS, 2 * WIDE), BF16),
    pltpu.VMEM((ROWS, WIDE), F32),
    pltpu.VMEM((2, WIDE, ROWS), F32),
    pltpu.VMEM((2, ROWS, 2 * ROWS), BF16),
    pltpu.VMEM((2, ROWS, 2 * ROWS), BF16),
    pltpu.VMEM((2, WIDE, ROWS), BF16),
    pltpu.VMEM((2, WIDE, ROWS), BF16),
    pltpu.VMEM((ROWS, WIDE), F32),
    pltpu.VMEM((ROWS, 2 * ROWS), F32),
    pltpu.VMEM((ROWS, 2 * ROWS), F32),
    pltpu.VMEM((2 * ROWS, 2 * WIDE), BF16),
    pltpu.VMEM((2 * ROWS, 2 * WIDE), BF16),
]
PARTS = [arr(ROWS_A, WIDE), arr(ROWS_B, WIDE), arr(ROWS_C, WIDE)]


def passed(parts, steps, sizes):
    slabs, rows = sizes
    moved = []
    for part, (ds, dm) in zip(parts, ((1, 0), (0, 1), (1, 1))):
        pairs = []
        for s in range(slabs):
            for m in range(rows):
                target = ((s + steps * ds) % slabs) * rows + (m + steps * dm) % rows
                pairs.append((s * rows + m, target))
        moved.append(lax.ppermute(part, ("slab", "mp"), pairs))
    return moved


SIDES = [arr(2 * WIN, 8, WIDE)] * 4


def beside(sides, sizes):
    slabs, rows = sizes
    low_d, high_d, low_h, high_h = sides
    up = [(i, i + 1) for i in range(slabs - 1)]
    down = [(i + 1, i) for i in range(slabs - 1)]
    before = lax.ppermute(high_d, "slab", up)
    after = lax.ppermute(low_d, "slab", down)

    def column(own, start):
        ends = [
            x.reshape(2, WIN, 8, WIDE)[:, start : start + 2].reshape(4, 8, WIDE)
            for x in (before, after)
        ]
        return jnp.concatenate([ends[0], own, ends[1]], 0)

    up = [(i, i + 1) for i in range(rows - 1)]
    down = [(i + 1, i) for i in range(rows - 1)]
    left = lax.ppermute(column(high_h, WIN - 2), "mp", up)
    right = lax.ppermute(column(low_h, 0), "mp", down)
    return before, after, left, right


REGION = [pltpu.VMEM((ROWS, ROWS), F32)]


def on_device(sizes, feats, labels, valid, params, moment_one, moment_two):
    slabs, rows = sizes
    count = slabs * rows

    def room(spans):
        sizes = [(span_of(groups)[1] + 8) * WIDE for groups in spans]
        return [
            [pltpu.VMEM((size,), F32) for size in sizes],
            pltpu.VMEM((2048, WIDE), F32),
            pltpu.SemaphoreType.DMA((len(spans),)),
        ]

    merge, lay0 = call(
        functools.partial(prep_kernel, FIRST_SPANS),
        [arr(MERGE_ROWS, WIDE), arr(1176, WIDE)],
        room(FIRST_SPANS),
        name="prep_first", us=2.0, far=(params[: FIRST_SPANS[-1][1] * 384],),
    )
    lay1, lay2 = call(
        functools.partial(prep_kernel, LAYER_SPANS),
        [arr(1168, WIDE)] * 2,
        room(LAYER_SPANS),
        name="prep_layers", us=2.0, far=(params,),
    )
    conv0, conv1, head_w, weights0, weights1, vectors = call(
        prep_conv_kernel,
        [arr(2596, WIDE), arr(2640, WIDE), arr(WIDE, WIDE)]
        + [jax.ShapeDtypeStruct((27 * 256, 256), BF16)] * 2
        + [arr(8, WIDE)],
        room(CONV_SPANS),
        params[NPARAM // WIDE * WIDE :],
        name="prep_conv", us=4.0, far=(params,),
    )

    dense, tok0, save0, lse0, mixed0, mid0, hpre0, tok1, ahead, *parts = call(
        first_kernel,
        [arr(ROWS, MERGE), SQUARE, SAVE, SQUARE, SQUARE, SQUARE, arr(ROWS, HID), SQUARE, SQUARE]
        + PARTS,
        FORWARD,
        feats.reshape(PLANE, WIN, MERGE), merge, lay0,
        name="first", us=6.0,
    )
    parts = passed(parts, -1, sizes)
    window, save1, lse1, mixed1, out1, *parts = call(
        functools.partial(shifted_kernel, sizes),
        [SQUARE, SAVE, SQUARE, SQUARE, SQUARE] + PARTS,
        REGION + FORWARD,
        ahead, *parts, lay1,
        name="shifted", us=4.5,
    )
    parts = passed(parts, 1, sizes)
    mid1, hpre1, tok2, save2, lse2, mixed2, mid2, hpre2, lines, *sides = call(
        second_kernel,
        [SQUARE, arr(ROWS, HID), SQUARE, SAVE, SQUARE, SQUARE, SQUARE, arr(ROWS, HID)]
        + [arr(PLANE, 8, WIDE)] + SIDES,
        [pltpu.VMEM((ROWS, WIDE), F32)] + FORWARD,
        tok1, out1, *parts, lay1, lay2,
        name="second", us=6.5, far=(weights0,),
    )
    sides = beside(sides, sizes)
    grown, pre, tok3, sums, *tok_sides = call(
        functools.partial(conv_kernel, sizes),
        [arr(11, 12, 8, WIDE), arr(9, 10, 8, WIDE), arr(PLANE, 8, WIDE), arr(8, WIDE)] + SIDES,
        [
            pltpu.VMEM((9, 10, 8, WIDE), F32),
            pltpu.VMEM((880, 2304), BF16),
            pltpu.VMEM((576, 2304), BF16),
            pltpu.VMEM((PLANE, 8, WIDE), F32),
        ],
        lines, *sides, labels, valid, weights0, weights1, vectors,
        name="conv", us=8.0, mib=20,
    )
    tok_sides = beside(tok_sides, sizes)
    side_act, side_grown = call(
        functools.partial(sides_back_kernel, sizes),
        [jax.ShapeDtypeStruct((640, 2304), BF16)] * 2,
        [pltpu.VMEM((10, 10, 8, WIDE), F32)],
        grown, pre,
        name="sides_back", us=2.0,
    )
    weights0, weights1 = call(
        weights_back_kernel,
        [jax.ShapeDtypeStruct((256, 27 * 256), BF16)] * 2,
        [],
        conv0, conv1,
        name="weights_back", us=1.5,
    )
    sums = exchanged_sum(sums, count)
    voxels = WIN * slabs * WIN * rows * WIN
    tok3, slope, tail, d_head, d_rows = call(
        functools.partial(head_kernel, voxels),
        [arr(11, 12, 8, WIDE), arr(11, 12, 8, WIDE), arr(8, WIDE), arr(WIDE, WIDE), arr(8, WIDE)],
        [],
        tok3, *tok_sides, sums, vectors, head_w,
        name="head", us=3.5,
    )
    tail = exchanged_sum(tail, count)
    late_rows = block_rows(LATE_ROWS, count) * count
    early_rows = EARLY_ROWS
    seam_rows = LATE_ROWS - 3 * CUTS[3]
    d_own, keep, send, carry3, seam = call(
        functools.partial(conv_back_kernel, sizes),
        [arr(PLANE, 8, WIDE)] + [arr(early_rows // 2, WIDE)] * 2
        + [arr(24, WIDE), arr(seam_rows, WIDE)],
        [
            pltpu.VMEM((5236, WIDE), F32),
            pltpu.VMEM((11, 12, 8, WIDE), F32),
            pltpu.VMEM((10, 10, 8, WIDE), F32),
            pltpu.VMEM((880, 2304), BF16),
            pltpu.VMEM((576, 2304), BF16),
            pltpu.VMEM((seam_rows + early_rows, WIDE), F32),
        ],
        tok3, slope, tail, pre, side_act, side_grown, weights0, weights1, d_rows, d_head,
        name="conv_back", us=14.0, mib=28,
    )
    early = summing(keep, send, count, EARLY_BLOCKS)
    next(early)
    d_mid2, grads2 = call(
        back_mlp_kernel,
        [SQUARE, arr(1168, WIDE)],
        [pltpu.VMEM((ROWS, WIDE), F32)],
        d_own, lay2, mid2, hpre2,
        name="back_mlp", us=3.0,
    )
    step = early.send(d_mid2)
    d_mid, grads1, flat2, carry2, *parts = call(
        back_two_kernel,
        [SQUARE, arr(1168, WIDE), arr(3 * (CUTS[3] - CUTS[2]), WIDE), arr(32, WIDE)] + PARTS,
        [pltpu.VMEM((1184, WIDE), F32)] + BACKWARD,
        d_mid2, grads2, carry3, lay1, lay2, tok2, save2, lse2, mixed2, mid1, hpre1,
        name="back_two", us=7.0,
    )
    parts = passed(parts, -1, sizes)
    early.send(d_mid)
    d_window, flat1, carry1, *parts = call(
        functools.partial(back_shifted_kernel, sizes),
        [SQUARE, arr(3 * (CUTS[2] - CUTS[1]), WIDE), arr(16, WIDE)] + PARTS,
        REGION + [pltpu.VMEM((1200, WIDE), F32), pltpu.VMEM((ROWS, WIDE), F32)] + BACKWARD,
        d_mid, *parts, lay1, window, save1, lse1, mixed1, grads1, carry2,
        name="back_shifted", us=6.0,
    )
    parts = passed(parts, 1, sizes)
    step = early.send(d_window)
    late = call(
        functools.partial(back_first_kernel, sizes),
        [arr(late_rows // 2, WIDE)] * 2,
        [
            pltpu.VMEM((late_rows, WIDE), F32),
            pltpu.VMEM((1572, WIDE), F32),
            pltpu.VMEM((ROWS, WIDE), F32),
        ]
        + BACKWARD,
        d_mid, d_window, *parts, tok1, lay0, lay1, merge, dense, tok0, save0, lse0, mixed0, mid0,
        hpre0, carry1, flat1, flat2, seam,
        name="back_first", us=8.0, far=(step,),
    )
    step = early.send(late[0])
    keep, send = later(list(late), step)
    late_sum = finished(summing(keep, send, count, count))
    early = finished(early)
    new_params, new_first, new_second, loss, valid_count, norm = adamw(
        sizes, (*late_sum, *early, tail, sums), (params, moment_one, moment_two)
    )
    return (
        loss.reshape(()), valid_count.reshape(()), norm.reshape(()),
        new_params, new_first, new_second,
    )


def solution(mesh):
    placed = (
        P("slab", "mp", None, None),
        P("slab", "mp", None),
        P("slab", "mp", None),
        P(),
        P(),
        P(),
    )
    sizes = (mesh.shape["slab"], mesh.shape["mp"])
    return jax.shard_map(
        functools.partial(on_device, sizes),
        mesh=mesh,
        in_specs=placed,
        out_specs=(P(), P(), P(), P(), P(), P()),
        check_vma=False,
    )
```

```python
import functools

import jax
import jax.numpy as jnp
from jax import lax
from jax.experimental import pallas as pl
from jax.experimental.pallas import tpu as pltpu
from jax.sharding import PartitionSpec as P

EMB = 96
HEADS = 6
HDIM = 16
HID = 384
MERGE = 384
CLASSES = 14
WIN = 7
SHIFT = 3
LAYERS = 3
STEP = 10

F32 = jnp.float32
BF16 = jnp.bfloat16
eps_norm = 1e-05
beta_one = 0.9
beta_two = 0.999
adam_eps = 1e-08
learn_rate = 0.05
decay_rate = 0.05
clip_norm = 0.01
LOG2E = 1.4426950408889634

VOX = WIN * WIN * WIN
ROWS = 384
BLK = 128
WIDE = 128
PLANE = WIN * WIN
FAR = WIN - SHIFT
ROWS_A = SHIFT * FAR * WIN
ROWS_B = FAR * SHIFT * WIN
ROWS_C = SHIFT * SHIFT * WIN

MERGE_ROWS = 392
LAYER_ROWS = 1165
TAP_ROWS = 27 * EMB
GROUPS = 2280
NPARAM = 872558
HEAD_ROW = 6806
HEAD_ROWS = 11
HEAD_LANE = 32
LATE_ROWS = 3072
EARLY_ROWS = 3840
LAYER_BASE = (98, 389, 680)
CONV_BASE = (971, 1620)
CUTS = (0, 392, 688, 976, 2280)

R_QKV, R_QKVB, R_PROJ, R_PROJB = 4, 292, 295, 391
R_HID, R_HIDB, R_OUT, R_OUTB = 392, 776, 780, 1164


def iota(shape, dim):
    return lax.broadcasted_iota(jnp.int32, shape, dim)


def split(x):
    hi = x.astype(BF16)
    return hi, (x - hi.astype(F32)).astype(BF16)


def pair(x):
    return jnp.concatenate(split(x), 1)


def fold(y):
    half = y.shape[1] // 2
    return y[:, :half] + y[:, half:]


def fold_rows(y):
    half = y.shape[0] // 2
    return y[:half] + y[half:]


def dot(a, b):
    return jnp.dot(a, b, preferred_element_type=F32)


def dot_nt(a, b):
    return lax.dot_general(a, b, (((1,), (1,)), ((), ())), preferred_element_type=F32)


def weight_nn(w):
    top = pair(w)
    return jnp.concatenate([top, top], 0)


def weight_nt(w):
    hi, lo = split(w)
    return jnp.concatenate(
        [jnp.concatenate([hi, hi], 1), jnp.concatenate([lo, lo], 1)], 0
    )


def mm(x, w):
    return fold(dot(pair(x), weight_nn(w)))


def mm_nt(x, w):
    return fold(dot_nt(pair(x), weight_nt(w)))


def rows_t(x):
    return jnp.concatenate(split(x.T), 0)


def mm_tn(xt, y):
    return fold_rows(fold(dot(xt, pair(y))))


def deep(w):
    return jnp.concatenate([w, jnp.zeros((WIDE - EMB, w.shape[1]), F32)], 0)


def roll(x, shift, axis):
    return pltpu.roll(x, shift, axis)


def four_to_three(y):
    lane = iota(y[0].shape, 1)
    a = jnp.where(lane < 96, y[0], roll(y[1], 96, 1))
    b = jnp.where(lane < 64, roll(y[1], 96, 1), roll(y[2], 64, 1))
    c = jnp.where(lane < 32, roll(y[2], 64, 1), roll(y[3], 32, 1))
    return a, b, c


def three_to_four(x):
    lane = iota(x[0].shape, 1)
    live = lane < EMB
    a = x[0]
    b = jnp.where(lane < 32, roll(x[0], 32, 1), roll(x[1], 32, 1))
    c = jnp.where(lane < 64, roll(x[1], 64, 1), roll(x[2], 64, 1))
    d = roll(x[2], 96, 1)
    return tuple(jnp.where(live, v, 0.0) for v in (a, b, c, d))


def hidden_rows(ref, start, count):
    return jnp.concatenate(
        four_to_three([ref[pl.ds(start + c, count, stride=4), :] for c in range(4)]), 1
    )


def put_hidden_rows(ref, start, count, x):
    parts = three_to_four([x[:, i * WIDE : (i + 1) * WIDE] for i in range(3)])
    for c in range(4):
        ref[pl.ds(start + c, count, stride=4), :] = parts[c]


def flatten(ref, start, groups, out):
    parts = four_to_three([ref[pl.ds(start + c, groups, stride=4), :] for c in range(4)])
    for c in range(3):
        out[pl.ds(c, groups, stride=3), :] = parts[c]


def norm_stats(x):
    live = iota(x.shape, 1) < EMB
    mean = jnp.sum(x, 1, keepdims=True) * (1.0 / EMB)
    centred = jnp.where(live, x - mean, 0.0)
    var = jnp.sum(centred * centred, 1, keepdims=True) * (1.0 / EMB)
    inv = lax.rsqrt(var + eps_norm)
    return centred * inv, inv


def norm(x, gain, bias):
    hat, _ = norm_stats(x)
    return hat * gain + bias


def norm_back(hat, inv, gain, grad):
    up = grad * gain
    one = jnp.sum(up, 1, keepdims=True) * (1.0 / EMB)
    two = jnp.sum(up * hat, 1, keepdims=True) * (1.0 / EMB)
    live = iota(hat.shape, 1) < EMB
    return jnp.where(live, inv * (up - one - hat * two), 0.0)


def colsum(x):
    return jnp.sum(x, 0, keepdims=True)


def gelu(x):
    return 0.5 * x * (1.0 + lax.erf(x * (0.5**0.5)))


def gelu_both(x):
    cdf = 0.5 * (1.0 + lax.erf(x * (0.5**0.5)))
    slope = cdf + x * (jnp.exp(x * x * -0.5) * 0.3989422804014327)
    return x * cdf, slope


def head_groups(x):
    lane = iota(x.shape, 1)
    swapped = roll(x, 64, 1)
    return jnp.where(lane < 64, x, swapped), jnp.where(lane < 64, swapped, x)


def as_left(x):
    both = []
    low = iota(x.shape, 1) < 64
    for part in head_groups(x):
        hi = part.astype(BF16).astype(F32)
        one = jnp.where(low, hi, part - hi).astype(BF16)
        both.append(jnp.concatenate([one, one], 1))
    return both


def as_right(x):
    return [pair(part) for part in head_groups(x)]


def head_mask(h, width):
    lane = iota((1, width), 1)
    lane = jnp.bitwise_and(lane, 63)
    low = jnp.bitwise_and(h, 3) * HDIM
    return jnp.where((lane >= low) & (lane < low + HDIM), 1.0, 0.0)


def own_lanes(h):
    lane = iota((1, WIDE), 1)
    return jnp.where((lane >= h * HDIM) & (lane < (h + 1) * HDIM), 1.0, 0.0)


def both_heads(right, heads, out):
    for k, h in enumerate(heads):
        out[k * ROWS : (k + 1) * ROWS, :] = right * head_mask(h, 2 * WIDE).astype(BF16)


def score_tiles(s, rows, region):
    tiles = [s[:, i * WIDE : (i + 1) * WIDE] for i in range(3)]
    if region is not None:
        return [t + region[rows, i * WIDE : (i + 1) * WIDE] for i, t in enumerate(tiles)]
    pad = jnp.where(iota((1, WIDE), 1) < VOX - 2 * WIDE, 0.0, -1e30)
    return tiles[:2] + [tiles[2] + pad]


def put_split(ref, rows, i, x):
    hi, lo = split(x)
    ref[rows, i * WIDE : (i + 1) * WIDE] = hi
    ref[rows, ROWS + i * WIDE : ROWS + (i + 1) * WIDE] = lo


def attention(normed, layer, save, lse, mixed, sc, region=None):
    left, right, values = sc
    x = pair(normed)
    qkv = []
    for i in range(3):
        w = deep(layer[pl.ds(R_QKV + i, EMB, stride=3), :])
        y = fold(dot(x, weight_nn(w))) + layer[R_QKVB + i : R_QKVB + i + 1, :]
        if i == 0:
            y = y * (HDIM**-0.5 * LOG2E)
        save[:, i * WIDE : (i + 1) * WIDE] = y
        qkv.append(y)
    for g, part in enumerate(as_left(qkv[0])):
        left[g] = part
    for g, part in enumerate(as_right(qkv[1])):
        right[g] = part
    v = pair(jnp.where(iota((ROWS, WIDE), 1) == EMB, 1.0, qkv[2]))
    values[0:ROWS, :] = v
    values[ROWS : 2 * ROWS, :] = v
    mixed[...] = jnp.zeros_like(mixed)
    lse[...] = jnp.zeros_like(lse)

    def per_pair(pair_of, carry):
        heads = [2 * pair_of, 2 * pair_of + 1]
        masks = [head_mask(h, 2 * WIDE).astype(BF16) for h in heads]
        lanes = [own_lanes(h) for h in heads]
        spots = [jnp.where(iota((1, WIDE), 1) == h, 1.0, 0.0) for h in heads]
        g = lax.div(pair_of, 2)
        for b in range(ROWS // BLK):
            rows = slice(b * BLK, (b + 1) * BLK)
            out = level = 0.0
            for k in range(2):
                s = dot_nt(left[g, rows, :] * masks[k], right[g])
                tiles = score_tiles(s, rows, region)
                top = jnp.maximum(jnp.maximum(tiles[0], tiles[1]), tiles[2])
                top = jnp.max(top, 1, keepdims=True)
                parts = [split(jnp.exp2(t - top)) for t in tiles]
                e = jnp.concatenate([p[0] for p in parts] + [p[1] for p in parts], 1)
                o = fold(dot(e, values[...]))
                total = o[:, EMB : EMB + 1]
                out = out + o * (lanes[k] / total)
                level = level + (top + jnp.log(total) * LOG2E) * spots[k]
            mixed[rows, :] += out
            lse[rows, :] += level
        return carry

    lax.fori_loop(0, HEADS // 2, per_pair, 0)
    proj = deep(layer[R_PROJ : R_PROJ + EMB, :])
    return mm(mixed[...], proj) + layer[R_PROJB : R_PROJB + 1, :]


def attention_back(grad, normed, layer, save, lse, mixed, sc, grads, at, region=None):
    left, right, gleft, vright, keys, dq, dkv_t, weights, slopes = sc[:9]
    q_t, do_t, dmix, s, dp, two_keys, two_values = sc[9:]
    proj = deep(layer[R_PROJ : R_PROJ + EMB, :])
    grads[at + R_PROJ : at + R_PROJ + EMB, :] = mm_tn(rows_t(mixed[...]), grad)[:EMB]
    grads[at + R_PROJB : at + R_PROJB + 1, :] = colsum(grad)
    d_mixed = mm_nt(grad, proj)
    dmix[...] = d_mixed * mixed[...]
    q, k, v = (save[:, i * WIDE : (i + 1) * WIDE] for i in range(3))
    for g, part in enumerate(as_left(q)):
        left[g] = part
    for g, part in enumerate(as_right(k)):
        right[g] = part
    for g, part in enumerate(as_left(d_mixed)):
        gleft[g] = part
    for g, part in enumerate(as_right(v)):
        vright[g] = part
    kk = pair(k)
    keys[0:ROWS, :] = kk
    keys[ROWS : 2 * ROWS, :] = kk
    for ref, x in ((q_t, q), (do_t, d_mixed)):
        hi, lo = split(x.T)
        ref[0] = hi
        ref[1] = lo
    dq[...] = jnp.zeros_like(dq)
    dkv_t[...] = jnp.zeros_like(dkv_t)

    def per_pair(pair_of, carry):
        g = lax.div(pair_of, 2)
        heads = [2 * pair_of, 2 * pair_of + 1]
        both_heads(right[g], heads, two_keys)
        both_heads(vright[g], heads, two_values)
        s[...] = dot_nt(left[g], two_keys[...])
        dp[...] = dot_nt(gleft[g], two_values[...])
        for k in range(2):
            h = 2 * pair_of + k
            lanes = own_lanes(h)
            at_h = jnp.where(iota((1, WIDE), 1) == h, 1.0, 0.0)
            for b in range(ROWS // BLK):
                rows = slice(b * BLK, (b + 1) * BLK)
                level = jnp.sum(lse[rows, :] * at_h, 1, keepdims=True)
                delta = jnp.sum(dmix[rows, :] * lanes, 1, keepdims=True)
                at_k = k * ROWS
                tiles = score_tiles(s[rows, at_k : at_k + ROWS], rows, region)
                for i, t in enumerate(tiles):
                    p = jnp.exp2(t - level)
                    put_split(weights.at[k], rows, i, p)
                    low = at_k + i * WIDE
                    p = p * (dp[rows, low : low + WIDE] - delta)
                    put_split(slopes.at[k], rows, i, p)
        total = 0.0
        for k in range(2):
            total = total + fold(dot(slopes[k], keys[...])) * own_lanes(2 * pair_of + k)
        dq[...] += total
        for k in range(2):
            here = pl.ds(pl.multiple_of((2 * pair_of + k) * HDIM, HDIM), HDIM)
            for i, (t, m) in enumerate(((q_t, slopes), (do_t, weights))):
                lhs = jnp.concatenate([t[0, here, :], t[1, here, :]], 0)
                dkv_t[i, here, :] = fold_rows(fold(dot(lhs, m[k])))
        return carry

    lax.fori_loop(0, HEADS // 2, per_pair, 0)
    d_q = dq[...] * HDIM**-0.5
    d_k = dkv_t[0].T * (1.0 / LOG2E)
    d_v = dkv_t[1].T
    x_t = rows_t(normed)
    d_normed = None
    for i, d in enumerate((d_q, d_k, d_v)):
        grads[pl.ds(at + R_QKV + i, EMB, stride=3), :] = mm_tn(x_t, d)[:EMB]
        grads[at + R_QKVB + i : at + R_QKVB + i + 1, :] = colsum(d)
        part = mm_nt(d, deep(layer[pl.ds(R_QKV + i, EMB, stride=3), :]))
        d_normed = part if d_normed is None else d_normed + part
    return d_normed


def mlp(middle, layer, hpre):
    normed = norm(middle, layer[2:3, :], layer[3:4, :])
    w = deep(hidden_rows(layer, R_HID, EMB))
    pre = mm(normed, w) + hidden_rows(layer, R_HIDB, 1)
    hpre[...] = pre
    out = mm(gelu(pre), layer[R_OUT : R_OUT + HID, :])
    return middle + out + layer[R_OUTB : R_OUTB + 1, :]


def mlp_back(grad, middle, hpre, layer, grads, at):
    hat, inv = norm_stats(middle)
    normed = hat * layer[2:3, :] + layer[3:4, :]
    act, slope = gelu_both(hpre[...])
    grads[at + R_OUTB : at + R_OUTB + 1, :] = colsum(grad)
    grads[at + R_OUT : at + R_OUT + HID, :] = mm_tn(rows_t(grad), act).T
    d_pre = mm_nt(grad, layer[R_OUT : R_OUT + HID, :]) * slope
    put_hidden_rows(grads, at + R_HIDB, 1, colsum(d_pre))
    put_hidden_rows(grads, at + R_HID, EMB, mm_tn(rows_t(normed), d_pre)[:EMB])
    d_normed = mm_nt(d_pre, deep(hidden_rows(layer, R_HID, EMB)))
    grads[at + 2 : at + 3, :] = colsum(d_normed * hat)
    grads[at + 3 : at + 4, :] = colsum(d_normed)
    return grad + norm_back(hat, inv, layer[2:3, :], d_normed)


def pre_norm_back(grad, tokens, layer, grads, at):
    hat, inv = norm_stats(tokens)
    grads[at : at + 1, :] = colsum(grad * hat)
    grads[at + 1 : at + 2, :] = colsum(grad)
    return norm_back(hat, inv, layer[0:1, :], grad)


def region_of(rows, sizes):
    d = lax.shift_right_logical(rows * 1338, 16)
    line = lax.shift_right_logical(rows * 9363, 16)
    places = (d, line - d * WIN, rows - line * WIN)
    starts = (lax.axis_index("slab") * WIN, lax.axis_index("mp") * WIN, 0)
    total = None
    for place, start, blocks in zip(places, starts, sizes + (1,)):
        turned = jnp.where(place < SHIFT, place + FAR, place - SHIFT) + start
        length = WIN * blocks
        part = jnp.where(turned < length - WIN, 0, jnp.where(turned < length - SHIFT, 1, 2))
        total = part if total is None else total * 3 + part
    return total


def put_region(region, sizes):
    rows = region_of(iota((ROWS, WIDE), 0), sizes)[:, 0:1]
    lanes = region_of(iota((8, ROWS), 1), sizes)[0:1, :]
    apart = jnp.where(rows == lanes, 0.0, -100.0 * LOG2E)
    region[...] = jnp.where(iota((ROWS, ROWS), 1) < VOX, apart, -1e30)


def send_parts(ref, a, b, c):
    far = FAR * WIN
    near = SHIFT * WIN
    for d in range(SHIFT):
        base = d * PLANE
        c[d * near : (d + 1) * near, :] = ref[base : base + near, :]
        a[d * far : (d + 1) * far, :] = ref[base + near : base + PLANE, :]
    for d in range(FAR):
        base = (d + SHIFT) * PLANE
        b[d * near : (d + 1) * near, :] = ref[base : base + near, :]


def take_parts(own, a, b, c, out):
    far = FAR * WIN
    near = SHIFT * WIN
    for d in range(WIN):
        base = d * PLANE
        if d < SHIFT:
            out[base : base + near, :] = c[d * near : (d + 1) * near, :]
            out[base + near : base + PLANE, :] = a[d * far : (d + 1) * far, :]
        else:
            e = d - SHIFT
            out[base : base + near, :] = b[e * near : (e + 1) * near, :]
            out[base + near : base + PLANE, :] = own[base + near : base + PLANE, :]
    out[VOX:, :] = jnp.zeros((ROWS - VOX, WIDE), F32)


def span_of(groups):
    low, high = groups
    first = 3 * low // 8 * 8
    last = -(-3 * high // 8) * 8
    return first, min(last, NPARAM // WIDE // 8 * 8) - first


def copied(params, groups, flat, sem):
    first, rows = span_of(groups)
    size = rows * WIDE
    return pltpu.make_async_copy(
        params.at[pl.ds(first * WIDE, size)], flat.at[pl.ds(0, size)], sem
    )


def relay(groups, flat, out, square, last=None):
    low, high = groups
    first, rows = span_of(groups)
    square[0:rows, :] = flat[0 : rows * WIDE].reshape(rows, WIDE)
    if last is not None:
        square[rows : rows + 24, :] = jnp.zeros((24, WIDE), F32)
        square[rows : rows + 1, 0 : last.shape[0]] = last[...].reshape(1, last.shape[0])
    skip = 3 * low - first
    n = high - low
    parts = three_to_four([square[pl.ds(skip + c, n, stride=3), :] for c in range(3)])
    for c in range(4):
        out[pl.ds(c, n, stride=4), :] = parts[c]


FIRST_SPANS = ((0, 98), (98, 392))
LAYER_SPANS = ((389, 681), (680, 972))
CONV_SPANS = ((971, 1620), (1620, GROUPS))


def prep_kernel(spans, params, *refs, last=None):
    outs, (flats, square, sems) = refs[: len(spans)], refs[-3:]
    for i, groups in enumerate(spans):
        copied(params, groups, flats[i], sems.at[i]).start()
    for i, groups in enumerate(spans):
        copied(params, groups, flats[i], sems.at[i]).wait()
        relay(groups, flats[i], outs[i], square, last if i == len(spans) - 1 else None)


def head_picks():
    width = HEAD_ROWS * WIDE
    place = iota((WIDE, width), 1) - HEAD_LANE
    row = iota((WIDE, width), 0)
    here = (place >= row * CLASSES) & (place < (row + 1) * CLASSES) & (row <= EMB)
    place = iota((width, WIDE), 0) - HEAD_LANE
    col = iota((width, WIDE), 1)
    row = lax.shift_right_logical(place * 4682, 16)
    there = (place - row * CLASSES == col) & (place >= 0)
    return jnp.where(here, 1.0, 0.0), jnp.where(there, 1.0, 0.0).astype(BF16)


def prep_conv_kernel(
    last, params, conv0, conv1, head, weights0, weights1, vectors, *scratch
):
    prep_kernel(CONV_SPANS, params, conv0, conv1, *scratch, last=last)
    tap_weights(conv0, 3, weights0)
    tap_weights(conv1, 0, weights1)
    vectors[0:1, :] = conv0[3 + TAP_ROWS : 4 + TAP_ROWS, :]
    vectors[1:4, :] = conv1[TAP_ROWS : TAP_ROWS + 3, :]
    vectors[4:8, :] = jnp.zeros((4, WIDE), F32)
    square = scratch[1]
    first, _ = span_of(CONV_SPANS[1])
    row = jnp.concatenate(
        [square[HEAD_ROW + i - first : HEAD_ROW + i - first + 1, :] for i in range(HEAD_ROWS)], 1
    )
    here, there = head_picks()
    hi, lo = split(here * row)
    head[...] = dot(hi, there) + dot(lo, there)


def head_rows(d_head, out, at):
    here, there = head_picks()
    hi, lo = split(d_head)
    spread = (dot_nt(hi, there) + dot_nt(lo, there)) * here
    row = colsum(spread)
    for i in range(HEAD_ROWS):
        out[at + i : at + i + 1, :] += row[:, i * WIDE : (i + 1) * WIDE]


class Rows:
    def __init__(self, ref, at):
        self.ref, self.at = ref, at

    def __getitem__(self, key):
        rows, lanes = key
        if isinstance(rows, slice):
            rows = slice(rows.start + self.at, rows.stop + self.at)
        else:
            rows = pl.ds(rows.start + self.at, rows.size, stride=rows.stride)
        return self.ref[rows, lanes]


def merged_norm(x):
    mean = jnp.sum(x, 1, keepdims=True) * (1.0 / MERGE)
    centred = x - mean
    var = jnp.sum(centred * centred, 1, keepdims=True) * (1.0 / MERGE)
    return centred * lax.rsqrt(var + eps_norm)


def first_kernel(
    feats, merge, lay0,
    dense, tok0, save, lse, mixed, middle, hpre, tok1, ahead, pa, pb, pc,
    *sc,
):
    dense[VOX:, :] = jnp.zeros((ROWS - VOX, MERGE), F32)
    for line in range(PLANE):
        dense[line * WIN : (line + 1) * WIN, :] = feats[line]
    hat = merged_norm(dense[...])
    normed = hat * hidden_rows(merge, 0, 1) + hidden_rows(merge, 4, 1)
    tokens = mm(normed, merge[8 : 8 + MERGE, :])
    tok0[...] = tokens
    layer = Rows(lay0, 0)
    normed = norm(tokens, layer[0:1, :], layer[1:2, :])
    attended = attention(normed, layer, save, lse, mixed, sc)
    mid = tokens + attended
    middle[...] = mid
    tokens = mlp(mid, layer, hpre)
    tok1[...] = tokens
    ahead[...] = norm(tokens, layer[1165:1166, :], layer[1166:1167, :])
    send_parts(ahead, pa, pb, pc)


def shifted_kernel(
    sizes,
    own, pa, pb, pc, lay1,
    window, save, lse, mixed, out, qa, qb, qc,
    region, *sc,
):
    put_region(region, sizes)
    take_parts(own, pa, pb, pc, window)
    out[...] = attention(
        window[...], Rows(lay1, 1), save, lse, mixed, sc, region
    )
    send_parts(out, qa, qb, qc)


def to_lines(ref, out):
    for line in range(PLANE):
        out[line, 0:WIN, :] = ref[line * WIN : (line + 1) * WIN, :]
        out[line, WIN:8, :] = jnp.zeros((8 - WIN, WIDE), F32)


def from_lines(ref, out):
    out[VOX:, :] = jnp.zeros((ROWS - VOX, WIDE), F32)
    for line in range(PLANE):
        out[line * WIN : (line + 1) * WIN, :] = ref[line, 0:WIN, :]


def send_sides(lines, near_d, far_d, near_h, far_h):
    odd_d = jnp.bitwise_and(lax.axis_index("slab"), 1) == 1
    odd_h = jnp.bitwise_and(lax.axis_index("mp"), 1) == 1
    low, high = lines[0 : 2 * WIN], lines[(WIN - 2) * WIN : PLANE]
    near_d[...] = jnp.where(odd_d, low, high)
    far_d[...] = jnp.where(odd_d, high, low)
    for d in range(WIN):
        low = lines[d * WIN : d * WIN + 2]
        high = lines[d * WIN + WIN - 2 : (d + 1) * WIN]
        near_h[2 * d : 2 * d + 2] = jnp.where(odd_h, low, high)
        far_h[2 * d : 2 * d + 2] = jnp.where(odd_h, high, low)


def second_kernel(
    tok1, own, qa, qb, qc, lay1, lay2, _,
    mid1, hpre1, tok2, save, lse, mixed, mid2, hpre2, lines,
    s0, s1, s2, s3,
    attended, *sc,
):
    take_parts(own, qa, qb, qc, attended)
    mid = tok1[...] + attended[...]
    mid1[...] = mid
    tokens = mlp(mid, Rows(lay1, 1), hpre1)
    tok2[...] = tokens
    layer = Rows(lay2, 2)
    normed = norm(tokens, layer[0:1, :], layer[1:2, :])
    mid = tokens + attention(normed, layer, save, lse, mixed, sc)
    mid2[...] = mid
    attended[...] = mlp(mid, layer, hpre2)
    to_lines(attended, lines)
    send_sides(lines, s0, s1, s2, s3)


def grown_lines(sizes, own, near_d, far_d, near_h, far_h, out):
    slab, row = lax.axis_index("slab"), lax.axis_index("mp")
    odd_d = jnp.bitwise_and(slab, 1) == 1
    odd_h = jnp.bitwise_and(row, 1) == 1
    out[:, 11:12] = jnp.zeros((11, 1, 8, WIDE), F32)
    for d in range(WIN):
        out[d + 2, 2 : 2 + WIN] = own[d * WIN : (d + 1) * WIN]
    for d in range(2):
        near = near_d[d * WIN : (d + 1) * WIN]
        far = far_d[d * WIN : (d + 1) * WIN]
        out[d, 2 : 2 + WIN] = jnp.where(odd_d, near, jnp.where(slab == 0, 0.0, far))
        out[d + 9, 2 : 2 + WIN] = jnp.where(
            odd_d, jnp.where(slab == sizes[0] - 1, 0.0, far), near
        )
    for d in range(11):
        near = near_h[2 * d : 2 * d + 2]
        far = far_h[2 * d : 2 * d + 2]
        out[d, 0:2] = jnp.where(odd_h, near, jnp.where(row == 0, 0.0, far))
        out[d, 9:11] = jnp.where(odd_h, jnp.where(row == sizes[1] - 1, 0.0, far), near)


def put_marks(labels, valid, out):
    across = iota((8, WIN), 1) == iota((8, WIN), 0)
    classes = iota((8, WIDE), 1) - EMB
    for d in range(WIN):
        code = jnp.where(valid[d] == 1, labels[d], -1 - EMB - WIDE)
        code = code.astype(F32)
        for h in range(WIN):
            line = jnp.where(across, code[h : h + 1, :], 0.0)
            column = jnp.sum(line, 1, keepdims=True)
            mark = jnp.where(column == classes.astype(F32), 1.0, 0.0)
            out[d * WIN + h] = jnp.where(iota((8, WIDE), 0) < WIN, mark, 0.0)


def taps(source, first_plane, planes, first_line, lines, out):
    def per_plane(d, carry):
        for c in range(3):
            for b in range(3):
                x = source[d + first_plane, first_line + b : first_line + b + lines]
                if c != 1:
                    x = roll(x, 1 if c == 0 else 7, 1)
                x = pair(x.reshape(lines * 8, WIDE))
                at = pl.multiple_of(d * (lines * 8), lines * 8)
                t = b * 3 + c
                out[pl.ds(at, lines * 8), t * 256 : (t + 1) * 256] = x
        return carry

    lax.fori_loop(0, planes, per_plane, 0)


def tap_weights(ref, at, out):
    def per_tap(i, carry):
        w = deep(ref[pl.ds(i * EMB + at, EMB), :])
        out[pl.ds(pl.multiple_of(i * 256, 256), 256), :] = weight_nn(w)
        return carry

    lax.fori_loop(0, 27, per_tap, 0)


def tap_weights_back(ref, at, out):
    for i in range(27):
        w = deep(ref[(26 - i) * EMB + at : (27 - i) * EMB + at, :])
        out[:, i * 256 : (i + 1) * 256] = weight_nt(w)


def conv(side, weights, planes, pitch, at_once, put, back=False):
    rows = at_once * pitch
    for start in range(0, planes, at_once):
        total = None
        for a in range(3):
            low = (start + a) * pitch
            x = side[low : low + rows, :]
            if back:
                part = dot_nt(x, weights[:, a * 2304 : (a + 1) * 2304])
            else:
                part = dot(x, weights[a * 2304 : (a + 1) * 2304, :])
            total = part if total is None else total + part
        put(start, fold(total))


def conv_weight_grad(side, grad_rows, pitch, out, at):
    rows = 512
    g = jnp.concatenate([grad_rows, jnp.zeros((rows - grad_rows.shape[0], WIDE), F32)], 0)
    left = jnp.concatenate(split(g.T[:EMB]), 0)
    for a in range(3):
        for bc in range(9):
            y = dot(left, side[a * pitch : a * pitch + rows, bc * 256 : (bc + 1) * 256])
            y = deep(fold_rows(fold(y))).T
            t = a * 9 + bc
            out[at + t * EMB : at + (t + 1) * EMB, :] = y[:EMB]


def volume_mask(sizes, planes, lines, reach, real_lines):
    slab, row = lax.axis_index("slab"), lax.axis_index("mp")
    ends = (slab == 0, slab == sizes[0] - 1, row == 0, row == sizes[1] - 1)
    shape = (planes, lines, 8, WIDE)
    d, h, w = iota(shape, 0), iota(shape, 1), iota(shape, 2)
    low_d = jnp.where(ends[0], reach, 0)
    high_d = jnp.where(ends[1], planes - reach, planes)
    low_h = jnp.where(ends[2], reach, 0)
    high_h = jnp.where(ends[3], real_lines - reach, real_lines)
    inside = (d >= low_d) & (d < high_d) & (h >= low_h) & (h < high_h) & (w < WIN)
    return jnp.where(inside, 1.0, 0.0)


def conv_kernel(
    sizes,
    own, s0, s1, s2, s3, labels, valid, weights0, weights1, vectors,
    grown, pre, tok, stats, t0, t1, t2, t3,
    act, side, side_own, marks,
):
    grown_lines(sizes, own, s0, s1, s2, s3, grown)
    put_marks(labels, valid, marks)
    taps(grown, 0, 11, 0, 10, side)
    bias0 = vectors[0:1, :]
    inside = volume_mask(sizes, 9, 10, 1, 9)


    def put(start, y):
        z = (y + bias0).reshape(3, 10, 8, WIDE)
        pre[start : start + 3] = z
        act[start : start + 3] = gelu(z) * inside[start : start + 3]

    conv(side, weights0, 9, 80, 3, put)
    taps(act, 0, 9, 0, 8, side_own)
    bias1 = vectors[1:2, :]
    sums = []

    def put_own(start, y):
        y = (y + bias1).reshape(WIN, 8, 8, WIDE)[:, 0:WIN]
        y = y + own[...].reshape(WIN, WIN, 8, WIDE)
        y = jnp.where(iota(y.shape, 2) < WIN, y, 0.0).reshape(PLANE, 8, WIDE)
        tok[...] = y + marks[...]
        send_sides(tok, t0, t1, t2, t3)
        flat = y.reshape(PLANE * 8, WIDE)
        sums.append(colsum(flat))
        sums.append(colsum(flat * flat))

    conv(side_own, weights1, WIN, 64, WIN, put_own)
    count = jnp.sum(marks[...].reshape(PLANE * 8, WIDE))
    row = iota((8, WIDE), 0)
    stats[...] = (
        jnp.where(row == 0, sums[0], 0.0)
        + jnp.where(row == 1, sums[1], 0.0)
        + jnp.where(row == 2, count, 0.0)
    )


def head_kernel(
    sizes, voxels,
    own, s0, s1, s2, s3, sums, vectors, head_w,
    grown, slope_out, stats, d_head, d_rows,
):
    grown_lines(sizes, own, s0, s1, s2, s3, grown)
    rows = 11 * 12 * 8
    both = grown[...].reshape(rows, WIDE)
    lane = iota((rows, WIDE), 1)
    tokens = jnp.where(lane < EMB, both, 0.0)
    target = jnp.where(lane < CLASSES, roll(both, WIDE - EMB, 1), 0.0)
    live = jnp.sum(target, 1, keepdims=True)
    count = F32(voxels)
    average = sums[0:1, :] / count
    spread = sums[1:2, :] / count - average * average
    inv = lax.rsqrt(spread + eps_norm)
    gain = vectors[2:3, :]
    bias = vectors[3:4, :]
    hat = (tokens - average) * inv
    act, slope = gelu_both(hat * gain + bias)
    act = jnp.where(lane == EMB, 1.0, act)
    w = head_w[...]
    logits = mm(act, w)
    logits = jnp.where(lane < CLASSES, logits, -1e30)
    top = jnp.max(logits, 1, keepdims=True)
    e = jnp.exp(logits - top)
    total = jnp.sum(e, 1, keepdims=True)
    logp = logits - top - jnp.log(total)
    scale = 1.0 / sums[2:3, 0:1]
    d_logits = (e / total * live - target) * scale
    d_normed = jnp.where(lane < EMB, mm_nt(d_logits, w) * slope, 0.0)
    d_tokens = d_normed * gain * inv
    slope_out[...] = d_tokens.reshape(11, 12, 8, WIDE)

    def own_rows(x):
        x = x.reshape(11, 12, 8, WIDE)[2:9, 2:9]
        x = jnp.where(iota(x.shape, 2) < WIN, x, 0.0)
        return x.reshape(PLANE * 8, WIDE)

    loss = -jnp.sum(own_rows(target * jnp.where(lane < CLASSES, logp, 0.0)))
    own_d = own_rows(d_logits)
    own_n = own_rows(d_normed)
    own_hat = own_rows(hat)
    zeros = jnp.zeros((512 - PLANE * 8, WIDE), F32)
    left = rows_t(jnp.concatenate([own_d, zeros], 0))
    d_head[...] = mm_tn(left, jnp.concatenate([own_rows(act), zeros], 0)).T
    d_gain = colsum(own_n * own_hat)
    d_bias = colsum(own_n)
    d_average = -d_bias * gain * inv
    d_spread = d_gain * gain * inv * inv * -0.5
    d_two = d_spread / count
    d_one = (d_average - 2.0 * average * d_spread) / count
    row = iota((8, WIDE), 0)
    live_lane = iota((8, WIDE), 1) < EMB
    stats[...] = (
        jnp.where((row == 0) & live_lane, d_one, 0.0)
        + jnp.where((row == 1) & live_lane, d_two, 0.0)
        + jnp.where(row == 2, loss, 0.0)
    )
    d_rows[...] = (
        jnp.where(row == 0, d_gain, 0.0)
        + jnp.where(row == 1, d_bias, 0.0)
    )


def sides_back_kernel(sizes, grown, pre, side_act, side_grown, act):
    act[0:9] = gelu(pre[...]) * volume_mask(sizes, 9, 10, 1, 9)
    act[9:10] = jnp.zeros((1, 10, 8, WIDE), F32)
    taps(act, 0, 10, 0, 8, side_act)
    taps(grown, 1, 10, 1, 8, side_grown)


def weights_back_kernel(conv0, conv1, weights0, weights1):
    tap_weights_back(conv0, 3, weights0)
    tap_weights_back(conv1, 0, weights1)


def conv_back_kernel(
    sizes,
    tok, slope, sums, pre, side_act, side_grown, weights0, weights1, d_rows, d_head,
    d_own, keep, send, carry, seam,
    grads, dgrown, act, side, side_own, flat,
):
    lane = iota((11, 12, 8, WIDE), 3)
    inside = volume_mask(sizes, 11, 12, 2, 11)
    steady = sums[0:1, :].reshape(1, 1, 1, WIDE)
    rising = 2.0 * sums[1:2, :].reshape(1, 1, 1, WIDE)
    d_tok = slope[...] + jnp.where(lane < EMB, (steady + tok[...] * rising) * inside, 0.0)
    dgrown[...] = d_tok
    grads[5191:, :] = jnp.zeros((45, WIDE), F32)
    grads[0:8, :] = jnp.zeros((8, WIDE), F32)
    grads[5189:5191, :] = d_rows[0:2, :]
    own = dgrown[2:9, 2:10]
    line = iota(own.shape, 1)
    own = jnp.where(line < WIN, own, 0.0).reshape(WIN * 64, WIDE)
    grads[5188:5189, :] = colsum(own)

    near = volume_mask(sizes, 9, 10, 1, 9)
    conv_weight_grad(side_act, own, 64, grads, 2596)
    taps(dgrown, 0, 11, 0, 10, side)


    def put(start, y):
        _, s = gelu_both(pre[start : start + 3])
        act[start : start + 3] = y.reshape(3, 10, 8, WIDE) * s * near[start : start + 3]

    conv(side, weights1, 9, 80, 3, put, back=True)

    own = act[1:8, 1:9]
    line = iota(own.shape, 1)
    own = jnp.where(line < WIN, own, 0.0).reshape(WIN * 64, WIDE)
    grads[2595:2596, :] = colsum(own)
    conv_weight_grad(side_grown, own, 64, grads, 3)
    carry[...] = grads[0:24, :]
    flat[3 * (GROUPS - CUTS[3]) :, :] = jnp.zeros((flat.shape[0] - 3912, WIDE), F32)
    flatten(grads, 20, GROUPS - CUTS[3], flat)
    start = 3 * CUTS[3]
    head_rows(d_head[...], flat, HEAD_ROW - start)
    seam[...] = flat[0 : LATE_ROWS - start, :]
    scatter(sizes, flat, LATE_ROWS - start, keep, send)
    taps(act, 0, 9, 0, 8, side_own)

    def put_own(start, y):
        y = y.reshape(WIN, 8, 8, WIDE)[:, 0:WIN] + dgrown[2:9, 2:9]
        y = jnp.where(iota(y.shape, 2) < WIN, y, 0.0)
        d_own[...] = y.reshape(PLANE, 8, WIDE)

    conv(side_own, weights0, WIN, 64, WIN, put_own, back=True)


def back_mlp_kernel(d_own, lay2, mid2, hpre2, d_mid, grads, dense):
    from_lines(d_own, dense)
    grads[...] = jnp.zeros_like(grads)
    d_mid[...] = mlp_back(dense[...], mid2[...], hpre2, Rows(lay2, 2), grads, 2)


def back_two_kernel(
    d_mid2, grads2, carry, lay1, lay2, tok2, save, lse, mixed, mid1, hpre1,
    d_mid, grads1, flat, carry2, pa, pb, pc,
    grads, *sc,
):
    layer = Rows(lay2, 2)
    grads[0:1168, :] = grads2[...]
    d = d_mid2[...]
    tokens = tok2[...]
    normed = norm(tokens, layer[0:1, :], layer[1:2, :])
    d_normed = attention_back(d, normed, layer, save, lse, mixed, sc, grads, 2)
    d = d + pre_norm_back(d_normed, tokens, layer, grads, 2)
    grads[1167:1184, :] = carry[3:20, :]
    flatten(grads, 32, CUTS[3] - CUTS[2], flat)
    carry2[...] = grads[0:32, :]
    layer = Rows(lay1, 1)
    d = mlp_back(d, mid1[...], hpre1, layer, grads1, 1)
    d_mid[...] = d
    send_parts(d_mid, pa, pb, pc)


def back_shifted_kernel(
    sizes,
    own, pa, pb, pc, lay1, window, save, lse, mixed, grads1, carry2, _,
    d_window, flat, carry1, qa, qb, qc,
    region, grads, grad, *sc,
):
    put_region(region, sizes)
    take_parts(own, pa, pb, pc, grad)
    grads[0:1168, :] = grads1[...]
    grads[0:3, :] = jnp.zeros((3, WIDE), F32)
    d_window[...] = attention_back(
        grad[...], window[...], Rows(lay1, 1), save, lse, mixed, sc, grads, 1,
        region,
    )
    send_parts(d_window, qa, qb, qc)
    grads[1166:1196, :] = carry2[2:32, :]
    flatten(grads, 12, CUTS[2] - CUTS[1], flat)
    carry1[...] = grads[0:16, :]


def back_first_kernel(
    sizes,
    d_mid, own, qa, qb, qc, tok1, lay0, lay1, merge, dense, tok0, save, lse, mixed, middle, hpre,
    carry1, flat1, flat2, seam, _,
    keep, send,
    flat, grads, grad, *sc,
):
    take_parts(own, qa, qb, qc, grad)
    grads[1556:1572, :] = carry1[...]
    d = d_mid[...] + pre_norm_back(grad[...], tok1[...], Rows(lay1, 1), grads, 1557)
    layer = Rows(lay0, 0)
    at = MERGE_ROWS
    d = mlp_back(d, middle[...], hpre, layer, grads, at)
    tokens = tok0[...]
    normed = norm(tokens, layer[0:1, :], layer[1:2, :])
    d_normed = attention_back(d, normed, layer, save, lse, mixed, sc, grads, at)
    d = d + pre_norm_back(d_normed, tokens, layer, grads, at)
    live = iota((ROWS, WIDE), 0) < VOX
    d = jnp.where(live, d, 0.0)
    hat = merged_norm(dense[...])
    gain = hidden_rows(merge, 0, 1)
    bias = hidden_rows(merge, 4, 1)
    w = merge[8 : 8 + MERGE, :]
    put_hidden_rows(grads, 8 - 8, 1, jnp.zeros((1, MERGE), F32))
    grads[8 : 8 + MERGE, :] = mm_tn(rows_t(d), hat * gain + bias).T
    d_hat = mm_nt(d, w)
    put_hidden_rows(grads, 0, 1, colsum(d_hat * hat))
    put_hidden_rows(grads, 4, 1, colsum(d_hat))
    flatten(grads, 0, CUTS[1], flat)
    at = 0
    for cut, part in ((CUTS[1], flat1), (CUTS[2], flat2), (CUTS[3], seam)):
        at = 3 * cut
        flat[at : at + part.shape[0], :] = part[...]
    at += seam.shape[0]
    if flat.shape[0] > at:
        flat[at:, :] = jnp.zeros((flat.shape[0] - at, WIDE), F32)
    scatter(sizes, flat, 0, keep, send)


def radices(count):
    steps = [2]
    left = count // 2
    while left > 1:
        steps.append(4 if left >= 4 else 2)
        left //= steps[-1]
    return steps


def block_rows(rows, count):
    return -(-rows // (8 * count)) * 8


def own_number(sizes):
    return lax.axis_index("slab") * sizes[1] + lax.axis_index("mp")


def place_in_half(distance, count):
    place = 0
    shift = 1
    for radix in radices(count)[1:]:
        digit = jnp.bitwise_and(lax.shift_right_logical(distance, shift), radix - 1)
        place = place * radix + digit
        shift += radix.bit_length() - 1
    return place


def scatter(sizes, source, first, keep, send):
    count = sizes[0] * sizes[1]
    rows = keep.shape[0] * 2 // count
    me = own_number(sizes)
    odd = jnp.bitwise_and(me, 1)

    def per_pair(t, carry):
        for block, out in ((2 * t + odd, keep), (2 * t + 1 - odd, send)):
            place = place_in_half(jnp.bitwise_xor(block, me), count)
            at = pl.multiple_of(first + block * rows, 8)
            to = pl.multiple_of(place * rows, 8)
            out[pl.ds(to, rows), :] = source[pl.ds(at, rows), :]
        return carry

    lax.fori_loop(0, count // 2, per_pair, 0)


def traded(value, distance, count):
    pairs = [(i, i ^ distance) for i in range(count)]
    return lax.ppermute(value, ("slab", "mp"), pairs)


def later(got, after):
    return got if after is None else list(lax.optimization_barrier((*got, after)))[:-1]


def summing(keep, send, count):
    steps = radices(count)
    got = [keep, traded(send, 1, count)]
    shift = 1
    after = yield None
    for radix in steps[1:]:
        got = later(got, after)
        total = sum(got[1:], got[0])
        rows = total.shape[0] // radix
        parts = [total[k * rows : (k + 1) * rows] for k in range(radix)]
        got = parts[:1] + [traded(parts[k], k << shift, count) for k in range(1, radix)]
        shift += radix.bit_length() - 1
        after = yield parts[0]
    got = later(got, after)
    own = sum(got[1:], got[0])
    for radix in reversed(steps[1:]):
        shift -= radix.bit_length() - 1
        got = [own] + [traded(own, k << shift, count) for k in range(1, radix)]
        after = yield own
        own = jnp.concatenate(later(got, after), 0)
        yield own
    yield own, traded(own, 1, count)


def finished(chain, after=None):
    last = next(chain) if after is None else chain.send(after)
    while not isinstance(last, tuple):
        last = next(chain)
    return last


def exchanged_sum(value, count):
    shift = 0
    for radix in radices(count):
        got = [value] + [traded(value, k << shift, count) for k in range(1, radix)]
        while len(got) > 1:
            got = [got[i] + got[i + 1] for i in range(0, len(got), 2)]
        value = got[0]
        shift += radix.bit_length() - 1
    return value


PIECE = 262144


def adamw_kernel(
    sizes,
    late, late_other, early, early_other, tail, sums, params, first, second,
    new_params, new_first, new_second, loss, valid, norm_out,
    grad, scale_ref,
):
    count = sizes[0] * sizes[1]
    step = pl.program_id(0)

    @pl.when(step == 0)
    def gather():
        me = own_number(sizes)
        total = jnp.zeros((8, WIDE), F32)
        for ref in (late, late_other, early, early_other):
            x = ref[...]
            total = total + jnp.sum((x * x).reshape(-1, 8, WIDE), 0)
        norm = jnp.sqrt(jnp.sum(total))
        loss[0] = jnp.sum(tail[2:3, 0:1])
        valid[0] = jnp.sum(sums[2:3, 0:1])
        norm_out[0] = norm
        scale_ref[0] = jnp.minimum(1.0, clip_norm / (norm + 1e-06))
        start = 0
        for own, other, size in ((late, late_other, LATE_ROWS), (early, early_other, EARLY_ROWS)):
            rows = own.shape[0] * 2 // count

            def per_block(block, carry, own=own, other=other, rows=rows, start=start):
                distance = jnp.bitwise_xor(block, me)
                at = pl.ds(pl.multiple_of(place_in_half(distance, count) * rows, 8), rows)
                near = jnp.bitwise_and(distance, 1) == 0
                to = pl.ds(pl.multiple_of(start + block * rows, 8), rows)
                grad[to, :] = jnp.where(near, own[at, :], other[at, :])
                return carry

            lax.fori_loop(0, size // rows, per_block, 0)
            start += size

    def update(base, low, size):
        rows = -(-size // 1024) * 8
        at = pl.ds(pl.multiple_of(base // WIDE + low // WIDE, 8), rows)
        g = grad[at, :].reshape(rows * WIDE)[:size] * scale_ref[0]
        here = pl.ds(pl.multiple_of(base + low, 1024), size)
        one = beta_one * first[here] + (1.0 - beta_one) * g
        two = beta_two * second[here] + (1.0 - beta_two) * g * g
        there = pl.ds(low, size)
        new_first[there] = one
        new_second[there] = two
        two = two * (1.0 / (1.0 - beta_two**STEP))
        low_by = two * lax.rsqrt(jnp.maximum(two, 1e-37)) + adam_eps
        inverse = pl.reciprocal(low_by, approx=True)
        inverse = inverse * (2.0 - low_by * inverse)
        new_params[there] = params[here] * (1.0 - learn_rate * decay_rate) - (
            one * (learn_rate / (1.0 - beta_one**STEP))
        ) * inverse

    whole = NPARAM // PIECE

    @pl.when(step < whole)
    def full():
        def part(i, carry):
            low = pl.multiple_of(i * 16384, 16384)
            update(step * PIECE, low, 16384)
            return carry

        lax.fori_loop(0, PIECE // 16384, part, 0)

    @pl.when(step == whole)
    def last():
        rest = NPARAM - whole * PIECE
        main = rest // 1024 * 1024
        for low in range(0, main, 16384):
            update(whole * PIECE, low, min(16384, main - low))
        update(whole * PIECE, main, rest - main)


def adamw(sizes, parts, arrays):
    pieces = -(-NPARAM // PIECE)
    piece = pl.BlockSpec((PIECE,), lambda i: (i,))
    vmem = pl.BlockSpec(memory_space=pltpu.VMEM)
    smem = pl.BlockSpec(memory_space=pltpu.SMEM)
    return pl.pallas_call(
        functools.partial(adamw_kernel, sizes),
        grid=(pieces,),
        out_shape=[arr(NPARAM)] * 3 + [arr(1)] * 3,
        in_specs=[vmem] * (len(parts) + len(arrays)),
        out_specs=[piece] * 3 + [smem] * 3,
        scratch_shapes=[pltpu.VMEM((LATE_ROWS + EARLY_ROWS, WIDE), F32), pltpu.SMEM((1,), F32)],
        compiler_params=pltpu.CompilerParams(vmem_limit_bytes=16 * 1024 * 1024),
        cost_estimate=pl.CostEstimate(flops=6 * 10**9, bytes_accessed=0, transcendentals=0),
        name="adamw",
    )(*parts, *arrays)


def arr(*shape):
    return jax.ShapeDtypeStruct(shape, F32)


def call(kernel, outs, scratch, *args, name=None, us=1.0, far=(), mib=16):
    vmem = pl.BlockSpec(memory_space=pltpu.VMEM)
    smem = pl.BlockSpec(memory_space=pltpu.SMEM)
    return pl.pallas_call(
        kernel,
        out_shape=list(outs),
        in_specs=[vmem] * len(args) + [pl.BlockSpec(memory_space=pl.ANY)] * len(far),
        out_specs=[smem if o.shape == (1,) else vmem for o in outs],
        scratch_shapes=list(scratch),
        compiler_params=pltpu.CompilerParams(vmem_limit_bytes=mib * 1024 * 1024),
        cost_estimate=pl.CostEstimate(
            flops=int(us * 1.15e9), bytes_accessed=0, transcendentals=0
        ),
        name=name,
    )(*args, *far)


SQUARE = arr(ROWS, WIDE)
SAVE = arr(ROWS, 3 * WIDE)
FORWARD = [
    pltpu.VMEM((2, ROWS, 2 * WIDE), BF16),
    pltpu.VMEM((2, ROWS, 2 * WIDE), BF16),
    pltpu.VMEM((2 * ROWS, 2 * WIDE), BF16),
]
BACKWARD = [
    pltpu.VMEM((2, ROWS, 2 * WIDE), BF16),
    pltpu.VMEM((2, ROWS, 2 * WIDE), BF16),
    pltpu.VMEM((2, ROWS, 2 * WIDE), BF16),
    pltpu.VMEM((2, ROWS, 2 * WIDE), BF16),
    pltpu.VMEM((2 * ROWS, 2 * WIDE), BF16),
    pltpu.VMEM((ROWS, WIDE), F32),
    pltpu.VMEM((2, WIDE, ROWS), F32),
    pltpu.VMEM((2, ROWS, 2 * ROWS), BF16),
    pltpu.VMEM((2, ROWS, 2 * ROWS), BF16),
    pltpu.VMEM((2, WIDE, ROWS), BF16),
    pltpu.VMEM((2, WIDE, ROWS), BF16),
    pltpu.VMEM((ROWS, WIDE), F32),
    pltpu.VMEM((ROWS, 2 * ROWS), F32),
    pltpu.VMEM((ROWS, 2 * ROWS), F32),
    pltpu.VMEM((2 * ROWS, 2 * WIDE), BF16),
    pltpu.VMEM((2 * ROWS, 2 * WIDE), BF16),
]
PARTS = [arr(ROWS_A, WIDE), arr(ROWS_B, WIDE), arr(ROWS_C, WIDE)]


def passed(parts, steps, sizes):
    slabs, rows = sizes
    moved = []
    for part, (ds, dm) in zip(parts, ((1, 0), (0, 1), (1, 1))):
        pairs = []
        for s in range(slabs):
            for m in range(rows):
                target = ((s + steps * ds) % slabs) * rows + (m + steps * dm) % rows
                pairs.append((s * rows + m, target))
        moved.append(lax.ppermute(part, ("slab", "mp"), pairs))
    return moved


SIDES = [arr(2 * WIN, 8, WIDE)] * 4


def paired(axis, size):
    near = [(i, i ^ 1) for i in range(size)]
    far = [(i, min(max(i + 1 if i % 2 else i - 1, 0), size - 1)) for i in range(size)]
    return (
        lambda value: lax.ppermute(value, axis, near),
        lambda value: lax.ppermute(value, axis, far),
    )


def beside(sides, sizes):
    near_d, far_d, near_h, far_h = sides
    slab, row = lax.axis_index("slab"), lax.axis_index("mp")
    odd_d, odd_h = jnp.bitwise_and(slab, 1) == 1, jnp.bitwise_and(row, 1) == 1
    near, far = paired("slab", sizes[0])
    near_d, far_d = near(near_d), far(far_d)
    before = jnp.where(odd_d, near_d, jnp.where(slab == 0, 0.0, far_d))
    after = jnp.where(odd_d, jnp.where(slab == sizes[0] - 1, 0.0, far_d), near_d)

    def column(own, low):
        ends = []
        for x in (before, after):
            x = x.reshape(2, WIN, 8, WIDE)
            x = jnp.where(low, x[:, 0:2], x[:, WIN - 2 :])
            ends.append(x.reshape(4, 8, WIDE))
        return jnp.concatenate([ends[0], own, ends[1]], 0)

    near, far = paired("mp", sizes[1])
    near_h = near(column(near_h, odd_h))
    far_h = far(column(far_h, jnp.logical_not(odd_h)))
    return near_d, far_d, near_h, far_h


REGION = [pltpu.VMEM((ROWS, ROWS), F32)]


def on_device(sizes, feats, labels, valid, params, moment_one, moment_two):
    slabs, rows = sizes
    count = slabs * rows

    def room(spans):
        sizes = [(span_of(groups)[1] + 8) * WIDE for groups in spans]
        return [
            [pltpu.VMEM((size,), F32) for size in sizes],
            pltpu.VMEM((2048, WIDE), F32),
            pltpu.SemaphoreType.DMA((len(spans),)),
        ]

    first_size = FIRST_SPANS[-1][1] * 384
    merge, lay0 = call(
        functools.partial(prep_kernel, FIRST_SPANS),
        [arr(MERGE_ROWS, WIDE), arr(1176, WIDE)],
        room(FIRST_SPANS),
        name="prep_first", us=2.0, far=(params[:first_size],),
    )
    lay1, lay2 = call(
        functools.partial(prep_kernel, LAYER_SPANS),
        [arr(1168, WIDE)] * 2,
        room(LAYER_SPANS),
        name="prep_layers", us=2.0, far=(params,),
    )
    conv0, conv1, head_w, weights0, weights1, vectors = call(
        prep_conv_kernel,
        [arr(2596, WIDE), arr(2640, WIDE), arr(WIDE, WIDE)]
        + [jax.ShapeDtypeStruct((27 * 256, 256), BF16)] * 2
        + [arr(8, WIDE)],
        room(CONV_SPANS),
        params[NPARAM // WIDE * WIDE :],
        name="prep_conv", us=4.0, far=(params,),
    )

    dense, tok0, save0, lse0, mixed0, mid0, hpre0, tok1, ahead, *parts = call(
        first_kernel,
        [arr(ROWS, MERGE), SQUARE, SAVE, SQUARE, SQUARE, SQUARE, arr(ROWS, HID), SQUARE, SQUARE]
        + PARTS,
        FORWARD,
        feats.reshape(PLANE, WIN, MERGE), merge, lay0,
        name="first", us=6.0,
    )
    parts = passed(parts, -1, sizes)
    window, save1, lse1, mixed1, out1, *parts = call(
        functools.partial(shifted_kernel, sizes),
        [SQUARE, SAVE, SQUARE, SQUARE, SQUARE] + PARTS,
        REGION + FORWARD,
        ahead, *parts, lay1,
        name="shifted", us=4.5,
    )
    parts = passed(parts, 1, sizes)
    mid1, hpre1, tok2, save2, lse2, mixed2, mid2, hpre2, lines, *sides = call(
        second_kernel,
        [SQUARE, arr(ROWS, HID), SQUARE, SAVE, SQUARE, SQUARE, SQUARE, arr(ROWS, HID)]
        + [arr(PLANE, 8, WIDE)] + SIDES,
        [pltpu.VMEM((ROWS, WIDE), F32)] + FORWARD,
        tok1, out1, *parts, lay1, lay2,
        name="second", us=6.5, far=(weights0,),
    )
    sides = beside(sides, sizes)
    grown, pre, tok3, sums, *tok_sides = call(
        functools.partial(conv_kernel, sizes),
        [arr(11, 12, 8, WIDE), arr(9, 10, 8, WIDE), arr(PLANE, 8, WIDE), arr(8, WIDE)] + SIDES,
        [
            pltpu.VMEM((9, 10, 8, WIDE), F32),
            pltpu.VMEM((880, 2304), BF16),
            pltpu.VMEM((576, 2304), BF16),
            pltpu.VMEM((PLANE, 8, WIDE), F32),
        ],
        lines, *sides, labels, valid, weights0, weights1, vectors,
        name="conv", us=8.0, mib=20,
    )
    tok_sides = beside(tok_sides, sizes)
    side_act, side_grown = call(
        functools.partial(sides_back_kernel, sizes),
        [jax.ShapeDtypeStruct((640, 2304), BF16)] * 2,
        [pltpu.VMEM((10, 10, 8, WIDE), F32)],
        grown, pre,
        name="sides_back", us=2.0,
    )
    weights0, weights1 = call(
        weights_back_kernel,
        [jax.ShapeDtypeStruct((256, 27 * 256), BF16)] * 2,
        [],
        conv0, conv1,
        name="weights_back", us=1.5,
    )
    sums = exchanged_sum(sums, count)
    voxels = WIN * slabs * WIN * rows * WIN
    tok3, slope, tail, d_head, d_rows = call(
        functools.partial(head_kernel, sizes, voxels),
        [arr(11, 12, 8, WIDE), arr(11, 12, 8, WIDE), arr(8, WIDE), arr(WIDE, WIDE), arr(8, WIDE)],
        [],
        tok3, *tok_sides, sums, vectors, head_w,
        name="head", us=3.5,
    )
    tail = exchanged_sum(tail, count)
    late_rows = block_rows(LATE_ROWS, count) * count
    early_rows = block_rows(EARLY_ROWS, count) * count
    seam_rows = LATE_ROWS - 3 * CUTS[3]
    d_own, keep, send, carry3, seam = call(
        functools.partial(conv_back_kernel, sizes),
        [arr(PLANE, 8, WIDE)] + [arr(early_rows // 2, WIDE)] * 2
        + [arr(24, WIDE), arr(seam_rows, WIDE)],
        [
            pltpu.VMEM((5236, WIDE), F32),
            pltpu.VMEM((11, 12, 8, WIDE), F32),
            pltpu.VMEM((10, 10, 8, WIDE), F32),
            pltpu.VMEM((880, 2304), BF16),
            pltpu.VMEM((576, 2304), BF16),
            pltpu.VMEM((seam_rows + early_rows, WIDE), F32),
        ],
        tok3, slope, tail, pre, side_act, side_grown, weights0, weights1, d_rows, d_head,
        name="conv_back", us=14.0, mib=28,
    )
    early = summing(keep, send, count)
    next(early)
    d_mid2, grads2 = call(
        back_mlp_kernel,
        [SQUARE, arr(1168, WIDE)],
        [pltpu.VMEM((ROWS, WIDE), F32)],
        d_own, lay2, mid2, hpre2,
        name="back_mlp", us=3.0,
    )
    step = early.send(d_mid2)
    d_mid, grads1, flat2, carry2, *parts = call(
        back_two_kernel,
        [SQUARE, arr(1168, WIDE), arr(3 * (CUTS[3] - CUTS[2]), WIDE), arr(32, WIDE)] + PARTS,
        [pltpu.VMEM((1184, WIDE), F32)] + BACKWARD,
        d_mid2, grads2, carry3, lay1, lay2, tok2, save2, lse2, mixed2, mid1, hpre1,
        name="back_two", us=9.0,
    )
    parts = passed(parts, -1, sizes)
    step = early.send(d_mid)
    d_window, flat1, carry1, *parts = call(
        functools.partial(back_shifted_kernel, sizes),
        [SQUARE, arr(3 * (CUTS[2] - CUTS[1]), WIDE), arr(16, WIDE)] + PARTS,
        REGION + [pltpu.VMEM((1200, WIDE), F32), pltpu.VMEM((ROWS, WIDE), F32)] + BACKWARD,
        d_mid, *parts, lay1, window, save1, lse1, mixed1, grads1, carry2,
        name="back_shifted", us=10.5, far=(step,),
    )
    early.send(d_window)
    parts = passed(parts, 1, sizes)
    next(early)
    step = next(early)
    late = call(
        functools.partial(back_first_kernel, sizes),
        [arr(late_rows // 2, WIDE)] * 2,
        [
            pltpu.VMEM((late_rows, WIDE), F32),
            pltpu.VMEM((1572, WIDE), F32),
            pltpu.VMEM((ROWS, WIDE), F32),
        ]
        + BACKWARD,
        d_mid, d_window, *parts, tok1, lay0, lay1, merge, dense, tok0, save0, lse0, mixed0, mid0,
        hpre0, carry1, flat1, flat2, seam,
        name="back_first", us=13.5, far=(step,),
    )
    step = early.send(late[0])
    keep, send = later(list(late), step)
    late_sum = finished(summing(keep, send, count))
    early = finished(early)
    new_params, new_first, new_second, loss, valid_count, norm = adamw(
        sizes, (*late_sum, *early, tail, sums), (params, moment_one, moment_two)
    )
    return (
        loss.reshape(()), valid_count.reshape(()), norm.reshape(()),
        new_params, new_first, new_second,
    )


def solution(mesh):
    placed = (
        P("slab", "mp", None, None),
        P("slab", "mp", None),
        P("slab", "mp", None),
        P(),
        P(),
        P(),
    )
    sizes = (mesh.shape["slab"], mesh.shape["mp"])
    return jax.shard_map(
        functools.partial(on_device, sizes),
        mesh=mesh,
        in_specs=placed,
        out_specs=(P(), P(), P(), P(), P(), P()),
        check_vma=False,
    )
```

```python
import functools

import jax
import jax.numpy as jnp
from jax import lax
from jax.experimental import pallas as pl
from jax.experimental.pallas import tpu as pltpu
from jax.sharding import PartitionSpec as P

EMB = 96
HEADS = 6
HDIM = 16
HID = 384
MERGE = 384
CLASSES = 14
WIN = 7
SHIFT = 3
LAYERS = 3
STEP = 10

F32 = jnp.float32
BF16 = jnp.bfloat16
eps_norm = 1e-05
beta_one = 0.9
beta_two = 0.999
adam_eps = 1e-08
learn_rate = 0.05
decay_rate = 0.05
clip_norm = 0.01
LOG2E = 1.4426950408889634

VOX = WIN * WIN * WIN
ROWS = 384
BLK = 128
WIDE = 128
PLANE = WIN * WIN
FAR = WIN - SHIFT
ROWS_A = SHIFT * FAR * WIN
ROWS_B = FAR * SHIFT * WIN
ROWS_C = SHIFT * SHIFT * WIN

MERGE_ROWS = 392
LAYER_ROWS = 1165
TAP_ROWS = 27 * EMB
GROUPS = 2280
NPARAM = 872558
HEAD_ROW = 6806
HEAD_ROWS = 11
HEAD_LANE = 32
LATE_ROWS = 3072
EARLY_ROWS = 3840
LAYER_BASE = (98, 389, 680)
CONV_BASE = (971, 1620)
CUTS = (0, 392, 688, 976, 2280)

R_QKV, R_QKVB, R_PROJ, R_PROJB = 4, 292, 295, 391
R_HID, R_HIDB, R_OUT, R_OUTB = 392, 776, 780, 1164


def iota(shape, dim):
    return lax.broadcasted_iota(jnp.int32, shape, dim)


def split(x):
    hi = x.astype(BF16)
    return hi, (x - hi.astype(F32)).astype(BF16)


def pair(x):
    return jnp.concatenate(split(x), 1)


def fold(y):
    half = y.shape[1] // 2
    return y[:, :half] + y[:, half:]


def fold_rows(y):
    half = y.shape[0] // 2
    return y[:half] + y[half:]


def dot(a, b):
    return jnp.dot(a, b, preferred_element_type=F32)


def dot_nt(a, b):
    return lax.dot_general(a, b, (((1,), (1,)), ((), ())), preferred_element_type=F32)


def weight_nn(w):
    top = pair(w)
    return jnp.concatenate([top, top], 0)


def weight_nt(w):
    hi, lo = split(w)
    return jnp.concatenate(
        [jnp.concatenate([hi, hi], 1), jnp.concatenate([lo, lo], 1)], 0
    )


def mm(x, w):
    return fold(dot(pair(x), weight_nn(w)))


def mm_nt(x, w):
    return fold(dot_nt(pair(x), weight_nt(w)))


def rows_t(x):
    return jnp.concatenate(split(x.T), 0)


def mm_tn(xt, y):
    return fold_rows(fold(dot(xt, pair(y))))


def deep(w):
    return jnp.concatenate([w, jnp.zeros((WIDE - EMB, w.shape[1]), F32)], 0)


def roll(x, shift, axis):
    return pltpu.roll(x, shift, axis)


def four_to_three(y):
    lane = iota(y[0].shape, 1)
    a = jnp.where(lane < 96, y[0], roll(y[1], 96, 1))
    b = jnp.where(lane < 64, roll(y[1], 96, 1), roll(y[2], 64, 1))
    c = jnp.where(lane < 32, roll(y[2], 64, 1), roll(y[3], 32, 1))
    return a, b, c


def three_to_four(x):
    lane = iota(x[0].shape, 1)
    live = lane < EMB
    a = x[0]
    b = jnp.where(lane < 32, roll(x[0], 32, 1), roll(x[1], 32, 1))
    c = jnp.where(lane < 64, roll(x[1], 64, 1), roll(x[2], 64, 1))
    d = roll(x[2], 96, 1)
    return tuple(jnp.where(live, v, 0.0) for v in (a, b, c, d))


def hidden_rows(ref, start, count):
    return jnp.concatenate(
        four_to_three([ref[pl.ds(start + c, count, stride=4), :] for c in range(4)]), 1
    )


def put_hidden_rows(ref, start, count, x):
    parts = three_to_four([x[:, i * WIDE : (i + 1) * WIDE] for i in range(3)])
    for c in range(4):
        ref[pl.ds(start + c, count, stride=4), :] = parts[c]


def flatten(ref, start, groups, out):
    parts = four_to_three([ref[pl.ds(start + c, groups, stride=4), :] for c in range(4)])
    for c in range(3):
        out[pl.ds(c, groups, stride=3), :] = parts[c]


def norm_stats(x):
    live = iota(x.shape, 1) < EMB
    mean = jnp.sum(x, 1, keepdims=True) * (1.0 / EMB)
    centred = jnp.where(live, x - mean, 0.0)
    var = jnp.sum(centred * centred, 1, keepdims=True) * (1.0 / EMB)
    inv = lax.rsqrt(var + eps_norm)
    return centred * inv, inv


def norm(x, gain, bias):
    hat, _ = norm_stats(x)
    return hat * gain + bias


def norm_back(hat, inv, gain, grad):
    up = grad * gain
    one = jnp.sum(up, 1, keepdims=True) * (1.0 / EMB)
    two = jnp.sum(up * hat, 1, keepdims=True) * (1.0 / EMB)
    live = iota(hat.shape, 1) < EMB
    return jnp.where(live, inv * (up - one - hat * two), 0.0)


def colsum(x):
    return jnp.sum(x, 0, keepdims=True)


def gelu(x):
    return 0.5 * x * (1.0 + lax.erf(x * (0.5**0.5)))


def gelu_both(x):
    cdf = 0.5 * (1.0 + lax.erf(x * (0.5**0.5)))
    slope = cdf + x * (jnp.exp(x * x * -0.5) * 0.3989422804014327)
    return x * cdf, slope


def head_groups(x):
    lane = iota(x.shape, 1)
    swapped = roll(x, 64, 1)
    return jnp.where(lane < 64, x, swapped), jnp.where(lane < 64, swapped, x)


def as_left(x):
    both = []
    low = iota(x.shape, 1) < 64
    for part in head_groups(x):
        hi = part.astype(BF16).astype(F32)
        one = jnp.where(low, hi, part - hi).astype(BF16)
        both.append(jnp.concatenate([one, one], 1))
    return both


def as_right(x):
    return [pair(part) for part in head_groups(x)]


def head_mask(h, width):
    lane = iota((1, width), 1)
    lane = jnp.bitwise_and(lane, 63)
    low = jnp.bitwise_and(h, 3) * HDIM
    return jnp.where((lane >= low) & (lane < low + HDIM), 1.0, 0.0)


def own_lanes(h):
    lane = iota((1, WIDE), 1)
    return jnp.where((lane >= h * HDIM) & (lane < (h + 1) * HDIM), 1.0, 0.0)


def both_heads(right, heads, out):
    for k, h in enumerate(heads):
        out[k * ROWS : (k + 1) * ROWS, :] = right * head_mask(h, 2 * WIDE).astype(BF16)


def score_tiles(s, rows, region):
    tiles = [s[:, i * WIDE : (i + 1) * WIDE] for i in range(3)]
    if region is not None:
        return [t + region[rows, i * WIDE : (i + 1) * WIDE] for i, t in enumerate(tiles)]
    pad = jnp.where(iota((1, WIDE), 1) < VOX - 2 * WIDE, 0.0, -1e30)
    return tiles[:2] + [tiles[2] + pad]


def put_split(ref, rows, i, x):
    hi, lo = split(x)
    ref[rows, i * WIDE : (i + 1) * WIDE] = hi
    ref[rows, ROWS + i * WIDE : ROWS + (i + 1) * WIDE] = lo


def attention(normed, layer, save, lse, mixed, sc, region=None):
    left, right, values = sc
    x = pair(normed)
    qkv = []
    for i in range(3):
        w = deep(layer[pl.ds(R_QKV + i, EMB, stride=3), :])
        y = fold(dot(x, weight_nn(w))) + layer[R_QKVB + i : R_QKVB + i + 1, :]
        if i == 0:
            y = y * (HDIM**-0.5 * LOG2E)
        save[:, i * WIDE : (i + 1) * WIDE] = y
        qkv.append(y)
    for g, part in enumerate(as_left(qkv[0])):
        left[g] = part
    for g, part in enumerate(as_right(qkv[1])):
        right[g] = part
    v = pair(jnp.where(iota((ROWS, WIDE), 1) == EMB, 1.0, qkv[2]))
    values[0:ROWS, :] = v
    values[ROWS : 2 * ROWS, :] = v
    mixed[...] = jnp.zeros_like(mixed)
    lse[...] = jnp.zeros_like(lse)

    def per_pair(pair_of, carry):
        heads = [2 * pair_of, 2 * pair_of + 1]
        masks = [head_mask(h, 2 * WIDE).astype(BF16) for h in heads]
        lanes = [own_lanes(h) for h in heads]
        spots = [jnp.where(iota((1, WIDE), 1) == h, 1.0, 0.0) for h in heads]
        g = lax.div(pair_of, 2)
        for b in range(ROWS // BLK):
            rows = slice(b * BLK, (b + 1) * BLK)
            out = level = 0.0
            for k in range(2):
                s = dot_nt(left[g, rows, :] * masks[k], right[g])
                tiles = score_tiles(s, rows, region)
                top = jnp.maximum(jnp.maximum(tiles[0], tiles[1]), tiles[2])
                top = jnp.max(top, 1, keepdims=True)
                parts = [split(jnp.exp2(t - top)) for t in tiles]
                e = jnp.concatenate([p[0] for p in parts] + [p[1] for p in parts], 1)
                o = fold(dot(e, values[...]))
                total = o[:, EMB : EMB + 1]
                out = out + o * (lanes[k] / total)
                level = level + (top + jnp.log(total) * LOG2E) * spots[k]
            mixed[rows, :] += out
            lse[rows, :] += level
        return carry

    lax.fori_loop(0, HEADS // 2, per_pair, 0)
    proj = deep(layer[R_PROJ : R_PROJ + EMB, :])
    return mm(mixed[...], proj) + layer[R_PROJB : R_PROJB + 1, :]


def attention_back(grad, normed, layer, save, lse, mixed, sc, grads, at, region=None):
    left, right, gleft, vright, keys, dq, dkv_t, weights, slopes = sc[:9]
    q_t, do_t, dmix, s, dp, two_keys, two_values = sc[9:]
    proj = deep(layer[R_PROJ : R_PROJ + EMB, :])
    grads[at + R_PROJ : at + R_PROJ + EMB, :] = mm_tn(rows_t(mixed[...]), grad)[:EMB]
    grads[at + R_PROJB : at + R_PROJB + 1, :] = colsum(grad)
    d_mixed = mm_nt(grad, proj)
    dmix[...] = d_mixed * mixed[...]
    q, k, v = (save[:, i * WIDE : (i + 1) * WIDE] for i in range(3))
    for g, part in enumerate(as_left(q)):
        left[g] = part
    for g, part in enumerate(as_right(k)):
        right[g] = part
    for g, part in enumerate(as_left(d_mixed)):
        gleft[g] = part
    for g, part in enumerate(as_right(v)):
        vright[g] = part
    kk = pair(k)
    keys[0:ROWS, :] = kk
    keys[ROWS : 2 * ROWS, :] = kk
    for ref, x in ((q_t, q), (do_t, d_mixed)):
        hi, lo = split(x.T)
        ref[0] = hi
        ref[1] = lo
    dq[...] = jnp.zeros_like(dq)
    dkv_t[...] = jnp.zeros_like(dkv_t)

    def per_pair(pair_of, carry):
        g = lax.div(pair_of, 2)
        heads = [2 * pair_of, 2 * pair_of + 1]
        both_heads(right[g], heads, two_keys)
        both_heads(vright[g], heads, two_values)
        s[...] = dot_nt(left[g], two_keys[...])
        dp[...] = dot_nt(gleft[g], two_values[...])
        for k in range(2):
            h = 2 * pair_of + k
            lanes = own_lanes(h)
            at_h = jnp.where(iota((1, WIDE), 1) == h, 1.0, 0.0)
            for b in range(ROWS // BLK):
                rows = slice(b * BLK, (b + 1) * BLK)
                level = jnp.sum(lse[rows, :] * at_h, 1, keepdims=True)
                delta = jnp.sum(dmix[rows, :] * lanes, 1, keepdims=True)
                at_k = k * ROWS
                tiles = score_tiles(s[rows, at_k : at_k + ROWS], rows, region)
                for i, t in enumerate(tiles):
                    p = jnp.exp2(t - level)
                    put_split(weights.at[k], rows, i, p)
                    low = at_k + i * WIDE
                    p = p * (dp[rows, low : low + WIDE] - delta)
                    put_split(slopes.at[k], rows, i, p)
        total = 0.0
        for k in range(2):
            total = total + fold(dot(slopes[k], keys[...])) * own_lanes(2 * pair_of + k)
        dq[...] += total
        for k in range(2):
            here = pl.ds(pl.multiple_of((2 * pair_of + k) * HDIM, HDIM), HDIM)
            for i, (t, m) in enumerate(((q_t, slopes), (do_t, weights))):
                lhs = jnp.concatenate([t[0, here, :], t[1, here, :]], 0)
                dkv_t[i, here, :] = fold_rows(fold(dot(lhs, m[k])))
        return carry

    lax.fori_loop(0, HEADS // 2, per_pair, 0)
    d_q = dq[...] * HDIM**-0.5
    d_k = dkv_t[0].T * (1.0 / LOG2E)
    d_v = dkv_t[1].T
    x_t = rows_t(normed)
    d_normed = None
    for i, d in enumerate((d_q, d_k, d_v)):
        grads[pl.ds(at + R_QKV + i, EMB, stride=3), :] = mm_tn(x_t, d)[:EMB]
        grads[at + R_QKVB + i : at + R_QKVB + i + 1, :] = colsum(d)
        part = mm_nt(d, deep(layer[pl.ds(R_QKV + i, EMB, stride=3), :]))
        d_normed = part if d_normed is None else d_normed + part
    return d_normed


def mlp(middle, layer, hpre):
    normed = norm(middle, layer[2:3, :], layer[3:4, :])
    w = deep(hidden_rows(layer, R_HID, EMB))
    pre = mm(normed, w) + hidden_rows(layer, R_HIDB, 1)
    hpre[...] = pre
    out = mm(gelu(pre), layer[R_OUT : R_OUT + HID, :])
    return middle + out + layer[R_OUTB : R_OUTB + 1, :]


def mlp_back(grad, middle, hpre, layer, grads, at):
    hat, inv = norm_stats(middle)
    normed = hat * layer[2:3, :] + layer[3:4, :]
    act, slope = gelu_both(hpre[...])
    grads[at + R_OUTB : at + R_OUTB + 1, :] = colsum(grad)
    grads[at + R_OUT : at + R_OUT + HID, :] = mm_tn(rows_t(grad), act).T
    d_pre = mm_nt(grad, layer[R_OUT : R_OUT + HID, :]) * slope
    put_hidden_rows(grads, at + R_HIDB, 1, colsum(d_pre))
    put_hidden_rows(grads, at + R_HID, EMB, mm_tn(rows_t(normed), d_pre)[:EMB])
    d_normed = mm_nt(d_pre, deep(hidden_rows(layer, R_HID, EMB)))
    grads[at + 2 : at + 3, :] = colsum(d_normed * hat)
    grads[at + 3 : at + 4, :] = colsum(d_normed)
    return grad + norm_back(hat, inv, layer[2:3, :], d_normed)


def pre_norm_back(grad, tokens, layer, grads, at):
    hat, inv = norm_stats(tokens)
    grads[at : at + 1, :] = colsum(grad * hat)
    grads[at + 1 : at + 2, :] = colsum(grad)
    return norm_back(hat, inv, layer[0:1, :], grad)


def region_of(rows, sizes):
    d = lax.shift_right_logical(rows * 1338, 16)
    line = lax.shift_right_logical(rows * 9363, 16)
    places = (d, line - d * WIN, rows - line * WIN)
    starts = (lax.axis_index("slab") * WIN, lax.axis_index("mp") * WIN, 0)
    total = None
    for place, start, blocks in zip(places, starts, sizes + (1,)):
        turned = jnp.where(place < SHIFT, place + FAR, place - SHIFT) + start
        length = WIN * blocks
        part = jnp.where(turned < length - WIN, 0, jnp.where(turned < length - SHIFT, 1, 2))
        total = part if total is None else total * 3 + part
    return total


def put_region(region, sizes):
    rows = region_of(iota((ROWS, WIDE), 0), sizes)[:, 0:1]
    lanes = region_of(iota((8, ROWS), 1), sizes)[0:1, :]
    apart = jnp.where(rows == lanes, 0.0, -100.0 * LOG2E)
    region[...] = jnp.where(iota((ROWS, ROWS), 1) < VOX, apart, -1e30)


def send_parts(ref, a, b, c):
    far = FAR * WIN
    near = SHIFT * WIN
    for d in range(SHIFT):
        base = d * PLANE
        c[d * near : (d + 1) * near, :] = ref[base : base + near, :]
        a[d * far : (d + 1) * far, :] = ref[base + near : base + PLANE, :]
    for d in range(FAR):
        base = (d + SHIFT) * PLANE
        b[d * near : (d + 1) * near, :] = ref[base : base + near, :]


def take_parts(own, a, b, c, out):
    far = FAR * WIN
    near = SHIFT * WIN
    for d in range(WIN):
        base = d * PLANE
        if d < SHIFT:
            out[base : base + near, :] = c[d * near : (d + 1) * near, :]
            out[base + near : base + PLANE, :] = a[d * far : (d + 1) * far, :]
        else:
            e = d - SHIFT
            out[base : base + near, :] = b[e * near : (e + 1) * near, :]
            out[base + near : base + PLANE, :] = own[base + near : base + PLANE, :]
    out[VOX:, :] = jnp.zeros((ROWS - VOX, WIDE), F32)


def span_of(groups):
    low, high = groups
    first = 3 * low // 8 * 8
    last = -(-3 * high // 8) * 8
    return first, min(last, NPARAM // WIDE // 8 * 8) - first


def copied(params, groups, flat, sem):
    first, rows = span_of(groups)
    size = rows * WIDE
    return pltpu.make_async_copy(
        params.at[pl.ds(first * WIDE, size)], flat.at[pl.ds(0, size)], sem
    )


def relay(groups, flat, out, square, last=None):
    low, high = groups
    first, rows = span_of(groups)
    square[0:rows, :] = flat[0 : rows * WIDE].reshape(rows, WIDE)
    if last is not None:
        square[rows : rows + 24, :] = jnp.zeros((24, WIDE), F32)
        square[rows : rows + 1, 0 : last.shape[0]] = last[...].reshape(1, last.shape[0])
    skip = 3 * low - first
    n = high - low
    parts = three_to_four([square[pl.ds(skip + c, n, stride=3), :] for c in range(3)])
    for c in range(4):
        out[pl.ds(c, n, stride=4), :] = parts[c]


FIRST_SPANS = ((0, 98), (98, 392))
LAYER_SPANS = ((389, 681), (680, 972))
CONV_SPANS = ((971, 1620), (1620, GROUPS))


def prep_kernel(spans, params, *refs, last=None):
    outs, (flats, square, sems) = refs[: len(spans)], refs[-3:]
    for i, groups in enumerate(spans):
        copied(params, groups, flats[i], sems.at[i]).start()
    for i, groups in enumerate(spans):
        copied(params, groups, flats[i], sems.at[i]).wait()
        relay(groups, flats[i], outs[i], square, last if i == len(spans) - 1 else None)


def head_picks():
    width = HEAD_ROWS * WIDE
    place = iota((WIDE, width), 1) - HEAD_LANE
    row = iota((WIDE, width), 0)
    here = (place >= row * CLASSES) & (place < (row + 1) * CLASSES) & (row <= EMB)
    place = iota((width, WIDE), 0) - HEAD_LANE
    col = iota((width, WIDE), 1)
    row = lax.shift_right_logical(place * 4682, 16)
    there = (place - row * CLASSES == col) & (place >= 0)
    return jnp.where(here, 1.0, 0.0), jnp.where(there, 1.0, 0.0).astype(BF16)


def prep_conv_kernel(
    last, params, conv0, conv1, head, weights0, weights1, vectors, *scratch
):
    prep_kernel(CONV_SPANS, params, conv0, conv1, *scratch, last=last)
    tap_weights(conv0, 3, weights0)
    tap_weights(conv1, 0, weights1)
    vectors[0:1, :] = conv0[3 + TAP_ROWS : 4 + TAP_ROWS, :]
    vectors[1:4, :] = conv1[TAP_ROWS : TAP_ROWS + 3, :]
    vectors[4:8, :] = jnp.zeros((4, WIDE), F32)
    square = scratch[1]
    first, _ = span_of(CONV_SPANS[1])
    row = jnp.concatenate(
        [square[HEAD_ROW + i - first : HEAD_ROW + i - first + 1, :] for i in range(HEAD_ROWS)], 1
    )
    here, there = head_picks()
    hi, lo = split(here * row)
    head[...] = dot(hi, there) + dot(lo, there)


def head_rows(d_head, out, at):
    here, there = head_picks()
    hi, lo = split(d_head)
    spread = (dot_nt(hi, there) + dot_nt(lo, there)) * here
    row = colsum(spread)
    for i in range(HEAD_ROWS):
        out[at + i : at + i + 1, :] += row[:, i * WIDE : (i + 1) * WIDE]


class Rows:
    def __init__(self, ref, at):
        self.ref, self.at = ref, at

    def __getitem__(self, key):
        rows, lanes = key
        if isinstance(rows, slice):
            rows = slice(rows.start + self.at, rows.stop + self.at)
        else:
            rows = pl.ds(rows.start + self.at, rows.size, stride=rows.stride)
        return self.ref[rows, lanes]


def merged_norm(x):
    mean = jnp.sum(x, 1, keepdims=True) * (1.0 / MERGE)
    centred = x - mean
    var = jnp.sum(centred * centred, 1, keepdims=True) * (1.0 / MERGE)
    return centred * lax.rsqrt(var + eps_norm)


def first_kernel(
    feats, merge, lay0,
    dense, tok0, save, lse, mixed, middle, hpre, tok1, ahead, pa, pb, pc,
    *sc,
):
    dense[VOX:, :] = jnp.zeros((ROWS - VOX, MERGE), F32)
    for line in range(PLANE):
        dense[line * WIN : (line + 1) * WIN, :] = feats[line]
    hat = merged_norm(dense[...])
    normed = hat * hidden_rows(merge, 0, 1) + hidden_rows(merge, 4, 1)
    tokens = mm(normed, merge[8 : 8 + MERGE, :])
    tok0[...] = tokens
    layer = Rows(lay0, 0)
    normed = norm(tokens, layer[0:1, :], layer[1:2, :])
    attended = attention(normed, layer, save, lse, mixed, sc)
    mid = tokens + attended
    middle[...] = mid
    tokens = mlp(mid, layer, hpre)
    tok1[...] = tokens
    ahead[...] = norm(tokens, layer[1165:1166, :], layer[1166:1167, :])
    send_parts(ahead, pa, pb, pc)


def shifted_kernel(
    sizes,
    own, pa, pb, pc, lay1,
    window, save, lse, mixed, out, qa, qb, qc,
    region, *sc,
):
    put_region(region, sizes)
    take_parts(own, pa, pb, pc, window)
    out[...] = attention(
        window[...], Rows(lay1, 1), save, lse, mixed, sc, region
    )
    send_parts(out, qa, qb, qc)


def to_lines(ref, out):
    for line in range(PLANE):
        out[line, 0:WIN, :] = ref[line * WIN : (line + 1) * WIN, :]
        out[line, WIN:8, :] = jnp.zeros((8 - WIN, WIDE), F32)


def from_lines(ref, out):
    out[VOX:, :] = jnp.zeros((ROWS - VOX, WIDE), F32)
    for line in range(PLANE):
        out[line * WIN : (line + 1) * WIN, :] = ref[line, 0:WIN, :]


def send_sides(lines, near_d, far_d, near_h, far_h):
    odd_d = jnp.bitwise_and(lax.axis_index("slab"), 1) == 1
    odd_h = jnp.bitwise_and(lax.axis_index("mp"), 1) == 1
    low, high = lines[0 : 2 * WIN], lines[(WIN - 2) * WIN : PLANE]
    near_d[...] = jnp.where(odd_d, low, high)
    far_d[...] = jnp.where(odd_d, high, low)
    for d in range(WIN):
        low = lines[d * WIN : d * WIN + 2]
        high = lines[d * WIN + WIN - 2 : (d + 1) * WIN]
        near_h[2 * d : 2 * d + 2] = jnp.where(odd_h, low, high)
        far_h[2 * d : 2 * d + 2] = jnp.where(odd_h, high, low)


def second_kernel(
    tok1, own, qa, qb, qc, lay1, lay2, _,
    mid1, hpre1, tok2, save, lse, mixed, mid2, hpre2, lines,
    s0, s1, s2, s3,
    attended, *sc,
):
    take_parts(own, qa, qb, qc, attended)
    mid = tok1[...] + attended[...]
    mid1[...] = mid
    tokens = mlp(mid, Rows(lay1, 1), hpre1)
    tok2[...] = tokens
    layer = Rows(lay2, 2)
    normed = norm(tokens, layer[0:1, :], layer[1:2, :])
    mid = tokens + attention(normed, layer, save, lse, mixed, sc)
    mid2[...] = mid
    attended[...] = mlp(mid, layer, hpre2)
    to_lines(attended, lines)
    send_sides(lines, s0, s1, s2, s3)


def grown_lines(sizes, own, near_d, far_d, near_h, far_h, out):
    slab, row = lax.axis_index("slab"), lax.axis_index("mp")
    odd_d = jnp.bitwise_and(slab, 1) == 1
    odd_h = jnp.bitwise_and(row, 1) == 1
    out[:, 11:12] = jnp.zeros((11, 1, 8, WIDE), F32)
    for d in range(WIN):
        out[d + 2, 2 : 2 + WIN] = own[d * WIN : (d + 1) * WIN]
    for d in range(2):
        near = near_d[d * WIN : (d + 1) * WIN]
        far = far_d[d * WIN : (d + 1) * WIN]
        out[d, 2 : 2 + WIN] = jnp.where(odd_d, near, jnp.where(slab == 0, 0.0, far))
        out[d + 9, 2 : 2 + WIN] = jnp.where(
            odd_d, jnp.where(slab == sizes[0] - 1, 0.0, far), near
        )
    for d in range(11):
        near = near_h[2 * d : 2 * d + 2]
        far = far_h[2 * d : 2 * d + 2]
        out[d, 0:2] = jnp.where(odd_h, near, jnp.where(row == 0, 0.0, far))
        out[d, 9:11] = jnp.where(odd_h, jnp.where(row == sizes[1] - 1, 0.0, far), near)


def put_marks(labels, valid, out):
    across = iota((8, WIN), 1) == iota((8, WIN), 0)
    classes = iota((8, WIDE), 1) - EMB
    for d in range(WIN):
        code = jnp.where(valid[d] == 1, labels[d], -1 - EMB - WIDE)
        code = code.astype(F32)
        for h in range(WIN):
            line = jnp.where(across, code[h : h + 1, :], 0.0)
            column = jnp.sum(line, 1, keepdims=True)
            mark = jnp.where(column == classes.astype(F32), 1.0, 0.0)
            out[d * WIN + h] = jnp.where(iota((8, WIDE), 0) < WIN, mark, 0.0)


def taps(source, first_plane, planes, first_line, lines, out):
    def per_plane(d, carry):
        for c in range(3):
            for b in range(3):
                x = source[d + first_plane, first_line + b : first_line + b + lines]
                if c != 1:
                    x = roll(x, 1 if c == 0 else 7, 1)
                x = pair(x.reshape(lines * 8, WIDE))
                at = pl.multiple_of(d * (lines * 8), lines * 8)
                t = b * 3 + c
                out[pl.ds(at, lines * 8), t * 256 : (t + 1) * 256] = x
        return carry

    lax.fori_loop(0, planes, per_plane, 0)


def tap_weights(ref, at, out):
    def per_tap(i, carry):
        w = deep(ref[pl.ds(i * EMB + at, EMB), :])
        out[pl.ds(pl.multiple_of(i * 256, 256), 256), :] = weight_nn(w)
        return carry

    lax.fori_loop(0, 27, per_tap, 0)


def tap_weights_back(ref, at, out):
    for i in range(27):
        w = deep(ref[(26 - i) * EMB + at : (27 - i) * EMB + at, :])
        out[:, i * 256 : (i + 1) * 256] = weight_nt(w)


def conv(side, weights, planes, pitch, at_once, put, back=False):
    rows = at_once * pitch
    for start in range(0, planes, at_once):
        total = None
        for a in range(3):
            low = (start + a) * pitch
            x = side[low : low + rows, :]
            if back:
                part = dot_nt(x, weights[:, a * 2304 : (a + 1) * 2304])
            else:
                part = dot(x, weights[a * 2304 : (a + 1) * 2304, :])
            total = part if total is None else total + part
        put(start, fold(total))


def conv_weight_grad(side, grad_rows, pitch, out, at):
    rows = 512
    g = jnp.concatenate([grad_rows, jnp.zeros((rows - grad_rows.shape[0], WIDE), F32)], 0)
    left = jnp.concatenate(split(g.T[:EMB]), 0)
    for a in range(3):
        for bc in range(9):
            y = dot(left, side[a * pitch : a * pitch + rows, bc * 256 : (bc + 1) * 256])
            y = deep(fold_rows(fold(y))).T
            t = a * 9 + bc
            out[at + t * EMB : at + (t + 1) * EMB, :] = y[:EMB]


def volume_mask(sizes, planes, lines, reach, real_lines):
    slab, row = lax.axis_index("slab"), lax.axis_index("mp")
    ends = (slab == 0, slab == sizes[0] - 1, row == 0, row == sizes[1] - 1)
    shape = (planes, lines, 8, WIDE)
    d, h, w = iota(shape, 0), iota(shape, 1), iota(shape, 2)
    low_d = jnp.where(ends[0], reach, 0)
    high_d = jnp.where(ends[1], planes - reach, planes)
    low_h = jnp.where(ends[2], reach, 0)
    high_h = jnp.where(ends[3], real_lines - reach, real_lines)
    inside = (d >= low_d) & (d < high_d) & (h >= low_h) & (h < high_h) & (w < WIN)
    return jnp.where(inside, 1.0, 0.0)


def conv_kernel(
    sizes,
    own, s0, s1, s2, s3, labels, valid, weights0, weights1, vectors,
    grown, pre, tok, stats, t0, t1, t2, t3,
    act, side, side_own, marks,
):
    grown_lines(sizes, own, s0, s1, s2, s3, grown)
    put_marks(labels, valid, marks)
    taps(grown, 0, 11, 0, 10, side)
    bias0 = vectors[0:1, :]
    inside = volume_mask(sizes, 9, 10, 1, 9)


    def put(start, y):
        z = (y + bias0).reshape(3, 10, 8, WIDE)
        pre[start : start + 3] = z
        act[start : start + 3] = gelu(z) * inside[start : start + 3]

    conv(side, weights0, 9, 80, 3, put)
    taps(act, 0, 9, 0, 8, side_own)
    bias1 = vectors[1:2, :]
    sums = []

    def put_own(start, y):
        y = (y + bias1).reshape(WIN, 8, 8, WIDE)[:, 0:WIN]
        y = y + own[...].reshape(WIN, WIN, 8, WIDE)
        y = jnp.where(iota(y.shape, 2) < WIN, y, 0.0).reshape(PLANE, 8, WIDE)
        tok[...] = y + marks[...]
        send_sides(tok, t0, t1, t2, t3)
        flat = y.reshape(PLANE * 8, WIDE)
        sums.append(colsum(flat))
        sums.append(colsum(flat * flat))

    conv(side_own, weights1, WIN, 64, WIN, put_own)
    count = jnp.sum(marks[...].reshape(PLANE * 8, WIDE))
    row = iota((8, WIDE), 0)
    stats[...] = (
        jnp.where(row == 0, sums[0], 0.0)
        + jnp.where(row == 1, sums[1], 0.0)
        + jnp.where(row == 2, count, 0.0)
    )


def head_kernel(
    sizes, voxels,
    own, s0, s1, s2, s3, sums, vectors, head_w,
    grown, slope_out, stats, d_head, d_rows,
):
    grown_lines(sizes, own, s0, s1, s2, s3, grown)
    rows = 11 * 12 * 8
    both = grown[...].reshape(rows, WIDE)
    lane = iota((rows, WIDE), 1)
    tokens = jnp.where(lane < EMB, both, 0.0)
    target = jnp.where(lane < CLASSES, roll(both, WIDE - EMB, 1), 0.0)
    live = jnp.sum(target, 1, keepdims=True)
    count = F32(voxels)
    average = sums[0:1, :] / count
    spread = sums[1:2, :] / count - average * average
    inv = lax.rsqrt(spread + eps_norm)
    gain = vectors[2:3, :]
    bias = vectors[3:4, :]
    hat = (tokens - average) * inv
    act, slope = gelu_both(hat * gain + bias)
    act = jnp.where(lane == EMB, 1.0, act)
    w = head_w[...]
    logits = mm(act, w)
    logits = jnp.where(lane < CLASSES, logits, -1e30)
    top = jnp.max(logits, 1, keepdims=True)
    e = jnp.exp(logits - top)
    total = jnp.sum(e, 1, keepdims=True)
    logp = logits - top - jnp.log(total)
    scale = 1.0 / sums[2:3, 0:1]
    d_logits = (e / total * live - target) * scale
    d_normed = jnp.where(lane < EMB, mm_nt(d_logits, w) * slope, 0.0)
    d_tokens = d_normed * gain * inv
    slope_out[...] = d_tokens.reshape(11, 12, 8, WIDE)

    def own_rows(x):
        x = x.reshape(11, 12, 8, WIDE)[2:9, 2:9]
        x = jnp.where(iota(x.shape, 2) < WIN, x, 0.0)
        return x.reshape(PLANE * 8, WIDE)

    loss = -jnp.sum(own_rows(target * jnp.where(lane < CLASSES, logp, 0.0)))
    own_d = own_rows(d_logits)
    own_n = own_rows(d_normed)
    own_hat = own_rows(hat)
    zeros = jnp.zeros((512 - PLANE * 8, WIDE), F32)
    left = rows_t(jnp.concatenate([own_d, zeros], 0))
    d_head[...] = mm_tn(left, jnp.concatenate([own_rows(act), zeros], 0)).T
    d_gain = colsum(own_n * own_hat)
    d_bias = colsum(own_n)
    d_average = -d_bias * gain * inv
    d_spread = d_gain * gain * inv * inv * -0.5
    d_two = d_spread / count
    d_one = (d_average - 2.0 * average * d_spread) / count
    row = iota((8, WIDE), 0)
    live_lane = iota((8, WIDE), 1) < EMB
    stats[...] = (
        jnp.where((row == 0) & live_lane, d_one, 0.0)
        + jnp.where((row == 1) & live_lane, d_two, 0.0)
        + jnp.where(row == 2, loss, 0.0)
    )
    d_rows[...] = (
        jnp.where(row == 0, d_gain, 0.0)
        + jnp.where(row == 1, d_bias, 0.0)
    )


def sides_back_kernel(sizes, grown, pre, side_act, side_grown, act):
    act[0:9] = gelu(pre[...]) * volume_mask(sizes, 9, 10, 1, 9)
    act[9:10] = jnp.zeros((1, 10, 8, WIDE), F32)
    taps(act, 0, 10, 0, 8, side_act)
    taps(grown, 1, 10, 1, 8, side_grown)


def weights_back_kernel(conv0, conv1, weights0, weights1):
    tap_weights_back(conv0, 3, weights0)
    tap_weights_back(conv1, 0, weights1)


def conv_back_kernel(
    sizes,
    tok, slope, sums, pre, side_act, side_grown, weights0, weights1, d_rows, d_head,
    d_own, keep, send, carry, seam,
    grads, dgrown, act, side, side_own, flat,
):
    lane = iota((11, 12, 8, WIDE), 3)
    inside = volume_mask(sizes, 11, 12, 2, 11)
    steady = sums[0:1, :].reshape(1, 1, 1, WIDE)
    rising = 2.0 * sums[1:2, :].reshape(1, 1, 1, WIDE)
    d_tok = slope[...] + jnp.where(lane < EMB, (steady + tok[...] * rising) * inside, 0.0)
    dgrown[...] = d_tok
    grads[5191:, :] = jnp.zeros((45, WIDE), F32)
    grads[0:8, :] = jnp.zeros((8, WIDE), F32)
    grads[5189:5191, :] = d_rows[0:2, :]
    own = dgrown[2:9, 2:10]
    line = iota(own.shape, 1)
    own = jnp.where(line < WIN, own, 0.0).reshape(WIN * 64, WIDE)
    grads[5188:5189, :] = colsum(own)

    near = volume_mask(sizes, 9, 10, 1, 9)
    conv_weight_grad(side_act, own, 64, grads, 2596)
    taps(dgrown, 0, 11, 0, 10, side)


    def put(start, y):
        _, s = gelu_both(pre[start : start + 3])
        act[start : start + 3] = y.reshape(3, 10, 8, WIDE) * s * near[start : start + 3]

    conv(side, weights1, 9, 80, 3, put, back=True)

    own = act[1:8, 1:9]
    line = iota(own.shape, 1)
    own = jnp.where(line < WIN, own, 0.0).reshape(WIN * 64, WIDE)
    grads[2595:2596, :] = colsum(own)
    conv_weight_grad(side_grown, own, 64, grads, 3)
    carry[...] = grads[0:24, :]
    flat[3 * (GROUPS - CUTS[3]) :, :] = jnp.zeros((flat.shape[0] - 3912, WIDE), F32)
    flatten(grads, 20, GROUPS - CUTS[3], flat)
    start = 3 * CUTS[3]
    head_rows(d_head[...], flat, HEAD_ROW - start)
    seam[...] = flat[0 : LATE_ROWS - start, :]
    scatter(sizes, flat, LATE_ROWS - start, keep, send)
    taps(act, 0, 9, 0, 8, side_own)

    def put_own(start, y):
        y = y.reshape(WIN, 8, 8, WIDE)[:, 0:WIN] + dgrown[2:9, 2:9]
        y = jnp.where(iota(y.shape, 2) < WIN, y, 0.0)
        d_own[...] = y.reshape(PLANE, 8, WIDE)

    conv(side_own, weights0, WIN, 64, WIN, put_own, back=True)


def back_mlp_kernel(d_own, lay2, mid2, hpre2, d_mid, grads, dense):
    from_lines(d_own, dense)
    grads[...] = jnp.zeros_like(grads)
    d_mid[...] = mlp_back(dense[...], mid2[...], hpre2, Rows(lay2, 2), grads, 2)


def back_two_kernel(
    d_mid2, grads2, carry, lay1, lay2, tok2, save, lse, mixed, mid1, hpre1,
    d_mid, grads1, flat, carry2, pa, pb, pc,
    grads, *sc,
):
    layer = Rows(lay2, 2)
    grads[0:1168, :] = grads2[...]
    d = d_mid2[...]
    tokens = tok2[...]
    normed = norm(tokens, layer[0:1, :], layer[1:2, :])
    d_normed = attention_back(d, normed, layer, save, lse, mixed, sc, grads, 2)
    d = d + pre_norm_back(d_normed, tokens, layer, grads, 2)
    grads[1167:1184, :] = carry[3:20, :]
    flatten(grads, 32, CUTS[3] - CUTS[2], flat)
    carry2[...] = grads[0:32, :]
    layer = Rows(lay1, 1)
    d = mlp_back(d, mid1[...], hpre1, layer, grads1, 1)
    d_mid[...] = d
    send_parts(d_mid, pa, pb, pc)


def back_shifted_kernel(
    sizes,
    own, pa, pb, pc, lay1, window, save, lse, mixed, grads1, carry2, _,
    d_window, flat, carry1, qa, qb, qc,
    region, grads, grad, *sc,
):
    put_region(region, sizes)
    take_parts(own, pa, pb, pc, grad)
    grads[0:1168, :] = grads1[...]
    grads[0:3, :] = jnp.zeros((3, WIDE), F32)
    d_window[...] = attention_back(
        grad[...], window[...], Rows(lay1, 1), save, lse, mixed, sc, grads, 1,
        region,
    )
    send_parts(d_window, qa, qb, qc)
    grads[1166:1196, :] = carry2[2:32, :]
    flatten(grads, 12, CUTS[2] - CUTS[1], flat)
    carry1[...] = grads[0:16, :]


def back_first_kernel(
    sizes,
    d_mid, own, qa, qb, qc, tok1, lay0, lay1, merge, dense, tok0, save, lse, mixed, middle, hpre,
    carry1, flat1, flat2, seam, _,
    keep, send,
    flat, grads, grad, *sc,
):
    take_parts(own, qa, qb, qc, grad)
    grads[1556:1572, :] = carry1[...]
    d = d_mid[...] + pre_norm_back(grad[...], tok1[...], Rows(lay1, 1), grads, 1557)
    layer = Rows(lay0, 0)
    at = MERGE_ROWS
    d = mlp_back(d, middle[...], hpre, layer, grads, at)
    tokens = tok0[...]
    normed = norm(tokens, layer[0:1, :], layer[1:2, :])
    d_normed = attention_back(d, normed, layer, save, lse, mixed, sc, grads, at)
    d = d + pre_norm_back(d_normed, tokens, layer, grads, at)
    live = iota((ROWS, WIDE), 0) < VOX
    d = jnp.where(live, d, 0.0)
    hat = merged_norm(dense[...])
    gain = hidden_rows(merge, 0, 1)
    bias = hidden_rows(merge, 4, 1)
    w = merge[8 : 8 + MERGE, :]
    put_hidden_rows(grads, 8 - 8, 1, jnp.zeros((1, MERGE), F32))
    grads[8 : 8 + MERGE, :] = mm_tn(rows_t(d), hat * gain + bias).T
    d_hat = mm_nt(d, w)
    put_hidden_rows(grads, 0, 1, colsum(d_hat * hat))
    put_hidden_rows(grads, 4, 1, colsum(d_hat))
    flatten(grads, 0, CUTS[1], flat)
    at = 0
    for cut, part in ((CUTS[1], flat1), (CUTS[2], flat2), (CUTS[3], seam)):
        at = 3 * cut
        flat[at : at + part.shape[0], :] = part[...]
    at += seam.shape[0]
    if flat.shape[0] > at:
        flat[at:, :] = jnp.zeros((flat.shape[0] - at, WIDE), F32)
    scatter(sizes, flat, 0, keep, send)


def radices(count):
    steps = [2]
    left = count // 2
    while left > 1:
        steps.append(4 if left >= 4 else 2)
        left //= steps[-1]
    return steps


def block_rows(rows, count):
    return -(-rows // (8 * count)) * 8


def own_number(sizes):
    return lax.axis_index("slab") * sizes[1] + lax.axis_index("mp")


def place_in_half(distance, count):
    place = 0
    shift = 1
    for radix in radices(count)[1:]:
        digit = jnp.bitwise_and(lax.shift_right_logical(distance, shift), radix - 1)
        place = place * radix + digit
        shift += radix.bit_length() - 1
    return place


def scatter(sizes, source, first, keep, send):
    count = sizes[0] * sizes[1]
    rows = keep.shape[0] * 2 // count
    me = own_number(sizes)
    odd = jnp.bitwise_and(me, 1)

    def per_pair(t, carry):
        for block, out in ((2 * t + odd, keep), (2 * t + 1 - odd, send)):
            place = place_in_half(jnp.bitwise_xor(block, me), count)
            at = pl.multiple_of(first + block * rows, 8)
            to = pl.multiple_of(place * rows, 8)
            out[pl.ds(to, rows), :] = source[pl.ds(at, rows), :]
        return carry

    lax.fori_loop(0, count // 2, per_pair, 0)


def traded(value, distance, count):
    pairs = [(i, i ^ distance) for i in range(count)]
    return lax.ppermute(value, ("slab", "mp"), pairs)


def later(got, after):
    return got if after is None else list(lax.optimization_barrier((*got, after)))[:-1]


def summing(keep, send, count):
    steps = radices(count)
    got = [keep, traded(send, 1, count)]
    shift = 1
    after = yield None
    for radix in steps[1:]:
        got = later(got, after)
        total = sum(got[1:], got[0])
        rows = total.shape[0] // radix
        parts = [total[k * rows : (k + 1) * rows] for k in range(radix)]
        got = parts[:1] + [traded(parts[k], k << shift, count) for k in range(1, radix)]
        shift += radix.bit_length() - 1
        after = yield parts[0]
    got = later(got, after)
    own = sum(got[1:], got[0])
    for radix in reversed(steps[1:]):
        shift -= radix.bit_length() - 1
        got = [own] + [traded(own, k << shift, count) for k in range(1, radix)]
        after = yield own
        own = jnp.concatenate(later(got, after), 0)
        yield own
    yield own, traded(own, 1, count)


def finished(chain, after=None):
    last = next(chain) if after is None else chain.send(after)
    while not isinstance(last, tuple):
        last = next(chain)
    return last


def exchanged_sum(value, count):
    shift = 0
    for radix in radices(count):
        got = [value] + [traded(value, k << shift, count) for k in range(1, radix)]
        while len(got) > 1:
            got = [got[i] + got[i + 1] for i in range(0, len(got), 2)]
        value = got[0]
        shift += radix.bit_length() - 1
    return value


PIECE = 262144


def adamw_kernel(
    sizes,
    late, late_other, early, early_other, tail, sums, params, first, second,
    new_params, new_first, new_second, loss, valid, norm_out,
    grad, scale_ref,
):
    count = sizes[0] * sizes[1]
    step = pl.program_id(0)

    @pl.when(step == 0)
    def gather():
        me = own_number(sizes)
        total = jnp.zeros((8, WIDE), F32)
        for ref in (late, late_other, early, early_other):
            x = ref[...]
            total = total + jnp.sum((x * x).reshape(-1, 8, WIDE), 0)
        norm = jnp.sqrt(jnp.sum(total))
        loss[0] = jnp.sum(tail[2:3, 0:1])
        valid[0] = jnp.sum(sums[2:3, 0:1])
        norm_out[0] = norm
        scale_ref[0] = jnp.minimum(1.0, clip_norm / (norm + 1e-06))
        start = 0
        for own, other, size in ((late, late_other, LATE_ROWS), (early, early_other, EARLY_ROWS)):
            rows = own.shape[0] * 2 // count

            def per_block(block, carry, own=own, other=other, rows=rows, start=start):
                distance = jnp.bitwise_xor(block, me)
                at = pl.ds(pl.multiple_of(place_in_half(distance, count) * rows, 8), rows)
                near = jnp.bitwise_and(distance, 1) == 0
                to = pl.ds(pl.multiple_of(start + block * rows, 8), rows)
                grad[to, :] = jnp.where(near, own[at, :], other[at, :])
                return carry

            lax.fori_loop(0, size // rows, per_block, 0)
            start += size

    def update(base, low, size):
        rows = -(-size // 1024) * 8
        at = pl.ds(pl.multiple_of(base // WIDE + low // WIDE, 8), rows)
        g = grad[at, :].reshape(rows * WIDE)[:size] * scale_ref[0]
        here = pl.ds(pl.multiple_of(base + low, 1024), size)
        one = beta_one * first[here] + (1.0 - beta_one) * g
        two = beta_two * second[here] + (1.0 - beta_two) * g * g
        there = pl.ds(low, size)
        new_first[there] = one
        new_second[there] = two
        two = two * (1.0 / (1.0 - beta_two**STEP))
        low_by = two * lax.rsqrt(jnp.maximum(two, 1e-37)) + adam_eps
        inverse = pl.reciprocal(low_by, approx=True)
        inverse = inverse * (2.0 - low_by * inverse)
        new_params[there] = params[here] * (1.0 - learn_rate * decay_rate) - (
            one * (learn_rate / (1.0 - beta_one**STEP))
        ) * inverse

    whole = NPARAM // PIECE

    @pl.when(step < whole)
    def full():
        def part(i, carry):
            low = pl.multiple_of(i * 16384, 16384)
            update(step * PIECE, low, 16384)
            return carry

        lax.fori_loop(0, PIECE // 16384, part, 0)

    @pl.when(step == whole)
    def last():
        rest = NPARAM - whole * PIECE
        main = rest // 1024 * 1024
        for low in range(0, main, 16384):
            update(whole * PIECE, low, min(16384, main - low))
        update(whole * PIECE, main, rest - main)


def adamw(sizes, parts, arrays):
    pieces = -(-NPARAM // PIECE)
    piece = pl.BlockSpec((PIECE,), lambda i: (i,))
    vmem = pl.BlockSpec(memory_space=pltpu.VMEM)
    smem = pl.BlockSpec(memory_space=pltpu.SMEM)
    return pl.pallas_call(
        functools.partial(adamw_kernel, sizes),
        grid=(pieces,),
        out_shape=[arr(NPARAM)] * 3 + [arr(1)] * 3,
        in_specs=[vmem] * (len(parts) + len(arrays)),
        out_specs=[piece] * 3 + [smem] * 3,
        scratch_shapes=[pltpu.VMEM((LATE_ROWS + EARLY_ROWS, WIDE), F32), pltpu.SMEM((1,), F32)],
        compiler_params=pltpu.CompilerParams(vmem_limit_bytes=16 * 1024 * 1024),
        cost_estimate=pl.CostEstimate(flops=6 * 10**9, bytes_accessed=0, transcendentals=0),
        name="adamw",
    )(*parts, *arrays)


def arr(*shape):
    return jax.ShapeDtypeStruct(shape, F32)


def call(kernel, outs, scratch, *args, name=None, us=1.0, far=(), mib=16):
    vmem = pl.BlockSpec(memory_space=pltpu.VMEM)
    smem = pl.BlockSpec(memory_space=pltpu.SMEM)
    return pl.pallas_call(
        kernel,
        out_shape=list(outs),
        in_specs=[vmem] * len(args) + [pl.BlockSpec(memory_space=pl.ANY)] * len(far),
        out_specs=[smem if o.shape == (1,) else vmem for o in outs],
        scratch_shapes=list(scratch),
        compiler_params=pltpu.CompilerParams(vmem_limit_bytes=mib * 1024 * 1024),
        cost_estimate=pl.CostEstimate(
            flops=int(us * 1.15e9), bytes_accessed=0, transcendentals=0
        ),
        name=name,
    )(*args, *far)


SQUARE = arr(ROWS, WIDE)
SAVE = arr(ROWS, 3 * WIDE)
FORWARD = [
    pltpu.VMEM((2, ROWS, 2 * WIDE), BF16),
    pltpu.VMEM((2, ROWS, 2 * WIDE), BF16),
    pltpu.VMEM((2 * ROWS, 2 * WIDE), BF16),
]
BACKWARD = [
    pltpu.VMEM((2, ROWS, 2 * WIDE), BF16),
    pltpu.VMEM((2, ROWS, 2 * WIDE), BF16),
    pltpu.VMEM((2, ROWS, 2 * WIDE), BF16),
    pltpu.VMEM((2, ROWS, 2 * WIDE), BF16),
    pltpu.VMEM((2 * ROWS, 2 * WIDE), BF16),
    pltpu.VMEM((ROWS, WIDE), F32),
    pltpu.VMEM((2, WIDE, ROWS), F32),
    pltpu.VMEM((2, ROWS, 2 * ROWS), BF16),
    pltpu.VMEM((2, ROWS, 2 * ROWS), BF16),
    pltpu.VMEM((2, WIDE, ROWS), BF16),
    pltpu.VMEM((2, WIDE, ROWS), BF16),
    pltpu.VMEM((ROWS, WIDE), F32),
    pltpu.VMEM((ROWS, 2 * ROWS), F32),
    pltpu.VMEM((ROWS, 2 * ROWS), F32),
    pltpu.VMEM((2 * ROWS, 2 * WIDE), BF16),
    pltpu.VMEM((2 * ROWS, 2 * WIDE), BF16),
]
PARTS = [arr(ROWS_A, WIDE), arr(ROWS_B, WIDE), arr(ROWS_C, WIDE)]


def passed(parts, steps, sizes):
    slabs, rows = sizes
    moved = []
    for part, (ds, dm) in zip(parts, ((1, 0), (0, 1), (1, 1))):
        pairs = []
        for s in range(slabs):
            for m in range(rows):
                target = ((s + steps * ds) % slabs) * rows + (m + steps * dm) % rows
                pairs.append((s * rows + m, target))
        moved.append(lax.ppermute(part, ("slab", "mp"), pairs))
    return moved


SIDES = [arr(2 * WIN, 8, WIDE)] * 4


def paired(axis, size):
    near = [(i, i ^ 1) for i in range(size)]
    far = [(i, (i + (1 if i % 2 else -1)) % size) for i in range(size)]
    return (
        lambda value: lax.ppermute(value, axis, near),
        lambda value: lax.ppermute(value, axis, far),
    )


def column_kernel(sizes, near_d, far_d, near_h, far_h, near_out, far_out):
    slab = lax.axis_index("slab")
    odd_d = jnp.bitwise_and(slab, 1) == 1
    odd_h = jnp.bitwise_and(lax.axis_index("mp"), 1) == 1
    at_low = slab == 0
    at_high = slab == sizes[0] - 1
    near_out[4:18] = near_h[...]
    far_out[4:18] = far_h[...]
    for d in range(2):
        near = near_d[d * WIN : (d + 1) * WIN]
        far = far_d[d * WIN : (d + 1) * WIN]
        before = jnp.where(odd_d, near, jnp.where(at_low, 0.0, far))
        after = jnp.where(odd_d, jnp.where(at_high, 0.0, far), near)
        for x, at in ((before, 2 * d), (after, 18 + 2 * d)):
            low, high = x[0:2], x[WIN - 2 : WIN]
            near_out[at : at + 2] = jnp.where(odd_h, low, high)
            far_out[at : at + 2] = jnp.where(odd_h, high, low)


def beside(sides, sizes):
    near, far = paired("slab", sizes[0])
    near_d, far_d = near(sides[0]), far(sides[1])
    near_h, far_h = call(
        functools.partial(column_kernel, sizes), [arr(22, 8, WIDE)] * 2, [],
        near_d, far_d, sides[2], sides[3],
        name="column", us=0.3,
    )
    near, far = paired("mp", sizes[1])
    return near_d, far_d, near(near_h), far(far_h)


REGION = [pltpu.VMEM((ROWS, ROWS), F32)]


def on_device(sizes, feats, labels, valid, params, moment_one, moment_two):
    slabs, rows = sizes
    count = slabs * rows

    def room(spans):
        sizes = [(span_of(groups)[1] + 8) * WIDE for groups in spans]
        return [
            [pltpu.VMEM((size,), F32) for size in sizes],
            pltpu.VMEM((2048, WIDE), F32),
            pltpu.SemaphoreType.DMA((len(spans),)),
        ]

    first_size = FIRST_SPANS[-1][1] * 384
    merge, lay0 = call(
        functools.partial(prep_kernel, FIRST_SPANS),
        [arr(MERGE_ROWS, WIDE), arr(1176, WIDE)],
        room(FIRST_SPANS),
        name="prep_first", us=2.0, far=(params[:first_size],),
    )
    lay1, lay2 = call(
        functools.partial(prep_kernel, LAYER_SPANS),
        [arr(1168, WIDE)] * 2,
        room(LAYER_SPANS),
        name="prep_layers", us=2.0, far=(params,),
    )
    conv0, conv1, head_w, weights0, weights1, vectors = call(
        prep_conv_kernel,
        [arr(2596, WIDE), arr(2640, WIDE), arr(WIDE, WIDE)]
        + [jax.ShapeDtypeStruct((27 * 256, 256), BF16)] * 2
        + [arr(8, WIDE)],
        room(CONV_SPANS),
        params[NPARAM // WIDE * WIDE :],
        name="prep_conv", us=4.0, far=(params,),
    )

    dense, tok0, save0, lse0, mixed0, mid0, hpre0, tok1, ahead, *parts = call(
        first_kernel,
        [arr(ROWS, MERGE), SQUARE, SAVE, SQUARE, SQUARE, SQUARE, arr(ROWS, HID), SQUARE, SQUARE]
        + PARTS,
        FORWARD,
        feats.reshape(PLANE, WIN, MERGE), merge, lay0,
        name="first", us=6.0,
    )
    parts = passed(parts, -1, sizes)
    window, save1, lse1, mixed1, out1, *parts = call(
        functools.partial(shifted_kernel, sizes),
        [SQUARE, SAVE, SQUARE, SQUARE, SQUARE] + PARTS,
        REGION + FORWARD,
        ahead, *parts, lay1,
        name="shifted", us=4.5,
    )
    parts = passed(parts, 1, sizes)
    mid1, hpre1, tok2, save2, lse2, mixed2, mid2, hpre2, lines, *sides = call(
        second_kernel,
        [SQUARE, arr(ROWS, HID), SQUARE, SAVE, SQUARE, SQUARE, SQUARE, arr(ROWS, HID)]
        + [arr(PLANE, 8, WIDE)] + SIDES,
        [pltpu.VMEM((ROWS, WIDE), F32)] + FORWARD,
        tok1, out1, *parts, lay1, lay2,
        name="second", us=6.5, far=(weights0,),
    )
    sides = beside(sides, sizes)
    grown, pre, tok3, sums, *tok_sides = call(
        functools.partial(conv_kernel, sizes),
        [arr(11, 12, 8, WIDE), arr(9, 10, 8, WIDE), arr(PLANE, 8, WIDE), arr(8, WIDE)] + SIDES,
        [
            pltpu.VMEM((9, 10, 8, WIDE), F32),
            pltpu.VMEM((880, 2304), BF16),
            pltpu.VMEM((576, 2304), BF16),
            pltpu.VMEM((PLANE, 8, WIDE), F32),
        ],
        lines, *sides, labels, valid, weights0, weights1, vectors,
        name="conv", us=8.0, mib=20,
    )
    tok_sides = beside(tok_sides, sizes)
    side_act, side_grown = call(
        functools.partial(sides_back_kernel, sizes),
        [jax.ShapeDtypeStruct((640, 2304), BF16)] * 2,
        [pltpu.VMEM((10, 10, 8, WIDE), F32)],
        grown, pre,
        name="sides_back", us=2.0,
    )
    weights0, weights1 = call(
        weights_back_kernel,
        [jax.ShapeDtypeStruct((256, 27 * 256), BF16)] * 2,
        [],
        conv0, conv1,
        name="weights_back", us=1.5,
    )
    sums = exchanged_sum(sums, count)
    voxels = WIN * slabs * WIN * rows * WIN
    tok3, slope, tail, d_head, d_rows = call(
        functools.partial(head_kernel, sizes, voxels),
        [arr(11, 12, 8, WIDE), arr(11, 12, 8, WIDE), arr(8, WIDE), arr(WIDE, WIDE), arr(8, WIDE)],
        [],
        tok3, *tok_sides, sums, vectors, head_w,
        name="head", us=3.5,
    )
    tail = exchanged_sum(tail, count)
    late_rows = block_rows(LATE_ROWS, count) * count
    early_rows = block_rows(EARLY_ROWS, count) * count
    seam_rows = LATE_ROWS - 3 * CUTS[3]
    d_own, keep, send, carry3, seam = call(
        functools.partial(conv_back_kernel, sizes),
        [arr(PLANE, 8, WIDE)] + [arr(early_rows // 2, WIDE)] * 2
        + [arr(24, WIDE), arr(seam_rows, WIDE)],
        [
            pltpu.VMEM((5236, WIDE), F32),
            pltpu.VMEM((11, 12, 8, WIDE), F32),
            pltpu.VMEM((10, 10, 8, WIDE), F32),
            pltpu.VMEM((880, 2304), BF16),
            pltpu.VMEM((576, 2304), BF16),
            pltpu.VMEM((seam_rows + early_rows, WIDE), F32),
        ],
        tok3, slope, tail, pre, side_act, side_grown, weights0, weights1, d_rows, d_head,
        name="conv_back", us=14.0, mib=28,
    )
    early = summing(keep, send, count)
    next(early)
    d_mid2, grads2 = call(
        back_mlp_kernel,
        [SQUARE, arr(1168, WIDE)],
        [pltpu.VMEM((ROWS, WIDE), F32)],
        d_own, lay2, mid2, hpre2,
        name="back_mlp", us=3.0,
    )
    step = early.send(d_mid2)
    d_mid, grads1, flat2, carry2, *parts = call(
        back_two_kernel,
        [SQUARE, arr(1168, WIDE), arr(3 * (CUTS[3] - CUTS[2]), WIDE), arr(32, WIDE)] + PARTS,
        [pltpu.VMEM((1184, WIDE), F32)] + BACKWARD,
        d_mid2, grads2, carry3, lay1, lay2, tok2, save2, lse2, mixed2, mid1, hpre1,
        name="back_two", us=9.0,
    )
    parts = passed(parts, -1, sizes)
    step = early.send(d_mid)
    d_window, flat1, carry1, *parts = call(
        functools.partial(back_shifted_kernel, sizes),
        [SQUARE, arr(3 * (CUTS[2] - CUTS[1]), WIDE), arr(16, WIDE)] + PARTS,
        REGION + [pltpu.VMEM((1200, WIDE), F32), pltpu.VMEM((ROWS, WIDE), F32)] + BACKWARD,
        d_mid, *parts, lay1, window, save1, lse1, mixed1, grads1, carry2,
        name="back_shifted", us=10.5, far=(step,),
    )
    early.send(d_window)
    parts = passed(parts, 1, sizes)
    next(early)
    step = next(early)
    late = call(
        functools.partial(back_first_kernel, sizes),
        [arr(late_rows // 2, WIDE)] * 2,
        [
            pltpu.VMEM((late_rows, WIDE), F32),
            pltpu.VMEM((1572, WIDE), F32),
            pltpu.VMEM((ROWS, WIDE), F32),
        ]
        + BACKWARD,
        d_mid, d_window, *parts, tok1, lay0, lay1, merge, dense, tok0, save0, lse0, mixed0, mid0,
        hpre0, carry1, flat1, flat2, seam,
        name="back_first", us=13.5, far=(step,),
    )
    step = early.send(late[0])
    keep, send = later(list(late), step)
    late_sum = finished(summing(keep, send, count))
    early = finished(early)
    new_params, new_first, new_second, loss, valid_count, norm = adamw(
        sizes, (*late_sum, *early, tail, sums), (params, moment_one, moment_two)
    )
    return (
        loss.reshape(()), valid_count.reshape(()), norm.reshape(()),
        new_params, new_first, new_second,
    )


def solution(mesh):
    placed = (
        P("slab", "mp", None, None),
        P("slab", "mp", None),
        P("slab", "mp", None),
        P(),
        P(),
        P(),
    )
    sizes = (mesh.shape["slab"], mesh.shape["mp"])
    return jax.shard_map(
        functools.partial(on_device, sizes),
        mesh=mesh,
        in_specs=placed,
        out_specs=(P(), P(), P(), P(), P(), P()),
        check_vma=False,
    )
```

```python
import functools

import jax
import jax.numpy as jnp
from jax import lax
from jax.experimental import pallas as pl
from jax.experimental.pallas import tpu as pltpu
from jax.sharding import PartitionSpec as P

EMB = 96
HEADS = 6
HDIM = 16
HID = 384
MERGE = 384
CLASSES = 14
WIN = 7
SHIFT = 3
LAYERS = 3
STEP = 10

F32 = jnp.float32
BF16 = jnp.bfloat16
eps_norm = 1e-05
beta_one = 0.9
beta_two = 0.999
adam_eps = 1e-08
learn_rate = 0.05
decay_rate = 0.05
clip_norm = 0.01
LOG2E = 1.4426950408889634

VOX = WIN * WIN * WIN
ROWS = 384
BLK = 128
WIDE = 128
PLANE = WIN * WIN
FAR = WIN - SHIFT
ROWS_A = SHIFT * FAR * WIN
ROWS_B = FAR * SHIFT * WIN
ROWS_C = SHIFT * SHIFT * WIN

MERGE_ROWS = 392
LAYER_ROWS = 1165
TAP_ROWS = 27 * EMB
GROUPS = 2280
NPARAM = 872558
HEAD_ROW = 6806
HEAD_ROWS = 11
HEAD_LANE = 32
LATE_ROWS = 3072
EARLY_ROWS = 3840
LAYER_BASE = (98, 389, 680)
CONV_BASE = (971, 1620)
CUTS = (0, 392, 688, 976, 2280)

R_QKV, R_QKVB, R_PROJ, R_PROJB = 4, 292, 295, 391
R_HID, R_HIDB, R_OUT, R_OUTB = 392, 776, 780, 1164


def iota(shape, dim):
    return lax.broadcasted_iota(jnp.int32, shape, dim)


def split(x):
    hi = x.astype(BF16)
    return hi, (x - hi.astype(F32)).astype(BF16)


def pair(x):
    return jnp.concatenate(split(x), 1)


def fold(y):
    half = y.shape[1] // 2
    return y[:, :half] + y[:, half:]


def fold_rows(y):
    half = y.shape[0] // 2
    return y[:half] + y[half:]


def dot(a, b):
    return jnp.dot(a, b, preferred_element_type=F32)


def dot_nt(a, b):
    return lax.dot_general(a, b, (((1,), (1,)), ((), ())), preferred_element_type=F32)


def weight_nn(w):
    top = pair(w)
    return jnp.concatenate([top, top], 0)


def weight_nt(w):
    hi, lo = split(w)
    return jnp.concatenate(
        [jnp.concatenate([hi, hi], 1), jnp.concatenate([lo, lo], 1)], 0
    )


def mm(x, w):
    return fold(dot(pair(x), weight_nn(w)))


def mm_nt(x, w):
    return fold(dot_nt(pair(x), weight_nt(w)))


def rows_t(x):
    return jnp.concatenate(split(x.T), 0)


def mm_tn(xt, y):
    return fold_rows(fold(dot(xt, pair(y))))


def deep(w):
    return jnp.concatenate([w, jnp.zeros((WIDE - EMB, w.shape[1]), F32)], 0)


def roll(x, shift, axis):
    return pltpu.roll(x, shift, axis)


def four_to_three(y):
    lane = iota(y[0].shape, 1)
    a = jnp.where(lane < 96, y[0], roll(y[1], 96, 1))
    b = jnp.where(lane < 64, roll(y[1], 96, 1), roll(y[2], 64, 1))
    c = jnp.where(lane < 32, roll(y[2], 64, 1), roll(y[3], 32, 1))
    return a, b, c


def three_to_four(x):
    lane = iota(x[0].shape, 1)
    live = lane < EMB
    a = x[0]
    b = jnp.where(lane < 32, roll(x[0], 32, 1), roll(x[1], 32, 1))
    c = jnp.where(lane < 64, roll(x[1], 64, 1), roll(x[2], 64, 1))
    d = roll(x[2], 96, 1)
    return tuple(jnp.where(live, v, 0.0) for v in (a, b, c, d))


def hidden_rows(ref, start, count):
    return jnp.concatenate(
        four_to_three([ref[pl.ds(start + c, count, stride=4), :] for c in range(4)]), 1
    )


def put_hidden_rows(ref, start, count, x):
    parts = three_to_four([x[:, i * WIDE : (i + 1) * WIDE] for i in range(3)])
    for c in range(4):
        ref[pl.ds(start + c, count, stride=4), :] = parts[c]


def flatten(ref, start, groups, out):
    parts = four_to_three([ref[pl.ds(start + c, groups, stride=4), :] for c in range(4)])
    for c in range(3):
        out[pl.ds(c, groups, stride=3), :] = parts[c]


def norm_stats(x):
    live = iota(x.shape, 1) < EMB
    mean = jnp.sum(x, 1, keepdims=True) * (1.0 / EMB)
    centred = jnp.where(live, x - mean, 0.0)
    var = jnp.sum(centred * centred, 1, keepdims=True) * (1.0 / EMB)
    inv = lax.rsqrt(var + eps_norm)
    return centred * inv, inv


def norm(x, gain, bias):
    hat, _ = norm_stats(x)
    return hat * gain + bias


def norm_back(hat, inv, gain, grad):
    up = grad * gain
    one = jnp.sum(up, 1, keepdims=True) * (1.0 / EMB)
    two = jnp.sum(up * hat, 1, keepdims=True) * (1.0 / EMB)
    live = iota(hat.shape, 1) < EMB
    return jnp.where(live, inv * (up - one - hat * two), 0.0)


def colsum(x):
    return jnp.sum(x, 0, keepdims=True)


def gelu(x):
    return 0.5 * x * (1.0 + lax.erf(x * (0.5**0.5)))


def gelu_both(x):
    cdf = 0.5 * (1.0 + lax.erf(x * (0.5**0.5)))
    slope = cdf + x * (jnp.exp(x * x * -0.5) * 0.3989422804014327)
    return x * cdf, slope


def head_groups(x):
    lane = iota(x.shape, 1)
    swapped = roll(x, 64, 1)
    return jnp.where(lane < 64, x, swapped), jnp.where(lane < 64, swapped, x)


def as_left(x):
    both = []
    low = iota(x.shape, 1) < 64
    for part in head_groups(x):
        hi = part.astype(BF16).astype(F32)
        one = jnp.where(low, hi, part - hi).astype(BF16)
        both.append(jnp.concatenate([one, one], 1))
    return both


def as_right(x):
    return [pair(part) for part in head_groups(x)]


def head_mask(h, width):
    lane = iota((1, width), 1)
    lane = jnp.bitwise_and(lane, 63)
    low = jnp.bitwise_and(h, 3) * HDIM
    return jnp.where((lane >= low) & (lane < low + HDIM), 1.0, 0.0)


def own_lanes(h):
    lane = iota((1, WIDE), 1)
    return jnp.where((lane >= h * HDIM) & (lane < (h + 1) * HDIM), 1.0, 0.0)


def both_heads(right, heads, out):
    for k, h in enumerate(heads):
        out[k * ROWS : (k + 1) * ROWS, :] = right * head_mask(h, 2 * WIDE).astype(BF16)


def score_tiles(s, rows, region):
    tiles = [s[:, i * WIDE : (i + 1) * WIDE] for i in range(3)]
    if region is not None:
        return [t + region[rows, i * WIDE : (i + 1) * WIDE] for i, t in enumerate(tiles)]
    pad = jnp.where(iota((1, WIDE), 1) < VOX - 2 * WIDE, 0.0, -1e30)
    return tiles[:2] + [tiles[2] + pad]


def put_split(ref, rows, i, x):
    hi, lo = split(x)
    ref[rows, i * WIDE : (i + 1) * WIDE] = hi
    ref[rows, ROWS + i * WIDE : ROWS + (i + 1) * WIDE] = lo


def attention(normed, layer, save, lse, mixed, sc, region=None):
    left, right, values = sc
    x = pair(normed)
    qkv = []
    for i in range(3):
        w = deep(layer[pl.ds(R_QKV + i, EMB, stride=3), :])
        y = fold(dot(x, weight_nn(w))) + layer[R_QKVB + i : R_QKVB + i + 1, :]
        if i == 0:
            y = y * (HDIM**-0.5 * LOG2E)
        save[:, i * WIDE : (i + 1) * WIDE] = y
        qkv.append(y)
    for g, part in enumerate(as_left(qkv[0])):
        left[g] = part
    for g, part in enumerate(as_right(qkv[1])):
        right[g] = part
    v = pair(jnp.where(iota((ROWS, WIDE), 1) == EMB, 1.0, qkv[2]))
    values[0:ROWS, :] = v
    values[ROWS : 2 * ROWS, :] = v
    mixed[...] = jnp.zeros_like(mixed)
    lse[...] = jnp.zeros_like(lse)

    def per_pair(pair_of, carry):
        heads = [2 * pair_of, 2 * pair_of + 1]
        masks = [head_mask(h, 2 * WIDE).astype(BF16) for h in heads]
        lanes = [own_lanes(h) for h in heads]
        spots = [jnp.where(iota((1, WIDE), 1) == h, 1.0, 0.0) for h in heads]
        g = lax.div(pair_of, 2)
        for b in range(ROWS // BLK):
            rows = slice(b * BLK, (b + 1) * BLK)
            out = level = 0.0
            for k in range(2):
                s = dot_nt(left[g, rows, :] * masks[k], right[g])
                tiles = score_tiles(s, rows, region)
                top = jnp.maximum(jnp.maximum(tiles[0], tiles[1]), tiles[2])
                top = jnp.max(top, 1, keepdims=True)
                parts = [split(jnp.exp2(t - top)) for t in tiles]
                e = jnp.concatenate([p[0] for p in parts] + [p[1] for p in parts], 1)
                o = fold(dot(e, values[...]))
                total = o[:, EMB : EMB + 1]
                out = out + o * (lanes[k] / total)
                level = level + (top + jnp.log(total) * LOG2E) * spots[k]
            mixed[rows, :] += out
            lse[rows, :] += level
        return carry

    lax.fori_loop(0, HEADS // 2, per_pair, 0)
    proj = deep(layer[R_PROJ : R_PROJ + EMB, :])
    return mm(mixed[...], proj) + layer[R_PROJB : R_PROJB + 1, :]


def attention_back(grad, normed, layer, save, lse, mixed, sc, grads, at, region=None):
    left, right, gleft, vright, keys, dq, dkv_t, weights, slopes = sc[:9]
    q_t, do_t, dmix, s, dp, two_keys, two_values = sc[9:]
    proj = deep(layer[R_PROJ : R_PROJ + EMB, :])
    grads[at + R_PROJ : at + R_PROJ + EMB, :] = mm_tn(rows_t(mixed[...]), grad)[:EMB]
    grads[at + R_PROJB : at + R_PROJB + 1, :] = colsum(grad)
    d_mixed = mm_nt(grad, proj)
    dmix[...] = d_mixed * mixed[...]
    q, k, v = (save[:, i * WIDE : (i + 1) * WIDE] for i in range(3))
    for g, part in enumerate(as_left(q)):
        left[g] = part
    for g, part in enumerate(as_right(k)):
        right[g] = part
    for g, part in enumerate(as_left(d_mixed)):
        gleft[g] = part
    for g, part in enumerate(as_right(v)):
        vright[g] = part
    kk = pair(k)
    keys[0:ROWS, :] = kk
    keys[ROWS : 2 * ROWS, :] = kk
    for ref, x in ((q_t, q), (do_t, d_mixed)):
        hi, lo = split(x.T)
        ref[0] = hi
        ref[1] = lo
    dq[...] = jnp.zeros_like(dq)
    dkv_t[...] = jnp.zeros_like(dkv_t)

    def per_pair(pair_of, carry):
        g = lax.div(pair_of, 2)
        heads = [2 * pair_of, 2 * pair_of + 1]
        both_heads(right[g], heads, two_keys)
        both_heads(vright[g], heads, two_values)
        s[...] = dot_nt(left[g], two_keys[...])
        dp[...] = dot_nt(gleft[g], two_values[...])
        for k in range(2):
            h = 2 * pair_of + k
            lanes = own_lanes(h)
            at_h = jnp.where(iota((1, WIDE), 1) == h, 1.0, 0.0)
            for b in range(ROWS // BLK):
                rows = slice(b * BLK, (b + 1) * BLK)
                level = jnp.sum(lse[rows, :] * at_h, 1, keepdims=True)
                delta = jnp.sum(dmix[rows, :] * lanes, 1, keepdims=True)
                at_k = k * ROWS
                tiles = score_tiles(s[rows, at_k : at_k + ROWS], rows, region)
                for i, t in enumerate(tiles):
                    p = jnp.exp2(t - level)
                    put_split(weights.at[k], rows, i, p)
                    low = at_k + i * WIDE
                    p = p * (dp[rows, low : low + WIDE] - delta)
                    put_split(slopes.at[k], rows, i, p)
        total = 0.0
        for k in range(2):
            total = total + fold(dot(slopes[k], keys[...])) * own_lanes(2 * pair_of + k)
        dq[...] += total
        for k in range(2):
            here = pl.ds(pl.multiple_of((2 * pair_of + k) * HDIM, HDIM), HDIM)
            for i, (t, m) in enumerate(((q_t, slopes), (do_t, weights))):
                lhs = jnp.concatenate([t[0, here, :], t[1, here, :]], 0)
                dkv_t[i, here, :] = fold_rows(fold(dot(lhs, m[k])))
        return carry

    lax.fori_loop(0, HEADS // 2, per_pair, 0)
    d_q = dq[...] * HDIM**-0.5
    d_k = dkv_t[0].T * (1.0 / LOG2E)
    d_v = dkv_t[1].T
    x_t = rows_t(normed)
    d_normed = None
    for i, d in enumerate((d_q, d_k, d_v)):
        grads[pl.ds(at + R_QKV + i, EMB, stride=3), :] = mm_tn(x_t, d)[:EMB]
        grads[at + R_QKVB + i : at + R_QKVB + i + 1, :] = colsum(d)
        part = mm_nt(d, deep(layer[pl.ds(R_QKV + i, EMB, stride=3), :]))
        d_normed = part if d_normed is None else d_normed + part
    return d_normed


def mlp(middle, layer, hpre):
    normed = norm(middle, layer[2:3, :], layer[3:4, :])
    w = deep(hidden_rows(layer, R_HID, EMB))
    pre = mm(normed, w) + hidden_rows(layer, R_HIDB, 1)
    hpre[...] = pre
    out = mm(gelu(pre), layer[R_OUT : R_OUT + HID, :])
    return middle + out + layer[R_OUTB : R_OUTB + 1, :]


def mlp_back(grad, middle, hpre, layer, grads, at):
    hat, inv = norm_stats(middle)
    normed = hat * layer[2:3, :] + layer[3:4, :]
    act, slope = gelu_both(hpre[...])
    grads[at + R_OUTB : at + R_OUTB + 1, :] = colsum(grad)
    grads[at + R_OUT : at + R_OUT + HID, :] = mm_tn(rows_t(grad), act).T
    d_pre = mm_nt(grad, layer[R_OUT : R_OUT + HID, :]) * slope
    put_hidden_rows(grads, at + R_HIDB, 1, colsum(d_pre))
    put_hidden_rows(grads, at + R_HID, EMB, mm_tn(rows_t(normed), d_pre)[:EMB])
    d_normed = mm_nt(d_pre, deep(hidden_rows(layer, R_HID, EMB)))
    grads[at + 2 : at + 3, :] = colsum(d_normed * hat)
    grads[at + 3 : at + 4, :] = colsum(d_normed)
    return grad + norm_back(hat, inv, layer[2:3, :], d_normed)


def pre_norm_back(grad, tokens, layer, grads, at):
    hat, inv = norm_stats(tokens)
    grads[at : at + 1, :] = colsum(grad * hat)
    grads[at + 1 : at + 2, :] = colsum(grad)
    return norm_back(hat, inv, layer[0:1, :], grad)


def region_of(rows, sizes):
    d = lax.shift_right_logical(rows * 1338, 16)
    line = lax.shift_right_logical(rows * 9363, 16)
    places = (d, line - d * WIN, rows - line * WIN)
    starts = (lax.axis_index("slab") * WIN, lax.axis_index("mp") * WIN, 0)
    total = None
    for place, start, blocks in zip(places, starts, sizes + (1,)):
        turned = jnp.where(place < SHIFT, place + FAR, place - SHIFT) + start
        length = WIN * blocks
        part = jnp.where(turned < length - WIN, 0, jnp.where(turned < length - SHIFT, 1, 2))
        total = part if total is None else total * 3 + part
    return total


def put_region(region, sizes):
    rows = region_of(iota((ROWS, WIDE), 0), sizes)[:, 0:1]
    lanes = region_of(iota((8, ROWS), 1), sizes)[0:1, :]
    apart = jnp.where(rows == lanes, 0.0, -100.0 * LOG2E)
    region[...] = jnp.where(iota((ROWS, ROWS), 1) < VOX, apart, -1e30)


def send_parts(ref, a, b, c):
    far = FAR * WIN
    near = SHIFT * WIN
    for d in range(SHIFT):
        base = d * PLANE
        c[d * near : (d + 1) * near, :] = ref[base : base + near, :]
        a[d * far : (d + 1) * far, :] = ref[base + near : base + PLANE, :]
    for d in range(FAR):
        base = (d + SHIFT) * PLANE
        b[d * near : (d + 1) * near, :] = ref[base : base + near, :]


def take_parts(own, a, b, c, out):
    far = FAR * WIN
    near = SHIFT * WIN
    for d in range(WIN):
        base = d * PLANE
        if d < SHIFT:
            out[base : base + near, :] = c[d * near : (d + 1) * near, :]
            out[base + near : base + PLANE, :] = a[d * far : (d + 1) * far, :]
        else:
            e = d - SHIFT
            out[base : base + near, :] = b[e * near : (e + 1) * near, :]
            out[base + near : base + PLANE, :] = own[base + near : base + PLANE, :]
    out[VOX:, :] = jnp.zeros((ROWS - VOX, WIDE), F32)


def span_of(groups):
    low, high = groups
    first = 3 * low // 8 * 8
    last = -(-3 * high // 8) * 8
    return first, min(last, NPARAM // WIDE // 8 * 8) - first


def copied(params, groups, flat, sem):
    first, rows = span_of(groups)
    size = rows * WIDE
    return pltpu.make_async_copy(
        params.at[pl.ds(first * WIDE, size)], flat.at[pl.ds(0, size)], sem
    )


def relay(groups, flat, out, square, last=None):
    low, high = groups
    first, rows = span_of(groups)
    square[0:rows, :] = flat[0 : rows * WIDE].reshape(rows, WIDE)
    if last is not None:
        square[rows : rows + 24, :] = jnp.zeros((24, WIDE), F32)
        square[rows : rows + 1, 0 : last.shape[0]] = last[...].reshape(1, last.shape[0])
    skip = 3 * low - first
    n = high - low
    parts = three_to_four([square[pl.ds(skip + c, n, stride=3), :] for c in range(3)])
    for c in range(4):
        out[pl.ds(c, n, stride=4), :] = parts[c]


FIRST_SPANS = ((0, 98), (98, 392))
LAYER_SPANS = ((389, 681), (680, 972))
CONV_SPANS = ((971, 1620), (1620, GROUPS))


def prep_kernel(spans, params, *refs, last=None):
    outs, (flats, square, sems) = refs[: len(spans)], refs[-3:]
    for i, groups in enumerate(spans):
        copied(params, groups, flats[i], sems.at[i]).start()
    for i, groups in enumerate(spans):
        copied(params, groups, flats[i], sems.at[i]).wait()
        relay(groups, flats[i], outs[i], square, last if i == len(spans) - 1 else None)


def head_picks():
    width = HEAD_ROWS * WIDE
    place = iota((WIDE, width), 1) - HEAD_LANE
    row = iota((WIDE, width), 0)
    here = (place >= row * CLASSES) & (place < (row + 1) * CLASSES) & (row <= EMB)
    place = iota((width, WIDE), 0) - HEAD_LANE
    col = iota((width, WIDE), 1)
    row = lax.shift_right_logical(place * 4682, 16)
    there = (place - row * CLASSES == col) & (place >= 0)
    return jnp.where(here, 1.0, 0.0), jnp.where(there, 1.0, 0.0).astype(BF16)


def prep_conv_kernel(
    last, params, conv0, conv1, head, weights0, weights1, vectors, *scratch
):
    prep_kernel(CONV_SPANS, params, conv0, conv1, *scratch, last=last)
    tap_weights(conv0, 3, weights0)
    tap_weights(conv1, 0, weights1)
    vectors[0:1, :] = conv0[3 + TAP_ROWS : 4 + TAP_ROWS, :]
    vectors[1:4, :] = conv1[TAP_ROWS : TAP_ROWS + 3, :]
    vectors[4:8, :] = jnp.zeros((4, WIDE), F32)
    square = scratch[1]
    first, _ = span_of(CONV_SPANS[1])
    row = jnp.concatenate(
        [square[HEAD_ROW + i - first : HEAD_ROW + i - first + 1, :] for i in range(HEAD_ROWS)], 1
    )
    here, there = head_picks()
    hi, lo = split(here * row)
    head[...] = dot(hi, there) + dot(lo, there)


def head_rows(d_head, out, at):
    here, there = head_picks()
    hi, lo = split(d_head)
    spread = (dot_nt(hi, there) + dot_nt(lo, there)) * here
    row = colsum(spread)
    for i in range(HEAD_ROWS):
        out[at + i : at + i + 1, :] += row[:, i * WIDE : (i + 1) * WIDE]


class Rows:
    def __init__(self, ref, at):
        self.ref, self.at = ref, at

    def __getitem__(self, key):
        rows, lanes = key
        if isinstance(rows, slice):
            rows = slice(rows.start + self.at, rows.stop + self.at)
        else:
            rows = pl.ds(rows.start + self.at, rows.size, stride=rows.stride)
        return self.ref[rows, lanes]


def merged_norm(x):
    mean = jnp.sum(x, 1, keepdims=True) * (1.0 / MERGE)
    centred = x - mean
    var = jnp.sum(centred * centred, 1, keepdims=True) * (1.0 / MERGE)
    return centred * lax.rsqrt(var + eps_norm)


def first_kernel(
    feats, merge, lay0,
    dense, tok0, save, lse, mixed, middle, hpre, tok1, ahead, pa, pb, pc,
    *sc,
):
    dense[VOX:, :] = jnp.zeros((ROWS - VOX, MERGE), F32)
    for line in range(PLANE):
        dense[line * WIN : (line + 1) * WIN, :] = feats[line]
    hat = merged_norm(dense[...])
    normed = hat * hidden_rows(merge, 0, 1) + hidden_rows(merge, 4, 1)
    tokens = mm(normed, merge[8 : 8 + MERGE, :])
    tok0[...] = tokens
    layer = Rows(lay0, 0)
    normed = norm(tokens, layer[0:1, :], layer[1:2, :])
    attended = attention(normed, layer, save, lse, mixed, sc)
    mid = tokens + attended
    middle[...] = mid
    tokens = mlp(mid, layer, hpre)
    tok1[...] = tokens
    ahead[...] = norm(tokens, layer[1165:1166, :], layer[1166:1167, :])
    send_parts(ahead, pa, pb, pc)


def shifted_kernel(
    sizes,
    own, pa, pb, pc, lay1,
    window, save, lse, mixed, out, qa, qb, qc,
    region, *sc,
):
    put_region(region, sizes)
    take_parts(own, pa, pb, pc, window)
    out[...] = attention(
        window[...], Rows(lay1, 1), save, lse, mixed, sc, region
    )
    send_parts(out, qa, qb, qc)


def to_lines(ref, out):
    for line in range(PLANE):
        out[line, 0:WIN, :] = ref[line * WIN : (line + 1) * WIN, :]
        out[line, WIN:8, :] = jnp.zeros((8 - WIN, WIDE), F32)


def from_lines(ref, out):
    out[VOX:, :] = jnp.zeros((ROWS - VOX, WIDE), F32)
    for line in range(PLANE):
        out[line * WIN : (line + 1) * WIN, :] = ref[line, 0:WIN, :]


def send_sides(lines, near_d, far_d, near_h, far_h):
    odd_d = jnp.bitwise_and(lax.axis_index("slab"), 1) == 1
    odd_h = jnp.bitwise_and(lax.axis_index("mp"), 1) == 1
    low, high = lines[0 : 2 * WIN], lines[(WIN - 2) * WIN : PLANE]
    near_d[...] = jnp.where(odd_d, low, high)
    far_d[...] = jnp.where(odd_d, high, low)
    for d in range(WIN):
        low = lines[d * WIN : d * WIN + 2]
        high = lines[d * WIN + WIN - 2 : (d + 1) * WIN]
        near_h[2 * d : 2 * d + 2] = jnp.where(odd_h, low, high)
        far_h[2 * d : 2 * d + 2] = jnp.where(odd_h, high, low)


def second_kernel(
    tok1, own, qa, qb, qc, lay1, lay2, _,
    mid1, hpre1, tok2, save, lse, mixed, mid2, hpre2, lines,
    s0, s1, s2, s3,
    attended, *sc,
):
    take_parts(own, qa, qb, qc, attended)
    mid = tok1[...] + attended[...]
    mid1[...] = mid
    tokens = mlp(mid, Rows(lay1, 1), hpre1)
    tok2[...] = tokens
    layer = Rows(lay2, 2)
    normed = norm(tokens, layer[0:1, :], layer[1:2, :])
    mid = tokens + attention(normed, layer, save, lse, mixed, sc)
    mid2[...] = mid
    attended[...] = mlp(mid, layer, hpre2)
    to_lines(attended, lines)
    send_sides(lines, s0, s1, s2, s3)


def grown_lines(sizes, own, near_d, far_d, near_h, far_h, out):
    slab, row = lax.axis_index("slab"), lax.axis_index("mp")
    odd_d = jnp.bitwise_and(slab, 1) == 1
    odd_h = jnp.bitwise_and(row, 1) == 1
    out[:, 11:12] = jnp.zeros((11, 1, 8, WIDE), F32)
    for d in range(WIN):
        out[d + 2, 2 : 2 + WIN] = own[d * WIN : (d + 1) * WIN]
    for d in range(2):
        near = near_d[d * WIN : (d + 1) * WIN]
        far = far_d[d * WIN : (d + 1) * WIN]
        out[d, 2 : 2 + WIN] = jnp.where(odd_d, near, jnp.where(slab == 0, 0.0, far))
        out[d + 9, 2 : 2 + WIN] = jnp.where(
            odd_d, jnp.where(slab == sizes[0] - 1, 0.0, far), near
        )
    for d in range(11):
        near = near_h[2 * d : 2 * d + 2]
        far = far_h[2 * d : 2 * d + 2]
        out[d, 0:2] = jnp.where(odd_h, near, jnp.where(row == 0, 0.0, far))
        out[d, 9:11] = jnp.where(odd_h, jnp.where(row == sizes[1] - 1, 0.0, far), near)


def put_marks(labels, valid, out):
    across = iota((8, WIN), 1) == iota((8, WIN), 0)
    classes = iota((8, WIDE), 1) - EMB
    for d in range(WIN):
        code = jnp.where(valid[d] == 1, labels[d], -1 - EMB - WIDE)
        code = code.astype(F32)
        for h in range(WIN):
            line = jnp.where(across, code[h : h + 1, :], 0.0)
            column = jnp.sum(line, 1, keepdims=True)
            mark = jnp.where(column == classes.astype(F32), 1.0, 0.0)
            out[d * WIN + h] = jnp.where(iota((8, WIDE), 0) < WIN, mark, 0.0)


def taps(source, first_plane, planes, first_line, lines, out):
    def per_plane(d, carry):
        for c in range(3):
            for b in range(3):
                x = source[d + first_plane, first_line + b : first_line + b + lines]
                if c != 1:
                    x = roll(x, 1 if c == 0 else 7, 1)
                x = pair(x.reshape(lines * 8, WIDE))
                at = pl.multiple_of(d * (lines * 8), lines * 8)
                t = b * 3 + c
                out[pl.ds(at, lines * 8), t * 256 : (t + 1) * 256] = x
        return carry

    lax.fori_loop(0, planes, per_plane, 0)


def tap_weights(ref, at, out):
    def per_tap(i, carry):
        w = deep(ref[pl.ds(i * EMB + at, EMB), :])
        out[pl.ds(pl.multiple_of(i * 256, 256), 256), :] = weight_nn(w)
        return carry

    lax.fori_loop(0, 27, per_tap, 0)


def tap_weights_back(ref, at, out):
    for i in range(27):
        w = deep(ref[(26 - i) * EMB + at : (27 - i) * EMB + at, :])
        out[:, i * 256 : (i + 1) * 256] = weight_nt(w)


def conv(side, weights, planes, pitch, at_once, put, back=False):
    rows = at_once * pitch
    for start in range(0, planes, at_once):
        total = None
        for a in range(3):
            low = (start + a) * pitch
            x = side[low : low + rows, :]
            if back:
                part = dot_nt(x, weights[:, a * 2304 : (a + 1) * 2304])
            else:
                part = dot(x, weights[a * 2304 : (a + 1) * 2304, :])
            total = part if total is None else total + part
        put(start, fold(total))


def conv_weight_grad(side, grad_rows, pitch, out, at):
    rows = 512
    g = jnp.concatenate([grad_rows, jnp.zeros((rows - grad_rows.shape[0], WIDE), F32)], 0)
    left = jnp.concatenate(split(g.T[:EMB]), 0)
    for a in range(3):
        for bc in range(9):
            y = dot(left, side[a * pitch : a * pitch + rows, bc * 256 : (bc + 1) * 256])
            y = deep(fold_rows(fold(y))).T
            t = a * 9 + bc
            out[at + t * EMB : at + (t + 1) * EMB, :] = y[:EMB]


def volume_mask(sizes, planes, lines, reach, real_lines):
    slab, row = lax.axis_index("slab"), lax.axis_index("mp")
    ends = (slab == 0, slab == sizes[0] - 1, row == 0, row == sizes[1] - 1)
    shape = (planes, lines, 8, WIDE)
    d, h, w = iota(shape, 0), iota(shape, 1), iota(shape, 2)
    low_d = jnp.where(ends[0], reach, 0)
    high_d = jnp.where(ends[1], planes - reach, planes)
    low_h = jnp.where(ends[2], reach, 0)
    high_h = jnp.where(ends[3], real_lines - reach, real_lines)
    inside = (d >= low_d) & (d < high_d) & (h >= low_h) & (h < high_h) & (w < WIN)
    return jnp.where(inside, 1.0, 0.0)


def conv_kernel(
    sizes,
    own, s0, s1, s2, s3, labels, valid, weights0, weights1, vectors,
    grown, pre, tok, stats, t0, t1, t2, t3,
    act, side, side_own, marks,
):
    grown_lines(sizes, own, s0, s1, s2, s3, grown)
    put_marks(labels, valid, marks)
    taps(grown, 0, 11, 0, 10, side)
    bias0 = vectors[0:1, :]
    inside = volume_mask(sizes, 9, 10, 1, 9)


    def put(start, y):
        z = (y + bias0).reshape(3, 10, 8, WIDE)
        pre[start : start + 3] = z
        act[start : start + 3] = gelu(z) * inside[start : start + 3]

    conv(side, weights0, 9, 80, 3, put)
    taps(act, 0, 9, 0, 8, side_own)
    bias1 = vectors[1:2, :]
    sums = []

    def put_own(start, y):
        y = (y + bias1).reshape(WIN, 8, 8, WIDE)[:, 0:WIN]
        y = y + own[...].reshape(WIN, WIN, 8, WIDE)
        y = jnp.where(iota(y.shape, 2) < WIN, y, 0.0).reshape(PLANE, 8, WIDE)
        tok[...] = y + marks[...]
        send_sides(tok, t0, t1, t2, t3)
        flat = y.reshape(PLANE * 8, WIDE)
        sums.append(colsum(flat))
        sums.append(colsum(flat * flat))

    conv(side_own, weights1, WIN, 64, WIN, put_own)
    count = jnp.sum(marks[...].reshape(PLANE * 8, WIDE))
    row = iota((8, WIDE), 0)
    stats[...] = (
        jnp.where(row == 0, sums[0], 0.0)
        + jnp.where(row == 1, sums[1], 0.0)
        + jnp.where(row == 2, count, 0.0)
    )


def head_kernel(
    sizes, voxels,
    own, s0, s1, s2, s3, sums, vectors, head_w,
    grown, slope_out, stats, d_head, d_rows,
):
    grown_lines(sizes, own, s0, s1, s2, s3, grown)
    rows = 11 * 12 * 8
    both = grown[...].reshape(rows, WIDE)
    lane = iota((rows, WIDE), 1)
    tokens = jnp.where(lane < EMB, both, 0.0)
    target = jnp.where(lane < CLASSES, roll(both, WIDE - EMB, 1), 0.0)
    live = jnp.sum(target, 1, keepdims=True)
    count = F32(voxels)
    average = sums[0:1, :] / count
    spread = sums[1:2, :] / count - average * average
    inv = lax.rsqrt(spread + eps_norm)
    gain = vectors[2:3, :]
    bias = vectors[3:4, :]
    hat = (tokens - average) * inv
    act, slope = gelu_both(hat * gain + bias)
    act = jnp.where(lane == EMB, 1.0, act)
    w = head_w[...]
    logits = mm(act, w)
    logits = jnp.where(lane < CLASSES, logits, -1e30)
    top = jnp.max(logits, 1, keepdims=True)
    e = jnp.exp(logits - top)
    total = jnp.sum(e, 1, keepdims=True)
    logp = logits - top - jnp.log(total)
    scale = 1.0 / sums[2:3, 0:1]
    d_logits = (e / total * live - target) * scale
    d_normed = jnp.where(lane < EMB, mm_nt(d_logits, w) * slope, 0.0)
    d_tokens = d_normed * gain * inv
    slope_out[...] = d_tokens.reshape(11, 12, 8, WIDE)

    def own_rows(x):
        x = x.reshape(11, 12, 8, WIDE)[2:9, 2:9]
        x = jnp.where(iota(x.shape, 2) < WIN, x, 0.0)
        return x.reshape(PLANE * 8, WIDE)

    loss = -jnp.sum(own_rows(target * jnp.where(lane < CLASSES, logp, 0.0)))
    own_d = own_rows(d_logits)
    own_n = own_rows(d_normed)
    own_hat = own_rows(hat)
    zeros = jnp.zeros((512 - PLANE * 8, WIDE), F32)
    left = rows_t(jnp.concatenate([own_d, zeros], 0))
    d_head[...] = mm_tn(left, jnp.concatenate([own_rows(act), zeros], 0)).T
    d_gain = colsum(own_n * own_hat)
    d_bias = colsum(own_n)
    d_average = -d_bias * gain * inv
    d_spread = d_gain * gain * inv * inv * -0.5
    d_two = d_spread / count
    d_one = (d_average - 2.0 * average * d_spread) / count
    row = iota((8, WIDE), 0)
    live_lane = iota((8, WIDE), 1) < EMB
    stats[...] = (
        jnp.where((row == 0) & live_lane, d_one, 0.0)
        + jnp.where((row == 1) & live_lane, d_two, 0.0)
        + jnp.where(row == 2, loss, 0.0)
    )
    d_rows[...] = (
        jnp.where(row == 0, d_gain, 0.0)
        + jnp.where(row == 1, d_bias, 0.0)
    )


def sides_back_kernel(sizes, grown, pre, side_act, side_grown, act):
    act[0:9] = gelu(pre[...]) * volume_mask(sizes, 9, 10, 1, 9)
    act[9:10] = jnp.zeros((1, 10, 8, WIDE), F32)
    taps(act, 0, 10, 0, 8, side_act)
    taps(grown, 1, 10, 1, 8, side_grown)


def weights_back_kernel(conv0, conv1, weights0, weights1):
    tap_weights_back(conv0, 3, weights0)
    tap_weights_back(conv1, 0, weights1)


def conv_back_kernel(
    sizes,
    tok, slope, sums, pre, side_act, side_grown, weights0, weights1, d_rows, d_head,
    d_own, keep, send, carry, seam,
    grads, dgrown, act, side, side_own, flat,
):
    lane = iota((11, 12, 8, WIDE), 3)
    inside = volume_mask(sizes, 11, 12, 2, 11)
    steady = sums[0:1, :].reshape(1, 1, 1, WIDE)
    rising = 2.0 * sums[1:2, :].reshape(1, 1, 1, WIDE)
    d_tok = slope[...] + jnp.where(lane < EMB, (steady + tok[...] * rising) * inside, 0.0)
    dgrown[...] = d_tok
    grads[5191:, :] = jnp.zeros((45, WIDE), F32)
    grads[0:8, :] = jnp.zeros((8, WIDE), F32)
    grads[5189:5191, :] = d_rows[0:2, :]
    own = dgrown[2:9, 2:10]
    line = iota(own.shape, 1)
    own = jnp.where(line < WIN, own, 0.0).reshape(WIN * 64, WIDE)
    grads[5188:5189, :] = colsum(own)

    near = volume_mask(sizes, 9, 10, 1, 9)
    conv_weight_grad(side_act, own, 64, grads, 2596)
    taps(dgrown, 0, 11, 0, 10, side)


    def put(start, y):
        _, s = gelu_both(pre[start : start + 3])
        act[start : start + 3] = y.reshape(3, 10, 8, WIDE) * s * near[start : start + 3]

    conv(side, weights1, 9, 80, 3, put, back=True)

    own = act[1:8, 1:9]
    line = iota(own.shape, 1)
    own = jnp.where(line < WIN, own, 0.0).reshape(WIN * 64, WIDE)
    grads[2595:2596, :] = colsum(own)
    conv_weight_grad(side_grown, own, 64, grads, 3)
    carry[...] = grads[0:24, :]
    flat[3 * (GROUPS - CUTS[3]) :, :] = jnp.zeros((flat.shape[0] - 3912, WIDE), F32)
    flatten(grads, 20, GROUPS - CUTS[3], flat)
    start = 3 * CUTS[3]
    head_rows(d_head[...], flat, HEAD_ROW - start)
    seam[...] = flat[0 : LATE_ROWS - start, :]
    scatter(sizes, flat, LATE_ROWS - start, keep, send)
    taps(act, 0, 9, 0, 8, side_own)

    def put_own(start, y):
        y = y.reshape(WIN, 8, 8, WIDE)[:, 0:WIN] + dgrown[2:9, 2:9]
        y = jnp.where(iota(y.shape, 2) < WIN, y, 0.0)
        d_own[...] = y.reshape(PLANE, 8, WIDE)

    conv(side_own, weights0, WIN, 64, WIN, put_own, back=True)


def back_mlp_kernel(d_own, lay2, mid2, hpre2, d_mid, grads, dense):
    from_lines(d_own, dense)
    grads[...] = jnp.zeros_like(grads)
    d_mid[...] = mlp_back(dense[...], mid2[...], hpre2, Rows(lay2, 2), grads, 2)


def back_two_kernel(
    d_mid2, grads2, carry, lay1, lay2, tok2, save, lse, mixed, mid1, hpre1,
    d_mid, grads1, flat, carry2, pa, pb, pc,
    grads, *sc,
):
    layer = Rows(lay2, 2)
    grads[0:1168, :] = grads2[...]
    d = d_mid2[...]
    tokens = tok2[...]
    normed = norm(tokens, layer[0:1, :], layer[1:2, :])
    d_normed = attention_back(d, normed, layer, save, lse, mixed, sc, grads, 2)
    d = d + pre_norm_back(d_normed, tokens, layer, grads, 2)
    grads[1167:1184, :] = carry[3:20, :]
    flatten(grads, 32, CUTS[3] - CUTS[2], flat)
    carry2[...] = grads[0:32, :]
    layer = Rows(lay1, 1)
    d = mlp_back(d, mid1[...], hpre1, layer, grads1, 1)
    d_mid[...] = d
    send_parts(d_mid, pa, pb, pc)


def back_shifted_kernel(
    sizes,
    own, pa, pb, pc, lay1, window, save, lse, mixed, grads1, carry2, _,
    d_window, flat, carry1, qa, qb, qc,
    region, grads, grad, *sc,
):
    put_region(region, sizes)
    take_parts(own, pa, pb, pc, grad)
    grads[0:1168, :] = grads1[...]
    grads[0:3, :] = jnp.zeros((3, WIDE), F32)
    d_window[...] = attention_back(
        grad[...], window[...], Rows(lay1, 1), save, lse, mixed, sc, grads, 1,
        region,
    )
    send_parts(d_window, qa, qb, qc)
    grads[1166:1196, :] = carry2[2:32, :]
    flatten(grads, 12, CUTS[2] - CUTS[1], flat)
    carry1[...] = grads[0:16, :]


def back_first_kernel(
    sizes,
    d_mid, own, qa, qb, qc, tok1, lay0, lay1, merge, dense, tok0, save, lse, mixed, middle, hpre,
    carry1, flat1, flat2, seam, *rest,
):
    keep, send, flat, grads, grad, *sc = rest[3:]
    take_parts(own, qa, qb, qc, grad)
    grads[1556:1572, :] = carry1[...]
    d = d_mid[...] + pre_norm_back(grad[...], tok1[...], Rows(lay1, 1), grads, 1557)
    layer = Rows(lay0, 0)
    at = MERGE_ROWS
    d = mlp_back(d, middle[...], hpre, layer, grads, at)
    tokens = tok0[...]
    normed = norm(tokens, layer[0:1, :], layer[1:2, :])
    d_normed = attention_back(d, normed, layer, save, lse, mixed, sc, grads, at)
    d = d + pre_norm_back(d_normed, tokens, layer, grads, at)
    live = iota((ROWS, WIDE), 0) < VOX
    d = jnp.where(live, d, 0.0)
    hat = merged_norm(dense[...])
    gain = hidden_rows(merge, 0, 1)
    bias = hidden_rows(merge, 4, 1)
    w = merge[8 : 8 + MERGE, :]
    put_hidden_rows(grads, 8 - 8, 1, jnp.zeros((1, MERGE), F32))
    grads[8 : 8 + MERGE, :] = mm_tn(rows_t(d), hat * gain + bias).T
    d_hat = mm_nt(d, w)
    put_hidden_rows(grads, 0, 1, colsum(d_hat * hat))
    put_hidden_rows(grads, 4, 1, colsum(d_hat))
    flatten(grads, 0, CUTS[1], flat)
    at = 0
    for cut, part in ((CUTS[1], flat1), (CUTS[2], flat2), (CUTS[3], seam)):
        at = 3 * cut
        flat[at : at + part.shape[0], :] = part[...]
    at += seam.shape[0]
    if flat.shape[0] > at:
        flat[at:, :] = jnp.zeros((flat.shape[0] - at, WIDE), F32)
    scatter(sizes, flat, 0, keep, send)


def radices(count):
    steps = [2]
    left = count // 2
    while left > 1:
        steps.append(4 if left >= 4 else 2)
        left //= steps[-1]
    return steps


def block_rows(rows, count):
    return -(-rows // (8 * count)) * 8


def own_number(sizes):
    return lax.axis_index("slab") * sizes[1] + lax.axis_index("mp")


def place_in_half(distance, count):
    place = 0
    shift = 1
    for radix in radices(count)[1:]:
        digit = jnp.bitwise_and(lax.shift_right_logical(distance, shift), radix - 1)
        place = place * radix + digit
        shift += radix.bit_length() - 1
    return place


def scatter(sizes, source, first, keep, send):
    count = sizes[0] * sizes[1]
    rows = keep.shape[0] * 2 // count
    me = own_number(sizes)
    odd = jnp.bitwise_and(me, 1)

    def per_pair(t, carry):
        for block, out in ((2 * t + odd, keep), (2 * t + 1 - odd, send)):
            place = place_in_half(jnp.bitwise_xor(block, me), count)
            at = pl.multiple_of(first + block * rows, 8)
            to = pl.multiple_of(place * rows, 8)
            out[pl.ds(to, rows), :] = source[pl.ds(at, rows), :]
        return carry

    lax.fori_loop(0, count // 2, per_pair, 0)


def traded(value, distance, count):
    pairs = [(i, i ^ distance) for i in range(count)]
    return lax.ppermute(value, ("slab", "mp"), pairs)


def add_kernel(count, outs, *refs):
    total = refs[0][...]
    for ref in refs[1:count]:
        total = total + ref[...]
    rows = total.shape[0] // outs
    for i, out in enumerate(refs[len(refs) - outs :]):
        out[...] = total[i * rows : (i + 1) * rows]


def added(got, parts, after):
    rows = got[0].shape[0] // parts
    return call(
        functools.partial(add_kernel, len(got), parts), [arr(rows, WIDE)] * parts, [], *got,
        name="add", us=0.3, far=after,
    )


def join_kernel(count, *refs):
    rows = refs[0].shape[0]
    for i, ref in enumerate(refs[:count]):
        refs[-1][i * rows : (i + 1) * rows, :] = ref[...]


def joined(got, after):
    (out,) = call(
        functools.partial(join_kernel, len(got)), [arr(len(got) * got[0].shape[0], WIDE)], [], *got,
        name="join", us=0.3, far=after,
    )
    return out


def summing(keep, send, count):
    steps = radices(count)
    got = [keep, traded(send, 1, count)]
    shift = 1
    after = yield got
    for radix in steps[1:]:
        parts = added(got, radix, after)
        got = [parts[0]] + [traded(parts[k], k << shift, count) for k in range(1, radix)]
        shift += radix.bit_length() - 1
        after = yield got
    (own,) = added(got, 1, after)
    for radix in reversed(steps[1:]):
        shift -= radix.bit_length() - 1
        got = [own] + [traded(own, k << shift, count) for k in range(1, radix)]
        after = yield got
        own = joined(got, after)
    yield own, traded(own, 1, count)


def exchanged_sum(value, count):
    shift = 0
    for radix in radices(count):
        got = [value] + [traded(value, k << shift, count) for k in range(1, radix)]
        while len(got) > 1:
            got = [got[i] + got[i + 1] for i in range(0, len(got), 2)]
        value = got[0]
        shift += radix.bit_length() - 1
    return value


PIECE = 262144


def adamw_kernel(
    sizes,
    late, late_other, early, early_other, tail, sums, params, first, second,
    new_params, new_first, new_second, loss, valid, norm_out,
    grad, scale_ref,
):
    count = sizes[0] * sizes[1]
    step = pl.program_id(0)

    @pl.when(step == 0)
    def gather():
        me = own_number(sizes)
        total = jnp.zeros((8, WIDE), F32)
        for ref in (late, late_other, early, early_other):
            x = ref[...]
            total = total + jnp.sum((x * x).reshape(-1, 8, WIDE), 0)
        norm = jnp.sqrt(jnp.sum(total))
        loss[0] = jnp.sum(tail[2:3, 0:1])
        valid[0] = jnp.sum(sums[2:3, 0:1])
        norm_out[0] = norm
        scale_ref[0] = jnp.minimum(1.0, clip_norm / (norm + 1e-06))
        start = 0
        for own, other, size in ((late, late_other, LATE_ROWS), (early, early_other, EARLY_ROWS)):
            rows = own.shape[0] * 2 // count

            def per_block(block, carry, own=own, other=other, rows=rows, start=start):
                distance = jnp.bitwise_xor(block, me)
                at = pl.ds(pl.multiple_of(place_in_half(distance, count) * rows, 8), rows)
                near = jnp.bitwise_and(distance, 1) == 0
                to = pl.ds(pl.multiple_of(start + block * rows, 8), rows)
                grad[to, :] = jnp.where(near, own[at, :], other[at, :])
                return carry

            lax.fori_loop(0, size // rows, per_block, 0)
            start += size

    def update(base, low, size):
        rows = -(-size // 1024) * 8
        at = pl.ds(pl.multiple_of(base // WIDE + low // WIDE, 8), rows)
        g = grad[at, :].reshape(rows * WIDE)[:size] * scale_ref[0]
        here = pl.ds(pl.multiple_of(base + low, 1024), size)
        one = beta_one * first[here] + (1.0 - beta_one) * g
        two = beta_two * second[here] + (1.0 - beta_two) * g * g
        there = pl.ds(low, size)
        new_first[there] = one
        new_second[there] = two
        two = two * (1.0 / (1.0 - beta_two**STEP))
        low_by = two * lax.rsqrt(jnp.maximum(two, 1e-37)) + adam_eps
        inverse = pl.reciprocal(low_by, approx=True)
        inverse = inverse * (2.0 - low_by * inverse)
        new_params[there] = params[here] * (1.0 - learn_rate * decay_rate) - (
            one * (learn_rate / (1.0 - beta_one**STEP))
        ) * inverse

    whole = NPARAM // PIECE

    @pl.when(step < whole)
    def full():
        def part(i, carry):
            low = pl.multiple_of(i * 16384, 16384)
            update(step * PIECE, low, 16384)
            return carry

        lax.fori_loop(0, PIECE // 16384, part, 0)

    @pl.when(step == whole)
    def last():
        rest = NPARAM - whole * PIECE
        main = rest // 1024 * 1024
        for low in range(0, main, 16384):
            update(whole * PIECE, low, min(16384, main - low))
        update(whole * PIECE, main, rest - main)


def adamw(sizes, parts, arrays):
    pieces = -(-NPARAM // PIECE)
    piece = pl.BlockSpec((PIECE,), lambda i: (i,))
    vmem = pl.BlockSpec(memory_space=pltpu.VMEM)
    smem = pl.BlockSpec(memory_space=pltpu.SMEM)
    return pl.pallas_call(
        functools.partial(adamw_kernel, sizes),
        grid=(pieces,),
        out_shape=[arr(NPARAM)] * 3 + [arr(1)] * 3,
        in_specs=[vmem] * (len(parts) + len(arrays)),
        out_specs=[piece] * 3 + [smem] * 3,
        scratch_shapes=[pltpu.VMEM((LATE_ROWS + EARLY_ROWS, WIDE), F32), pltpu.SMEM((1,), F32)],
        compiler_params=pltpu.CompilerParams(vmem_limit_bytes=16 * 1024 * 1024),
        cost_estimate=pl.CostEstimate(flops=6 * 10**9, bytes_accessed=0, transcendentals=0),
        name="adamw",
    )(*parts, *arrays)


def arr(*shape):
    return jax.ShapeDtypeStruct(shape, F32)


def call(kernel, outs, scratch, *args, name=None, us=1.0, far=(), mib=16):
    vmem = pl.BlockSpec(memory_space=pltpu.VMEM)
    smem = pl.BlockSpec(memory_space=pltpu.SMEM)
    return pl.pallas_call(
        kernel,
        out_shape=list(outs),
        in_specs=[vmem] * len(args) + [pl.BlockSpec(memory_space=pl.ANY)] * len(far),
        out_specs=[smem if o.shape == (1,) else vmem for o in outs],
        scratch_shapes=list(scratch),
        compiler_params=pltpu.CompilerParams(vmem_limit_bytes=mib * 1024 * 1024),
        cost_estimate=pl.CostEstimate(
            flops=int(us * 1.15e9), bytes_accessed=0, transcendentals=0
        ),
        name=name,
    )(*args, *far)


SQUARE = arr(ROWS, WIDE)
SAVE = arr(ROWS, 3 * WIDE)
FORWARD = [
    pltpu.VMEM((2, ROWS, 2 * WIDE), BF16),
    pltpu.VMEM((2, ROWS, 2 * WIDE), BF16),
    pltpu.VMEM((2 * ROWS, 2 * WIDE), BF16),
]
BACKWARD = [
    pltpu.VMEM((2, ROWS, 2 * WIDE), BF16),
    pltpu.VMEM((2, ROWS, 2 * WIDE), BF16),
    pltpu.VMEM((2, ROWS, 2 * WIDE), BF16),
    pltpu.VMEM((2, ROWS, 2 * WIDE), BF16),
    pltpu.VMEM((2 * ROWS, 2 * WIDE), BF16),
    pltpu.VMEM((ROWS, WIDE), F32),
    pltpu.VMEM((2, WIDE, ROWS), F32),
    pltpu.VMEM((2, ROWS, 2 * ROWS), BF16),
    pltpu.VMEM((2, ROWS, 2 * ROWS), BF16),
    pltpu.VMEM((2, WIDE, ROWS), BF16),
    pltpu.VMEM((2, WIDE, ROWS), BF16),
    pltpu.VMEM((ROWS, WIDE), F32),
    pltpu.VMEM((ROWS, 2 * ROWS), F32),
    pltpu.VMEM((ROWS, 2 * ROWS), F32),
    pltpu.VMEM((2 * ROWS, 2 * WIDE), BF16),
    pltpu.VMEM((2 * ROWS, 2 * WIDE), BF16),
]
PARTS = [arr(ROWS_A, WIDE), arr(ROWS_B, WIDE), arr(ROWS_C, WIDE)]


def passed(parts, steps, sizes):
    slabs, rows = sizes
    moved = []
    for part, (ds, dm) in zip(parts, ((1, 0), (0, 1), (1, 1))):
        pairs = []
        for s in range(slabs):
            for m in range(rows):
                target = ((s + steps * ds) % slabs) * rows + (m + steps * dm) % rows
                pairs.append((s * rows + m, target))
        moved.append(lax.ppermute(part, ("slab", "mp"), pairs))
    return moved


SIDES = [arr(2 * WIN, 8, WIDE)] * 4


def paired(axis, size):
    near = [(i, i ^ 1) for i in range(size)]
    far = [(i, (i + (1 if i % 2 else -1)) % size) for i in range(size)]
    return (
        lambda value: lax.ppermute(value, axis, near),
        lambda value: lax.ppermute(value, axis, far),
    )


def column_kernel(sizes, near_d, far_d, near_h, far_h, near_out, far_out):
    slab = lax.axis_index("slab")
    odd_d = jnp.bitwise_and(slab, 1) == 1
    odd_h = jnp.bitwise_and(lax.axis_index("mp"), 1) == 1
    at_low = slab == 0
    at_high = slab == sizes[0] - 1
    near_out[4:18] = near_h[...]
    far_out[4:18] = far_h[...]
    for d in range(2):
        near = near_d[d * WIN : (d + 1) * WIN]
        far = far_d[d * WIN : (d + 1) * WIN]
        before = jnp.where(odd_d, near, jnp.where(at_low, 0.0, far))
        after = jnp.where(odd_d, jnp.where(at_high, 0.0, far), near)
        for x, at in ((before, 2 * d), (after, 18 + 2 * d)):
            low, high = x[0:2], x[WIN - 2 : WIN]
            near_out[at : at + 2] = jnp.where(odd_h, low, high)
            far_out[at : at + 2] = jnp.where(odd_h, high, low)


def beside(sides, sizes):
    near, far = paired("slab", sizes[0])
    near_d, far_d = near(sides[0]), far(sides[1])
    near_h, far_h = call(
        functools.partial(column_kernel, sizes), [arr(22, 8, WIDE)] * 2, [],
        near_d, far_d, sides[2], sides[3],
        name="column", us=0.3,
    )
    near, far = paired("mp", sizes[1])
    return near_d, far_d, near(near_h), far(far_h)


REGION = [pltpu.VMEM((ROWS, ROWS), F32)]


def on_device(sizes, feats, labels, valid, params, moment_one, moment_two):
    slabs, rows = sizes
    count = slabs * rows

    def room(spans):
        sizes = [(span_of(groups)[1] + 8) * WIDE for groups in spans]
        return [
            [pltpu.VMEM((size,), F32) for size in sizes],
            pltpu.VMEM((2048, WIDE), F32),
            pltpu.SemaphoreType.DMA((len(spans),)),
        ]

    first_size = FIRST_SPANS[-1][1] * 384
    merge, lay0 = call(
        functools.partial(prep_kernel, FIRST_SPANS),
        [arr(MERGE_ROWS, WIDE), arr(1176, WIDE)],
        room(FIRST_SPANS),
        name="prep_first", us=2.0, far=(params[:first_size],),
    )
    lay1, lay2 = call(
        functools.partial(prep_kernel, LAYER_SPANS),
        [arr(1168, WIDE)] * 2,
        room(LAYER_SPANS),
        name="prep_layers", us=2.0, far=(params,),
    )
    conv0, conv1, head_w, weights0, weights1, vectors = call(
        prep_conv_kernel,
        [arr(2596, WIDE), arr(2640, WIDE), arr(WIDE, WIDE)]
        + [jax.ShapeDtypeStruct((27 * 256, 256), BF16)] * 2
        + [arr(8, WIDE)],
        room(CONV_SPANS),
        params[NPARAM // WIDE * WIDE :],
        name="prep_conv", us=4.0, far=(params,),
    )

    dense, tok0, save0, lse0, mixed0, mid0, hpre0, tok1, ahead, *parts = call(
        first_kernel,
        [arr(ROWS, MERGE), SQUARE, SAVE, SQUARE, SQUARE, SQUARE, arr(ROWS, HID), SQUARE, SQUARE]
        + PARTS,
        FORWARD,
        feats.reshape(PLANE, WIN, MERGE), merge, lay0,
        name="first", us=6.0,
    )
    parts = passed(parts, -1, sizes)
    window, save1, lse1, mixed1, out1, *parts = call(
        functools.partial(shifted_kernel, sizes),
        [SQUARE, SAVE, SQUARE, SQUARE, SQUARE] + PARTS,
        REGION + FORWARD,
        ahead, *parts, lay1,
        name="shifted", us=4.5,
    )
    parts = passed(parts, 1, sizes)
    mid1, hpre1, tok2, save2, lse2, mixed2, mid2, hpre2, lines, *sides = call(
        second_kernel,
        [SQUARE, arr(ROWS, HID), SQUARE, SAVE, SQUARE, SQUARE, SQUARE, arr(ROWS, HID)]
        + [arr(PLANE, 8, WIDE)] + SIDES,
        [pltpu.VMEM((ROWS, WIDE), F32)] + FORWARD,
        tok1, out1, *parts, lay1, lay2,
        name="second", us=6.5, far=(weights0,),
    )
    sides = beside(sides, sizes)
    grown, pre, tok3, sums, *tok_sides = call(
        functools.partial(conv_kernel, sizes),
        [arr(11, 12, 8, WIDE), arr(9, 10, 8, WIDE), arr(PLANE, 8, WIDE), arr(8, WIDE)] + SIDES,
        [
            pltpu.VMEM((9, 10, 8, WIDE), F32),
            pltpu.VMEM((880, 2304), BF16),
            pltpu.VMEM((576, 2304), BF16),
            pltpu.VMEM((PLANE, 8, WIDE), F32),
        ],
        lines, *sides, labels, valid, weights0, weights1, vectors,
        name="conv", us=8.0, mib=20,
    )
    tok_sides = beside(tok_sides, sizes)
    side_act, side_grown = call(
        functools.partial(sides_back_kernel, sizes),
        [jax.ShapeDtypeStruct((640, 2304), BF16)] * 2,
        [pltpu.VMEM((10, 10, 8, WIDE), F32)],
        grown, pre,
        name="sides_back", us=2.0,
    )
    weights0, weights1 = call(
        weights_back_kernel,
        [jax.ShapeDtypeStruct((256, 27 * 256), BF16)] * 2,
        [],
        conv0, conv1,
        name="weights_back", us=1.5,
    )
    sums = exchanged_sum(sums, count)
    voxels = WIN * slabs * WIN * rows * WIN
    tok3, slope, tail, d_head, d_rows = call(
        functools.partial(head_kernel, sizes, voxels),
        [arr(11, 12, 8, WIDE), arr(11, 12, 8, WIDE), arr(8, WIDE), arr(WIDE, WIDE), arr(8, WIDE)],
        [],
        tok3, *tok_sides, sums, vectors, head_w,
        name="head", us=3.5,
    )
    tail = exchanged_sum(tail, count)
    late_rows = block_rows(LATE_ROWS, count) * count
    early_rows = block_rows(EARLY_ROWS, count) * count
    seam_rows = LATE_ROWS - 3 * CUTS[3]
    d_own, keep, send, carry3, seam = call(
        functools.partial(conv_back_kernel, sizes),
        [arr(PLANE, 8, WIDE)] + [arr(early_rows // 2, WIDE)] * 2
        + [arr(24, WIDE), arr(seam_rows, WIDE)],
        [
            pltpu.VMEM((5236, WIDE), F32),
            pltpu.VMEM((11, 12, 8, WIDE), F32),
            pltpu.VMEM((10, 10, 8, WIDE), F32),
            pltpu.VMEM((880, 2304), BF16),
            pltpu.VMEM((576, 2304), BF16),
            pltpu.VMEM((seam_rows + early_rows, WIDE), F32),
        ],
        tok3, slope, tail, pre, side_act, side_grown, weights0, weights1, d_rows, d_head,
        name="conv_back", us=14.0, mib=28,
    )
    early = summing(keep, send, count)
    next(early)
    d_mid2, grads2 = call(
        back_mlp_kernel,
        [SQUARE, arr(1168, WIDE)],
        [pltpu.VMEM((ROWS, WIDE), F32)],
        d_own, lay2, mid2, hpre2,
        name="back_mlp", us=1.5,
    )
    d_mid, grads1, flat2, carry2, *parts = call(
        back_two_kernel,
        [SQUARE, arr(1168, WIDE), arr(3 * (CUTS[3] - CUTS[2]), WIDE), arr(32, WIDE)] + PARTS,
        [pltpu.VMEM((1184, WIDE), F32)] + BACKWARD,
        d_mid2, grads2, carry3, lay1, lay2, tok2, save2, lse2, mixed2, mid1, hpre1,
        name="back_two", us=7.0,
    )
    got = early.send((d_mid,))
    parts = passed(parts, -1, sizes)
    d_window, flat1, carry1, *parts = call(
        functools.partial(back_shifted_kernel, sizes),
        [SQUARE, arr(3 * (CUTS[2] - CUTS[1]), WIDE), arr(16, WIDE)] + PARTS,
        REGION + [pltpu.VMEM((1200, WIDE), F32), pltpu.VMEM((ROWS, WIDE), F32)] + BACKWARD,
        d_mid, *parts, lay1, window, save1, lse1, mixed1, grads1, carry2,
        name="back_shifted", us=6.0, far=(got[0],),
    )
    parts = passed(parts, 1, sizes)
    late = call(
        functools.partial(back_first_kernel, sizes),
        [arr(late_rows // 2, WIDE)] * 2,
        [
            pltpu.VMEM((late_rows, WIDE), F32),
            pltpu.VMEM((1572, WIDE), F32),
            pltpu.VMEM((ROWS, WIDE), F32),
        ]
        + BACKWARD,
        d_mid, d_window, *parts, tok1, lay0, lay1, merge, dense, tok0, save0, lse0, mixed0, mid0,
        hpre0, carry1, flat1, flat2, seam,
        name="back_first", us=8.0, far=got[1:],
    )
    more = radices(count)[3:]
    late = summing(*late, count)
    next(late)
    got = early.send(())
    for _ in more:
        got = early.send(())
    kept = late.send(tuple(got[1:]))
    early.send((kept[0],))
    for _ in more:
        early.send(())
    got = early.send(())
    late.send((got[0],))
    for _ in more:
        late.send(())
    late.send(())
    for _ in more:
        late.send(())
    kept = late.send(tuple(got[1:]))
    early = early.send((kept[0],))
    late = late.send(())
    new_params, new_first, new_second, loss, valid_count, norm = adamw(
        sizes, (*late, *early, tail, sums), (params, moment_one, moment_two)
    )
    return (
        loss.reshape(()), valid_count.reshape(()), norm.reshape(()),
        new_params, new_first, new_second,
    )


def solution(mesh):
    placed = (
        P("slab", "mp", None, None),
        P("slab", "mp", None),
        P("slab", "mp", None),
        P(),
        P(),
        P(),
    )
    sizes = (mesh.shape["slab"], mesh.shape["mp"])
    return jax.shard_map(
        functools.partial(on_device, sizes),
        mesh=mesh,
        in_specs=placed,
        out_specs=(P(), P(), P(), P(), P(), P()),
        check_vma=False,
    )
```

```python
import functools

import jax
import jax.numpy as jnp
from jax import lax
from jax.experimental import pallas as pl
from jax.experimental.pallas import tpu as pltpu
from jax.sharding import PartitionSpec as P

EMB = 96
HEADS = 6
HDIM = 16
HID = 384
MERGE = 384
CLASSES = 14
WIN = 7
SHIFT = 3
LAYERS = 3
STEP = 10

F32 = jnp.float32
BF16 = jnp.bfloat16
eps_norm = 1e-05
beta_one = 0.9
beta_two = 0.999
adam_eps = 1e-08
learn_rate = 0.05
decay_rate = 0.05
clip_norm = 0.01
LOG2E = 1.4426950408889634

VOX = WIN * WIN * WIN
ROWS = 384
BLK = 128
WIDE = 128
PLANE = WIN * WIN
FAR = WIN - SHIFT
ROWS_A = SHIFT * FAR * WIN
ROWS_B = FAR * SHIFT * WIN
ROWS_C = SHIFT * SHIFT * WIN

MERGE_ROWS = 392
LAYER_ROWS = 1165
TAP_ROWS = 27 * EMB
GROUPS = 2280
NPARAM = 872558
HEAD_ROW = 6806
HEAD_ROWS = 11
HEAD_LANE = 32
LATE_ROWS = 3072
EARLY_ROWS = 3840
LAYER_BASE = (98, 389, 680)
CONV_BASE = (971, 1620)
CUTS = (0, 392, 688, 976, 2280)

R_QKV, R_QKVB, R_PROJ, R_PROJB = 4, 292, 295, 391
R_HID, R_HIDB, R_OUT, R_OUTB = 392, 776, 780, 1164


def iota(shape, dim):
    return lax.broadcasted_iota(jnp.int32, shape, dim)


def split(x):
    hi = x.astype(BF16)
    return hi, (x - hi.astype(F32)).astype(BF16)


def pair(x):
    return jnp.concatenate(split(x), 1)


def fold(y):
    half = y.shape[1] // 2
    return y[:, :half] + y[:, half:]


def fold_rows(y):
    half = y.shape[0] // 2
    return y[:half] + y[half:]


def dot(a, b):
    return jnp.dot(a, b, preferred_element_type=F32)


def dot_nt(a, b):
    return lax.dot_general(a, b, (((1,), (1,)), ((), ())), preferred_element_type=F32)


def weight_nn(w):
    top = pair(w)
    return jnp.concatenate([top, top], 0)


def weight_nt(w):
    hi, lo = split(w)
    return jnp.concatenate(
        [jnp.concatenate([hi, hi], 1), jnp.concatenate([lo, lo], 1)], 0
    )


def mm(x, w):
    return fold(dot(pair(x), weight_nn(w)))


def mm_nt(x, w):
    return fold(dot_nt(pair(x), weight_nt(w)))


def rows_t(x):
    return jnp.concatenate(split(x.T), 0)


def mm_tn(xt, y):
    return fold_rows(fold(dot(xt, pair(y))))


def deep(w):
    return jnp.concatenate([w, jnp.zeros((WIDE - EMB, w.shape[1]), F32)], 0)


def roll(x, shift, axis):
    return pltpu.roll(x, shift, axis)


def four_to_three(y):
    lane = iota(y[0].shape, 1)
    a = jnp.where(lane < 96, y[0], roll(y[1], 96, 1))
    b = jnp.where(lane < 64, roll(y[1], 96, 1), roll(y[2], 64, 1))
    c = jnp.where(lane < 32, roll(y[2], 64, 1), roll(y[3], 32, 1))
    return a, b, c


def three_to_four(x):
    lane = iota(x[0].shape, 1)
    live = lane < EMB
    a = x[0]
    b = jnp.where(lane < 32, roll(x[0], 32, 1), roll(x[1], 32, 1))
    c = jnp.where(lane < 64, roll(x[1], 64, 1), roll(x[2], 64, 1))
    d = roll(x[2], 96, 1)
    return tuple(jnp.where(live, v, 0.0) for v in (a, b, c, d))


def hidden_rows(ref, start, count):
    return jnp.concatenate(
        four_to_three([ref[pl.ds(start + c, count, stride=4), :] for c in range(4)]), 1
    )


def put_hidden_rows(ref, start, count, x):
    parts = three_to_four([x[:, i * WIDE : (i + 1) * WIDE] for i in range(3)])
    for c in range(4):
        ref[pl.ds(start + c, count, stride=4), :] = parts[c]


def flatten(ref, start, groups, out):
    parts = four_to_three([ref[pl.ds(start + c, groups, stride=4), :] for c in range(4)])
    for c in range(3):
        out[pl.ds(c, groups, stride=3), :] = parts[c]


def norm_stats(x):
    live = iota(x.shape, 1) < EMB
    mean = jnp.sum(x, 1, keepdims=True) * (1.0 / EMB)
    centred = jnp.where(live, x - mean, 0.0)
    var = jnp.sum(centred * centred, 1, keepdims=True) * (1.0 / EMB)
    inv = lax.rsqrt(var + eps_norm)
    return centred * inv, inv


def norm(x, gain, bias):
    hat, _ = norm_stats(x)
    return hat * gain + bias


def norm_back(hat, inv, gain, grad):
    up = grad * gain
    one = jnp.sum(up, 1, keepdims=True) * (1.0 / EMB)
    two = jnp.sum(up * hat, 1, keepdims=True) * (1.0 / EMB)
    live = iota(hat.shape, 1) < EMB
    return jnp.where(live, inv * (up - one - hat * two), 0.0)


def colsum(x):
    return jnp.sum(x, 0, keepdims=True)


def gelu(x):
    return 0.5 * x * (1.0 + lax.erf(x * (0.5**0.5)))


def gelu_both(x):
    cdf = 0.5 * (1.0 + lax.erf(x * (0.5**0.5)))
    slope = cdf + x * (jnp.exp(x * x * -0.5) * 0.3989422804014327)
    return x * cdf, slope


def head_groups(x):
    lane = iota(x.shape, 1)
    swapped = roll(x, 64, 1)
    return jnp.where(lane < 64, x, swapped), jnp.where(lane < 64, swapped, x)


def as_left(x):
    both = []
    low = iota(x.shape, 1) < 64
    for part in head_groups(x):
        hi = part.astype(BF16).astype(F32)
        one = jnp.where(low, hi, part - hi).astype(BF16)
        both.append(jnp.concatenate([one, one], 1))
    return both


def as_right(x):
    return [pair(part) for part in head_groups(x)]


def head_mask(h, width):
    lane = iota((1, width), 1)
    lane = jnp.bitwise_and(lane, 63)
    low = jnp.bitwise_and(h, 3) * HDIM
    return jnp.where((lane >= low) & (lane < low + HDIM), 1.0, 0.0)


def own_lanes(h):
    lane = iota((1, WIDE), 1)
    return jnp.where((lane >= h * HDIM) & (lane < (h + 1) * HDIM), 1.0, 0.0)


def both_heads(right, heads, out):
    for k, h in enumerate(heads):
        out[k * ROWS : (k + 1) * ROWS, :] = right * head_mask(h, 2 * WIDE).astype(BF16)


def score_tiles(s, rows, region):
    tiles = [s[:, i * WIDE : (i + 1) * WIDE] for i in range(3)]
    if region is not None:
        return [t + region[rows, i * WIDE : (i + 1) * WIDE] for i, t in enumerate(tiles)]
    pad = jnp.where(iota((1, WIDE), 1) < VOX - 2 * WIDE, 0.0, -1e30)
    return tiles[:2] + [tiles[2] + pad]


def put_split(ref, rows, i, x):
    hi, lo = split(x)
    ref[rows, i * WIDE : (i + 1) * WIDE] = hi
    ref[rows, ROWS + i * WIDE : ROWS + (i + 1) * WIDE] = lo


def attention(normed, layer, save, lse, mixed, sc, region=None):
    left, right, values = sc
    x = pair(normed)
    qkv = []
    for i in range(3):
        w = deep(layer[pl.ds(R_QKV + i, EMB, stride=3), :])
        y = fold(dot(x, weight_nn(w))) + layer[R_QKVB + i : R_QKVB + i + 1, :]
        if i == 0:
            y = y * (HDIM**-0.5 * LOG2E)
        save[:, i * WIDE : (i + 1) * WIDE] = y
        qkv.append(y)
    for g, part in enumerate(as_left(qkv[0])):
        left[g] = part
    for g, part in enumerate(as_right(qkv[1])):
        right[g] = part
    v = pair(jnp.where(iota((ROWS, WIDE), 1) == EMB, 1.0, qkv[2]))
    values[0:ROWS, :] = v
    values[ROWS : 2 * ROWS, :] = v
    mixed[...] = jnp.zeros_like(mixed)
    lse[...] = jnp.zeros_like(lse)

    def per_pair(pair_of, carry):
        heads = [2 * pair_of, 2 * pair_of + 1]
        masks = [head_mask(h, 2 * WIDE).astype(BF16) for h in heads]
        lanes = [own_lanes(h) for h in heads]
        spots = [jnp.where(iota((1, WIDE), 1) == h, 1.0, 0.0) for h in heads]
        g = lax.div(pair_of, 2)
        for b in range(ROWS // BLK):
            rows = slice(b * BLK, (b + 1) * BLK)
            out = level = 0.0
            for k in range(2):
                s = dot_nt(left[g, rows, :] * masks[k], right[g])
                tiles = score_tiles(s, rows, region)
                top = jnp.maximum(jnp.maximum(tiles[0], tiles[1]), tiles[2])
                top = jnp.max(top, 1, keepdims=True)
                parts = [split(jnp.exp2(t - top)) for t in tiles]
                e = jnp.concatenate([p[0] for p in parts] + [p[1] for p in parts], 1)
                o = fold(dot(e, values[...]))
                total = o[:, EMB : EMB + 1]
                out = out + o * (lanes[k] / total)
                level = level + (top + jnp.log(total) * LOG2E) * spots[k]
            mixed[rows, :] += out
            lse[rows, :] += level
        return carry

    lax.fori_loop(0, HEADS // 2, per_pair, 0)
    proj = deep(layer[R_PROJ : R_PROJ + EMB, :])
    return mm(mixed[...], proj) + layer[R_PROJB : R_PROJB + 1, :]


def attention_back(grad, normed, layer, save, lse, mixed, sc, grads, at, region=None):
    left, right, gleft, vright, keys, dq, dkv_t, weights, slopes = sc[:9]
    q_t, do_t, dmix, s, dp, two_keys, two_values = sc[9:]
    proj = deep(layer[R_PROJ : R_PROJ + EMB, :])
    grads[at + R_PROJ : at + R_PROJ + EMB, :] = mm_tn(rows_t(mixed[...]), grad)[:EMB]
    grads[at + R_PROJB : at + R_PROJB + 1, :] = colsum(grad)
    d_mixed = mm_nt(grad, proj)
    dmix[...] = d_mixed * mixed[...]
    q, k, v = (save[:, i * WIDE : (i + 1) * WIDE] for i in range(3))
    for g, part in enumerate(as_left(q)):
        left[g] = part
    for g, part in enumerate(as_right(k)):
        right[g] = part
    for g, part in enumerate(as_left(d_mixed)):
        gleft[g] = part
    for g, part in enumerate(as_right(v)):
        vright[g] = part
    kk = pair(k)
    keys[0:ROWS, :] = kk
    keys[ROWS : 2 * ROWS, :] = kk
    for ref, x in ((q_t, q), (do_t, d_mixed)):
        hi, lo = split(x.T)
        ref[0] = hi
        ref[1] = lo
    dq[...] = jnp.zeros_like(dq)
    dkv_t[...] = jnp.zeros_like(dkv_t)

    def per_pair(pair_of, carry):
        g = lax.div(pair_of, 2)
        heads = [2 * pair_of, 2 * pair_of + 1]
        both_heads(right[g], heads, two_keys)
        both_heads(vright[g], heads, two_values)
        s[...] = dot_nt(left[g], two_keys[...])
        dp[...] = dot_nt(gleft[g], two_values[...])
        for k in range(2):
            h = 2 * pair_of + k
            lanes = own_lanes(h)
            at_h = jnp.where(iota((1, WIDE), 1) == h, 1.0, 0.0)
            for b in range(ROWS // BLK):
                rows = slice(b * BLK, (b + 1) * BLK)
                level = jnp.sum(lse[rows, :] * at_h, 1, keepdims=True)
                delta = jnp.sum(dmix[rows, :] * lanes, 1, keepdims=True)
                at_k = k * ROWS
                tiles = score_tiles(s[rows, at_k : at_k + ROWS], rows, region)
                for i, t in enumerate(tiles):
                    p = jnp.exp2(t - level)
                    put_split(weights.at[k], rows, i, p)
                    low = at_k + i * WIDE
                    p = p * (dp[rows, low : low + WIDE] - delta)
                    put_split(slopes.at[k], rows, i, p)
        total = 0.0
        for k in range(2):
            total = total + fold(dot(slopes[k], keys[...])) * own_lanes(2 * pair_of + k)
        dq[...] += total
        for k in range(2):
            here = pl.ds(pl.multiple_of((2 * pair_of + k) * HDIM, HDIM), HDIM)
            for i, (t, m) in enumerate(((q_t, slopes), (do_t, weights))):
                lhs = jnp.concatenate([t[0, here, :], t[1, here, :]], 0)
                dkv_t[i, here, :] = fold_rows(fold(dot(lhs, m[k])))
        return carry

    lax.fori_loop(0, HEADS // 2, per_pair, 0)
    d_q = dq[...] * HDIM**-0.5
    d_k = dkv_t[0].T * (1.0 / LOG2E)
    d_v = dkv_t[1].T
    x_t = rows_t(normed)
    d_normed = None
    for i, d in enumerate((d_q, d_k, d_v)):
        grads[pl.ds(at + R_QKV + i, EMB, stride=3), :] = mm_tn(x_t, d)[:EMB]
        grads[at + R_QKVB + i : at + R_QKVB + i + 1, :] = colsum(d)
        part = mm_nt(d, deep(layer[pl.ds(R_QKV + i, EMB, stride=3), :]))
        d_normed = part if d_normed is None else d_normed + part
    return d_normed


def mlp(middle, layer, hpre):
    normed = norm(middle, layer[2:3, :], layer[3:4, :])
    w = deep(hidden_rows(layer, R_HID, EMB))
    pre = mm(normed, w) + hidden_rows(layer, R_HIDB, 1)
    hpre[...] = pre
    out = mm(gelu(pre), layer[R_OUT : R_OUT + HID, :])
    return middle + out + layer[R_OUTB : R_OUTB + 1, :]


def mlp_back(grad, middle, hpre, layer, grads, at):
    hat, inv = norm_stats(middle)
    normed = hat * layer[2:3, :] + layer[3:4, :]
    act, slope = gelu_both(hpre[...])
    grads[at + R_OUTB : at + R_OUTB + 1, :] = colsum(grad)
    grads[at + R_OUT : at + R_OUT + HID, :] = mm_tn(rows_t(grad), act).T
    d_pre = mm_nt(grad, layer[R_OUT : R_OUT + HID, :]) * slope
    put_hidden_rows(grads, at + R_HIDB, 1, colsum(d_pre))
    put_hidden_rows(grads, at + R_HID, EMB, mm_tn(rows_t(normed), d_pre)[:EMB])
    d_normed = mm_nt(d_pre, deep(hidden_rows(layer, R_HID, EMB)))
    grads[at + 2 : at + 3, :] = colsum(d_normed * hat)
    grads[at + 3 : at + 4, :] = colsum(d_normed)
    return grad + norm_back(hat, inv, layer[2:3, :], d_normed)


def pre_norm_back(grad, tokens, layer, grads, at):
    hat, inv = norm_stats(tokens)
    grads[at : at + 1, :] = colsum(grad * hat)
    grads[at + 1 : at + 2, :] = colsum(grad)
    return norm_back(hat, inv, layer[0:1, :], grad)


def region_of(rows, sizes):
    d = lax.shift_right_logical(rows * 1338, 16)
    line = lax.shift_right_logical(rows * 9363, 16)
    places = (d, line - d * WIN, rows - line * WIN)
    starts = (lax.axis_index("slab") * WIN, lax.axis_index("mp") * WIN, 0)
    total = None
    for place, start, blocks in zip(places, starts, sizes + (1,)):
        turned = jnp.where(place < SHIFT, place + FAR, place - SHIFT) + start
        length = WIN * blocks
        part = jnp.where(turned < length - WIN, 0, jnp.where(turned < length - SHIFT, 1, 2))
        total = part if total is None else total * 3 + part
    return total


def put_region(region, sizes):
    rows = region_of(iota((ROWS, WIDE), 0), sizes)[:, 0:1]
    lanes = region_of(iota((8, ROWS), 1), sizes)[0:1, :]
    apart = jnp.where(rows == lanes, 0.0, -100.0 * LOG2E)
    region[...] = jnp.where(iota((ROWS, ROWS), 1) < VOX, apart, -1e30)


def send_parts(ref, a, b, c):
    far = FAR * WIN
    near = SHIFT * WIN
    for d in range(SHIFT):
        base = d * PLANE
        c[d * near : (d + 1) * near, :] = ref[base : base + near, :]
        a[d * far : (d + 1) * far, :] = ref[base + near : base + PLANE, :]
    for d in range(FAR):
        base = (d + SHIFT) * PLANE
        b[d * near : (d + 1) * near, :] = ref[base : base + near, :]


def take_parts(own, a, b, c, out):
    far = FAR * WIN
    near = SHIFT * WIN
    for d in range(WIN):
        base = d * PLANE
        if d < SHIFT:
            out[base : base + near, :] = c[d * near : (d + 1) * near, :]
            out[base + near : base + PLANE, :] = a[d * far : (d + 1) * far, :]
        else:
            e = d - SHIFT
            out[base : base + near, :] = b[e * near : (e + 1) * near, :]
            out[base + near : base + PLANE, :] = own[base + near : base + PLANE, :]
    out[VOX:, :] = jnp.zeros((ROWS - VOX, WIDE), F32)


def span_of(groups):
    low, high = groups
    first = 3 * low // 8 * 8
    last = -(-3 * high // 8) * 8
    return first, min(last, NPARAM // WIDE // 8 * 8) - first


def copied(params, groups, flat, sem):
    first, rows = span_of(groups)
    size = rows * WIDE
    return pltpu.make_async_copy(
        params.at[pl.ds(first * WIDE, size)], flat.at[pl.ds(0, size)], sem
    )


def relay(groups, flat, out, square, last=None):
    low, high = groups
    first, rows = span_of(groups)
    square[0:rows, :] = flat[0 : rows * WIDE].reshape(rows, WIDE)
    if last is not None:
        square[rows : rows + 24, :] = jnp.zeros((24, WIDE), F32)
        square[rows : rows + 1, 0 : last.shape[0]] = last[...].reshape(1, last.shape[0])
    skip = 3 * low - first
    n = high - low
    parts = three_to_four([square[pl.ds(skip + c, n, stride=3), :] for c in range(3)])
    for c in range(4):
        out[pl.ds(c, n, stride=4), :] = parts[c]


FIRST_SPANS = ((0, 98), (98, 392))
LAYER_SPANS = ((389, 681), (680, 972))
CONV_SPANS = ((971, 1620), (1620, GROUPS))


def prep_kernel(spans, params, *refs, last=None):
    outs, (flats, square, sems) = refs[: len(spans)], refs[-3:]
    for i, groups in enumerate(spans):
        copied(params, groups, flats[i], sems.at[i]).start()
    for i, groups in enumerate(spans):
        copied(params, groups, flats[i], sems.at[i]).wait()
        relay(groups, flats[i], outs[i], square, last if i == len(spans) - 1 else None)


def head_picks():
    width = HEAD_ROWS * WIDE
    place = iota((WIDE, width), 1) - HEAD_LANE
    row = iota((WIDE, width), 0)
    here = (place >= row * CLASSES) & (place < (row + 1) * CLASSES) & (row <= EMB)
    place = iota((width, WIDE), 0) - HEAD_LANE
    col = iota((width, WIDE), 1)
    row = lax.shift_right_logical(place * 4682, 16)
    there = (place - row * CLASSES == col) & (place >= 0)
    return jnp.where(here, 1.0, 0.0), jnp.where(there, 1.0, 0.0).astype(BF16)


def prep_conv0_kernel(params, conv0, weights0, bias, *scratch):
    prep_kernel(CONV_SPANS[:1], params, conv0, *scratch)
    tap_weights(conv0, 3, weights0)
    bias[0:1, :] = conv0[3 + TAP_ROWS : 4 + TAP_ROWS, :]
    bias[1:8, :] = jnp.zeros((7, WIDE), F32)


def prep_conv1_kernel(last, bias, params, conv1, head, weights1, vectors, *scratch):
    prep_kernel(CONV_SPANS[1:], params, conv1, *scratch, last=last)
    tap_weights(conv1, 0, weights1)
    vectors[0:1, :] = bias[0:1, :]
    vectors[1:4, :] = conv1[TAP_ROWS : TAP_ROWS + 3, :]
    vectors[4:8, :] = jnp.zeros((4, WIDE), F32)
    square = scratch[1]
    first, _ = span_of(CONV_SPANS[1])
    row = jnp.concatenate(
        [square[HEAD_ROW + i - first : HEAD_ROW + i - first + 1, :] for i in range(HEAD_ROWS)], 1
    )
    here, there = head_picks()
    hi, lo = split(here * row)
    head[...] = dot(hi, there) + dot(lo, there)


def head_rows(d_head, out, at):
    here, there = head_picks()
    hi, lo = split(d_head)
    spread = (dot_nt(hi, there) + dot_nt(lo, there)) * here
    row = colsum(spread)
    for i in range(HEAD_ROWS):
        out[at + i : at + i + 1, :] += row[:, i * WIDE : (i + 1) * WIDE]


class Rows:
    def __init__(self, ref, at):
        self.ref, self.at = ref, at

    def __getitem__(self, key):
        rows, lanes = key
        if isinstance(rows, slice):
            rows = slice(rows.start + self.at, rows.stop + self.at)
        else:
            rows = pl.ds(rows.start + self.at, rows.size, stride=rows.stride)
        return self.ref[rows, lanes]


def merged_norm(x):
    mean = jnp.sum(x, 1, keepdims=True) * (1.0 / MERGE)
    centred = x - mean
    var = jnp.sum(centred * centred, 1, keepdims=True) * (1.0 / MERGE)
    return centred * lax.rsqrt(var + eps_norm)


def first_kernel(
    feats, merge, lay0,
    dense, tok0, save, lse, mixed, middle, hpre, tok1, ahead, pa, pb, pc,
    *sc,
):
    dense[VOX:, :] = jnp.zeros((ROWS - VOX, MERGE), F32)
    for line in range(PLANE):
        dense[line * WIN : (line + 1) * WIN, :] = feats[line]
    hat = merged_norm(dense[...])
    normed = hat * hidden_rows(merge, 0, 1) + hidden_rows(merge, 4, 1)
    tokens = mm(normed, merge[8 : 8 + MERGE, :])
    tok0[...] = tokens
    layer = Rows(lay0, 0)
    normed = norm(tokens, layer[0:1, :], layer[1:2, :])
    attended = attention(normed, layer, save, lse, mixed, sc)
    mid = tokens + attended
    middle[...] = mid
    tokens = mlp(mid, layer, hpre)
    tok1[...] = tokens
    ahead[...] = norm(tokens, layer[1165:1166, :], layer[1166:1167, :])
    send_parts(ahead, pa, pb, pc)


def shifted_kernel(
    sizes,
    own, pa, pb, pc, lay1, _,
    window, save, lse, mixed, out, qa, qb, qc,
    region, *sc,
):
    put_region(region, sizes)
    take_parts(own, pa, pb, pc, window)
    out[...] = attention(
        window[...], Rows(lay1, 1), save, lse, mixed, sc, region
    )
    send_parts(out, qa, qb, qc)


def to_lines(ref, out):
    for line in range(PLANE):
        out[line, 0:WIN, :] = ref[line * WIN : (line + 1) * WIN, :]
        out[line, WIN:8, :] = jnp.zeros((8 - WIN, WIDE), F32)


def from_lines(ref, out):
    out[VOX:, :] = jnp.zeros((ROWS - VOX, WIDE), F32)
    for line in range(PLANE):
        out[line * WIN : (line + 1) * WIN, :] = ref[line, 0:WIN, :]


def send_sides(lines, near_d, far_d, near_h, far_h):
    odd_d = jnp.bitwise_and(lax.axis_index("slab"), 1) == 1
    odd_h = jnp.bitwise_and(lax.axis_index("mp"), 1) == 1
    low, high = lines[0 : 2 * WIN], lines[(WIN - 2) * WIN : PLANE]
    near_d[...] = jnp.where(odd_d, low, high)
    far_d[...] = jnp.where(odd_d, high, low)
    for d in range(WIN):
        low = lines[d * WIN : d * WIN + 2]
        high = lines[d * WIN + WIN - 2 : (d + 1) * WIN]
        near_h[2 * d : 2 * d + 2] = jnp.where(odd_h, low, high)
        far_h[2 * d : 2 * d + 2] = jnp.where(odd_h, high, low)


def second_kernel(
    tok1, own, qa, qb, qc, lay1, lay2, _,
    mid1, hpre1, tok2, save, lse, mixed, mid2, hpre2, lines,
    s0, s1, s2, s3,
    attended, *sc,
):
    take_parts(own, qa, qb, qc, attended)
    mid = tok1[...] + attended[...]
    mid1[...] = mid
    tokens = mlp(mid, Rows(lay1, 1), hpre1)
    tok2[...] = tokens
    layer = Rows(lay2, 2)
    normed = norm(tokens, layer[0:1, :], layer[1:2, :])
    mid = tokens + attention(normed, layer, save, lse, mixed, sc)
    mid2[...] = mid
    attended[...] = mlp(mid, layer, hpre2)
    to_lines(attended, lines)
    send_sides(lines, s0, s1, s2, s3)


def grown_lines(sizes, own, near_d, far_d, near_h, far_h, out):
    slab, row = lax.axis_index("slab"), lax.axis_index("mp")
    odd_d = jnp.bitwise_and(slab, 1) == 1
    odd_h = jnp.bitwise_and(row, 1) == 1
    out[:, 11:12] = jnp.zeros((11, 1, 8, WIDE), F32)
    for d in range(WIN):
        out[d + 2, 2 : 2 + WIN] = own[d * WIN : (d + 1) * WIN]
    for d in range(2):
        near = near_d[d * WIN : (d + 1) * WIN]
        far = far_d[d * WIN : (d + 1) * WIN]
        out[d, 2 : 2 + WIN] = jnp.where(odd_d, near, jnp.where(slab == 0, 0.0, far))
        out[d + 9, 2 : 2 + WIN] = jnp.where(
            odd_d, jnp.where(slab == sizes[0] - 1, 0.0, far), near
        )
    for d in range(11):
        near = near_h[2 * d : 2 * d + 2]
        far = far_h[2 * d : 2 * d + 2]
        out[d, 0:2] = jnp.where(odd_h, near, jnp.where(row == 0, 0.0, far))
        out[d, 9:11] = jnp.where(odd_h, jnp.where(row == sizes[1] - 1, 0.0, far), near)


def put_marks(labels, valid, out):
    across = iota((8, WIN), 1) == iota((8, WIN), 0)
    classes = iota((8, WIDE), 1) - EMB
    for d in range(WIN):
        code = jnp.where(valid[d] == 1, labels[d], -1 - EMB - WIDE)
        code = code.astype(F32)
        for h in range(WIN):
            line = jnp.where(across, code[h : h + 1, :], 0.0)
            column = jnp.sum(line, 1, keepdims=True)
            mark = jnp.where(column == classes.astype(F32), 1.0, 0.0)
            out[d * WIN + h] = jnp.where(iota((8, WIDE), 0) < WIN, mark, 0.0)


def taps(source, first_plane, planes, first_line, lines, out):
    def per_plane(d, carry):
        for c in range(3):
            for b in range(3):
                x = source[d + first_plane, first_line + b : first_line + b + lines]
                if c != 1:
                    x = roll(x, 1 if c == 0 else 7, 1)
                x = pair(x.reshape(lines * 8, WIDE))
                at = pl.multiple_of(d * (lines * 8), lines * 8)
                t = b * 3 + c
                out[pl.ds(at, lines * 8), t * 256 : (t + 1) * 256] = x
        return carry

    lax.fori_loop(0, planes, per_plane, 0)


def tap_weights(ref, at, out):
    def per_tap(i, carry):
        w = deep(ref[pl.ds(i * EMB + at, EMB), :])
        out[pl.ds(pl.multiple_of(i * 256, 256), 256), :] = weight_nn(w)
        return carry

    lax.fori_loop(0, 27, per_tap, 0)


def tap_weights_back(ref, at, out):
    for i in range(27):
        w = deep(ref[(26 - i) * EMB + at : (27 - i) * EMB + at, :])
        out[:, i * 256 : (i + 1) * 256] = weight_nt(w)


def conv(side, weights, planes, pitch, at_once, put, back=False):
    rows = at_once * pitch
    for start in range(0, planes, at_once):
        total = None
        for a in range(3):
            low = (start + a) * pitch
            x = side[low : low + rows, :]
            if back:
                part = dot_nt(x, weights[:, a * 2304 : (a + 1) * 2304])
            else:
                part = dot(x, weights[a * 2304 : (a + 1) * 2304, :])
            total = part if total is None else total + part
        put(start, fold(total))


def conv_weight_grad(side, grad_rows, pitch, out, at):
    rows = 512
    g = jnp.concatenate([grad_rows, jnp.zeros((rows - grad_rows.shape[0], WIDE), F32)], 0)
    left = jnp.concatenate(split(g.T[:EMB]), 0)
    for a in range(3):
        for bc in range(9):
            y = dot(left, side[a * pitch : a * pitch + rows, bc * 256 : (bc + 1) * 256])
            y = deep(fold_rows(fold(y))).T
            t = a * 9 + bc
            out[at + t * EMB : at + (t + 1) * EMB, :] = y[:EMB]


def volume_mask(sizes, planes, lines, reach, real_lines):
    slab, row = lax.axis_index("slab"), lax.axis_index("mp")
    ends = (slab == 0, slab == sizes[0] - 1, row == 0, row == sizes[1] - 1)
    shape = (planes, lines, 8, WIDE)
    d, h, w = iota(shape, 0), iota(shape, 1), iota(shape, 2)
    low_d = jnp.where(ends[0], reach, 0)
    high_d = jnp.where(ends[1], planes - reach, planes)
    low_h = jnp.where(ends[2], reach, 0)
    high_h = jnp.where(ends[3], real_lines - reach, real_lines)
    inside = (d >= low_d) & (d < high_d) & (h >= low_h) & (h < high_h) & (w < WIN)
    return jnp.where(inside, 1.0, 0.0)


def conv_kernel(
    sizes,
    own, s0, s1, s2, s3, labels, valid, weights0, weights1, vectors,
    grown, pre, tok, stats, t0, t1, t2, t3,
    act, side, side_own, marks,
):
    grown_lines(sizes, own, s0, s1, s2, s3, grown)
    put_marks(labels, valid, marks)
    taps(grown, 0, 11, 0, 10, side)
    bias0 = vectors[0:1, :]
    inside = volume_mask(sizes, 9, 10, 1, 9)


    def put(start, y):
        z = (y + bias0).reshape(3, 10, 8, WIDE)
        pre[start : start + 3] = z
        act[start : start + 3] = gelu(z) * inside[start : start + 3]

    conv(side, weights0, 9, 80, 3, put)
    taps(act, 0, 9, 0, 8, side_own)
    bias1 = vectors[1:2, :]
    sums = []

    def put_own(start, y):
        y = (y + bias1).reshape(WIN, 8, 8, WIDE)[:, 0:WIN]
        y = y + own[...].reshape(WIN, WIN, 8, WIDE)
        y = jnp.where(iota(y.shape, 2) < WIN, y, 0.0).reshape(PLANE, 8, WIDE)
        tok[...] = y + marks[...]
        send_sides(tok, t0, t1, t2, t3)
        flat = y.reshape(PLANE * 8, WIDE)
        sums.append(colsum(flat))
        sums.append(colsum(flat * flat))

    conv(side_own, weights1, WIN, 64, WIN, put_own)
    count = jnp.sum(marks[...].reshape(PLANE * 8, WIDE))
    row = iota((8, WIDE), 0)
    stats[...] = (
        jnp.where(row == 0, sums[0], 0.0)
        + jnp.where(row == 1, sums[1], 0.0)
        + jnp.where(row == 2, count, 0.0)
    )


def head_kernel(
    sizes, voxels,
    own, s0, s1, s2, s3, sums, vectors, head_w,
    grown, slope_out, stats, d_head, d_rows,
):
    grown_lines(sizes, own, s0, s1, s2, s3, grown)
    rows = 11 * 12 * 8
    both = grown[...].reshape(rows, WIDE)
    lane = iota((rows, WIDE), 1)
    tokens = jnp.where(lane < EMB, both, 0.0)
    target = jnp.where(lane < CLASSES, roll(both, WIDE - EMB, 1), 0.0)
    live = jnp.sum(target, 1, keepdims=True)
    count = F32(voxels)
    average = sums[0:1, :] / count
    spread = sums[1:2, :] / count - average * average
    inv = lax.rsqrt(spread + eps_norm)
    gain = vectors[2:3, :]
    bias = vectors[3:4, :]
    hat = (tokens - average) * inv
    act, slope = gelu_both(hat * gain + bias)
    act = jnp.where(lane == EMB, 1.0, act)
    w = head_w[...]
    logits = mm(act, w)
    logits = jnp.where(lane < CLASSES, logits, -1e30)
    top = jnp.max(logits, 1, keepdims=True)
    e = jnp.exp(logits - top)
    total = jnp.sum(e, 1, keepdims=True)
    logp = logits - top - jnp.log(total)
    scale = 1.0 / sums[2:3, 0:1]
    d_logits = (e / total * live - target) * scale
    d_normed = jnp.where(lane < EMB, mm_nt(d_logits, w) * slope, 0.0)
    d_tokens = d_normed * gain * inv
    slope_out[...] = d_tokens.reshape(11, 12, 8, WIDE)

    def own_rows(x):
        x = x.reshape(11, 12, 8, WIDE)[2:9, 2:9]
        x = jnp.where(iota(x.shape, 2) < WIN, x, 0.0)
        return x.reshape(PLANE * 8, WIDE)

    loss = -jnp.sum(own_rows(target * jnp.where(lane < CLASSES, logp, 0.0)))
    own_d = own_rows(d_logits)
    own_n = own_rows(d_normed)
    own_hat = own_rows(hat)
    zeros = jnp.zeros((512 - PLANE * 8, WIDE), F32)
    left = rows_t(jnp.concatenate([own_d, zeros], 0))
    d_head[...] = mm_tn(left, jnp.concatenate([own_rows(act), zeros], 0)).T
    d_gain = colsum(own_n * own_hat)
    d_bias = colsum(own_n)
    d_average = -d_bias * gain * inv
    d_spread = d_gain * gain * inv * inv * -0.5
    d_two = d_spread / count
    d_one = (d_average - 2.0 * average * d_spread) / count
    row = iota((8, WIDE), 0)
    live_lane = iota((8, WIDE), 1) < EMB
    stats[...] = (
        jnp.where((row == 0) & live_lane, d_one, 0.0)
        + jnp.where((row == 1) & live_lane, d_two, 0.0)
        + jnp.where(row == 2, loss, 0.0)
    )
    d_rows[...] = (
        jnp.where(row == 0, d_gain, 0.0)
        + jnp.where(row == 1, d_bias, 0.0)
    )


def sides_back_kernel(sizes, grown, pre, side_act, side_grown, act):
    act[0:9] = gelu(pre[...]) * volume_mask(sizes, 9, 10, 1, 9)
    act[9:10] = jnp.zeros((1, 10, 8, WIDE), F32)
    taps(act, 0, 10, 0, 8, side_act)
    taps(grown, 1, 10, 1, 8, side_grown)


def weights_back_kernel(conv0, conv1, weights0, weights1):
    tap_weights_back(conv0, 3, weights0)
    tap_weights_back(conv1, 0, weights1)


def conv_back_kernel(
    sizes,
    tok, slope, sums, pre, side_act, side_grown, weights0, weights1, d_rows, d_head,
    d_own, keep, send, carry, seam,
    grads, dgrown, act, side, side_own, flat,
):
    lane = iota((11, 12, 8, WIDE), 3)
    inside = volume_mask(sizes, 11, 12, 2, 11)
    steady = sums[0:1, :].reshape(1, 1, 1, WIDE)
    rising = 2.0 * sums[1:2, :].reshape(1, 1, 1, WIDE)
    d_tok = slope[...] + jnp.where(lane < EMB, (steady + tok[...] * rising) * inside, 0.0)
    dgrown[...] = d_tok
    grads[5191:, :] = jnp.zeros((45, WIDE), F32)
    grads[0:8, :] = jnp.zeros((8, WIDE), F32)
    grads[5189:5191, :] = d_rows[0:2, :]
    own = dgrown[2:9, 2:10]
    line = iota(own.shape, 1)
    own = jnp.where(line < WIN, own, 0.0).reshape(WIN * 64, WIDE)
    grads[5188:5189, :] = colsum(own)

    near = volume_mask(sizes, 9, 10, 1, 9)
    conv_weight_grad(side_act, own, 64, grads, 2596)
    taps(dgrown, 0, 11, 0, 10, side)


    def put(start, y):
        _, s = gelu_both(pre[start : start + 3])
        act[start : start + 3] = y.reshape(3, 10, 8, WIDE) * s * near[start : start + 3]

    conv(side, weights1, 9, 80, 3, put, back=True)

    own = act[1:8, 1:9]
    line = iota(own.shape, 1)
    own = jnp.where(line < WIN, own, 0.0).reshape(WIN * 64, WIDE)
    grads[2595:2596, :] = colsum(own)
    conv_weight_grad(side_grown, own, 64, grads, 3)
    carry[...] = grads[0:24, :]
    flat[3 * (GROUPS - CUTS[3]) :, :] = jnp.zeros((flat.shape[0] - 3912, WIDE), F32)
    flatten(grads, 20, GROUPS - CUTS[3], flat)
    start = 3 * CUTS[3]
    head_rows(d_head[...], flat, HEAD_ROW - start)
    seam[...] = flat[0 : LATE_ROWS - start, :]
    scatter(sizes, flat, LATE_ROWS - start, keep, send)
    taps(act, 0, 9, 0, 8, side_own)

    def put_own(start, y):
        y = y.reshape(WIN, 8, 8, WIDE)[:, 0:WIN] + dgrown[2:9, 2:9]
        y = jnp.where(iota(y.shape, 2) < WIN, y, 0.0)
        d_own[...] = y.reshape(PLANE, 8, WIDE)

    conv(side_own, weights0, WIN, 64, WIN, put_own, back=True)


def back_mlp_kernel(d_own, lay2, mid2, hpre2, d_mid, grads, dense):
    from_lines(d_own, dense)
    grads[...] = jnp.zeros_like(grads)
    d_mid[...] = mlp_back(dense[...], mid2[...], hpre2, Rows(lay2, 2), grads, 2)


def back_two_kernel(
    d_mid2, grads2, carry, lay1, lay2, tok2, save, lse, mixed, mid1, hpre1,
    d_mid, grads1, flat, carry2, pa, pb, pc,
    grads, *sc,
):
    layer = Rows(lay2, 2)
    grads[0:1168, :] = grads2[...]
    d = d_mid2[...]
    tokens = tok2[...]
    normed = norm(tokens, layer[0:1, :], layer[1:2, :])
    d_normed = attention_back(d, normed, layer, save, lse, mixed, sc, grads, 2)
    d = d + pre_norm_back(d_normed, tokens, layer, grads, 2)
    grads[1167:1184, :] = carry[3:20, :]
    flatten(grads, 32, CUTS[3] - CUTS[2], flat)
    carry2[...] = grads[0:32, :]
    layer = Rows(lay1, 1)
    d = mlp_back(d, mid1[...], hpre1, layer, grads1, 1)
    d_mid[...] = d
    send_parts(d_mid, pa, pb, pc)


def back_shifted_kernel(
    sizes,
    own, pa, pb, pc, lay1, window, save, lse, mixed, grads1, carry2, _,
    d_window, flat, carry1,
    region, grads, grad, *sc,
):
    put_region(region, sizes)
    take_parts(own, pa, pb, pc, grad)
    grads[0:1168, :] = grads1[...]
    grads[0:3, :] = jnp.zeros((3, WIDE), F32)
    d_window[...] = attention_back(
        grad[...], window[...], Rows(lay1, 1), save, lse, mixed, sc, grads, 1,
        region,
    )
    grads[1166:1196, :] = carry2[2:32, :]
    flatten(grads, 12, CUTS[2] - CUTS[1], flat)
    carry1[...] = grads[0:16, :]


def parts_kernel(whole, *refs):
    send_parts(whole, *refs[-3:])


def back_first_kernel(
    sizes,
    d_mid, own, qa, qb, qc, tok1, lay0, lay1, merge, dense, tok0, save, lse, mixed, middle, hpre,
    carry1, flat1, flat2, seam, keep, send, flat, grads, grad, *sc,
):
    take_parts(own, qa, qb, qc, grad)
    grads[1556:1572, :] = carry1[...]
    d = d_mid[...] + pre_norm_back(grad[...], tok1[...], Rows(lay1, 1), grads, 1557)
    layer = Rows(lay0, 0)
    at = MERGE_ROWS
    d = mlp_back(d, middle[...], hpre, layer, grads, at)
    tokens = tok0[...]
    normed = norm(tokens, layer[0:1, :], layer[1:2, :])
    d_normed = attention_back(d, normed, layer, save, lse, mixed, sc, grads, at)
    d = d + pre_norm_back(d_normed, tokens, layer, grads, at)
    live = iota((ROWS, WIDE), 0) < VOX
    d = jnp.where(live, d, 0.0)
    hat = merged_norm(dense[...])
    gain = hidden_rows(merge, 0, 1)
    bias = hidden_rows(merge, 4, 1)
    w = merge[8 : 8 + MERGE, :]
    put_hidden_rows(grads, 8 - 8, 1, jnp.zeros((1, MERGE), F32))
    grads[8 : 8 + MERGE, :] = mm_tn(rows_t(d), hat * gain + bias).T
    d_hat = mm_nt(d, w)
    put_hidden_rows(grads, 0, 1, colsum(d_hat * hat))
    put_hidden_rows(grads, 4, 1, colsum(d_hat))
    flatten(grads, 0, CUTS[1], flat)
    at = 0
    for cut, part in ((CUTS[1], flat1), (CUTS[2], flat2), (CUTS[3], seam)):
        at = 3 * cut
        flat[at : at + part.shape[0], :] = part[...]
    at += seam.shape[0]
    if flat.shape[0] > at:
        flat[at:, :] = jnp.zeros((flat.shape[0] - at, WIDE), F32)
    scatter(sizes, flat, 0, keep, send)


def radices(count):
    steps = [2]
    left = count // 2
    while left > 1:
        steps.append(4 if left >= 4 else 2)
        left //= steps[-1]
    return steps


def block_rows(rows, count):
    return -(-rows // (8 * count)) * 8


def own_number(sizes):
    return lax.axis_index("slab") * sizes[1] + lax.axis_index("mp")


def place_in_half(distance, count):
    place = 0
    shift = 1
    for radix in radices(count)[1:]:
        digit = jnp.bitwise_and(lax.shift_right_logical(distance, shift), radix - 1)
        place = place * radix + digit
        shift += radix.bit_length() - 1
    return place


def scatter(sizes, source, first, keep, send):
    count = sizes[0] * sizes[1]
    rows = keep.shape[0] * 2 // count
    me = own_number(sizes)
    odd = jnp.bitwise_and(me, 1)

    def per_pair(t, carry):
        for block, out in ((2 * t + odd, keep), (2 * t + 1 - odd, send)):
            place = place_in_half(jnp.bitwise_xor(block, me), count)
            at = pl.multiple_of(first + block * rows, 8)
            to = pl.multiple_of(place * rows, 8)
            out[pl.ds(to, rows), :] = source[pl.ds(at, rows), :]
        return carry

    lax.fori_loop(0, count // 2, per_pair, 0)


def traded(value, distance, count):
    pairs = [(i, i ^ distance) for i in range(count)]
    return lax.ppermute(value, ("slab", "mp"), pairs)


def add_kernel(count, outs, *refs):
    total = refs[0][...]
    for ref in refs[1:count]:
        total = total + ref[...]
    rows = total.shape[0] // outs
    for i, out in enumerate(refs[len(refs) - outs :]):
        out[...] = total[i * rows : (i + 1) * rows]


def added(got, parts, after):
    rows = got[0].shape[0] // parts
    return call(
        functools.partial(add_kernel, len(got), parts), [arr(rows, WIDE)] * parts, [], *got,
        name="add", us=0.3, far=after,
    )


def join_kernel(count, *refs):
    rows = refs[0].shape[0]
    for i, ref in enumerate(refs[:count]):
        refs[-1][i * rows : (i + 1) * rows, :] = ref[...]


def joined(got, after):
    (out,) = call(
        functools.partial(join_kernel, len(got)), [arr(len(got) * got[0].shape[0], WIDE)], [], *got,
        name="join", us=0.3, far=after,
    )
    return out


def summing(keep, send, count):
    steps = radices(count)
    got = [keep, traded(send, 1, count)]
    shift = 1
    after = yield got
    for radix in steps[1:]:
        parts = added(got, radix, after)
        got = [parts[0]] + [traded(parts[k], k << shift, count) for k in range(1, radix)]
        shift += radix.bit_length() - 1
        after = yield got
    (own,) = added(got, 1, after)
    for radix in reversed(steps[1:]):
        shift -= radix.bit_length() - 1
        got = [own] + [traded(own, k << shift, count) for k in range(1, radix)]
        after = yield got
        own = joined(got, after)
    yield own, traded(own, 1, count)


def exchanged_sum(value, count):
    shift = 0
    for radix in radices(count):
        got = [value] + [traded(value, k << shift, count) for k in range(1, radix)]
        while len(got) > 1:
            got = [got[i] + got[i + 1] for i in range(0, len(got), 2)]
        value = got[0]
        shift += radix.bit_length() - 1
    return value


PIECE = 262144


def adamw_kernel(
    sizes,
    late, late_other, early, early_other, tail, sums, params, first, second,
    new_params, new_first, new_second, loss, valid, norm_out,
    grad, scale_ref,
):
    count = sizes[0] * sizes[1]
    step = pl.program_id(0)

    @pl.when(step == 0)
    def gather():
        me = own_number(sizes)
        total = jnp.zeros((8, WIDE), F32)
        for ref in (late, late_other, early, early_other):
            x = ref[...]
            total = total + jnp.sum((x * x).reshape(-1, 8, WIDE), 0)
        norm = jnp.sqrt(jnp.sum(total))
        loss[0] = jnp.sum(tail[2:3, 0:1])
        valid[0] = jnp.sum(sums[2:3, 0:1])
        norm_out[0] = norm
        scale_ref[0] = jnp.minimum(1.0, clip_norm / (norm + 1e-06))
        start = 0
        for own, other, size in ((late, late_other, LATE_ROWS), (early, early_other, EARLY_ROWS)):
            rows = own.shape[0] * 2 // count

            def per_block(block, carry, own=own, other=other, rows=rows, start=start):
                distance = jnp.bitwise_xor(block, me)
                at = pl.ds(pl.multiple_of(place_in_half(distance, count) * rows, 8), rows)
                near = jnp.bitwise_and(distance, 1) == 0
                to = pl.ds(pl.multiple_of(start + block * rows, 8), rows)
                grad[to, :] = jnp.where(near, own[at, :], other[at, :])
                return carry

            lax.fori_loop(0, size // rows, per_block, 0)
            start += size

    def update(base, low, size):
        rows = -(-size // 1024) * 8
        at = pl.ds(pl.multiple_of(base // WIDE + low // WIDE, 8), rows)
        g = grad[at, :].reshape(rows * WIDE)[:size] * scale_ref[0]
        here = pl.ds(pl.multiple_of(base + low, 1024), size)
        one = beta_one * first[here] + (1.0 - beta_one) * g
        two = beta_two * second[here] + (1.0 - beta_two) * g * g
        there = pl.ds(low, size)
        new_first[there] = one
        new_second[there] = two
        two = two * (1.0 / (1.0 - beta_two**STEP))
        low_by = two * lax.rsqrt(jnp.maximum(two, 1e-37)) + adam_eps
        inverse = pl.reciprocal(low_by, approx=True)
        inverse = inverse * (2.0 - low_by * inverse)
        new_params[there] = params[here] * (1.0 - learn_rate * decay_rate) - (
            one * (learn_rate / (1.0 - beta_one**STEP))
        ) * inverse

    whole = NPARAM // PIECE

    @pl.when(step < whole)
    def full():
        def part(i, carry):
            low = pl.multiple_of(i * 16384, 16384)
            update(step * PIECE, low, 16384)
            return carry

        lax.fori_loop(0, PIECE // 16384, part, 0)

    @pl.when(step == whole)
    def last():
        rest = NPARAM - whole * PIECE
        main = rest // 1024 * 1024
        for low in range(0, main, 16384):
            update(whole * PIECE, low, min(16384, main - low))
        update(whole * PIECE, main, rest - main)


def adamw(sizes, parts, arrays):
    pieces = -(-NPARAM // PIECE)
    piece = pl.BlockSpec((PIECE,), lambda i: (i,))
    vmem = pl.BlockSpec(memory_space=pltpu.VMEM)
    smem = pl.BlockSpec(memory_space=pltpu.SMEM)
    return pl.pallas_call(
        functools.partial(adamw_kernel, sizes),
        grid=(pieces,),
        out_shape=[arr(NPARAM)] * 3 + [arr(1)] * 3,
        in_specs=[vmem] * (len(parts) + len(arrays)),
        out_specs=[piece] * 3 + [smem] * 3,
        scratch_shapes=[pltpu.VMEM((LATE_ROWS + EARLY_ROWS, WIDE), F32), pltpu.SMEM((1,), F32)],
        compiler_params=pltpu.CompilerParams(vmem_limit_bytes=16 * 1024 * 1024),
        cost_estimate=pl.CostEstimate(flops=6 * 10**9, bytes_accessed=0, transcendentals=0),
        name="adamw",
    )(*parts, *arrays)


def arr(*shape):
    return jax.ShapeDtypeStruct(shape, F32)


def call(kernel, outs, scratch, *args, name=None, us=1.0, far=(), mib=16):
    vmem = pl.BlockSpec(memory_space=pltpu.VMEM)
    smem = pl.BlockSpec(memory_space=pltpu.SMEM)
    return pl.pallas_call(
        kernel,
        out_shape=list(outs),
        in_specs=[vmem] * len(args) + [pl.BlockSpec(memory_space=pl.ANY)] * len(far),
        out_specs=[smem if o.shape == (1,) else vmem for o in outs],
        scratch_shapes=list(scratch),
        compiler_params=pltpu.CompilerParams(vmem_limit_bytes=mib * 1024 * 1024),
        cost_estimate=pl.CostEstimate(
            flops=int(us * 1.15e9), bytes_accessed=0, transcendentals=0
        ),
        name=name,
    )(*args, *far)


SQUARE = arr(ROWS, WIDE)
SAVE = arr(ROWS, 3 * WIDE)
FORWARD = [
    pltpu.VMEM((2, ROWS, 2 * WIDE), BF16),
    pltpu.VMEM((2, ROWS, 2 * WIDE), BF16),
    pltpu.VMEM((2 * ROWS, 2 * WIDE), BF16),
]
BACKWARD = [
    pltpu.VMEM((2, ROWS, 2 * WIDE), BF16),
    pltpu.VMEM((2, ROWS, 2 * WIDE), BF16),
    pltpu.VMEM((2, ROWS, 2 * WIDE), BF16),
    pltpu.VMEM((2, ROWS, 2 * WIDE), BF16),
    pltpu.VMEM((2 * ROWS, 2 * WIDE), BF16),
    pltpu.VMEM((ROWS, WIDE), F32),
    pltpu.VMEM((2, WIDE, ROWS), F32),
    pltpu.VMEM((2, ROWS, 2 * ROWS), BF16),
    pltpu.VMEM((2, ROWS, 2 * ROWS), BF16),
    pltpu.VMEM((2, WIDE, ROWS), BF16),
    pltpu.VMEM((2, WIDE, ROWS), BF16),
    pltpu.VMEM((ROWS, WIDE), F32),
    pltpu.VMEM((ROWS, 2 * ROWS), F32),
    pltpu.VMEM((ROWS, 2 * ROWS), F32),
    pltpu.VMEM((2 * ROWS, 2 * WIDE), BF16),
    pltpu.VMEM((2 * ROWS, 2 * WIDE), BF16),
]
PARTS = [arr(ROWS_A, WIDE), arr(ROWS_B, WIDE), arr(ROWS_C, WIDE)]


def passed(parts, steps, sizes):
    slabs, rows = sizes
    moved = []
    for part, (ds, dm) in zip(parts, ((1, 0), (0, 1), (1, 1))):
        pairs = []
        for s in range(slabs):
            for m in range(rows):
                target = ((s + steps * ds) % slabs) * rows + (m + steps * dm) % rows
                pairs.append((s * rows + m, target))
        moved.append(lax.ppermute(part, ("slab", "mp"), pairs))
    return moved


SIDES = [arr(2 * WIN, 8, WIDE)] * 4


def paired(axis, size):
    near = [(i, i ^ 1) for i in range(size)]
    far = [(i, (i + (1 if i % 2 else -1)) % size) for i in range(size)]
    if axis == "mp":
        far = [(0, 0), *far[1:-1], (size - 1, size - 1)]
    return (
        lambda value: lax.ppermute(value, axis, near),
        lambda value: lax.ppermute(value, axis, far),
    )


def column_kernel(sizes, near_d, far_d, near_h, far_h, near_out, far_out):
    slab = lax.axis_index("slab")
    odd_d = jnp.bitwise_and(slab, 1) == 1
    odd_h = jnp.bitwise_and(lax.axis_index("mp"), 1) == 1
    at_low = slab == 0
    at_high = slab == sizes[0] - 1
    near_out[4:18] = near_h[...]
    far_out[4:18] = far_h[...]
    for d in range(2):
        near = near_d[d * WIN : (d + 1) * WIN]
        far = far_d[d * WIN : (d + 1) * WIN]
        before = jnp.where(odd_d, near, jnp.where(at_low, 0.0, far))
        after = jnp.where(odd_d, jnp.where(at_high, 0.0, far), near)
        for x, at in ((before, 2 * d), (after, 18 + 2 * d)):
            low, high = x[0:2], x[WIN - 2 : WIN]
            near_out[at : at + 2] = jnp.where(odd_h, low, high)
            far_out[at : at + 2] = jnp.where(odd_h, high, low)


def beside(sides, sizes):
    near, far = paired("slab", sizes[0])
    near_d, far_d = near(sides[0]), far(sides[1])
    near_h, far_h = call(
        functools.partial(column_kernel, sizes), [arr(22, 8, WIDE)] * 2, [],
        near_d, far_d, sides[2], sides[3],
        name="column", us=0.3,
    )
    near, far = paired("mp", sizes[1])
    return near_d, far_d, near(near_h), far(far_h)


REGION = [pltpu.VMEM((ROWS, ROWS), F32)]


def on_device(sizes, feats, labels, valid, params, moment_one, moment_two):
    slabs, rows = sizes
    count = slabs * rows

    def room(spans):
        sizes = [(span_of(groups)[1] + 8) * WIDE for groups in spans]
        return [
            [pltpu.VMEM((size,), F32) for size in sizes],
            pltpu.VMEM((2048, WIDE), F32),
            pltpu.SemaphoreType.DMA((len(spans),)),
        ]

    first_size = FIRST_SPANS[-1][1] * 384
    merge, lay0 = call(
        functools.partial(prep_kernel, FIRST_SPANS),
        [arr(MERGE_ROWS, WIDE), arr(1176, WIDE)],
        room(FIRST_SPANS),
        name="prep_first", us=2.0, far=(params[:first_size],),
    )
    lay1, lay2 = call(
        functools.partial(prep_kernel, LAYER_SPANS),
        [arr(1168, WIDE)] * 2,
        room(LAYER_SPANS),
        name="prep_layers", us=2.0, far=(params,),
    )
    taps_shape = jax.ShapeDtypeStruct((27 * 256, 256), BF16)
    conv0, weights0, bias0 = call(
        prep_conv0_kernel,
        [arr(2596, WIDE), taps_shape, arr(8, WIDE)],
        room(CONV_SPANS[:1]),
        name="prep_conv0", us=1.5, far=(params,),
    )
    conv1, head_w, weights1, vectors = call(
        prep_conv1_kernel,
        [arr(2640, WIDE), arr(WIDE, WIDE), taps_shape, arr(8, WIDE)],
        room(CONV_SPANS[1:]),
        params[NPARAM // WIDE * WIDE :], bias0,
        name="prep_conv1", us=1.5, far=(params,),
    )

    dense, tok0, save0, lse0, mixed0, mid0, hpre0, tok1, ahead, *parts = call(
        first_kernel,
        [arr(ROWS, MERGE), SQUARE, SAVE, SQUARE, SQUARE, SQUARE, arr(ROWS, HID), SQUARE, SQUARE]
        + PARTS,
        FORWARD,
        feats.reshape(PLANE, WIN, MERGE), merge, lay0,
        name="first", us=6.0,
    )
    parts = passed(parts, -1, sizes)
    window, save1, lse1, mixed1, out1, *parts = call(
        functools.partial(shifted_kernel, sizes),
        [SQUARE, SAVE, SQUARE, SQUARE, SQUARE] + PARTS,
        REGION + FORWARD,
        ahead, *parts, lay1,
        name="shifted", us=4.5, far=(weights0,),
    )
    parts = passed(parts, 1, sizes)
    mid1, hpre1, tok2, save2, lse2, mixed2, mid2, hpre2, lines, *sides = call(
        second_kernel,
        [SQUARE, arr(ROWS, HID), SQUARE, SAVE, SQUARE, SQUARE, SQUARE, arr(ROWS, HID)]
        + [arr(PLANE, 8, WIDE)] + SIDES,
        [pltpu.VMEM((ROWS, WIDE), F32)] + FORWARD,
        tok1, out1, *parts, lay1, lay2,
        name="second", us=6.5, far=(weights1,),
    )
    sides = beside(sides, sizes)
    grown, pre, tok3, sums, *tok_sides = call(
        functools.partial(conv_kernel, sizes),
        [arr(11, 12, 8, WIDE), arr(9, 10, 8, WIDE), arr(PLANE, 8, WIDE), arr(8, WIDE)] + SIDES,
        [
            pltpu.VMEM((9, 10, 8, WIDE), F32),
            pltpu.VMEM((880, 2304), BF16),
            pltpu.VMEM((576, 2304), BF16),
            pltpu.VMEM((PLANE, 8, WIDE), F32),
        ],
        lines, *sides, labels, valid, weights0, weights1, vectors,
        name="conv", us=8.0, mib=20,
    )
    tok_sides = beside(tok_sides, sizes)
    side_act, side_grown = call(
        functools.partial(sides_back_kernel, sizes),
        [jax.ShapeDtypeStruct((640, 2304), BF16)] * 2,
        [pltpu.VMEM((10, 10, 8, WIDE), F32)],
        grown, pre,
        name="sides_back", us=2.0,
    )
    weights0, weights1 = call(
        weights_back_kernel,
        [jax.ShapeDtypeStruct((256, 27 * 256), BF16)] * 2,
        [],
        conv0, conv1,
        name="weights_back", us=1.5,
    )
    sums = exchanged_sum(sums, count)
    voxels = WIN * slabs * WIN * rows * WIN
    tok3, slope, tail, d_head, d_rows = call(
        functools.partial(head_kernel, sizes, voxels),
        [arr(11, 12, 8, WIDE), arr(11, 12, 8, WIDE), arr(8, WIDE), arr(WIDE, WIDE), arr(8, WIDE)],
        [],
        tok3, *tok_sides, sums, vectors, head_w,
        name="head", us=3.5,
    )
    tail = exchanged_sum(tail, count)
    late_rows = block_rows(LATE_ROWS, count) * count
    early_rows = block_rows(EARLY_ROWS, count) * count
    seam_rows = LATE_ROWS - 3 * CUTS[3]
    d_own, keep, send, carry3, seam = call(
        functools.partial(conv_back_kernel, sizes),
        [arr(PLANE, 8, WIDE)] + [arr(early_rows // 2, WIDE)] * 2
        + [arr(24, WIDE), arr(seam_rows, WIDE)],
        [
            pltpu.VMEM((5236, WIDE), F32),
            pltpu.VMEM((11, 12, 8, WIDE), F32),
            pltpu.VMEM((10, 10, 8, WIDE), F32),
            pltpu.VMEM((880, 2304), BF16),
            pltpu.VMEM((576, 2304), BF16),
            pltpu.VMEM((seam_rows + early_rows, WIDE), F32),
        ],
        tok3, slope, tail, pre, side_act, side_grown, weights0, weights1, d_rows, d_head,
        name="conv_back", us=14.0, mib=28,
    )
    early = summing(keep, send, count)
    next(early)
    d_mid2, grads2 = call(
        back_mlp_kernel,
        [SQUARE, arr(1168, WIDE)],
        [pltpu.VMEM((ROWS, WIDE), F32)],
        d_own, lay2, mid2, hpre2,
        name="back_mlp", us=1.5,
    )
    early.send((d_mid2,))
    d_mid, grads1, flat2, carry2, *parts = call(
        back_two_kernel,
        [SQUARE, arr(1168, WIDE), arr(3 * (CUTS[3] - CUTS[2]), WIDE), arr(32, WIDE)] + PARTS,
        [pltpu.VMEM((1184, WIDE), F32)] + BACKWARD,
        d_mid2, grads2, carry3, lay1, lay2, tok2, save2, lse2, mixed2, mid1, hpre1,
        name="back_two", us=7.0,
    )
    got = early.send((d_mid,))
    parts = passed(parts, -1, sizes)
    d_window, flat1, carry1 = call(
        functools.partial(back_shifted_kernel, sizes),
        [SQUARE, arr(3 * (CUTS[2] - CUTS[1]), WIDE), arr(16, WIDE)],
        REGION + [pltpu.VMEM((1200, WIDE), F32), pltpu.VMEM((ROWS, WIDE), F32)] + BACKWARD,
        d_mid, *parts, lay1, window, save1, lse1, mixed1, grads1, carry2,
        name="back_shifted", us=6.0, far=(got[0],),
    )
    parts = call(
        parts_kernel, PARTS, [], d_window, name="parts", us=0.2, far=got[1:]
    )
    parts = passed(parts, 1, sizes)
    late = call(
        functools.partial(back_first_kernel, sizes),
        [arr(late_rows // 2, WIDE)] * 2,
        [
            pltpu.VMEM((late_rows, WIDE), F32),
            pltpu.VMEM((1572, WIDE), F32),
            pltpu.VMEM((ROWS, WIDE), F32),
        ]
        + BACKWARD,
        d_mid, d_window, *parts, tok1, lay0, lay1, merge, dense, tok0, save0, lse0, mixed0, mid0,
        hpre0, carry1, flat1, flat2, seam,
        name="back_first", us=8.0,
    )
    more = radices(count)[3:]
    late = summing(*late, count)
    next(late)
    kept = late.send(())
    for _ in more:
        early.send(())
    early.send((kept[0],))
    for _ in more:
        early.send(())
    got = early.send(())
    late.send((got[0],))
    for _ in more:
        late.send(())
    late.send(())
    for _ in more:
        late.send(())
    kept = late.send(tuple(got[1:]))
    early = early.send((kept[0],))
    late = late.send(())
    new_params, new_first, new_second, loss, valid_count, norm = adamw(
        sizes, (*late, *early, tail, sums), (params, moment_one, moment_two)
    )
    return (
        loss.reshape(()), valid_count.reshape(()), norm.reshape(()),
        new_params, new_first, new_second,
    )


def solution(mesh):
    placed = (
        P("slab", "mp", None, None),
        P("slab", "mp", None),
        P("slab", "mp", None),
        P(),
        P(),
        P(),
    )
    sizes = (mesh.shape["slab"], mesh.shape["mp"])
    return jax.shard_map(
        functools.partial(on_device, sizes),
        mesh=mesh,
        in_specs=placed,
        out_specs=(P(), P(), P(), P(), P(), P()),
        check_vma=False,
    )
```

```python
import functools

import jax
import jax.numpy as jnp
from jax import lax
from jax.experimental import pallas as pl
from jax.experimental.pallas import tpu as pltpu
from jax.sharding import PartitionSpec as P

EMB = 96
HEADS = 6
HDIM = 16
HID = 384
MERGE = 384
CLASSES = 14
WIN = 7
SHIFT = 3
LAYERS = 3
STEP = 10

F32 = jnp.float32
BF16 = jnp.bfloat16
eps_norm = 1e-05
beta_one = 0.9
beta_two = 0.999
adam_eps = 1e-08
learn_rate = 0.05
decay_rate = 0.05
clip_norm = 0.01
LOG2E = 1.4426950408889634

VOX = WIN * WIN * WIN
ROWS = 384
BLK = 128
WIDE = 128
PLANE = WIN * WIN
FAR = WIN - SHIFT
ROWS_A = SHIFT * FAR * WIN
ROWS_B = FAR * SHIFT * WIN
ROWS_C = SHIFT * SHIFT * WIN

MERGE_ROWS = 392
LAYER_ROWS = 1165
TAP_ROWS = 27 * EMB
GROUPS = 2280
NPARAM = 872558
HEAD_ROW = 6806
HEAD_ROWS = 11
HEAD_LANE = 32
LATE_ROWS = 3072
EARLY_ROWS = 3840
LAYER_BASE = (98, 389, 680)
CONV_BASE = (971, 1620)
CUTS = (0, 392, 688, 976, 2280)

R_QKV, R_QKVB, R_PROJ, R_PROJB = 4, 292, 295, 391
R_HID, R_HIDB, R_OUT, R_OUTB = 392, 776, 780, 1164


def iota(shape, dim):
    return lax.broadcasted_iota(jnp.int32, shape, dim)


def split(x):
    hi = x.astype(BF16)
    return hi, (x - hi.astype(F32)).astype(BF16)


def pair(x):
    return jnp.concatenate(split(x), 1)


def fold(y):
    half = y.shape[1] // 2
    return y[:, :half] + y[:, half:]


def fold_rows(y):
    half = y.shape[0] // 2
    return y[:half] + y[half:]


def dot(a, b):
    return jnp.dot(a, b, preferred_element_type=F32)


def dot_nt(a, b):
    return lax.dot_general(a, b, (((1,), (1,)), ((), ())), preferred_element_type=F32)


def weight_nn(w):
    top = pair(w)
    return jnp.concatenate([top, top], 0)


def weight_nt(w):
    hi, lo = split(w)
    return jnp.concatenate(
        [jnp.concatenate([hi, hi], 1), jnp.concatenate([lo, lo], 1)], 0
    )


def mm(x, w):
    return fold(dot(pair(x), weight_nn(w)))


def mm_nt(x, w):
    return fold(dot_nt(pair(x), weight_nt(w)))


def rows_t(x):
    return jnp.concatenate(split(x.T), 0)


def mm_tn(xt, y):
    return fold_rows(fold(dot(xt, pair(y))))


def deep(w):
    return jnp.concatenate([w, jnp.zeros((WIDE - EMB, w.shape[1]), F32)], 0)


def roll(x, shift, axis):
    return pltpu.roll(x, shift, axis)


def four_to_three(y):
    lane = iota(y[0].shape, 1)
    a = jnp.where(lane < 96, y[0], roll(y[1], 96, 1))
    b = jnp.where(lane < 64, roll(y[1], 96, 1), roll(y[2], 64, 1))
    c = jnp.where(lane < 32, roll(y[2], 64, 1), roll(y[3], 32, 1))
    return a, b, c


def three_to_four(x):
    lane = iota(x[0].shape, 1)
    live = lane < EMB
    a = x[0]
    b = jnp.where(lane < 32, roll(x[0], 32, 1), roll(x[1], 32, 1))
    c = jnp.where(lane < 64, roll(x[1], 64, 1), roll(x[2], 64, 1))
    d = roll(x[2], 96, 1)
    return tuple(jnp.where(live, v, 0.0) for v in (a, b, c, d))


def hidden_rows(ref, start, count):
    return jnp.concatenate(
        four_to_three([ref[pl.ds(start + c, count, stride=4), :] for c in range(4)]), 1
    )


def put_hidden_rows(ref, start, count, x):
    parts = three_to_four([x[:, i * WIDE : (i + 1) * WIDE] for i in range(3)])
    for c in range(4):
        ref[pl.ds(start + c, count, stride=4), :] = parts[c]


def flatten(ref, start, groups, out):
    parts = four_to_three([ref[pl.ds(start + c, groups, stride=4), :] for c in range(4)])
    for c in range(3):
        out[pl.ds(c, groups, stride=3), :] = parts[c]


def norm_stats(x):
    live = iota(x.shape, 1) < EMB
    mean = jnp.sum(x, 1, keepdims=True) * (1.0 / EMB)
    centred = jnp.where(live, x - mean, 0.0)
    var = jnp.sum(centred * centred, 1, keepdims=True) * (1.0 / EMB)
    inv = lax.rsqrt(var + eps_norm)
    return centred * inv, inv


def norm(x, gain, bias):
    hat, _ = norm_stats(x)
    return hat * gain + bias


def norm_back(hat, inv, gain, grad):
    up = grad * gain
    one = jnp.sum(up, 1, keepdims=True) * (1.0 / EMB)
    two = jnp.sum(up * hat, 1, keepdims=True) * (1.0 / EMB)
    live = iota(hat.shape, 1) < EMB
    return jnp.where(live, inv * (up - one - hat * two), 0.0)


def colsum(x):
    return jnp.sum(x, 0, keepdims=True)


def gelu(x):
    return 0.5 * x * (1.0 + lax.erf(x * (0.5**0.5)))


def gelu_both(x):
    cdf = 0.5 * (1.0 + lax.erf(x * (0.5**0.5)))
    slope = cdf + x * (jnp.exp(x * x * -0.5) * 0.3989422804014327)
    return x * cdf, slope


def head_groups(x):
    lane = iota(x.shape, 1)
    swapped = roll(x, 64, 1)
    return jnp.where(lane < 64, x, swapped), jnp.where(lane < 64, swapped, x)


def as_left(x):
    both = []
    low = iota(x.shape, 1) < 64
    for part in head_groups(x):
        hi = part.astype(BF16).astype(F32)
        one = jnp.where(low, hi, part - hi).astype(BF16)
        both.append(jnp.concatenate([one, one], 1))
    return both


def as_right(x):
    return [pair(part) for part in head_groups(x)]


def head_mask(h, width):
    lane = iota((1, width), 1)
    lane = jnp.bitwise_and(lane, 63)
    low = jnp.bitwise_and(h, 3) * HDIM
    return jnp.where((lane >= low) & (lane < low + HDIM), 1.0, 0.0)


def own_lanes(h):
    lane = iota((1, WIDE), 1)
    return jnp.where((lane >= h * HDIM) & (lane < (h + 1) * HDIM), 1.0, 0.0)


def both_heads(right, heads, out):
    for k, h in enumerate(heads):
        out[k * ROWS : (k + 1) * ROWS, :] = right * head_mask(h, 2 * WIDE).astype(BF16)


def score_tiles(s, rows, region):
    tiles = [s[:, i * WIDE : (i + 1) * WIDE] for i in range(3)]
    if region is not None:
        return [t + region[rows, i * WIDE : (i + 1) * WIDE] for i, t in enumerate(tiles)]
    pad = jnp.where(iota((1, WIDE), 1) < VOX - 2 * WIDE, 0.0, -1e30)
    return tiles[:2] + [tiles[2] + pad]


def put_split(ref, rows, i, x):
    hi, lo = split(x)
    ref[rows, i * WIDE : (i + 1) * WIDE] = hi
    ref[rows, ROWS + i * WIDE : ROWS + (i + 1) * WIDE] = lo


def attention(normed, layer, save, lse, mixed, sc, region=None):
    left, right, values = sc
    x = pair(normed)
    qkv = []
    for i in range(3):
        w = deep(layer[pl.ds(R_QKV + i, EMB, stride=3), :])
        y = fold(dot(x, weight_nn(w))) + layer[R_QKVB + i : R_QKVB + i + 1, :]
        if i == 0:
            y = y * (HDIM**-0.5 * LOG2E)
        save[:, i * WIDE : (i + 1) * WIDE] = y
        qkv.append(y)
    for g, part in enumerate(as_left(qkv[0])):
        left[g] = part
    for g, part in enumerate(as_right(qkv[1])):
        right[g] = part
    v = pair(jnp.where(iota((ROWS, WIDE), 1) == EMB, 1.0, qkv[2]))
    values[0:ROWS, :] = v
    values[ROWS : 2 * ROWS, :] = v
    mixed[...] = jnp.zeros_like(mixed)
    lse[...] = jnp.zeros_like(lse)

    def per_pair(pair_of, carry):
        heads = [2 * pair_of, 2 * pair_of + 1]
        masks = [head_mask(h, 2 * WIDE).astype(BF16) for h in heads]
        lanes = [own_lanes(h) for h in heads]
        spots = [jnp.where(iota((1, WIDE), 1) == h, 1.0, 0.0) for h in heads]
        g = lax.div(pair_of, 2)
        for b in range(ROWS // BLK):
            rows = slice(b * BLK, (b + 1) * BLK)
            out = level = 0.0
            for k in range(2):
                s = dot_nt(left[g, rows, :] * masks[k], right[g])
                tiles = score_tiles(s, rows, region)
                top = jnp.maximum(jnp.maximum(tiles[0], tiles[1]), tiles[2])
                top = jnp.max(top, 1, keepdims=True)
                parts = [split(jnp.exp2(t - top)) for t in tiles]
                e = jnp.concatenate([p[0] for p in parts] + [p[1] for p in parts], 1)
                o = fold(dot(e, values[...]))
                total = o[:, EMB : EMB + 1]
                out = out + o * (lanes[k] / total)
                level = level + (top + jnp.log(total) * LOG2E) * spots[k]
            mixed[rows, :] += out
            lse[rows, :] += level
        return carry

    lax.fori_loop(0, HEADS // 2, per_pair, 0)
    proj = deep(layer[R_PROJ : R_PROJ + EMB, :])
    return mm(mixed[...], proj) + layer[R_PROJB : R_PROJB + 1, :]


def attention_back(grad, normed, layer, save, lse, mixed, sc, grads, at, region=None):
    left, right, gleft, vright, keys, dq, dkv_t, weights, slopes = sc[:9]
    q_t, do_t, dmix, s, dp, two_keys, two_values = sc[9:]
    proj = deep(layer[R_PROJ : R_PROJ + EMB, :])
    grads[at + R_PROJ : at + R_PROJ + EMB, :] = mm_tn(rows_t(mixed[...]), grad)[:EMB]
    grads[at + R_PROJB : at + R_PROJB + 1, :] = colsum(grad)
    d_mixed = mm_nt(grad, proj)
    dmix[...] = d_mixed * mixed[...]
    q, k, v = (save[:, i * WIDE : (i + 1) * WIDE] for i in range(3))
    for g, part in enumerate(as_left(q)):
        left[g] = part
    for g, part in enumerate(as_right(k)):
        right[g] = part
    for g, part in enumerate(as_left(d_mixed)):
        gleft[g] = part
    for g, part in enumerate(as_right(v)):
        vright[g] = part
    kk = pair(k)
    keys[0:ROWS, :] = kk
    keys[ROWS : 2 * ROWS, :] = kk
    for ref, x in ((q_t, q), (do_t, d_mixed)):
        hi, lo = split(x.T)
        ref[0] = hi
        ref[1] = lo
    dq[...] = jnp.zeros_like(dq)
    dkv_t[...] = jnp.zeros_like(dkv_t)

    def per_pair(pair_of, carry):
        g = lax.div(pair_of, 2)
        heads = [2 * pair_of, 2 * pair_of + 1]
        both_heads(right[g], heads, two_keys)
        both_heads(vright[g], heads, two_values)
        s[...] = dot_nt(left[g], two_keys[...])
        dp[...] = dot_nt(gleft[g], two_values[...])
        for k in range(2):
            h = 2 * pair_of + k
            lanes = own_lanes(h)
            at_h = jnp.where(iota((1, WIDE), 1) == h, 1.0, 0.0)
            for b in range(ROWS // BLK):
                rows = slice(b * BLK, (b + 1) * BLK)
                level = jnp.sum(lse[rows, :] * at_h, 1, keepdims=True)
                delta = jnp.sum(dmix[rows, :] * lanes, 1, keepdims=True)
                at_k = k * ROWS
                tiles = score_tiles(s[rows, at_k : at_k + ROWS], rows, region)
                for i, t in enumerate(tiles):
                    p = jnp.exp2(t - level)
                    put_split(weights.at[k], rows, i, p)
                    low = at_k + i * WIDE
                    p = p * (dp[rows, low : low + WIDE] - delta)
                    put_split(slopes.at[k], rows, i, p)
        total = 0.0
        for k in range(2):
            total = total + fold(dot(slopes[k], keys[...])) * own_lanes(2 * pair_of + k)
        dq[...] += total
        for k in range(2):
            here = pl.ds(pl.multiple_of((2 * pair_of + k) * HDIM, HDIM), HDIM)
            for i, (t, m) in enumerate(((q_t, slopes), (do_t, weights))):
                lhs = jnp.concatenate([t[0, here, :], t[1, here, :]], 0)
                dkv_t[i, here, :] = fold_rows(fold(dot(lhs, m[k])))
        return carry

    lax.fori_loop(0, HEADS // 2, per_pair, 0)
    d_q = dq[...] * HDIM**-0.5
    d_k = dkv_t[0].T * (1.0 / LOG2E)
    d_v = dkv_t[1].T
    x_t = rows_t(normed)
    d_normed = None
    for i, d in enumerate((d_q, d_k, d_v)):
        grads[pl.ds(at + R_QKV + i, EMB, stride=3), :] = mm_tn(x_t, d)[:EMB]
        grads[at + R_QKVB + i : at + R_QKVB + i + 1, :] = colsum(d)
        part = mm_nt(d, deep(layer[pl.ds(R_QKV + i, EMB, stride=3), :]))
        d_normed = part if d_normed is None else d_normed + part
    return d_normed


def mlp(middle, layer, hpre):
    normed = norm(middle, layer[2:3, :], layer[3:4, :])
    w = deep(hidden_rows(layer, R_HID, EMB))
    pre = mm(normed, w) + hidden_rows(layer, R_HIDB, 1)
    hpre[...] = pre
    out = mm(gelu(pre), layer[R_OUT : R_OUT + HID, :])
    return middle + out + layer[R_OUTB : R_OUTB + 1, :]


def mlp_back(grad, middle, hpre, layer, grads, at):
    hat, inv = norm_stats(middle)
    normed = hat * layer[2:3, :] + layer[3:4, :]
    act, slope = gelu_both(hpre[...])
    grads[at + R_OUTB : at + R_OUTB + 1, :] = colsum(grad)
    grads[at + R_OUT : at + R_OUT + HID, :] = mm_tn(rows_t(grad), act).T
    d_pre = mm_nt(grad, layer[R_OUT : R_OUT + HID, :]) * slope
    put_hidden_rows(grads, at + R_HIDB, 1, colsum(d_pre))
    put_hidden_rows(grads, at + R_HID, EMB, mm_tn(rows_t(normed), d_pre)[:EMB])
    d_normed = mm_nt(d_pre, deep(hidden_rows(layer, R_HID, EMB)))
    grads[at + 2 : at + 3, :] = colsum(d_normed * hat)
    grads[at + 3 : at + 4, :] = colsum(d_normed)
    return grad + norm_back(hat, inv, layer[2:3, :], d_normed)


def pre_norm_back(grad, tokens, layer, grads, at):
    hat, inv = norm_stats(tokens)
    grads[at : at + 1, :] = colsum(grad * hat)
    grads[at + 1 : at + 2, :] = colsum(grad)
    return norm_back(hat, inv, layer[0:1, :], grad)


def region_of(rows, sizes):
    d = lax.shift_right_logical(rows * 1338, 16)
    line = lax.shift_right_logical(rows * 9363, 16)
    places = (d, line - d * WIN, rows - line * WIN)
    starts = (lax.axis_index("slab") * WIN, lax.axis_index("mp") * WIN, 0)
    total = None
    for place, start, blocks in zip(places, starts, sizes + (1,)):
        turned = jnp.where(place < SHIFT, place + FAR, place - SHIFT) + start
        length = WIN * blocks
        part = jnp.where(turned < length - WIN, 0, jnp.where(turned < length - SHIFT, 1, 2))
        total = part if total is None else total * 3 + part
    return total


def put_region(region, sizes):
    rows = region_of(iota((ROWS, WIDE), 0), sizes)[:, 0:1]
    lanes = region_of(iota((8, ROWS), 1), sizes)[0:1, :]
    apart = jnp.where(rows == lanes, 0.0, -100.0 * LOG2E)
    region[...] = jnp.where(iota((ROWS, ROWS), 1) < VOX, apart, -1e30)


def send_parts(ref, a, b, c):
    far = FAR * WIN
    near = SHIFT * WIN
    for d in range(SHIFT):
        base = d * PLANE
        c[d * near : (d + 1) * near, :] = ref[base : base + near, :]
        a[d * far : (d + 1) * far, :] = ref[base + near : base + PLANE, :]
    for d in range(FAR):
        base = (d + SHIFT) * PLANE
        b[d * near : (d + 1) * near, :] = ref[base : base + near, :]


def take_parts(own, a, b, c, out):
    far = FAR * WIN
    near = SHIFT * WIN
    for d in range(WIN):
        base = d * PLANE
        if d < SHIFT:
            out[base : base + near, :] = c[d * near : (d + 1) * near, :]
            out[base + near : base + PLANE, :] = a[d * far : (d + 1) * far, :]
        else:
            e = d - SHIFT
            out[base : base + near, :] = b[e * near : (e + 1) * near, :]
            out[base + near : base + PLANE, :] = own[base + near : base + PLANE, :]
    out[VOX:, :] = jnp.zeros((ROWS - VOX, WIDE), F32)


def span_of(groups):
    low, high = groups
    first = 3 * low // 8 * 8
    last = -(-3 * high // 8) * 8
    return first, min(last, NPARAM // WIDE // 8 * 8) - first


def copied(params, groups, flat, sem):
    first, rows = span_of(groups)
    size = rows * WIDE
    return pltpu.make_async_copy(
        params.at[pl.ds(first * WIDE, size)], flat.at[pl.ds(0, size)], sem
    )


def relay(groups, flat, out, square, last=None):
    low, high = groups
    first, rows = span_of(groups)
    square[0:rows, :] = flat[0 : rows * WIDE].reshape(rows, WIDE)
    if last is not None:
        square[rows : rows + 24, :] = jnp.zeros((24, WIDE), F32)
        square[rows : rows + 1, 0 : last.shape[0]] = last[...].reshape(1, last.shape[0])
    skip = 3 * low - first
    n = high - low
    parts = three_to_four([square[pl.ds(skip + c, n, stride=3), :] for c in range(3)])
    for c in range(4):
        out[pl.ds(c, n, stride=4), :] = parts[c]


FIRST_SPANS = ((0, 98), (98, 392))
LAYER_SPANS = ((389, 681), (680, 972))
CONV_SPANS = ((971, 1620), (1620, GROUPS))


def prep_kernel(spans, params, *refs, last=None):
    outs, (flats, square, sems) = refs[: len(spans)], refs[-3:]
    for i, groups in enumerate(spans):
        copied(params, groups, flats[i], sems.at[i]).start()
    for i, groups in enumerate(spans):
        copied(params, groups, flats[i], sems.at[i]).wait()
        relay(groups, flats[i], outs[i], square, last if i == len(spans) - 1 else None)


def head_picks():
    width = HEAD_ROWS * WIDE
    place = iota((WIDE, width), 1) - HEAD_LANE
    row = iota((WIDE, width), 0)
    here = (place >= row * CLASSES) & (place < (row + 1) * CLASSES) & (row <= EMB)
    place = iota((width, WIDE), 0) - HEAD_LANE
    col = iota((width, WIDE), 1)
    row = lax.shift_right_logical(place * 4682, 16)
    there = (place - row * CLASSES == col) & (place >= 0)
    return jnp.where(here, 1.0, 0.0), jnp.where(there, 1.0, 0.0).astype(BF16)


def prep_conv0_kernel(params, conv0, weights0, bias, *scratch):
    prep_kernel(CONV_SPANS[:1], params, conv0, *scratch)
    tap_weights(conv0, 3, weights0)
    bias[0:1, :] = conv0[3 + TAP_ROWS : 4 + TAP_ROWS, :]
    bias[1:8, :] = jnp.zeros((7, WIDE), F32)


def prep_conv1_kernel(last, bias, params, conv1, head, weights1, vectors, *scratch):
    prep_kernel(CONV_SPANS[1:], params, conv1, *scratch, last=last)
    tap_weights(conv1, 0, weights1)
    vectors[0:1, :] = bias[0:1, :]
    vectors[1:4, :] = conv1[TAP_ROWS : TAP_ROWS + 3, :]
    vectors[4:8, :] = jnp.zeros((4, WIDE), F32)
    square = scratch[1]
    first, _ = span_of(CONV_SPANS[1])
    row = jnp.concatenate(
        [square[HEAD_ROW + i - first : HEAD_ROW + i - first + 1, :] for i in range(HEAD_ROWS)], 1
    )
    here, there = head_picks()
    hi, lo = split(here * row)
    head[...] = dot(hi, there) + dot(lo, there)


def head_rows(d_head, out, at):
    here, there = head_picks()
    hi, lo = split(d_head)
    spread = (dot_nt(hi, there) + dot_nt(lo, there)) * here
    row = colsum(spread)
    for i in range(HEAD_ROWS):
        out[at + i : at + i + 1, :] += row[:, i * WIDE : (i + 1) * WIDE]


class Rows:
    def __init__(self, ref, at):
        self.ref, self.at = ref, at

    def __getitem__(self, key):
        rows, lanes = key
        if isinstance(rows, slice):
            rows = slice(rows.start + self.at, rows.stop + self.at)
        else:
            rows = pl.ds(rows.start + self.at, rows.size, stride=rows.stride)
        return self.ref[rows, lanes]


def merged_norm(x):
    mean = jnp.sum(x, 1, keepdims=True) * (1.0 / MERGE)
    centred = x - mean
    var = jnp.sum(centred * centred, 1, keepdims=True) * (1.0 / MERGE)
    return centred * lax.rsqrt(var + eps_norm)


def first_kernel(
    feats, merge, lay0,
    dense, tok0, save, lse, mixed, middle, hpre, tok1, ahead, pa, pb, pc,
    *sc,
):
    dense[VOX:, :] = jnp.zeros((ROWS - VOX, MERGE), F32)
    for line in range(PLANE):
        dense[line * WIN : (line + 1) * WIN, :] = feats[line]
    hat = merged_norm(dense[...])
    normed = hat * hidden_rows(merge, 0, 1) + hidden_rows(merge, 4, 1)
    tokens = mm(normed, merge[8 : 8 + MERGE, :])
    tok0[...] = tokens
    layer = Rows(lay0, 0)
    normed = norm(tokens, layer[0:1, :], layer[1:2, :])
    attended = attention(normed, layer, save, lse, mixed, sc)
    mid = tokens + attended
    middle[...] = mid
    tokens = mlp(mid, layer, hpre)
    tok1[...] = tokens
    ahead[...] = norm(tokens, layer[1165:1166, :], layer[1166:1167, :])
    send_parts(ahead, pa, pb, pc)


def shifted_kernel(
    sizes,
    own, pa, pb, pc, lay1, _,
    window, save, lse, mixed, out, qa, qb, qc,
    region, *sc,
):
    put_region(region, sizes)
    take_parts(own, pa, pb, pc, window)
    out[...] = attention(
        window[...], Rows(lay1, 1), save, lse, mixed, sc, region
    )
    send_parts(out, qa, qb, qc)


def to_lines(ref, out):
    for line in range(PLANE):
        out[line, 0:WIN, :] = ref[line * WIN : (line + 1) * WIN, :]
        out[line, WIN:8, :] = jnp.zeros((8 - WIN, WIDE), F32)


def from_lines(ref, out):
    out[VOX:, :] = jnp.zeros((ROWS - VOX, WIDE), F32)
    for line in range(PLANE):
        out[line * WIN : (line + 1) * WIN, :] = ref[line, 0:WIN, :]


def send_sides(lines, near_d, far_d, near_h, far_h):
    odd_d = jnp.bitwise_and(lax.axis_index("slab"), 1) == 1
    odd_h = jnp.bitwise_and(lax.axis_index("mp"), 1) == 1
    low, high = lines[0 : 2 * WIN], lines[(WIN - 2) * WIN : PLANE]
    near_d[...] = jnp.where(odd_d, low, high)
    far_d[...] = jnp.where(odd_d, high, low)
    for d in range(WIN):
        low = lines[d * WIN : d * WIN + 2]
        high = lines[d * WIN + WIN - 2 : (d + 1) * WIN]
        near_h[2 * d : 2 * d + 2] = jnp.where(odd_h, low, high)
        far_h[2 * d : 2 * d + 2] = jnp.where(odd_h, high, low)


def second_kernel(
    tok1, own, qa, qb, qc, lay1, lay2, _,
    mid1, hpre1, tok2, save, lse, mixed, mid2, hpre2, lines,
    s0, s1, s2, s3,
    attended, *sc,
):
    take_parts(own, qa, qb, qc, attended)
    mid = tok1[...] + attended[...]
    mid1[...] = mid
    tokens = mlp(mid, Rows(lay1, 1), hpre1)
    tok2[...] = tokens
    layer = Rows(lay2, 2)
    normed = norm(tokens, layer[0:1, :], layer[1:2, :])
    mid = tokens + attention(normed, layer, save, lse, mixed, sc)
    mid2[...] = mid
    attended[...] = mlp(mid, layer, hpre2)
    to_lines(attended, lines)
    send_sides(lines, s0, s1, s2, s3)


def grown_lines(sizes, own, near_d, far_d, near_h, far_h, out):
    slab, row = lax.axis_index("slab"), lax.axis_index("mp")
    odd_d = jnp.bitwise_and(slab, 1) == 1
    odd_h = jnp.bitwise_and(row, 1) == 1
    out[:, 11:12] = jnp.zeros((11, 1, 8, WIDE), F32)
    for d in range(WIN):
        out[d + 2, 2 : 2 + WIN] = own[d * WIN : (d + 1) * WIN]
    for d in range(2):
        near = near_d[d * WIN : (d + 1) * WIN]
        far = far_d[d * WIN : (d + 1) * WIN]
        out[d, 2 : 2 + WIN] = jnp.where(odd_d, near, jnp.where(slab == 0, 0.0, far))
        out[d + 9, 2 : 2 + WIN] = jnp.where(
            odd_d, jnp.where(slab == sizes[0] - 1, 0.0, far), near
        )
    for d in range(11):
        near = near_h[2 * d : 2 * d + 2]
        far = far_h[2 * d : 2 * d + 2]
        out[d, 0:2] = jnp.where(odd_h, near, jnp.where(row == 0, 0.0, far))
        out[d, 9:11] = jnp.where(odd_h, jnp.where(row == sizes[1] - 1, 0.0, far), near)


def put_marks(labels, valid, out):
    across = iota((8, WIN), 1) == iota((8, WIN), 0)
    classes = iota((8, WIDE), 1) - EMB
    for d in range(WIN):
        code = jnp.where(valid[d] == 1, labels[d], -1 - EMB - WIDE)
        code = code.astype(F32)
        for h in range(WIN):
            line = jnp.where(across, code[h : h + 1, :], 0.0)
            column = jnp.sum(line, 1, keepdims=True)
            mark = jnp.where(column == classes.astype(F32), 1.0, 0.0)
            out[d * WIN + h] = jnp.where(iota((8, WIDE), 0) < WIN, mark, 0.0)


def taps(source, first_plane, planes, first_line, lines, out):
    def per_plane(d, carry):
        at = pl.ds(pl.multiple_of(d * (lines * 8), lines * 8), lines * 8)
        x = source[d + first_plane, first_line : first_line + lines + 2]
        for c in range(3):
            y = x if c == 1 else roll(x, 1 if c == 0 else 7, 1)
            hi = y.astype(BF16).astype(F32)
            lo = y - hi
            for b in range(3):
                t = (b * 3 + c) * 256
                part = hi[b : b + lines].reshape(lines * 8, WIDE)
                out[at, t : t + WIDE] = part.astype(BF16)
                part = lo[b : b + lines].reshape(lines * 8, WIDE)
                out[at, t + WIDE : t + 256] = part.astype(BF16)
        return carry

    lax.fori_loop(0, planes, per_plane, 0)


def tap_weights(ref, at, out):
    def per_tap(i, carry):
        w = deep(ref[pl.ds(i * EMB + at, EMB), :])
        out[pl.ds(pl.multiple_of(i * 256, 256), 256), :] = weight_nn(w)
        return carry

    lax.fori_loop(0, 27, per_tap, 0)


def tap_weights_back(ref, at, out):
    for i in range(27):
        w = deep(ref[(26 - i) * EMB + at : (27 - i) * EMB + at, :])
        out[:, i * 256 : (i + 1) * 256] = weight_nt(w)


def conv(side, weights, planes, pitch, at_once, put, back=False):
    rows = at_once * pitch
    for start in range(0, planes, at_once):
        total = None
        for a in range(3):
            low = (start + a) * pitch
            x = side[low : low + rows, :]
            if back:
                part = dot_nt(x, weights[:, a * 2304 : (a + 1) * 2304])
            else:
                part = dot(x, weights[a * 2304 : (a + 1) * 2304, :])
            total = part if total is None else total + part
        put(start, fold(total))


def conv_weight_grad(side, grad_rows, pitch, out, at):
    rows = 512
    g = jnp.concatenate([grad_rows, jnp.zeros((rows - grad_rows.shape[0], WIDE), F32)], 0)
    left = jnp.concatenate(split(g.T[:EMB]), 0)
    for a in range(3):
        for bc in range(9):
            y = dot(left, side[a * pitch : a * pitch + rows, bc * 256 : (bc + 1) * 256])
            y = deep(fold_rows(fold(y))).T
            t = a * 9 + bc
            out[at + t * EMB : at + (t + 1) * EMB, :] = y[:EMB]


def volume_mask(sizes, planes, lines, reach, real_lines):
    slab, row = lax.axis_index("slab"), lax.axis_index("mp")
    ends = (slab == 0, slab == sizes[0] - 1, row == 0, row == sizes[1] - 1)
    shape = (planes, lines, 8, WIDE)
    d, h, w = iota(shape, 0), iota(shape, 1), iota(shape, 2)
    low_d = jnp.where(ends[0], reach, 0)
    high_d = jnp.where(ends[1], planes - reach, planes)
    low_h = jnp.where(ends[2], reach, 0)
    high_h = jnp.where(ends[3], real_lines - reach, real_lines)
    inside = (d >= low_d) & (d < high_d) & (h >= low_h) & (h < high_h) & (w < WIN)
    return jnp.where(inside, 1.0, 0.0)


def conv_kernel(
    sizes,
    own, s0, s1, s2, s3, labels, valid, weights0, weights1, vectors,
    grown, pre, tok, stats, t0, t1, t2, t3,
    act, side, side_own, marks,
):
    grown_lines(sizes, own, s0, s1, s2, s3, grown)
    put_marks(labels, valid, marks)
    taps(grown, 0, 11, 0, 10, side)
    bias0 = vectors[0:1, :]
    inside = volume_mask(sizes, 9, 10, 1, 9)


    def put(start, y):
        z = (y + bias0).reshape(3, 10, 8, WIDE)
        pre[start : start + 3] = z
        act[start : start + 3] = gelu(z) * inside[start : start + 3]

    conv(side, weights0, 9, 80, 3, put)
    taps(act, 0, 9, 0, 8, side_own)
    bias1 = vectors[1:2, :]
    sums = []

    def put_own(start, y):
        y = (y + bias1).reshape(WIN, 8, 8, WIDE)[:, 0:WIN]
        y = y + own[...].reshape(WIN, WIN, 8, WIDE)
        y = jnp.where(iota(y.shape, 2) < WIN, y, 0.0).reshape(PLANE, 8, WIDE)
        tok[...] = y + marks[...]
        send_sides(tok, t0, t1, t2, t3)
        flat = y.reshape(PLANE * 8, WIDE)
        sums.append(colsum(flat))
        sums.append(colsum(flat * flat))

    conv(side_own, weights1, WIN, 64, WIN, put_own)
    count = jnp.sum(marks[...].reshape(PLANE * 8, WIDE))
    row = iota((8, WIDE), 0)
    stats[...] = (
        jnp.where(row == 0, sums[0], 0.0)
        + jnp.where(row == 1, sums[1], 0.0)
        + jnp.where(row == 2, count, 0.0)
    )


def head_math(voxels, both, sums, vectors, w):
    lane = iota(both.shape, 1)
    tokens = jnp.where(lane < EMB, both, 0.0)
    target = jnp.where(lane < CLASSES, roll(both, WIDE - EMB, 1), 0.0)
    live = jnp.sum(target, 1, keepdims=True)
    count = F32(voxels)
    average = sums[0:1, :] / count
    spread = sums[1:2, :] / count - average * average
    inv = lax.rsqrt(spread + eps_norm)
    gain, bias = vectors[2:3, :], vectors[3:4, :]
    hat = (tokens - average) * inv
    act, slope = gelu_both(hat * gain + bias)
    act = jnp.where(lane == EMB, 1.0, act)
    logits = jnp.where(lane < CLASSES, mm(act, w), -1e30)
    top = jnp.max(logits, 1, keepdims=True)
    e = jnp.exp(logits - top)
    total = jnp.sum(e, 1, keepdims=True)
    logp = logits - top - jnp.log(total)
    loss = jnp.where(lane < CLASSES, logp, 0.0) * target
    d_logits = (e / total * live - target) * (1.0 / sums[2:3, 0:1])
    d_normed = jnp.where(lane < EMB, mm_nt(d_logits, w) * slope, 0.0)
    return loss, act, hat, d_logits, d_normed, average, gain * inv, inv


def head_kernel(voxels, own, sums, vectors, head_w, stats, d_head, d_rows):
    both = own[...].reshape(PLANE * 8, WIDE)
    loss, act, hat, d_logits, d_normed, average, scale, inv = head_math(
        voxels, both, sums, vectors, head_w[...]
    )
    inside = jnp.bitwise_and(iota(both.shape, 0), 7) < WIN
    d_logits = jnp.where(inside, d_logits, 0.0)
    d_normed = jnp.where(inside, d_normed, 0.0)
    loss = -jnp.sum(jnp.where(inside, loss, 0.0))
    zeros = jnp.zeros((512 - PLANE * 8, WIDE), F32)
    left = rows_t(jnp.concatenate([d_logits, zeros], 0))
    d_head[...] = mm_tn(left, jnp.concatenate([act, zeros], 0)).T
    d_gain = colsum(d_normed * hat)
    d_bias = colsum(d_normed)
    d_average = -d_bias * scale
    d_spread = d_gain * scale * inv * -0.5
    count = F32(voxels)
    d_two = d_spread / count
    d_one = (d_average - 2.0 * average * d_spread) / count
    row = iota((8, WIDE), 0)
    live_lane = iota((8, WIDE), 1) < EMB
    stats[...] = (
        jnp.where((row == 0) & live_lane, d_one, 0.0)
        + jnp.where((row == 1) & live_lane, d_two, 0.0)
        + jnp.where(row == 2, loss, 0.0)
    )
    d_rows[...] = jnp.where(row == 0, d_gain, 0.0) + jnp.where(row == 1, d_bias, 0.0)


def head_wide_kernel(
    sizes, voxels, own, s0, s1, s2, s3, sums, vectors, head_w, grown, slope
):
    grown_lines(sizes, own, s0, s1, s2, s3, grown)
    both = grown[...].reshape(11 * 12 * 8, WIDE)
    _, _, _, _, d_normed, _, scale, _ = head_math(voxels, both, sums, vectors, head_w[...])
    slope[...] = (d_normed * scale).reshape(11, 12, 8, WIDE)


def sides_back_kernel(sizes, grown, pre, side_act, side_grown, act):
    act[0:9] = gelu(pre[...]) * volume_mask(sizes, 9, 10, 1, 9)
    act[9:10] = jnp.zeros((1, 10, 8, WIDE), F32)
    taps(act, 0, 10, 0, 8, side_act)
    taps(grown, 1, 10, 1, 8, side_grown)


def weights_back_kernel(conv0, conv1, weights0, weights1):
    tap_weights_back(conv0, 3, weights0)
    tap_weights_back(conv1, 0, weights1)


def conv_back_kernel(
    sizes,
    tok, slope, sums, pre, side_act, side_grown, weights0, weights1, d_rows, d_head,
    d_own, keep, send, carry, seam,
    grads, dgrown, act, side, side_own, flat,
):
    lane = iota((11, 12, 8, WIDE), 3)
    inside = volume_mask(sizes, 11, 12, 2, 11)
    steady = sums[0:1, :].reshape(1, 1, 1, WIDE)
    rising = 2.0 * sums[1:2, :].reshape(1, 1, 1, WIDE)
    d_tok = slope[...] + jnp.where(lane < EMB, (steady + tok[...] * rising) * inside, 0.0)
    dgrown[...] = d_tok
    grads[5191:, :] = jnp.zeros((45, WIDE), F32)
    grads[0:8, :] = jnp.zeros((8, WIDE), F32)
    grads[5189:5191, :] = d_rows[0:2, :]
    own = dgrown[2:9, 2:10]
    line = iota(own.shape, 1)
    own = jnp.where(line < WIN, own, 0.0).reshape(WIN * 64, WIDE)
    grads[5188:5189, :] = colsum(own)

    near = volume_mask(sizes, 9, 10, 1, 9)
    conv_weight_grad(side_act, own, 64, grads, 2596)
    taps(dgrown, 0, 11, 0, 10, side)


    def put(start, y):
        _, s = gelu_both(pre[start : start + 3])
        act[start : start + 3] = y.reshape(3, 10, 8, WIDE) * s * near[start : start + 3]

    conv(side, weights1, 9, 80, 3, put, back=True)

    own = act[1:8, 1:9]
    line = iota(own.shape, 1)
    own = jnp.where(line < WIN, own, 0.0).reshape(WIN * 64, WIDE)
    grads[2595:2596, :] = colsum(own)
    conv_weight_grad(side_grown, own, 64, grads, 3)
    carry[...] = grads[0:24, :]
    flat[3 * (GROUPS - CUTS[3]) :, :] = jnp.zeros((flat.shape[0] - 3912, WIDE), F32)
    flatten(grads, 20, GROUPS - CUTS[3], flat)
    start = 3 * CUTS[3]
    head_rows(d_head[...], flat, HEAD_ROW - start)
    seam[...] = flat[0 : LATE_ROWS - start, :]
    scatter(sizes, flat, LATE_ROWS - start, keep, send)
    taps(act, 0, 9, 0, 8, side_own)

    def put_own(start, y):
        y = y.reshape(WIN, 8, 8, WIDE)[:, 0:WIN] + dgrown[2:9, 2:9]
        y = jnp.where(iota(y.shape, 2) < WIN, y, 0.0)
        d_own[...] = y.reshape(PLANE, 8, WIDE)

    conv(side_own, weights0, WIN, 64, WIN, put_own, back=True)


def back_mlp_kernel(d_own, lay2, mid2, hpre2, d_mid, grads, dense):
    from_lines(d_own, dense)
    grads[...] = jnp.zeros_like(grads)
    d_mid[...] = mlp_back(dense[...], mid2[...], hpre2, Rows(lay2, 2), grads, 2)


def back_two_kernel(
    d_mid2, grads2, carry, lay1, lay2, tok2, save, lse, mixed, mid1, hpre1,
    d_mid, grads1, flat, carry2, pa, pb, pc,
    grads, *sc,
):
    layer = Rows(lay2, 2)
    grads[0:1168, :] = grads2[...]
    d = d_mid2[...]
    tokens = tok2[...]
    normed = norm(tokens, layer[0:1, :], layer[1:2, :])
    d_normed = attention_back(d, normed, layer, save, lse, mixed, sc, grads, 2)
    d = d + pre_norm_back(d_normed, tokens, layer, grads, 2)
    grads[1167:1184, :] = carry[3:20, :]
    flatten(grads, 32, CUTS[3] - CUTS[2], flat)
    carry2[...] = grads[0:32, :]
    layer = Rows(lay1, 1)
    d = mlp_back(d, mid1[...], hpre1, layer, grads1, 1)
    d_mid[...] = d
    send_parts(d_mid, pa, pb, pc)


def back_shifted_kernel(
    sizes,
    own, pa, pb, pc, lay1, window, save, lse, mixed, grads1, carry2, _,
    d_window, flat, carry1, qa, qb, qc,
    region, grads, grad, *sc,
):
    put_region(region, sizes)
    take_parts(own, pa, pb, pc, grad)
    grads[0:1168, :] = grads1[...]
    grads[0:3, :] = jnp.zeros((3, WIDE), F32)
    d_window[...] = attention_back(
        grad[...], window[...], Rows(lay1, 1), save, lse, mixed, sc, grads, 1,
        region,
    )
    send_parts(d_window, qa, qb, qc)
    grads[1166:1196, :] = carry2[2:32, :]
    flatten(grads, 12, CUTS[2] - CUTS[1], flat)
    carry1[...] = grads[0:16, :]


def back_first_kernel(
    sizes,
    d_mid, own, qa, qb, qc, tok1, lay0, lay1, merge, dense, tok0, save, lse, mixed, middle, hpre,
    carry1, flat1, flat2, seam, _,
    keep, send,
    flat, grads, grad, *sc,
):
    take_parts(own, qa, qb, qc, grad)
    grads[1556:1572, :] = carry1[...]
    d = d_mid[...] + pre_norm_back(grad[...], tok1[...], Rows(lay1, 1), grads, 1557)
    layer = Rows(lay0, 0)
    at = MERGE_ROWS
    d = mlp_back(d, middle[...], hpre, layer, grads, at)
    tokens = tok0[...]
    normed = norm(tokens, layer[0:1, :], layer[1:2, :])
    d_normed = attention_back(d, normed, layer, save, lse, mixed, sc, grads, at)
    d = d + pre_norm_back(d_normed, tokens, layer, grads, at)
    live = iota((ROWS, WIDE), 0) < VOX
    d = jnp.where(live, d, 0.0)
    hat = merged_norm(dense[...])
    gain = hidden_rows(merge, 0, 1)
    bias = hidden_rows(merge, 4, 1)
    w = merge[8 : 8 + MERGE, :]
    put_hidden_rows(grads, 8 - 8, 1, jnp.zeros((1, MERGE), F32))
    grads[8 : 8 + MERGE, :] = mm_tn(rows_t(d), hat * gain + bias).T
    d_hat = mm_nt(d, w)
    put_hidden_rows(grads, 0, 1, colsum(d_hat * hat))
    put_hidden_rows(grads, 4, 1, colsum(d_hat))
    flatten(grads, 0, CUTS[1], flat)
    at = 0
    for cut, part in ((CUTS[1], flat1), (CUTS[2], flat2), (CUTS[3], seam)):
        at = 3 * cut
        flat[at : at + part.shape[0], :] = part[...]
    at += seam.shape[0]
    if flat.shape[0] > at:
        flat[at:, :] = jnp.zeros((flat.shape[0] - at, WIDE), F32)
    scatter(sizes, flat, 0, keep, send)


def radices(count):
    steps = [2]
    left = count // 2
    while left > 1:
        steps.append(4 if left >= 4 else 2)
        left //= steps[-1]
    return steps


def block_rows(rows, count):
    return -(-rows // (8 * count)) * 8


def own_number(sizes):
    return lax.axis_index("slab") * sizes[1] + lax.axis_index("mp")


def place_in_half(distance, count):
    place = 0
    shift = 1
    for radix in radices(count)[1:]:
        digit = jnp.bitwise_and(lax.shift_right_logical(distance, shift), radix - 1)
        place = place * radix + digit
        shift += radix.bit_length() - 1
    return place


def scatter(sizes, source, first, keep, send):
    count = sizes[0] * sizes[1]
    rows = keep.shape[0] * 2 // count
    me = own_number(sizes)
    odd = jnp.bitwise_and(me, 1)

    def per_pair(t, carry):
        for block, out in ((2 * t + odd, keep), (2 * t + 1 - odd, send)):
            place = place_in_half(jnp.bitwise_xor(block, me), count)
            at = pl.multiple_of(first + block * rows, 8)
            to = pl.multiple_of(place * rows, 8)
            out[pl.ds(to, rows), :] = source[pl.ds(at, rows), :]
        return carry

    lax.fori_loop(0, count // 2, per_pair, 0)


def traded(value, distance, count):
    pairs = [(i, i ^ distance) for i in range(count)]
    return lax.ppermute(value, ("slab", "mp"), pairs)


def later(got, after):
    return got if after is None else list(lax.optimization_barrier((*got, after)))[:-1]


def summing(keep, send, count):
    steps = radices(count)
    got = [keep, traded(send, 1, count)]
    shift = 1
    after = yield None
    for radix in steps[1:]:
        got = later(got, after)
        total = sum(got[1:], got[0])
        rows = total.shape[0] // radix
        parts = [total[k * rows : (k + 1) * rows] for k in range(radix)]
        got = parts[:1] + [traded(parts[k], k << shift, count) for k in range(1, radix)]
        shift += radix.bit_length() - 1
        after = yield parts[0]
    got = later(got, after)
    own = sum(got[1:], got[0])
    for radix in reversed(steps[1:]):
        shift -= radix.bit_length() - 1
        got = [own] + [traded(own, k << shift, count) for k in range(1, radix)]
        after = yield own
        own = jnp.concatenate(later(got, after), 0)
        yield own
    yield own, traded(own, 1, count)


def finished(chain, after=None):
    last = next(chain) if after is None else chain.send(after)
    while not isinstance(last, tuple):
        last = next(chain)
    return last


def pairs_kernel(count, *refs):
    got = [ref[...] for ref in refs[:count]]
    while len(got) > 1:
        got = [got[i] + got[i + 1] for i in range(0, len(got), 2)]
    refs[-1][...] = got[0]


def exchanged_sum(value, count, after):
    shift = 0
    for step, radix in enumerate(radices(count)):
        got = [value] + [traded(value, k << shift, count) for k in range(1, radix)]
        (value,) = call(
            functools.partial(pairs_kernel, radix), [arr(*value.shape)], [], *got,
            name="pairs", us=0.2, far=after[step] if step < len(after) else (),
        )
        shift += radix.bit_length() - 1
    return value


PIECE = 131072


def adamw_kernel(
    sizes,
    late, late_other, early, early_other, tail, sums, params, first, second,
    new_params, new_first, new_second, loss, valid, norm_out,
    grad, scale_ref,
):
    count = sizes[0] * sizes[1]
    step = pl.program_id(0)

    @pl.when(step == 0)
    def gather():
        me = own_number(sizes)
        total = jnp.zeros((8, WIDE), F32)
        for ref in (late, late_other, early, early_other):
            x = ref[...]
            total = total + jnp.sum((x * x).reshape(-1, 8, WIDE), 0)
        norm = jnp.sqrt(jnp.sum(total))
        loss[0] = jnp.sum(tail[2:3, 0:1])
        valid[0] = jnp.sum(sums[2:3, 0:1])
        norm_out[0] = norm
        scale_ref[0] = jnp.minimum(1.0, clip_norm / (norm + 1e-06))
        start = 0
        for own, other, size in ((late, late_other, LATE_ROWS), (early, early_other, EARLY_ROWS)):
            rows = own.shape[0] * 2 // count

            def per_block(block, carry, own=own, other=other, rows=rows, start=start):
                distance = jnp.bitwise_xor(block, me)
                at = pl.ds(pl.multiple_of(place_in_half(distance, count) * rows, 8), rows)
                near = jnp.bitwise_and(distance, 1) == 0
                to = pl.ds(pl.multiple_of(start + block * rows, 8), rows)
                grad[to, :] = jnp.where(near, own[at, :], other[at, :])
                return carry

            lax.fori_loop(0, size // rows, per_block, 0)
            start += size

    def update(base, low, size):
        rows = -(-size // 1024) * 8
        at = pl.ds(pl.multiple_of(base // WIDE + low // WIDE, 8), rows)
        g = grad[at, :].reshape(rows * WIDE)[:size] * scale_ref[0]
        here = pl.ds(pl.multiple_of(base + low, 1024), size)
        one = beta_one * first[here] + (1.0 - beta_one) * g
        two = beta_two * second[here] + (1.0 - beta_two) * g * g
        there = pl.ds(low, size)
        new_first[there] = one
        new_second[there] = two
        two = two * (1.0 / (1.0 - beta_two**STEP))
        low_by = two * lax.rsqrt(jnp.maximum(two, 1e-37)) + adam_eps
        inverse = pl.reciprocal(low_by, approx=True)
        inverse = inverse * (2.0 - low_by * inverse)
        new_params[there] = params[here] * (1.0 - learn_rate * decay_rate) - (
            one * (learn_rate / (1.0 - beta_one**STEP))
        ) * inverse

    whole = NPARAM // PIECE

    @pl.when(step < whole)
    def full():
        def part(i, carry):
            low = pl.multiple_of(i * 16384, 16384)
            update(step * PIECE, low, 16384)
            return carry

        lax.fori_loop(0, PIECE // 16384, part, 0)

    @pl.when(step == whole)
    def last():
        rest = NPARAM - whole * PIECE
        main = rest // 1024 * 1024
        for low in range(0, main, 16384):
            update(whole * PIECE, low, min(16384, main - low))
        update(whole * PIECE, main, rest - main)


def adamw(sizes, parts, arrays):
    pieces = -(-NPARAM // PIECE)
    piece = pl.BlockSpec((PIECE,), lambda i: (i,))
    vmem = pl.BlockSpec(memory_space=pltpu.VMEM)
    smem = pl.BlockSpec(memory_space=pltpu.SMEM)
    return pl.pallas_call(
        functools.partial(adamw_kernel, sizes),
        grid=(pieces,),
        out_shape=[arr(NPARAM)] * 3 + [arr(1)] * 3,
        in_specs=[vmem] * (len(parts) + len(arrays)),
        out_specs=[piece] * 3 + [smem] * 3,
        scratch_shapes=[pltpu.VMEM((LATE_ROWS + EARLY_ROWS, WIDE), F32), pltpu.SMEM((1,), F32)],
        compiler_params=pltpu.CompilerParams(vmem_limit_bytes=16 * 1024 * 1024),
        cost_estimate=pl.CostEstimate(flops=6 * 10**9, bytes_accessed=0, transcendentals=0),
        name="adamw",
    )(*parts, *arrays)


def arr(*shape):
    return jax.ShapeDtypeStruct(shape, F32)


def call(kernel, outs, scratch, *args, name=None, us=1.0, far=(), mib=16):
    vmem = pl.BlockSpec(memory_space=pltpu.VMEM)
    smem = pl.BlockSpec(memory_space=pltpu.SMEM)
    return pl.pallas_call(
        kernel,
        out_shape=list(outs),
        in_specs=[vmem] * len(args) + [pl.BlockSpec(memory_space=pl.ANY)] * len(far),
        out_specs=[smem if o.shape == (1,) else vmem for o in outs],
        scratch_shapes=list(scratch),
        compiler_params=pltpu.CompilerParams(vmem_limit_bytes=mib * 1024 * 1024),
        cost_estimate=pl.CostEstimate(
            flops=int(us * 1.15e9), bytes_accessed=0, transcendentals=0
        ),
        name=name,
    )(*args, *far)


SQUARE = arr(ROWS, WIDE)
SAVE = arr(ROWS, 3 * WIDE)
FORWARD = [
    pltpu.VMEM((2, ROWS, 2 * WIDE), BF16),
    pltpu.VMEM((2, ROWS, 2 * WIDE), BF16),
    pltpu.VMEM((2 * ROWS, 2 * WIDE), BF16),
]
BACKWARD = [
    pltpu.VMEM((2, ROWS, 2 * WIDE), BF16),
    pltpu.VMEM((2, ROWS, 2 * WIDE), BF16),
    pltpu.VMEM((2, ROWS, 2 * WIDE), BF16),
    pltpu.VMEM((2, ROWS, 2 * WIDE), BF16),
    pltpu.VMEM((2 * ROWS, 2 * WIDE), BF16),
    pltpu.VMEM((ROWS, WIDE), F32),
    pltpu.VMEM((2, WIDE, ROWS), F32),
    pltpu.VMEM((2, ROWS, 2 * ROWS), BF16),
    pltpu.VMEM((2, ROWS, 2 * ROWS), BF16),
    pltpu.VMEM((2, WIDE, ROWS), BF16),
    pltpu.VMEM((2, WIDE, ROWS), BF16),
    pltpu.VMEM((ROWS, WIDE), F32),
    pltpu.VMEM((ROWS, 2 * ROWS), F32),
    pltpu.VMEM((ROWS, 2 * ROWS), F32),
    pltpu.VMEM((2 * ROWS, 2 * WIDE), BF16),
    pltpu.VMEM((2 * ROWS, 2 * WIDE), BF16),
]
PARTS = [arr(ROWS_A, WIDE), arr(ROWS_B, WIDE), arr(ROWS_C, WIDE)]


def passed(parts, steps, sizes):
    slabs, rows = sizes
    moved = []
    for part, (ds, dm) in zip(parts, ((1, 0), (0, 1), (1, 1))):
        pairs = []
        for s in range(slabs):
            for m in range(rows):
                target = ((s + steps * ds) % slabs) * rows + (m + steps * dm) % rows
                pairs.append((s * rows + m, target))
        moved.append(lax.ppermute(part, ("slab", "mp"), pairs))
    return moved


SIDES = [arr(2 * WIN, 8, WIDE)] * 4


def paired(axis, size):
    near = [(i, i ^ 1) for i in range(size)]
    far = [(i, (i + (1 if i % 2 else -1)) % size) for i in range(size)]
    return (
        lambda value: lax.ppermute(value, axis, near),
        lambda value: lax.ppermute(value, axis, far),
    )


def column_kernel(sizes, near_d, far_d, near_h, far_h, near_out, far_out):
    slab = lax.axis_index("slab")
    odd_d = jnp.bitwise_and(slab, 1) == 1
    odd_h = jnp.bitwise_and(lax.axis_index("mp"), 1) == 1
    at_low = slab == 0
    at_high = slab == sizes[0] - 1
    near_out[4:18] = near_h[...]
    far_out[4:18] = far_h[...]
    for d in range(2):
        near = near_d[d * WIN : (d + 1) * WIN]
        far = far_d[d * WIN : (d + 1) * WIN]
        before = jnp.where(odd_d, near, jnp.where(at_low, 0.0, far))
        after = jnp.where(odd_d, jnp.where(at_high, 0.0, far), near)
        for x, at in ((before, 2 * d), (after, 18 + 2 * d)):
            low, high = x[0:2], x[WIN - 2 : WIN]
            near_out[at : at + 2] = jnp.where(odd_h, low, high)
            far_out[at : at + 2] = jnp.where(odd_h, high, low)


def beside(sides, sizes):
    near, far = paired("slab", sizes[0])
    near_d, far_d = near(sides[0]), far(sides[1])
    near_h, far_h = call(
        functools.partial(column_kernel, sizes), [arr(22, 8, WIDE)] * 2, [],
        near_d, far_d, sides[2], sides[3],
        name="column", us=0.3,
    )
    near, far = paired("mp", sizes[1])
    return (near_d, far_d, near(near_h), far(far_h)), (near_h, far_h)


REGION = [pltpu.VMEM((ROWS, ROWS), F32)]


def on_device(sizes, feats, labels, valid, params, moment_one, moment_two):
    slabs, rows = sizes
    count = slabs * rows

    def room(spans):
        sizes = [(span_of(groups)[1] + 8) * WIDE for groups in spans]
        return [
            [pltpu.VMEM((size,), F32) for size in sizes],
            pltpu.VMEM((2048, WIDE), F32),
            pltpu.SemaphoreType.DMA((len(spans),)),
        ]

    first_size = FIRST_SPANS[-1][1] * 384
    merge, lay0 = call(
        functools.partial(prep_kernel, FIRST_SPANS),
        [arr(MERGE_ROWS, WIDE), arr(1176, WIDE)],
        room(FIRST_SPANS),
        name="prep_first", us=2.0, far=(params[:first_size],),
    )
    lay1, lay2 = call(
        functools.partial(prep_kernel, LAYER_SPANS),
        [arr(1168, WIDE)] * 2,
        room(LAYER_SPANS),
        name="prep_layers", us=2.0, far=(params,),
    )
    taps_shape = jax.ShapeDtypeStruct((27 * 256, 256), BF16)
    conv0, weights0, bias0 = call(
        prep_conv0_kernel,
        [arr(2596, WIDE), taps_shape, arr(8, WIDE)],
        room(CONV_SPANS[:1]),
        name="prep_conv0", us=1.5, far=(params,),
    )
    conv1, head_w, weights1, vectors = call(
        prep_conv1_kernel,
        [arr(2640, WIDE), arr(WIDE, WIDE), taps_shape, arr(8, WIDE)],
        room(CONV_SPANS[1:]),
        params[NPARAM // WIDE * WIDE :], bias0,
        name="prep_conv1", us=1.5, far=(params,),
    )

    dense, tok0, save0, lse0, mixed0, mid0, hpre0, tok1, ahead, *parts = call(
        first_kernel,
        [arr(ROWS, MERGE), SQUARE, SAVE, SQUARE, SQUARE, SQUARE, arr(ROWS, HID), SQUARE, SQUARE]
        + PARTS,
        FORWARD,
        feats.reshape(PLANE, WIN, MERGE), merge, lay0,
        name="first", us=6.0,
    )
    parts = passed(parts, -1, sizes)
    window, save1, lse1, mixed1, out1, *parts = call(
        functools.partial(shifted_kernel, sizes),
        [SQUARE, SAVE, SQUARE, SQUARE, SQUARE] + PARTS,
        REGION + FORWARD,
        ahead, *parts, lay1,
        name="shifted", us=4.5, far=(weights0,),
    )
    parts = passed(parts, 1, sizes)
    mid1, hpre1, tok2, save2, lse2, mixed2, mid2, hpre2, lines, *sides = call(
        second_kernel,
        [SQUARE, arr(ROWS, HID), SQUARE, SAVE, SQUARE, SQUARE, SQUARE, arr(ROWS, HID)]
        + [arr(PLANE, 8, WIDE)] + SIDES,
        [pltpu.VMEM((ROWS, WIDE), F32)] + FORWARD,
        tok1, out1, *parts, lay1, lay2,
        name="second", us=6.5, far=(weights1,),
    )
    sides, _ = beside(sides, sizes)
    grown, pre, tok3, sums, *tok_sides = call(
        functools.partial(conv_kernel, sizes),
        [arr(11, 12, 8, WIDE), arr(9, 10, 8, WIDE), arr(PLANE, 8, WIDE), arr(8, WIDE)] + SIDES,
        [
            pltpu.VMEM((9, 10, 8, WIDE), F32),
            pltpu.VMEM((880, 2304), BF16),
            pltpu.VMEM((576, 2304), BF16),
            pltpu.VMEM((PLANE, 8, WIDE), F32),
        ],
        lines, *sides, labels, valid, weights0, weights1, vectors,
        name="conv", us=8.0, mib=20,
    )
    tok_sides, columns = beside(tok_sides, sizes)
    weights0, weights1 = call(
        weights_back_kernel,
        [jax.ShapeDtypeStruct((256, 27 * 256), BF16)] * 2,
        [],
        conv0, conv1,
        name="weights_back", us=1.5,
    )
    sums = exchanged_sum(sums, count, ((), tok_sides[:2], columns))
    voxels = WIN * slabs * WIN * rows * WIN
    tail, d_head, d_rows = call(
        functools.partial(head_kernel, voxels),
        [arr(8, WIDE), arr(WIDE, WIDE), arr(8, WIDE)],
        [],
        tok3, sums, vectors, head_w,
        name="head", us=0.8,
    )
    tok3, slope = call(
        functools.partial(head_wide_kernel, sizes, voxels),
        [arr(11, 12, 8, WIDE)] * 2,
        [],
        tok3, *tok_sides, sums, vectors, head_w,
        name="head_wide", us=1.0,
    )
    side_act, side_grown = call(
        functools.partial(sides_back_kernel, sizes),
        [jax.ShapeDtypeStruct((640, 2304), BF16)] * 2,
        [pltpu.VMEM((10, 10, 8, WIDE), F32)],
        grown, pre,
        name="sides_back", us=0.9,
    )
    tail = exchanged_sum(tail, count, ((), tok_sides[2:], (slope, side_act)))
    late_rows = block_rows(LATE_ROWS, count) * count
    early_rows = block_rows(EARLY_ROWS, count) * count
    seam_rows = LATE_ROWS - 3 * CUTS[3]
    d_own, keep, send, carry3, seam = call(
        functools.partial(conv_back_kernel, sizes),
        [arr(PLANE, 8, WIDE)] + [arr(early_rows // 2, WIDE)] * 2
        + [arr(24, WIDE), arr(seam_rows, WIDE)],
        [
            pltpu.VMEM((5236, WIDE), F32),
            pltpu.VMEM((11, 12, 8, WIDE), F32),
            pltpu.VMEM((10, 10, 8, WIDE), F32),
            pltpu.VMEM((880, 2304), BF16),
            pltpu.VMEM((576, 2304), BF16),
            pltpu.VMEM((seam_rows + early_rows, WIDE), F32),
        ],
        tok3, slope, tail, pre, side_act, side_grown, weights0, weights1, d_rows, d_head,
        name="conv_back", us=14.0, mib=28,
    )
    early = summing(keep, send, count)
    next(early)
    d_mid2, grads2 = call(
        back_mlp_kernel,
        [SQUARE, arr(1168, WIDE)],
        [pltpu.VMEM((ROWS, WIDE), F32)],
        d_own, lay2, mid2, hpre2,
        name="back_mlp", us=3.0,
    )
    step = early.send(d_mid2)
    d_mid, grads1, flat2, carry2, *parts = call(
        back_two_kernel,
        [SQUARE, arr(1168, WIDE), arr(3 * (CUTS[3] - CUTS[2]), WIDE), arr(32, WIDE)] + PARTS,
        [pltpu.VMEM((1184, WIDE), F32)] + BACKWARD,
        d_mid2, grads2, carry3, lay1, lay2, tok2, save2, lse2, mixed2, mid1, hpre1,
        name="back_two", us=9.0,
    )
    parts = passed(parts, -1, sizes)
    step = early.send(d_mid)
    d_window, flat1, carry1, *parts = call(
        functools.partial(back_shifted_kernel, sizes),
        [SQUARE, arr(3 * (CUTS[2] - CUTS[1]), WIDE), arr(16, WIDE)] + PARTS,
        REGION + [pltpu.VMEM((1200, WIDE), F32), pltpu.VMEM((ROWS, WIDE), F32)] + BACKWARD,
        d_mid, *parts, lay1, window, save1, lse1, mixed1, grads1, carry2,
        name="back_shifted", us=10.5, far=(step,),
    )
    early.send(d_window)
    parts = passed(parts, 1, sizes)
    next(early)
    step = next(early)
    late = call(
        functools.partial(back_first_kernel, sizes),
        [arr(late_rows // 2, WIDE)] * 2,
        [
            pltpu.VMEM((late_rows, WIDE), F32),
            pltpu.VMEM((1572, WIDE), F32),
            pltpu.VMEM((ROWS, WIDE), F32),
        ]
        + BACKWARD,
        d_mid, d_window, *parts, tok1, lay0, lay1, merge, dense, tok0, save0, lse0, mixed0, mid0,
        hpre0, carry1, flat1, flat2, seam,
        name="back_first", us=13.5, far=(step,),
    )
    step = early.send(late[0])
    keep, send = later(list(late), step)
    late_sum = finished(summing(keep, send, count))
    early = finished(early)
    new_params, new_first, new_second, loss, valid_count, norm = adamw(
        sizes, (*late_sum, *early, tail, sums), (params, moment_one, moment_two)
    )
    return (
        loss.reshape(()), valid_count.reshape(()), norm.reshape(()),
        new_params, new_first, new_second,
    )


def solution(mesh):
    placed = (
        P("slab", "mp", None, None),
        P("slab", "mp", None),
        P("slab", "mp", None),
        P(),
        P(),
        P(),
    )
    sizes = (mesh.shape["slab"], mesh.shape["mp"])
    return jax.shard_map(
        functools.partial(on_device, sizes),
        mesh=mesh,
        in_specs=placed,
        out_specs=(P(), P(), P(), P(), P(), P()),
        check_vma=False,
    )
```

```python
import functools

import jax
import jax.numpy as jnp
from jax import lax
from jax.experimental import pallas as pl
from jax.experimental.pallas import tpu as pltpu
from jax.sharding import PartitionSpec as P

EMB = 96
HEADS = 6
HDIM = 16
HID = 384
MERGE = 384
CLASSES = 14
WIN = 7
SHIFT = 3
LAYERS = 3
STEP = 10

F32 = jnp.float32
BF16 = jnp.bfloat16
eps_norm = 1e-05
beta_one = 0.9
beta_two = 0.999
adam_eps = 1e-08
learn_rate = 0.05
decay_rate = 0.05
clip_norm = 0.01
LOG2E = 1.4426950408889634

VOX = WIN * WIN * WIN
ROWS = 384
BLK = 128
WIDE = 128
PLANE = WIN * WIN
FAR = WIN - SHIFT
ROWS_A = SHIFT * FAR * WIN
ROWS_B = FAR * SHIFT * WIN
ROWS_C = SHIFT * SHIFT * WIN

MERGE_ROWS = 392
LAYER_ROWS = 1165
TAP_ROWS = 27 * EMB
GROUPS = 2280
NPARAM = 872558
HEAD_ROW = 6806
HEAD_ROWS = 11
HEAD_LANE = 32
LATE_ROWS = 3072
EARLY_ROWS = 3840
LAYER_BASE = (98, 389, 680)
CONV_BASE = (971, 1620)
CUTS = (0, 392, 688, 976, 2280)

R_QKV, R_QKVB, R_PROJ, R_PROJB = 4, 292, 295, 391
R_HID, R_HIDB, R_OUT, R_OUTB = 392, 776, 780, 1164


def iota(shape, dim):
    return lax.broadcasted_iota(jnp.int32, shape, dim)


def split(x):
    hi = x.astype(BF16)
    return hi, (x - hi.astype(F32)).astype(BF16)


def pair(x):
    return jnp.concatenate(split(x), 1)


def fold(y):
    half = y.shape[1] // 2
    return y[:, :half] + y[:, half:]


def fold_rows(y):
    half = y.shape[0] // 2
    return y[:half] + y[half:]


def dot(a, b):
    return jnp.dot(a, b, preferred_element_type=F32)


def dot_nt(a, b):
    return lax.dot_general(a, b, (((1,), (1,)), ((), ())), preferred_element_type=F32)


def weight_nn(w):
    top = pair(w)
    return jnp.concatenate([top, top], 0)


def weight_nt(w):
    hi, lo = split(w)
    return jnp.concatenate(
        [jnp.concatenate([hi, hi], 1), jnp.concatenate([lo, lo], 1)], 0
    )


def mm(x, w):
    return fold(dot(pair(x), weight_nn(w)))


def mm_nt(x, w):
    return fold(dot_nt(pair(x), weight_nt(w)))


def rows_t(x):
    return jnp.concatenate(split(x.T), 0)


def mm_tn(xt, y):
    return fold_rows(fold(dot(xt, pair(y))))


def deep(w):
    return jnp.concatenate([w, jnp.zeros((WIDE - EMB, w.shape[1]), F32)], 0)


def roll(x, shift, axis):
    return pltpu.roll(x, shift, axis)


def four_to_three(y):
    lane = iota(y[0].shape, 1)
    a = jnp.where(lane < 96, y[0], roll(y[1], 96, 1))
    b = jnp.where(lane < 64, roll(y[1], 96, 1), roll(y[2], 64, 1))
    c = jnp.where(lane < 32, roll(y[2], 64, 1), roll(y[3], 32, 1))
    return a, b, c


def three_to_four(x):
    lane = iota(x[0].shape, 1)
    live = lane < EMB
    a = x[0]
    b = jnp.where(lane < 32, roll(x[0], 32, 1), roll(x[1], 32, 1))
    c = jnp.where(lane < 64, roll(x[1], 64, 1), roll(x[2], 64, 1))
    d = roll(x[2], 96, 1)
    return tuple(jnp.where(live, v, 0.0) for v in (a, b, c, d))


def hidden_rows(ref, start, count):
    return jnp.concatenate(
        four_to_three([ref[pl.ds(start + c, count, stride=4), :] for c in range(4)]), 1
    )


def put_hidden_rows(ref, start, count, x):
    parts = three_to_four([x[:, i * WIDE : (i + 1) * WIDE] for i in range(3)])
    for c in range(4):
        ref[pl.ds(start + c, count, stride=4), :] = parts[c]


def flatten(ref, start, groups, out):
    parts = four_to_three([ref[pl.ds(start + c, groups, stride=4), :] for c in range(4)])
    for c in range(3):
        out[pl.ds(c, groups, stride=3), :] = parts[c]


def norm_stats(x):
    live = iota(x.shape, 1) < EMB
    mean = jnp.sum(x, 1, keepdims=True) * (1.0 / EMB)
    centred = jnp.where(live, x - mean, 0.0)
    var = jnp.sum(centred * centred, 1, keepdims=True) * (1.0 / EMB)
    inv = lax.rsqrt(var + eps_norm)
    return centred * inv, inv


def norm(x, gain, bias):
    hat, _ = norm_stats(x)
    return hat * gain + bias


def norm_back(hat, inv, gain, grad):
    up = grad * gain
    one = jnp.sum(up, 1, keepdims=True) * (1.0 / EMB)
    two = jnp.sum(up * hat, 1, keepdims=True) * (1.0 / EMB)
    live = iota(hat.shape, 1) < EMB
    return jnp.where(live, inv * (up - one - hat * two), 0.0)


def colsum(x):
    return jnp.sum(x, 0, keepdims=True)


def gelu(x):
    return 0.5 * x * (1.0 + lax.erf(x * (0.5**0.5)))


def gelu_both(x):
    cdf = 0.5 * (1.0 + lax.erf(x * (0.5**0.5)))
    slope = cdf + x * (jnp.exp(x * x * -0.5) * 0.3989422804014327)
    return x * cdf, slope


def head_groups(x):
    lane = iota(x.shape, 1)
    swapped = roll(x, 64, 1)
    return jnp.where(lane < 64, x, swapped), jnp.where(lane < 64, swapped, x)


def as_left(x):
    both = []
    low = iota(x.shape, 1) < 64
    for part in head_groups(x):
        hi = part.astype(BF16).astype(F32)
        one = jnp.where(low, hi, part - hi).astype(BF16)
        both.append(jnp.concatenate([one, one], 1))
    return both


def as_right(x):
    x_t = x.T
    parts = (x_t[0:64], x_t[64:128])
    return [jnp.concatenate(split(jnp.concatenate([p, p], 0)), 0) for p in parts]


def head_mask(h, width):
    lane = iota((1, width), 1)
    lane = jnp.bitwise_and(lane, 63)
    low = jnp.bitwise_and(h, 3) * HDIM
    return jnp.where((lane >= low) & (lane < low + HDIM), 1.0, 0.0)


def own_lanes(h):
    lane = iota((1, WIDE), 1)
    return jnp.where((lane >= h * HDIM) & (lane < (h + 1) * HDIM), 1.0, 0.0)


def both_heads(right, heads, out):
    row = jnp.bitwise_and(iota((2 * WIDE, WIDE), 0), 63)
    for k, h in enumerate(heads):
        low = jnp.bitwise_and(h, 3) * HDIM
        mask = jnp.where((row >= low) & (row < low + HDIM), 1.0, 0.0).astype(BF16)
        for i in range(3):
            at = k * ROWS + i * WIDE
            out[:, at : at + WIDE] = right[:, i * WIDE : (i + 1) * WIDE] * mask


def score_tiles(s, rows, region):
    tiles = [s[:, i * WIDE : (i + 1) * WIDE] for i in range(3)]
    if region is not None:
        return [t + region[rows, i * WIDE : (i + 1) * WIDE] for i, t in enumerate(tiles)]
    pad = jnp.where(iota((1, WIDE), 1) < VOX - 2 * WIDE, 0.0, -1e30)
    return tiles[:2] + [tiles[2] + pad]


def put_split(ref, rows, i, x):
    hi, lo = split(x)
    ref[rows, i * WIDE : (i + 1) * WIDE] = hi
    ref[rows, ROWS + i * WIDE : ROWS + (i + 1) * WIDE] = lo


def attention(normed, layer, save, lse, mixed, sc, region=None):
    left, right, values = sc
    x = pair(normed)
    qkv = []
    for i in range(3):
        w = deep(layer[pl.ds(R_QKV + i, EMB, stride=3), :])
        y = fold(dot(x, weight_nn(w))) + layer[R_QKVB + i : R_QKVB + i + 1, :]
        if i == 0:
            y = y * (HDIM**-0.5 * LOG2E)
        save[:, i * WIDE : (i + 1) * WIDE] = y
        qkv.append(y)
    for g, part in enumerate(as_left(qkv[0])):
        left[g] = part
    for g, part in enumerate(as_right(qkv[1])):
        right[g] = part
    v = pair(jnp.where(iota((ROWS, WIDE), 1) == EMB, 1.0, qkv[2]))
    values[0:ROWS, :] = v
    values[ROWS : 2 * ROWS, :] = v
    mixed[...] = jnp.zeros_like(mixed)
    lse[...] = jnp.zeros_like(lse)

    def per_pair(pair_of, carry):
        heads = [2 * pair_of, 2 * pair_of + 1]
        masks = [head_mask(h, 2 * WIDE).astype(BF16) for h in heads]
        lanes = [own_lanes(h) for h in heads]
        spots = [jnp.where(iota((1, WIDE), 1) == h, 1.0, 0.0) for h in heads]
        g = lax.div(pair_of, 2)
        for b in range(ROWS // BLK):
            rows = slice(b * BLK, (b + 1) * BLK)
            out = level = 0.0
            for k in range(2):
                s = dot(left[g, rows, :] * masks[k], right[g])
                tiles = score_tiles(s, rows, region)
                top = jnp.maximum(jnp.maximum(tiles[0], tiles[1]), tiles[2])
                top = jnp.max(top, 1, keepdims=True)
                parts = [split(jnp.exp2(t - top)) for t in tiles]
                e = jnp.concatenate([p[0] for p in parts] + [p[1] for p in parts], 1)
                o = fold(dot(e, values[...]))
                total = o[:, EMB : EMB + 1]
                out = out + o * (lanes[k] / total)
                level = level + (top + jnp.log(total) * LOG2E) * spots[k]
            mixed[rows, :] += out
            lse[rows, :] += level
        return carry

    lax.fori_loop(0, HEADS // 2, per_pair, 0)
    proj = deep(layer[R_PROJ : R_PROJ + EMB, :])
    return mm(mixed[...], proj) + layer[R_PROJB : R_PROJB + 1, :]


def attention_back(grad, normed, layer, save, lse, mixed, sc, grads, at, region=None):
    left, right, gleft, vright, keys, dq, dkv_t, weights, slopes = sc[:9]
    q_t, do_t, dmix, s, dp, two_keys, two_values = sc[9:]
    proj = deep(layer[R_PROJ : R_PROJ + EMB, :])
    grads[at + R_PROJ : at + R_PROJ + EMB, :] = mm_tn(rows_t(mixed[...]), grad)[:EMB]
    grads[at + R_PROJB : at + R_PROJB + 1, :] = colsum(grad)
    d_mixed = mm_nt(grad, proj)
    dmix[...] = d_mixed * mixed[...]
    q, k, v = (save[:, i * WIDE : (i + 1) * WIDE] for i in range(3))
    for g, part in enumerate(as_left(q)):
        left[g] = part
    for g, part in enumerate(as_right(k)):
        right[g] = part
    for g, part in enumerate(as_left(d_mixed)):
        gleft[g] = part
    for g, part in enumerate(as_right(v)):
        vright[g] = part
    kk = pair(k)
    keys[0:ROWS, :] = kk
    keys[ROWS : 2 * ROWS, :] = kk
    for ref, x in ((q_t, q), (do_t, d_mixed)):
        hi, lo = split(x.T)
        ref[0] = hi
        ref[1] = lo
    dq[...] = jnp.zeros_like(dq)
    dkv_t[...] = jnp.zeros_like(dkv_t)

    def per_pair(pair_of, carry):
        g = lax.div(pair_of, 2)
        heads = [2 * pair_of, 2 * pair_of + 1]
        both_heads(right[g], heads, two_keys)
        both_heads(vright[g], heads, two_values)
        s[...] = dot(left[g], two_keys[...])
        dp[...] = dot(gleft[g], two_values[...])
        for k in range(2):
            h = 2 * pair_of + k
            lanes = own_lanes(h)
            at_h = jnp.where(iota((1, WIDE), 1) == h, 1.0, 0.0)
            for b in range(ROWS // BLK):
                rows = slice(b * BLK, (b + 1) * BLK)
                level = jnp.sum(lse[rows, :] * at_h, 1, keepdims=True)
                delta = jnp.sum(dmix[rows, :] * lanes, 1, keepdims=True)
                at_k = k * ROWS
                tiles = score_tiles(s[rows, at_k : at_k + ROWS], rows, region)
                for i, t in enumerate(tiles):
                    p = jnp.exp2(t - level)
                    put_split(weights.at[k], rows, i, p)
                    low = at_k + i * WIDE
                    p = p * (dp[rows, low : low + WIDE] - delta)
                    put_split(slopes.at[k], rows, i, p)
        total = 0.0
        for k in range(2):
            total = total + fold(dot(slopes[k], keys[...])) * own_lanes(2 * pair_of + k)
        dq[...] += total
        for k in range(2):
            here = pl.ds(pl.multiple_of((2 * pair_of + k) * HDIM, HDIM), HDIM)
            for i, (t, m) in enumerate(((q_t, slopes), (do_t, weights))):
                lhs = jnp.concatenate([t[0, here, :], t[1, here, :]], 0)
                dkv_t[i, here, :] = fold_rows(fold(dot(lhs, m[k])))
        return carry

    lax.fori_loop(0, HEADS // 2, per_pair, 0)
    d_q = dq[...] * HDIM**-0.5
    d_k = dkv_t[0].T * (1.0 / LOG2E)
    d_v = dkv_t[1].T
    x_t = rows_t(normed)
    d_normed = None
    for i, d in enumerate((d_q, d_k, d_v)):
        grads[pl.ds(at + R_QKV + i, EMB, stride=3), :] = mm_tn(x_t, d)[:EMB]
        grads[at + R_QKVB + i : at + R_QKVB + i + 1, :] = colsum(d)
        part = mm_nt(d, deep(layer[pl.ds(R_QKV + i, EMB, stride=3), :]))
        d_normed = part if d_normed is None else d_normed + part
    return d_normed


def mlp(middle, layer, hpre):
    normed = norm(middle, layer[2:3, :], layer[3:4, :])
    w = deep(hidden_rows(layer, R_HID, EMB))
    pre = mm(normed, w) + hidden_rows(layer, R_HIDB, 1)
    hpre[...] = pre
    out = mm(gelu(pre), layer[R_OUT : R_OUT + HID, :])
    return middle + out + layer[R_OUTB : R_OUTB + 1, :]


def mlp_back(grad, middle, hpre, layer, grads, at):
    hat, inv = norm_stats(middle)
    normed = hat * layer[2:3, :] + layer[3:4, :]
    act, slope = gelu_both(hpre[...])
    grads[at + R_OUTB : at + R_OUTB + 1, :] = colsum(grad)
    grads[at + R_OUT : at + R_OUT + HID, :] = mm_tn(rows_t(grad), act).T
    d_pre = mm_nt(grad, layer[R_OUT : R_OUT + HID, :]) * slope
    put_hidden_rows(grads, at + R_HIDB, 1, colsum(d_pre))
    put_hidden_rows(grads, at + R_HID, EMB, mm_tn(rows_t(normed), d_pre)[:EMB])
    d_normed = mm_nt(d_pre, deep(hidden_rows(layer, R_HID, EMB)))
    grads[at + 2 : at + 3, :] = colsum(d_normed * hat)
    grads[at + 3 : at + 4, :] = colsum(d_normed)
    return grad + norm_back(hat, inv, layer[2:3, :], d_normed)


def pre_norm_back(grad, tokens, layer, grads, at):
    hat, inv = norm_stats(tokens)
    grads[at : at + 1, :] = colsum(grad * hat)
    grads[at + 1 : at + 2, :] = colsum(grad)
    return norm_back(hat, inv, layer[0:1, :], grad)


def region_of(rows, sizes):
    d = lax.shift_right_logical(rows * 1338, 16)
    line = lax.shift_right_logical(rows * 9363, 16)
    places = (d, line - d * WIN, rows - line * WIN)
    starts = (lax.axis_index("slab") * WIN, lax.axis_index("mp") * WIN, 0)
    total = None
    for place, start, blocks in zip(places, starts, sizes + (1,)):
        turned = jnp.where(place < SHIFT, place + FAR, place - SHIFT) + start
        length = WIN * blocks
        part = jnp.where(turned < length - WIN, 0, jnp.where(turned < length - SHIFT, 1, 2))
        total = part if total is None else total * 3 + part
    return total


def put_region(region, sizes):
    rows = region_of(iota((ROWS, WIDE), 0), sizes)[:, 0:1]
    lanes = region_of(iota((8, ROWS), 1), sizes)[0:1, :]
    apart = jnp.where(rows == lanes, 0.0, -100.0 * LOG2E)
    region[...] = jnp.where(iota((ROWS, ROWS), 1) < VOX, apart, -1e30)


def send_parts(ref, a, b, c):
    far = FAR * WIN
    near = SHIFT * WIN
    for d in range(SHIFT):
        base = d * PLANE
        c[d * near : (d + 1) * near, :] = ref[base : base + near, :]
        a[d * far : (d + 1) * far, :] = ref[base + near : base + PLANE, :]
    for d in range(FAR):
        base = (d + SHIFT) * PLANE
        b[d * near : (d + 1) * near, :] = ref[base : base + near, :]


def take_parts(own, a, b, c, out):
    far = FAR * WIN
    near = SHIFT * WIN
    for d in range(WIN):
        base = d * PLANE
        if d < SHIFT:
            out[base : base + near, :] = c[d * near : (d + 1) * near, :]
            out[base + near : base + PLANE, :] = a[d * far : (d + 1) * far, :]
        else:
            e = d - SHIFT
            out[base : base + near, :] = b[e * near : (e + 1) * near, :]
            out[base + near : base + PLANE, :] = own[base + near : base + PLANE, :]
    out[VOX:, :] = jnp.zeros((ROWS - VOX, WIDE), F32)


def span_of(groups):
    low, high = groups
    first = 3 * low // 8 * 8
    last = -(-3 * high // 8) * 8
    return first, min(last, NPARAM // WIDE // 8 * 8) - first


def copied(params, groups, flat, sem):
    first, rows = span_of(groups)
    size = rows * WIDE
    return pltpu.make_async_copy(
        params.at[pl.ds(first * WIDE, size)], flat.at[pl.ds(0, size)], sem
    )


def relay(groups, flat, out, square, last=None):
    low, high = groups
    first, rows = span_of(groups)
    square[0:rows, :] = flat[0 : rows * WIDE].reshape(rows, WIDE)
    if last is not None:
        square[rows : rows + 24, :] = jnp.zeros((24, WIDE), F32)
        square[rows : rows + 1, 0 : last.shape[0]] = last[...].reshape(1, last.shape[0])
    skip = 3 * low - first
    n = high - low
    parts = three_to_four([square[pl.ds(skip + c, n, stride=3), :] for c in range(3)])
    for c in range(4):
        out[pl.ds(c, n, stride=4), :] = parts[c]


FIRST_SPANS = ((0, 98), (98, 392))
LAYER_SPANS = ((389, 681), (680, 972))
CONV_SPANS = ((971, 1620), (1620, GROUPS))


def prep_kernel(spans, params, *refs, last=None):
    outs, (flats, square, sems) = refs[: len(spans)], refs[-3:]
    for i, groups in enumerate(spans):
        copied(params, groups, flats[i], sems.at[i]).start()
    for i, groups in enumerate(spans):
        copied(params, groups, flats[i], sems.at[i]).wait()
        relay(groups, flats[i], outs[i], square, last if i == len(spans) - 1 else None)


def head_picks():
    width = HEAD_ROWS * WIDE
    place = iota((WIDE, width), 1) - HEAD_LANE
    row = iota((WIDE, width), 0)
    here = (place >= row * CLASSES) & (place < (row + 1) * CLASSES) & (row <= EMB)
    place = iota((width, WIDE), 0) - HEAD_LANE
    col = iota((width, WIDE), 1)
    row = lax.shift_right_logical(place * 4682, 16)
    there = (place - row * CLASSES == col) & (place >= 0)
    return jnp.where(here, 1.0, 0.0), jnp.where(there, 1.0, 0.0).astype(BF16)


def prep_conv0_kernel(params, conv0, weights0, bias, *scratch):
    prep_kernel(CONV_SPANS[:1], params, conv0, *scratch)
    tap_weights(conv0, 3, weights0)
    bias[0:1, :] = conv0[3 + TAP_ROWS : 4 + TAP_ROWS, :]
    bias[1:8, :] = jnp.zeros((7, WIDE), F32)


def prep_conv1_kernel(last, bias, params, conv1, head, weights1, vectors, *scratch):
    prep_kernel(CONV_SPANS[1:], params, conv1, *scratch, last=last)
    tap_weights(conv1, 0, weights1)
    vectors[0:1, :] = bias[0:1, :]
    vectors[1:4, :] = conv1[TAP_ROWS : TAP_ROWS + 3, :]
    vectors[4:8, :] = jnp.zeros((4, WIDE), F32)
    square = scratch[1]
    first, _ = span_of(CONV_SPANS[1])
    row = jnp.concatenate(
        [square[HEAD_ROW + i - first : HEAD_ROW + i - first + 1, :] for i in range(HEAD_ROWS)], 1
    )
    here, there = head_picks()
    hi, lo = split(here * row)
    head[...] = dot(hi, there) + dot(lo, there)


def head_rows(d_head, out, at):
    here, there = head_picks()
    hi, lo = split(d_head)
    spread = (dot_nt(hi, there) + dot_nt(lo, there)) * here
    row = colsum(spread)
    for i in range(HEAD_ROWS):
        out[at + i : at + i + 1, :] += row[:, i * WIDE : (i + 1) * WIDE]


class Rows:
    def __init__(self, ref, at):
        self.ref, self.at = ref, at

    def __getitem__(self, key):
        rows, lanes = key
        if isinstance(rows, slice):
            rows = slice(rows.start + self.at, rows.stop + self.at)
        else:
            rows = pl.ds(rows.start + self.at, rows.size, stride=rows.stride)
        return self.ref[rows, lanes]


def merged_norm(x):
    mean = jnp.sum(x, 1, keepdims=True) * (1.0 / MERGE)
    centred = x - mean
    var = jnp.sum(centred * centred, 1, keepdims=True) * (1.0 / MERGE)
    return centred * lax.rsqrt(var + eps_norm)


def first_kernel(
    feats, merge, lay0,
    dense, tok0, save, lse, mixed, middle, hpre, tok1, ahead, pa, pb, pc,
    *sc,
):
    dense[VOX:, :] = jnp.zeros((ROWS - VOX, MERGE), F32)
    for line in range(PLANE):
        dense[line * WIN : (line + 1) * WIN, :] = feats[line]
    hat = merged_norm(dense[...])
    normed = hat * hidden_rows(merge, 0, 1) + hidden_rows(merge, 4, 1)
    tokens = mm(normed, merge[8 : 8 + MERGE, :])
    tok0[...] = tokens
    layer = Rows(lay0, 0)
    normed = norm(tokens, layer[0:1, :], layer[1:2, :])
    attended = attention(normed, layer, save, lse, mixed, sc)
    mid = tokens + attended
    middle[...] = mid
    tokens = mlp(mid, layer, hpre)
    tok1[...] = tokens
    ahead[...] = norm(tokens, layer[1165:1166, :], layer[1166:1167, :])
    send_parts(ahead, pa, pb, pc)


def shifted_kernel(
    sizes,
    own, pa, pb, pc, lay1, _,
    window, save, lse, mixed, out, qa, qb, qc,
    region, *sc,
):
    put_region(region, sizes)
    take_parts(own, pa, pb, pc, window)
    out[...] = attention(
        window[...], Rows(lay1, 1), save, lse, mixed, sc, region
    )
    send_parts(out, qa, qb, qc)


def to_lines(ref, out):
    for line in range(PLANE):
        out[line, 0:WIN, :] = ref[line * WIN : (line + 1) * WIN, :]
        out[line, WIN:8, :] = jnp.zeros((8 - WIN, WIDE), F32)


def from_lines(ref, out):
    out[VOX:, :] = jnp.zeros((ROWS - VOX, WIDE), F32)
    for line in range(PLANE):
        out[line * WIN : (line + 1) * WIN, :] = ref[line, 0:WIN, :]


def send_sides(lines, near_d, far_d, near_h, far_h):
    odd_d = jnp.bitwise_and(lax.axis_index("slab"), 1) == 1
    odd_h = jnp.bitwise_and(lax.axis_index("mp"), 1) == 1
    low, high = lines[0 : 2 * WIN], lines[(WIN - 2) * WIN : PLANE]
    near_d[...] = jnp.where(odd_d, low, high)
    far_d[...] = jnp.where(odd_d, high, low)
    for d in range(WIN):
        low = lines[d * WIN : d * WIN + 2]
        high = lines[d * WIN + WIN - 2 : (d + 1) * WIN]
        near_h[2 * d : 2 * d + 2] = jnp.where(odd_h, low, high)
        far_h[2 * d : 2 * d + 2] = jnp.where(odd_h, high, low)


def second_kernel(
    tok1, own, qa, qb, qc, lay1, lay2, _,
    mid1, hpre1, tok2, save, lse, mixed, mid2, hpre2, lines,
    s0, s1, s2, s3,
    attended, *sc,
):
    take_parts(own, qa, qb, qc, attended)
    mid = tok1[...] + attended[...]
    mid1[...] = mid
    tokens = mlp(mid, Rows(lay1, 1), hpre1)
    tok2[...] = tokens
    layer = Rows(lay2, 2)
    normed = norm(tokens, layer[0:1, :], layer[1:2, :])
    mid = tokens + attention(normed, layer, save, lse, mixed, sc)
    mid2[...] = mid
    attended[...] = mlp(mid, layer, hpre2)
    to_lines(attended, lines)
    send_sides(lines, s0, s1, s2, s3)


def grown_lines(sizes, own, near_d, far_d, near_h, far_h, out):
    slab, row = lax.axis_index("slab"), lax.axis_index("mp")
    odd_d = jnp.bitwise_and(slab, 1) == 1
    odd_h = jnp.bitwise_and(row, 1) == 1
    out[:, 11:12] = jnp.zeros((11, 1, 8, WIDE), F32)
    for d in range(WIN):
        out[d + 2, 2 : 2 + WIN] = own[d * WIN : (d + 1) * WIN]
    for d in range(2):
        near = near_d[d * WIN : (d + 1) * WIN]
        far = far_d[d * WIN : (d + 1) * WIN]
        out[d, 2 : 2 + WIN] = jnp.where(odd_d, near, jnp.where(slab == 0, 0.0, far))
        out[d + 9, 2 : 2 + WIN] = jnp.where(
            odd_d, jnp.where(slab == sizes[0] - 1, 0.0, far), near
        )
    for d in range(11):
        near = near_h[2 * d : 2 * d + 2]
        far = far_h[2 * d : 2 * d + 2]
        out[d, 0:2] = jnp.where(odd_h, near, jnp.where(row == 0, 0.0, far))
        out[d, 9:11] = jnp.where(odd_h, jnp.where(row == sizes[1] - 1, 0.0, far), near)


def put_marks(labels, valid, out):
    across = iota((8, WIN), 1) == iota((8, WIN), 0)
    classes = iota((8, WIDE), 1) - EMB
    for d in range(WIN):
        code = jnp.where(valid[d] == 1, labels[d], -1 - EMB - WIDE)
        code = code.astype(F32)
        for h in range(WIN):
            line = jnp.where(across, code[h : h + 1, :], 0.0)
            column = jnp.sum(line, 1, keepdims=True)
            mark = jnp.where(column == classes.astype(F32), 1.0, 0.0)
            out[d * WIN + h] = jnp.where(iota((8, WIDE), 0) < WIN, mark, 0.0)


def taps(source, first_plane, planes, first_line, lines, out):
    def per_plane(d, carry):
        for c in range(3):
            for b in range(3):
                x = source[d + first_plane, first_line + b : first_line + b + lines]
                if c != 1:
                    x = roll(x, 1 if c == 0 else 7, 1)
                x = pair(x.reshape(lines * 8, WIDE))
                at = pl.multiple_of(d * (lines * 8), lines * 8)
                t = b * 3 + c
                out[pl.ds(at, lines * 8), t * 256 : (t + 1) * 256] = x
        return carry

    lax.fori_loop(0, planes, per_plane, 0)


def tap_weights(ref, at, out):
    def per_tap(i, carry):
        w = deep(ref[pl.ds(i * EMB + at, EMB), :])
        out[pl.ds(pl.multiple_of(i * 256, 256), 256), :] = weight_nn(w)
        return carry

    lax.fori_loop(0, 27, per_tap, 0)


def tap_weights_back(ref, at, out):
    for i in range(27):
        w = deep(ref[(26 - i) * EMB + at : (27 - i) * EMB + at, :]).T
        out[i * 256 : (i + 1) * 256, :] = weight_nn(w)


def conv(side, weights, planes, pitch, at_once, put):
    rows = at_once * pitch
    for start in range(0, planes, at_once):
        total = None
        for a in range(3):
            low = (start + a) * pitch
            x = side[low : low + rows, :]
            part = dot(x, weights[a * 2304 : (a + 1) * 2304, :])
            total = part if total is None else total + part
        put(start, fold(total))


def conv_weight_grad(side, grad_rows, pitch, out, at):
    rows = 512
    g = jnp.concatenate([grad_rows, jnp.zeros((rows - grad_rows.shape[0], WIDE), F32)], 0)
    left = jnp.concatenate(split(g.T[:EMB]), 0)
    for a in range(3):
        for bc in range(9):
            y = dot(left, side[a * pitch : a * pitch + rows, bc * 256 : (bc + 1) * 256])
            y = deep(fold_rows(fold(y))).T
            t = a * 9 + bc
            out[at + t * EMB : at + (t + 1) * EMB, :] = y[:EMB]


def volume_mask(sizes, planes, lines, reach, real_lines):
    slab, row = lax.axis_index("slab"), lax.axis_index("mp")
    ends = (slab == 0, slab == sizes[0] - 1, row == 0, row == sizes[1] - 1)
    shape = (planes, lines, 8, WIDE)
    d, h, w = iota(shape, 0), iota(shape, 1), iota(shape, 2)
    low_d = jnp.where(ends[0], reach, 0)
    high_d = jnp.where(ends[1], planes - reach, planes)
    low_h = jnp.where(ends[2], reach, 0)
    high_h = jnp.where(ends[3], real_lines - reach, real_lines)
    inside = (d >= low_d) & (d < high_d) & (h >= low_h) & (h < high_h) & (w < WIN)
    return jnp.where(inside, 1.0, 0.0)


def conv_kernel(
    sizes,
    own, s0, s1, s2, s3, labels, valid, weights0, weights1, vectors,
    grown, pre, tok, stats, t0, t1, t2, t3,
    act, side, side_own, marks,
):
    grown_lines(sizes, own, s0, s1, s2, s3, grown)
    put_marks(labels, valid, marks)
    taps(grown, 0, 11, 0, 10, side)
    bias0 = vectors[0:1, :]
    inside = volume_mask(sizes, 9, 10, 1, 9)


    def put(start, y):
        z = (y + bias0).reshape(3, 10, 8, WIDE)
        pre[start : start + 3] = z
        act[start : start + 3] = gelu(z) * inside[start : start + 3]

    conv(side, weights0, 9, 80, 3, put)
    taps(act, 0, 9, 0, 8, side_own)
    bias1 = vectors[1:2, :]
    sums = []

    def put_own(start, y):
        y = (y + bias1).reshape(WIN, 8, 8, WIDE)[:, 0:WIN]
        y = y + own[...].reshape(WIN, WIN, 8, WIDE)
        y = jnp.where(iota(y.shape, 2) < WIN, y, 0.0).reshape(PLANE, 8, WIDE)
        tok[...] = y + marks[...]
        send_sides(tok, t0, t1, t2, t3)
        flat = y.reshape(PLANE * 8, WIDE)
        sums.append(colsum(flat))
        sums.append(colsum(flat * flat))

    conv(side_own, weights1, WIN, 64, WIN, put_own)
    count = jnp.sum(marks[...].reshape(PLANE * 8, WIDE))
    row = iota((8, WIDE), 0)
    stats[...] = (
        jnp.where(row == 0, sums[0], 0.0)
        + jnp.where(row == 1, sums[1], 0.0)
        + jnp.where(row == 2, count, 0.0)
    )


def head_kernel(
    sizes, voxels,
    own, s0, s1, s2, s3, sums, vectors, head_w,
    grown, slope_out, stats, d_head, d_rows,
):
    grown_lines(sizes, own, s0, s1, s2, s3, grown)
    rows = 11 * 12 * 8
    both = grown[...].reshape(rows, WIDE)
    lane = iota((rows, WIDE), 1)
    tokens = jnp.where(lane < EMB, both, 0.0)
    target = jnp.where(lane < CLASSES, roll(both, WIDE - EMB, 1), 0.0)
    live = jnp.sum(target, 1, keepdims=True)
    count = F32(voxels)
    average = sums[0:1, :] / count
    spread = sums[1:2, :] / count - average * average
    inv = lax.rsqrt(spread + eps_norm)
    gain = vectors[2:3, :]
    bias = vectors[3:4, :]
    hat = (tokens - average) * inv
    act, slope = gelu_both(hat * gain + bias)
    act = jnp.where(lane == EMB, 1.0, act)
    w = head_w[...]
    logits = mm(act, w)
    logits = jnp.where(lane < CLASSES, logits, -1e30)
    top = jnp.max(logits, 1, keepdims=True)
    e = jnp.exp(logits - top)
    total = jnp.sum(e, 1, keepdims=True)
    logp = logits - top - jnp.log(total)
    scale = 1.0 / sums[2:3, 0:1]
    d_logits = (e / total * live - target) * scale
    d_normed = jnp.where(lane < EMB, mm_nt(d_logits, w) * slope, 0.0)
    d_tokens = d_normed * gain * inv
    slope_out[...] = d_tokens.reshape(11, 12, 8, WIDE)

    def own_rows(x):
        x = x.reshape(11, 12, 8, WIDE)[2:9, 2:9]
        x = jnp.where(iota(x.shape, 2) < WIN, x, 0.0)
        return x.reshape(PLANE * 8, WIDE)

    loss = -jnp.sum(own_rows(target * jnp.where(lane < CLASSES, logp, 0.0)))
    own_d = own_rows(d_logits)
    own_n = own_rows(d_normed)
    own_hat = own_rows(hat)
    zeros = jnp.zeros((512 - PLANE * 8, WIDE), F32)
    left = rows_t(jnp.concatenate([own_d, zeros], 0))
    d_head[...] = mm_tn(left, jnp.concatenate([own_rows(act), zeros], 0)).T
    d_gain = colsum(own_n * own_hat)
    d_bias = colsum(own_n)
    d_average = -d_bias * gain * inv
    d_spread = d_gain * gain * inv * inv * -0.5
    d_two = d_spread / count
    d_one = (d_average - 2.0 * average * d_spread) / count
    row = iota((8, WIDE), 0)
    live_lane = iota((8, WIDE), 1) < EMB
    stats[...] = (
        jnp.where((row == 0) & live_lane, d_one, 0.0)
        + jnp.where((row == 1) & live_lane, d_two, 0.0)
        + jnp.where(row == 2, loss, 0.0)
    )
    d_rows[...] = (
        jnp.where(row == 0, d_gain, 0.0)
        + jnp.where(row == 1, d_bias, 0.0)
    )


def sides_back_kernel(sizes, grown, pre, side_act, side_grown, act):
    act[0:9] = gelu(pre[...]) * volume_mask(sizes, 9, 10, 1, 9)
    act[9:10] = jnp.zeros((1, 10, 8, WIDE), F32)
    taps(act, 0, 10, 0, 8, side_act)
    taps(grown, 1, 10, 1, 8, side_grown)


def weights_back_kernel(conv0, conv1, weights0, weights1):
    tap_weights_back(conv0, 3, weights0)
    tap_weights_back(conv1, 0, weights1)


def conv_back_kernel(
    sizes,
    tok, slope, sums, pre, side_act, side_grown, weights0, weights1, d_rows, d_head,
    d_own, keep, send, carry, seam,
    grads, dgrown, act, side, side_own, flat,
):
    lane = iota((11, 12, 8, WIDE), 3)
    inside = volume_mask(sizes, 11, 12, 2, 11)
    steady = sums[0:1, :].reshape(1, 1, 1, WIDE)
    rising = 2.0 * sums[1:2, :].reshape(1, 1, 1, WIDE)
    d_tok = slope[...] + jnp.where(lane < EMB, (steady + tok[...] * rising) * inside, 0.0)
    dgrown[...] = d_tok
    grads[5191:, :] = jnp.zeros((45, WIDE), F32)
    grads[0:8, :] = jnp.zeros((8, WIDE), F32)
    grads[5189:5191, :] = d_rows[0:2, :]
    own = dgrown[2:9, 2:10]
    line = iota(own.shape, 1)
    own = jnp.where(line < WIN, own, 0.0).reshape(WIN * 64, WIDE)
    grads[5188:5189, :] = colsum(own)

    near = volume_mask(sizes, 9, 10, 1, 9)
    conv_weight_grad(side_act, own, 64, grads, 2596)
    taps(dgrown, 0, 11, 0, 10, side)


    def put(start, y):
        _, s = gelu_both(pre[start : start + 3])
        act[start : start + 3] = y.reshape(3, 10, 8, WIDE) * s * near[start : start + 3]

    conv(side, weights1, 9, 80, 3, put)

    own = act[1:8, 1:9]
    line = iota(own.shape, 1)
    own = jnp.where(line < WIN, own, 0.0).reshape(WIN * 64, WIDE)
    grads[2595:2596, :] = colsum(own)
    conv_weight_grad(side_grown, own, 64, grads, 3)
    carry[...] = grads[0:24, :]
    flat[3 * (GROUPS - CUTS[3]) :, :] = jnp.zeros((flat.shape[0] - 3912, WIDE), F32)
    flatten(grads, 20, GROUPS - CUTS[3], flat)
    start = 3 * CUTS[3]
    head_rows(d_head[...], flat, HEAD_ROW - start)
    seam[...] = flat[0 : LATE_ROWS - start, :]
    scatter(sizes, flat, LATE_ROWS - start, keep, send)
    taps(act, 0, 9, 0, 8, side_own)

    def put_own(start, y):
        y = y.reshape(WIN, 8, 8, WIDE)[:, 0:WIN] + dgrown[2:9, 2:9]
        y = jnp.where(iota(y.shape, 2) < WIN, y, 0.0)
        d_own[...] = y.reshape(PLANE, 8, WIDE)

    conv(side_own, weights0, WIN, 64, WIN, put_own)


def back_mlp_kernel(d_own, lay2, mid2, hpre2, d_mid, grads, dense):
    from_lines(d_own, dense)
    grads[...] = jnp.zeros_like(grads)
    d_mid[...] = mlp_back(dense[...], mid2[...], hpre2, Rows(lay2, 2), grads, 2)


def back_two_kernel(
    d_mid2, grads2, carry, lay1, lay2, tok2, save, lse, mixed, mid1, hpre1,
    d_mid, grads1, flat, carry2, pa, pb, pc,
    grads, *sc,
):
    layer = Rows(lay2, 2)
    grads[0:1168, :] = grads2[...]
    d = d_mid2[...]
    tokens = tok2[...]
    normed = norm(tokens, layer[0:1, :], layer[1:2, :])
    d_normed = attention_back(d, normed, layer, save, lse, mixed, sc, grads, 2)
    d = d + pre_norm_back(d_normed, tokens, layer, grads, 2)
    grads[1167:1184, :] = carry[3:20, :]
    flatten(grads, 32, CUTS[3] - CUTS[2], flat)
    carry2[...] = grads[0:32, :]
    layer = Rows(lay1, 1)
    d = mlp_back(d, mid1[...], hpre1, layer, grads1, 1)
    d_mid[...] = d
    send_parts(d_mid, pa, pb, pc)


def back_shifted_kernel(
    sizes,
    own, pa, pb, pc, lay1, window, save, lse, mixed, grads1, carry2, _,
    d_window, flat, carry1, qa, qb, qc,
    region, grads, grad, *sc,
):
    put_region(region, sizes)
    take_parts(own, pa, pb, pc, grad)
    grads[0:1168, :] = grads1[...]
    grads[0:3, :] = jnp.zeros((3, WIDE), F32)
    d_window[...] = attention_back(
        grad[...], window[...], Rows(lay1, 1), save, lse, mixed, sc, grads, 1,
        region,
    )
    send_parts(d_window, qa, qb, qc)
    grads[1166:1196, :] = carry2[2:32, :]
    flatten(grads, 12, CUTS[2] - CUTS[1], flat)
    carry1[...] = grads[0:16, :]


def back_first_kernel(
    sizes,
    d_mid, own, qa, qb, qc, tok1, lay0, lay1, merge, dense, tok0, save, lse, mixed, middle, hpre,
    carry1, flat1, flat2, seam, _,
    keep, send,
    flat, grads, grad, *sc,
):
    take_parts(own, qa, qb, qc, grad)
    grads[1556:1572, :] = carry1[...]
    d = d_mid[...] + pre_norm_back(grad[...], tok1[...], Rows(lay1, 1), grads, 1557)
    layer = Rows(lay0, 0)
    at = MERGE_ROWS
    d = mlp_back(d, middle[...], hpre, layer, grads, at)
    tokens = tok0[...]
    normed = norm(tokens, layer[0:1, :], layer[1:2, :])
    d_normed = attention_back(d, normed, layer, save, lse, mixed, sc, grads, at)
    d = d + pre_norm_back(d_normed, tokens, layer, grads, at)
    live = iota((ROWS, WIDE), 0) < VOX
    d = jnp.where(live, d, 0.0)
    hat = merged_norm(dense[...])
    gain = hidden_rows(merge, 0, 1)
    bias = hidden_rows(merge, 4, 1)
    w = merge[8 : 8 + MERGE, :]
    put_hidden_rows(grads, 8 - 8, 1, jnp.zeros((1, MERGE), F32))
    grads[8 : 8 + MERGE, :] = mm_tn(rows_t(d), hat * gain + bias).T
    d_hat = mm_nt(d, w)
    put_hidden_rows(grads, 0, 1, colsum(d_hat * hat))
    put_hidden_rows(grads, 4, 1, colsum(d_hat))
    flatten(grads, 0, CUTS[1], flat)
    at = 0
    for cut, part in ((CUTS[1], flat1), (CUTS[2], flat2), (CUTS[3], seam)):
        at = 3 * cut
        flat[at : at + part.shape[0], :] = part[...]
    at += seam.shape[0]
    if flat.shape[0] > at:
        flat[at:, :] = jnp.zeros((flat.shape[0] - at, WIDE), F32)
    scatter(sizes, flat, 0, keep, send)


def radices(count):
    steps = [2]
    left = count // 2
    while left > 1:
        steps.append(4 if left >= 4 else 2)
        left //= steps[-1]
    return steps


def block_rows(rows, count):
    return -(-rows // (8 * count)) * 8


def own_number(sizes):
    return lax.axis_index("slab") * sizes[1] + lax.axis_index("mp")


def place_in_half(distance, count):
    place = 0
    shift = 1
    for radix in radices(count)[1:]:
        digit = jnp.bitwise_and(lax.shift_right_logical(distance, shift), radix - 1)
        place = place * radix + digit
        shift += radix.bit_length() - 1
    return place


def scatter(sizes, source, first, keep, send):
    count = sizes[0] * sizes[1]
    rows = keep.shape[0] * 2 // count
    me = own_number(sizes)
    odd = jnp.bitwise_and(me, 1)

    def per_pair(t, carry):
        for block, out in ((2 * t + odd, keep), (2 * t + 1 - odd, send)):
            place = place_in_half(jnp.bitwise_xor(block, me), count)
            at = pl.multiple_of(first + block * rows, 8)
            to = pl.multiple_of(place * rows, 8)
            out[pl.ds(to, rows), :] = source[pl.ds(at, rows), :]
        return carry

    lax.fori_loop(0, count // 2, per_pair, 0)


def traded(value, distance, count):
    pairs = [(i, i ^ distance) for i in range(count)]
    return lax.ppermute(value, ("slab", "mp"), pairs)


def later(got, after):
    return got if after is None else list(lax.optimization_barrier((*got, after)))[:-1]


def summing(keep, send, count):
    steps = radices(count)
    got = [keep, traded(send, 1, count)]
    shift = 1
    after = yield None
    for radix in steps[1:]:
        got = later(got, after)
        total = sum(got[1:], got[0])
        rows = total.shape[0] // radix
        parts = [total[k * rows : (k + 1) * rows] for k in range(radix)]
        got = parts[:1] + [traded(parts[k], k << shift, count) for k in range(1, radix)]
        shift += radix.bit_length() - 1
        after = yield parts[0]
    got = later(got, after)
    own = sum(got[1:], got[0])
    for radix in reversed(steps[1:]):
        shift -= radix.bit_length() - 1
        got = [own] + [traded(own, k << shift, count) for k in range(1, radix)]
        after = yield own
        own = jnp.concatenate(later(got, after), 0)
        yield own
    yield own, traded(own, 1, count)


def finished(chain, after=None):
    last = next(chain) if after is None else chain.send(after)
    while not isinstance(last, tuple):
        last = next(chain)
    return last


def exchanged_sum(value, count):
    shift = 0
    for radix in radices(count):
        got = [value] + [traded(value, k << shift, count) for k in range(1, radix)]
        while len(got) > 1:
            got = [got[i] + got[i + 1] for i in range(0, len(got), 2)]
        value = got[0]
        shift += radix.bit_length() - 1
    return value


PIECE = 262144


def place_blocks(sizes, own, other, out, size):
    count = sizes[0] * sizes[1]
    me = own_number(sizes)
    rows = own.shape[0] * 2 // count

    def per_block(block, carry):
        distance = jnp.bitwise_xor(block, me)
        at = pl.ds(pl.multiple_of(place_in_half(distance, count) * rows, 8), rows)
        near = jnp.bitwise_and(distance, 1) == 0
        to = pl.ds(pl.multiple_of(block * rows, 8), rows)
        out[to, :] = jnp.where(near, own[at, :], other[at, :])
        return carry

    lax.fori_loop(0, size // rows, per_block, 0)


def squares(*refs):
    total = jnp.zeros((8, WIDE), F32)
    for ref in refs:
        x = ref[...]
        total = total + jnp.sum((x * x).reshape(-1, 8, WIDE), 0)
    return total


def place_early_kernel(sizes, own, other, out, square):
    place_blocks(sizes, own, other, out, EARLY_ROWS)
    square[...] = squares(own, other)


def adamw_kernel(
    sizes,
    late, late_other, early, square, tail, sums, params, first, second,
    new_params, new_first, new_second, loss, valid, norm_out,
    grad, scale_ref,
):
    step = pl.program_id(0)

    @pl.when(step == 0)
    def gather():
        norm = jnp.sqrt(jnp.sum(squares(late, late_other) + square[...]))
        loss[0] = jnp.sum(tail[2:3, 0:1])
        valid[0] = jnp.sum(sums[2:3, 0:1])
        norm_out[0] = norm
        scale_ref[0] = jnp.minimum(1.0, clip_norm / (norm + 1e-06))
        place_blocks(sizes, late, late_other, grad, LATE_ROWS)
        grad[LATE_ROWS:, :] = early[...]

    def update(base, low, size):
        rows = -(-size // 1024) * 8
        at = pl.ds(pl.multiple_of(base // WIDE + low // WIDE, 8), rows)
        g = grad[at, :].reshape(rows * WIDE)[:size] * scale_ref[0]
        here = pl.ds(pl.multiple_of(base + low, 1024), size)
        one = beta_one * first[here] + (1.0 - beta_one) * g
        two = beta_two * second[here] + (1.0 - beta_two) * g * g
        there = pl.ds(low, size)
        new_first[there] = one
        new_second[there] = two
        two = two * (1.0 / (1.0 - beta_two**STEP))
        low_by = two * lax.rsqrt(jnp.maximum(two, 1e-37)) + adam_eps
        inverse = pl.reciprocal(low_by, approx=True)
        inverse = inverse * (2.0 - low_by * inverse)
        new_params[there] = params[here] * (1.0 - learn_rate * decay_rate) - (
            one * (learn_rate / (1.0 - beta_one**STEP))
        ) * inverse

    whole = NPARAM // PIECE

    @pl.when(step < whole)
    def full():
        def part(i, carry):
            low = pl.multiple_of(i * 16384, 16384)
            update(step * PIECE, low, 16384)
            return carry

        lax.fori_loop(0, PIECE // 16384, part, 0)

    @pl.when(step == whole)
    def last():
        rest = NPARAM - whole * PIECE
        main = rest // 1024 * 1024
        for low in range(0, main, 16384):
            update(whole * PIECE, low, min(16384, main - low))
        update(whole * PIECE, main, rest - main)


def adamw(sizes, parts, arrays):
    pieces = -(-NPARAM // PIECE)
    piece = pl.BlockSpec((PIECE,), lambda i: (i,))
    vmem = pl.BlockSpec(memory_space=pltpu.VMEM)
    smem = pl.BlockSpec(memory_space=pltpu.SMEM)
    return pl.pallas_call(
        functools.partial(adamw_kernel, sizes),
        grid=(pieces,),
        out_shape=[arr(NPARAM)] * 3 + [arr(1)] * 3,
        in_specs=[vmem] * (len(parts) + len(arrays)),
        out_specs=[piece] * 3 + [smem] * 3,
        scratch_shapes=[pltpu.VMEM((LATE_ROWS + EARLY_ROWS, WIDE), F32), pltpu.SMEM((1,), F32)],
        compiler_params=pltpu.CompilerParams(vmem_limit_bytes=16 * 1024 * 1024),
        cost_estimate=pl.CostEstimate(flops=6 * 10**9, bytes_accessed=0, transcendentals=0),
        name="adamw",
    )(*parts, *arrays)


def arr(*shape):
    return jax.ShapeDtypeStruct(shape, F32)


def call(kernel, outs, scratch, *args, name=None, us=1.0, far=(), mib=16):
    vmem = pl.BlockSpec(memory_space=pltpu.VMEM)
    smem = pl.BlockSpec(memory_space=pltpu.SMEM)
    return pl.pallas_call(
        kernel,
        out_shape=list(outs),
        in_specs=[vmem] * len(args) + [pl.BlockSpec(memory_space=pl.ANY)] * len(far),
        out_specs=[smem if o.shape == (1,) else vmem for o in outs],
        scratch_shapes=list(scratch),
        compiler_params=pltpu.CompilerParams(vmem_limit_bytes=mib * 1024 * 1024),
        cost_estimate=pl.CostEstimate(
            flops=int(us * 1.15e9), bytes_accessed=0, transcendentals=0
        ),
        name=name,
    )(*args, *far)


SQUARE = arr(ROWS, WIDE)
SAVE = arr(ROWS, 3 * WIDE)
FORWARD = [
    pltpu.VMEM((2, ROWS, 2 * WIDE), BF16),
    pltpu.VMEM((2, 2 * WIDE, ROWS), BF16),
    pltpu.VMEM((2 * ROWS, 2 * WIDE), BF16),
]
BACKWARD = [
    pltpu.VMEM((2, ROWS, 2 * WIDE), BF16),
    pltpu.VMEM((2, 2 * WIDE, ROWS), BF16),
    pltpu.VMEM((2, ROWS, 2 * WIDE), BF16),
    pltpu.VMEM((2, 2 * WIDE, ROWS), BF16),
    pltpu.VMEM((2 * ROWS, 2 * WIDE), BF16),
    pltpu.VMEM((ROWS, WIDE), F32),
    pltpu.VMEM((2, WIDE, ROWS), F32),
    pltpu.VMEM((2, ROWS, 2 * ROWS), BF16),
    pltpu.VMEM((2, ROWS, 2 * ROWS), BF16),
    pltpu.VMEM((2, WIDE, ROWS), BF16),
    pltpu.VMEM((2, WIDE, ROWS), BF16),
    pltpu.VMEM((ROWS, WIDE), F32),
    pltpu.VMEM((ROWS, 2 * ROWS), F32),
    pltpu.VMEM((ROWS, 2 * ROWS), F32),
    pltpu.VMEM((2 * WIDE, 2 * ROWS), BF16),
    pltpu.VMEM((2 * WIDE, 2 * ROWS), BF16),
]
PARTS = [arr(ROWS_A, WIDE), arr(ROWS_B, WIDE), arr(ROWS_C, WIDE)]


def passed(parts, steps, sizes):
    slabs, rows = sizes
    moved = []
    for part, (ds, dm) in zip(parts, ((1, 0), (0, 1), (1, 1))):
        pairs = []
        for s in range(slabs):
            for m in range(rows):
                target = ((s + steps * ds) % slabs) * rows + (m + steps * dm) % rows
                pairs.append((s * rows + m, target))
        moved.append(lax.ppermute(part, ("slab", "mp"), pairs))
    return moved


SIDES = [arr(2 * WIN, 8, WIDE)] * 4


def paired(axis, size):
    near = [(i, i ^ 1) for i in range(size)]
    far = [(i, (i + (1 if i % 2 else -1)) % size) for i in range(size)]
    return (
        lambda value: lax.ppermute(value, axis, near),
        lambda value: lax.ppermute(value, axis, far),
    )


def column_kernel(sizes, near_d, far_d, near_h, far_h, near_out, far_out):
    slab = lax.axis_index("slab")
    odd_d = jnp.bitwise_and(slab, 1) == 1
    odd_h = jnp.bitwise_and(lax.axis_index("mp"), 1) == 1
    at_low = slab == 0
    at_high = slab == sizes[0] - 1
    near_out[4:18] = near_h[...]
    far_out[4:18] = far_h[...]
    for d in range(2):
        near = near_d[d * WIN : (d + 1) * WIN]
        far = far_d[d * WIN : (d + 1) * WIN]
        before = jnp.where(odd_d, near, jnp.where(at_low, 0.0, far))
        after = jnp.where(odd_d, jnp.where(at_high, 0.0, far), near)
        for x, at in ((before, 2 * d), (after, 18 + 2 * d)):
            low, high = x[0:2], x[WIN - 2 : WIN]
            near_out[at : at + 2] = jnp.where(odd_h, low, high)
            far_out[at : at + 2] = jnp.where(odd_h, high, low)


def beside(sides, sizes):
    near, far = paired("slab", sizes[0])
    near_d, far_d = near(sides[0]), far(sides[1])
    near_h, far_h = call(
        functools.partial(column_kernel, sizes), [arr(22, 8, WIDE)] * 2, [],
        near_d, far_d, sides[2], sides[3],
        name="column", us=0.3,
    )
    near, far = paired("mp", sizes[1])
    return near_d, far_d, near(near_h), far(far_h)


REGION = [pltpu.VMEM((ROWS, ROWS), F32)]


def on_device(sizes, feats, labels, valid, params, moment_one, moment_two):
    slabs, rows = sizes
    count = slabs * rows

    def room(spans):
        sizes = [(span_of(groups)[1] + 8) * WIDE for groups in spans]
        return [
            [pltpu.VMEM((size,), F32) for size in sizes],
            pltpu.VMEM((2048, WIDE), F32),
            pltpu.SemaphoreType.DMA((len(spans),)),
        ]

    first_size = FIRST_SPANS[-1][1] * 384
    merge, lay0 = call(
        functools.partial(prep_kernel, FIRST_SPANS),
        [arr(MERGE_ROWS, WIDE), arr(1176, WIDE)],
        room(FIRST_SPANS),
        name="prep_first", us=2.0, far=(params[:first_size],),
    )
    lay1, lay2 = call(
        functools.partial(prep_kernel, LAYER_SPANS),
        [arr(1168, WIDE)] * 2,
        room(LAYER_SPANS),
        name="prep_layers", us=2.0, far=(params,),
    )
    taps_shape = jax.ShapeDtypeStruct((27 * 256, 256), BF16)
    conv0, weights0, bias0 = call(
        prep_conv0_kernel,
        [arr(2596, WIDE), taps_shape, arr(8, WIDE)],
        room(CONV_SPANS[:1]),
        name="prep_conv0", us=1.5, far=(params,),
    )
    conv1, head_w, weights1, vectors = call(
        prep_conv1_kernel,
        [arr(2640, WIDE), arr(WIDE, WIDE), taps_shape, arr(8, WIDE)],
        room(CONV_SPANS[1:]),
        params[NPARAM // WIDE * WIDE :], bias0,
        name="prep_conv1", us=1.5, far=(params,),
    )

    dense, tok0, save0, lse0, mixed0, mid0, hpre0, tok1, ahead, *parts = call(
        first_kernel,
        [arr(ROWS, MERGE), SQUARE, SAVE, SQUARE, SQUARE, SQUARE, arr(ROWS, HID), SQUARE, SQUARE]
        + PARTS,
        FORWARD,
        feats.reshape(PLANE, WIN, MERGE), merge, lay0,
        name="first", us=6.0,
    )
    parts = passed(parts, -1, sizes)
    window, save1, lse1, mixed1, out1, *parts = call(
        functools.partial(shifted_kernel, sizes),
        [SQUARE, SAVE, SQUARE, SQUARE, SQUARE] + PARTS,
        REGION + FORWARD,
        ahead, *parts, lay1,
        name="shifted", us=4.5, far=(weights0,),
    )
    parts = passed(parts, 1, sizes)
    mid1, hpre1, tok2, save2, lse2, mixed2, mid2, hpre2, lines, *sides = call(
        second_kernel,
        [SQUARE, arr(ROWS, HID), SQUARE, SAVE, SQUARE, SQUARE, SQUARE, arr(ROWS, HID)]
        + [arr(PLANE, 8, WIDE)] + SIDES,
        [pltpu.VMEM((ROWS, WIDE), F32)] + FORWARD,
        tok1, out1, *parts, lay1, lay2,
        name="second", us=6.5, far=(weights1,),
    )
    sides = beside(sides, sizes)
    grown, pre, tok3, sums, *tok_sides = call(
        functools.partial(conv_kernel, sizes),
        [arr(11, 12, 8, WIDE), arr(9, 10, 8, WIDE), arr(PLANE, 8, WIDE), arr(8, WIDE)] + SIDES,
        [
            pltpu.VMEM((9, 10, 8, WIDE), F32),
            pltpu.VMEM((880, 2304), BF16),
            pltpu.VMEM((576, 2304), BF16),
            pltpu.VMEM((PLANE, 8, WIDE), F32),
        ],
        lines, *sides, labels, valid, weights0, weights1, vectors,
        name="conv", us=8.0, mib=20,
    )
    tok_sides = beside(tok_sides, sizes)
    side_act, side_grown = call(
        functools.partial(sides_back_kernel, sizes),
        [jax.ShapeDtypeStruct((640, 2304), BF16)] * 2,
        [pltpu.VMEM((10, 10, 8, WIDE), F32)],
        grown, pre,
        name="sides_back", us=2.0,
    )
    weights0, weights1 = call(
        weights_back_kernel,
        [taps_shape] * 2,
        [],
        conv0, conv1,
        name="weights_back", us=1.5,
    )
    sums = exchanged_sum(sums, count)
    voxels = WIN * slabs * WIN * rows * WIN
    tok3, slope, tail, d_head, d_rows = call(
        functools.partial(head_kernel, sizes, voxels),
        [arr(11, 12, 8, WIDE), arr(11, 12, 8, WIDE), arr(8, WIDE), arr(WIDE, WIDE), arr(8, WIDE)],
        [],
        tok3, *tok_sides, sums, vectors, head_w,
        name="head", us=3.5,
    )
    tail = exchanged_sum(tail, count)
    late_rows = block_rows(LATE_ROWS, count) * count
    early_rows = block_rows(EARLY_ROWS, count) * count
    seam_rows = LATE_ROWS - 3 * CUTS[3]
    d_own, keep, send, carry3, seam = call(
        functools.partial(conv_back_kernel, sizes),
        [arr(PLANE, 8, WIDE)] + [arr(early_rows // 2, WIDE)] * 2
        + [arr(24, WIDE), arr(seam_rows, WIDE)],
        [
            pltpu.VMEM((5236, WIDE), F32),
            pltpu.VMEM((11, 12, 8, WIDE), F32),
            pltpu.VMEM((10, 10, 8, WIDE), F32),
            pltpu.VMEM((880, 2304), BF16),
            pltpu.VMEM((576, 2304), BF16),
            pltpu.VMEM((seam_rows + early_rows, WIDE), F32),
        ],
        tok3, slope, tail, pre, side_act, side_grown, weights0, weights1, d_rows, d_head,
        name="conv_back", us=14.0, mib=28,
    )
    early = summing(keep, send, count)
    next(early)
    d_mid2, grads2 = call(
        back_mlp_kernel,
        [SQUARE, arr(1168, WIDE)],
        [pltpu.VMEM((ROWS, WIDE), F32)],
        d_own, lay2, mid2, hpre2,
        name="back_mlp", us=3.0,
    )
    step = early.send(d_mid2)
    d_mid, grads1, flat2, carry2, *parts = call(
        back_two_kernel,
        [SQUARE, arr(1168, WIDE), arr(3 * (CUTS[3] - CUTS[2]), WIDE), arr(32, WIDE)] + PARTS,
        [pltpu.VMEM((1184, WIDE), F32)] + BACKWARD,
        d_mid2, grads2, carry3, lay1, lay2, tok2, save2, lse2, mixed2, mid1, hpre1,
        name="back_two", us=9.0,
    )
    parts = passed(parts, -1, sizes)
    step = early.send(d_mid)
    d_window, flat1, carry1, *parts = call(
        functools.partial(back_shifted_kernel, sizes),
        [SQUARE, arr(3 * (CUTS[2] - CUTS[1]), WIDE), arr(16, WIDE)] + PARTS,
        REGION + [pltpu.VMEM((1200, WIDE), F32), pltpu.VMEM((ROWS, WIDE), F32)] + BACKWARD,
        d_mid, *parts, lay1, window, save1, lse1, mixed1, grads1, carry2,
        name="back_shifted", us=10.5, far=(step,),
    )
    early.send(d_window)
    parts = passed(parts, 1, sizes)
    next(early)
    step = next(early)
    late = call(
        functools.partial(back_first_kernel, sizes),
        [arr(late_rows // 2, WIDE)] * 2,
        [
            pltpu.VMEM((late_rows, WIDE), F32),
            pltpu.VMEM((1572, WIDE), F32),
            pltpu.VMEM((ROWS, WIDE), F32),
        ]
        + BACKWARD,
        d_mid, d_window, *parts, tok1, lay0, lay1, merge, dense, tok0, save0, lse0, mixed0, mid0,
        hpre0, carry1, flat1, flat2, seam,
        name="back_first", us=13.5, far=(step,),
    )
    step = early.send(late[0])
    keep, send = later(list(late), step)
    late_sum = finished(summing(keep, send, count))
    early = finished(early)
    early = call(
        functools.partial(place_early_kernel, sizes),
        [arr(EARLY_ROWS, WIDE), arr(8, WIDE)],
        [],
        *early,
        name="place_early", us=0.6,
    )
    new_params, new_first, new_second, loss, valid_count, norm = adamw(
        sizes, (*late_sum, *early, tail, sums), (params, moment_one, moment_two)
    )
    return (
        loss.reshape(()), valid_count.reshape(()), norm.reshape(()),
        new_params, new_first, new_second,
    )


def solution(mesh):
    placed = (
        P("slab", "mp", None, None),
        P("slab", "mp", None),
        P("slab", "mp", None),
        P(),
        P(),
        P(),
    )
    sizes = (mesh.shape["slab"], mesh.shape["mp"])
    return jax.shard_map(
        functools.partial(on_device, sizes),
        mesh=mesh,
        in_specs=placed,
        out_specs=(P(), P(), P(), P(), P(), P()),
        check_vma=False,
    )
```

```python
import functools

import jax
import jax.numpy as jnp
from jax import lax
from jax.experimental import pallas as pl
from jax.experimental.pallas import tpu as pltpu
from jax.sharding import PartitionSpec as P

EMB = 96
HEADS = 6
HDIM = 16
HID = 384
MERGE = 384
CLASSES = 14
WIN = 7
SHIFT = 3
LAYERS = 3
STEP = 10

F32 = jnp.float32
BF16 = jnp.bfloat16
eps_norm = 1e-05
beta_one = 0.9
beta_two = 0.999
adam_eps = 1e-08
learn_rate = 0.05
decay_rate = 0.05
clip_norm = 0.01
LOG2E = 1.4426950408889634

VOX = WIN * WIN * WIN
ROWS = 352
KEYS = 384
BLOCKS = ((0, 128), (128, 256), (256, 352))
WIDE = 128
PLANE = WIN * WIN
FAR = WIN - SHIFT
ROWS_A = SHIFT * FAR * WIN
ROWS_B = FAR * SHIFT * WIN
ROWS_C = SHIFT * SHIFT * WIN

MERGE_ROWS = 392
LAYER_ROWS = 1165
TAP_ROWS = 27 * EMB
GROUPS = 2280
NPARAM = 872558
HEAD_ROW = 6806
HEAD_ROWS = 11
HEAD_LANE = 32
LATE_ROWS = 3072
EARLY_ROWS = 3840
LAYER_BASE = (98, 389, 680)
CONV_BASE = (971, 1620)
CUTS = (0, 392, 688, 976, 2280)

R_QKV, R_QKVB, R_PROJ, R_PROJB = 4, 292, 295, 391
R_HID, R_HIDB, R_OUT, R_OUTB = 392, 776, 780, 1164


def iota(shape, dim):
    return lax.broadcasted_iota(jnp.int32, shape, dim)


def split(x):
    hi = x.astype(BF16)
    return hi, (x - hi.astype(F32)).astype(BF16)


def pair(x):
    return jnp.concatenate(split(x), 1)


def fold(y):
    half = y.shape[1] // 2
    return y[:, :half] + y[:, half:]


def fold_rows(y):
    half = y.shape[0] // 2
    return y[:half] + y[half:]


def dot(a, b):
    return jnp.dot(a, b, preferred_element_type=F32)


def dot_nt(a, b):
    return lax.dot_general(a, b, (((1,), (1,)), ((), ())), preferred_element_type=F32)


def weight_nn(w):
    top = pair(w)
    return jnp.concatenate([top, top], 0)


def weight_nt(w):
    hi, lo = split(w)
    return jnp.concatenate(
        [jnp.concatenate([hi, hi], 1), jnp.concatenate([lo, lo], 1)], 0
    )


def mm(x, w):
    return fold(dot(pair(x), weight_nn(w)))


def mm_nt(x, w):
    return fold(dot_nt(pair(x), weight_nt(w)))


def with_rows(x, rows):
    if x.shape[0] == rows:
        return x
    return jnp.concatenate([x, jnp.zeros((rows - x.shape[0], x.shape[1]), F32)], 0)


def rows_t(x):
    return jnp.concatenate(split(with_rows(x, -(-x.shape[0] // WIDE) * WIDE).T), 0)


def mm_tn(xt, y):
    return fold_rows(fold(dot(xt, pair(with_rows(y, xt.shape[1])))))


def deep(w):
    return jnp.concatenate([w, jnp.zeros((WIDE - EMB, w.shape[1]), F32)], 0)


def roll(x, shift, axis):
    return pltpu.roll(x, shift, axis)


def four_to_three(y):
    lane = iota(y[0].shape, 1)
    a = jnp.where(lane < 96, y[0], roll(y[1], 96, 1))
    b = jnp.where(lane < 64, roll(y[1], 96, 1), roll(y[2], 64, 1))
    c = jnp.where(lane < 32, roll(y[2], 64, 1), roll(y[3], 32, 1))
    return a, b, c


def three_to_four(x):
    lane = iota(x[0].shape, 1)
    live = lane < EMB
    a = x[0]
    b = jnp.where(lane < 32, roll(x[0], 32, 1), roll(x[1], 32, 1))
    c = jnp.where(lane < 64, roll(x[1], 64, 1), roll(x[2], 64, 1))
    d = roll(x[2], 96, 1)
    return tuple(jnp.where(live, v, 0.0) for v in (a, b, c, d))


def hidden_rows(ref, start, count):
    return jnp.concatenate(
        four_to_three([ref[pl.ds(start + c, count, stride=4), :] for c in range(4)]), 1
    )


def put_hidden_rows(ref, start, count, x):
    parts = three_to_four([x[:, i * WIDE : (i + 1) * WIDE] for i in range(3)])
    for c in range(4):
        ref[pl.ds(start + c, count, stride=4), :] = parts[c]


def flatten(ref, start, groups, out):
    parts = four_to_three([ref[pl.ds(start + c, groups, stride=4), :] for c in range(4)])
    for c in range(3):
        out[pl.ds(c, groups, stride=3), :] = parts[c]


def norm_stats(x):
    live = iota(x.shape, 1) < EMB
    mean = jnp.sum(x, 1, keepdims=True) * (1.0 / EMB)
    centred = jnp.where(live, x - mean, 0.0)
    var = jnp.sum(centred * centred, 1, keepdims=True) * (1.0 / EMB)
    inv = lax.rsqrt(var + eps_norm)
    return centred * inv, inv


def norm(x, gain, bias):
    hat, _ = norm_stats(x)
    return hat * gain + bias


def norm_back(hat, inv, gain, grad):
    up = grad * gain
    one = jnp.sum(up, 1, keepdims=True) * (1.0 / EMB)
    two = jnp.sum(up * hat, 1, keepdims=True) * (1.0 / EMB)
    live = iota(hat.shape, 1) < EMB
    return jnp.where(live, inv * (up - one - hat * two), 0.0)


def colsum(x):
    return jnp.sum(x, 0, keepdims=True)


def gelu(x):
    return 0.5 * x * (1.0 + lax.erf(x * (0.5**0.5)))


def gelu_both(x):
    cdf = 0.5 * (1.0 + lax.erf(x * (0.5**0.5)))
    slope = cdf + x * (jnp.exp(x * x * -0.5) * 0.3989422804014327)
    return x * cdf, slope


def head_groups(x):
    lane = iota(x.shape, 1)
    swapped = roll(x, 64, 1)
    return jnp.where(lane < 64, x, swapped), jnp.where(lane < 64, swapped, x)


def as_left(x):
    both = []
    low = iota(x.shape, 1) < 64
    for part in head_groups(x):
        hi = part.astype(BF16).astype(F32)
        one = jnp.where(low, hi, part - hi).astype(BF16)
        both.append(jnp.concatenate([one, one], 1))
    return both


def as_right(x):
    return [pair(part) for part in head_groups(with_rows(x, KEYS))]


def head_mask(h, width):
    lane = iota((1, width), 1)
    lane = jnp.bitwise_and(lane, 63)
    low = jnp.bitwise_and(h, 3) * HDIM
    return jnp.where((lane >= low) & (lane < low + HDIM), 1.0, 0.0)


def own_lanes(h):
    lane = iota((1, WIDE), 1)
    return jnp.where((lane >= h * HDIM) & (lane < (h + 1) * HDIM), 1.0, 0.0)


def both_heads(right, heads, out):
    for k, h in enumerate(heads):
        out[k * KEYS : (k + 1) * KEYS, :] = right * head_mask(h, 2 * WIDE).astype(BF16)


def score_tiles(s, rows, region):
    tiles = [s[:, i * WIDE : (i + 1) * WIDE] for i in range(3)]
    if region is not None:
        return [t + region[rows, i * WIDE : (i + 1) * WIDE] for i, t in enumerate(tiles)]
    pad = jnp.where(iota((1, WIDE), 1) < VOX - 2 * WIDE, 0.0, -1e30)
    return tiles[:2] + [tiles[2] + pad]


def put_split(ref, rows, i, x):
    hi, lo = split(x)
    ref[rows, i * WIDE : (i + 1) * WIDE] = hi
    ref[rows, KEYS + i * WIDE : KEYS + (i + 1) * WIDE] = lo


def attention(normed, layer, save, lse, mixed, sc, region=None):
    left, right, values = sc
    x = pair(normed)
    qkv = []
    for i in range(3):
        w = deep(layer[pl.ds(R_QKV + i, EMB, stride=3), :])
        y = fold(dot(x, weight_nn(w))) + layer[R_QKVB + i : R_QKVB + i + 1, :]
        if i == 0:
            y = y * (HDIM**-0.5 * LOG2E)
        save[:, i * WIDE : (i + 1) * WIDE] = y
        qkv.append(y)
    for g, part in enumerate(as_left(qkv[0])):
        left[g] = part
    for g, part in enumerate(as_right(qkv[1])):
        right[g] = part
    v = jnp.where(iota((ROWS, WIDE), 1) == EMB, 1.0, qkv[2])
    v = pair(with_rows(v, KEYS))
    values[0:KEYS, :] = v
    values[KEYS : 2 * KEYS, :] = v
    mixed[...] = jnp.zeros_like(mixed)
    lse[...] = jnp.zeros_like(lse)

    def per_pair(pair_of, carry):
        heads = [2 * pair_of, 2 * pair_of + 1]
        masks = [head_mask(h, 2 * WIDE).astype(BF16) for h in heads]
        lanes = [own_lanes(h) for h in heads]
        spots = [jnp.where(iota((1, WIDE), 1) == h, 1.0, 0.0) for h in heads]
        g = lax.div(pair_of, 2)
        for block in BLOCKS:
            rows = slice(*block)
            out = level = 0.0
            for k in range(2):
                s = dot_nt(left[g, rows, :] * masks[k], right[g])
                tiles = score_tiles(s, rows, region)
                top = jnp.maximum(jnp.maximum(tiles[0], tiles[1]), tiles[2])
                top = jnp.max(top, 1, keepdims=True)
                parts = [split(jnp.exp2(t - top)) for t in tiles]
                e = jnp.concatenate([p[0] for p in parts] + [p[1] for p in parts], 1)
                o = fold(dot(e, values[...]))
                total = o[:, EMB : EMB + 1]
                out = out + o * (lanes[k] / total)
                level = level + (top + jnp.log(total) * LOG2E) * spots[k]
            mixed[rows, :] += out
            lse[rows, :] += level
        return carry

    lax.fori_loop(0, HEADS // 2, per_pair, 0)
    proj = deep(layer[R_PROJ : R_PROJ + EMB, :])
    return mm(mixed[...], proj) + layer[R_PROJB : R_PROJB + 1, :]


def attention_back(grad, normed, layer, save, lse, mixed, sc, grads, at, region=None):
    left, right, gleft, vright, keys, dq, dkv_t, weights, slopes = sc[:9]
    q_t, do_t, dmix, s, dp, two_keys, two_values = sc[9:]
    proj = deep(layer[R_PROJ : R_PROJ + EMB, :])
    grads[at + R_PROJ : at + R_PROJ + EMB, :] = mm_tn(rows_t(mixed[...]), grad)[:EMB]
    grads[at + R_PROJB : at + R_PROJB + 1, :] = colsum(grad)
    d_mixed = mm_nt(grad, proj)
    dmix[...] = d_mixed * mixed[...]
    q, k, v = (save[:, i * WIDE : (i + 1) * WIDE] for i in range(3))
    for g, part in enumerate(as_left(q)):
        left[g] = part
    for g, part in enumerate(as_right(k)):
        right[g] = part
    for g, part in enumerate(as_left(d_mixed)):
        gleft[g] = part
    for g, part in enumerate(as_right(v)):
        vright[g] = part
    kk = pair(with_rows(k, KEYS))
    keys[0:KEYS, :] = kk
    keys[KEYS : 2 * KEYS, :] = kk
    weights[:, ROWS:, :] = jnp.zeros((2, KEYS - ROWS, 2 * KEYS), BF16)
    slopes[:, ROWS:, :] = jnp.zeros((2, KEYS - ROWS, 2 * KEYS), BF16)
    for ref, x in ((q_t, q), (do_t, d_mixed)):
        hi, lo = split(with_rows(x, KEYS).T)
        ref[0] = hi
        ref[1] = lo
    dq[...] = jnp.zeros_like(dq)
    dkv_t[...] = jnp.zeros_like(dkv_t)

    def per_pair(pair_of, carry):
        g = lax.div(pair_of, 2)
        heads = [2 * pair_of, 2 * pair_of + 1]
        both_heads(right[g], heads, two_keys)
        both_heads(vright[g], heads, two_values)
        s[...] = dot_nt(left[g], two_keys[...])
        dp[...] = dot_nt(gleft[g], two_values[...])
        for k in range(2):
            h = 2 * pair_of + k
            lanes = own_lanes(h)
            at_h = jnp.where(iota((1, WIDE), 1) == h, 1.0, 0.0)
            for block in BLOCKS:
                rows = slice(*block)
                level = jnp.sum(lse[rows, :] * at_h, 1, keepdims=True)
                delta = jnp.sum(dmix[rows, :] * lanes, 1, keepdims=True)
                at_k = k * KEYS
                tiles = score_tiles(s[rows, at_k : at_k + KEYS], rows, region)
                for i, t in enumerate(tiles):
                    p = jnp.exp2(t - level)
                    put_split(weights.at[k], rows, i, p)
                    low = at_k + i * WIDE
                    p = p * (dp[rows, low : low + WIDE] - delta)
                    put_split(slopes.at[k], rows, i, p)
        total = 0.0
        for k in range(2):
            out = fold(dot(slopes[k, 0:ROWS, :], keys[...]))
            total = total + out * own_lanes(2 * pair_of + k)
        dq[...] += total
        for k in range(2):
            here = pl.ds(pl.multiple_of((2 * pair_of + k) * HDIM, HDIM), HDIM)
            for i, (t, m) in enumerate(((q_t, slopes), (do_t, weights))):
                lhs = jnp.concatenate([t[0, here, :], t[1, here, :]], 0)
                dkv_t[i, here, :] = fold_rows(fold(dot(lhs, m[k])))
        return carry

    lax.fori_loop(0, HEADS // 2, per_pair, 0)
    d_q = dq[...] * HDIM**-0.5
    d_k = dkv_t[0].T[0:ROWS] * (1.0 / LOG2E)
    d_v = dkv_t[1].T[0:ROWS]
    x_t = rows_t(normed)
    d_normed = None
    for i, d in enumerate((d_q, d_k, d_v)):
        grads[pl.ds(at + R_QKV + i, EMB, stride=3), :] = mm_tn(x_t, d)[:EMB]
        grads[at + R_QKVB + i : at + R_QKVB + i + 1, :] = colsum(d)
        part = mm_nt(d, deep(layer[pl.ds(R_QKV + i, EMB, stride=3), :]))
        d_normed = part if d_normed is None else d_normed + part
    return d_normed


def mlp(middle, layer, hpre):
    normed = norm(middle, layer[2:3, :], layer[3:4, :])
    w = deep(hidden_rows(layer, R_HID, EMB))
    pre = mm(normed, w) + hidden_rows(layer, R_HIDB, 1)
    hpre[...] = pre
    out = mm(gelu(pre), layer[R_OUT : R_OUT + HID, :])
    return middle + out + layer[R_OUTB : R_OUTB + 1, :]


def mlp_back(grad, middle, hpre, layer, grads, at):
    hat, inv = norm_stats(middle)
    normed = hat * layer[2:3, :] + layer[3:4, :]
    act, slope = gelu_both(hpre[...])
    grads[at + R_OUTB : at + R_OUTB + 1, :] = colsum(grad)
    grads[at + R_OUT : at + R_OUT + HID, :] = mm_tn(rows_t(grad), act).T
    d_pre = mm_nt(grad, layer[R_OUT : R_OUT + HID, :]) * slope
    put_hidden_rows(grads, at + R_HIDB, 1, colsum(d_pre))
    put_hidden_rows(grads, at + R_HID, EMB, mm_tn(rows_t(normed), d_pre)[:EMB])
    d_normed = mm_nt(d_pre, deep(hidden_rows(layer, R_HID, EMB)))
    grads[at + 2 : at + 3, :] = colsum(d_normed * hat)
    grads[at + 3 : at + 4, :] = colsum(d_normed)
    return grad + norm_back(hat, inv, layer[2:3, :], d_normed)


def pre_norm_back(grad, tokens, layer, grads, at):
    hat, inv = norm_stats(tokens)
    grads[at : at + 1, :] = colsum(grad * hat)
    grads[at + 1 : at + 2, :] = colsum(grad)
    return norm_back(hat, inv, layer[0:1, :], grad)


def region_of(rows, sizes):
    d = lax.shift_right_logical(rows * 1338, 16)
    line = lax.shift_right_logical(rows * 9363, 16)
    places = (d, line - d * WIN, rows - line * WIN)
    starts = (lax.axis_index("slab") * WIN, lax.axis_index("mp") * WIN, 0)
    total = None
    for place, start, blocks in zip(places, starts, sizes + (1,)):
        turned = jnp.where(place < SHIFT, place + FAR, place - SHIFT) + start
        length = WIN * blocks
        part = jnp.where(turned < length - WIN, 0, jnp.where(turned < length - SHIFT, 1, 2))
        total = part if total is None else total * 3 + part
    return total


def put_region(region, sizes):
    rows = region_of(iota((ROWS, WIDE), 0), sizes)[:, 0:1]
    lanes = region_of(iota((8, KEYS), 1), sizes)[0:1, :]
    apart = jnp.where(rows == lanes, 0.0, -100.0 * LOG2E)
    region[...] = jnp.where(iota((ROWS, KEYS), 1) < VOX, apart, -1e30)


def send_parts(ref, a, b, c):
    far = FAR * WIN
    near = SHIFT * WIN
    for d in range(SHIFT):
        base = d * PLANE
        c[d * near : (d + 1) * near, :] = ref[base : base + near, :]
        a[d * far : (d + 1) * far, :] = ref[base + near : base + PLANE, :]
    for d in range(FAR):
        base = (d + SHIFT) * PLANE
        b[d * near : (d + 1) * near, :] = ref[base : base + near, :]


def take_parts(own, a, b, c, out):
    far = FAR * WIN
    near = SHIFT * WIN
    for d in range(WIN):
        base = d * PLANE
        if d < SHIFT:
            out[base : base + near, :] = c[d * near : (d + 1) * near, :]
            out[base + near : base + PLANE, :] = a[d * far : (d + 1) * far, :]
        else:
            e = d - SHIFT
            out[base : base + near, :] = b[e * near : (e + 1) * near, :]
            out[base + near : base + PLANE, :] = own[base + near : base + PLANE, :]
    out[VOX:, :] = jnp.zeros((ROWS - VOX, WIDE), F32)


def span_of(groups):
    low, high = groups
    first = 3 * low // 8 * 8
    last = -(-3 * high // 8) * 8
    return first, min(last, NPARAM // WIDE // 8 * 8) - first


def copied(params, groups, flat, sem):
    first, rows = span_of(groups)
    size = rows * WIDE
    return pltpu.make_async_copy(
        params.at[pl.ds(first * WIDE, size)], flat.at[pl.ds(0, size)], sem
    )


def relay(groups, flat, out, square, last=None):
    low, high = groups
    first, rows = span_of(groups)
    square[0:rows, :] = flat[0 : rows * WIDE].reshape(rows, WIDE)
    if last is not None:
        square[rows : rows + 24, :] = jnp.zeros((24, WIDE), F32)
        square[rows : rows + 1, 0 : last.shape[0]] = last[...].reshape(1, last.shape[0])
    skip = 3 * low - first
    n = high - low
    parts = three_to_four([square[pl.ds(skip + c, n, stride=3), :] for c in range(3)])
    for c in range(4):
        out[pl.ds(c, n, stride=4), :] = parts[c]


FIRST_SPANS = ((0, 98), (98, 392))
LAYER_SPANS = ((389, 681), (680, 972))
CONV_SPANS = ((971, 1620), (1620, GROUPS))


def prep_kernel(spans, params, *refs, last=None):
    outs, (flats, square, sems) = refs[: len(spans)], refs[-3:]
    for i, groups in enumerate(spans):
        copied(params, groups, flats[i], sems.at[i]).start()
    for i, groups in enumerate(spans):
        copied(params, groups, flats[i], sems.at[i]).wait()
        relay(groups, flats[i], outs[i], square, last if i == len(spans) - 1 else None)


def head_picks():
    width = HEAD_ROWS * WIDE
    place = iota((WIDE, width), 1) - HEAD_LANE
    row = iota((WIDE, width), 0)
    here = (place >= row * CLASSES) & (place < (row + 1) * CLASSES) & (row <= EMB)
    place = iota((width, WIDE), 0) - HEAD_LANE
    col = iota((width, WIDE), 1)
    row = lax.shift_right_logical(place * 4682, 16)
    there = (place - row * CLASSES == col) & (place >= 0)
    return jnp.where(here, 1.0, 0.0), jnp.where(there, 1.0, 0.0).astype(BF16)


def prep_conv0_kernel(params, conv0, weights0, bias, *scratch):
    prep_kernel(CONV_SPANS[:1], params, conv0, *scratch)
    tap_weights(conv0, 3, weights0)
    bias[0:1, :] = conv0[3 + TAP_ROWS : 4 + TAP_ROWS, :]
    bias[1:8, :] = jnp.zeros((7, WIDE), F32)


def prep_conv1_kernel(last, bias, params, conv1, head, weights1, vectors, *scratch):
    prep_kernel(CONV_SPANS[1:], params, conv1, *scratch, last=last)
    tap_weights(conv1, 0, weights1)
    vectors[0:1, :] = bias[0:1, :]
    vectors[1:4, :] = conv1[TAP_ROWS : TAP_ROWS + 3, :]
    vectors[4:8, :] = jnp.zeros((4, WIDE), F32)
    square = scratch[1]
    first, _ = span_of(CONV_SPANS[1])
    row = jnp.concatenate(
        [square[HEAD_ROW + i - first : HEAD_ROW + i - first + 1, :] for i in range(HEAD_ROWS)], 1
    )
    here, there = head_picks()
    hi, lo = split(here * row)
    head[...] = dot(hi, there) + dot(lo, there)


def head_rows(d_head, out, at):
    here, there = head_picks()
    hi, lo = split(d_head)
    spread = (dot_nt(hi, there) + dot_nt(lo, there)) * here
    row = colsum(spread)
    for i in range(HEAD_ROWS):
        out[at + i : at + i + 1, :] += row[:, i * WIDE : (i + 1) * WIDE]


class Rows:
    def __init__(self, ref, at):
        self.ref, self.at = ref, at

    def __getitem__(self, key):
        rows, lanes = key
        if isinstance(rows, slice):
            rows = slice(rows.start + self.at, rows.stop + self.at)
        else:
            rows = pl.ds(rows.start + self.at, rows.size, stride=rows.stride)
        return self.ref[rows, lanes]


def merged_norm(x):
    mean = jnp.sum(x, 1, keepdims=True) * (1.0 / MERGE)
    centred = x - mean
    var = jnp.sum(centred * centred, 1, keepdims=True) * (1.0 / MERGE)
    return centred * lax.rsqrt(var + eps_norm)


def first_kernel(
    feats, merge, lay0,
    dense, tok0, save, lse, mixed, middle, hpre, tok1, ahead, pa, pb, pc,
    *sc,
):
    dense[VOX:, :] = jnp.zeros((ROWS - VOX, MERGE), F32)
    for line in range(PLANE):
        dense[line * WIN : (line + 1) * WIN, :] = feats[line]
    hat = merged_norm(dense[...])
    normed = hat * hidden_rows(merge, 0, 1) + hidden_rows(merge, 4, 1)
    tokens = mm(normed, merge[8 : 8 + MERGE, :])
    tok0[...] = tokens
    layer = Rows(lay0, 0)
    normed = norm(tokens, layer[0:1, :], layer[1:2, :])
    attended = attention(normed, layer, save, lse, mixed, sc)
    mid = tokens + attended
    middle[...] = mid
    tokens = mlp(mid, layer, hpre)
    tok1[...] = tokens
    ahead[...] = norm(tokens, layer[1165:1166, :], layer[1166:1167, :])
    send_parts(ahead, pa, pb, pc)


def shifted_kernel(
    sizes,
    own, pa, pb, pc, lay1, _,
    window, save, lse, mixed, out, qa, qb, qc,
    region, *sc,
):
    put_region(region, sizes)
    take_parts(own, pa, pb, pc, window)
    out[...] = attention(
        window[...], Rows(lay1, 1), save, lse, mixed, sc, region
    )
    send_parts(out, qa, qb, qc)


def to_lines(ref, out):
    for line in range(PLANE):
        out[line, 0:WIN, :] = ref[line * WIN : (line + 1) * WIN, :]
        out[line, WIN:8, :] = jnp.zeros((8 - WIN, WIDE), F32)


def from_lines(ref, out):
    out[VOX:, :] = jnp.zeros((ROWS - VOX, WIDE), F32)
    for line in range(PLANE):
        out[line * WIN : (line + 1) * WIN, :] = ref[line, 0:WIN, :]


def send_sides(lines, near_d, far_d, near_h, far_h):
    odd_d = jnp.bitwise_and(lax.axis_index("slab"), 1) == 1
    odd_h = jnp.bitwise_and(lax.axis_index("mp"), 1) == 1
    low, high = lines[0 : 2 * WIN], lines[(WIN - 2) * WIN : PLANE]
    near_d[...] = jnp.where(odd_d, low, high)
    far_d[...] = jnp.where(odd_d, high, low)
    for d in range(WIN):
        low = lines[d * WIN : d * WIN + 2]
        high = lines[d * WIN + WIN - 2 : (d + 1) * WIN]
        near_h[2 * d : 2 * d + 2] = jnp.where(odd_h, low, high)
        far_h[2 * d : 2 * d + 2] = jnp.where(odd_h, high, low)


def second_kernel(
    tok1, own, qa, qb, qc, lay1, lay2, _,
    mid1, hpre1, tok2, save, lse, mixed, mid2, hpre2, lines,
    s0, s1, s2, s3,
    attended, *sc,
):
    take_parts(own, qa, qb, qc, attended)
    mid = tok1[...] + attended[...]
    mid1[...] = mid
    tokens = mlp(mid, Rows(lay1, 1), hpre1)
    tok2[...] = tokens
    layer = Rows(lay2, 2)
    normed = norm(tokens, layer[0:1, :], layer[1:2, :])
    mid = tokens + attention(normed, layer, save, lse, mixed, sc)
    mid2[...] = mid
    attended[...] = mlp(mid, layer, hpre2)
    to_lines(attended, lines)
    send_sides(lines, s0, s1, s2, s3)


def grown_lines(sizes, own, near_d, far_d, near_h, far_h, out):
    slab, row = lax.axis_index("slab"), lax.axis_index("mp")
    odd_d = jnp.bitwise_and(slab, 1) == 1
    odd_h = jnp.bitwise_and(row, 1) == 1
    out[:, 11:12] = jnp.zeros((11, 1, 8, WIDE), F32)
    for d in range(WIN):
        out[d + 2, 2 : 2 + WIN] = own[d * WIN : (d + 1) * WIN]
    for d in range(2):
        near = near_d[d * WIN : (d + 1) * WIN]
        far = far_d[d * WIN : (d + 1) * WIN]
        out[d, 2 : 2 + WIN] = jnp.where(odd_d, near, jnp.where(slab == 0, 0.0, far))
        out[d + 9, 2 : 2 + WIN] = jnp.where(
            odd_d, jnp.where(slab == sizes[0] - 1, 0.0, far), near
        )
    for d in range(11):
        near = near_h[2 * d : 2 * d + 2]
        far = far_h[2 * d : 2 * d + 2]
        out[d, 0:2] = jnp.where(odd_h, near, jnp.where(row == 0, 0.0, far))
        out[d, 9:11] = jnp.where(odd_h, jnp.where(row == sizes[1] - 1, 0.0, far), near)


def put_marks(labels, valid, out):
    across = iota((8, WIN), 1) == iota((8, WIN), 0)
    classes = iota((8, WIDE), 1) - EMB
    for d in range(WIN):
        code = jnp.where(valid[d] == 1, labels[d], -1 - EMB - WIDE)
        code = code.astype(F32)
        for h in range(WIN):
            line = jnp.where(across, code[h : h + 1, :], 0.0)
            column = jnp.sum(line, 1, keepdims=True)
            mark = jnp.where(column == classes.astype(F32), 1.0, 0.0)
            out[d * WIN + h] = jnp.where(iota((8, WIDE), 0) < WIN, mark, 0.0)


def taps(source, first_plane, planes, first_line, lines, out):
    def per_plane(d, carry):
        for c in range(3):
            for b in range(3):
                x = source[d + first_plane, first_line + b : first_line + b + lines]
                if c != 1:
                    x = roll(x, 1 if c == 0 else 7, 1)
                x = pair(x.reshape(lines * 8, WIDE))
                at = pl.multiple_of(d * (lines * 8), lines * 8)
                t = b * 3 + c
                out[pl.ds(at, lines * 8), t * 256 : (t + 1) * 256] = x
        return carry

    lax.fori_loop(0, planes, per_plane, 0)


def tap_weights(ref, at, out):
    def per_tap(i, carry):
        w = deep(ref[pl.ds(i * EMB + at, EMB), :])
        out[pl.ds(pl.multiple_of(i * 256, 256), 256), :] = weight_nn(w)
        return carry

    lax.fori_loop(0, 27, per_tap, 0)


def tap_weights_back(ref, at, out):
    for i in range(27):
        w = deep(ref[(26 - i) * EMB + at : (27 - i) * EMB + at, :])
        out[:, i * 256 : (i + 1) * 256] = weight_nt(w)


def conv(side, weights, planes, pitch, at_once, put, back=False):
    rows = at_once * pitch
    for start in range(0, planes, at_once):
        total = None
        for a in range(3):
            low = (start + a) * pitch
            x = side[low : low + rows, :]
            if back:
                part = dot_nt(x, weights[:, a * 2304 : (a + 1) * 2304])
            else:
                part = dot(x, weights[a * 2304 : (a + 1) * 2304, :])
            total = part if total is None else total + part
        put(start, fold(total))


def conv_weight_grad(side, grad_rows, pitch, out, at):
    rows = 512
    g = jnp.concatenate([grad_rows, jnp.zeros((rows - grad_rows.shape[0], WIDE), F32)], 0)
    left = jnp.concatenate(split(g.T[:EMB]), 0)
    for a in range(3):
        for bc in range(9):
            y = dot(left, side[a * pitch : a * pitch + rows, bc * 256 : (bc + 1) * 256])
            y = deep(fold_rows(fold(y))).T
            t = a * 9 + bc
            out[at + t * EMB : at + (t + 1) * EMB, :] = y[:EMB]


def volume_mask(sizes, planes, lines, reach, real_lines):
    slab, row = lax.axis_index("slab"), lax.axis_index("mp")
    ends = (slab == 0, slab == sizes[0] - 1, row == 0, row == sizes[1] - 1)
    shape = (planes, lines, 8, WIDE)
    d, h, w = iota(shape, 0), iota(shape, 1), iota(shape, 2)
    low_d = jnp.where(ends[0], reach, 0)
    high_d = jnp.where(ends[1], planes - reach, planes)
    low_h = jnp.where(ends[2], reach, 0)
    high_h = jnp.where(ends[3], real_lines - reach, real_lines)
    inside = (d >= low_d) & (d < high_d) & (h >= low_h) & (h < high_h) & (w < WIN)
    return jnp.where(inside, 1.0, 0.0)


def conv_kernel(
    sizes,
    own, s0, s1, s2, s3, labels, valid, weights0, weights1, vectors,
    grown, pre, tok, stats, t0, t1, t2, t3,
    act, side, side_own, marks,
):
    grown_lines(sizes, own, s0, s1, s2, s3, grown)
    put_marks(labels, valid, marks)
    taps(grown, 0, 11, 0, 10, side)
    bias0 = vectors[0:1, :]
    inside = volume_mask(sizes, 9, 10, 1, 9)


    def put(start, y):
        z = (y + bias0).reshape(3, 10, 8, WIDE)
        pre[start : start + 3] = z
        act[start : start + 3] = gelu(z) * inside[start : start + 3]

    conv(side, weights0, 9, 80, 3, put)
    taps(act, 0, 9, 0, 8, side_own)
    bias1 = vectors[1:2, :]
    sums = []

    def put_own(start, y):
        y = (y + bias1).reshape(WIN, 8, 8, WIDE)[:, 0:WIN]
        y = y + own[...].reshape(WIN, WIN, 8, WIDE)
        y = jnp.where(iota(y.shape, 2) < WIN, y, 0.0).reshape(PLANE, 8, WIDE)
        tok[...] = y + marks[...]
        send_sides(tok, t0, t1, t2, t3)
        flat = y.reshape(PLANE * 8, WIDE)
        sums.append(colsum(flat))
        sums.append(colsum(flat * flat))

    conv(side_own, weights1, WIN, 64, WIN, put_own)
    count = jnp.sum(marks[...].reshape(PLANE * 8, WIDE))
    row = iota((8, WIDE), 0)
    stats[...] = (
        jnp.where(row == 0, sums[0], 0.0)
        + jnp.where(row == 1, sums[1], 0.0)
        + jnp.where(row == 2, count, 0.0)
    )


def head_kernel(
    sizes, voxels,
    own, s0, s1, s2, s3, sums, vectors, head_w,
    grown, slope_out, stats, d_head, d_rows,
):
    grown_lines(sizes, own, s0, s1, s2, s3, grown)
    rows = 11 * 12 * 8
    both = grown[...].reshape(rows, WIDE)
    lane = iota((rows, WIDE), 1)
    tokens = jnp.where(lane < EMB, both, 0.0)
    target = jnp.where(lane < CLASSES, roll(both, WIDE - EMB, 1), 0.0)
    live = jnp.sum(target, 1, keepdims=True)
    count = F32(voxels)
    average = sums[0:1, :] / count
    spread = sums[1:2, :] / count - average * average
    inv = lax.rsqrt(spread + eps_norm)
    gain = vectors[2:3, :]
    bias = vectors[3:4, :]
    hat = (tokens - average) * inv
    act, slope = gelu_both(hat * gain + bias)
    act = jnp.where(lane == EMB, 1.0, act)
    w = head_w[...]
    logits = mm(act, w)
    logits = jnp.where(lane < CLASSES, logits, -1e30)
    top = jnp.max(logits, 1, keepdims=True)
    e = jnp.exp(logits - top)
    total = jnp.sum(e, 1, keepdims=True)
    logp = logits - top - jnp.log(total)
    scale = 1.0 / sums[2:3, 0:1]
    d_logits = (e / total * live - target) * scale
    d_normed = jnp.where(lane < EMB, mm_nt(d_logits, w) * slope, 0.0)
    d_tokens = d_normed * gain * inv
    slope_out[...] = d_tokens.reshape(11, 12, 8, WIDE)

    def own_rows(x):
        x = x.reshape(11, 12, 8, WIDE)[2:9, 2:9]
        x = jnp.where(iota(x.shape, 2) < WIN, x, 0.0)
        return x.reshape(PLANE * 8, WIDE)

    loss = -jnp.sum(own_rows(target * jnp.where(lane < CLASSES, logp, 0.0)))
    own_d = own_rows(d_logits)
    own_n = own_rows(d_normed)
    own_hat = own_rows(hat)
    zeros = jnp.zeros((512 - PLANE * 8, WIDE), F32)
    left = rows_t(jnp.concatenate([own_d, zeros], 0))
    d_head[...] = mm_tn(left, jnp.concatenate([own_rows(act), zeros], 0)).T
    d_gain = colsum(own_n * own_hat)
    d_bias = colsum(own_n)
    d_average = -d_bias * gain * inv
    d_spread = d_gain * gain * inv * inv * -0.5
    d_two = d_spread / count
    d_one = (d_average - 2.0 * average * d_spread) / count
    row = iota((8, WIDE), 0)
    live_lane = iota((8, WIDE), 1) < EMB
    stats[...] = (
        jnp.where((row == 0) & live_lane, d_one, 0.0)
        + jnp.where((row == 1) & live_lane, d_two, 0.0)
        + jnp.where(row == 2, loss, 0.0)
    )
    d_rows[...] = (
        jnp.where(row == 0, d_gain, 0.0)
        + jnp.where(row == 1, d_bias, 0.0)
    )


def sides_back_kernel(sizes, grown, pre, side_act, side_grown, act):
    act[0:9] = gelu(pre[...]) * volume_mask(sizes, 9, 10, 1, 9)
    act[9:10] = jnp.zeros((1, 10, 8, WIDE), F32)
    taps(act, 0, 10, 0, 8, side_act)
    taps(grown, 1, 10, 1, 8, side_grown)


def weights_back_kernel(conv0, conv1, weights0, weights1):
    tap_weights_back(conv0, 3, weights0)
    tap_weights_back(conv1, 0, weights1)


def conv_back_kernel(
    sizes,
    tok, slope, sums, pre, side_act, side_grown, weights0, weights1, d_rows, d_head,
    d_own, keep, send, carry, seam,
    grads, dgrown, act, side, side_own, flat,
):
    lane = iota((11, 12, 8, WIDE), 3)
    inside = volume_mask(sizes, 11, 12, 2, 11)
    steady = sums[0:1, :].reshape(1, 1, 1, WIDE)
    rising = 2.0 * sums[1:2, :].reshape(1, 1, 1, WIDE)
    d_tok = slope[...] + jnp.where(lane < EMB, (steady + tok[...] * rising) * inside, 0.0)
    dgrown[...] = d_tok
    grads[5191:, :] = jnp.zeros((45, WIDE), F32)
    grads[0:8, :] = jnp.zeros((8, WIDE), F32)
    grads[5189:5191, :] = d_rows[0:2, :]
    own = dgrown[2:9, 2:10]
    line = iota(own.shape, 1)
    own = jnp.where(line < WIN, own, 0.0).reshape(WIN * 64, WIDE)
    grads[5188:5189, :] = colsum(own)

    near = volume_mask(sizes, 9, 10, 1, 9)
    conv_weight_grad(side_act, own, 64, grads, 2596)
    taps(dgrown, 0, 11, 0, 10, side)


    def put(start, y):
        _, s = gelu_both(pre[start : start + 3])
        act[start : start + 3] = y.reshape(3, 10, 8, WIDE) * s * near[start : start + 3]

    conv(side, weights1, 9, 80, 3, put, back=True)

    own = act[1:8, 1:9]
    line = iota(own.shape, 1)
    own = jnp.where(line < WIN, own, 0.0).reshape(WIN * 64, WIDE)
    grads[2595:2596, :] = colsum(own)
    conv_weight_grad(side_grown, own, 64, grads, 3)
    carry[...] = grads[0:24, :]
    flat[3 * (GROUPS - CUTS[3]) :, :] = jnp.zeros((flat.shape[0] - 3912, WIDE), F32)
    flatten(grads, 20, GROUPS - CUTS[3], flat)
    start = 3 * CUTS[3]
    head_rows(d_head[...], flat, HEAD_ROW - start)
    seam[...] = flat[0 : LATE_ROWS - start, :]
    scatter(sizes, flat, LATE_ROWS - start, keep, send)
    taps(act, 0, 9, 0, 8, side_own)

    def put_own(start, y):
        y = y.reshape(WIN, 8, 8, WIDE)[:, 0:WIN] + dgrown[2:9, 2:9]
        y = jnp.where(iota(y.shape, 2) < WIN, y, 0.0)
        d_own[...] = y.reshape(PLANE, 8, WIDE)

    conv(side_own, weights0, WIN, 64, WIN, put_own, back=True)


def back_mlp_kernel(d_own, lay2, mid2, hpre2, d_mid, grads, dense):
    from_lines(d_own, dense)
    grads[...] = jnp.zeros_like(grads)
    d_mid[...] = mlp_back(dense[...], mid2[...], hpre2, Rows(lay2, 2), grads, 2)


def back_two_kernel(
    d_mid2, grads2, carry, lay1, lay2, tok2, save, lse, mixed, mid1, hpre1,
    d_mid, grads1, flat, carry2, pa, pb, pc,
    grads, *sc,
):
    layer = Rows(lay2, 2)
    grads[0:1168, :] = grads2[...]
    d = d_mid2[...]
    tokens = tok2[...]
    normed = norm(tokens, layer[0:1, :], layer[1:2, :])
    d_normed = attention_back(d, normed, layer, save, lse, mixed, sc, grads, 2)
    d = d + pre_norm_back(d_normed, tokens, layer, grads, 2)
    grads[1167:1184, :] = carry[3:20, :]
    flatten(grads, 32, CUTS[3] - CUTS[2], flat)
    carry2[...] = grads[0:32, :]
    layer = Rows(lay1, 1)
    d = mlp_back(d, mid1[...], hpre1, layer, grads1, 1)
    d_mid[...] = d
    send_parts(d_mid, pa, pb, pc)


def back_shifted_kernel(
    sizes,
    own, pa, pb, pc, lay1, window, save, lse, mixed, grads1, carry2, _,
    d_window, flat, carry1, qa, qb, qc,
    region, grads, grad, *sc,
):
    put_region(region, sizes)
    take_parts(own, pa, pb, pc, grad)
    grads[0:1168, :] = grads1[...]
    grads[0:3, :] = jnp.zeros((3, WIDE), F32)
    d_window[...] = attention_back(
        grad[...], window[...], Rows(lay1, 1), save, lse, mixed, sc, grads, 1,
        region,
    )
    send_parts(d_window, qa, qb, qc)
    grads[1166:1196, :] = carry2[2:32, :]
    flatten(grads, 12, CUTS[2] - CUTS[1], flat)
    carry1[...] = grads[0:16, :]


def back_first_kernel(
    sizes,
    d_mid, own, qa, qb, qc, tok1, lay0, lay1, merge, dense, tok0, save, lse, mixed, middle, hpre,
    carry1, flat1, flat2, seam, _,
    keep, send,
    flat, grads, grad, *sc,
):
    take_parts(own, qa, qb, qc, grad)
    grads[1556:1572, :] = carry1[...]
    d = d_mid[...] + pre_norm_back(grad[...], tok1[...], Rows(lay1, 1), grads, 1557)
    layer = Rows(lay0, 0)
    at = MERGE_ROWS
    d = mlp_back(d, middle[...], hpre, layer, grads, at)
    tokens = tok0[...]
    normed = norm(tokens, layer[0:1, :], layer[1:2, :])
    d_normed = attention_back(d, normed, layer, save, lse, mixed, sc, grads, at)
    d = d + pre_norm_back(d_normed, tokens, layer, grads, at)
    live = iota((ROWS, WIDE), 0) < VOX
    d = jnp.where(live, d, 0.0)
    hat = merged_norm(dense[...])
    gain = hidden_rows(merge, 0, 1)
    bias = hidden_rows(merge, 4, 1)
    w = merge[8 : 8 + MERGE, :]
    put_hidden_rows(grads, 8 - 8, 1, jnp.zeros((1, MERGE), F32))
    grads[8 : 8 + MERGE, :] = mm_tn(rows_t(d), hat * gain + bias).T
    d_hat = mm_nt(d, w)
    put_hidden_rows(grads, 0, 1, colsum(d_hat * hat))
    put_hidden_rows(grads, 4, 1, colsum(d_hat))
    flatten(grads, 0, CUTS[1], flat)
    at = 0
    for cut, part in ((CUTS[1], flat1), (CUTS[2], flat2), (CUTS[3], seam)):
        at = 3 * cut
        flat[at : at + part.shape[0], :] = part[...]
    at += seam.shape[0]
    if flat.shape[0] > at:
        flat[at:, :] = jnp.zeros((flat.shape[0] - at, WIDE), F32)
    scatter(sizes, flat, 0, keep, send)


def radices(count):
    steps = [2]
    left = count // 2
    while left > 1:
        steps.append(4 if left >= 4 else 2)
        left //= steps[-1]
    return steps


def block_rows(rows, count):
    return -(-rows // (8 * count)) * 8


def own_number(sizes):
    return lax.axis_index("slab") * sizes[1] + lax.axis_index("mp")


def place_in_half(distance, count):
    place = 0
    shift = 1
    for radix in radices(count)[1:]:
        digit = jnp.bitwise_and(lax.shift_right_logical(distance, shift), radix - 1)
        place = place * radix + digit
        shift += radix.bit_length() - 1
    return place


def scatter(sizes, source, first, keep, send):
    count = sizes[0] * sizes[1]
    rows = keep.shape[0] * 2 // count
    me = own_number(sizes)
    odd = jnp.bitwise_and(me, 1)

    def per_pair(t, carry):
        for block, out in ((2 * t + odd, keep), (2 * t + 1 - odd, send)):
            place = place_in_half(jnp.bitwise_xor(block, me), count)
            at = pl.multiple_of(first + block * rows, 8)
            to = pl.multiple_of(place * rows, 8)
            out[pl.ds(to, rows), :] = source[pl.ds(at, rows), :]
        return carry

    lax.fori_loop(0, count // 2, per_pair, 0)


def traded(value, distance, count):
    pairs = [(i, i ^ distance) for i in range(count)]
    return lax.ppermute(value, ("slab", "mp"), pairs)


def later(got, after):
    return got if after is None else list(lax.optimization_barrier((*got, after)))[:-1]


def summing(keep, send, count):
    steps = radices(count)
    got = [keep, traded(send, 1, count)]
    shift = 1
    after = yield None
    for radix in steps[1:]:
        got = later(got, after)
        total = sum(got[1:], got[0])
        rows = total.shape[0] // radix
        parts = [total[k * rows : (k + 1) * rows] for k in range(radix)]
        got = parts[:1] + [traded(parts[k], k << shift, count) for k in range(1, radix)]
        shift += radix.bit_length() - 1
        after = yield parts[0]
    got = later(got, after)
    own = sum(got[1:], got[0])
    for radix in reversed(steps[1:]):
        shift -= radix.bit_length() - 1
        got = [own] + [traded(own, k << shift, count) for k in range(1, radix)]
        after = yield own
        own = jnp.concatenate(later(got, after), 0)
        yield own
    yield own, traded(own, 1, count)


def finished(chain, after=None):
    last = next(chain) if after is None else chain.send(after)
    while not isinstance(last, tuple):
        last = next(chain)
    return last


def exchanged_sum(value, count):
    shift = 0
    for radix in radices(count):
        got = [value] + [traded(value, k << shift, count) for k in range(1, radix)]
        while len(got) > 1:
            got = [got[i] + got[i + 1] for i in range(0, len(got), 2)]
        value = got[0]
        shift += radix.bit_length() - 1
    return value


PIECE = 262144


def adamw_kernel(
    sizes,
    late, late_other, early, early_other, tail, sums, params, first, second,
    new_params, new_first, new_second, loss, valid, norm_out,
    grad, scale_ref,
):
    count = sizes[0] * sizes[1]
    step = pl.program_id(0)

    @pl.when(step == 0)
    def gather():
        me = own_number(sizes)
        total = jnp.zeros((8, WIDE), F32)
        for ref in (late, late_other, early, early_other):
            x = ref[...]
            total = total + jnp.sum((x * x).reshape(-1, 8, WIDE), 0)
        norm = jnp.sqrt(jnp.sum(total))
        loss[0] = jnp.sum(tail[2:3, 0:1])
        valid[0] = jnp.sum(sums[2:3, 0:1])
        norm_out[0] = norm
        scale_ref[0] = jnp.minimum(1.0, clip_norm / (norm + 1e-06))
        start = 0
        for own, other, size in ((late, late_other, LATE_ROWS), (early, early_other, EARLY_ROWS)):
            rows = own.shape[0] * 2 // count

            def per_block(block, carry, own=own, other=other, rows=rows, start=start):
                distance = jnp.bitwise_xor(block, me)
                at = pl.ds(pl.multiple_of(place_in_half(distance, count) * rows, 8), rows)
                near = jnp.bitwise_and(distance, 1) == 0
                to = pl.ds(pl.multiple_of(start + block * rows, 8), rows)
                grad[to, :] = jnp.where(near, own[at, :], other[at, :])
                return carry

            lax.fori_loop(0, size // rows, per_block, 0)
            start += size

    def update(base, low, size):
        rows = -(-size // 1024) * 8
        at = pl.ds(pl.multiple_of(base // WIDE + low // WIDE, 8), rows)
        g = grad[at, :].reshape(rows * WIDE)[:size] * scale_ref[0]
        here = pl.ds(pl.multiple_of(base + low, 1024), size)
        one = beta_one * first[here] + (1.0 - beta_one) * g
        two = beta_two * second[here] + (1.0 - beta_two) * g * g
        there = pl.ds(low, size)
        new_first[there] = one
        new_second[there] = two
        two = two * (1.0 / (1.0 - beta_two**STEP))
        low_by = two * lax.rsqrt(jnp.maximum(two, 1e-37)) + adam_eps
        inverse = pl.reciprocal(low_by, approx=True)
        inverse = inverse * (2.0 - low_by * inverse)
        new_params[there] = params[here] * (1.0 - learn_rate * decay_rate) - (
            one * (learn_rate / (1.0 - beta_one**STEP))
        ) * inverse

    whole = NPARAM // PIECE

    @pl.when(step < whole)
    def full():
        def part(i, carry):
            low = pl.multiple_of(i * 16384, 16384)
            update(step * PIECE, low, 16384)
            return carry

        lax.fori_loop(0, PIECE // 16384, part, 0)

    @pl.when(step == whole)
    def last():
        rest = NPARAM - whole * PIECE
        main = rest // 1024 * 1024
        for low in range(0, main, 16384):
            update(whole * PIECE, low, min(16384, main - low))
        update(whole * PIECE, main, rest - main)


def adamw(sizes, parts, arrays):
    pieces = -(-NPARAM // PIECE)
    piece = pl.BlockSpec((PIECE,), lambda i: (i,))
    vmem = pl.BlockSpec(memory_space=pltpu.VMEM)
    smem = pl.BlockSpec(memory_space=pltpu.SMEM)
    return pl.pallas_call(
        functools.partial(adamw_kernel, sizes),
        grid=(pieces,),
        out_shape=[arr(NPARAM)] * 3 + [arr(1)] * 3,
        in_specs=[vmem] * (len(parts) + len(arrays)),
        out_specs=[piece] * 3 + [smem] * 3,
        scratch_shapes=[pltpu.VMEM((LATE_ROWS + EARLY_ROWS, WIDE), F32), pltpu.SMEM((1,), F32)],
        compiler_params=pltpu.CompilerParams(vmem_limit_bytes=16 * 1024 * 1024),
        cost_estimate=pl.CostEstimate(flops=6 * 10**9, bytes_accessed=0, transcendentals=0),
        name="adamw",
    )(*parts, *arrays)


def arr(*shape):
    return jax.ShapeDtypeStruct(shape, F32)


def call(kernel, outs, scratch, *args, name=None, us=1.0, far=(), mib=16):
    vmem = pl.BlockSpec(memory_space=pltpu.VMEM)
    smem = pl.BlockSpec(memory_space=pltpu.SMEM)
    return pl.pallas_call(
        kernel,
        out_shape=list(outs),
        in_specs=[vmem] * len(args) + [pl.BlockSpec(memory_space=pl.ANY)] * len(far),
        out_specs=[smem if o.shape == (1,) else vmem for o in outs],
        scratch_shapes=list(scratch),
        compiler_params=pltpu.CompilerParams(vmem_limit_bytes=mib * 1024 * 1024),
        cost_estimate=pl.CostEstimate(
            flops=int(us * 1.15e9), bytes_accessed=0, transcendentals=0
        ),
        name=name,
    )(*args, *far)


SQUARE = arr(ROWS, WIDE)
SAVE = arr(ROWS, 3 * WIDE)
FORWARD = [
    pltpu.VMEM((2, ROWS, 2 * WIDE), BF16),
    pltpu.VMEM((2, KEYS, 2 * WIDE), BF16),
    pltpu.VMEM((2 * KEYS, 2 * WIDE), BF16),
]
BACKWARD = [
    pltpu.VMEM((2, ROWS, 2 * WIDE), BF16),
    pltpu.VMEM((2, KEYS, 2 * WIDE), BF16),
    pltpu.VMEM((2, ROWS, 2 * WIDE), BF16),
    pltpu.VMEM((2, KEYS, 2 * WIDE), BF16),
    pltpu.VMEM((2 * KEYS, 2 * WIDE), BF16),
    pltpu.VMEM((ROWS, WIDE), F32),
    pltpu.VMEM((2, WIDE, KEYS), F32),
    pltpu.VMEM((2, KEYS, 2 * KEYS), BF16),
    pltpu.VMEM((2, KEYS, 2 * KEYS), BF16),
    pltpu.VMEM((2, WIDE, KEYS), BF16),
    pltpu.VMEM((2, WIDE, KEYS), BF16),
    pltpu.VMEM((ROWS, WIDE), F32),
    pltpu.VMEM((ROWS, 2 * KEYS), F32),
    pltpu.VMEM((ROWS, 2 * KEYS), F32),
    pltpu.VMEM((2 * KEYS, 2 * WIDE), BF16),
    pltpu.VMEM((2 * KEYS, 2 * WIDE), BF16),
]
PARTS = [arr(ROWS_A, WIDE), arr(ROWS_B, WIDE), arr(ROWS_C, WIDE)]


def passed(parts, steps, sizes):
    slabs, rows = sizes
    moved = []
    for part, (ds, dm) in zip(parts, ((1, 0), (0, 1), (1, 1))):
        pairs = []
        for s in range(slabs):
            for m in range(rows):
                target = ((s + steps * ds) % slabs) * rows + (m + steps * dm) % rows
                pairs.append((s * rows + m, target))
        moved.append(lax.ppermute(part, ("slab", "mp"), pairs))
    return moved


SIDES = [arr(2 * WIN, 8, WIDE)] * 4


def paired(axis, size):
    near = [(i, i ^ 1) for i in range(size)]
    far = [(i, (i + (1 if i % 2 else -1)) % size) for i in range(size)]
    return (
        lambda value: lax.ppermute(value, axis, near),
        lambda value: lax.ppermute(value, axis, far),
    )


def column_kernel(sizes, near_d, far_d, near_h, far_h, near_out, far_out):
    slab = lax.axis_index("slab")
    odd_d = jnp.bitwise_and(slab, 1) == 1
    odd_h = jnp.bitwise_and(lax.axis_index("mp"), 1) == 1
    at_low = slab == 0
    at_high = slab == sizes[0] - 1
    near_out[4:18] = near_h[...]
    far_out[4:18] = far_h[...]
    for d in range(2):
        near = near_d[d * WIN : (d + 1) * WIN]
        far = far_d[d * WIN : (d + 1) * WIN]
        before = jnp.where(odd_d, near, jnp.where(at_low, 0.0, far))
        after = jnp.where(odd_d, jnp.where(at_high, 0.0, far), near)
        for x, at in ((before, 2 * d), (after, 18 + 2 * d)):
            low, high = x[0:2], x[WIN - 2 : WIN]
            near_out[at : at + 2] = jnp.where(odd_h, low, high)
            far_out[at : at + 2] = jnp.where(odd_h, high, low)


def beside(sides, sizes):
    near, far = paired("slab", sizes[0])
    near_d, far_d = near(sides[0]), far(sides[1])
    near_h, far_h = call(
        functools.partial(column_kernel, sizes), [arr(22, 8, WIDE)] * 2, [],
        near_d, far_d, sides[2], sides[3],
        name="column", us=0.3,
    )
    near, far = paired("mp", sizes[1])
    return near_d, far_d, near(near_h), far(far_h)


REGION = [pltpu.VMEM((ROWS, KEYS), F32)]


def on_device(sizes, feats, labels, valid, params, moment_one, moment_two):
    slabs, rows = sizes
    count = slabs * rows

    def room(spans):
        sizes = [(span_of(groups)[1] + 8) * WIDE for groups in spans]
        return [
            [pltpu.VMEM((size,), F32) for size in sizes],
            pltpu.VMEM((2048, WIDE), F32),
            pltpu.SemaphoreType.DMA((len(spans),)),
        ]

    first_size = FIRST_SPANS[-1][1] * 384
    merge, lay0 = call(
        functools.partial(prep_kernel, FIRST_SPANS),
        [arr(MERGE_ROWS, WIDE), arr(1176, WIDE)],
        room(FIRST_SPANS),
        name="prep_first", us=2.0, far=(params[:first_size],),
    )
    lay1, lay2 = call(
        functools.partial(prep_kernel, LAYER_SPANS),
        [arr(1168, WIDE)] * 2,
        room(LAYER_SPANS),
        name="prep_layers", us=2.0, far=(params,),
    )
    taps_shape = jax.ShapeDtypeStruct((27 * 256, 256), BF16)
    conv0, weights0, bias0 = call(
        prep_conv0_kernel,
        [arr(2596, WIDE), taps_shape, arr(8, WIDE)],
        room(CONV_SPANS[:1]),
        name="prep_conv0", us=1.5, far=(params,),
    )
    conv1, head_w, weights1, vectors = call(
        prep_conv1_kernel,
        [arr(2640, WIDE), arr(WIDE, WIDE), taps_shape, arr(8, WIDE)],
        room(CONV_SPANS[1:]),
        params[NPARAM // WIDE * WIDE :], bias0,
        name="prep_conv1", us=1.5, far=(params,),
    )

    dense, tok0, save0, lse0, mixed0, mid0, hpre0, tok1, ahead, *parts = call(
        first_kernel,
        [arr(ROWS, MERGE), SQUARE, SAVE, SQUARE, SQUARE, SQUARE, arr(ROWS, HID), SQUARE, SQUARE]
        + PARTS,
        FORWARD,
        feats.reshape(PLANE, WIN, MERGE), merge, lay0,
        name="first", us=6.0,
    )
    parts = passed(parts, -1, sizes)
    window, save1, lse1, mixed1, out1, *parts = call(
        functools.partial(shifted_kernel, sizes),
        [SQUARE, SAVE, SQUARE, SQUARE, SQUARE] + PARTS,
        REGION + FORWARD,
        ahead, *parts, lay1,
        name="shifted", us=4.5, far=(weights0,),
    )
    parts = passed(parts, 1, sizes)
    mid1, hpre1, tok2, save2, lse2, mixed2, mid2, hpre2, lines, *sides = call(
        second_kernel,
        [SQUARE, arr(ROWS, HID), SQUARE, SAVE, SQUARE, SQUARE, SQUARE, arr(ROWS, HID)]
        + [arr(PLANE, 8, WIDE)] + SIDES,
        [pltpu.VMEM((ROWS, WIDE), F32)] + FORWARD,
        tok1, out1, *parts, lay1, lay2,
        name="second", us=6.5, far=(weights1,),
    )
    sides = beside(sides, sizes)
    grown, pre, tok3, sums, *tok_sides = call(
        functools.partial(conv_kernel, sizes),
        [arr(11, 12, 8, WIDE), arr(9, 10, 8, WIDE), arr(PLANE, 8, WIDE), arr(8, WIDE)] + SIDES,
        [
            pltpu.VMEM((9, 10, 8, WIDE), F32),
            pltpu.VMEM((880, 2304), BF16),
            pltpu.VMEM((576, 2304), BF16),
            pltpu.VMEM((PLANE, 8, WIDE), F32),
        ],
        lines, *sides, labels, valid, weights0, weights1, vectors,
        name="conv", us=8.0, mib=20,
    )
    tok_sides = beside(tok_sides, sizes)
    side_act, side_grown = call(
        functools.partial(sides_back_kernel, sizes),
        [jax.ShapeDtypeStruct((640, 2304), BF16)] * 2,
        [pltpu.VMEM((10, 10, 8, WIDE), F32)],
        grown, pre,
        name="sides_back", us=2.0,
    )
    weights0, weights1 = call(
        weights_back_kernel,
        [jax.ShapeDtypeStruct((256, 27 * 256), BF16)] * 2,
        [],
        conv0, conv1,
        name="weights_back", us=1.5,
    )
    sums = exchanged_sum(sums, count)
    voxels = WIN * slabs * WIN * rows * WIN
    tok3, slope, tail, d_head, d_rows = call(
        functools.partial(head_kernel, sizes, voxels),
        [arr(11, 12, 8, WIDE), arr(11, 12, 8, WIDE), arr(8, WIDE), arr(WIDE, WIDE), arr(8, WIDE)],
        [],
        tok3, *tok_sides, sums, vectors, head_w,
        name="head", us=3.5,
    )
    tail = exchanged_sum(tail, count)
    late_rows = block_rows(LATE_ROWS, count) * count
    early_rows = block_rows(EARLY_ROWS, count) * count
    seam_rows = LATE_ROWS - 3 * CUTS[3]
    d_own, keep, send, carry3, seam = call(
        functools.partial(conv_back_kernel, sizes),
        [arr(PLANE, 8, WIDE)] + [arr(early_rows // 2, WIDE)] * 2
        + [arr(24, WIDE), arr(seam_rows, WIDE)],
        [
            pltpu.VMEM((5236, WIDE), F32),
            pltpu.VMEM((11, 12, 8, WIDE), F32),
            pltpu.VMEM((10, 10, 8, WIDE), F32),
            pltpu.VMEM((880, 2304), BF16),
            pltpu.VMEM((576, 2304), BF16),
            pltpu.VMEM((seam_rows + early_rows, WIDE), F32),
        ],
        tok3, slope, tail, pre, side_act, side_grown, weights0, weights1, d_rows, d_head,
        name="conv_back", us=14.0, mib=28,
    )
    early = summing(keep, send, count)
    next(early)
    d_mid2, grads2 = call(
        back_mlp_kernel,
        [SQUARE, arr(1168, WIDE)],
        [pltpu.VMEM((ROWS, WIDE), F32)],
        d_own, lay2, mid2, hpre2,
        name="back_mlp", us=3.0,
    )
    step = early.send(d_mid2)
    d_mid, grads1, flat2, carry2, *parts = call(
        back_two_kernel,
        [SQUARE, arr(1168, WIDE), arr(3 * (CUTS[3] - CUTS[2]), WIDE), arr(32, WIDE)] + PARTS,
        [pltpu.VMEM((1184, WIDE), F32)] + BACKWARD,
        d_mid2, grads2, carry3, lay1, lay2, tok2, save2, lse2, mixed2, mid1, hpre1,
        name="back_two", us=9.0,
    )
    parts = passed(parts, -1, sizes)
    step = early.send(d_mid)
    d_window, flat1, carry1, *parts = call(
        functools.partial(back_shifted_kernel, sizes),
        [SQUARE, arr(3 * (CUTS[2] - CUTS[1]), WIDE), arr(16, WIDE)] + PARTS,
        REGION + [pltpu.VMEM((1200, WIDE), F32), pltpu.VMEM((ROWS, WIDE), F32)] + BACKWARD,
        d_mid, *parts, lay1, window, save1, lse1, mixed1, grads1, carry2,
        name="back_shifted", us=10.5, far=(step,),
    )
    early.send(d_window)
    parts = passed(parts, 1, sizes)
    next(early)
    step = next(early)
    late = call(
        functools.partial(back_first_kernel, sizes),
        [arr(late_rows // 2, WIDE)] * 2,
        [
            pltpu.VMEM((late_rows, WIDE), F32),
            pltpu.VMEM((1572, WIDE), F32),
            pltpu.VMEM((ROWS, WIDE), F32),
        ]
        + BACKWARD,
        d_mid, d_window, *parts, tok1, lay0, lay1, merge, dense, tok0, save0, lse0, mixed0, mid0,
        hpre0, carry1, flat1, flat2, seam,
        name="back_first", us=13.5, far=(step,),
    )
    step = early.send(late[0])
    keep, send = later(list(late), step)
    late_sum = finished(summing(keep, send, count))
    early = finished(early)
    new_params, new_first, new_second, loss, valid_count, norm = adamw(
        sizes, (*late_sum, *early, tail, sums), (params, moment_one, moment_two)
    )
    return (
        loss.reshape(()), valid_count.reshape(()), norm.reshape(()),
        new_params, new_first, new_second,
    )


def solution(mesh):
    placed = (
        P("slab", "mp", None, None),
        P("slab", "mp", None),
        P("slab", "mp", None),
        P(),
        P(),
        P(),
    )
    sizes = (mesh.shape["slab"], mesh.shape["mp"])
    return jax.shard_map(
        functools.partial(on_device, sizes),
        mesh=mesh,
        in_specs=placed,
        out_specs=(P(), P(), P(), P(), P(), P()),
        check_vma=False,
    )
```

```python
import functools

import jax
import jax.numpy as jnp
from jax import lax
from jax.experimental import pallas as pl
from jax.experimental.pallas import tpu as pltpu
from jax.sharding import PartitionSpec as P

EMB = 96
HEADS = 6
HDIM = 16
HID = 384
MERGE = 384
CLASSES = 14
WIN = 7
SHIFT = 3
LAYERS = 3
STEP = 10

F32 = jnp.float32
BF16 = jnp.bfloat16
eps_norm = 1e-05
beta_one = 0.9
beta_two = 0.999
adam_eps = 1e-08
learn_rate = 0.05
decay_rate = 0.05
clip_norm = 0.01
LOG2E = 1.4426950408889634

VOX = WIN * WIN * WIN
ROWS = 352
KEYS = 384
BLOCKS = ((0, 128), (128, 256), (256, 352))
WIDE = 128
PLANE = WIN * WIN
FAR = WIN - SHIFT
ROWS_A = SHIFT * FAR * WIN
ROWS_B = FAR * SHIFT * WIN
ROWS_C = SHIFT * SHIFT * WIN

MERGE_ROWS = 392
LAYER_ROWS = 1165
TAP_ROWS = 27 * EMB
GROUPS = 2280
NPARAM = 872558
HEAD_ROW = 6806
HEAD_ROWS = 11
HEAD_LANE = 32
LATE_ROWS = 3072
EARLY_ROWS = 3840
LAYER_BASE = (98, 389, 680)
CONV_BASE = (971, 1620)
CUTS = (0, 392, 688, 976, 2280)

R_QKV, R_QKVB, R_PROJ, R_PROJB = 4, 292, 295, 391
R_HID, R_HIDB, R_OUT, R_OUTB = 392, 776, 780, 1164


def iota(shape, dim):
    return lax.broadcasted_iota(jnp.int32, shape, dim)


def split(x):
    hi = x.astype(BF16)
    return hi, (x - hi.astype(F32)).astype(BF16)


def pair(x):
    return jnp.concatenate(split(x), 1)


def fold(y):
    half = y.shape[1] // 2
    return y[:, :half] + y[:, half:]


def fold_rows(y):
    half = y.shape[0] // 2
    return y[:half] + y[half:]


def dot(a, b):
    return jnp.dot(a, b, preferred_element_type=F32)


def dot_nt(a, b):
    return lax.dot_general(a, b, (((1,), (1,)), ((), ())), preferred_element_type=F32)


def weight_nn(w):
    top = pair(w)
    return jnp.concatenate([top, top], 0)


def weight_nt(w):
    hi, lo = split(w)
    return jnp.concatenate(
        [jnp.concatenate([hi, hi], 1), jnp.concatenate([lo, lo], 1)], 0
    )


def mm(x, w):
    return fold(dot(pair(x), weight_nn(w)))


def mm_nt(x, w):
    return fold(dot_nt(pair(x), weight_nt(w)))


def with_rows(x, rows):
    if x.shape[0] == rows:
        return x
    return jnp.concatenate([x, jnp.zeros((rows - x.shape[0], x.shape[1]), F32)], 0)


def rows_t(x):
    return jnp.concatenate(split(with_rows(x, -(-x.shape[0] // WIDE) * WIDE).T), 0)


def mm_tn(xt, y):
    return fold_rows(fold(dot(xt, pair(with_rows(y, xt.shape[1])))))


def deep(w):
    return jnp.concatenate([w, jnp.zeros((WIDE - EMB, w.shape[1]), F32)], 0)


def roll(x, shift, axis):
    return pltpu.roll(x, shift, axis)


def four_to_three(y):
    lane = iota(y[0].shape, 1)
    a = jnp.where(lane < 96, y[0], roll(y[1], 96, 1))
    b = jnp.where(lane < 64, roll(y[1], 96, 1), roll(y[2], 64, 1))
    c = jnp.where(lane < 32, roll(y[2], 64, 1), roll(y[3], 32, 1))
    return a, b, c


def three_to_four(x):
    lane = iota(x[0].shape, 1)
    live = lane < EMB
    a = x[0]
    b = jnp.where(lane < 32, roll(x[0], 32, 1), roll(x[1], 32, 1))
    c = jnp.where(lane < 64, roll(x[1], 64, 1), roll(x[2], 64, 1))
    d = roll(x[2], 96, 1)
    return tuple(jnp.where(live, v, 0.0) for v in (a, b, c, d))


def hidden_rows(ref, start, count):
    return jnp.concatenate(
        four_to_three([ref[pl.ds(start + c, count, stride=4), :] for c in range(4)]), 1
    )


def put_hidden_rows(ref, start, count, x):
    parts = three_to_four([x[:, i * WIDE : (i + 1) * WIDE] for i in range(3)])
    for c in range(4):
        ref[pl.ds(start + c, count, stride=4), :] = parts[c]


def flatten(ref, start, groups, out):
    parts = four_to_three([ref[pl.ds(start + c, groups, stride=4), :] for c in range(4)])
    for c in range(3):
        out[pl.ds(c, groups, stride=3), :] = parts[c]


def norm_stats(x):
    live = iota(x.shape, 1) < EMB
    mean = jnp.sum(x, 1, keepdims=True) * (1.0 / EMB)
    centred = jnp.where(live, x - mean, 0.0)
    var = jnp.sum(centred * centred, 1, keepdims=True) * (1.0 / EMB)
    inv = lax.rsqrt(var + eps_norm)
    return centred * inv, inv


def norm(x, gain, bias):
    hat, _ = norm_stats(x)
    return hat * gain + bias


def norm_back(hat, inv, gain, grad):
    up = grad * gain
    one = jnp.sum(up, 1, keepdims=True) * (1.0 / EMB)
    two = jnp.sum(up * hat, 1, keepdims=True) * (1.0 / EMB)
    live = iota(hat.shape, 1) < EMB
    return jnp.where(live, inv * (up - one - hat * two), 0.0)


def colsum(x):
    return jnp.sum(x, 0, keepdims=True)


def gelu(x):
    return 0.5 * x * (1.0 + lax.erf(x * (0.5**0.5)))


def gelu_both(x):
    cdf = 0.5 * (1.0 + lax.erf(x * (0.5**0.5)))
    slope = cdf + x * (jnp.exp(x * x * -0.5) * 0.3989422804014327)
    return x * cdf, slope


def head_groups(x):
    lane = iota(x.shape, 1)
    swapped = roll(x, 64, 1)
    return jnp.where(lane < 64, x, swapped), jnp.where(lane < 64, swapped, x)


def as_left(x):
    both = []
    low = iota(x.shape, 1) < 64
    for part in head_groups(x):
        hi = part.astype(BF16).astype(F32)
        one = jnp.where(low, hi, part - hi).astype(BF16)
        both.append(jnp.concatenate([one, one], 1))
    return both


def as_right(x, rows):
    return [pair(part) for part in head_groups(with_rows(x, rows))]


def head_mask(h, width):
    lane = iota((1, width), 1)
    lane = jnp.bitwise_and(lane, 63)
    low = jnp.bitwise_and(h, 3) * HDIM
    return jnp.where((lane >= low) & (lane < low + HDIM), 1.0, 0.0)


def own_lanes(h):
    lane = iota((1, WIDE), 1)
    return jnp.where((lane >= h * HDIM) & (lane < (h + 1) * HDIM), 1.0, 0.0)


def both_heads(right, heads, out):
    for k, h in enumerate(heads):
        out[k * KEYS : (k + 1) * KEYS, :] = right * head_mask(h, 2 * WIDE).astype(BF16)


def score_tiles(s, rows, region):
    tiles = [s[:, i * WIDE : (i + 1) * WIDE] for i in range(3)]
    if region is not None:
        return [t + region[rows, i * WIDE : (i + 1) * WIDE] for i, t in enumerate(tiles)]
    pad = jnp.where(iota((1, WIDE), 1) < VOX - 2 * WIDE, 0.0, -1e30)
    return tiles[:2] + [tiles[2] + pad]


def put_split(ref, rows, i, x):
    hi, lo = split(x)
    ref[rows, i * WIDE : (i + 1) * WIDE] = hi
    ref[rows, KEYS + i * WIDE : KEYS + (i + 1) * WIDE] = lo


def attention(normed, layer, save, lse, mixed, sc, region=None):
    left, right, values, mixed_t, lse_t = sc
    x = pair(normed)
    qkv = []
    for i in range(3):
        w = deep(layer[pl.ds(R_QKV + i, EMB, stride=3), :])
        y = fold(dot(x, weight_nn(w))) + layer[R_QKVB + i : R_QKVB + i + 1, :]
        if i == 0:
            y = y * (HDIM**-0.5 * LOG2E)
        save[:, i * WIDE : (i + 1) * WIDE] = y
        qkv.append(y)
    for g, part in enumerate(as_left(with_rows(qkv[0], KEYS))):
        left[g] = part
    for g, part in enumerate(as_right(qkv[1], ROWS)):
        right[g] = part
    hi, lo = split(with_rows(qkv[2], KEYS).T)
    for h in range(HEADS):
        rows = slice(h * HDIM, (h + 1) * HDIM)
        values[h, 0:HDIM, :] = hi[rows]
        values[h, HDIM : 2 * HDIM, :] = lo[rows]
        values[h, 2 * HDIM :, :] = jnp.ones((HDIM, KEYS), BF16)
    mixed_t[HEADS * HDIM :, :] = jnp.zeros((WIDE - HEADS * HDIM, KEYS), F32)
    lse_t[...] = jnp.zeros_like(lse_t)
    last = ROWS - 2 * 8
    pad = jnp.where(iota((ROWS - last, 1), 0) + last < VOX, 0.0, -1e30)
    none = jnp.zeros((KEYS - ROWS, 2 * WIDE), BF16)

    def per_pair(pair_of, carry):
        g = lax.div(pair_of, 2)
        for b in range(KEYS // WIDE):
            block = slice(b * WIDE, (b + 1) * WIDE)
            for k in range(2):
                h = 2 * pair_of + k
                s = dot_nt(right[g], left[g, block, :] * head_mask(h, 2 * WIDE).astype(BF16))
                if region is None:
                    s = jnp.concatenate([s[:last], s[last:] + pad], 0)
                else:
                    s = s + region[:, block]
                top = jnp.max(s, 0, keepdims=True)
                e = jnp.concatenate([pair(jnp.exp2(s - top)), none], 0)
                y = fold(dot(values[h], e))
                total = y[2 * HDIM : 2 * HDIM + 1, :]
                here = pl.ds(pl.multiple_of(h * HDIM, HDIM), HDIM)
                mixed_t[here, block] = (y[0:HDIM, :] + y[HDIM : 2 * HDIM, :]) * (1.0 / total)
                level = top + jnp.log(total) * LOG2E
                lse_t[0:8, block] += jnp.where(iota((8, WIDE), 0) == h, level, 0.0)
        return carry

    lax.fori_loop(0, HEADS // 2, per_pair, 0)
    mixed[...] = mixed_t[...].T[0:ROWS]
    lse[...] = lse_t[...].T[0:ROWS]
    proj = deep(layer[R_PROJ : R_PROJ + EMB, :])
    return mm(mixed[...], proj) + layer[R_PROJB : R_PROJB + 1, :]


def attention_back(grad, normed, layer, save, lse, mixed, sc, grads, at, region=None):
    left, right, gleft, vright, keys, dq, dkv_t, weights, slopes = sc[:9]
    q_t, do_t, dmix, s, dp, two_keys, two_values = sc[9:]
    proj = deep(layer[R_PROJ : R_PROJ + EMB, :])
    grads[at + R_PROJ : at + R_PROJ + EMB, :] = mm_tn(rows_t(mixed[...]), grad)[:EMB]
    grads[at + R_PROJB : at + R_PROJB + 1, :] = colsum(grad)
    d_mixed = mm_nt(grad, proj)
    dmix[...] = d_mixed * mixed[...]
    q, k, v = (save[:, i * WIDE : (i + 1) * WIDE] for i in range(3))
    for g, part in enumerate(as_left(q)):
        left[g] = part
    for g, part in enumerate(as_right(k, KEYS)):
        right[g] = part
    for g, part in enumerate(as_left(d_mixed)):
        gleft[g] = part
    for g, part in enumerate(as_right(v, KEYS)):
        vright[g] = part
    kk = pair(with_rows(k, KEYS))
    keys[0:KEYS, :] = kk
    keys[KEYS : 2 * KEYS, :] = kk
    weights[:, ROWS:, :] = jnp.zeros((2, KEYS - ROWS, 2 * KEYS), BF16)
    slopes[:, ROWS:, :] = jnp.zeros((2, KEYS - ROWS, 2 * KEYS), BF16)
    for ref, x in ((q_t, q), (do_t, d_mixed)):
        hi, lo = split(with_rows(x, KEYS).T)
        ref[0] = hi
        ref[1] = lo
    dq[...] = jnp.zeros_like(dq)
    dkv_t[...] = jnp.zeros_like(dkv_t)

    def per_pair(pair_of, carry):
        g = lax.div(pair_of, 2)
        heads = [2 * pair_of, 2 * pair_of + 1]
        both_heads(right[g], heads, two_keys)
        both_heads(vright[g], heads, two_values)
        s[...] = dot_nt(left[g], two_keys[...])
        dp[...] = dot_nt(gleft[g], two_values[...])
        for k in range(2):
            h = 2 * pair_of + k
            lanes = own_lanes(h)
            at_h = jnp.where(iota((1, WIDE), 1) == h, 1.0, 0.0)
            for block in BLOCKS:
                rows = slice(*block)
                level = jnp.sum(lse[rows, :] * at_h, 1, keepdims=True)
                delta = jnp.sum(dmix[rows, :] * lanes, 1, keepdims=True)
                at_k = k * KEYS
                tiles = score_tiles(s[rows, at_k : at_k + KEYS], rows, region)
                for i, t in enumerate(tiles):
                    p = jnp.exp2(t - level)
                    put_split(weights.at[k], rows, i, p)
                    low = at_k + i * WIDE
                    p = p * (dp[rows, low : low + WIDE] - delta)
                    put_split(slopes.at[k], rows, i, p)
        total = 0.0
        for k in range(2):
            out = fold(dot(slopes[k, 0:ROWS, :], keys[...]))
            total = total + out * own_lanes(2 * pair_of + k)
        dq[...] += total
        for k in range(2):
            here = pl.ds(pl.multiple_of((2 * pair_of + k) * HDIM, HDIM), HDIM)
            for i, (t, m) in enumerate(((q_t, slopes), (do_t, weights))):
                lhs = jnp.concatenate([t[0, here, :], t[1, here, :]], 0)
                dkv_t[i, here, :] = fold_rows(fold(dot(lhs, m[k])))
        return carry

    lax.fori_loop(0, HEADS // 2, per_pair, 0)
    d_q = dq[...] * HDIM**-0.5
    d_k = dkv_t[0].T[0:ROWS] * (1.0 / LOG2E)
    d_v = dkv_t[1].T[0:ROWS]
    x_t = rows_t(normed)
    d_normed = None
    for i, d in enumerate((d_q, d_k, d_v)):
        grads[pl.ds(at + R_QKV + i, EMB, stride=3), :] = mm_tn(x_t, d)[:EMB]
        grads[at + R_QKVB + i : at + R_QKVB + i + 1, :] = colsum(d)
        part = mm_nt(d, deep(layer[pl.ds(R_QKV + i, EMB, stride=3), :]))
        d_normed = part if d_normed is None else d_normed + part
    return d_normed


def mlp(middle, layer, hpre):
    normed = norm(middle, layer[2:3, :], layer[3:4, :])
    w = deep(hidden_rows(layer, R_HID, EMB))
    pre = mm(normed, w) + hidden_rows(layer, R_HIDB, 1)
    hpre[...] = pre
    out = mm(gelu(pre), layer[R_OUT : R_OUT + HID, :])
    return middle + out + layer[R_OUTB : R_OUTB + 1, :]


def mlp_back(grad, middle, hpre, layer, grads, at):
    hat, inv = norm_stats(middle)
    normed = hat * layer[2:3, :] + layer[3:4, :]
    act, slope = gelu_both(hpre[...])
    grads[at + R_OUTB : at + R_OUTB + 1, :] = colsum(grad)
    grads[at + R_OUT : at + R_OUT + HID, :] = mm_tn(rows_t(grad), act).T
    d_pre = mm_nt(grad, layer[R_OUT : R_OUT + HID, :]) * slope
    put_hidden_rows(grads, at + R_HIDB, 1, colsum(d_pre))
    put_hidden_rows(grads, at + R_HID, EMB, mm_tn(rows_t(normed), d_pre)[:EMB])
    d_normed = mm_nt(d_pre, deep(hidden_rows(layer, R_HID, EMB)))
    grads[at + 2 : at + 3, :] = colsum(d_normed * hat)
    grads[at + 3 : at + 4, :] = colsum(d_normed)
    return grad + norm_back(hat, inv, layer[2:3, :], d_normed)


def pre_norm_back(grad, tokens, layer, grads, at):
    hat, inv = norm_stats(tokens)
    grads[at : at + 1, :] = colsum(grad * hat)
    grads[at + 1 : at + 2, :] = colsum(grad)
    return norm_back(hat, inv, layer[0:1, :], grad)


def region_of(rows, sizes):
    d = lax.shift_right_logical(rows * 1338, 16)
    line = lax.shift_right_logical(rows * 9363, 16)
    places = (d, line - d * WIN, rows - line * WIN)
    starts = (lax.axis_index("slab") * WIN, lax.axis_index("mp") * WIN, 0)
    total = None
    for place, start, blocks in zip(places, starts, sizes + (1,)):
        turned = jnp.where(place < SHIFT, place + FAR, place - SHIFT) + start
        length = WIN * blocks
        part = jnp.where(turned < length - WIN, 0, jnp.where(turned < length - SHIFT, 1, 2))
        total = part if total is None else total * 3 + part
    return total


def put_region(region, sizes, keys):
    rows = region_of(iota((ROWS, WIDE), 0), sizes)[:, 0:1]
    lanes = region_of(iota((8, KEYS), 1), sizes)[0:1, :]
    apart = jnp.where(rows == lanes, 0.0, -100.0 * LOG2E)
    region[...] = jnp.where(iota((ROWS, KEYS), keys) < VOX, apart, -1e30)


def send_parts(ref, a, b, c):
    far = FAR * WIN
    near = SHIFT * WIN
    for d in range(SHIFT):
        base = d * PLANE
        c[d * near : (d + 1) * near, :] = ref[base : base + near, :]
        a[d * far : (d + 1) * far, :] = ref[base + near : base + PLANE, :]
    for d in range(FAR):
        base = (d + SHIFT) * PLANE
        b[d * near : (d + 1) * near, :] = ref[base : base + near, :]


def take_parts(own, a, b, c, out):
    far = FAR * WIN
    near = SHIFT * WIN
    for d in range(WIN):
        base = d * PLANE
        if d < SHIFT:
            out[base : base + near, :] = c[d * near : (d + 1) * near, :]
            out[base + near : base + PLANE, :] = a[d * far : (d + 1) * far, :]
        else:
            e = d - SHIFT
            out[base : base + near, :] = b[e * near : (e + 1) * near, :]
            out[base + near : base + PLANE, :] = own[base + near : base + PLANE, :]
    out[VOX:, :] = jnp.zeros((ROWS - VOX, WIDE), F32)


def span_of(groups):
    low, high = groups
    first = 3 * low // 8 * 8
    last = -(-3 * high // 8) * 8
    return first, min(last, NPARAM // WIDE // 8 * 8) - first


def copied(params, groups, flat, sem):
    first, rows = span_of(groups)
    size = rows * WIDE
    return pltpu.make_async_copy(
        params.at[pl.ds(first * WIDE, size)], flat.at[pl.ds(0, size)], sem
    )


def relay(groups, flat, out, square, last=None):
    low, high = groups
    first, rows = span_of(groups)
    square[0:rows, :] = flat[0 : rows * WIDE].reshape(rows, WIDE)
    if last is not None:
        square[rows : rows + 24, :] = jnp.zeros((24, WIDE), F32)
        square[rows : rows + 1, 0 : last.shape[0]] = last[...].reshape(1, last.shape[0])
    skip = 3 * low - first
    n = high - low
    parts = three_to_four([square[pl.ds(skip + c, n, stride=3), :] for c in range(3)])
    for c in range(4):
        out[pl.ds(c, n, stride=4), :] = parts[c]


FIRST_SPANS = ((0, 98), (98, 392))
LAYER_SPANS = ((389, 681), (680, 972))
CONV_SPANS = ((971, 1620), (1620, GROUPS))


def prep_kernel(spans, params, *refs, last=None):
    outs, (flats, square, sems) = refs[: len(spans)], refs[-3:]
    for i, groups in enumerate(spans):
        copied(params, groups, flats[i], sems.at[i]).start()
    for i, groups in enumerate(spans):
        copied(params, groups, flats[i], sems.at[i]).wait()
        relay(groups, flats[i], outs[i], square, last if i == len(spans) - 1 else None)


def head_picks():
    width = HEAD_ROWS * WIDE
    place = iota((WIDE, width), 1) - HEAD_LANE
    row = iota((WIDE, width), 0)
    here = (place >= row * CLASSES) & (place < (row + 1) * CLASSES) & (row <= EMB)
    place = iota((width, WIDE), 0) - HEAD_LANE
    col = iota((width, WIDE), 1)
    row = lax.shift_right_logical(place * 4682, 16)
    there = (place - row * CLASSES == col) & (place >= 0)
    return jnp.where(here, 1.0, 0.0), jnp.where(there, 1.0, 0.0).astype(BF16)


def prep_conv0_kernel(params, conv0, weights0, bias, *scratch):
    prep_kernel(CONV_SPANS[:1], params, conv0, *scratch)
    tap_weights(conv0, 3, weights0)
    bias[0:1, :] = conv0[3 + TAP_ROWS : 4 + TAP_ROWS, :]
    bias[1:8, :] = jnp.zeros((7, WIDE), F32)


def prep_conv1_kernel(last, bias, params, conv1, head, weights1, vectors, *scratch):
    prep_kernel(CONV_SPANS[1:], params, conv1, *scratch, last=last)
    tap_weights(conv1, 0, weights1)
    vectors[0:1, :] = bias[0:1, :]
    vectors[1:4, :] = conv1[TAP_ROWS : TAP_ROWS + 3, :]
    vectors[4:8, :] = jnp.zeros((4, WIDE), F32)
    square = scratch[1]
    first, _ = span_of(CONV_SPANS[1])
    row = jnp.concatenate(
        [square[HEAD_ROW + i - first : HEAD_ROW + i - first + 1, :] for i in range(HEAD_ROWS)], 1
    )
    here, there = head_picks()
    hi, lo = split(here * row)
    head[...] = dot(hi, there) + dot(lo, there)


def head_rows(d_head, out, at):
    here, there = head_picks()
    hi, lo = split(d_head)
    spread = (dot_nt(hi, there) + dot_nt(lo, there)) * here
    row = colsum(spread)
    for i in range(HEAD_ROWS):
        out[at + i : at + i + 1, :] += row[:, i * WIDE : (i + 1) * WIDE]


class Rows:
    def __init__(self, ref, at):
        self.ref, self.at = ref, at

    def __getitem__(self, key):
        rows, lanes = key
        if isinstance(rows, slice):
            rows = slice(rows.start + self.at, rows.stop + self.at)
        else:
            rows = pl.ds(rows.start + self.at, rows.size, stride=rows.stride)
        return self.ref[rows, lanes]


def merged_norm(x):
    mean = jnp.sum(x, 1, keepdims=True) * (1.0 / MERGE)
    centred = x - mean
    var = jnp.sum(centred * centred, 1, keepdims=True) * (1.0 / MERGE)
    return centred * lax.rsqrt(var + eps_norm)


def first_kernel(
    feats, merge, lay0,
    dense, tok0, save, lse, mixed, middle, hpre, tok1, ahead, pa, pb, pc,
    *sc,
):
    dense[VOX:, :] = jnp.zeros((ROWS - VOX, MERGE), F32)
    for line in range(PLANE):
        dense[line * WIN : (line + 1) * WIN, :] = feats[line]
    hat = merged_norm(dense[...])
    normed = hat * hidden_rows(merge, 0, 1) + hidden_rows(merge, 4, 1)
    tokens = mm(normed, merge[8 : 8 + MERGE, :])
    tok0[...] = tokens
    layer = Rows(lay0, 0)
    normed = norm(tokens, layer[0:1, :], layer[1:2, :])
    attended = attention(normed, layer, save, lse, mixed, sc)
    mid = tokens + attended
    middle[...] = mid
    tokens = mlp(mid, layer, hpre)
    tok1[...] = tokens
    ahead[...] = norm(tokens, layer[1165:1166, :], layer[1166:1167, :])
    send_parts(ahead, pa, pb, pc)


def shifted_kernel(
    sizes,
    own, pa, pb, pc, lay1, _,
    window, save, lse, mixed, out, qa, qb, qc,
    region, *sc,
):
    put_region(region, sizes, 0)
    take_parts(own, pa, pb, pc, window)
    out[...] = attention(
        window[...], Rows(lay1, 1), save, lse, mixed, sc, region
    )
    send_parts(out, qa, qb, qc)


def to_lines(ref, out):
    for line in range(PLANE):
        out[line, 0:WIN, :] = ref[line * WIN : (line + 1) * WIN, :]
        out[line, WIN:8, :] = jnp.zeros((8 - WIN, WIDE), F32)


def from_lines(ref, out):
    out[VOX:, :] = jnp.zeros((ROWS - VOX, WIDE), F32)
    for line in range(PLANE):
        out[line * WIN : (line + 1) * WIN, :] = ref[line, 0:WIN, :]


def send_sides(lines, near_d, far_d, near_h, far_h):
    odd_d = jnp.bitwise_and(lax.axis_index("slab"), 1) == 1
    odd_h = jnp.bitwise_and(lax.axis_index("mp"), 1) == 1
    low, high = lines[0 : 2 * WIN], lines[(WIN - 2) * WIN : PLANE]
    near_d[...] = jnp.where(odd_d, low, high)
    far_d[...] = jnp.where(odd_d, high, low)
    for d in range(WIN):
        low = lines[d * WIN : d * WIN + 2]
        high = lines[d * WIN + WIN - 2 : (d + 1) * WIN]
        near_h[2 * d : 2 * d + 2] = jnp.where(odd_h, low, high)
        far_h[2 * d : 2 * d + 2] = jnp.where(odd_h, high, low)


def second_kernel(
    tok1, own, qa, qb, qc, lay1, lay2, _,
    mid1, hpre1, tok2, save, lse, mixed, mid2, hpre2, lines,
    s0, s1, s2, s3,
    attended, *sc,
):
    take_parts(own, qa, qb, qc, attended)
    mid = tok1[...] + attended[...]
    mid1[...] = mid
    tokens = mlp(mid, Rows(lay1, 1), hpre1)
    tok2[...] = tokens
    layer = Rows(lay2, 2)
    normed = norm(tokens, layer[0:1, :], layer[1:2, :])
    mid = tokens + attention(normed, layer, save, lse, mixed, sc)
    mid2[...] = mid
    attended[...] = mlp(mid, layer, hpre2)
    to_lines(attended, lines)
    send_sides(lines, s0, s1, s2, s3)


def grown_lines(sizes, own, near_d, far_d, near_h, far_h, out):
    slab, row = lax.axis_index("slab"), lax.axis_index("mp")
    odd_d = jnp.bitwise_and(slab, 1) == 1
    odd_h = jnp.bitwise_and(row, 1) == 1
    out[:, 11:12] = jnp.zeros((11, 1, 8, WIDE), F32)
    for d in range(WIN):
        out[d + 2, 2 : 2 + WIN] = own[d * WIN : (d + 1) * WIN]
    for d in range(2):
        near = near_d[d * WIN : (d + 1) * WIN]
        far = far_d[d * WIN : (d + 1) * WIN]
        out[d, 2 : 2 + WIN] = jnp.where(odd_d, near, jnp.where(slab == 0, 0.0, far))
        out[d + 9, 2 : 2 + WIN] = jnp.where(
            odd_d, jnp.where(slab == sizes[0] - 1, 0.0, far), near
        )
    for d in range(11):
        near = near_h[2 * d : 2 * d + 2]
        far = far_h[2 * d : 2 * d + 2]
        out[d, 0:2] = jnp.where(odd_h, near, jnp.where(row == 0, 0.0, far))
        out[d, 9:11] = jnp.where(odd_h, jnp.where(row == sizes[1] - 1, 0.0, far), near)


def put_marks(labels, valid, out):
    across = iota((8, WIN), 1) == iota((8, WIN), 0)
    classes = iota((8, WIDE), 1) - EMB
    for d in range(WIN):
        code = jnp.where(valid[d] == 1, labels[d], -1 - EMB - WIDE)
        code = code.astype(F32)
        for h in range(WIN):
            line = jnp.where(across, code[h : h + 1, :], 0.0)
            column = jnp.sum(line, 1, keepdims=True)
            mark = jnp.where(column == classes.astype(F32), 1.0, 0.0)
            out[d * WIN + h] = jnp.where(iota((8, WIDE), 0) < WIN, mark, 0.0)


def taps(source, first_plane, planes, first_line, lines, out):
    def per_plane(d, carry):
        for c in range(3):
            for b in range(3):
                x = source[d + first_plane, first_line + b : first_line + b + lines]
                if c != 1:
                    x = roll(x, 1 if c == 0 else 7, 1)
                x = pair(x.reshape(lines * 8, WIDE))
                at = pl.multiple_of(d * (lines * 8), lines * 8)
                t = b * 3 + c
                out[pl.ds(at, lines * 8), t * 256 : (t + 1) * 256] = x
        return carry

    lax.fori_loop(0, planes, per_plane, 0)


def tap_weights(ref, at, out):
    def per_tap(i, carry):
        w = deep(ref[pl.ds(i * EMB + at, EMB), :])
        out[pl.ds(pl.multiple_of(i * 256, 256), 256), :] = weight_nn(w)
        return carry

    lax.fori_loop(0, 27, per_tap, 0)


def tap_weights_back(ref, at, out):
    for i in range(27):
        w = deep(ref[(26 - i) * EMB + at : (27 - i) * EMB + at, :])
        out[:, i * 256 : (i + 1) * 256] = weight_nt(w)


def conv(side, weights, planes, pitch, at_once, put, back=False):
    rows = at_once * pitch
    for start in range(0, planes, at_once):
        total = None
        for a in range(3):
            low = (start + a) * pitch
            x = side[low : low + rows, :]
            if back:
                part = dot_nt(x, weights[:, a * 2304 : (a + 1) * 2304])
            else:
                part = dot(x, weights[a * 2304 : (a + 1) * 2304, :])
            total = part if total is None else total + part
        put(start, fold(total))


def conv_weight_grad(side, grad_rows, pitch, out, at):
    rows = 512
    g = jnp.concatenate([grad_rows, jnp.zeros((rows - grad_rows.shape[0], WIDE), F32)], 0)
    left = jnp.concatenate(split(g.T[:EMB]), 0)
    for a in range(3):
        for bc in range(9):
            y = dot(left, side[a * pitch : a * pitch + rows, bc * 256 : (bc + 1) * 256])
            y = deep(fold_rows(fold(y))).T
            t = a * 9 + bc
            out[at + t * EMB : at + (t + 1) * EMB, :] = y[:EMB]


def volume_mask(sizes, planes, lines, reach, real_lines):
    slab, row = lax.axis_index("slab"), lax.axis_index("mp")
    ends = (slab == 0, slab == sizes[0] - 1, row == 0, row == sizes[1] - 1)
    shape = (planes, lines, 8, WIDE)
    d, h, w = iota(shape, 0), iota(shape, 1), iota(shape, 2)
    low_d = jnp.where(ends[0], reach, 0)
    high_d = jnp.where(ends[1], planes - reach, planes)
    low_h = jnp.where(ends[2], reach, 0)
    high_h = jnp.where(ends[3], real_lines - reach, real_lines)
    inside = (d >= low_d) & (d < high_d) & (h >= low_h) & (h < high_h) & (w < WIN)
    return jnp.where(inside, 1.0, 0.0)


def conv_kernel(
    sizes,
    own, s0, s1, s2, s3, labels, valid, weights0, weights1, vectors,
    grown, pre, tok, stats, t0, t1, t2, t3,
    act, side, side_own, marks,
):
    grown_lines(sizes, own, s0, s1, s2, s3, grown)
    put_marks(labels, valid, marks)
    taps(grown, 0, 11, 0, 10, side)
    bias0 = vectors[0:1, :]
    inside = volume_mask(sizes, 9, 10, 1, 9)


    def put(start, y):
        z = (y + bias0).reshape(3, 10, 8, WIDE)
        pre[start : start + 3] = z
        act[start : start + 3] = gelu(z) * inside[start : start + 3]

    conv(side, weights0, 9, 80, 3, put)
    taps(act, 0, 9, 0, 8, side_own)
    bias1 = vectors[1:2, :]
    sums = []

    def put_own(start, y):
        y = (y + bias1).reshape(WIN, 8, 8, WIDE)[:, 0:WIN]
        y = y + own[...].reshape(WIN, WIN, 8, WIDE)
        y = jnp.where(iota(y.shape, 2) < WIN, y, 0.0).reshape(PLANE, 8, WIDE)
        tok[...] = y + marks[...]
        send_sides(tok, t0, t1, t2, t3)
        flat = y.reshape(PLANE * 8, WIDE)
        sums.append(colsum(flat))
        sums.append(colsum(flat * flat))

    conv(side_own, weights1, WIN, 64, WIN, put_own)
    count = jnp.sum(marks[...].reshape(PLANE * 8, WIDE))
    row = iota((8, WIDE), 0)
    stats[...] = (
        jnp.where(row == 0, sums[0], 0.0)
        + jnp.where(row == 1, sums[1], 0.0)
        + jnp.where(row == 2, count, 0.0)
    )


def head_kernel(
    sizes, voxels,
    own, s0, s1, s2, s3, sums, vectors, head_w,
    grown, slope_out, stats, d_head, d_rows,
):
    grown_lines(sizes, own, s0, s1, s2, s3, grown)
    rows = 11 * 12 * 8
    both = grown[...].reshape(rows, WIDE)
    lane = iota((rows, WIDE), 1)
    tokens = jnp.where(lane < EMB, both, 0.0)
    target = jnp.where(lane < CLASSES, roll(both, WIDE - EMB, 1), 0.0)
    live = jnp.sum(target, 1, keepdims=True)
    count = F32(voxels)
    average = sums[0:1, :] / count
    spread = sums[1:2, :] / count - average * average
    inv = lax.rsqrt(spread + eps_norm)
    gain = vectors[2:3, :]
    bias = vectors[3:4, :]
    hat = (tokens - average) * inv
    act, slope = gelu_both(hat * gain + bias)
    act = jnp.where(lane == EMB, 1.0, act)
    w = head_w[...]
    logits = mm(act, w)
    logits = jnp.where(lane < CLASSES, logits, -1e30)
    top = jnp.max(logits, 1, keepdims=True)
    e = jnp.exp(logits - top)
    total = jnp.sum(e, 1, keepdims=True)
    logp = logits - top - jnp.log(total)
    scale = 1.0 / sums[2:3, 0:1]
    d_logits = (e / total * live - target) * scale
    d_normed = jnp.where(lane < EMB, mm_nt(d_logits, w) * slope, 0.0)
    d_tokens = d_normed * gain * inv
    slope_out[...] = d_tokens.reshape(11, 12, 8, WIDE)

    def own_rows(x):
        x = x.reshape(11, 12, 8, WIDE)[2:9, 2:9]
        x = jnp.where(iota(x.shape, 2) < WIN, x, 0.0)
        return x.reshape(PLANE * 8, WIDE)

    loss = -jnp.sum(own_rows(target * jnp.where(lane < CLASSES, logp, 0.0)))
    own_d = own_rows(d_logits)
    own_n = own_rows(d_normed)
    own_hat = own_rows(hat)
    zeros = jnp.zeros((512 - PLANE * 8, WIDE), F32)
    left = rows_t(jnp.concatenate([own_d, zeros], 0))
    d_head[...] = mm_tn(left, jnp.concatenate([own_rows(act), zeros], 0)).T
    d_gain = colsum(own_n * own_hat)
    d_bias = colsum(own_n)
    d_average = -d_bias * gain * inv
    d_spread = d_gain * gain * inv * inv * -0.5
    d_two = d_spread / count
    d_one = (d_average - 2.0 * average * d_spread) / count
    row = iota((8, WIDE), 0)
    live_lane = iota((8, WIDE), 1) < EMB
    stats[...] = (
        jnp.where((row == 0) & live_lane, d_one, 0.0)
        + jnp.where((row == 1) & live_lane, d_two, 0.0)
        + jnp.where(row == 2, loss, 0.0)
    )
    d_rows[...] = (
        jnp.where(row == 0, d_gain, 0.0)
        + jnp.where(row == 1, d_bias, 0.0)
    )


def sides_back_kernel(sizes, grown, pre, side_act, side_grown, act):
    act[0:9] = gelu(pre[...]) * volume_mask(sizes, 9, 10, 1, 9)
    act[9:10] = jnp.zeros((1, 10, 8, WIDE), F32)
    taps(act, 0, 10, 0, 8, side_act)
    taps(grown, 1, 10, 1, 8, side_grown)


def weights_back_kernel(conv0, conv1, weights0, weights1):
    tap_weights_back(conv0, 3, weights0)
    tap_weights_back(conv1, 0, weights1)


def conv_back_kernel(
    sizes,
    tok, slope, sums, pre, side_act, side_grown, weights0, weights1, d_rows, d_head,
    d_own, keep, send, carry, seam,
    grads, dgrown, act, side, side_own, flat,
):
    lane = iota((11, 12, 8, WIDE), 3)
    inside = volume_mask(sizes, 11, 12, 2, 11)
    steady = sums[0:1, :].reshape(1, 1, 1, WIDE)
    rising = 2.0 * sums[1:2, :].reshape(1, 1, 1, WIDE)
    d_tok = slope[...] + jnp.where(lane < EMB, (steady + tok[...] * rising) * inside, 0.0)
    dgrown[...] = d_tok
    grads[5191:, :] = jnp.zeros((45, WIDE), F32)
    grads[0:8, :] = jnp.zeros((8, WIDE), F32)
    grads[5189:5191, :] = d_rows[0:2, :]
    own = dgrown[2:9, 2:10]
    line = iota(own.shape, 1)
    own = jnp.where(line < WIN, own, 0.0).reshape(WIN * 64, WIDE)
    grads[5188:5189, :] = colsum(own)

    near = volume_mask(sizes, 9, 10, 1, 9)
    conv_weight_grad(side_act, own, 64, grads, 2596)
    taps(dgrown, 0, 11, 0, 10, side)


    def put(start, y):
        _, s = gelu_both(pre[start : start + 3])
        act[start : start + 3] = y.reshape(3, 10, 8, WIDE) * s * near[start : start + 3]

    conv(side, weights1, 9, 80, 3, put, back=True)

    own = act[1:8, 1:9]
    line = iota(own.shape, 1)
    own = jnp.where(line < WIN, own, 0.0).reshape(WIN * 64, WIDE)
    grads[2595:2596, :] = colsum(own)
    conv_weight_grad(side_grown, own, 64, grads, 3)
    carry[...] = grads[0:24, :]
    flat[3 * (GROUPS - CUTS[3]) :, :] = jnp.zeros((flat.shape[0] - 3912, WIDE), F32)
    flatten(grads, 20, GROUPS - CUTS[3], flat)
    start = 3 * CUTS[3]
    head_rows(d_head[...], flat, HEAD_ROW - start)
    seam[...] = flat[0 : LATE_ROWS - start, :]
    scatter(sizes, flat, LATE_ROWS - start, keep, send)
    taps(act, 0, 9, 0, 8, side_own)

    def put_own(start, y):
        y = y.reshape(WIN, 8, 8, WIDE)[:, 0:WIN] + dgrown[2:9, 2:9]
        y = jnp.where(iota(y.shape, 2) < WIN, y, 0.0)
        d_own[...] = y.reshape(PLANE, 8, WIDE)

    conv(side_own, weights0, WIN, 64, WIN, put_own, back=True)


def back_mlp_kernel(d_own, lay2, mid2, hpre2, d_mid, grads, dense):
    from_lines(d_own, dense)
    grads[...] = jnp.zeros_like(grads)
    d_mid[...] = mlp_back(dense[...], mid2[...], hpre2, Rows(lay2, 2), grads, 2)


def back_two_kernel(
    d_mid2, grads2, carry, lay1, lay2, tok2, save, lse, mixed, mid1, hpre1,
    d_mid, grads1, flat, carry2, pa, pb, pc,
    grads, *sc,
):
    layer = Rows(lay2, 2)
    grads[0:1168, :] = grads2[...]
    d = d_mid2[...]
    tokens = tok2[...]
    normed = norm(tokens, layer[0:1, :], layer[1:2, :])
    d_normed = attention_back(d, normed, layer, save, lse, mixed, sc, grads, 2)
    d = d + pre_norm_back(d_normed, tokens, layer, grads, 2)
    grads[1167:1184, :] = carry[3:20, :]
    flatten(grads, 32, CUTS[3] - CUTS[2], flat)
    carry2[...] = grads[0:32, :]
    layer = Rows(lay1, 1)
    d = mlp_back(d, mid1[...], hpre1, layer, grads1, 1)
    d_mid[...] = d
    send_parts(d_mid, pa, pb, pc)


def back_shifted_kernel(
    sizes,
    own, pa, pb, pc, lay1, window, save, lse, mixed, grads1, carry2, _,
    d_window, flat, carry1, qa, qb, qc,
    region, grads, grad, *sc,
):
    put_region(region, sizes, 1)
    take_parts(own, pa, pb, pc, grad)
    grads[0:1168, :] = grads1[...]
    grads[0:3, :] = jnp.zeros((3, WIDE), F32)
    d_window[...] = attention_back(
        grad[...], window[...], Rows(lay1, 1), save, lse, mixed, sc, grads, 1,
        region,
    )
    send_parts(d_window, qa, qb, qc)
    grads[1166:1196, :] = carry2[2:32, :]
    flatten(grads, 12, CUTS[2] - CUTS[1], flat)
    carry1[...] = grads[0:16, :]


def back_first_kernel(
    sizes,
    d_mid, own, qa, qb, qc, tok1, lay0, lay1, merge, dense, tok0, save, lse, mixed, middle, hpre,
    carry1, flat1, flat2, seam, _,
    keep, send,
    flat, grads, grad, *sc,
):
    take_parts(own, qa, qb, qc, grad)
    grads[1556:1572, :] = carry1[...]
    d = d_mid[...] + pre_norm_back(grad[...], tok1[...], Rows(lay1, 1), grads, 1557)
    layer = Rows(lay0, 0)
    at = MERGE_ROWS
    d = mlp_back(d, middle[...], hpre, layer, grads, at)
    tokens = tok0[...]
    normed = norm(tokens, layer[0:1, :], layer[1:2, :])
    d_normed = attention_back(d, normed, layer, save, lse, mixed, sc, grads, at)
    d = d + pre_norm_back(d_normed, tokens, layer, grads, at)
    live = iota((ROWS, WIDE), 0) < VOX
    d = jnp.where(live, d, 0.0)
    hat = merged_norm(dense[...])
    gain = hidden_rows(merge, 0, 1)
    bias = hidden_rows(merge, 4, 1)
    w = merge[8 : 8 + MERGE, :]
    put_hidden_rows(grads, 8 - 8, 1, jnp.zeros((1, MERGE), F32))
    grads[8 : 8 + MERGE, :] = mm_tn(rows_t(d), hat * gain + bias).T
    d_hat = mm_nt(d, w)
    put_hidden_rows(grads, 0, 1, colsum(d_hat * hat))
    put_hidden_rows(grads, 4, 1, colsum(d_hat))
    flatten(grads, 0, CUTS[1], flat)
    at = 0
    for cut, part in ((CUTS[1], flat1), (CUTS[2], flat2), (CUTS[3], seam)):
        at = 3 * cut
        flat[at : at + part.shape[0], :] = part[...]
    at += seam.shape[0]
    if flat.shape[0] > at:
        flat[at:, :] = jnp.zeros((flat.shape[0] - at, WIDE), F32)
    scatter(sizes, flat, 0, keep, send)


def radices(count):
    steps = [2]
    left = count // 2
    while left > 1:
        steps.append(4 if left >= 4 else 2)
        left //= steps[-1]
    return steps


def block_rows(rows, count):
    return -(-rows // (8 * count)) * 8


def own_number(sizes):
    return lax.axis_index("slab") * sizes[1] + lax.axis_index("mp")


def place_in_half(distance, count):
    place = 0
    shift = 1
    for radix in radices(count)[1:]:
        digit = jnp.bitwise_and(lax.shift_right_logical(distance, shift), radix - 1)
        place = place * radix + digit
        shift += radix.bit_length() - 1
    return place


def scatter(sizes, source, first, keep, send):
    count = sizes[0] * sizes[1]
    rows = keep.shape[0] * 2 // count
    me = own_number(sizes)
    odd = jnp.bitwise_and(me, 1)

    def per_pair(t, carry):
        for block, out in ((2 * t + odd, keep), (2 * t + 1 - odd, send)):
            place = place_in_half(jnp.bitwise_xor(block, me), count)
            at = pl.multiple_of(first + block * rows, 8)
            to = pl.multiple_of(place * rows, 8)
            out[pl.ds(to, rows), :] = source[pl.ds(at, rows), :]
        return carry

    lax.fori_loop(0, count // 2, per_pair, 0)


def traded(value, distance, count):
    pairs = [(i, i ^ distance) for i in range(count)]
    return lax.ppermute(value, ("slab", "mp"), pairs)


def later(got, after):
    return got if after is None else list(lax.optimization_barrier((*got, after)))[:-1]


def summing(keep, send, count):
    steps = radices(count)
    got = [keep, traded(send, 1, count)]
    shift = 1
    after = yield None
    for radix in steps[1:]:
        got = later(got, after)
        total = sum(got[1:], got[0])
        rows = total.shape[0] // radix
        parts = [total[k * rows : (k + 1) * rows] for k in range(radix)]
        got = parts[:1] + [traded(parts[k], k << shift, count) for k in range(1, radix)]
        shift += radix.bit_length() - 1
        after = yield parts[0]
    got = later(got, after)
    own = sum(got[1:], got[0])
    for radix in reversed(steps[1:]):
        shift -= radix.bit_length() - 1
        got = [own] + [traded(own, k << shift, count) for k in range(1, radix)]
        after = yield own
        own = jnp.concatenate(later(got, after), 0)
        yield own
    yield own, traded(own, 1, count)


def finished(chain, after=None):
    last = next(chain) if after is None else chain.send(after)
    while not isinstance(last, tuple):
        last = next(chain)
    return last


def exchanged_sum(value, count):
    shift = 0
    for radix in radices(count):
        got = [value] + [traded(value, k << shift, count) for k in range(1, radix)]
        while len(got) > 1:
            got = [got[i] + got[i + 1] for i in range(0, len(got), 2)]
        value = got[0]
        shift += radix.bit_length() - 1
    return value


PIECE = 262144


def adamw_kernel(
    sizes,
    late, late_other, early, early_other, tail, sums, params, first, second,
    new_params, new_first, new_second, loss, valid, norm_out,
    grad, scale_ref,
):
    count = sizes[0] * sizes[1]
    step = pl.program_id(0)

    @pl.when(step == 0)
    def gather():
        me = own_number(sizes)
        total = jnp.zeros((8, WIDE), F32)
        for ref in (late, late_other, early, early_other):
            x = ref[...]
            total = total + jnp.sum((x * x).reshape(-1, 8, WIDE), 0)
        norm = jnp.sqrt(jnp.sum(total))
        loss[0] = jnp.sum(tail[2:3, 0:1])
        valid[0] = jnp.sum(sums[2:3, 0:1])
        norm_out[0] = norm
        scale_ref[0] = jnp.minimum(1.0, clip_norm / (norm + 1e-06))
        start = 0
        for own, other, size in ((late, late_other, LATE_ROWS), (early, early_other, EARLY_ROWS)):
            rows = own.shape[0] * 2 // count

            def per_block(block, carry, own=own, other=other, rows=rows, start=start):
                distance = jnp.bitwise_xor(block, me)
                at = pl.ds(pl.multiple_of(place_in_half(distance, count) * rows, 8), rows)
                near = jnp.bitwise_and(distance, 1) == 0
                to = pl.ds(pl.multiple_of(start + block * rows, 8), rows)
                grad[to, :] = jnp.where(near, own[at, :], other[at, :])
                return carry

            lax.fori_loop(0, size // rows, per_block, 0)
            start += size

    def update(base, low, size):
        rows = -(-size // 1024) * 8
        at = pl.ds(pl.multiple_of(base // WIDE + low // WIDE, 8), rows)
        g = grad[at, :].reshape(rows * WIDE)[:size] * scale_ref[0]
        here = pl.ds(pl.multiple_of(base + low, 1024), size)
        one = beta_one * first[here] + (1.0 - beta_one) * g
        two = beta_two * second[here] + (1.0 - beta_two) * g * g
        there = pl.ds(low, size)
        new_first[there] = one
        new_second[there] = two
        two = two * (1.0 / (1.0 - beta_two**STEP))
        low_by = two * lax.rsqrt(jnp.maximum(two, 1e-37)) + adam_eps
        inverse = pl.reciprocal(low_by, approx=True)
        inverse = inverse * (2.0 - low_by * inverse)
        new_params[there] = params[here] * (1.0 - learn_rate * decay_rate) - (
            one * (learn_rate / (1.0 - beta_one**STEP))
        ) * inverse

    whole = NPARAM // PIECE

    @pl.when(step < whole)
    def full():
        def part(i, carry):
            low = pl.multiple_of(i * 16384, 16384)
            update(step * PIECE, low, 16384)
            return carry

        lax.fori_loop(0, PIECE // 16384, part, 0)

    @pl.when(step == whole)
    def last():
        rest = NPARAM - whole * PIECE
        main = rest // 1024 * 1024
        for low in range(0, main, 16384):
            update(whole * PIECE, low, min(16384, main - low))
        update(whole * PIECE, main, rest - main)


def adamw(sizes, parts, arrays):
    pieces = -(-NPARAM // PIECE)
    piece = pl.BlockSpec((PIECE,), lambda i: (i,))
    vmem = pl.BlockSpec(memory_space=pltpu.VMEM)
    smem = pl.BlockSpec(memory_space=pltpu.SMEM)
    return pl.pallas_call(
        functools.partial(adamw_kernel, sizes),
        grid=(pieces,),
        out_shape=[arr(NPARAM)] * 3 + [arr(1)] * 3,
        in_specs=[vmem] * (len(parts) + len(arrays)),
        out_specs=[piece] * 3 + [smem] * 3,
        scratch_shapes=[pltpu.VMEM((LATE_ROWS + EARLY_ROWS, WIDE), F32), pltpu.SMEM((1,), F32)],
        compiler_params=pltpu.CompilerParams(vmem_limit_bytes=16 * 1024 * 1024),
        cost_estimate=pl.CostEstimate(flops=6 * 10**9, bytes_accessed=0, transcendentals=0),
        name="adamw",
    )(*parts, *arrays)


def arr(*shape):
    return jax.ShapeDtypeStruct(shape, F32)


def call(kernel, outs, scratch, *args, name=None, us=1.0, far=(), mib=16):
    vmem = pl.BlockSpec(memory_space=pltpu.VMEM)
    smem = pl.BlockSpec(memory_space=pltpu.SMEM)
    return pl.pallas_call(
        kernel,
        out_shape=list(outs),
        in_specs=[vmem] * len(args) + [pl.BlockSpec(memory_space=pl.ANY)] * len(far),
        out_specs=[smem if o.shape == (1,) else vmem for o in outs],
        scratch_shapes=list(scratch),
        compiler_params=pltpu.CompilerParams(vmem_limit_bytes=mib * 1024 * 1024),
        cost_estimate=pl.CostEstimate(
            flops=int(us * 1.15e9), bytes_accessed=0, transcendentals=0
        ),
        name=name,
    )(*args, *far)


SQUARE = arr(ROWS, WIDE)
SAVE = arr(ROWS, 3 * WIDE)
FORWARD = [
    pltpu.VMEM((2, KEYS, 2 * WIDE), BF16),
    pltpu.VMEM((2, ROWS, 2 * WIDE), BF16),
    pltpu.VMEM((HEADS, 3 * HDIM, KEYS), BF16),
    pltpu.VMEM((WIDE, KEYS), F32),
    pltpu.VMEM((WIDE, KEYS), F32),
]
BACKWARD = [
    pltpu.VMEM((2, ROWS, 2 * WIDE), BF16),
    pltpu.VMEM((2, KEYS, 2 * WIDE), BF16),
    pltpu.VMEM((2, ROWS, 2 * WIDE), BF16),
    pltpu.VMEM((2, KEYS, 2 * WIDE), BF16),
    pltpu.VMEM((2 * KEYS, 2 * WIDE), BF16),
    pltpu.VMEM((ROWS, WIDE), F32),
    pltpu.VMEM((2, WIDE, KEYS), F32),
    pltpu.VMEM((2, KEYS, 2 * KEYS), BF16),
    pltpu.VMEM((2, KEYS, 2 * KEYS), BF16),
    pltpu.VMEM((2, WIDE, KEYS), BF16),
    pltpu.VMEM((2, WIDE, KEYS), BF16),
    pltpu.VMEM((ROWS, WIDE), F32),
    pltpu.VMEM((ROWS, 2 * KEYS), F32),
    pltpu.VMEM((ROWS, 2 * KEYS), F32),
    pltpu.VMEM((2 * KEYS, 2 * WIDE), BF16),
    pltpu.VMEM((2 * KEYS, 2 * WIDE), BF16),
]
PARTS = [arr(ROWS_A, WIDE), arr(ROWS_B, WIDE), arr(ROWS_C, WIDE)]


def passed(parts, steps, sizes):
    slabs, rows = sizes
    moved = []
    for part, (ds, dm) in zip(parts, ((1, 0), (0, 1), (1, 1))):
        pairs = []
        for s in range(slabs):
            for m in range(rows):
                target = ((s + steps * ds) % slabs) * rows + (m + steps * dm) % rows
                pairs.append((s * rows + m, target))
        moved.append(lax.ppermute(part, ("slab", "mp"), pairs))
    return moved


SIDES = [arr(2 * WIN, 8, WIDE)] * 4


def paired(axis, size):
    near = [(i, i ^ 1) for i in range(size)]
    far = [(i, (i + (1 if i % 2 else -1)) % size) for i in range(size)]
    return (
        lambda value: lax.ppermute(value, axis, near),
        lambda value: lax.ppermute(value, axis, far),
    )


def column_kernel(sizes, near_d, far_d, near_h, far_h, near_out, far_out):
    slab = lax.axis_index("slab")
    odd_d = jnp.bitwise_and(slab, 1) == 1
    odd_h = jnp.bitwise_and(lax.axis_index("mp"), 1) == 1
    at_low = slab == 0
    at_high = slab == sizes[0] - 1
    near_out[4:18] = near_h[...]
    far_out[4:18] = far_h[...]
    for d in range(2):
        near = near_d[d * WIN : (d + 1) * WIN]
        far = far_d[d * WIN : (d + 1) * WIN]
        before = jnp.where(odd_d, near, jnp.where(at_low, 0.0, far))
        after = jnp.where(odd_d, jnp.where(at_high, 0.0, far), near)
        for x, at in ((before, 2 * d), (after, 18 + 2 * d)):
            low, high = x[0:2], x[WIN - 2 : WIN]
            near_out[at : at + 2] = jnp.where(odd_h, low, high)
            far_out[at : at + 2] = jnp.where(odd_h, high, low)


def beside(sides, sizes):
    near, far = paired("slab", sizes[0])
    near_d, far_d = near(sides[0]), far(sides[1])
    near_h, far_h = call(
        functools.partial(column_kernel, sizes), [arr(22, 8, WIDE)] * 2, [],
        near_d, far_d, sides[2], sides[3],
        name="column", us=0.3,
    )
    near, far = paired("mp", sizes[1])
    return near_d, far_d, near(near_h), far(far_h)


REGION = [pltpu.VMEM((ROWS, KEYS), F32)]


def on_device(sizes, feats, labels, valid, params, moment_one, moment_two):
    slabs, rows = sizes
    count = slabs * rows

    def room(spans):
        sizes = [(span_of(groups)[1] + 8) * WIDE for groups in spans]
        return [
            [pltpu.VMEM((size,), F32) for size in sizes],
            pltpu.VMEM((2048, WIDE), F32),
            pltpu.SemaphoreType.DMA((len(spans),)),
        ]

    first_size = FIRST_SPANS[-1][1] * 384
    merge, lay0 = call(
        functools.partial(prep_kernel, FIRST_SPANS),
        [arr(MERGE_ROWS, WIDE), arr(1176, WIDE)],
        room(FIRST_SPANS),
        name="prep_first", us=2.0, far=(params[:first_size],),
    )
    lay1, lay2 = call(
        functools.partial(prep_kernel, LAYER_SPANS),
        [arr(1168, WIDE)] * 2,
        room(LAYER_SPANS),
        name="prep_layers", us=2.0, far=(params,),
    )
    taps_shape = jax.ShapeDtypeStruct((27 * 256, 256), BF16)
    conv0, weights0, bias0 = call(
        prep_conv0_kernel,
        [arr(2596, WIDE), taps_shape, arr(8, WIDE)],
        room(CONV_SPANS[:1]),
        name="prep_conv0", us=1.5, far=(params,),
    )
    conv1, head_w, weights1, vectors = call(
        prep_conv1_kernel,
        [arr(2640, WIDE), arr(WIDE, WIDE), taps_shape, arr(8, WIDE)],
        room(CONV_SPANS[1:]),
        params[NPARAM // WIDE * WIDE :], bias0,
        name="prep_conv1", us=1.5, far=(params,),
    )

    dense, tok0, save0, lse0, mixed0, mid0, hpre0, tok1, ahead, *parts = call(
        first_kernel,
        [arr(ROWS, MERGE), SQUARE, SAVE, SQUARE, SQUARE, SQUARE, arr(ROWS, HID), SQUARE, SQUARE]
        + PARTS,
        FORWARD,
        feats.reshape(PLANE, WIN, MERGE), merge, lay0,
        name="first", us=6.0,
    )
    parts = passed(parts, -1, sizes)
    window, save1, lse1, mixed1, out1, *parts = call(
        functools.partial(shifted_kernel, sizes),
        [SQUARE, SAVE, SQUARE, SQUARE, SQUARE] + PARTS,
        REGION + FORWARD,
        ahead, *parts, lay1,
        name="shifted", us=4.5, far=(weights0,),
    )
    parts = passed(parts, 1, sizes)
    mid1, hpre1, tok2, save2, lse2, mixed2, mid2, hpre2, lines, *sides = call(
        second_kernel,
        [SQUARE, arr(ROWS, HID), SQUARE, SAVE, SQUARE, SQUARE, SQUARE, arr(ROWS, HID)]
        + [arr(PLANE, 8, WIDE)] + SIDES,
        [pltpu.VMEM((ROWS, WIDE), F32)] + FORWARD,
        tok1, out1, *parts, lay1, lay2,
        name="second", us=6.5, far=(weights1,),
    )
    sides = beside(sides, sizes)
    grown, pre, tok3, sums, *tok_sides = call(
        functools.partial(conv_kernel, sizes),
        [arr(11, 12, 8, WIDE), arr(9, 10, 8, WIDE), arr(PLANE, 8, WIDE), arr(8, WIDE)] + SIDES,
        [
            pltpu.VMEM((9, 10, 8, WIDE), F32),
            pltpu.VMEM((880, 2304), BF16),
            pltpu.VMEM((576, 2304), BF16),
            pltpu.VMEM((PLANE, 8, WIDE), F32),
        ],
        lines, *sides, labels, valid, weights0, weights1, vectors,
        name="conv", us=8.0, mib=20,
    )
    tok_sides = beside(tok_sides, sizes)
    side_act, side_grown = call(
        functools.partial(sides_back_kernel, sizes),
        [jax.ShapeDtypeStruct((640, 2304), BF16)] * 2,
        [pltpu.VMEM((10, 10, 8, WIDE), F32)],
        grown, pre,
        name="sides_back", us=2.0,
    )
    weights0, weights1 = call(
        weights_back_kernel,
        [jax.ShapeDtypeStruct((256, 27 * 256), BF16)] * 2,
        [],
        conv0, conv1,
        name="weights_back", us=1.5,
    )
    sums = exchanged_sum(sums, count)
    voxels = WIN * slabs * WIN * rows * WIN
    tok3, slope, tail, d_head, d_rows = call(
        functools.partial(head_kernel, sizes, voxels),
        [arr(11, 12, 8, WIDE), arr(11, 12, 8, WIDE), arr(8, WIDE), arr(WIDE, WIDE), arr(8, WIDE)],
        [],
        tok3, *tok_sides, sums, vectors, head_w,
        name="head", us=3.5,
    )
    tail = exchanged_sum(tail, count)
    late_rows = block_rows(LATE_ROWS, count) * count
    early_rows = block_rows(EARLY_ROWS, count) * count
    seam_rows = LATE_ROWS - 3 * CUTS[3]
    d_own, keep, send, carry3, seam = call(
        functools.partial(conv_back_kernel, sizes),
        [arr(PLANE, 8, WIDE)] + [arr(early_rows // 2, WIDE)] * 2
        + [arr(24, WIDE), arr(seam_rows, WIDE)],
        [
            pltpu.VMEM((5236, WIDE), F32),
            pltpu.VMEM((11, 12, 8, WIDE), F32),
            pltpu.VMEM((10, 10, 8, WIDE), F32),
            pltpu.VMEM((880, 2304), BF16),
            pltpu.VMEM((576, 2304), BF16),
            pltpu.VMEM((seam_rows + early_rows, WIDE), F32),
        ],
        tok3, slope, tail, pre, side_act, side_grown, weights0, weights1, d_rows, d_head,
        name="conv_back", us=14.0, mib=28,
    )
    early = summing(keep, send, count)
    next(early)
    d_mid2, grads2 = call(
        back_mlp_kernel,
        [SQUARE, arr(1168, WIDE)],
        [pltpu.VMEM((ROWS, WIDE), F32)],
        d_own, lay2, mid2, hpre2,
        name="back_mlp", us=3.0,
    )
    step = early.send(d_mid2)
    d_mid, grads1, flat2, carry2, *parts = call(
        back_two_kernel,
        [SQUARE, arr(1168, WIDE), arr(3 * (CUTS[3] - CUTS[2]), WIDE), arr(32, WIDE)] + PARTS,
        [pltpu.VMEM((1184, WIDE), F32)] + BACKWARD,
        d_mid2, grads2, carry3, lay1, lay2, tok2, save2, lse2, mixed2, mid1, hpre1,
        name="back_two", us=9.0,
    )
    parts = passed(parts, -1, sizes)
    step = early.send(d_mid)
    d_window, flat1, carry1, *parts = call(
        functools.partial(back_shifted_kernel, sizes),
        [SQUARE, arr(3 * (CUTS[2] - CUTS[1]), WIDE), arr(16, WIDE)] + PARTS,
        REGION + [pltpu.VMEM((1200, WIDE), F32), pltpu.VMEM((ROWS, WIDE), F32)] + BACKWARD,
        d_mid, *parts, lay1, window, save1, lse1, mixed1, grads1, carry2,
        name="back_shifted", us=10.5, far=(step,),
    )
    early.send(d_window)
    parts = passed(parts, 1, sizes)
    next(early)
    step = next(early)
    late = call(
        functools.partial(back_first_kernel, sizes),
        [arr(late_rows // 2, WIDE)] * 2,
        [
            pltpu.VMEM((late_rows, WIDE), F32),
            pltpu.VMEM((1572, WIDE), F32),
            pltpu.VMEM((ROWS, WIDE), F32),
        ]
        + BACKWARD,
        d_mid, d_window, *parts, tok1, lay0, lay1, merge, dense, tok0, save0, lse0, mixed0, mid0,
        hpre0, carry1, flat1, flat2, seam,
        name="back_first", us=13.5, far=(step,),
    )
    step = early.send(late[0])
    keep, send = later(list(late), step)
    late_sum = finished(summing(keep, send, count))
    early = finished(early)
    new_params, new_first, new_second, loss, valid_count, norm = adamw(
        sizes, (*late_sum, *early, tail, sums), (params, moment_one, moment_two)
    )
    return (
        loss.reshape(()), valid_count.reshape(()), norm.reshape(()),
        new_params, new_first, new_second,
    )


def solution(mesh):
    placed = (
        P("slab", "mp", None, None),
        P("slab", "mp", None),
        P("slab", "mp", None),
        P(),
        P(),
        P(),
    )
    sizes = (mesh.shape["slab"], mesh.shape["mp"])
    return jax.shard_map(
        functools.partial(on_device, sizes),
        mesh=mesh,
        in_specs=placed,
        out_specs=(P(), P(), P(), P(), P(), P()),
        check_vma=False,
    )
```

```python
import functools

import jax
import jax.numpy as jnp
from jax import lax
from jax.experimental import pallas as pl
from jax.experimental.pallas import tpu as pltpu
from jax.sharding import PartitionSpec as P

EMB = 96
HEADS = 6
HDIM = 16
HID = 384
MERGE = 384
CLASSES = 14
WIN = 7
SHIFT = 3
LAYERS = 3
STEP = 10

F32 = jnp.float32
BF16 = jnp.bfloat16
eps_norm = 1e-05
beta_one = 0.9
beta_two = 0.999
adam_eps = 1e-08
learn_rate = 0.05
decay_rate = 0.05
clip_norm = 0.01
LOG2E = 1.4426950408889634

VOX = WIN * WIN * WIN
ROWS = 352
KEYS = 384
BLOCKS = ((0, 128), (128, 256), (256, 352))
WIDE = 128
PLANE = WIN * WIN
FAR = WIN - SHIFT
ROWS_A = SHIFT * FAR * WIN
ROWS_B = FAR * SHIFT * WIN
ROWS_C = SHIFT * SHIFT * WIN

MERGE_ROWS = 392
LAYER_ROWS = 1165
TAP_ROWS = 27 * EMB
GROUPS = 2280
NPARAM = 872558
HEAD_ROW = 6806
HEAD_ROWS = 11
HEAD_LANE = 32
LATE_ROWS = 3072
EARLY_ROWS = 3840
LAYER_BASE = (98, 389, 680)
CONV_BASE = (971, 1620)
CUTS = (0, 392, 688, 976, 2280)

R_QKV, R_QKVB, R_PROJ, R_PROJB = 4, 292, 295, 391
R_HID, R_HIDB, R_OUT, R_OUTB = 392, 776, 780, 1164


def iota(shape, dim):
    return lax.broadcasted_iota(jnp.int32, shape, dim)


def split(x):
    hi = x.astype(BF16)
    return hi, (x - hi.astype(F32)).astype(BF16)


def pair(x):
    return jnp.concatenate(split(x), 1)


def fold(y):
    half = y.shape[1] // 2
    return y[:, :half] + y[:, half:]


def fold_rows(y):
    half = y.shape[0] // 2
    return y[:half] + y[half:]


def dot(a, b):
    return jnp.dot(a, b, preferred_element_type=F32)


def dot_nt(a, b):
    return lax.dot_general(a, b, (((1,), (1,)), ((), ())), preferred_element_type=F32)


def weight_nn(w):
    top = pair(w)
    return jnp.concatenate([top, top], 0)


def weight_nt(w):
    hi, lo = split(w)
    return jnp.concatenate(
        [jnp.concatenate([hi, hi], 1), jnp.concatenate([lo, lo], 1)], 0
    )


def mm(x, w):
    return fold(dot(pair(x), weight_nn(w)))


def mm_nt(x, w):
    return fold(dot_nt(pair(x), weight_nt(w)))


def with_rows(x, rows):
    if x.shape[0] == rows:
        return x
    return jnp.concatenate([x, jnp.zeros((rows - x.shape[0], x.shape[1]), F32)], 0)


def rows_t(x):
    return jnp.concatenate(split(with_rows(x, -(-x.shape[0] // WIDE) * WIDE).T), 0)


def mm_tn(xt, y):
    return fold_rows(fold(dot(xt, pair(with_rows(y, xt.shape[1])))))


def deep(w):
    return jnp.concatenate([w, jnp.zeros((WIDE - EMB, w.shape[1]), F32)], 0)


def roll(x, shift, axis):
    return pltpu.roll(x, shift, axis)


def four_to_three(y):
    lane = iota(y[0].shape, 1)
    a = jnp.where(lane < 96, y[0], roll(y[1], 96, 1))
    b = jnp.where(lane < 64, roll(y[1], 96, 1), roll(y[2], 64, 1))
    c = jnp.where(lane < 32, roll(y[2], 64, 1), roll(y[3], 32, 1))
    return a, b, c


def three_to_four(x):
    lane = iota(x[0].shape, 1)
    live = lane < EMB
    a = x[0]
    b = jnp.where(lane < 32, roll(x[0], 32, 1), roll(x[1], 32, 1))
    c = jnp.where(lane < 64, roll(x[1], 64, 1), roll(x[2], 64, 1))
    d = roll(x[2], 96, 1)
    return tuple(jnp.where(live, v, 0.0) for v in (a, b, c, d))


def hidden_rows(ref, start, count):
    return jnp.concatenate(
        four_to_three([ref[pl.ds(start + c, count, stride=4), :] for c in range(4)]), 1
    )


def put_hidden_rows(ref, start, count, x):
    parts = three_to_four([x[:, i * WIDE : (i + 1) * WIDE] for i in range(3)])
    for c in range(4):
        ref[pl.ds(start + c, count, stride=4), :] = parts[c]


def flatten(ref, start, groups, out):
    parts = four_to_three([ref[pl.ds(start + c, groups, stride=4), :] for c in range(4)])
    for c in range(3):
        out[pl.ds(c, groups, stride=3), :] = parts[c]


def norm_stats(x):
    live = iota(x.shape, 1) < EMB
    mean = jnp.sum(x, 1, keepdims=True) * (1.0 / EMB)
    centred = jnp.where(live, x - mean, 0.0)
    var = jnp.sum(centred * centred, 1, keepdims=True) * (1.0 / EMB)
    inv = lax.rsqrt(var + eps_norm)
    return centred * inv, inv


def norm(x, gain, bias):
    hat, _ = norm_stats(x)
    return hat * gain + bias


def norm_back(hat, inv, gain, grad):
    up = grad * gain
    one = jnp.sum(up, 1, keepdims=True) * (1.0 / EMB)
    two = jnp.sum(up * hat, 1, keepdims=True) * (1.0 / EMB)
    live = iota(hat.shape, 1) < EMB
    return jnp.where(live, inv * (up - one - hat * two), 0.0)


def colsum(x):
    return jnp.sum(x, 0, keepdims=True)


def gelu(x):
    return 0.5 * x * (1.0 + lax.erf(x * (0.5**0.5)))


def gelu_both(x):
    cdf = 0.5 * (1.0 + lax.erf(x * (0.5**0.5)))
    slope = cdf + x * (jnp.exp(x * x * -0.5) * 0.3989422804014327)
    return x * cdf, slope


def head_groups(x):
    lane = iota(x.shape, 1)
    swapped = roll(x, 64, 1)
    return jnp.where(lane < 64, x, swapped), jnp.where(lane < 64, swapped, x)


def as_left(x):
    both = []
    low = iota(x.shape, 1) < 64
    for part in head_groups(x):
        hi = part.astype(BF16).astype(F32)
        one = jnp.where(low, hi, part - hi).astype(BF16)
        both.append(jnp.concatenate([one, one], 1))
    return both


def as_right(x):
    return [pair(part) for part in head_groups(with_rows(x, KEYS))]


def head_mask(h, width):
    lane = iota((1, width), 1)
    lane = jnp.bitwise_and(lane, 63)
    low = jnp.bitwise_and(h, 3) * HDIM
    return jnp.where((lane >= low) & (lane < low + HDIM), 1.0, 0.0)


def own_lanes(h):
    lane = iota((1, WIDE), 1)
    return jnp.where((lane >= h * HDIM) & (lane < (h + 1) * HDIM), 1.0, 0.0)


def score_tiles(s, rows, region):
    tiles = [s[:, i * WIDE : (i + 1) * WIDE] for i in range(3)]
    if region is not None:
        return [t + region[rows, i * WIDE : (i + 1) * WIDE] for i, t in enumerate(tiles)]
    pad = jnp.where(iota((1, WIDE), 1) < VOX - 2 * WIDE, 0.0, -1e30)
    return tiles[:2] + [tiles[2] + pad]


def put_split(ref, rows, i, x):
    hi, lo = split(x)
    ref[rows, i * WIDE : (i + 1) * WIDE] = hi
    ref[rows, KEYS + i * WIDE : KEYS + (i + 1) * WIDE] = lo


def attention(normed, layer, save, lse, mixed, sc, region=None):
    left, right, values = sc
    x = pair(normed)
    qkv = []
    for i in range(3):
        w = deep(layer[pl.ds(R_QKV + i, EMB, stride=3), :])
        y = fold(dot(x, weight_nn(w))) + layer[R_QKVB + i : R_QKVB + i + 1, :]
        if i == 0:
            y = y * (HDIM**-0.5 * LOG2E)
        save[:, i * WIDE : (i + 1) * WIDE] = y
        qkv.append(y)
    for g, part in enumerate(as_left(qkv[0])):
        left[g] = part
    for g, part in enumerate(as_right(qkv[1])):
        right[g] = part
    v = jnp.where(iota((ROWS, WIDE), 1) == EMB, 1.0, qkv[2])
    v = pair(with_rows(v, KEYS))
    values[0:KEYS, :] = v
    values[KEYS : 2 * KEYS, :] = v
    mixed[...] = jnp.zeros_like(mixed)
    lse[...] = jnp.zeros_like(lse)

    def per_pair(pair_of, carry):
        heads = [2 * pair_of, 2 * pair_of + 1]
        masks = [head_mask(h, 2 * WIDE).astype(BF16) for h in heads]
        lanes = [own_lanes(h) for h in heads]
        spots = [jnp.where(iota((1, WIDE), 1) == h, 1.0, 0.0) for h in heads]
        g = lax.div(pair_of, 2)
        for block in BLOCKS:
            rows = slice(*block)
            out = level = 0.0
            for k in range(2):
                s = dot_nt(left[g, rows, :] * masks[k], right[g])
                tiles = score_tiles(s, rows, region)
                top = jnp.maximum(jnp.maximum(tiles[0], tiles[1]), tiles[2])
                top = jnp.max(top, 1, keepdims=True)
                parts = [split(jnp.exp2(t - top)) for t in tiles]
                e = jnp.concatenate([p[0] for p in parts] + [p[1] for p in parts], 1)
                o = fold(dot(e, values[...]))
                total = o[:, EMB : EMB + 1]
                out = out + o * (lanes[k] / total)
                level = level + (top + jnp.log(total) * LOG2E) * spots[k]
            mixed[rows, :] += out
            lse[rows, :] += level
        return carry

    lax.fori_loop(0, HEADS // 2, per_pair, 0)
    proj = deep(layer[R_PROJ : R_PROJ + EMB, :])
    return mm(mixed[...], proj) + layer[R_PROJB : R_PROJB + 1, :]


def attention_back(grad, normed, layer, save, lse, mixed, sc, grads, at, region=None):
    left, right, gleft, vright, keys, dq, dkv_t, weights, slopes = sc[:9]
    q_t, do_t, dmix = sc[9:]
    proj = deep(layer[R_PROJ : R_PROJ + EMB, :])
    grads[at + R_PROJ : at + R_PROJ + EMB, :] = mm_tn(rows_t(mixed[...]), grad)[:EMB]
    grads[at + R_PROJB : at + R_PROJB + 1, :] = colsum(grad)
    d_mixed = mm_nt(grad, proj)
    dmix[...] = d_mixed * mixed[...]
    q, k, v = (save[:, i * WIDE : (i + 1) * WIDE] for i in range(3))
    for g, part in enumerate(as_left(q)):
        left[g] = part
    for g, part in enumerate(as_right(k)):
        right[g] = part
    for g, part in enumerate(as_left(d_mixed)):
        gleft[g] = part
    for g, part in enumerate(as_right(v)):
        vright[g] = part
    kk = pair(with_rows(k, KEYS))
    keys[0:KEYS, :] = kk
    keys[KEYS : 2 * KEYS, :] = kk
    weights[:, ROWS:, :] = jnp.zeros((2, KEYS - ROWS, 2 * KEYS), BF16)
    slopes[:, ROWS:, :] = jnp.zeros((2, KEYS - ROWS, 2 * KEYS), BF16)
    for ref, x in ((q_t, q), (do_t, d_mixed)):
        hi, lo = split(with_rows(x, KEYS).T)
        ref[0] = hi
        ref[1] = lo
    dq[...] = jnp.zeros_like(dq)
    dkv_t[...] = jnp.zeros_like(dkv_t)

    def per_pair(pair_of, carry):
        g = lax.div(pair_of, 2)
        heads = [2 * pair_of, 2 * pair_of + 1]
        masks = [head_mask(h, 2 * WIDE).astype(BF16) for h in heads]
        lanes = [own_lanes(h) for h in heads]
        spots = [jnp.where(iota((1, WIDE), 1) == h, 1.0, 0.0) for h in heads]
        for block in BLOCKS:
            rows = slice(*block)
            out = 0.0
            for k in range(2):
                s = dot_nt(left[g, rows, :] * masks[k], right[g])
                dp = dot_nt(gleft[g, rows, :] * masks[k], vright[g])
                level = jnp.sum(lse[rows, :] * spots[k], 1, keepdims=True)
                delta = jnp.sum(dmix[rows, :] * lanes[k], 1, keepdims=True)
                parts = []
                for i, t in enumerate(score_tiles(s, rows, region)):
                    p = jnp.exp2(t - level)
                    put_split(weights.at[k], rows, i, p)
                    parts.append(split(p * (dp[:, i * WIDE : (i + 1) * WIDE] - delta)))
                ds = jnp.concatenate([p[0] for p in parts] + [p[1] for p in parts], 1)
                slopes[k, rows, :] = ds
                out = out + fold(dot(ds, keys[...])) * lanes[k]
            dq[rows, :] += out
        for k in range(2):
            here = pl.ds(pl.multiple_of((2 * pair_of + k) * HDIM, HDIM), HDIM)
            for i, (t, m) in enumerate(((q_t, slopes), (do_t, weights))):
                lhs = jnp.concatenate([t[0, here, :], t[1, here, :]], 0)
                dkv_t[i, here, :] = fold_rows(fold(dot(lhs, m[k])))
        return carry

    lax.fori_loop(0, HEADS // 2, per_pair, 0)
    d_q = dq[...] * HDIM**-0.5
    d_k = dkv_t[0].T[0:ROWS] * (1.0 / LOG2E)
    d_v = dkv_t[1].T[0:ROWS]
    x_t = rows_t(normed)
    d_normed = None
    for i, d in enumerate((d_q, d_k, d_v)):
        grads[pl.ds(at + R_QKV + i, EMB, stride=3), :] = mm_tn(x_t, d)[:EMB]
        grads[at + R_QKVB + i : at + R_QKVB + i + 1, :] = colsum(d)
        part = mm_nt(d, deep(layer[pl.ds(R_QKV + i, EMB, stride=3), :]))
        d_normed = part if d_normed is None else d_normed + part
    return d_normed


def mlp(middle, layer, hpre):
    normed = norm(middle, layer[2:3, :], layer[3:4, :])
    w = deep(hidden_rows(layer, R_HID, EMB))
    pre = mm(normed, w) + hidden_rows(layer, R_HIDB, 1)
    hpre[...] = pre
    out = mm(gelu(pre), layer[R_OUT : R_OUT + HID, :])
    return middle + out + layer[R_OUTB : R_OUTB + 1, :]


def mlp_back(grad, middle, hpre, layer, grads, at):
    hat, inv = norm_stats(middle)
    normed = hat * layer[2:3, :] + layer[3:4, :]
    act, slope = gelu_both(hpre[...])
    grads[at + R_OUTB : at + R_OUTB + 1, :] = colsum(grad)
    grads[at + R_OUT : at + R_OUT + HID, :] = mm_tn(rows_t(grad), act).T
    d_pre = mm_nt(grad, layer[R_OUT : R_OUT + HID, :]) * slope
    put_hidden_rows(grads, at + R_HIDB, 1, colsum(d_pre))
    put_hidden_rows(grads, at + R_HID, EMB, mm_tn(rows_t(normed), d_pre)[:EMB])
    d_normed = mm_nt(d_pre, deep(hidden_rows(layer, R_HID, EMB)))
    grads[at + 2 : at + 3, :] = colsum(d_normed * hat)
    grads[at + 3 : at + 4, :] = colsum(d_normed)
    return grad + norm_back(hat, inv, layer[2:3, :], d_normed)


def pre_norm_back(grad, tokens, layer, grads, at):
    hat, inv = norm_stats(tokens)
    grads[at : at + 1, :] = colsum(grad * hat)
    grads[at + 1 : at + 2, :] = colsum(grad)
    return norm_back(hat, inv, layer[0:1, :], grad)


def region_of(rows, sizes):
    d = lax.shift_right_logical(rows * 1338, 16)
    line = lax.shift_right_logical(rows * 9363, 16)
    places = (d, line - d * WIN, rows - line * WIN)
    starts = (lax.axis_index("slab") * WIN, lax.axis_index("mp") * WIN, 0)
    total = None
    for place, start, blocks in zip(places, starts, sizes + (1,)):
        turned = jnp.where(place < SHIFT, place + FAR, place - SHIFT) + start
        length = WIN * blocks
        part = jnp.where(turned < length - WIN, 0, jnp.where(turned < length - SHIFT, 1, 2))
        total = part if total is None else total * 3 + part
    return total


def put_region(region, sizes):
    rows = region_of(iota((ROWS, WIDE), 0), sizes)[:, 0:1]
    lanes = region_of(iota((8, KEYS), 1), sizes)[0:1, :]
    apart = jnp.where(rows == lanes, 0.0, -100.0 * LOG2E)
    region[...] = jnp.where(iota((ROWS, KEYS), 1) < VOX, apart, -1e30)


def send_parts(ref, a, b, c):
    far = FAR * WIN
    near = SHIFT * WIN
    for d in range(SHIFT):
        base = d * PLANE
        c[d * near : (d + 1) * near, :] = ref[base : base + near, :]
        a[d * far : (d + 1) * far, :] = ref[base + near : base + PLANE, :]
    for d in range(FAR):
        base = (d + SHIFT) * PLANE
        b[d * near : (d + 1) * near, :] = ref[base : base + near, :]


def take_parts(own, a, b, c, out):
    far = FAR * WIN
    near = SHIFT * WIN
    for d in range(WIN):
        base = d * PLANE
        if d < SHIFT:
            out[base : base + near, :] = c[d * near : (d + 1) * near, :]
            out[base + near : base + PLANE, :] = a[d * far : (d + 1) * far, :]
        else:
            e = d - SHIFT
            out[base : base + near, :] = b[e * near : (e + 1) * near, :]
            out[base + near : base + PLANE, :] = own[base + near : base + PLANE, :]
    out[VOX:, :] = jnp.zeros((ROWS - VOX, WIDE), F32)


def span_of(groups):
    low, high = groups
    first = 3 * low // 8 * 8
    last = -(-3 * high // 8) * 8
    return first, min(last, NPARAM // WIDE // 8 * 8) - first


def copied(params, groups, flat, sem):
    first, rows = span_of(groups)
    size = rows * WIDE
    return pltpu.make_async_copy(
        params.at[pl.ds(first * WIDE, size)], flat.at[pl.ds(0, size)], sem
    )


def relay(groups, flat, out, square, last=None):
    low, high = groups
    first, rows = span_of(groups)
    square[0:rows, :] = flat[0 : rows * WIDE].reshape(rows, WIDE)
    if last is not None:
        square[rows : rows + 24, :] = jnp.zeros((24, WIDE), F32)
        square[rows : rows + 1, 0 : last.shape[0]] = last[...].reshape(1, last.shape[0])
    skip = 3 * low - first
    n = high - low
    parts = three_to_four([square[pl.ds(skip + c, n, stride=3), :] for c in range(3)])
    for c in range(4):
        out[pl.ds(c, n, stride=4), :] = parts[c]


FIRST_SPANS = ((0, 98), (98, 392))
LAYER_SPANS = ((389, 681), (680, 972))
CONV_SPANS = ((971, 1620), (1620, GROUPS))


def prep_kernel(spans, params, *refs, last=None):
    outs, (flats, square, sems) = refs[: len(spans)], refs[-3:]
    for i, groups in enumerate(spans):
        copied(params, groups, flats[i], sems.at[i]).start()
    for i, groups in enumerate(spans):
        copied(params, groups, flats[i], sems.at[i]).wait()
        relay(groups, flats[i], outs[i], square, last if i == len(spans) - 1 else None)


def head_picks():
    width = HEAD_ROWS * WIDE
    place = iota((WIDE, width), 1) - HEAD_LANE
    row = iota((WIDE, width), 0)
    here = (place >= row * CLASSES) & (place < (row + 1) * CLASSES) & (row <= EMB)
    place = iota((width, WIDE), 0) - HEAD_LANE
    col = iota((width, WIDE), 1)
    row = lax.shift_right_logical(place * 4682, 16)
    there = (place - row * CLASSES == col) & (place >= 0)
    return jnp.where(here, 1.0, 0.0), jnp.where(there, 1.0, 0.0).astype(BF16)


def prep_conv0_kernel(params, conv0, weights0, bias, *scratch):
    prep_kernel(CONV_SPANS[:1], params, conv0, *scratch)
    tap_weights(conv0, 3, weights0)
    bias[0:1, :] = conv0[3 + TAP_ROWS : 4 + TAP_ROWS, :]
    bias[1:8, :] = jnp.zeros((7, WIDE), F32)


def prep_conv1_kernel(last, bias, params, conv1, head, weights1, vectors, *scratch):
    prep_kernel(CONV_SPANS[1:], params, conv1, *scratch, last=last)
    tap_weights(conv1, 0, weights1)
    vectors[0:1, :] = bias[0:1, :]
    vectors[1:4, :] = conv1[TAP_ROWS : TAP_ROWS + 3, :]
    vectors[4:8, :] = jnp.zeros((4, WIDE), F32)
    square = scratch[1]
    first, _ = span_of(CONV_SPANS[1])
    row = jnp.concatenate(
        [square[HEAD_ROW + i - first : HEAD_ROW + i - first + 1, :] for i in range(HEAD_ROWS)], 1
    )
    here, there = head_picks()
    hi, lo = split(here * row)
    head[...] = dot(hi, there) + dot(lo, there)


def head_rows(d_head, out, at):
    here, there = head_picks()
    hi, lo = split(d_head)
    spread = (dot_nt(hi, there) + dot_nt(lo, there)) * here
    row = colsum(spread)
    for i in range(HEAD_ROWS):
        out[at + i : at + i + 1, :] += row[:, i * WIDE : (i + 1) * WIDE]


class Rows:
    def __init__(self, ref, at):
        self.ref, self.at = ref, at

    def __getitem__(self, key):
        rows, lanes = key
        if isinstance(rows, slice):
            rows = slice(rows.start + self.at, rows.stop + self.at)
        else:
            rows = pl.ds(rows.start + self.at, rows.size, stride=rows.stride)
        return self.ref[rows, lanes]


def merged_norm(x):
    mean = jnp.sum(x, 1, keepdims=True) * (1.0 / MERGE)
    centred = x - mean
    var = jnp.sum(centred * centred, 1, keepdims=True) * (1.0 / MERGE)
    return centred * lax.rsqrt(var + eps_norm)


def first_kernel(
    feats, merge, lay0,
    dense, tok0, save, lse, mixed, middle, hpre, tok1, ahead, pa, pb, pc,
    *sc,
):
    dense[VOX:, :] = jnp.zeros((ROWS - VOX, MERGE), F32)
    for line in range(PLANE):
        dense[line * WIN : (line + 1) * WIN, :] = feats[line]
    hat = merged_norm(dense[...])
    normed = hat * hidden_rows(merge, 0, 1) + hidden_rows(merge, 4, 1)
    tokens = mm(normed, merge[8 : 8 + MERGE, :])
    tok0[...] = tokens
    layer = Rows(lay0, 0)
    normed = norm(tokens, layer[0:1, :], layer[1:2, :])
    attended = attention(normed, layer, save, lse, mixed, sc)
    mid = tokens + attended
    middle[...] = mid
    tokens = mlp(mid, layer, hpre)
    tok1[...] = tokens
    ahead[...] = norm(tokens, layer[1165:1166, :], layer[1166:1167, :])
    send_parts(ahead, pa, pb, pc)


def shifted_kernel(
    sizes,
    own, pa, pb, pc, lay1, _,
    window, save, lse, mixed, out, qa, qb, qc,
    region, *sc,
):
    put_region(region, sizes)
    take_parts(own, pa, pb, pc, window)
    out[...] = attention(
        window[...], Rows(lay1, 1), save, lse, mixed, sc, region
    )
    send_parts(out, qa, qb, qc)


def to_lines(ref, out):
    for line in range(PLANE):
        out[line, 0:WIN, :] = ref[line * WIN : (line + 1) * WIN, :]
        out[line, WIN:8, :] = jnp.zeros((8 - WIN, WIDE), F32)


def from_lines(ref, out):
    out[VOX:, :] = jnp.zeros((ROWS - VOX, WIDE), F32)
    for line in range(PLANE):
        out[line * WIN : (line + 1) * WIN, :] = ref[line, 0:WIN, :]


def send_sides(lines, near_d, far_d, near_h, far_h):
    odd_d = jnp.bitwise_and(lax.axis_index("slab"), 1) == 1
    odd_h = jnp.bitwise_and(lax.axis_index("mp"), 1) == 1
    low, high = lines[0 : 2 * WIN], lines[(WIN - 2) * WIN : PLANE]
    near_d[...] = jnp.where(odd_d, low, high)
    far_d[...] = jnp.where(odd_d, high, low)
    for d in range(WIN):
        low = lines[d * WIN : d * WIN + 2]
        high = lines[d * WIN + WIN - 2 : (d + 1) * WIN]
        near_h[2 * d : 2 * d + 2] = jnp.where(odd_h, low, high)
        far_h[2 * d : 2 * d + 2] = jnp.where(odd_h, high, low)


def second_kernel(
    tok1, own, qa, qb, qc, lay1, lay2, _,
    mid1, hpre1, tok2, save, lse, mixed, mid2, hpre2, lines,
    s0, s1, s2, s3,
    attended, *sc,
):
    take_parts(own, qa, qb, qc, attended)
    mid = tok1[...] + attended[...]
    mid1[...] = mid
    tokens = mlp(mid, Rows(lay1, 1), hpre1)
    tok2[...] = tokens
    layer = Rows(lay2, 2)
    normed = norm(tokens, layer[0:1, :], layer[1:2, :])
    mid = tokens + attention(normed, layer, save, lse, mixed, sc)
    mid2[...] = mid
    attended[...] = mlp(mid, layer, hpre2)
    to_lines(attended, lines)
    send_sides(lines, s0, s1, s2, s3)


def grown_lines(sizes, own, near_d, far_d, near_h, far_h, out):
    slab, row = lax.axis_index("slab"), lax.axis_index("mp")
    odd_d = jnp.bitwise_and(slab, 1) == 1
    odd_h = jnp.bitwise_and(row, 1) == 1
    out[:, 11:12] = jnp.zeros((11, 1, 8, WIDE), F32)
    for d in range(WIN):
        out[d + 2, 2 : 2 + WIN] = own[d * WIN : (d + 1) * WIN]
    for d in range(2):
        near = near_d[d * WIN : (d + 1) * WIN]
        far = far_d[d * WIN : (d + 1) * WIN]
        out[d, 2 : 2 + WIN] = jnp.where(odd_d, near, jnp.where(slab == 0, 0.0, far))
        out[d + 9, 2 : 2 + WIN] = jnp.where(
            odd_d, jnp.where(slab == sizes[0] - 1, 0.0, far), near
        )
    for d in range(11):
        near = near_h[2 * d : 2 * d + 2]
        far = far_h[2 * d : 2 * d + 2]
        out[d, 0:2] = jnp.where(odd_h, near, jnp.where(row == 0, 0.0, far))
        out[d, 9:11] = jnp.where(odd_h, jnp.where(row == sizes[1] - 1, 0.0, far), near)


def put_marks(labels, valid, out):
    across = iota((8, WIN), 1) == iota((8, WIN), 0)
    classes = iota((8, WIDE), 1) - EMB
    for d in range(WIN):
        code = jnp.where(valid[d] == 1, labels[d], -1 - EMB - WIDE)
        code = code.astype(F32)
        for h in range(WIN):
            line = jnp.where(across, code[h : h + 1, :], 0.0)
            column = jnp.sum(line, 1, keepdims=True)
            mark = jnp.where(column == classes.astype(F32), 1.0, 0.0)
            out[d * WIN + h] = jnp.where(iota((8, WIDE), 0) < WIN, mark, 0.0)


def taps(source, first_plane, planes, first_line, lines, out):
    def per_plane(d, carry):
        for c in range(3):
            for b in range(3):
                x = source[d + first_plane, first_line + b : first_line + b + lines]
                if c != 1:
                    x = roll(x, 1 if c == 0 else 7, 1)
                x = pair(x.reshape(lines * 8, WIDE))
                at = pl.multiple_of(d * (lines * 8), lines * 8)
                t = b * 3 + c
                out[pl.ds(at, lines * 8), t * 256 : (t + 1) * 256] = x
        return carry

    lax.fori_loop(0, planes, per_plane, 0)


def tap_weights(ref, at, out):
    def per_tap(i, carry):
        w = deep(ref[pl.ds(i * EMB + at, EMB), :])
        out[pl.ds(pl.multiple_of(i * 256, 256), 256), :] = weight_nn(w)
        return carry

    lax.fori_loop(0, 27, per_tap, 0)


def tap_weights_back(ref, at, out):
    for i in range(27):
        w = deep(ref[(26 - i) * EMB + at : (27 - i) * EMB + at, :])
        out[:, i * 256 : (i + 1) * 256] = weight_nt(w)


def conv(side, weights, planes, pitch, at_once, put, back=False):
    rows = at_once * pitch
    for start in range(0, planes, at_once):
        total = None
        for a in range(3):
            low = (start + a) * pitch
            x = side[low : low + rows, :]
            if back:
                part = dot_nt(x, weights[:, a * 2304 : (a + 1) * 2304])
            else:
                part = dot(x, weights[a * 2304 : (a + 1) * 2304, :])
            total = part if total is None else total + part
        put(start, fold(total))


def conv_weight_grad(side, grad_rows, pitch, out, at):
    rows = 512
    g = jnp.concatenate([grad_rows, jnp.zeros((rows - grad_rows.shape[0], WIDE), F32)], 0)
    left = jnp.concatenate(split(g.T[:EMB]), 0)
    for a in range(3):
        for bc in range(9):
            y = dot(left, side[a * pitch : a * pitch + rows, bc * 256 : (bc + 1) * 256])
            y = deep(fold_rows(fold(y))).T
            t = a * 9 + bc
            out[at + t * EMB : at + (t + 1) * EMB, :] = y[:EMB]


def volume_mask(sizes, planes, lines, reach, real_lines):
    slab, row = lax.axis_index("slab"), lax.axis_index("mp")
    ends = (slab == 0, slab == sizes[0] - 1, row == 0, row == sizes[1] - 1)
    shape = (planes, lines, 8, WIDE)
    d, h, w = iota(shape, 0), iota(shape, 1), iota(shape, 2)
    low_d = jnp.where(ends[0], reach, 0)
    high_d = jnp.where(ends[1], planes - reach, planes)
    low_h = jnp.where(ends[2], reach, 0)
    high_h = jnp.where(ends[3], real_lines - reach, real_lines)
    inside = (d >= low_d) & (d < high_d) & (h >= low_h) & (h < high_h) & (w < WIN)
    return jnp.where(inside, 1.0, 0.0)


def conv_kernel(
    sizes,
    own, s0, s1, s2, s3, labels, valid, weights0, weights1, vectors,
    grown, pre, tok, stats, t0, t1, t2, t3,
    act, side, side_own, marks,
):
    grown_lines(sizes, own, s0, s1, s2, s3, grown)
    put_marks(labels, valid, marks)
    taps(grown, 0, 11, 0, 10, side)
    bias0 = vectors[0:1, :]
    inside = volume_mask(sizes, 9, 10, 1, 9)


    def put(start, y):
        z = (y + bias0).reshape(3, 10, 8, WIDE)
        pre[start : start + 3] = z
        act[start : start + 3] = gelu(z) * inside[start : start + 3]

    conv(side, weights0, 9, 80, 3, put)
    taps(act, 0, 9, 0, 8, side_own)
    bias1 = vectors[1:2, :]
    sums = []

    def put_own(start, y):
        y = (y + bias1).reshape(WIN, 8, 8, WIDE)[:, 0:WIN]
        y = y + own[...].reshape(WIN, WIN, 8, WIDE)
        y = jnp.where(iota(y.shape, 2) < WIN, y, 0.0).reshape(PLANE, 8, WIDE)
        tok[...] = y + marks[...]
        send_sides(tok, t0, t1, t2, t3)
        flat = y.reshape(PLANE * 8, WIDE)
        sums.append(colsum(flat))
        sums.append(colsum(flat * flat))

    conv(side_own, weights1, WIN, 64, WIN, put_own)
    count = jnp.sum(marks[...].reshape(PLANE * 8, WIDE))
    row = iota((8, WIDE), 0)
    stats[...] = (
        jnp.where(row == 0, sums[0], 0.0)
        + jnp.where(row == 1, sums[1], 0.0)
        + jnp.where(row == 2, count, 0.0)
    )


def head_kernel(
    sizes, voxels,
    own, s0, s1, s2, s3, sums, vectors, head_w,
    grown, slope_out, stats, d_head, d_rows,
):
    grown_lines(sizes, own, s0, s1, s2, s3, grown)
    rows = 11 * 12 * 8
    both = grown[...].reshape(rows, WIDE)
    lane = iota((rows, WIDE), 1)
    tokens = jnp.where(lane < EMB, both, 0.0)
    target = jnp.where(lane < CLASSES, roll(both, WIDE - EMB, 1), 0.0)
    live = jnp.sum(target, 1, keepdims=True)
    count = F32(voxels)
    average = sums[0:1, :] / count
    spread = sums[1:2, :] / count - average * average
    inv = lax.rsqrt(spread + eps_norm)
    gain = vectors[2:3, :]
    bias = vectors[3:4, :]
    hat = (tokens - average) * inv
    act, slope = gelu_both(hat * gain + bias)
    act = jnp.where(lane == EMB, 1.0, act)
    w = head_w[...]
    logits = mm(act, w)
    logits = jnp.where(lane < CLASSES, logits, -1e30)
    top = jnp.max(logits, 1, keepdims=True)
    e = jnp.exp(logits - top)
    total = jnp.sum(e, 1, keepdims=True)
    logp = logits - top - jnp.log(total)
    scale = 1.0 / sums[2:3, 0:1]
    d_logits = (e / total * live - target) * scale
    d_normed = jnp.where(lane < EMB, mm_nt(d_logits, w) * slope, 0.0)
    d_tokens = d_normed * gain * inv
    slope_out[...] = d_tokens.reshape(11, 12, 8, WIDE)

    def own_rows(x):
        x = x.reshape(11, 12, 8, WIDE)[2:9, 2:9]
        x = jnp.where(iota(x.shape, 2) < WIN, x, 0.0)
        return x.reshape(PLANE * 8, WIDE)

    loss = -jnp.sum(own_rows(target * jnp.where(lane < CLASSES, logp, 0.0)))
    own_d = own_rows(d_logits)
    own_n = own_rows(d_normed)
    own_hat = own_rows(hat)
    zeros = jnp.zeros((512 - PLANE * 8, WIDE), F32)
    left = rows_t(jnp.concatenate([own_d, zeros], 0))
    d_head[...] = mm_tn(left, jnp.concatenate([own_rows(act), zeros], 0)).T
    d_gain = colsum(own_n * own_hat)
    d_bias = colsum(own_n)
    d_average = -d_bias * gain * inv
    d_spread = d_gain * gain * inv * inv * -0.5
    d_two = d_spread / count
    d_one = (d_average - 2.0 * average * d_spread) / count
    row = iota((8, WIDE), 0)
    live_lane = iota((8, WIDE), 1) < EMB
    stats[...] = (
        jnp.where((row == 0) & live_lane, d_one, 0.0)
        + jnp.where((row == 1) & live_lane, d_two, 0.0)
        + jnp.where(row == 2, loss, 0.0)
    )
    d_rows[...] = (
        jnp.where(row == 0, d_gain, 0.0)
        + jnp.where(row == 1, d_bias, 0.0)
    )


def sides_back_kernel(sizes, grown, pre, side_act, side_grown, act):
    act[0:9] = gelu(pre[...]) * volume_mask(sizes, 9, 10, 1, 9)
    act[9:10] = jnp.zeros((1, 10, 8, WIDE), F32)
    taps(act, 0, 10, 0, 8, side_act)
    taps(grown, 1, 10, 1, 8, side_grown)


def weights_back_kernel(conv0, conv1, weights0, weights1):
    tap_weights_back(conv0, 3, weights0)
    tap_weights_back(conv1, 0, weights1)


def conv_back_kernel(
    sizes,
    tok, slope, sums, pre, side_act, side_grown, weights0, weights1, d_rows, d_head,
    d_own, keep, send, carry, seam,
    grads, dgrown, act, side, side_own, flat,
):
    lane = iota((11, 12, 8, WIDE), 3)
    inside = volume_mask(sizes, 11, 12, 2, 11)
    steady = sums[0:1, :].reshape(1, 1, 1, WIDE)
    rising = 2.0 * sums[1:2, :].reshape(1, 1, 1, WIDE)
    d_tok = slope[...] + jnp.where(lane < EMB, (steady + tok[...] * rising) * inside, 0.0)
    dgrown[...] = d_tok
    grads[5191:, :] = jnp.zeros((45, WIDE), F32)
    grads[0:8, :] = jnp.zeros((8, WIDE), F32)
    grads[5189:5191, :] = d_rows[0:2, :]
    own = dgrown[2:9, 2:10]
    line = iota(own.shape, 1)
    own = jnp.where(line < WIN, own, 0.0).reshape(WIN * 64, WIDE)
    grads[5188:5189, :] = colsum(own)

    near = volume_mask(sizes, 9, 10, 1, 9)
    conv_weight_grad(side_act, own, 64, grads, 2596)
    taps(dgrown, 0, 11, 0, 10, side)


    def put(start, y):
        _, s = gelu_both(pre[start : start + 3])
        act[start : start + 3] = y.reshape(3, 10, 8, WIDE) * s * near[start : start + 3]

    conv(side, weights1, 9, 80, 3, put, back=True)

    own = act[1:8, 1:9]
    line = iota(own.shape, 1)
    own = jnp.where(line < WIN, own, 0.0).reshape(WIN * 64, WIDE)
    grads[2595:2596, :] = colsum(own)
    conv_weight_grad(side_grown, own, 64, grads, 3)
    carry[...] = grads[0:24, :]
    flat[3 * (GROUPS - CUTS[3]) :, :] = jnp.zeros((flat.shape[0] - 3912, WIDE), F32)
    flatten(grads, 20, GROUPS - CUTS[3], flat)
    start = 3 * CUTS[3]
    head_rows(d_head[...], flat, HEAD_ROW - start)
    seam[...] = flat[0 : LATE_ROWS - start, :]
    scatter(sizes, flat, LATE_ROWS - start, keep, send)
    taps(act, 0, 9, 0, 8, side_own)

    def put_own(start, y):
        y = y.reshape(WIN, 8, 8, WIDE)[:, 0:WIN] + dgrown[2:9, 2:9]
        y = jnp.where(iota(y.shape, 2) < WIN, y, 0.0)
        d_own[...] = y.reshape(PLANE, 8, WIDE)

    conv(side_own, weights0, WIN, 64, WIN, put_own, back=True)


def back_mlp_kernel(d_own, lay2, mid2, hpre2, d_mid, grads, dense):
    from_lines(d_own, dense)
    grads[...] = jnp.zeros_like(grads)
    d_mid[...] = mlp_back(dense[...], mid2[...], hpre2, Rows(lay2, 2), grads, 2)


def back_two_kernel(
    d_mid2, grads2, carry, lay1, lay2, tok2, save, lse, mixed, mid1, hpre1,
    d_mid, grads1, flat, carry2, pa, pb, pc,
    grads, *sc,
):
    layer = Rows(lay2, 2)
    grads[0:1168, :] = grads2[...]
    d = d_mid2[...]
    tokens = tok2[...]
    normed = norm(tokens, layer[0:1, :], layer[1:2, :])
    d_normed = attention_back(d, normed, layer, save, lse, mixed, sc, grads, 2)
    d = d + pre_norm_back(d_normed, tokens, layer, grads, 2)
    grads[1167:1184, :] = carry[3:20, :]
    flatten(grads, 32, CUTS[3] - CUTS[2], flat)
    carry2[...] = grads[0:32, :]
    layer = Rows(lay1, 1)
    d = mlp_back(d, mid1[...], hpre1, layer, grads1, 1)
    d_mid[...] = d
    send_parts(d_mid, pa, pb, pc)


def back_shifted_kernel(
    sizes,
    own, pa, pb, pc, lay1, window, save, lse, mixed, grads1, carry2, _,
    d_window, flat, carry1, qa, qb, qc,
    region, grads, grad, *sc,
):
    put_region(region, sizes)
    take_parts(own, pa, pb, pc, grad)
    grads[0:1168, :] = grads1[...]
    grads[0:3, :] = jnp.zeros((3, WIDE), F32)
    d_window[...] = attention_back(
        grad[...], window[...], Rows(lay1, 1), save, lse, mixed, sc, grads, 1,
        region,
    )
    send_parts(d_window, qa, qb, qc)
    grads[1166:1196, :] = carry2[2:32, :]
    flatten(grads, 12, CUTS[2] - CUTS[1], flat)
    carry1[...] = grads[0:16, :]


def back_first_kernel(
    sizes,
    d_mid, own, qa, qb, qc, tok1, lay0, lay1, merge, dense, tok0, save, lse, mixed, middle, hpre,
    carry1, flat1, flat2, seam, _,
    keep, send,
    flat, grads, grad, *sc,
):
    take_parts(own, qa, qb, qc, grad)
    grads[1556:1572, :] = carry1[...]
    d = d_mid[...] + pre_norm_back(grad[...], tok1[...], Rows(lay1, 1), grads, 1557)
    layer = Rows(lay0, 0)
    at = MERGE_ROWS
    d = mlp_back(d, middle[...], hpre, layer, grads, at)
    tokens = tok0[...]
    normed = norm(tokens, layer[0:1, :], layer[1:2, :])
    d_normed = attention_back(d, normed, layer, save, lse, mixed, sc, grads, at)
    d = d + pre_norm_back(d_normed, tokens, layer, grads, at)
    live = iota((ROWS, WIDE), 0) < VOX
    d = jnp.where(live, d, 0.0)
    hat = merged_norm(dense[...])
    gain = hidden_rows(merge, 0, 1)
    bias = hidden_rows(merge, 4, 1)
    w = merge[8 : 8 + MERGE, :]
    put_hidden_rows(grads, 8 - 8, 1, jnp.zeros((1, MERGE), F32))
    grads[8 : 8 + MERGE, :] = mm_tn(rows_t(d), hat * gain + bias).T
    d_hat = mm_nt(d, w)
    put_hidden_rows(grads, 0, 1, colsum(d_hat * hat))
    put_hidden_rows(grads, 4, 1, colsum(d_hat))
    flatten(grads, 0, CUTS[1], flat)
    at = 0
    for cut, part in ((CUTS[1], flat1), (CUTS[2], flat2), (CUTS[3], seam)):
        at = 3 * cut
        flat[at : at + part.shape[0], :] = part[...]
    at += seam.shape[0]
    if flat.shape[0] > at:
        flat[at:, :] = jnp.zeros((flat.shape[0] - at, WIDE), F32)
    scatter(sizes, flat, 0, keep, send)


def radices(count):
    steps = [2]
    left = count // 2
    while left > 1:
        steps.append(4 if left >= 4 else 2)
        left //= steps[-1]
    return steps


def block_rows(rows, count):
    return -(-rows // (8 * count)) * 8


def own_number(sizes):
    return lax.axis_index("slab") * sizes[1] + lax.axis_index("mp")


def place_in_half(distance, count):
    place = 0
    shift = 1
    for radix in radices(count)[1:]:
        digit = jnp.bitwise_and(lax.shift_right_logical(distance, shift), radix - 1)
        place = place * radix + digit
        shift += radix.bit_length() - 1
    return place


def scatter(sizes, source, first, keep, send):
    count = sizes[0] * sizes[1]
    rows = keep.shape[0] * 2 // count
    me = own_number(sizes)
    odd = jnp.bitwise_and(me, 1)

    def per_pair(t, carry):
        for block, out in ((2 * t + odd, keep), (2 * t + 1 - odd, send)):
            place = place_in_half(jnp.bitwise_xor(block, me), count)
            at = pl.multiple_of(first + block * rows, 8)
            to = pl.multiple_of(place * rows, 8)
            out[pl.ds(to, rows), :] = source[pl.ds(at, rows), :]
        return carry

    lax.fori_loop(0, count // 2, per_pair, 0)


def traded(value, distance, count):
    pairs = [(i, i ^ distance) for i in range(count)]
    return lax.ppermute(value, ("slab", "mp"), pairs)


def later(got, after):
    return got if after is None else list(lax.optimization_barrier((*got, after)))[:-1]


def summing(keep, send, count):
    steps = radices(count)
    got = [keep, traded(send, 1, count)]
    shift = 1
    after = yield None
    for radix in steps[1:]:
        got = later(got, after)
        total = sum(got[1:], got[0])
        rows = total.shape[0] // radix
        parts = [total[k * rows : (k + 1) * rows] for k in range(radix)]
        got = parts[:1] + [traded(parts[k], k << shift, count) for k in range(1, radix)]
        shift += radix.bit_length() - 1
        after = yield parts[0]
    got = later(got, after)
    own = sum(got[1:], got[0])
    for radix in reversed(steps[1:]):
        shift -= radix.bit_length() - 1
        got = [own] + [traded(own, k << shift, count) for k in range(1, radix)]
        after = yield own
        own = jnp.concatenate(later(got, after), 0)
        yield own
    yield own, traded(own, 1, count)


def finished(chain, after=None):
    last = next(chain) if after is None else chain.send(after)
    while not isinstance(last, tuple):
        last = next(chain)
    return last


def exchanged_sum(value, count):
    shift = 0
    for radix in radices(count):
        got = [value] + [traded(value, k << shift, count) for k in range(1, radix)]
        while len(got) > 1:
            got = [got[i] + got[i + 1] for i in range(0, len(got), 2)]
        value = got[0]
        shift += radix.bit_length() - 1
    return value


PIECE = 262144


def adamw_kernel(
    sizes,
    late, late_other, early, early_other, tail, sums, params, first, second,
    new_params, new_first, new_second, loss, valid, norm_out,
    grad, scale_ref,
):
    count = sizes[0] * sizes[1]
    step = pl.program_id(0)

    @pl.when(step == 0)
    def gather():
        me = own_number(sizes)
        total = jnp.zeros((8, WIDE), F32)
        for ref in (late, late_other, early, early_other):
            x = ref[...]
            total = total + jnp.sum((x * x).reshape(-1, 8, WIDE), 0)
        norm = jnp.sqrt(jnp.sum(total))
        loss[0] = jnp.sum(tail[2:3, 0:1])
        valid[0] = jnp.sum(sums[2:3, 0:1])
        norm_out[0] = norm
        scale_ref[0] = jnp.minimum(1.0, clip_norm / (norm + 1e-06))
        start = 0
        for own, other, size in ((late, late_other, LATE_ROWS), (early, early_other, EARLY_ROWS)):
            rows = own.shape[0] * 2 // count

            def per_block(block, carry, own=own, other=other, rows=rows, start=start):
                distance = jnp.bitwise_xor(block, me)
                at = pl.ds(pl.multiple_of(place_in_half(distance, count) * rows, 8), rows)
                near = jnp.bitwise_and(distance, 1) == 0
                to = pl.ds(pl.multiple_of(start + block * rows, 8), rows)
                grad[to, :] = jnp.where(near, own[at, :], other[at, :])
                return carry

            lax.fori_loop(0, size // rows, per_block, 0)
            start += size

    def update(base, low, size):
        rows = -(-size // 1024) * 8
        at = pl.ds(pl.multiple_of(base // WIDE + low // WIDE, 8), rows)
        g = grad[at, :].reshape(rows * WIDE)[:size] * scale_ref[0]
        here = pl.ds(pl.multiple_of(base + low, 1024), size)
        one = beta_one * first[here] + (1.0 - beta_one) * g
        two = beta_two * second[here] + (1.0 - beta_two) * g * g
        there = pl.ds(low, size)
        new_first[there] = one
        new_second[there] = two
        two = two * (1.0 / (1.0 - beta_two**STEP))
        low_by = two * lax.rsqrt(jnp.maximum(two, 1e-37)) + adam_eps
        inverse = pl.reciprocal(low_by, approx=True)
        inverse = inverse * (2.0 - low_by * inverse)
        new_params[there] = params[here] * (1.0 - learn_rate * decay_rate) - (
            one * (learn_rate / (1.0 - beta_one**STEP))
        ) * inverse

    whole = NPARAM // PIECE

    @pl.when(step < whole)
    def full():
        def part(i, carry):
            low = pl.multiple_of(i * 16384, 16384)
            update(step * PIECE, low, 16384)
            return carry

        lax.fori_loop(0, PIECE // 16384, part, 0)

    @pl.when(step == whole)
    def last():
        rest = NPARAM - whole * PIECE
        main = rest // 1024 * 1024
        for low in range(0, main, 16384):
            update(whole * PIECE, low, min(16384, main - low))
        update(whole * PIECE, main, rest - main)


def adamw(sizes, parts, arrays):
    pieces = -(-NPARAM // PIECE)
    piece = pl.BlockSpec((PIECE,), lambda i: (i,))
    vmem = pl.BlockSpec(memory_space=pltpu.VMEM)
    smem = pl.BlockSpec(memory_space=pltpu.SMEM)
    return pl.pallas_call(
        functools.partial(adamw_kernel, sizes),
        grid=(pieces,),
        out_shape=[arr(NPARAM)] * 3 + [arr(1)] * 3,
        in_specs=[vmem] * (len(parts) + len(arrays)),
        out_specs=[piece] * 3 + [smem] * 3,
        scratch_shapes=[pltpu.VMEM((LATE_ROWS + EARLY_ROWS, WIDE), F32), pltpu.SMEM((1,), F32)],
        compiler_params=pltpu.CompilerParams(vmem_limit_bytes=16 * 1024 * 1024),
        cost_estimate=pl.CostEstimate(flops=6 * 10**9, bytes_accessed=0, transcendentals=0),
        name="adamw",
    )(*parts, *arrays)


def arr(*shape):
    return jax.ShapeDtypeStruct(shape, F32)


def call(kernel, outs, scratch, *args, name=None, us=1.0, far=(), mib=16):
    vmem = pl.BlockSpec(memory_space=pltpu.VMEM)
    smem = pl.BlockSpec(memory_space=pltpu.SMEM)
    return pl.pallas_call(
        kernel,
        out_shape=list(outs),
        in_specs=[vmem] * len(args) + [pl.BlockSpec(memory_space=pl.ANY)] * len(far),
        out_specs=[smem if o.shape == (1,) else vmem for o in outs],
        scratch_shapes=list(scratch),
        compiler_params=pltpu.CompilerParams(vmem_limit_bytes=mib * 1024 * 1024),
        cost_estimate=pl.CostEstimate(
            flops=int(us * 1.15e9), bytes_accessed=0, transcendentals=0
        ),
        name=name,
    )(*args, *far)


SQUARE = arr(ROWS, WIDE)
SAVE = arr(ROWS, 3 * WIDE)
FORWARD = [
    pltpu.VMEM((2, ROWS, 2 * WIDE), BF16),
    pltpu.VMEM((2, KEYS, 2 * WIDE), BF16),
    pltpu.VMEM((2 * KEYS, 2 * WIDE), BF16),
]
BACKWARD = [
    pltpu.VMEM((2, ROWS, 2 * WIDE), BF16),
    pltpu.VMEM((2, KEYS, 2 * WIDE), BF16),
    pltpu.VMEM((2, ROWS, 2 * WIDE), BF16),
    pltpu.VMEM((2, KEYS, 2 * WIDE), BF16),
    pltpu.VMEM((2 * KEYS, 2 * WIDE), BF16),
    pltpu.VMEM((ROWS, WIDE), F32),
    pltpu.VMEM((2, WIDE, KEYS), F32),
    pltpu.VMEM((2, KEYS, 2 * KEYS), BF16),
    pltpu.VMEM((2, KEYS, 2 * KEYS), BF16),
    pltpu.VMEM((2, WIDE, KEYS), BF16),
    pltpu.VMEM((2, WIDE, KEYS), BF16),
    pltpu.VMEM((ROWS, WIDE), F32),
]
PARTS = [arr(ROWS_A, WIDE), arr(ROWS_B, WIDE), arr(ROWS_C, WIDE)]


def passed(parts, steps, sizes):
    slabs, rows = sizes
    moved = []
    for part, (ds, dm) in zip(parts, ((1, 0), (0, 1), (1, 1))):
        pairs = []
        for s in range(slabs):
            for m in range(rows):
                target = ((s + steps * ds) % slabs) * rows + (m + steps * dm) % rows
                pairs.append((s * rows + m, target))
        moved.append(lax.ppermute(part, ("slab", "mp"), pairs))
    return moved


SIDES = [arr(2 * WIN, 8, WIDE)] * 4


def paired(axis, size):
    near = [(i, i ^ 1) for i in range(size)]
    far = [(i, (i + (1 if i % 2 else -1)) % size) for i in range(size)]
    return (
        lambda value: lax.ppermute(value, axis, near),
        lambda value: lax.ppermute(value, axis, far),
    )


def column_kernel(sizes, near_d, far_d, near_h, far_h, near_out, far_out):
    slab = lax.axis_index("slab")
    odd_d = jnp.bitwise_and(slab, 1) == 1
    odd_h = jnp.bitwise_and(lax.axis_index("mp"), 1) == 1
    at_low = slab == 0
    at_high = slab == sizes[0] - 1
    near_out[4:18] = near_h[...]
    far_out[4:18] = far_h[...]
    for d in range(2):
        near = near_d[d * WIN : (d + 1) * WIN]
        far = far_d[d * WIN : (d + 1) * WIN]
        before = jnp.where(odd_d, near, jnp.where(at_low, 0.0, far))
        after = jnp.where(odd_d, jnp.where(at_high, 0.0, far), near)
        for x, at in ((before, 2 * d), (after, 18 + 2 * d)):
            low, high = x[0:2], x[WIN - 2 : WIN]
            near_out[at : at + 2] = jnp.where(odd_h, low, high)
            far_out[at : at + 2] = jnp.where(odd_h, high, low)


def beside(sides, sizes):
    near, far = paired("slab", sizes[0])
    near_d, far_d = near(sides[0]), far(sides[1])
    near_h, far_h = call(
        functools.partial(column_kernel, sizes), [arr(22, 8, WIDE)] * 2, [],
        near_d, far_d, sides[2], sides[3],
        name="column", us=0.3,
    )
    near, far = paired("mp", sizes[1])
    return near_d, far_d, near(near_h), far(far_h)


REGION = [pltpu.VMEM((ROWS, KEYS), F32)]


def on_device(sizes, feats, labels, valid, params, moment_one, moment_two):
    slabs, rows = sizes
    count = slabs * rows

    def room(spans):
        sizes = [(span_of(groups)[1] + 8) * WIDE for groups in spans]
        return [
            [pltpu.VMEM((size,), F32) for size in sizes],
            pltpu.VMEM((2048, WIDE), F32),
            pltpu.SemaphoreType.DMA((len(spans),)),
        ]

    first_size = FIRST_SPANS[-1][1] * 384
    merge, lay0 = call(
        functools.partial(prep_kernel, FIRST_SPANS),
        [arr(MERGE_ROWS, WIDE), arr(1176, WIDE)],
        room(FIRST_SPANS),
        name="prep_first", us=2.0, far=(params[:first_size],),
    )
    lay1, lay2 = call(
        functools.partial(prep_kernel, LAYER_SPANS),
        [arr(1168, WIDE)] * 2,
        room(LAYER_SPANS),
        name="prep_layers", us=2.0, far=(params,),
    )
    taps_shape = jax.ShapeDtypeStruct((27 * 256, 256), BF16)
    conv0, weights0, bias0 = call(
        prep_conv0_kernel,
        [arr(2596, WIDE), taps_shape, arr(8, WIDE)],
        room(CONV_SPANS[:1]),
        name="prep_conv0", us=1.5, far=(params,),
    )
    conv1, head_w, weights1, vectors = call(
        prep_conv1_kernel,
        [arr(2640, WIDE), arr(WIDE, WIDE), taps_shape, arr(8, WIDE)],
        room(CONV_SPANS[1:]),
        params[NPARAM // WIDE * WIDE :], bias0,
        name="prep_conv1", us=1.5, far=(params,),
    )

    dense, tok0, save0, lse0, mixed0, mid0, hpre0, tok1, ahead, *parts = call(
        first_kernel,
        [arr(ROWS, MERGE), SQUARE, SAVE, SQUARE, SQUARE, SQUARE, arr(ROWS, HID), SQUARE, SQUARE]
        + PARTS,
        FORWARD,
        feats.reshape(PLANE, WIN, MERGE), merge, lay0,
        name="first", us=6.0,
    )
    parts = passed(parts, -1, sizes)
    window, save1, lse1, mixed1, out1, *parts = call(
        functools.partial(shifted_kernel, sizes),
        [SQUARE, SAVE, SQUARE, SQUARE, SQUARE] + PARTS,
        REGION + FORWARD,
        ahead, *parts, lay1,
        name="shifted", us=4.5, far=(weights0,),
    )
    parts = passed(parts, 1, sizes)
    mid1, hpre1, tok2, save2, lse2, mixed2, mid2, hpre2, lines, *sides = call(
        second_kernel,
        [SQUARE, arr(ROWS, HID), SQUARE, SAVE, SQUARE, SQUARE, SQUARE, arr(ROWS, HID)]
        + [arr(PLANE, 8, WIDE)] + SIDES,
        [pltpu.VMEM((ROWS, WIDE), F32)] + FORWARD,
        tok1, out1, *parts, lay1, lay2,
        name="second", us=6.5, far=(weights1,),
    )
    sides = beside(sides, sizes)
    grown, pre, tok3, sums, *tok_sides = call(
        functools.partial(conv_kernel, sizes),
        [arr(11, 12, 8, WIDE), arr(9, 10, 8, WIDE), arr(PLANE, 8, WIDE), arr(8, WIDE)] + SIDES,
        [
            pltpu.VMEM((9, 10, 8, WIDE), F32),
            pltpu.VMEM((880, 2304), BF16),
            pltpu.VMEM((576, 2304), BF16),
            pltpu.VMEM((PLANE, 8, WIDE), F32),
        ],
        lines, *sides, labels, valid, weights0, weights1, vectors,
        name="conv", us=8.0, mib=20,
    )
    tok_sides = beside(tok_sides, sizes)
    side_act, side_grown = call(
        functools.partial(sides_back_kernel, sizes),
        [jax.ShapeDtypeStruct((640, 2304), BF16)] * 2,
        [pltpu.VMEM((10, 10, 8, WIDE), F32)],
        grown, pre,
        name="sides_back", us=2.0,
    )
    weights0, weights1 = call(
        weights_back_kernel,
        [jax.ShapeDtypeStruct((256, 27 * 256), BF16)] * 2,
        [],
        conv0, conv1,
        name="weights_back", us=1.5,
    )
    sums = exchanged_sum(sums, count)
    voxels = WIN * slabs * WIN * rows * WIN
    tok3, slope, tail, d_head, d_rows = call(
        functools.partial(head_kernel, sizes, voxels),
        [arr(11, 12, 8, WIDE), arr(11, 12, 8, WIDE), arr(8, WIDE), arr(WIDE, WIDE), arr(8, WIDE)],
        [],
        tok3, *tok_sides, sums, vectors, head_w,
        name="head", us=3.5,
    )
    tail = exchanged_sum(tail, count)
    late_rows = block_rows(LATE_ROWS, count) * count
    early_rows = block_rows(EARLY_ROWS, count) * count
    seam_rows = LATE_ROWS - 3 * CUTS[3]
    d_own, keep, send, carry3, seam = call(
        functools.partial(conv_back_kernel, sizes),
        [arr(PLANE, 8, WIDE)] + [arr(early_rows // 2, WIDE)] * 2
        + [arr(24, WIDE), arr(seam_rows, WIDE)],
        [
            pltpu.VMEM((5236, WIDE), F32),
            pltpu.VMEM((11, 12, 8, WIDE), F32),
            pltpu.VMEM((10, 10, 8, WIDE), F32),
            pltpu.VMEM((880, 2304), BF16),
            pltpu.VMEM((576, 2304), BF16),
            pltpu.VMEM((seam_rows + early_rows, WIDE), F32),
        ],
        tok3, slope, tail, pre, side_act, side_grown, weights0, weights1, d_rows, d_head,
        name="conv_back", us=14.0, mib=28,
    )
    early = summing(keep, send, count)
    next(early)
    d_mid2, grads2 = call(
        back_mlp_kernel,
        [SQUARE, arr(1168, WIDE)],
        [pltpu.VMEM((ROWS, WIDE), F32)],
        d_own, lay2, mid2, hpre2,
        name="back_mlp", us=3.0,
    )
    step = early.send(d_mid2)
    d_mid, grads1, flat2, carry2, *parts = call(
        back_two_kernel,
        [SQUARE, arr(1168, WIDE), arr(3 * (CUTS[3] - CUTS[2]), WIDE), arr(32, WIDE)] + PARTS,
        [pltpu.VMEM((1184, WIDE), F32)] + BACKWARD,
        d_mid2, grads2, carry3, lay1, lay2, tok2, save2, lse2, mixed2, mid1, hpre1,
        name="back_two", us=9.0,
    )
    parts = passed(parts, -1, sizes)
    step = early.send(d_mid)
    d_window, flat1, carry1, *parts = call(
        functools.partial(back_shifted_kernel, sizes),
        [SQUARE, arr(3 * (CUTS[2] - CUTS[1]), WIDE), arr(16, WIDE)] + PARTS,
        REGION + [pltpu.VMEM((1200, WIDE), F32), pltpu.VMEM((ROWS, WIDE), F32)] + BACKWARD,
        d_mid, *parts, lay1, window, save1, lse1, mixed1, grads1, carry2,
        name="back_shifted", us=10.5, far=(step,),
    )
    early.send(d_window)
    parts = passed(parts, 1, sizes)
    next(early)
    step = next(early)
    late = call(
        functools.partial(back_first_kernel, sizes),
        [arr(late_rows // 2, WIDE)] * 2,
        [
            pltpu.VMEM((late_rows, WIDE), F32),
            pltpu.VMEM((1572, WIDE), F32),
            pltpu.VMEM((ROWS, WIDE), F32),
        ]
        + BACKWARD,
        d_mid, d_window, *parts, tok1, lay0, lay1, merge, dense, tok0, save0, lse0, mixed0, mid0,
        hpre0, carry1, flat1, flat2, seam,
        name="back_first", us=13.5, far=(step,),
    )
    step = early.send(late[0])
    keep, send = later(list(late), step)
    late_sum = finished(summing(keep, send, count))
    early = finished(early)
    new_params, new_first, new_second, loss, valid_count, norm = adamw(
        sizes, (*late_sum, *early, tail, sums), (params, moment_one, moment_two)
    )
    return (
        loss.reshape(()), valid_count.reshape(()), norm.reshape(()),
        new_params, new_first, new_second,
    )


def solution(mesh):
    placed = (
        P("slab", "mp", None, None),
        P("slab", "mp", None),
        P("slab", "mp", None),
        P(),
        P(),
        P(),
    )
    sizes = (mesh.shape["slab"], mesh.shape["mp"])
    return jax.shard_map(
        functools.partial(on_device, sizes),
        mesh=mesh,
        in_specs=placed,
        out_specs=(P(), P(), P(), P(), P(), P()),
        check_vma=False,
    )
```

```python
import functools

import jax
import jax.numpy as jnp
from jax import lax
from jax.experimental import pallas as pl
from jax.experimental.pallas import tpu as pltpu
from jax.sharding import PartitionSpec as P

EMB = 96
HEADS = 6
HDIM = 16
HID = 384
MERGE = 384
CLASSES = 14
WIN = 7
SHIFT = 3
LAYERS = 3
STEP = 10

F32 = jnp.float32
BF16 = jnp.bfloat16
eps_norm = 1e-05
beta_one = 0.9
beta_two = 0.999
adam_eps = 1e-08
learn_rate = 0.05
decay_rate = 0.05
clip_norm = 0.01
LOG2E = 1.4426950408889634

VOX = WIN * WIN * WIN
ROWS = 352
KEYS = 384
BLOCKS = ((0, 128), (128, 256), (256, 352))
HALVES = ((0, 176), (176, 352))
WIDE = 128
PLANE = WIN * WIN
FAR = WIN - SHIFT
ROWS_A = SHIFT * FAR * WIN
ROWS_B = FAR * SHIFT * WIN
ROWS_C = SHIFT * SHIFT * WIN

MERGE_ROWS = 392
LAYER_ROWS = 1165
TAP_ROWS = 27 * EMB
GROUPS = 2280
NPARAM = 872558
HEAD_ROW = 6806
HEAD_ROWS = 11
HEAD_LANE = 32
LATE_ROWS = 3072
EARLY_ROWS = 3840
LAYER_BASE = (98, 389, 680)
CONV_BASE = (971, 1620)
CUTS = (0, 392, 688, 976, 2280)

R_QKV, R_QKVB, R_PROJ, R_PROJB = 4, 292, 295, 391
R_HID, R_HIDB, R_OUT, R_OUTB = 392, 776, 780, 1164


def iota(shape, dim):
    return lax.broadcasted_iota(jnp.int32, shape, dim)


def split(x):
    hi = x.astype(BF16)
    return hi, (x - hi.astype(F32)).astype(BF16)


def pair(x):
    return jnp.concatenate(split(x), 1)


def fold(y):
    half = y.shape[1] // 2
    return y[:, :half] + y[:, half:]


def fold_rows(y):
    half = y.shape[0] // 2
    return y[:half] + y[half:]


def dot(a, b):
    return jnp.dot(a, b, preferred_element_type=F32)


def dot_nt(a, b):
    return lax.dot_general(a, b, (((1,), (1,)), ((), ())), preferred_element_type=F32)


def weight_nn(w):
    top = pair(w)
    return jnp.concatenate([top, top], 0)


def weight_nt(w):
    hi, lo = split(w)
    return jnp.concatenate(
        [jnp.concatenate([hi, hi], 1), jnp.concatenate([lo, lo], 1)], 0
    )


def mm(x, w):
    return fold(dot(pair(x), weight_nn(w)))


def mm_nt(x, w):
    return fold(dot_nt(pair(x), weight_nt(w)))


def with_rows(x, rows):
    if x.shape[0] == rows:
        return x
    return jnp.concatenate([x, jnp.zeros((rows - x.shape[0], x.shape[1]), F32)], 0)


def rows_t(x):
    return jnp.concatenate(split(with_rows(x, -(-x.shape[0] // WIDE) * WIDE).T), 0)


def mm_tn(xt, y):
    return fold_rows(fold(dot(xt, pair(with_rows(y, xt.shape[1])))))


def deep(w):
    return jnp.concatenate([w, jnp.zeros((WIDE - EMB, w.shape[1]), F32)], 0)


def roll(x, shift, axis):
    return pltpu.roll(x, shift, axis)


def four_to_three(y):
    lane = iota(y[0].shape, 1)
    a = jnp.where(lane < 96, y[0], roll(y[1], 96, 1))
    b = jnp.where(lane < 64, roll(y[1], 96, 1), roll(y[2], 64, 1))
    c = jnp.where(lane < 32, roll(y[2], 64, 1), roll(y[3], 32, 1))
    return a, b, c


def three_to_four(x):
    lane = iota(x[0].shape, 1)
    live = lane < EMB
    a = x[0]
    b = jnp.where(lane < 32, roll(x[0], 32, 1), roll(x[1], 32, 1))
    c = jnp.where(lane < 64, roll(x[1], 64, 1), roll(x[2], 64, 1))
    d = roll(x[2], 96, 1)
    return tuple(jnp.where(live, v, 0.0) for v in (a, b, c, d))


def hidden_rows(ref, start, count):
    return jnp.concatenate(
        four_to_three([ref[pl.ds(start + c, count, stride=4), :] for c in range(4)]), 1
    )


def put_hidden_rows(ref, start, count, x):
    parts = three_to_four([x[:, i * WIDE : (i + 1) * WIDE] for i in range(3)])
    for c in range(4):
        ref[pl.ds(start + c, count, stride=4), :] = parts[c]


def flatten(ref, start, groups, out):
    parts = four_to_three([ref[pl.ds(start + c, groups, stride=4), :] for c in range(4)])
    for c in range(3):
        out[pl.ds(c, groups, stride=3), :] = parts[c]


def norm_stats(x):
    live = iota(x.shape, 1) < EMB
    mean = jnp.sum(x, 1, keepdims=True) * (1.0 / EMB)
    centred = jnp.where(live, x - mean, 0.0)
    var = jnp.sum(centred * centred, 1, keepdims=True) * (1.0 / EMB)
    inv = lax.rsqrt(var + eps_norm)
    return centred * inv, inv


def norm(x, gain, bias):
    hat, _ = norm_stats(x)
    return hat * gain + bias


def norm_back(hat, inv, gain, grad):
    up = grad * gain
    one = jnp.sum(up, 1, keepdims=True) * (1.0 / EMB)
    two = jnp.sum(up * hat, 1, keepdims=True) * (1.0 / EMB)
    live = iota(hat.shape, 1) < EMB
    return jnp.where(live, inv * (up - one - hat * two), 0.0)


def colsum(x):
    return jnp.sum(x, 0, keepdims=True)


def gelu(x):
    return 0.5 * x * (1.0 + lax.erf(x * (0.5**0.5)))


def gelu_both(x):
    cdf = 0.5 * (1.0 + lax.erf(x * (0.5**0.5)))
    slope = cdf + x * (jnp.exp(x * x * -0.5) * 0.3989422804014327)
    return x * cdf, slope


def head_groups(x):
    lane = iota(x.shape, 1)
    swapped = roll(x, 64, 1)
    return jnp.where(lane < 64, x, swapped), jnp.where(lane < 64, swapped, x)


def as_left(x):
    both = []
    low = iota(x.shape, 1) < 64
    for part in head_groups(x):
        hi = part.astype(BF16).astype(F32)
        one = jnp.where(low, hi, part - hi).astype(BF16)
        both.append(jnp.concatenate([one, one], 1))
    return both


def as_right(x):
    return [pair(part) for part in head_groups(with_rows(x, KEYS))]


def head_mask(h, width):
    lane = iota((1, width), 1)
    lane = jnp.bitwise_and(lane, 63)
    low = jnp.bitwise_and(h, 3) * HDIM
    return jnp.where((lane >= low) & (lane < low + HDIM), 1.0, 0.0)


def own_lanes(h):
    lane = iota((1, WIDE), 1)
    return jnp.where((lane >= h * HDIM) & (lane < (h + 1) * HDIM), 1.0, 0.0)


def both_heads(right, heads, out):
    for k, h in enumerate(heads):
        out[k * KEYS : (k + 1) * KEYS, :] = right * head_mask(h, 2 * WIDE).astype(BF16)


def score_tiles(s, rows, region):
    tiles = [s[:, i * WIDE : (i + 1) * WIDE] for i in range(3)]
    if region is not None:
        return [t + region[rows, i * WIDE : (i + 1) * WIDE] for i, t in enumerate(tiles)]
    pad = jnp.where(iota((1, WIDE), 1) < VOX - 2 * WIDE, 0.0, -1e30)
    return tiles[:2] + [tiles[2] + pad]


def put_split(ref, rows, i, x):
    hi, lo = split(x)
    ref[rows, i * WIDE : (i + 1) * WIDE] = hi
    ref[rows, KEYS + i * WIDE : KEYS + (i + 1) * WIDE] = lo


def attention(normed, layer, save, lse, mixed, sc, region=None):
    left, right, values = sc
    x = pair(normed)
    qkv = []
    for i in range(3):
        w = deep(layer[pl.ds(R_QKV + i, EMB, stride=3), :])
        y = fold(dot(x, weight_nn(w))) + layer[R_QKVB + i : R_QKVB + i + 1, :]
        if i == 0:
            y = y * (HDIM**-0.5 * LOG2E)
        save[:, i * WIDE : (i + 1) * WIDE] = y
        qkv.append(y)
    for g, part in enumerate(as_left(qkv[0])):
        left[g] = part
    for g, part in enumerate(as_right(qkv[1])):
        right[g] = part
    v = jnp.where(iota((ROWS, WIDE), 1) == EMB, 1.0, qkv[2])
    v = pair(with_rows(v, KEYS))
    values[0:KEYS, :] = v
    values[KEYS : 2 * KEYS, :] = v
    mixed[...] = jnp.zeros_like(mixed)
    lse[...] = jnp.zeros_like(lse)

    def per_pair(pair_of, carry):
        heads = [2 * pair_of, 2 * pair_of + 1]
        masks = [head_mask(h, 2 * WIDE).astype(BF16) for h in heads]
        lanes = [own_lanes(h) for h in heads]
        spots = [jnp.where(iota((1, WIDE), 1) == h, 1.0, 0.0) for h in heads]
        g = lax.div(pair_of, 2)
        for block in HALVES:
            rows = slice(*block)
            out = level = 0.0
            for k in range(2):
                s = dot_nt(left[g, rows, :] * masks[k], right[g])
                tiles = score_tiles(s, rows, region)
                top = jnp.maximum(jnp.maximum(tiles[0], tiles[1]), tiles[2])
                top = jnp.max(top, 1, keepdims=True)
                parts = [split(jnp.exp2(t - top)) for t in tiles]
                e = jnp.concatenate([p[0] for p in parts] + [p[1] for p in parts], 1)
                o = fold(dot(e, values[...]))
                total = o[:, EMB : EMB + 1]
                out = out + o * (lanes[k] / total)
                level = level + (top + jnp.log(total) * LOG2E) * spots[k]
            mixed[rows, :] += out
            lse[rows, :] += level
        return carry

    lax.fori_loop(0, HEADS // 2, per_pair, 0)
    proj = deep(layer[R_PROJ : R_PROJ + EMB, :])
    return mm(mixed[...], proj) + layer[R_PROJB : R_PROJB + 1, :]


def attention_back(grad, normed, layer, save, lse, mixed, sc, grads, at, region=None):
    left, right, gleft, vright, keys, dq, dkv_t, weights, slopes = sc[:9]
    q_t, do_t, dmix, s, dp, two_keys, two_values = sc[9:]
    proj = deep(layer[R_PROJ : R_PROJ + EMB, :])
    grads[at + R_PROJ : at + R_PROJ + EMB, :] = mm_tn(rows_t(mixed[...]), grad)[:EMB]
    grads[at + R_PROJB : at + R_PROJB + 1, :] = colsum(grad)
    d_mixed = mm_nt(grad, proj)
    dmix[...] = d_mixed * mixed[...]
    q, k, v = (save[:, i * WIDE : (i + 1) * WIDE] for i in range(3))
    for g, part in enumerate(as_left(q)):
        left[g] = part
    for g, part in enumerate(as_right(k)):
        right[g] = part
    for g, part in enumerate(as_left(d_mixed)):
        gleft[g] = part
    for g, part in enumerate(as_right(v)):
        vright[g] = part
    kk = pair(with_rows(k, KEYS))
    keys[0:KEYS, :] = kk
    keys[KEYS : 2 * KEYS, :] = kk
    weights[:, ROWS:, :] = jnp.zeros((2, KEYS - ROWS, 2 * KEYS), BF16)
    slopes[:, ROWS:, :] = jnp.zeros((2, KEYS - ROWS, 2 * KEYS), BF16)
    for ref, x in ((q_t, q), (do_t, d_mixed)):
        hi, lo = split(with_rows(x, KEYS).T)
        ref[0] = hi
        ref[1] = lo
    dq[...] = jnp.zeros_like(dq)
    dkv_t[...] = jnp.zeros_like(dkv_t)

    def per_pair(pair_of, carry):
        g = lax.div(pair_of, 2)
        heads = [2 * pair_of, 2 * pair_of + 1]
        both_heads(right[g], heads, two_keys)
        both_heads(vright[g], heads, two_values)
        s[...] = dot_nt(left[g], two_keys[...])
        dp[...] = dot_nt(gleft[g], two_values[...])
        for k in range(2):
            h = 2 * pair_of + k
            lanes = own_lanes(h)
            at_h = jnp.where(iota((1, WIDE), 1) == h, 1.0, 0.0)
            for block in BLOCKS:
                rows = slice(*block)
                level = jnp.sum(lse[rows, :] * at_h, 1, keepdims=True)
                delta = jnp.sum(dmix[rows, :] * lanes, 1, keepdims=True)
                at_k = k * KEYS
                tiles = score_tiles(s[rows, at_k : at_k + KEYS], rows, region)
                for i, t in enumerate(tiles):
                    p = jnp.exp2(t - level)
                    put_split(weights.at[k], rows, i, p)
                    low = at_k + i * WIDE
                    p = p * (dp[rows, low : low + WIDE] - delta)
                    put_split(slopes.at[k], rows, i, p)
        total = 0.0
        for k in range(2):
            out = fold(dot(slopes[k, 0:ROWS, :], keys[...]))
            total = total + out * own_lanes(2 * pair_of + k)
        dq[...] += total
        for k in range(2):
            here = pl.ds(pl.multiple_of((2 * pair_of + k) * HDIM, HDIM), HDIM)
            for i, (t, m) in enumerate(((q_t, slopes), (do_t, weights))):
                lhs = jnp.concatenate([t[0, here, :], t[1, here, :]], 0)
                dkv_t[i, here, :] = fold_rows(fold(dot(lhs, m[k])))
        return carry

    lax.fori_loop(0, HEADS // 2, per_pair, 0)
    d_q = dq[...] * HDIM**-0.5
    d_k = dkv_t[0].T[0:ROWS] * (1.0 / LOG2E)
    d_v = dkv_t[1].T[0:ROWS]
    x_t = rows_t(normed)
    d_normed = None
    for i, d in enumerate((d_q, d_k, d_v)):
        grads[pl.ds(at + R_QKV + i, EMB, stride=3), :] = mm_tn(x_t, d)[:EMB]
        grads[at + R_QKVB + i : at + R_QKVB + i + 1, :] = colsum(d)
        part = mm_nt(d, deep(layer[pl.ds(R_QKV + i, EMB, stride=3), :]))
        d_normed = part if d_normed is None else d_normed + part
    return d_normed


def mlp(middle, layer, hpre):
    normed = norm(middle, layer[2:3, :], layer[3:4, :])
    w = deep(hidden_rows(layer, R_HID, EMB))
    pre = mm(normed, w) + hidden_rows(layer, R_HIDB, 1)
    hpre[...] = pre
    out = mm(gelu(pre), layer[R_OUT : R_OUT + HID, :])
    return middle + out + layer[R_OUTB : R_OUTB + 1, :]


def mlp_back(grad, middle, hpre, layer, grads, at):
    hat, inv = norm_stats(middle)
    normed = hat * layer[2:3, :] + layer[3:4, :]
    act, slope = gelu_both(hpre[...])
    grads[at + R_OUTB : at + R_OUTB + 1, :] = colsum(grad)
    grads[at + R_OUT : at + R_OUT + HID, :] = mm_tn(rows_t(grad), act).T
    d_pre = mm_nt(grad, layer[R_OUT : R_OUT + HID, :]) * slope
    put_hidden_rows(grads, at + R_HIDB, 1, colsum(d_pre))
    put_hidden_rows(grads, at + R_HID, EMB, mm_tn(rows_t(normed), d_pre)[:EMB])
    d_normed = mm_nt(d_pre, deep(hidden_rows(layer, R_HID, EMB)))
    grads[at + 2 : at + 3, :] = colsum(d_normed * hat)
    grads[at + 3 : at + 4, :] = colsum(d_normed)
    return grad + norm_back(hat, inv, layer[2:3, :], d_normed)


def pre_norm_back(grad, tokens, layer, grads, at):
    hat, inv = norm_stats(tokens)
    grads[at : at + 1, :] = colsum(grad * hat)
    grads[at + 1 : at + 2, :] = colsum(grad)
    return norm_back(hat, inv, layer[0:1, :], grad)


def region_of(rows, sizes):
    d = lax.shift_right_logical(rows * 1338, 16)
    line = lax.shift_right_logical(rows * 9363, 16)
    places = (d, line - d * WIN, rows - line * WIN)
    starts = (lax.axis_index("slab") * WIN, lax.axis_index("mp") * WIN, 0)
    total = None
    for place, start, blocks in zip(places, starts, sizes + (1,)):
        turned = jnp.where(place < SHIFT, place + FAR, place - SHIFT) + start
        length = WIN * blocks
        part = jnp.where(turned < length - WIN, 0, jnp.where(turned < length - SHIFT, 1, 2))
        total = part if total is None else total * 3 + part
    return total


def put_region(region, sizes):
    rows = region_of(iota((ROWS, WIDE), 0), sizes)[:, 0:1]
    lanes = region_of(iota((8, KEYS), 1), sizes)[0:1, :]
    apart = jnp.where(rows == lanes, 0.0, -100.0 * LOG2E)
    region[...] = jnp.where(iota((ROWS, KEYS), 1) < VOX, apart, -1e30)


def send_parts(ref, a, b, c):
    far = FAR * WIN
    near = SHIFT * WIN
    for d in range(SHIFT):
        base = d * PLANE
        c[d * near : (d + 1) * near, :] = ref[base : base + near, :]
        a[d * far : (d + 1) * far, :] = ref[base + near : base + PLANE, :]
    for d in range(FAR):
        base = (d + SHIFT) * PLANE
        b[d * near : (d + 1) * near, :] = ref[base : base + near, :]


def take_parts(own, a, b, c, out):
    far = FAR * WIN
    near = SHIFT * WIN
    for d in range(WIN):
        base = d * PLANE
        if d < SHIFT:
            out[base : base + near, :] = c[d * near : (d + 1) * near, :]
            out[base + near : base + PLANE, :] = a[d * far : (d + 1) * far, :]
        else:
            e = d - SHIFT
            out[base : base + near, :] = b[e * near : (e + 1) * near, :]
            out[base + near : base + PLANE, :] = own[base + near : base + PLANE, :]
    out[VOX:, :] = jnp.zeros((ROWS - VOX, WIDE), F32)


def span_of(groups):
    low, high = groups
    first = 3 * low // 8 * 8
    last = -(-3 * high // 8) * 8
    return first, min(last, NPARAM // WIDE // 8 * 8) - first


def copied(params, groups, flat, sem):
    first, rows = span_of(groups)
    size = rows * WIDE
    return pltpu.make_async_copy(
        params.at[pl.ds(first * WIDE, size)], flat.at[pl.ds(0, size)], sem
    )


def relay(groups, flat, out, square, last=None):
    low, high = groups
    first, rows = span_of(groups)
    square[0:rows, :] = flat[0 : rows * WIDE].reshape(rows, WIDE)
    if last is not None:
        square[rows : rows + 24, :] = jnp.zeros((24, WIDE), F32)
        square[rows : rows + 1, 0 : last.shape[0]] = last[...].reshape(1, last.shape[0])
    skip = 3 * low - first
    n = high - low
    parts = three_to_four([square[pl.ds(skip + c, n, stride=3), :] for c in range(3)])
    for c in range(4):
        out[pl.ds(c, n, stride=4), :] = parts[c]


FIRST_SPANS = ((0, 98), (98, 392))
LAYER_SPANS = ((389, 681), (680, 972))
CONV_SPANS = ((971, 1620), (1620, GROUPS))


def prep_kernel(spans, params, *refs, last=None):
    outs, (flats, square, sems) = refs[: len(spans)], refs[-3:]
    for i, groups in enumerate(spans):
        copied(params, groups, flats[i], sems.at[i]).start()
    for i, groups in enumerate(spans):
        copied(params, groups, flats[i], sems.at[i]).wait()
        relay(groups, flats[i], outs[i], square, last if i == len(spans) - 1 else None)


def head_picks():
    width = HEAD_ROWS * WIDE
    place = iota((WIDE, width), 1) - HEAD_LANE
    row = iota((WIDE, width), 0)
    here = (place >= row * CLASSES) & (place < (row + 1) * CLASSES) & (row <= EMB)
    place = iota((width, WIDE), 0) - HEAD_LANE
    col = iota((width, WIDE), 1)
    row = lax.shift_right_logical(place * 4682, 16)
    there = (place - row * CLASSES == col) & (place >= 0)
    return jnp.where(here, 1.0, 0.0), jnp.where(there, 1.0, 0.0).astype(BF16)


def prep_conv0_kernel(params, conv0, weights0, bias, *scratch):
    prep_kernel(CONV_SPANS[:1], params, conv0, *scratch)
    tap_weights(conv0, 3, weights0)
    bias[0:1, :] = conv0[3 + TAP_ROWS : 4 + TAP_ROWS, :]
    bias[1:8, :] = jnp.zeros((7, WIDE), F32)


def prep_conv1_kernel(last, bias, params, conv1, head, weights1, vectors, *scratch):
    prep_kernel(CONV_SPANS[1:], params, conv1, *scratch, last=last)
    tap_weights(conv1, 0, weights1)
    vectors[0:1, :] = bias[0:1, :]
    vectors[1:4, :] = conv1[TAP_ROWS : TAP_ROWS + 3, :]
    vectors[4:8, :] = jnp.zeros((4, WIDE), F32)
    square = scratch[1]
    first, _ = span_of(CONV_SPANS[1])
    row = jnp.concatenate(
        [square[HEAD_ROW + i - first : HEAD_ROW + i - first + 1, :] for i in range(HEAD_ROWS)], 1
    )
    here, there = head_picks()
    hi, lo = split(here * row)
    head[...] = dot(hi, there) + dot(lo, there)


def head_rows(d_head, out, at):
    here, there = head_picks()
    hi, lo = split(d_head)
    spread = (dot_nt(hi, there) + dot_nt(lo, there)) * here
    row = colsum(spread)
    for i in range(HEAD_ROWS):
        out[at + i : at + i + 1, :] += row[:, i * WIDE : (i + 1) * WIDE]


class Rows:
    def __init__(self, ref, at):
        self.ref, self.at = ref, at

    def __getitem__(self, key):
        rows, lanes = key
        if isinstance(rows, slice):
            rows = slice(rows.start + self.at, rows.stop + self.at)
        else:
            rows = pl.ds(rows.start + self.at, rows.size, stride=rows.stride)
        return self.ref[rows, lanes]


def merged_norm(x):
    mean = jnp.sum(x, 1, keepdims=True) * (1.0 / MERGE)
    centred = x - mean
    var = jnp.sum(centred * centred, 1, keepdims=True) * (1.0 / MERGE)
    return centred * lax.rsqrt(var + eps_norm)


def first_kernel(
    feats, merge, lay0,
    dense, tok0, save, lse, mixed, middle, hpre, tok1, ahead, pa, pb, pc,
    *sc,
):
    dense[VOX:, :] = jnp.zeros((ROWS - VOX, MERGE), F32)
    for line in range(PLANE):
        dense[line * WIN : (line + 1) * WIN, :] = feats[line]
    hat = merged_norm(dense[...])
    normed = hat * hidden_rows(merge, 0, 1) + hidden_rows(merge, 4, 1)
    tokens = mm(normed, merge[8 : 8 + MERGE, :])
    tok0[...] = tokens
    layer = Rows(lay0, 0)
    normed = norm(tokens, layer[0:1, :], layer[1:2, :])
    attended = attention(normed, layer, save, lse, mixed, sc)
    mid = tokens + attended
    middle[...] = mid
    tokens = mlp(mid, layer, hpre)
    tok1[...] = tokens
    ahead[...] = norm(tokens, layer[1165:1166, :], layer[1166:1167, :])
    send_parts(ahead, pa, pb, pc)


def shifted_kernel(
    sizes,
    own, pa, pb, pc, lay1, _,
    window, save, lse, mixed, out, qa, qb, qc,
    region, *sc,
):
    put_region(region, sizes)
    take_parts(own, pa, pb, pc, window)
    out[...] = attention(
        window[...], Rows(lay1, 1), save, lse, mixed, sc, region
    )
    send_parts(out, qa, qb, qc)


def to_lines(ref, out):
    for line in range(PLANE):
        out[line, 0:WIN, :] = ref[line * WIN : (line + 1) * WIN, :]
        out[line, WIN:8, :] = jnp.zeros((8 - WIN, WIDE), F32)


def from_lines(ref, out):
    out[VOX:, :] = jnp.zeros((ROWS - VOX, WIDE), F32)
    for line in range(PLANE):
        out[line * WIN : (line + 1) * WIN, :] = ref[line, 0:WIN, :]


def send_sides(lines, near_d, far_d, near_h, far_h):
    odd_d = jnp.bitwise_and(lax.axis_index("slab"), 1) == 1
    odd_h = jnp.bitwise_and(lax.axis_index("mp"), 1) == 1
    low, high = lines[0 : 2 * WIN], lines[(WIN - 2) * WIN : PLANE]
    near_d[...] = jnp.where(odd_d, low, high)
    far_d[...] = jnp.where(odd_d, high, low)
    for d in range(WIN):
        low = lines[d * WIN : d * WIN + 2]
        high = lines[d * WIN + WIN - 2 : (d + 1) * WIN]
        near_h[2 * d : 2 * d + 2] = jnp.where(odd_h, low, high)
        far_h[2 * d : 2 * d + 2] = jnp.where(odd_h, high, low)


def second_kernel(
    tok1, own, qa, qb, qc, lay1, lay2, _,
    mid1, hpre1, tok2, save, lse, mixed, mid2, hpre2, lines,
    s0, s1, s2, s3,
    attended, *sc,
):
    take_parts(own, qa, qb, qc, attended)
    mid = tok1[...] + attended[...]
    mid1[...] = mid
    tokens = mlp(mid, Rows(lay1, 1), hpre1)
    tok2[...] = tokens
    layer = Rows(lay2, 2)
    normed = norm(tokens, layer[0:1, :], layer[1:2, :])
    mid = tokens + attention(normed, layer, save, lse, mixed, sc)
    mid2[...] = mid
    attended[...] = mlp(mid, layer, hpre2)
    to_lines(attended, lines)
    send_sides(lines, s0, s1, s2, s3)


def grown_lines(sizes, own, near_d, far_d, near_h, far_h, out):
    slab, row = lax.axis_index("slab"), lax.axis_index("mp")
    odd_d = jnp.bitwise_and(slab, 1) == 1
    odd_h = jnp.bitwise_and(row, 1) == 1
    out[:, 11:12] = jnp.zeros((11, 1, 8, WIDE), F32)
    for d in range(WIN):
        out[d + 2, 2 : 2 + WIN] = own[d * WIN : (d + 1) * WIN]
    for d in range(2):
        near = near_d[d * WIN : (d + 1) * WIN]
        far = far_d[d * WIN : (d + 1) * WIN]
        out[d, 2 : 2 + WIN] = jnp.where(odd_d, near, jnp.where(slab == 0, 0.0, far))
        out[d + 9, 2 : 2 + WIN] = jnp.where(
            odd_d, jnp.where(slab == sizes[0] - 1, 0.0, far), near
        )
    for d in range(11):
        near = near_h[2 * d : 2 * d + 2]
        far = far_h[2 * d : 2 * d + 2]
        out[d, 0:2] = jnp.where(odd_h, near, jnp.where(row == 0, 0.0, far))
        out[d, 9:11] = jnp.where(odd_h, jnp.where(row == sizes[1] - 1, 0.0, far), near)


def put_marks(labels, valid, out):
    across = iota((8, WIN), 1) == iota((8, WIN), 0)
    classes = iota((8, WIDE), 1) - EMB
    for d in range(WIN):
        code = jnp.where(valid[d] == 1, labels[d], -1 - EMB - WIDE)
        code = code.astype(F32)
        for h in range(WIN):
            line = jnp.where(across, code[h : h + 1, :], 0.0)
            column = jnp.sum(line, 1, keepdims=True)
            mark = jnp.where(column == classes.astype(F32), 1.0, 0.0)
            out[d * WIN + h] = jnp.where(iota((8, WIDE), 0) < WIN, mark, 0.0)


def taps(source, first_plane, planes, first_line, lines, out):
    def per_plane(d, carry):
        for c in range(3):
            for b in range(3):
                x = source[d + first_plane, first_line + b : first_line + b + lines]
                if c != 1:
                    x = roll(x, 1 if c == 0 else 7, 1)
                x = pair(x.reshape(lines * 8, WIDE))
                at = pl.multiple_of(d * (lines * 8), lines * 8)
                t = b * 3 + c
                out[pl.ds(at, lines * 8), t * 256 : (t + 1) * 256] = x
        return carry

    lax.fori_loop(0, planes, per_plane, 0)


def tap_weights(ref, at, out):
    def per_tap(i, carry):
        w = deep(ref[pl.ds(i * EMB + at, EMB), :])
        out[pl.ds(pl.multiple_of(i * 256, 256), 256), :] = weight_nn(w)
        return carry

    lax.fori_loop(0, 27, per_tap, 0)


def tap_weights_back(ref, at, out):
    for i in range(27):
        w = deep(ref[(26 - i) * EMB + at : (27 - i) * EMB + at, :]).T
        out[i * 256 : (i + 1) * 256, :] = weight_nn(w)


def conv(side, weights, planes, pitch, at_once, put):
    rows = at_once * pitch
    for start in range(0, planes, at_once):
        total = None
        for a in range(3):
            low = (start + a) * pitch
            x = side[low : low + rows, :]
            part = dot(x, weights[a * 2304 : (a + 1) * 2304, :])
            total = part if total is None else total + part
        put(start, fold(total))


def conv_weight_grad(side, grad_rows, pitch, out, at):
    rows = 512
    g = jnp.concatenate([grad_rows, jnp.zeros((rows - grad_rows.shape[0], WIDE), F32)], 0)
    left = jnp.concatenate(split(g.T[:EMB]), 0)
    for a in range(3):
        for bc in range(9):
            y = dot(left, side[a * pitch : a * pitch + rows, bc * 256 : (bc + 1) * 256])
            y = deep(fold_rows(fold(y))).T
            t = a * 9 + bc
            out[at + t * EMB : at + (t + 1) * EMB, :] = y[:EMB]


def volume_mask(sizes, planes, lines, reach, real_lines):
    slab, row = lax.axis_index("slab"), lax.axis_index("mp")
    ends = (slab == 0, slab == sizes[0] - 1, row == 0, row == sizes[1] - 1)
    shape = (planes, lines, 8, WIDE)
    d, h, w = iota(shape, 0), iota(shape, 1), iota(shape, 2)
    low_d = jnp.where(ends[0], reach, 0)
    high_d = jnp.where(ends[1], planes - reach, planes)
    low_h = jnp.where(ends[2], reach, 0)
    high_h = jnp.where(ends[3], real_lines - reach, real_lines)
    inside = (d >= low_d) & (d < high_d) & (h >= low_h) & (h < high_h) & (w < WIN)
    return jnp.where(inside, 1.0, 0.0)


def conv_kernel(
    sizes,
    own, s0, s1, s2, s3, labels, valid, weights0, weights1, vectors, _,
    grown, pre, tok, stats, t0, t1, t2, t3,
    act, side, side_own, marks,
):
    grown_lines(sizes, own, s0, s1, s2, s3, grown)
    put_marks(labels, valid, marks)
    taps(grown, 0, 11, 0, 10, side)
    bias0 = vectors[0:1, :]
    inside = volume_mask(sizes, 9, 10, 1, 9)


    def put(start, y):
        z = (y + bias0).reshape(3, 10, 8, WIDE)
        pre[start : start + 3] = z
        act[start : start + 3] = gelu(z) * inside[start : start + 3]

    conv(side, weights0, 9, 80, 3, put)
    taps(act, 0, 9, 0, 8, side_own)
    bias1 = vectors[1:2, :]
    sums = []

    def put_own(start, y):
        y = (y + bias1).reshape(WIN, 8, 8, WIDE)[:, 0:WIN]
        y = y + own[...].reshape(WIN, WIN, 8, WIDE)
        y = jnp.where(iota(y.shape, 2) < WIN, y, 0.0).reshape(PLANE, 8, WIDE)
        tok[...] = y + marks[...]
        send_sides(tok, t0, t1, t2, t3)
        flat = y.reshape(PLANE * 8, WIDE)
        sums.append(colsum(flat))
        sums.append(colsum(flat * flat))

    conv(side_own, weights1, WIN, 64, WIN, put_own)
    count = jnp.sum(marks[...].reshape(PLANE * 8, WIDE))
    row = iota((8, WIDE), 0)
    stats[...] = (
        jnp.where(row == 0, sums[0], 0.0)
        + jnp.where(row == 1, sums[1], 0.0)
        + jnp.where(row == 2, count, 0.0)
    )


def head_kernel(
    sizes, voxels,
    own, s0, s1, s2, s3, sums, vectors, head_w,
    grown, slope_out, stats, d_head, d_rows,
):
    grown_lines(sizes, own, s0, s1, s2, s3, grown)
    rows = 11 * 12 * 8
    both = grown[...].reshape(rows, WIDE)
    lane = iota((rows, WIDE), 1)
    tokens = jnp.where(lane < EMB, both, 0.0)
    target = jnp.where(lane < CLASSES, roll(both, WIDE - EMB, 1), 0.0)
    live = jnp.sum(target, 1, keepdims=True)
    count = F32(voxels)
    average = sums[0:1, :] / count
    spread = sums[1:2, :] / count - average * average
    inv = lax.rsqrt(spread + eps_norm)
    gain = vectors[2:3, :]
    bias = vectors[3:4, :]
    hat = (tokens - average) * inv
    act, slope = gelu_both(hat * gain + bias)
    act = jnp.where(lane == EMB, 1.0, act)
    w = head_w[...]
    logits = mm(act, w)
    logits = jnp.where(lane < CLASSES, logits, -1e30)
    top = jnp.max(logits, 1, keepdims=True)
    e = jnp.exp(logits - top)
    total = jnp.sum(e, 1, keepdims=True)
    logp = logits - top - jnp.log(total)
    scale = 1.0 / sums[2:3, 0:1]
    d_logits = (e / total * live - target) * scale
    d_normed = jnp.where(lane < EMB, mm_nt(d_logits, w) * slope, 0.0)
    d_tokens = d_normed * gain * inv
    slope_out[...] = d_tokens.reshape(11, 12, 8, WIDE)

    def own_rows(x):
        x = x.reshape(11, 12, 8, WIDE)[2:9, 2:9]
        x = jnp.where(iota(x.shape, 2) < WIN, x, 0.0)
        return x.reshape(PLANE * 8, WIDE)

    loss = -jnp.sum(own_rows(target * jnp.where(lane < CLASSES, logp, 0.0)))
    own_d = own_rows(d_logits)
    own_n = own_rows(d_normed)
    own_hat = own_rows(hat)
    zeros = jnp.zeros((512 - PLANE * 8, WIDE), F32)
    left = rows_t(jnp.concatenate([own_d, zeros], 0))
    d_head[...] = mm_tn(left, jnp.concatenate([own_rows(act), zeros], 0)).T
    d_gain = colsum(own_n * own_hat)
    d_bias = colsum(own_n)
    d_average = -d_bias * gain * inv
    d_spread = d_gain * gain * inv * inv * -0.5
    d_two = d_spread / count
    d_one = (d_average - 2.0 * average * d_spread) / count
    row = iota((8, WIDE), 0)
    live_lane = iota((8, WIDE), 1) < EMB
    stats[...] = (
        jnp.where((row == 0) & live_lane, d_one, 0.0)
        + jnp.where((row == 1) & live_lane, d_two, 0.0)
        + jnp.where(row == 2, loss, 0.0)
    )
    d_rows[...] = (
        jnp.where(row == 0, d_gain, 0.0)
        + jnp.where(row == 1, d_bias, 0.0)
    )


def sides_back_kernel(sizes, grown, pre, side_act, side_grown, act):
    act[0:9] = gelu(pre[...]) * volume_mask(sizes, 9, 10, 1, 9)
    act[9:10] = jnp.zeros((1, 10, 8, WIDE), F32)
    taps(act, 0, 10, 0, 8, side_act)
    taps(grown, 1, 10, 1, 8, side_grown)


def weights_back_kernel(conv0, conv1, weights0, weights1):
    tap_weights_back(conv0, 3, weights0)
    tap_weights_back(conv1, 0, weights1)


def conv_back_kernel(
    sizes,
    tok, slope, sums, pre, side_act, side_grown, weights0, weights1, d_rows, d_head,
    d_own, keep, send, carry, seam,
    grads, dgrown, act, side, side_own, flat,
):
    lane = iota((11, 12, 8, WIDE), 3)
    inside = volume_mask(sizes, 11, 12, 2, 11)
    steady = sums[0:1, :].reshape(1, 1, 1, WIDE)
    rising = 2.0 * sums[1:2, :].reshape(1, 1, 1, WIDE)
    d_tok = slope[...] + jnp.where(lane < EMB, (steady + tok[...] * rising) * inside, 0.0)
    dgrown[...] = d_tok
    grads[5191:, :] = jnp.zeros((45, WIDE), F32)
    grads[0:8, :] = jnp.zeros((8, WIDE), F32)
    grads[5189:5191, :] = d_rows[0:2, :]
    own = dgrown[2:9, 2:10]
    line = iota(own.shape, 1)
    own = jnp.where(line < WIN, own, 0.0).reshape(WIN * 64, WIDE)
    grads[5188:5189, :] = colsum(own)

    near = volume_mask(sizes, 9, 10, 1, 9)
    conv_weight_grad(side_act, own, 64, grads, 2596)
    taps(dgrown, 0, 11, 0, 10, side)


    def put(start, y):
        _, s = gelu_both(pre[start : start + 3])
        act[start : start + 3] = y.reshape(3, 10, 8, WIDE) * s * near[start : start + 3]

    conv(side, weights1, 9, 80, 3, put)

    own = act[1:8, 1:9]
    line = iota(own.shape, 1)
    own = jnp.where(line < WIN, own, 0.0).reshape(WIN * 64, WIDE)
    grads[2595:2596, :] = colsum(own)
    conv_weight_grad(side_grown, own, 64, grads, 3)
    carry[...] = grads[0:24, :]
    flat[3 * (GROUPS - CUTS[3]) :, :] = jnp.zeros((flat.shape[0] - 3912, WIDE), F32)
    flatten(grads, 20, GROUPS - CUTS[3], flat)
    start = 3 * CUTS[3]
    head_rows(d_head[...], flat, HEAD_ROW - start)
    seam[...] = flat[0 : LATE_ROWS - start, :]
    scatter(sizes, flat, LATE_ROWS - start, keep, send)
    taps(act, 0, 9, 0, 8, side_own)

    def put_own(start, y):
        y = y.reshape(WIN, 8, 8, WIDE)[:, 0:WIN] + dgrown[2:9, 2:9]
        y = jnp.where(iota(y.shape, 2) < WIN, y, 0.0)
        d_own[...] = y.reshape(PLANE, 8, WIDE)

    conv(side_own, weights0, WIN, 64, WIN, put_own)


def back_mlp_kernel(d_own, lay2, mid2, hpre2, d_mid, grads, dense):
    from_lines(d_own, dense)
    grads[...] = jnp.zeros_like(grads)
    d_mid[...] = mlp_back(dense[...], mid2[...], hpre2, Rows(lay2, 2), grads, 2)


def back_two_kernel(
    d_mid2, grads2, carry, lay1, lay2, tok2, save, lse, mixed, mid1, hpre1,
    d_mid, grads1, flat, carry2, pa, pb, pc,
    grads, *sc,
):
    layer = Rows(lay2, 2)
    grads[0:1168, :] = grads2[...]
    d = d_mid2[...]
    tokens = tok2[...]
    normed = norm(tokens, layer[0:1, :], layer[1:2, :])
    d_normed = attention_back(d, normed, layer, save, lse, mixed, sc, grads, 2)
    d = d + pre_norm_back(d_normed, tokens, layer, grads, 2)
    grads[1167:1184, :] = carry[3:20, :]
    flatten(grads, 32, CUTS[3] - CUTS[2], flat)
    carry2[...] = grads[0:32, :]
    layer = Rows(lay1, 1)
    d = mlp_back(d, mid1[...], hpre1, layer, grads1, 1)
    d_mid[...] = d
    send_parts(d_mid, pa, pb, pc)


def back_shifted_kernel(
    sizes,
    own, pa, pb, pc, lay1, window, save, lse, mixed, grads1, carry2, _,
    d_window, flat, carry1, qa, qb, qc,
    region, grads, grad, *sc,
):
    put_region(region, sizes)
    take_parts(own, pa, pb, pc, grad)
    grads[0:1168, :] = grads1[...]
    grads[0:3, :] = jnp.zeros((3, WIDE), F32)
    d_window[...] = attention_back(
        grad[...], window[...], Rows(lay1, 1), save, lse, mixed, sc, grads, 1,
        region,
    )
    send_parts(d_window, qa, qb, qc)
    grads[1166:1196, :] = carry2[2:32, :]
    flatten(grads, 12, CUTS[2] - CUTS[1], flat)
    carry1[...] = grads[0:16, :]


def back_first_kernel(
    sizes,
    d_mid, own, qa, qb, qc, tok1, lay0, lay1, merge, dense, tok0, save, lse, mixed, middle, hpre,
    carry1, flat1, flat2, seam, _,
    keep, send,
    flat, grads, grad, *sc,
):
    take_parts(own, qa, qb, qc, grad)
    grads[1556:1572, :] = carry1[...]
    d = d_mid[...] + pre_norm_back(grad[...], tok1[...], Rows(lay1, 1), grads, 1557)
    layer = Rows(lay0, 0)
    at = MERGE_ROWS
    d = mlp_back(d, middle[...], hpre, layer, grads, at)
    tokens = tok0[...]
    normed = norm(tokens, layer[0:1, :], layer[1:2, :])
    d_normed = attention_back(d, normed, layer, save, lse, mixed, sc, grads, at)
    d = d + pre_norm_back(d_normed, tokens, layer, grads, at)
    live = iota((ROWS, WIDE), 0) < VOX
    d = jnp.where(live, d, 0.0)
    hat = merged_norm(dense[...])
    gain = hidden_rows(merge, 0, 1)
    bias = hidden_rows(merge, 4, 1)
    w = merge[8 : 8 + MERGE, :]
    put_hidden_rows(grads, 8 - 8, 1, jnp.zeros((1, MERGE), F32))
    grads[8 : 8 + MERGE, :] = mm_tn(rows_t(d), hat * gain + bias).T
    d_hat = mm_nt(d, w)
    put_hidden_rows(grads, 0, 1, colsum(d_hat * hat))
    put_hidden_rows(grads, 4, 1, colsum(d_hat))
    flatten(grads, 0, CUTS[1], flat)
    at = 0
    for cut, part in ((CUTS[1], flat1), (CUTS[2], flat2), (CUTS[3], seam)):
        at = 3 * cut
        flat[at : at + part.shape[0], :] = part[...]
    at += seam.shape[0]
    if flat.shape[0] > at:
        flat[at:, :] = jnp.zeros((flat.shape[0] - at, WIDE), F32)
    scatter(sizes, flat, 0, keep, send)


def radices(count):
    steps = [2]
    left = count // 2
    while left > 1:
        steps.append(4 if left >= 4 else 2)
        left //= steps[-1]
    return steps


def block_rows(rows, count):
    return -(-rows // (8 * count)) * 8


def own_number(sizes):
    return lax.axis_index("slab") * sizes[1] + lax.axis_index("mp")


def place_in_half(distance, count):
    place = 0
    shift = 1
    for radix in radices(count)[1:]:
        digit = jnp.bitwise_and(lax.shift_right_logical(distance, shift), radix - 1)
        place = place * radix + digit
        shift += radix.bit_length() - 1
    return place


def scatter(sizes, source, first, keep, send):
    count = sizes[0] * sizes[1]
    rows = keep.shape[0] * 2 // count
    me = own_number(sizes)
    odd = jnp.bitwise_and(me, 1)

    def per_pair(t, carry):
        for block, out in ((2 * t + odd, keep), (2 * t + 1 - odd, send)):
            place = place_in_half(jnp.bitwise_xor(block, me), count)
            at = pl.multiple_of(first + block * rows, 8)
            to = pl.multiple_of(place * rows, 8)
            out[pl.ds(to, rows), :] = source[pl.ds(at, rows), :]
        return carry

    lax.fori_loop(0, count // 2, per_pair, 0)


def traded(value, distance, count):
    pairs = [(i, i ^ distance) for i in range(count)]
    return lax.ppermute(value, ("slab", "mp"), pairs)


def later(got, after):
    return got if after is None else list(lax.optimization_barrier((*got, after)))[:-1]


def summing(keep, send, count):
    steps = radices(count)
    got = [keep, traded(send, 1, count)]
    shift = 1
    after = yield None
    for radix in steps[1:]:
        got = later(got, after)
        total = sum(got[1:], got[0])
        rows = total.shape[0] // radix
        parts = [total[k * rows : (k + 1) * rows] for k in range(radix)]
        got = parts[:1] + [traded(parts[k], k << shift, count) for k in range(1, radix)]
        shift += radix.bit_length() - 1
        after = yield parts[0]
    got = later(got, after)
    own = sum(got[1:], got[0])
    for radix in reversed(steps[1:]):
        shift -= radix.bit_length() - 1
        got = [own] + [traded(own, k << shift, count) for k in range(1, radix)]
        after = yield own
        own = jnp.concatenate(later(got, after), 0)
        yield own
    yield own, traded(own, 1, count)


def finished(chain, after=None):
    last = next(chain) if after is None else chain.send(after)
    while not isinstance(last, tuple):
        last = next(chain)
    return last


def exchanged_sum(value, count):
    shift = 0
    for radix in radices(count):
        got = [value] + [traded(value, k << shift, count) for k in range(1, radix)]
        while len(got) > 1:
            got = [got[i] + got[i + 1] for i in range(0, len(got), 2)]
        value = got[0]
        shift += radix.bit_length() - 1
    return value


PIECE = 294912


def place_blocks(sizes, own, other, out, size):
    count = sizes[0] * sizes[1]
    me = own_number(sizes)
    rows = own.shape[0] * 2 // count

    def per_block(block, carry):
        distance = jnp.bitwise_xor(block, me)
        at = pl.ds(pl.multiple_of(place_in_half(distance, count) * rows, 8), rows)
        near = jnp.bitwise_and(distance, 1) == 0
        to = pl.ds(pl.multiple_of(block * rows, 8), rows)
        out[to, :] = jnp.where(near, own[at, :], other[at, :])
        return carry

    lax.fori_loop(0, size // rows, per_block, 0)


def squares(*refs):
    total = jnp.zeros((8, WIDE), F32)
    for ref in refs:
        x = ref[...]
        total = total + jnp.sum((x * x).reshape(-1, 8, WIDE), 0)
    return total


def place_early_kernel(sizes, own, other, out, square):
    place_blocks(sizes, own, other, out, EARLY_ROWS)
    square[...] = squares(own, other)


def adamw_kernel(
    sizes,
    late, late_other, early, square, tail, sums, params, first, second,
    new_params, new_first, new_second, loss, valid, norm_out,
    grad, scale_ref,
):
    step = pl.program_id(0)

    @pl.when(step == 0)
    def gather():
        norm = jnp.sqrt(jnp.sum(squares(late, late_other) + square[...]))
        loss[0] = jnp.sum(tail[2:3, 0:1])
        valid[0] = jnp.sum(sums[2:3, 0:1])
        norm_out[0] = norm
        scale_ref[0] = jnp.minimum(1.0, clip_norm / (norm + 1e-06))
        place_blocks(sizes, late, late_other, grad, LATE_ROWS)
        grad[LATE_ROWS:, :] = early[...]

    def update(base, low, size):
        rows = -(-size // 1024) * 8
        at = pl.ds(pl.multiple_of(base // WIDE + low // WIDE, 8), rows)
        g = grad[at, :].reshape(rows * WIDE)[:size] * scale_ref[0]
        here = pl.ds(pl.multiple_of(base + low, 1024), size)
        one = beta_one * first[here] + (1.0 - beta_one) * g
        two = beta_two * second[here] + (1.0 - beta_two) * g * g
        there = pl.ds(low, size)
        new_first[there] = one
        new_second[there] = two
        two = two * (1.0 / (1.0 - beta_two**STEP))
        low_by = two * lax.rsqrt(jnp.maximum(two, 1e-37)) + adam_eps
        inverse = pl.reciprocal(low_by, approx=True)
        inverse = inverse * (2.0 - low_by * inverse)
        new_params[there] = params[here] * (1.0 - learn_rate * decay_rate) - (
            one * (learn_rate / (1.0 - beta_one**STEP))
        ) * inverse

    whole = NPARAM // PIECE

    @pl.when(step < whole)
    def full():
        def part(i, carry):
            low = pl.multiple_of(i * 16384, 16384)
            update(step * PIECE, low, 16384)
            return carry

        lax.fori_loop(0, PIECE // 16384, part, 0)

    @pl.when(step == whole)
    def last():
        rest = NPARAM - whole * PIECE
        main = rest // 1024 * 1024
        for low in range(0, main, 16384):
            update(whole * PIECE, low, min(16384, main - low))
        update(whole * PIECE, main, rest - main)


def adamw(sizes, parts, arrays):
    pieces = -(-NPARAM // PIECE)
    piece = pl.BlockSpec((PIECE,), lambda i: (i,))
    vmem = pl.BlockSpec(memory_space=pltpu.VMEM)
    smem = pl.BlockSpec(memory_space=pltpu.SMEM)
    return pl.pallas_call(
        functools.partial(adamw_kernel, sizes),
        grid=(pieces,),
        out_shape=[arr(NPARAM)] * 3 + [arr(1)] * 3,
        in_specs=[vmem] * (len(parts) + len(arrays)),
        out_specs=[piece] * 3 + [smem] * 3,
        scratch_shapes=[pltpu.VMEM((LATE_ROWS + EARLY_ROWS, WIDE), F32), pltpu.SMEM((1,), F32)],
        compiler_params=pltpu.CompilerParams(vmem_limit_bytes=16 * 1024 * 1024),
        cost_estimate=pl.CostEstimate(flops=6 * 10**9, bytes_accessed=0, transcendentals=0),
        name="adamw",
    )(*parts, *arrays)


def arr(*shape):
    return jax.ShapeDtypeStruct(shape, F32)


def call(kernel, outs, scratch, *args, name=None, us=1.0, far=(), mib=16):
    vmem = pl.BlockSpec(memory_space=pltpu.VMEM)
    smem = pl.BlockSpec(memory_space=pltpu.SMEM)
    return pl.pallas_call(
        kernel,
        out_shape=list(outs),
        in_specs=[vmem] * len(args) + [pl.BlockSpec(memory_space=pl.ANY)] * len(far),
        out_specs=[smem if o.shape == (1,) else vmem for o in outs],
        scratch_shapes=list(scratch),
        compiler_params=pltpu.CompilerParams(vmem_limit_bytes=mib * 1024 * 1024),
        cost_estimate=pl.CostEstimate(
            flops=int(us * 1.15e9), bytes_accessed=0, transcendentals=0
        ),
        name=name,
    )(*args, *far)


SQUARE = arr(ROWS, WIDE)
SAVE = arr(ROWS, 3 * WIDE)
FORWARD = [
    pltpu.VMEM((2, ROWS, 2 * WIDE), BF16),
    pltpu.VMEM((2, KEYS, 2 * WIDE), BF16),
    pltpu.VMEM((2 * KEYS, 2 * WIDE), BF16),
]
BACKWARD = [
    pltpu.VMEM((2, ROWS, 2 * WIDE), BF16),
    pltpu.VMEM((2, KEYS, 2 * WIDE), BF16),
    pltpu.VMEM((2, ROWS, 2 * WIDE), BF16),
    pltpu.VMEM((2, KEYS, 2 * WIDE), BF16),
    pltpu.VMEM((2 * KEYS, 2 * WIDE), BF16),
    pltpu.VMEM((ROWS, WIDE), F32),
    pltpu.VMEM((2, WIDE, KEYS), F32),
    pltpu.VMEM((2, KEYS, 2 * KEYS), BF16),
    pltpu.VMEM((2, KEYS, 2 * KEYS), BF16),
    pltpu.VMEM((2, WIDE, KEYS), BF16),
    pltpu.VMEM((2, WIDE, KEYS), BF16),
    pltpu.VMEM((ROWS, WIDE), F32),
    pltpu.VMEM((ROWS, 2 * KEYS), F32),
    pltpu.VMEM((ROWS, 2 * KEYS), F32),
    pltpu.VMEM((2 * KEYS, 2 * WIDE), BF16),
    pltpu.VMEM((2 * KEYS, 2 * WIDE), BF16),
]
PARTS = [arr(ROWS_A, WIDE), arr(ROWS_B, WIDE), arr(ROWS_C, WIDE)]


def passed(parts, steps, sizes):
    slabs, rows = sizes
    moved = []
    for part, (ds, dm) in zip(parts, ((1, 0), (0, 1), (1, 1))):
        pairs = []
        for s in range(slabs):
            for m in range(rows):
                target = ((s + steps * ds) % slabs) * rows + (m + steps * dm) % rows
                pairs.append((s * rows + m, target))
        moved.append(lax.ppermute(part, ("slab", "mp"), pairs))
    return moved


SIDES = [arr(2 * WIN, 8, WIDE)] * 4


def paired(axis, size):
    near = [(i, i ^ 1) for i in range(size)]
    far = [(i, (i + (1 if i % 2 else -1)) % size) for i in range(size)]
    return (
        lambda value: lax.ppermute(value, axis, near),
        lambda value: lax.ppermute(value, axis, far),
    )


def column_kernel(sizes, near_d, far_d, near_h, far_h, near_out, far_out):
    slab = lax.axis_index("slab")
    odd_d = jnp.bitwise_and(slab, 1) == 1
    odd_h = jnp.bitwise_and(lax.axis_index("mp"), 1) == 1
    at_low = slab == 0
    at_high = slab == sizes[0] - 1
    near_out[4:18] = near_h[...]
    far_out[4:18] = far_h[...]
    for d in range(2):
        near = near_d[d * WIN : (d + 1) * WIN]
        far = far_d[d * WIN : (d + 1) * WIN]
        before = jnp.where(odd_d, near, jnp.where(at_low, 0.0, far))
        after = jnp.where(odd_d, jnp.where(at_high, 0.0, far), near)
        for x, at in ((before, 2 * d), (after, 18 + 2 * d)):
            low, high = x[0:2], x[WIN - 2 : WIN]
            near_out[at : at + 2] = jnp.where(odd_h, low, high)
            far_out[at : at + 2] = jnp.where(odd_h, high, low)


def beside(sides, sizes):
    near, far = paired("slab", sizes[0])
    near_d, far_d = near(sides[0]), far(sides[1])
    near_h, far_h = call(
        functools.partial(column_kernel, sizes), [arr(22, 8, WIDE)] * 2, [],
        near_d, far_d, sides[2], sides[3],
        name="column", us=0.3,
    )
    near, far = paired("mp", sizes[1])
    return near_d, far_d, near(near_h), far(far_h)


REGION = [pltpu.VMEM((ROWS, KEYS), F32)]


def on_device(sizes, feats, labels, valid, params, moment_one, moment_two):
    slabs, rows = sizes
    count = slabs * rows

    def room(spans):
        sizes = [(span_of(groups)[1] + 8) * WIDE for groups in spans]
        return [
            [pltpu.VMEM((size,), F32) for size in sizes],
            pltpu.VMEM((2048, WIDE), F32),
            pltpu.SemaphoreType.DMA((len(spans),)),
        ]

    first_size = FIRST_SPANS[-1][1] * 384
    merge, lay0 = call(
        functools.partial(prep_kernel, FIRST_SPANS),
        [arr(MERGE_ROWS, WIDE), arr(1176, WIDE)],
        room(FIRST_SPANS),
        name="prep_first", us=2.0, far=(params[:first_size],),
    )
    lay1, lay2 = call(
        functools.partial(prep_kernel, LAYER_SPANS),
        [arr(1168, WIDE)] * 2,
        room(LAYER_SPANS),
        name="prep_layers", us=2.0, far=(params,),
    )
    taps_shape = jax.ShapeDtypeStruct((27 * 256, 256), BF16)
    conv0, weights0, bias0 = call(
        prep_conv0_kernel,
        [arr(2596, WIDE), taps_shape, arr(8, WIDE)],
        room(CONV_SPANS[:1]),
        name="prep_conv0", us=1.5, far=(params,),
    )
    conv1, head_w, weights1, vectors = call(
        prep_conv1_kernel,
        [arr(2640, WIDE), arr(WIDE, WIDE), taps_shape, arr(8, WIDE)],
        room(CONV_SPANS[1:]),
        params[NPARAM // WIDE * WIDE :], bias0,
        name="prep_conv1", us=1.5, far=(params,),
    )

    dense, tok0, save0, lse0, mixed0, mid0, hpre0, tok1, ahead, *parts = call(
        first_kernel,
        [arr(ROWS, MERGE), SQUARE, SAVE, SQUARE, SQUARE, SQUARE, arr(ROWS, HID), SQUARE, SQUARE]
        + PARTS,
        FORWARD,
        feats.reshape(PLANE, WIN, MERGE), merge, lay0,
        name="first", us=6.0,
    )
    parts = passed(parts, -1, sizes)
    window, save1, lse1, mixed1, out1, *parts = call(
        functools.partial(shifted_kernel, sizes),
        [SQUARE, SAVE, SQUARE, SQUARE, SQUARE] + PARTS,
        REGION + FORWARD,
        ahead, *parts, lay1,
        name="shifted", us=4.5, far=(weights0,),
    )
    parts = passed(parts, 1, sizes)
    mid1, hpre1, tok2, save2, lse2, mixed2, mid2, hpre2, lines, *sides = call(
        second_kernel,
        [SQUARE, arr(ROWS, HID), SQUARE, SAVE, SQUARE, SQUARE, SQUARE, arr(ROWS, HID)]
        + [arr(PLANE, 8, WIDE)] + SIDES,
        [pltpu.VMEM((ROWS, WIDE), F32)] + FORWARD,
        tok1, out1, *parts, lay1, lay2,
        name="second", us=6.5, far=(weights1,),
    )
    sides = beside(sides, sizes)
    back0, back1 = call(
        weights_back_kernel,
        [taps_shape] * 2,
        [],
        conv0, conv1,
        name="weights_back", us=1.5,
    )
    grown, pre, tok3, sums, *tok_sides = call(
        functools.partial(conv_kernel, sizes),
        [arr(11, 12, 8, WIDE), arr(9, 10, 8, WIDE), arr(PLANE, 8, WIDE), arr(8, WIDE)] + SIDES,
        [
            pltpu.VMEM((9, 10, 8, WIDE), F32),
            pltpu.VMEM((880, 2304), BF16),
            pltpu.VMEM((576, 2304), BF16),
            pltpu.VMEM((PLANE, 8, WIDE), F32),
        ],
        lines, *sides, labels, valid, weights0, weights1, vectors,
        name="conv", us=8.0, mib=20, far=(back0,),
    )
    tok_sides = beside(tok_sides, sizes)
    side_act, side_grown = call(
        functools.partial(sides_back_kernel, sizes),
        [jax.ShapeDtypeStruct((640, 2304), BF16)] * 2,
        [pltpu.VMEM((10, 10, 8, WIDE), F32)],
        grown, pre,
        name="sides_back", us=2.0,
    )
    sums = exchanged_sum(sums, count)
    voxels = WIN * slabs * WIN * rows * WIN
    tok3, slope, tail, d_head, d_rows = call(
        functools.partial(head_kernel, sizes, voxels),
        [arr(11, 12, 8, WIDE), arr(11, 12, 8, WIDE), arr(8, WIDE), arr(WIDE, WIDE), arr(8, WIDE)],
        [],
        tok3, *tok_sides, sums, vectors, head_w,
        name="head", us=3.5,
    )
    tail = exchanged_sum(tail, count)
    late_rows = block_rows(LATE_ROWS, count) * count
    early_rows = block_rows(EARLY_ROWS, count) * count
    seam_rows = LATE_ROWS - 3 * CUTS[3]
    d_own, keep, send, carry3, seam = call(
        functools.partial(conv_back_kernel, sizes),
        [arr(PLANE, 8, WIDE)] + [arr(early_rows // 2, WIDE)] * 2
        + [arr(24, WIDE), arr(seam_rows, WIDE)],
        [
            pltpu.VMEM((5236, WIDE), F32),
            pltpu.VMEM((11, 12, 8, WIDE), F32),
            pltpu.VMEM((10, 10, 8, WIDE), F32),
            pltpu.VMEM((880, 2304), BF16),
            pltpu.VMEM((576, 2304), BF16),
            pltpu.VMEM((seam_rows + early_rows, WIDE), F32),
        ],
        tok3, slope, tail, pre, side_act, side_grown, back0, back1, d_rows, d_head,
        name="conv_back", us=14.0, mib=28,
    )
    early = summing(keep, send, count)
    next(early)
    d_mid2, grads2 = call(
        back_mlp_kernel,
        [SQUARE, arr(1168, WIDE)],
        [pltpu.VMEM((ROWS, WIDE), F32)],
        d_own, lay2, mid2, hpre2,
        name="back_mlp", us=3.0,
    )
    step = early.send(d_mid2)
    d_mid, grads1, flat2, carry2, *parts = call(
        back_two_kernel,
        [SQUARE, arr(1168, WIDE), arr(3 * (CUTS[3] - CUTS[2]), WIDE), arr(32, WIDE)] + PARTS,
        [pltpu.VMEM((1184, WIDE), F32)] + BACKWARD,
        d_mid2, grads2, carry3, lay1, lay2, tok2, save2, lse2, mixed2, mid1, hpre1,
        name="back_two", us=9.0,
    )
    parts = passed(parts, -1, sizes)
    step = early.send(d_mid)
    d_window, flat1, carry1, *parts = call(
        functools.partial(back_shifted_kernel, sizes),
        [SQUARE, arr(3 * (CUTS[2] - CUTS[1]), WIDE), arr(16, WIDE)] + PARTS,
        REGION + [pltpu.VMEM((1200, WIDE), F32), pltpu.VMEM((ROWS, WIDE), F32)] + BACKWARD,
        d_mid, *parts, lay1, window, save1, lse1, mixed1, grads1, carry2,
        name="back_shifted", us=10.5, far=(step,),
    )
    early.send(d_window)
    parts = passed(parts, 1, sizes)
    next(early)
    step = next(early)
    late = call(
        functools.partial(back_first_kernel, sizes),
        [arr(late_rows // 2, WIDE)] * 2,
        [
            pltpu.VMEM((late_rows, WIDE), F32),
            pltpu.VMEM((1572, WIDE), F32),
            pltpu.VMEM((ROWS, WIDE), F32),
        ]
        + BACKWARD,
        d_mid, d_window, *parts, tok1, lay0, lay1, merge, dense, tok0, save0, lse0, mixed0, mid0,
        hpre0, carry1, flat1, flat2, seam,
        name="back_first", us=13.5, far=(step,),
    )
    step = early.send(late[0])
    keep, send = later(list(late), step)
    late_sum = finished(summing(keep, send, count))
    early = finished(early)
    early = call(
        functools.partial(place_early_kernel, sizes),
        [arr(EARLY_ROWS, WIDE), arr(8, WIDE)],
        [],
        *early,
        name="place_early", us=0.6,
    )
    new_params, new_first, new_second, loss, valid_count, norm = adamw(
        sizes, (*late_sum, *early, tail, sums), (params, moment_one, moment_two)
    )
    return (
        loss.reshape(()), valid_count.reshape(()), norm.reshape(()),
        new_params, new_first, new_second,
    )


def solution(mesh):
    placed = (
        P("slab", "mp", None, None),
        P("slab", "mp", None),
        P("slab", "mp", None),
        P(),
        P(),
        P(),
    )
    sizes = (mesh.shape["slab"], mesh.shape["mp"])
    return jax.shard_map(
        functools.partial(on_device, sizes),
        mesh=mesh,
        in_specs=placed,
        out_specs=(P(), P(), P(), P(), P(), P()),
        check_vma=False,
    )
```

```python
import functools

import jax
import jax.numpy as jnp
from jax import lax
from jax.experimental import pallas as pl
from jax.experimental.pallas import tpu as pltpu
from jax.sharding import PartitionSpec as P

EMB = 96
HEADS = 6
HDIM = 16
HID = 384
MERGE = 384
CLASSES = 14
WIN = 7
SHIFT = 3
LAYERS = 3
STEP = 10

F32 = jnp.float32
BF16 = jnp.bfloat16
eps_norm = 1e-05
beta_one = 0.9
beta_two = 0.999
adam_eps = 1e-08
learn_rate = 0.05
decay_rate = 0.05
clip_norm = 0.01
LOG2E = 1.4426950408889634

VOX = WIN * WIN * WIN
ROWS = 352
KEYS = 384
BLOCKS = ((0, 128), (128, 256), (256, 352))
WIDE = 128
PLANE = WIN * WIN
FAR = WIN - SHIFT
ROWS_A = SHIFT * FAR * WIN
ROWS_B = FAR * SHIFT * WIN
ROWS_C = SHIFT * SHIFT * WIN

MERGE_ROWS = 392
LAYER_ROWS = 1165
TAP_ROWS = 27 * EMB
GROUPS = 2280
NPARAM = 872558
HEAD_ROW = 6806
HEAD_ROWS = 11
HEAD_LANE = 32
LATE_ROWS = 3072
EARLY_ROWS = 3840
LAYER_BASE = (98, 389, 680)
CONV_BASE = (971, 1620)
CUTS = (0, 392, 688, 976, 2280)

R_QKV, R_QKVB, R_PROJ, R_PROJB = 4, 292, 295, 391
R_HID, R_HIDB, R_OUT, R_OUTB = 392, 776, 780, 1164


def iota(shape, dim):
    return lax.broadcasted_iota(jnp.int32, shape, dim)


def split(x):
    hi = x.astype(BF16)
    return hi, (x - hi.astype(F32)).astype(BF16)


def pair(x):
    return jnp.concatenate(split(x), 1)


def fold(y):
    half = y.shape[1] // 2
    return y[:, :half] + y[:, half:]


def fold_rows(y):
    half = y.shape[0] // 2
    return y[:half] + y[half:]


def dot(a, b):
    return jnp.dot(a, b, preferred_element_type=F32)


def dot_nt(a, b):
    return lax.dot_general(a, b, (((1,), (1,)), ((), ())), preferred_element_type=F32)


def weight_nn(w):
    top = pair(w)
    return jnp.concatenate([top, top], 0)


def weight_nt(w):
    hi, lo = split(w)
    return jnp.concatenate(
        [jnp.concatenate([hi, hi], 1), jnp.concatenate([lo, lo], 1)], 0
    )


def mm(x, w):
    return fold(dot(pair(x), weight_nn(w)))


def mm_nt(x, w):
    return fold(dot_nt(pair(x), weight_nt(w)))


def with_rows(x, rows):
    if x.shape[0] == rows:
        return x
    return jnp.concatenate([x, jnp.zeros((rows - x.shape[0], x.shape[1]), F32)], 0)


def rows_t(x):
    return jnp.concatenate(split(with_rows(x, -(-x.shape[0] // WIDE) * WIDE).T), 0)


def mm_tn(xt, y):
    return fold_rows(fold(dot(xt, pair(with_rows(y, xt.shape[1])))))


def deep(w):
    return jnp.concatenate([w, jnp.zeros((WIDE - EMB, w.shape[1]), F32)], 0)


def roll(x, shift, axis):
    return pltpu.roll(x, shift, axis)


def four_to_three(y):
    lane = iota(y[0].shape, 1)
    a = jnp.where(lane < 96, y[0], roll(y[1], 96, 1))
    b = jnp.where(lane < 64, roll(y[1], 96, 1), roll(y[2], 64, 1))
    c = jnp.where(lane < 32, roll(y[2], 64, 1), roll(y[3], 32, 1))
    return a, b, c


def three_to_four(x):
    lane = iota(x[0].shape, 1)
    live = lane < EMB
    a = x[0]
    b = jnp.where(lane < 32, roll(x[0], 32, 1), roll(x[1], 32, 1))
    c = jnp.where(lane < 64, roll(x[1], 64, 1), roll(x[2], 64, 1))
    d = roll(x[2], 96, 1)
    return tuple(jnp.where(live, v, 0.0) for v in (a, b, c, d))


def hidden_rows(ref, start, count):
    return jnp.concatenate(
        four_to_three([ref[pl.ds(start + c, count, stride=4), :] for c in range(4)]), 1
    )


def put_hidden_rows(ref, start, count, x):
    parts = three_to_four([x[:, i * WIDE : (i + 1) * WIDE] for i in range(3)])
    for c in range(4):
        ref[pl.ds(start + c, count, stride=4), :] = parts[c]


def flatten(ref, start, groups, out):
    parts = four_to_three([ref[pl.ds(start + c, groups, stride=4), :] for c in range(4)])
    for c in range(3):
        out[pl.ds(c, groups, stride=3), :] = parts[c]


def norm_stats(x):
    live = iota(x.shape, 1) < EMB
    mean = jnp.sum(x, 1, keepdims=True) * (1.0 / EMB)
    centred = jnp.where(live, x - mean, 0.0)
    var = jnp.sum(centred * centred, 1, keepdims=True) * (1.0 / EMB)
    inv = lax.rsqrt(var + eps_norm)
    return centred * inv, inv


def norm(x, gain, bias):
    hat, _ = norm_stats(x)
    return hat * gain + bias


def norm_back(hat, inv, gain, grad):
    up = grad * gain
    one = jnp.sum(up, 1, keepdims=True) * (1.0 / EMB)
    two = jnp.sum(up * hat, 1, keepdims=True) * (1.0 / EMB)
    live = iota(hat.shape, 1) < EMB
    return jnp.where(live, inv * (up - one - hat * two), 0.0)


def colsum(x):
    return jnp.sum(x, 0, keepdims=True)


def gelu(x):
    return 0.5 * x * (1.0 + lax.erf(x * (0.5**0.5)))


def gelu_both(x):
    cdf = 0.5 * (1.0 + lax.erf(x * (0.5**0.5)))
    slope = cdf + x * (jnp.exp(x * x * -0.5) * 0.3989422804014327)
    return x * cdf, slope


def head_groups(x):
    lane = iota(x.shape, 1)
    swapped = roll(x, 64, 1)
    return jnp.where(lane < 64, x, swapped), jnp.where(lane < 64, swapped, x)


def as_left(x):
    both = []
    low = iota(x.shape, 1) < 64
    for part in head_groups(x):
        hi = part.astype(BF16).astype(F32)
        one = jnp.where(low, hi, part - hi).astype(BF16)
        both.append(jnp.concatenate([one, one], 1))
    return both


def as_right(x):
    return [pair(part) for part in head_groups(with_rows(x, KEYS))]


def head_mask(h, width):
    lane = iota((1, width), 1)
    lane = jnp.bitwise_and(lane, 63)
    low = jnp.bitwise_and(h, 3) * HDIM
    return jnp.where((lane >= low) & (lane < low + HDIM), 1.0, 0.0)


def own_lanes(h):
    lane = iota((1, WIDE), 1)
    return jnp.where((lane >= h * HDIM) & (lane < (h + 1) * HDIM), 1.0, 0.0)


def both_heads(right, heads, out):
    for k, h in enumerate(heads):
        out[k * KEYS : (k + 1) * KEYS, :] = right * head_mask(h, 2 * WIDE).astype(BF16)


def score_tiles(s, rows, region):
    tiles = [s[:, i * WIDE : (i + 1) * WIDE] for i in range(3)]
    if region is not None:
        return [t + region[rows, i * WIDE : (i + 1) * WIDE] for i, t in enumerate(tiles)]
    pad = jnp.where(iota((1, WIDE), 1) < VOX - 2 * WIDE, 0.0, -1e30)
    return tiles[:2] + [tiles[2] + pad]


def put_split(ref, rows, i, x):
    hi, lo = split(x)
    ref[rows, i * WIDE : (i + 1) * WIDE] = hi
    ref[rows, KEYS + i * WIDE : KEYS + (i + 1) * WIDE] = lo


def attention(normed, layer, save, lse, mixed, sc, region=None):
    left, right, values = sc
    x = pair(normed)
    qkv = []
    for i in range(3):
        w = deep(layer[pl.ds(R_QKV + i, EMB, stride=3), :])
        y = fold(dot(x, weight_nn(w))) + layer[R_QKVB + i : R_QKVB + i + 1, :]
        if i == 0:
            y = y * (HDIM**-0.5 * LOG2E)
        save[:, i * WIDE : (i + 1) * WIDE] = y
        qkv.append(y)
    for g, part in enumerate(as_left(qkv[0])):
        left[g] = part
    for g, part in enumerate(as_right(qkv[1])):
        right[g] = part
    v = jnp.where(iota((ROWS, WIDE), 1) == EMB, 1.0, qkv[2])
    v = pair(with_rows(v, KEYS))
    values[0:KEYS, :] = v
    values[KEYS : 2 * KEYS, :] = v
    mixed[...] = jnp.zeros_like(mixed)
    lse[...] = jnp.zeros_like(lse)

    def per_pair(pair_of, carry):
        heads = [2 * pair_of, 2 * pair_of + 1]
        masks = [head_mask(h, 2 * WIDE).astype(BF16) for h in heads]
        lanes = [own_lanes(h) for h in heads]
        spots = [jnp.where(iota((1, WIDE), 1) == h, 1.0, 0.0) for h in heads]
        g = lax.div(pair_of, 2)
        for block in BLOCKS:
            rows = slice(*block)
            out = level = 0.0
            for k in range(2):
                s = dot_nt(left[g, rows, :] * masks[k], right[g])
                tiles = score_tiles(s, rows, region)
                top = jnp.maximum(jnp.maximum(tiles[0], tiles[1]), tiles[2])
                top = jnp.max(top, 1, keepdims=True)
                parts = [split(jnp.exp2(t - top)) for t in tiles]
                e = jnp.concatenate([p[0] for p in parts] + [p[1] for p in parts], 1)
                o = fold(dot(e, values[...]))
                total = o[:, EMB : EMB + 1]
                out = out + o * (lanes[k] / total)
                level = level + (top + jnp.log(total) * LOG2E) * spots[k]
            mixed[rows, :] += out
            lse[rows, :] += level
        return carry

    lax.fori_loop(0, HEADS // 2, per_pair, 0)
    proj = deep(layer[R_PROJ : R_PROJ + EMB, :])
    return mm(mixed[...], proj) + layer[R_PROJB : R_PROJB + 1, :]


def attention_back(grad, normed, layer, save, lse, mixed, sc, grads, at, region=None):
    left, right, gleft, vright, keys, dq, dkv_t, weights, slopes = sc[:9]
    q_t, do_t, dmix, s, dp, two_keys, two_values = sc[9:]
    proj = deep(layer[R_PROJ : R_PROJ + EMB, :])
    grads[at + R_PROJ : at + R_PROJ + EMB, :] = mm_tn(rows_t(mixed[...]), grad)[:EMB]
    grads[at + R_PROJB : at + R_PROJB + 1, :] = colsum(grad)
    d_mixed = mm_nt(grad, proj)
    dmix[...] = d_mixed * mixed[...]
    q, k, v = (save[:, i * WIDE : (i + 1) * WIDE] for i in range(3))
    for g, part in enumerate(as_left(q)):
        left[g] = part
    for g, part in enumerate(as_right(k)):
        right[g] = part
    for g, part in enumerate(as_left(d_mixed)):
        gleft[g] = part
    for g, part in enumerate(as_right(v)):
        vright[g] = part
    kk = pair(with_rows(k, KEYS))
    keys[0:KEYS, :] = kk
    keys[KEYS : 2 * KEYS, :] = kk
    weights[:, ROWS:, :] = jnp.zeros((2, KEYS - ROWS, 2 * KEYS), BF16)
    slopes[:, ROWS:, :] = jnp.zeros((2, KEYS - ROWS, 2 * KEYS), BF16)
    for ref, x in ((q_t, q), (do_t, d_mixed)):
        hi, lo = split(with_rows(x, KEYS).T)
        ref[0] = hi
        ref[1] = lo
    dq[...] = jnp.zeros_like(dq)
    dkv_t[...] = jnp.zeros_like(dkv_t)

    def per_pair(pair_of, carry):
        g = lax.div(pair_of, 2)
        heads = [2 * pair_of, 2 * pair_of + 1]
        both_heads(right[g], heads, two_keys)
        both_heads(vright[g], heads, two_values)
        s[...] = dot_nt(left[g], two_keys[...])
        dp[...] = dot_nt(gleft[g], two_values[...])
        for k in range(2):
            h = 2 * pair_of + k
            lanes = own_lanes(h)
            at_h = jnp.where(iota((1, WIDE), 1) == h, 1.0, 0.0)
            for block in BLOCKS:
                rows = slice(*block)
                level = jnp.sum(lse[rows, :] * at_h, 1, keepdims=True)
                delta = jnp.sum(dmix[rows, :] * lanes, 1, keepdims=True)
                at_k = k * KEYS
                tiles = score_tiles(s[rows, at_k : at_k + KEYS], rows, region)
                for i, t in enumerate(tiles):
                    p = jnp.exp2(t - level)
                    put_split(weights.at[k], rows, i, p)
                    low = at_k + i * WIDE
                    p = p * (dp[rows, low : low + WIDE] - delta)
                    put_split(slopes.at[k], rows, i, p)
        total = 0.0
        for k in range(2):
            out = fold(dot(slopes[k, 0:ROWS, :], keys[...]))
            total = total + out * own_lanes(2 * pair_of + k)
        dq[...] += total
        for k in range(2):
            here = pl.ds(pl.multiple_of((2 * pair_of + k) * HDIM, HDIM), HDIM)
            for i, (t, m) in enumerate(((q_t, slopes), (do_t, weights))):
                lhs = jnp.concatenate([t[0, here, :], t[1, here, :]], 0)
                dkv_t[i, here, :] = fold_rows(fold(dot(lhs, m[k])))
        return carry

    lax.fori_loop(0, HEADS // 2, per_pair, 0)
    d_q = dq[...] * HDIM**-0.5
    d_k = dkv_t[0].T[0:ROWS] * (1.0 / LOG2E)
    d_v = dkv_t[1].T[0:ROWS]
    x_t = rows_t(normed)
    d_normed = None
    for i, d in enumerate((d_q, d_k, d_v)):
        grads[pl.ds(at + R_QKV + i, EMB, stride=3), :] = mm_tn(x_t, d)[:EMB]
        grads[at + R_QKVB + i : at + R_QKVB + i + 1, :] = colsum(d)
        part = mm_nt(d, deep(layer[pl.ds(R_QKV + i, EMB, stride=3), :]))
        d_normed = part if d_normed is None else d_normed + part
    return d_normed


def mlp(middle, layer, hpre):
    normed = norm(middle, layer[2:3, :], layer[3:4, :])
    w = deep(hidden_rows(layer, R_HID, EMB))
    pre = mm(normed, w) + hidden_rows(layer, R_HIDB, 1)
    hpre[...] = pre
    out = mm(gelu(pre), layer[R_OUT : R_OUT + HID, :])
    return middle + out + layer[R_OUTB : R_OUTB + 1, :]


def mlp_back(grad, middle, hpre, layer, grads, at):
    hat, inv = norm_stats(middle)
    normed = hat * layer[2:3, :] + layer[3:4, :]
    act, slope = gelu_both(hpre[...])
    grads[at + R_OUTB : at + R_OUTB + 1, :] = colsum(grad)
    grads[at + R_OUT : at + R_OUT + HID, :] = mm_tn(rows_t(grad), act).T
    d_pre = mm_nt(grad, layer[R_OUT : R_OUT + HID, :]) * slope
    put_hidden_rows(grads, at + R_HIDB, 1, colsum(d_pre))
    put_hidden_rows(grads, at + R_HID, EMB, mm_tn(rows_t(normed), d_pre)[:EMB])
    d_normed = mm_nt(d_pre, deep(hidden_rows(layer, R_HID, EMB)))
    grads[at + 2 : at + 3, :] = colsum(d_normed * hat)
    grads[at + 3 : at + 4, :] = colsum(d_normed)
    return grad + norm_back(hat, inv, layer[2:3, :], d_normed)


def pre_norm_back(grad, tokens, layer, grads, at):
    hat, inv = norm_stats(tokens)
    grads[at : at + 1, :] = colsum(grad * hat)
    grads[at + 1 : at + 2, :] = colsum(grad)
    return norm_back(hat, inv, layer[0:1, :], grad)


def region_of(rows, sizes):
    d = lax.shift_right_logical(rows * 1338, 16)
    line = lax.shift_right_logical(rows * 9363, 16)
    places = (d, line - d * WIN, rows - line * WIN)
    starts = (lax.axis_index("slab") * WIN, lax.axis_index("mp") * WIN, 0)
    total = None
    for place, start, blocks in zip(places, starts, sizes + (1,)):
        turned = jnp.where(place < SHIFT, place + FAR, place - SHIFT) + start
        length = WIN * blocks
        part = jnp.where(turned < length - WIN, 0, jnp.where(turned < length - SHIFT, 1, 2))
        total = part if total is None else total * 3 + part
    return total


def put_region(region, sizes):
    rows = region_of(iota((ROWS, WIDE), 0), sizes)[:, 0:1]
    lanes = region_of(iota((8, KEYS), 1), sizes)[0:1, :]
    apart = jnp.where(rows == lanes, 0.0, -100.0 * LOG2E)
    region[...] = jnp.where(iota((ROWS, KEYS), 1) < VOX, apart, -1e30)


def send_parts(ref, a, b, c):
    far = FAR * WIN
    near = SHIFT * WIN
    for d in range(SHIFT):
        base = d * PLANE
        c[d * near : (d + 1) * near, :] = ref[base : base + near, :]
        a[d * far : (d + 1) * far, :] = ref[base + near : base + PLANE, :]
    for d in range(FAR):
        base = (d + SHIFT) * PLANE
        b[d * near : (d + 1) * near, :] = ref[base : base + near, :]


def take_parts(own, a, b, c, out):
    far = FAR * WIN
    near = SHIFT * WIN
    for d in range(WIN):
        base = d * PLANE
        if d < SHIFT:
            out[base : base + near, :] = c[d * near : (d + 1) * near, :]
            out[base + near : base + PLANE, :] = a[d * far : (d + 1) * far, :]
        else:
            e = d - SHIFT
            out[base : base + near, :] = b[e * near : (e + 1) * near, :]
            out[base + near : base + PLANE, :] = own[base + near : base + PLANE, :]
    out[VOX:, :] = jnp.zeros((ROWS - VOX, WIDE), F32)


def span_of(groups):
    low, high = groups
    first = 3 * low // 8 * 8
    last = -(-3 * high // 8) * 8
    return first, min(last, NPARAM // WIDE // 8 * 8) - first


def copied(params, groups, flat, sem):
    first, rows = span_of(groups)
    size = rows * WIDE
    return pltpu.make_async_copy(
        params.at[pl.ds(first * WIDE, size)], flat.at[pl.ds(0, size)], sem
    )


def relay(groups, flat, out, square, last=None):
    low, high = groups
    first, rows = span_of(groups)
    square[0:rows, :] = flat[0 : rows * WIDE].reshape(rows, WIDE)
    if last is not None:
        square[rows : rows + 24, :] = jnp.zeros((24, WIDE), F32)
        square[rows : rows + 1, 0 : last.shape[0]] = last[...].reshape(1, last.shape[0])
    skip = 3 * low - first
    n = high - low
    parts = three_to_four([square[pl.ds(skip + c, n, stride=3), :] for c in range(3)])
    for c in range(4):
        out[pl.ds(c, n, stride=4), :] = parts[c]


FIRST_SPANS = ((0, 98), (98, 392))
LAYER_SPANS = ((389, 681), (680, 972))
CONV_SPANS = ((971, 1620), (1620, GROUPS))


def prep_kernel(spans, params, *refs, last=None):
    outs, (flats, square, sems) = refs[: len(spans)], refs[-3:]
    for i, groups in enumerate(spans):
        copied(params, groups, flats[i], sems.at[i]).start()
    for i, groups in enumerate(spans):
        copied(params, groups, flats[i], sems.at[i]).wait()
        relay(groups, flats[i], outs[i], square, last if i == len(spans) - 1 else None)


def head_picks():
    width = HEAD_ROWS * WIDE
    place = iota((WIDE, width), 1) - HEAD_LANE
    row = iota((WIDE, width), 0)
    here = (place >= row * CLASSES) & (place < (row + 1) * CLASSES) & (row <= EMB)
    place = iota((width, WIDE), 0) - HEAD_LANE
    col = iota((width, WIDE), 1)
    row = lax.shift_right_logical(place * 4682, 16)
    there = (place - row * CLASSES == col) & (place >= 0)
    return jnp.where(here, 1.0, 0.0), jnp.where(there, 1.0, 0.0).astype(BF16)


def prep_conv0_kernel(params, conv0, weights0, bias, *scratch):
    prep_kernel(CONV_SPANS[:1], params, conv0, *scratch)
    tap_weights(conv0, 3, weights0)
    bias[0:1, :] = conv0[3 + TAP_ROWS : 4 + TAP_ROWS, :]
    bias[1:8, :] = jnp.zeros((7, WIDE), F32)


def prep_conv1_kernel(last, bias, params, conv1, head, weights1, vectors, *scratch):
    prep_kernel(CONV_SPANS[1:], params, conv1, *scratch, last=last)
    tap_weights(conv1, 0, weights1)
    vectors[0:1, :] = bias[0:1, :]
    vectors[1:4, :] = conv1[TAP_ROWS : TAP_ROWS + 3, :]
    vectors[4:8, :] = jnp.zeros((4, WIDE), F32)
    square = scratch[1]
    first, _ = span_of(CONV_SPANS[1])
    row = jnp.concatenate(
        [square[HEAD_ROW + i - first : HEAD_ROW + i - first + 1, :] for i in range(HEAD_ROWS)], 1
    )
    here, there = head_picks()
    hi, lo = split(here * row)
    head[...] = dot(hi, there) + dot(lo, there)


def head_rows(d_head, out, at):
    here, there = head_picks()
    hi, lo = split(d_head)
    spread = (dot_nt(hi, there) + dot_nt(lo, there)) * here
    row = colsum(spread)
    for i in range(HEAD_ROWS):
        out[at + i : at + i + 1, :] += row[:, i * WIDE : (i + 1) * WIDE]


class Rows:
    def __init__(self, ref, at):
        self.ref, self.at = ref, at

    def __getitem__(self, key):
        rows, lanes = key
        if isinstance(rows, slice):
            rows = slice(rows.start + self.at, rows.stop + self.at)
        else:
            rows = pl.ds(rows.start + self.at, rows.size, stride=rows.stride)
        return self.ref[rows, lanes]


def merged_norm(x):
    mean = jnp.sum(x, 1, keepdims=True) * (1.0 / MERGE)
    centred = x - mean
    var = jnp.sum(centred * centred, 1, keepdims=True) * (1.0 / MERGE)
    return centred * lax.rsqrt(var + eps_norm)


def first_kernel(
    feats, merge, lay0,
    dense, tok0, save, lse, mixed, middle, hpre, tok1, ahead, pa, pb, pc,
    *sc,
):
    dense[VOX:, :] = jnp.zeros((ROWS - VOX, MERGE), F32)
    for line in range(PLANE):
        dense[line * WIN : (line + 1) * WIN, :] = feats[line]
    hat = merged_norm(dense[...])
    normed = hat * hidden_rows(merge, 0, 1) + hidden_rows(merge, 4, 1)
    tokens = mm(normed, merge[8 : 8 + MERGE, :])
    tok0[...] = tokens
    layer = Rows(lay0, 0)
    normed = norm(tokens, layer[0:1, :], layer[1:2, :])
    attended = attention(normed, layer, save, lse, mixed, sc)
    mid = tokens + attended
    middle[...] = mid
    tokens = mlp(mid, layer, hpre)
    tok1[...] = tokens
    ahead[...] = norm(tokens, layer[1165:1166, :], layer[1166:1167, :])
    send_parts(ahead, pa, pb, pc)


def shifted_kernel(
    sizes,
    own, pa, pb, pc, lay1, _,
    window, save, lse, mixed, out, qa, qb, qc,
    region, *sc,
):
    put_region(region, sizes)
    take_parts(own, pa, pb, pc, window)
    out[...] = attention(
        window[...], Rows(lay1, 1), save, lse, mixed, sc, region
    )
    send_parts(out, qa, qb, qc)


def to_lines(ref, out):
    for line in range(PLANE):
        out[line, 0:WIN, :] = ref[line * WIN : (line + 1) * WIN, :]
        out[line, WIN:8, :] = jnp.zeros((8 - WIN, WIDE), F32)


def from_lines(ref, out):
    out[VOX:, :] = jnp.zeros((ROWS - VOX, WIDE), F32)
    for line in range(PLANE):
        out[line * WIN : (line + 1) * WIN, :] = ref[line, 0:WIN, :]


def send_sides(lines, near_d, far_d, near_h, far_h):
    odd_d = jnp.bitwise_and(lax.axis_index("slab"), 1) == 1
    odd_h = jnp.bitwise_and(lax.axis_index("mp"), 1) == 1
    low, high = lines[0 : 2 * WIN], lines[(WIN - 2) * WIN : PLANE]
    near_d[...] = jnp.where(odd_d, low, high)
    far_d[...] = jnp.where(odd_d, high, low)
    for d in range(WIN):
        low = lines[d * WIN : d * WIN + 2]
        high = lines[d * WIN + WIN - 2 : (d + 1) * WIN]
        near_h[2 * d : 2 * d + 2] = jnp.where(odd_h, low, high)
        far_h[2 * d : 2 * d + 2] = jnp.where(odd_h, high, low)


def second_kernel(
    tok1, own, qa, qb, qc, lay1, lay2, _,
    mid1, hpre1, tok2, save, lse, mixed, mid2, hpre2, lines,
    s0, s1, s2, s3,
    attended, *sc,
):
    take_parts(own, qa, qb, qc, attended)
    mid = tok1[...] + attended[...]
    mid1[...] = mid
    tokens = mlp(mid, Rows(lay1, 1), hpre1)
    tok2[...] = tokens
    layer = Rows(lay2, 2)
    normed = norm(tokens, layer[0:1, :], layer[1:2, :])
    mid = tokens + attention(normed, layer, save, lse, mixed, sc)
    mid2[...] = mid
    attended[...] = mlp(mid, layer, hpre2)
    to_lines(attended, lines)
    send_sides(lines, s0, s1, s2, s3)


def grown_lines(sizes, own, near_d, far_d, near_h, far_h, out):
    slab, row = lax.axis_index("slab"), lax.axis_index("mp")
    odd_d = jnp.bitwise_and(slab, 1) == 1
    odd_h = jnp.bitwise_and(row, 1) == 1
    out[:, 11:12] = jnp.zeros((11, 1, 8, WIDE), F32)
    for d in range(WIN):
        out[d + 2, 2 : 2 + WIN] = own[d * WIN : (d + 1) * WIN]
    for d in range(2):
        near = near_d[d * WIN : (d + 1) * WIN]
        far = far_d[d * WIN : (d + 1) * WIN]
        out[d, 2 : 2 + WIN] = jnp.where(odd_d, near, jnp.where(slab == 0, 0.0, far))
        out[d + 9, 2 : 2 + WIN] = jnp.where(
            odd_d, jnp.where(slab == sizes[0] - 1, 0.0, far), near
        )
    for d in range(11):
        near = near_h[2 * d : 2 * d + 2]
        far = far_h[2 * d : 2 * d + 2]
        out[d, 0:2] = jnp.where(odd_h, near, jnp.where(row == 0, 0.0, far))
        out[d, 9:11] = jnp.where(odd_h, jnp.where(row == sizes[1] - 1, 0.0, far), near)


def put_marks(labels, valid, out):
    across = iota((8, WIN), 1) == iota((8, WIN), 0)
    classes = iota((8, WIDE), 1) - EMB
    for d in range(WIN):
        code = jnp.where(valid[d] == 1, labels[d], -1 - EMB - WIDE)
        code = code.astype(F32)
        for h in range(WIN):
            line = jnp.where(across, code[h : h + 1, :], 0.0)
            column = jnp.sum(line, 1, keepdims=True)
            mark = jnp.where(column == classes.astype(F32), 1.0, 0.0)
            out[d * WIN + h] = jnp.where(iota((8, WIDE), 0) < WIN, mark, 0.0)


def taps(source, first_plane, planes, first_line, lines, out):
    def per_plane(d, carry):
        for c in range(3):
            for b in range(3):
                x = source[d + first_plane, first_line + b : first_line + b + lines]
                if c != 1:
                    x = roll(x, 1 if c == 0 else 7, 1)
                x = pair(x.reshape(lines * 8, WIDE))
                at = pl.multiple_of(d * (lines * 8), lines * 8)
                t = b * 3 + c
                out[pl.ds(at, lines * 8), t * 256 : (t + 1) * 256] = x
        return carry

    lax.fori_loop(0, planes, per_plane, 0)


def tap_weights(ref, at, out):
    def per_tap(i, carry):
        w = deep(ref[pl.ds(i * EMB + at, EMB), :])
        out[pl.ds(pl.multiple_of(i * 256, 256), 256), :] = weight_nn(w)
        return carry

    lax.fori_loop(0, 27, per_tap, 0)


def tap_weights_back(ref, at, out):
    for i in range(27):
        w = deep(ref[(26 - i) * EMB + at : (27 - i) * EMB + at, :]).T
        out[i * 256 : (i + 1) * 256, :] = weight_nn(w)


def conv(side, weights, planes, pitch, out):
    for start in range(planes):
        total = None
        for a in range(3):
            low = (start + a) * pitch
            x = side[low : low + pitch, :]
            part = dot(x, weights[a * 2304 : (a + 1) * 2304, :])
            total = part if total is None else total + part
        out[start * pitch : (start + 1) * pitch, :] = fold(total)


def conv_weight_grad(side, grad_rows, pitch, out, at):
    rows = 512
    g = jnp.concatenate([grad_rows, jnp.zeros((rows - grad_rows.shape[0], WIDE), F32)], 0)
    left = jnp.concatenate(split(g.T[:EMB]), 0)
    for a in range(3):
        for bc in range(9):
            y = dot(left, side[a * pitch : a * pitch + rows, bc * 256 : (bc + 1) * 256])
            y = deep(fold_rows(fold(y))).T
            t = a * 9 + bc
            out[at + t * EMB : at + (t + 1) * EMB, :] = y[:EMB]


def volume_mask(sizes, planes, lines, reach, real_lines):
    slab, row = lax.axis_index("slab"), lax.axis_index("mp")
    ends = (slab == 0, slab == sizes[0] - 1, row == 0, row == sizes[1] - 1)
    shape = (planes, lines, 8, WIDE)
    d, h, w = iota(shape, 0), iota(shape, 1), iota(shape, 2)
    low_d = jnp.where(ends[0], reach, 0)
    high_d = jnp.where(ends[1], planes - reach, planes)
    low_h = jnp.where(ends[2], reach, 0)
    high_h = jnp.where(ends[3], real_lines - reach, real_lines)
    inside = (d >= low_d) & (d < high_d) & (h >= low_h) & (h < high_h) & (w < WIN)
    return jnp.where(inside, 1.0, 0.0)


def conv_kernel(
    sizes,
    own, s0, s1, s2, s3, labels, valid, weights0, weights1, vectors, _,
    grown, pre, tok, stats, t0, t1, t2, t3,
    act, side, side_own, marks, result,
):
    grown_lines(sizes, own, s0, s1, s2, s3, grown)
    put_marks(labels, valid, marks)
    taps(grown, 0, 11, 0, 10, side)
    bias0 = vectors[0:1, :]
    inside = volume_mask(sizes, 9, 10, 1, 9)

    conv(side, weights0, 9, 80, result)
    z = (result[...] + bias0).reshape(9, 10, 8, WIDE)
    pre[...] = z
    act[...] = gelu(z) * inside
    taps(act, 0, 9, 0, 8, side_own)
    bias1 = vectors[1:2, :]
    conv(side_own, weights1, WIN, 64, result)
    y = (result[0 : WIN * 64, :] + bias1).reshape(WIN, 8, 8, WIDE)[:, 0:WIN]
    y = y + own[...].reshape(WIN, WIN, 8, WIDE)
    y = jnp.where(iota(y.shape, 2) < WIN, y, 0.0).reshape(PLANE, 8, WIDE)
    tok[...] = y + marks[...]
    send_sides(tok, t0, t1, t2, t3)
    flat = y.reshape(PLANE * 8, WIDE)
    count = jnp.sum(marks[...].reshape(PLANE * 8, WIDE))
    row = iota((8, WIDE), 0)
    stats[...] = (
        jnp.where(row == 0, colsum(flat), 0.0)
        + jnp.where(row == 1, colsum(flat * flat), 0.0)
        + jnp.where(row == 2, count, 0.0)
    )


def head_kernel(
    sizes, voxels,
    own, s0, s1, s2, s3, sums, vectors, head_w,
    grown, slope_out, stats, d_head, d_rows,
):
    grown_lines(sizes, own, s0, s1, s2, s3, grown)
    rows = 11 * 12 * 8
    both = grown[...].reshape(rows, WIDE)
    lane = iota((rows, WIDE), 1)
    tokens = jnp.where(lane < EMB, both, 0.0)
    target = jnp.where(lane < CLASSES, roll(both, WIDE - EMB, 1), 0.0)
    live = jnp.sum(target, 1, keepdims=True)
    count = F32(voxels)
    average = sums[0:1, :] / count
    spread = sums[1:2, :] / count - average * average
    inv = lax.rsqrt(spread + eps_norm)
    gain = vectors[2:3, :]
    bias = vectors[3:4, :]
    hat = (tokens - average) * inv
    act, slope = gelu_both(hat * gain + bias)
    act = jnp.where(lane == EMB, 1.0, act)
    w = head_w[...]
    logits = mm(act, w)
    logits = jnp.where(lane < CLASSES, logits, -1e30)
    top = jnp.max(logits, 1, keepdims=True)
    e = jnp.exp(logits - top)
    total = jnp.sum(e, 1, keepdims=True)
    logp = logits - top - jnp.log(total)
    scale = 1.0 / sums[2:3, 0:1]
    d_logits = (e / total * live - target) * scale
    d_normed = jnp.where(lane < EMB, mm_nt(d_logits, w) * slope, 0.0)
    d_tokens = d_normed * gain * inv
    slope_out[...] = d_tokens.reshape(11, 12, 8, WIDE)

    def own_rows(x):
        x = x.reshape(11, 12, 8, WIDE)[2:9, 2:9]
        x = jnp.where(iota(x.shape, 2) < WIN, x, 0.0)
        return x.reshape(PLANE * 8, WIDE)

    loss = -jnp.sum(own_rows(target * jnp.where(lane < CLASSES, logp, 0.0)))
    own_d = own_rows(d_logits)
    own_n = own_rows(d_normed)
    own_hat = own_rows(hat)
    zeros = jnp.zeros((512 - PLANE * 8, WIDE), F32)
    left = rows_t(jnp.concatenate([own_d, zeros], 0))
    d_head[...] = mm_tn(left, jnp.concatenate([own_rows(act), zeros], 0)).T
    d_gain = colsum(own_n * own_hat)
    d_bias = colsum(own_n)
    d_average = -d_bias * gain * inv
    d_spread = d_gain * gain * inv * inv * -0.5
    d_two = d_spread / count
    d_one = (d_average - 2.0 * average * d_spread) / count
    row = iota((8, WIDE), 0)
    live_lane = iota((8, WIDE), 1) < EMB
    stats[...] = (
        jnp.where((row == 0) & live_lane, d_one, 0.0)
        + jnp.where((row == 1) & live_lane, d_two, 0.0)
        + jnp.where(row == 2, loss, 0.0)
    )
    d_rows[...] = (
        jnp.where(row == 0, d_gain, 0.0)
        + jnp.where(row == 1, d_bias, 0.0)
    )


def sides_back_kernel(sizes, grown, pre, side_act, side_grown, act):
    act[0:9] = gelu(pre[...]) * volume_mask(sizes, 9, 10, 1, 9)
    act[9:10] = jnp.zeros((1, 10, 8, WIDE), F32)
    taps(act, 0, 10, 0, 8, side_act)
    taps(grown, 1, 10, 1, 8, side_grown)


def weights_back_kernel(conv0, conv1, weights0, weights1):
    tap_weights_back(conv0, 3, weights0)
    tap_weights_back(conv1, 0, weights1)


def conv_back_kernel(
    sizes,
    tok, slope, sums, pre, side_act, side_grown, weights0, weights1, d_rows, d_head,
    d_own, keep, send, carry, seam,
    grads, dgrown, act, side, side_own, flat, result,
):
    lane = iota((11, 12, 8, WIDE), 3)
    inside = volume_mask(sizes, 11, 12, 2, 11)
    steady = sums[0:1, :].reshape(1, 1, 1, WIDE)
    rising = 2.0 * sums[1:2, :].reshape(1, 1, 1, WIDE)
    d_tok = slope[...] + jnp.where(lane < EMB, (steady + tok[...] * rising) * inside, 0.0)
    dgrown[...] = d_tok
    grads[5191:, :] = jnp.zeros((45, WIDE), F32)
    grads[0:8, :] = jnp.zeros((8, WIDE), F32)
    grads[5189:5191, :] = d_rows[0:2, :]
    own = dgrown[2:9, 2:10]
    line = iota(own.shape, 1)
    own = jnp.where(line < WIN, own, 0.0).reshape(WIN * 64, WIDE)
    grads[5188:5189, :] = colsum(own)

    near = volume_mask(sizes, 9, 10, 1, 9)
    conv_weight_grad(side_act, own, 64, grads, 2596)
    taps(dgrown, 0, 11, 0, 10, side)

    conv(side, weights1, 9, 80, result)
    act[0:9] = result[...].reshape(9, 10, 8, WIDE) * gelu_both(pre[...])[1] * near

    own = act[1:8, 1:9]
    line = iota(own.shape, 1)
    own = jnp.where(line < WIN, own, 0.0).reshape(WIN * 64, WIDE)
    grads[2595:2596, :] = colsum(own)
    conv_weight_grad(side_grown, own, 64, grads, 3)
    carry[...] = grads[0:24, :]
    flat[3 * (GROUPS - CUTS[3]) :, :] = jnp.zeros((flat.shape[0] - 3912, WIDE), F32)
    flatten(grads, 20, GROUPS - CUTS[3], flat)
    start = 3 * CUTS[3]
    head_rows(d_head[...], flat, HEAD_ROW - start)
    seam[...] = flat[0 : LATE_ROWS - start, :]
    scatter(sizes, flat, LATE_ROWS - start, keep, send)
    taps(act, 0, 9, 0, 8, side_own)
    conv(side_own, weights0, WIN, 64, result)
    y = result[0 : WIN * 64, :].reshape(WIN, 8, 8, WIDE)[:, 0:WIN] + dgrown[2:9, 2:9]
    y = jnp.where(iota(y.shape, 2) < WIN, y, 0.0)
    d_own[...] = y.reshape(PLANE, 8, WIDE)


def back_mlp_kernel(d_own, lay2, mid2, hpre2, d_mid, grads, dense):
    from_lines(d_own, dense)
    grads[...] = jnp.zeros_like(grads)
    d_mid[...] = mlp_back(dense[...], mid2[...], hpre2, Rows(lay2, 2), grads, 2)


def back_two_kernel(
    d_mid2, grads2, carry, lay1, lay2, tok2, save, lse, mixed, mid1, hpre1,
    d_mid, grads1, flat, carry2, pa, pb, pc,
    grads, *sc,
):
    layer = Rows(lay2, 2)
    grads[0:1168, :] = grads2[...]
    d = d_mid2[...]
    tokens = tok2[...]
    normed = norm(tokens, layer[0:1, :], layer[1:2, :])
    d_normed = attention_back(d, normed, layer, save, lse, mixed, sc, grads, 2)
    d = d + pre_norm_back(d_normed, tokens, layer, grads, 2)
    grads[1167:1184, :] = carry[3:20, :]
    flatten(grads, 32, CUTS[3] - CUTS[2], flat)
    carry2[...] = grads[0:32, :]
    layer = Rows(lay1, 1)
    d = mlp_back(d, mid1[...], hpre1, layer, grads1, 1)
    d_mid[...] = d
    send_parts(d_mid, pa, pb, pc)


def back_shifted_kernel(
    sizes,
    own, pa, pb, pc, lay1, window, save, lse, mixed, grads1, carry2, _,
    d_window, flat, carry1, qa, qb, qc,
    region, grads, grad, *sc,
):
    put_region(region, sizes)
    take_parts(own, pa, pb, pc, grad)
    grads[0:1168, :] = grads1[...]
    grads[0:3, :] = jnp.zeros((3, WIDE), F32)
    d_window[...] = attention_back(
        grad[...], window[...], Rows(lay1, 1), save, lse, mixed, sc, grads, 1,
        region,
    )
    send_parts(d_window, qa, qb, qc)
    grads[1166:1196, :] = carry2[2:32, :]
    flatten(grads, 12, CUTS[2] - CUTS[1], flat)
    carry1[...] = grads[0:16, :]


def back_first_kernel(
    sizes,
    d_mid, own, qa, qb, qc, tok1, lay0, lay1, merge, dense, tok0, save, lse, mixed, middle, hpre,
    carry1, flat1, flat2, seam, _,
    keep, send,
    flat, grads, grad, *sc,
):
    take_parts(own, qa, qb, qc, grad)
    grads[1556:1572, :] = carry1[...]
    d = d_mid[...] + pre_norm_back(grad[...], tok1[...], Rows(lay1, 1), grads, 1557)
    layer = Rows(lay0, 0)
    at = MERGE_ROWS
    d = mlp_back(d, middle[...], hpre, layer, grads, at)
    tokens = tok0[...]
    normed = norm(tokens, layer[0:1, :], layer[1:2, :])
    d_normed = attention_back(d, normed, layer, save, lse, mixed, sc, grads, at)
    d = d + pre_norm_back(d_normed, tokens, layer, grads, at)
    live = iota((ROWS, WIDE), 0) < VOX
    d = jnp.where(live, d, 0.0)
    hat = merged_norm(dense[...])
    gain = hidden_rows(merge, 0, 1)
    bias = hidden_rows(merge, 4, 1)
    w = merge[8 : 8 + MERGE, :]
    put_hidden_rows(grads, 8 - 8, 1, jnp.zeros((1, MERGE), F32))
    grads[8 : 8 + MERGE, :] = mm_tn(rows_t(d), hat * gain + bias).T
    d_hat = mm_nt(d, w)
    put_hidden_rows(grads, 0, 1, colsum(d_hat * hat))
    put_hidden_rows(grads, 4, 1, colsum(d_hat))
    flatten(grads, 0, CUTS[1], flat)
    at = 0
    for cut, part in ((CUTS[1], flat1), (CUTS[2], flat2), (CUTS[3], seam)):
        at = 3 * cut
        flat[at : at + part.shape[0], :] = part[...]
    at += seam.shape[0]
    if flat.shape[0] > at:
        flat[at:, :] = jnp.zeros((flat.shape[0] - at, WIDE), F32)
    scatter(sizes, flat, 0, keep, send)


def radices(count):
    steps = [2]
    left = count // 2
    while left > 1:
        steps.append(4 if left >= 4 else 2)
        left //= steps[-1]
    return steps


def block_rows(rows, count):
    return -(-rows // (8 * count)) * 8


def own_number(sizes):
    return lax.axis_index("slab") * sizes[1] + lax.axis_index("mp")


def place_in_half(distance, count):
    place = 0
    shift = 1
    for radix in radices(count)[1:]:
        digit = jnp.bitwise_and(lax.shift_right_logical(distance, shift), radix - 1)
        place = place * radix + digit
        shift += radix.bit_length() - 1
    return place


def scatter(sizes, source, first, keep, send):
    count = sizes[0] * sizes[1]
    rows = keep.shape[0] * 2 // count
    me = own_number(sizes)
    odd = jnp.bitwise_and(me, 1)

    def per_pair(t, carry):
        for block, out in ((2 * t + odd, keep), (2 * t + 1 - odd, send)):
            place = place_in_half(jnp.bitwise_xor(block, me), count)
            at = pl.multiple_of(first + block * rows, 8)
            to = pl.multiple_of(place * rows, 8)
            out[pl.ds(to, rows), :] = source[pl.ds(at, rows), :]
        return carry

    lax.fori_loop(0, count // 2, per_pair, 0)


def traded(value, distance, count):
    pairs = [(i, i ^ distance) for i in range(count)]
    return lax.ppermute(value, ("slab", "mp"), pairs)


def later(got, after):
    return got if after is None else list(lax.optimization_barrier((*got, after)))[:-1]


def summing(keep, send, count):
    steps = radices(count)
    got = [keep, traded(send, 1, count)]
    shift = 1
    after = yield None
    for radix in steps[1:]:
        got = later(got, after)
        total = sum(got[1:], got[0])
        rows = total.shape[0] // radix
        parts = [total[k * rows : (k + 1) * rows] for k in range(radix)]
        got = parts[:1] + [traded(parts[k], k << shift, count) for k in range(1, radix)]
        shift += radix.bit_length() - 1
        after = yield parts[0]
    got = later(got, after)
    own = sum(got[1:], got[0])
    for radix in reversed(steps[1:]):
        shift -= radix.bit_length() - 1
        got = [own] + [traded(own, k << shift, count) for k in range(1, radix)]
        after = yield own
        own = jnp.concatenate(later(got, after), 0)
        yield own
    yield own, traded(own, 1, count)


def finished(chain, after=None):
    last = next(chain) if after is None else chain.send(after)
    while not isinstance(last, tuple):
        last = next(chain)
    return last


def exchanged_sum(value, count):
    shift = 0
    for radix in radices(count):
        got = [value] + [traded(value, k << shift, count) for k in range(1, radix)]
        while len(got) > 1:
            got = [got[i] + got[i + 1] for i in range(0, len(got), 2)]
        value = got[0]
        shift += radix.bit_length() - 1
    return value


PIECE = 294912


def place_blocks(sizes, own, other, out, size):
    count = sizes[0] * sizes[1]
    me = own_number(sizes)
    rows = own.shape[0] * 2 // count

    def per_block(block, carry):
        distance = jnp.bitwise_xor(block, me)
        at = pl.ds(pl.multiple_of(place_in_half(distance, count) * rows, 8), rows)
        near = jnp.bitwise_and(distance, 1) == 0
        to = pl.ds(pl.multiple_of(block * rows, 8), rows)
        out[to, :] = jnp.where(near, own[at, :], other[at, :])
        return carry

    lax.fori_loop(0, size // rows, per_block, 0)


def squares(*refs):
    total = jnp.zeros((8, WIDE), F32)
    for ref in refs:
        x = ref[...]
        total = total + jnp.sum((x * x).reshape(-1, 8, WIDE), 0)
    return total


def place_early_kernel(sizes, own, other, out, square):
    place_blocks(sizes, own, other, out, EARLY_ROWS)
    square[...] = squares(own, other)


def adamw_kernel(
    sizes,
    late, late_other, early, square, tail, sums, params, first, second,
    new_params, new_first, new_second, loss, valid, norm_out,
    grad, scale_ref,
):
    step = pl.program_id(0)

    @pl.when(step == 0)
    def gather():
        norm = jnp.sqrt(jnp.sum(squares(late, late_other) + square[...]))
        loss[0] = jnp.sum(tail[2:3, 0:1])
        valid[0] = jnp.sum(sums[2:3, 0:1])
        norm_out[0] = norm
        scale_ref[0] = jnp.minimum(1.0, clip_norm / (norm + 1e-06))
        place_blocks(sizes, late, late_other, grad, LATE_ROWS)
        grad[LATE_ROWS:, :] = early[...]

    def update(base, low, size):
        rows = -(-size // 1024) * 8
        at = pl.ds(pl.multiple_of(base // WIDE + low // WIDE, 8), rows)
        g = grad[at, :].reshape(rows * WIDE)[:size] * scale_ref[0]
        here = pl.ds(pl.multiple_of(base + low, 1024), size)
        one = beta_one * first[here] + (1.0 - beta_one) * g
        two = beta_two * second[here] + (1.0 - beta_two) * g * g
        there = pl.ds(low, size)
        new_first[there] = one
        new_second[there] = two
        two = two * (1.0 / (1.0 - beta_two**STEP))
        low_by = two * lax.rsqrt(jnp.maximum(two, 1e-37)) + adam_eps
        inverse = pl.reciprocal(low_by, approx=True)
        inverse = inverse * (2.0 - low_by * inverse)
        new_params[there] = params[here] * (1.0 - learn_rate * decay_rate) - (
            one * (learn_rate / (1.0 - beta_one**STEP))
        ) * inverse

    whole = NPARAM // PIECE

    @pl.when(step < whole)
    def full():
        def part(i, carry):
            low = pl.multiple_of(i * 16384, 16384)
            update(step * PIECE, low, 16384)
            return carry

        lax.fori_loop(0, PIECE // 16384, part, 0)

    @pl.when(step == whole)
    def last():
        rest = NPARAM - whole * PIECE
        main = rest // 1024 * 1024
        for low in range(0, main, 16384):
            update(whole * PIECE, low, min(16384, main - low))
        update(whole * PIECE, main, rest - main)


def adamw(sizes, parts, arrays):
    pieces = -(-NPARAM // PIECE)
    piece = pl.BlockSpec((PIECE,), lambda i: (i,))
    vmem = pl.BlockSpec(memory_space=pltpu.VMEM)
    smem = pl.BlockSpec(memory_space=pltpu.SMEM)
    return pl.pallas_call(
        functools.partial(adamw_kernel, sizes),
        grid=(pieces,),
        out_shape=[arr(NPARAM)] * 3 + [arr(1)] * 3,
        in_specs=[vmem] * (len(parts) + len(arrays)),
        out_specs=[piece] * 3 + [smem] * 3,
        scratch_shapes=[pltpu.VMEM((LATE_ROWS + EARLY_ROWS, WIDE), F32), pltpu.SMEM((1,), F32)],
        compiler_params=pltpu.CompilerParams(vmem_limit_bytes=16 * 1024 * 1024),
        cost_estimate=pl.CostEstimate(flops=6 * 10**9, bytes_accessed=0, transcendentals=0),
        name="adamw",
    )(*parts, *arrays)


def arr(*shape):
    return jax.ShapeDtypeStruct(shape, F32)


def call(kernel, outs, scratch, *args, name=None, us=1.0, far=(), mib=16):
    vmem = pl.BlockSpec(memory_space=pltpu.VMEM)
    smem = pl.BlockSpec(memory_space=pltpu.SMEM)
    return pl.pallas_call(
        kernel,
        out_shape=list(outs),
        in_specs=[vmem] * len(args) + [pl.BlockSpec(memory_space=pl.ANY)] * len(far),
        out_specs=[smem if o.shape == (1,) else vmem for o in outs],
        scratch_shapes=list(scratch),
        compiler_params=pltpu.CompilerParams(vmem_limit_bytes=mib * 1024 * 1024),
        cost_estimate=pl.CostEstimate(
            flops=int(us * 1.15e9), bytes_accessed=0, transcendentals=0
        ),
        name=name,
    )(*args, *far)


SQUARE = arr(ROWS, WIDE)
SAVE = arr(ROWS, 3 * WIDE)
FORWARD = [
    pltpu.VMEM((2, ROWS, 2 * WIDE), BF16),
    pltpu.VMEM((2, KEYS, 2 * WIDE), BF16),
    pltpu.VMEM((2 * KEYS, 2 * WIDE), BF16),
]
BACKWARD = [
    pltpu.VMEM((2, ROWS, 2 * WIDE), BF16),
    pltpu.VMEM((2, KEYS, 2 * WIDE), BF16),
    pltpu.VMEM((2, ROWS, 2 * WIDE), BF16),
    pltpu.VMEM((2, KEYS, 2 * WIDE), BF16),
    pltpu.VMEM((2 * KEYS, 2 * WIDE), BF16),
    pltpu.VMEM((ROWS, WIDE), F32),
    pltpu.VMEM((2, WIDE, KEYS), F32),
    pltpu.VMEM((2, KEYS, 2 * KEYS), BF16),
    pltpu.VMEM((2, KEYS, 2 * KEYS), BF16),
    pltpu.VMEM((2, WIDE, KEYS), BF16),
    pltpu.VMEM((2, WIDE, KEYS), BF16),
    pltpu.VMEM((ROWS, WIDE), F32),
    pltpu.VMEM((ROWS, 2 * KEYS), F32),
    pltpu.VMEM((ROWS, 2 * KEYS), F32),
    pltpu.VMEM((2 * KEYS, 2 * WIDE), BF16),
    pltpu.VMEM((2 * KEYS, 2 * WIDE), BF16),
]
PARTS = [arr(ROWS_A, WIDE), arr(ROWS_B, WIDE), arr(ROWS_C, WIDE)]


def passed(parts, steps, sizes):
    slabs, rows = sizes
    moved = []
    for part, (ds, dm) in zip(parts, ((1, 0), (0, 1), (1, 1))):
        pairs = []
        for s in range(slabs):
            for m in range(rows):
                target = ((s + steps * ds) % slabs) * rows + (m + steps * dm) % rows
                pairs.append((s * rows + m, target))
        moved.append(lax.ppermute(part, ("slab", "mp"), pairs))
    return moved


SIDES = [arr(2 * WIN, 8, WIDE)] * 4


def paired(axis, size):
    near = [(i, i ^ 1) for i in range(size)]
    far = [(i, (i + (1 if i % 2 else -1)) % size) for i in range(size)]
    return (
        lambda value: lax.ppermute(value, axis, near),
        lambda value: lax.ppermute(value, axis, far),
    )


def column_kernel(sizes, near_d, far_d, near_h, far_h, near_out, far_out):
    slab = lax.axis_index("slab")
    odd_d = jnp.bitwise_and(slab, 1) == 1
    odd_h = jnp.bitwise_and(lax.axis_index("mp"), 1) == 1
    at_low = slab == 0
    at_high = slab == sizes[0] - 1
    near_out[4:18] = near_h[...]
    far_out[4:18] = far_h[...]
    for d in range(2):
        near = near_d[d * WIN : (d + 1) * WIN]
        far = far_d[d * WIN : (d + 1) * WIN]
        before = jnp.where(odd_d, near, jnp.where(at_low, 0.0, far))
        after = jnp.where(odd_d, jnp.where(at_high, 0.0, far), near)
        for x, at in ((before, 2 * d), (after, 18 + 2 * d)):
            low, high = x[0:2], x[WIN - 2 : WIN]
            near_out[at : at + 2] = jnp.where(odd_h, low, high)
            far_out[at : at + 2] = jnp.where(odd_h, high, low)


def beside(sides, sizes):
    near, far = paired("slab", sizes[0])
    near_d, far_d = near(sides[0]), far(sides[1])
    near_h, far_h = call(
        functools.partial(column_kernel, sizes), [arr(22, 8, WIDE)] * 2, [],
        near_d, far_d, sides[2], sides[3],
        name="column", us=0.3,
    )
    near, far = paired("mp", sizes[1])
    return near_d, far_d, near(near_h), far(far_h)


REGION = [pltpu.VMEM((ROWS, KEYS), F32)]


def on_device(sizes, feats, labels, valid, params, moment_one, moment_two):
    slabs, rows = sizes
    count = slabs * rows

    def room(spans):
        sizes = [(span_of(groups)[1] + 8) * WIDE for groups in spans]
        return [
            [pltpu.VMEM((size,), F32) for size in sizes],
            pltpu.VMEM((2048, WIDE), F32),
            pltpu.SemaphoreType.DMA((len(spans),)),
        ]

    first_size = FIRST_SPANS[-1][1] * 384
    merge, lay0 = call(
        functools.partial(prep_kernel, FIRST_SPANS),
        [arr(MERGE_ROWS, WIDE), arr(1176, WIDE)],
        room(FIRST_SPANS),
        name="prep_first", us=2.0, far=(params[:first_size],),
    )
    lay1, lay2 = call(
        functools.partial(prep_kernel, LAYER_SPANS),
        [arr(1168, WIDE)] * 2,
        room(LAYER_SPANS),
        name="prep_layers", us=2.0, far=(params,),
    )
    taps_shape = jax.ShapeDtypeStruct((27 * 256, 256), BF16)
    conv0, weights0, bias0 = call(
        prep_conv0_kernel,
        [arr(2596, WIDE), taps_shape, arr(8, WIDE)],
        room(CONV_SPANS[:1]),
        name="prep_conv0", us=1.5, far=(params,),
    )
    conv1, head_w, weights1, vectors = call(
        prep_conv1_kernel,
        [arr(2640, WIDE), arr(WIDE, WIDE), taps_shape, arr(8, WIDE)],
        room(CONV_SPANS[1:]),
        params[NPARAM // WIDE * WIDE :], bias0,
        name="prep_conv1", us=1.5, far=(params,),
    )

    dense, tok0, save0, lse0, mixed0, mid0, hpre0, tok1, ahead, *parts = call(
        first_kernel,
        [arr(ROWS, MERGE), SQUARE, SAVE, SQUARE, SQUARE, SQUARE, arr(ROWS, HID), SQUARE, SQUARE]
        + PARTS,
        FORWARD,
        feats.reshape(PLANE, WIN, MERGE), merge, lay0,
        name="first", us=6.0,
    )
    parts = passed(parts, -1, sizes)
    window, save1, lse1, mixed1, out1, *parts = call(
        functools.partial(shifted_kernel, sizes),
        [SQUARE, SAVE, SQUARE, SQUARE, SQUARE] + PARTS,
        REGION + FORWARD,
        ahead, *parts, lay1,
        name="shifted", us=4.5, far=(weights0,),
    )
    parts = passed(parts, 1, sizes)
    mid1, hpre1, tok2, save2, lse2, mixed2, mid2, hpre2, lines, *sides = call(
        second_kernel,
        [SQUARE, arr(ROWS, HID), SQUARE, SAVE, SQUARE, SQUARE, SQUARE, arr(ROWS, HID)]
        + [arr(PLANE, 8, WIDE)] + SIDES,
        [pltpu.VMEM((ROWS, WIDE), F32)] + FORWARD,
        tok1, out1, *parts, lay1, lay2,
        name="second", us=6.5, far=(weights1,),
    )
    sides = beside(sides, sizes)
    back0, back1 = call(
        weights_back_kernel,
        [taps_shape] * 2,
        [],
        conv0, conv1,
        name="weights_back", us=1.5,
    )
    grown, pre, tok3, sums, *tok_sides = call(
        functools.partial(conv_kernel, sizes),
        [arr(11, 12, 8, WIDE), arr(9, 10, 8, WIDE), arr(PLANE, 8, WIDE), arr(8, WIDE)] + SIDES,
        [
            pltpu.VMEM((9, 10, 8, WIDE), F32),
            pltpu.VMEM((880, 2304), BF16),
            pltpu.VMEM((576, 2304), BF16),
            pltpu.VMEM((PLANE, 8, WIDE), F32),
            pltpu.VMEM((720, WIDE), F32),
        ],
        lines, *sides, labels, valid, weights0, weights1, vectors,
        name="conv", us=8.0, mib=20, far=(back0,),
    )
    tok_sides = beside(tok_sides, sizes)
    side_act, side_grown = call(
        functools.partial(sides_back_kernel, sizes),
        [jax.ShapeDtypeStruct((640, 2304), BF16)] * 2,
        [pltpu.VMEM((10, 10, 8, WIDE), F32)],
        grown, pre,
        name="sides_back", us=2.0,
    )
    sums = exchanged_sum(sums, count)
    voxels = WIN * slabs * WIN * rows * WIN
    tok3, slope, tail, d_head, d_rows = call(
        functools.partial(head_kernel, sizes, voxels),
        [arr(11, 12, 8, WIDE), arr(11, 12, 8, WIDE), arr(8, WIDE), arr(WIDE, WIDE), arr(8, WIDE)],
        [],
        tok3, *tok_sides, sums, vectors, head_w,
        name="head", us=3.5,
    )
    tail = exchanged_sum(tail, count)
    late_rows = block_rows(LATE_ROWS, count) * count
    early_rows = block_rows(EARLY_ROWS, count) * count
    seam_rows = LATE_ROWS - 3 * CUTS[3]
    d_own, keep, send, carry3, seam = call(
        functools.partial(conv_back_kernel, sizes),
        [arr(PLANE, 8, WIDE)] + [arr(early_rows // 2, WIDE)] * 2
        + [arr(24, WIDE), arr(seam_rows, WIDE)],
        [
            pltpu.VMEM((5236, WIDE), F32),
            pltpu.VMEM((11, 12, 8, WIDE), F32),
            pltpu.VMEM((10, 10, 8, WIDE), F32),
            pltpu.VMEM((880, 2304), BF16),
            pltpu.VMEM((576, 2304), BF16),
            pltpu.VMEM((seam_rows + early_rows, WIDE), F32),
            pltpu.VMEM((720, WIDE), F32),
        ],
        tok3, slope, tail, pre, side_act, side_grown, back0, back1, d_rows, d_head,
        name="conv_back", us=14.0, mib=28,
    )
    early = summing(keep, send, count)
    next(early)
    d_mid2, grads2 = call(
        back_mlp_kernel,
        [SQUARE, arr(1168, WIDE)],
        [pltpu.VMEM((ROWS, WIDE), F32)],
        d_own, lay2, mid2, hpre2,
        name="back_mlp", us=3.0,
    )
    step = early.send(d_mid2)
    d_mid, grads1, flat2, carry2, *parts = call(
        back_two_kernel,
        [SQUARE, arr(1168, WIDE), arr(3 * (CUTS[3] - CUTS[2]), WIDE), arr(32, WIDE)] + PARTS,
        [pltpu.VMEM((1184, WIDE), F32)] + BACKWARD,
        d_mid2, grads2, carry3, lay1, lay2, tok2, save2, lse2, mixed2, mid1, hpre1,
        name="back_two", us=9.0,
    )
    parts = passed(parts, -1, sizes)
    step = early.send(d_mid)
    d_window, flat1, carry1, *parts = call(
        functools.partial(back_shifted_kernel, sizes),
        [SQUARE, arr(3 * (CUTS[2] - CUTS[1]), WIDE), arr(16, WIDE)] + PARTS,
        REGION + [pltpu.VMEM((1200, WIDE), F32), pltpu.VMEM((ROWS, WIDE), F32)] + BACKWARD,
        d_mid, *parts, lay1, window, save1, lse1, mixed1, grads1, carry2,
        name="back_shifted", us=10.5, far=(step,),
    )
    early.send(d_window)
    parts = passed(parts, 1, sizes)
    next(early)
    step = next(early)
    late = call(
        functools.partial(back_first_kernel, sizes),
        [arr(late_rows // 2, WIDE)] * 2,
        [
            pltpu.VMEM((late_rows, WIDE), F32),
            pltpu.VMEM((1572, WIDE), F32),
            pltpu.VMEM((ROWS, WIDE), F32),
        ]
        + BACKWARD,
        d_mid, d_window, *parts, tok1, lay0, lay1, merge, dense, tok0, save0, lse0, mixed0, mid0,
        hpre0, carry1, flat1, flat2, seam,
        name="back_first", us=13.5, far=(step,),
    )
    step = early.send(late[0])
    keep, send = later(list(late), step)
    late_sum = finished(summing(keep, send, count))
    early = finished(early)
    early = call(
        functools.partial(place_early_kernel, sizes),
        [arr(EARLY_ROWS, WIDE), arr(8, WIDE)],
        [],
        *early,
        name="place_early", us=0.6,
    )
    new_params, new_first, new_second, loss, valid_count, norm = adamw(
        sizes, (*late_sum, *early, tail, sums), (params, moment_one, moment_two)
    )
    return (
        loss.reshape(()), valid_count.reshape(()), norm.reshape(()),
        new_params, new_first, new_second,
    )


def solution(mesh):
    placed = (
        P("slab", "mp", None, None),
        P("slab", "mp", None),
        P("slab", "mp", None),
        P(),
        P(),
        P(),
    )
    sizes = (mesh.shape["slab"], mesh.shape["mp"])
    return jax.shard_map(
        functools.partial(on_device, sizes),
        mesh=mesh,
        in_specs=placed,
        out_specs=(P(), P(), P(), P(), P(), P()),
        check_vma=False,
    )
```

```python
import functools

import jax
import jax.numpy as jnp
from jax import lax
from jax.experimental import pallas as pl
from jax.experimental.pallas import tpu as pltpu
from jax.sharding import PartitionSpec as P

EMB = 96
HEADS = 6
HDIM = 16
HID = 384
MERGE = 384
CLASSES = 14
WIN = 7
SHIFT = 3
LAYERS = 3
STEP = 10

F32 = jnp.float32
BF16 = jnp.bfloat16
eps_norm = 1e-05
beta_one = 0.9
beta_two = 0.999
adam_eps = 1e-08
learn_rate = 0.05
decay_rate = 0.05
clip_norm = 0.01
LOG2E = 1.4426950408889634

VOX = WIN * WIN * WIN
ROWS = 352
KEYS = 384
BLOCKS = ((0, 128), (128, 256), (256, 352))
WIDE = 128
PLANE = WIN * WIN
FAR = WIN - SHIFT
ROWS_A = SHIFT * FAR * WIN
ROWS_B = FAR * SHIFT * WIN
ROWS_C = SHIFT * SHIFT * WIN

MERGE_ROWS = 392
LAYER_ROWS = 1165
TAP_ROWS = 27 * EMB
GROUPS = 2280
NPARAM = 872558
HEAD_ROW = 6806
HEAD_ROWS = 11
HEAD_LANE = 32
LATE_ROWS = 3072
EARLY_ROWS = 3840
LAYER_BASE = (98, 389, 680)
CONV_BASE = (971, 1620)
CUTS = (0, 392, 688, 976, 2280)

R_QKV, R_QKVB, R_PROJ, R_PROJB = 4, 292, 295, 391
R_HID, R_HIDB, R_OUT, R_OUTB = 392, 776, 780, 1164


def iota(shape, dim):
    return lax.broadcasted_iota(jnp.int32, shape, dim)


def split(x):
    hi = x.astype(BF16)
    return hi, (x - hi.astype(F32)).astype(BF16)


def pair(x):
    return jnp.concatenate(split(x), 1)


def fold(y):
    half = y.shape[1] // 2
    return y[:, :half] + y[:, half:]


def fold_rows(y):
    half = y.shape[0] // 2
    return y[:half] + y[half:]


def dot(a, b):
    return jnp.dot(a, b, preferred_element_type=F32)


def dot_nt(a, b):
    return lax.dot_general(a, b, (((1,), (1,)), ((), ())), preferred_element_type=F32)


def weight_nn(w):
    top = pair(w)
    return jnp.concatenate([top, top], 0)


def weight_nt(w):
    hi, lo = split(w)
    return jnp.concatenate(
        [jnp.concatenate([hi, hi], 1), jnp.concatenate([lo, lo], 1)], 0
    )


def mm(x, w):
    return fold(dot(pair(x), weight_nn(w)))


def mm_nt(x, w):
    return fold(dot_nt(pair(x), weight_nt(w)))


def with_rows(x, rows):
    if x.shape[0] == rows:
        return x
    return jnp.concatenate([x, jnp.zeros((rows - x.shape[0], x.shape[1]), F32)], 0)


def rows_t(x):
    return jnp.concatenate(split(with_rows(x, -(-x.shape[0] // WIDE) * WIDE).T), 0)


def mm_tn(xt, y):
    return fold_rows(fold(dot(xt, pair(with_rows(y, xt.shape[1])))))


def deep(w):
    return jnp.concatenate([w, jnp.zeros((WIDE - EMB, w.shape[1]), F32)], 0)


def roll(x, shift, axis):
    return pltpu.roll(x, shift, axis)


def four_to_three(y):
    lane = iota(y[0].shape, 1)
    a = jnp.where(lane < 96, y[0], roll(y[1], 96, 1))
    b = jnp.where(lane < 64, roll(y[1], 96, 1), roll(y[2], 64, 1))
    c = jnp.where(lane < 32, roll(y[2], 64, 1), roll(y[3], 32, 1))
    return a, b, c


def three_to_four(x):
    lane = iota(x[0].shape, 1)
    live = lane < EMB
    a = x[0]
    b = jnp.where(lane < 32, roll(x[0], 32, 1), roll(x[1], 32, 1))
    c = jnp.where(lane < 64, roll(x[1], 64, 1), roll(x[2], 64, 1))
    d = roll(x[2], 96, 1)
    return tuple(jnp.where(live, v, 0.0) for v in (a, b, c, d))


def hidden_rows(ref, start, count):
    return jnp.concatenate(
        four_to_three([ref[pl.ds(start + c, count, stride=4), :] for c in range(4)]), 1
    )


def put_hidden_rows(ref, start, count, x):
    parts = three_to_four([x[:, i * WIDE : (i + 1) * WIDE] for i in range(3)])
    for c in range(4):
        ref[pl.ds(start + c, count, stride=4), :] = parts[c]


def flatten(ref, start, groups, out):
    parts = four_to_three([ref[pl.ds(start + c, groups, stride=4), :] for c in range(4)])
    for c in range(3):
        out[pl.ds(c, groups, stride=3), :] = parts[c]


def norm_stats(x):
    live = iota(x.shape, 1) < EMB
    mean = jnp.sum(x, 1, keepdims=True) * (1.0 / EMB)
    centred = jnp.where(live, x - mean, 0.0)
    var = jnp.sum(centred * centred, 1, keepdims=True) * (1.0 / EMB)
    inv = lax.rsqrt(var + eps_norm)
    return centred * inv, inv


def norm(x, gain, bias):
    hat, _ = norm_stats(x)
    return hat * gain + bias


def norm_back(hat, inv, gain, grad):
    up = grad * gain
    one = jnp.sum(up, 1, keepdims=True) * (1.0 / EMB)
    two = jnp.sum(up * hat, 1, keepdims=True) * (1.0 / EMB)
    live = iota(hat.shape, 1) < EMB
    return jnp.where(live, inv * (up - one - hat * two), 0.0)


def colsum(x):
    return jnp.sum(x, 0, keepdims=True)


def gelu(x):
    return 0.5 * x * (1.0 + lax.erf(x * (0.5**0.5)))


def gelu_both(x):
    cdf = 0.5 * (1.0 + lax.erf(x * (0.5**0.5)))
    slope = cdf + x * (jnp.exp(x * x * -0.5) * 0.3989422804014327)
    return x * cdf, slope


def head_groups(x):
    lane = iota(x.shape, 1)
    swapped = roll(x, 64, 1)
    return jnp.where(lane < 64, x, swapped), jnp.where(lane < 64, swapped, x)


def as_left(x):
    both = []
    low = iota(x.shape, 1) < 64
    for part in head_groups(x):
        hi = part.astype(BF16).astype(F32)
        one = jnp.where(low, hi, part - hi).astype(BF16)
        both.append(jnp.concatenate([one, one], 1))
    return both


def as_right(x):
    return [pair(part) for part in head_groups(with_rows(x, KEYS))]


def head_mask(h, width):
    lane = iota((1, width), 1)
    lane = jnp.bitwise_and(lane, 63)
    low = jnp.bitwise_and(h, 3) * HDIM
    return jnp.where((lane >= low) & (lane < low + HDIM), 1.0, 0.0)


def own_lanes(h):
    lane = iota((1, WIDE), 1)
    return jnp.where((lane >= h * HDIM) & (lane < (h + 1) * HDIM), 1.0, 0.0)


def both_heads(right, heads, out):
    for k, h in enumerate(heads):
        out[k * KEYS : (k + 1) * KEYS, :] = right * head_mask(h, 2 * WIDE).astype(BF16)


def score_tiles(s, rows, region):
    tiles = [s[:, i * WIDE : (i + 1) * WIDE] for i in range(3)]
    if region is not None:
        return [t + region[rows, i * WIDE : (i + 1) * WIDE] for i, t in enumerate(tiles)]
    pad = jnp.where(iota((1, WIDE), 1) < VOX - 2 * WIDE, 0.0, -1e30)
    return tiles[:2] + [tiles[2] + pad]


def put_split(ref, rows, i, x):
    hi, lo = split(x)
    ref[rows, i * WIDE : (i + 1) * WIDE] = hi
    ref[rows, KEYS + i * WIDE : KEYS + (i + 1) * WIDE] = lo


def attention(normed, layer, save, lse, mixed, sc, region=None):
    left, right, values = sc
    x = pair(normed)
    qkv = []
    for i in range(3):
        w = deep(layer[pl.ds(R_QKV + i, EMB, stride=3), :])
        y = fold(dot(x, weight_nn(w))) + layer[R_QKVB + i : R_QKVB + i + 1, :]
        if i == 0:
            y = y * (HDIM**-0.5 * LOG2E)
        save[:, i * WIDE : (i + 1) * WIDE] = y
        qkv.append(y)
    for g, part in enumerate(as_left(qkv[0])):
        left[g] = part
    for g, part in enumerate(as_right(qkv[1])):
        right[g] = part
    v = jnp.where(iota((ROWS, WIDE), 1) == EMB, 1.0, qkv[2])
    v = pair(with_rows(v, KEYS))
    values[0:KEYS, :] = v
    values[KEYS : 2 * KEYS, :] = v
    mixed[...] = jnp.zeros_like(mixed)
    lse[...] = jnp.zeros_like(lse)

    def per_pair(pair_of, carry):
        heads = [2 * pair_of, 2 * pair_of + 1]
        masks = [head_mask(h, 2 * WIDE).astype(BF16) for h in heads]
        lanes = [own_lanes(h) for h in heads]
        spots = [jnp.where(iota((1, WIDE), 1) == h, 1.0, 0.0) for h in heads]
        g = lax.div(pair_of, 2)
        for block in BLOCKS:
            rows = slice(*block)
            out = level = 0.0
            for k in range(2):
                s = dot_nt(left[g, rows, :] * masks[k], right[g])
                tiles = score_tiles(s, rows, region)
                top = jnp.maximum(jnp.maximum(tiles[0], tiles[1]), tiles[2])
                top = jnp.max(top, 1, keepdims=True)
                parts = [split(jnp.exp2(t - top)) for t in tiles]
                e = jnp.concatenate([p[0] for p in parts] + [p[1] for p in parts], 1)
                o = fold(dot(e, values[...]))
                total = o[:, EMB : EMB + 1]
                out = out + o * (lanes[k] / total)
                level = level + (top + jnp.log(total) * LOG2E) * spots[k]
            mixed[rows, :] += out
            lse[rows, :] += level
        return carry

    lax.fori_loop(0, HEADS // 2, per_pair, 0)
    proj = deep(layer[R_PROJ : R_PROJ + EMB, :])
    return mm(mixed[...], proj) + layer[R_PROJB : R_PROJB + 1, :]


def attention_back(grad, normed, layer, save, lse, mixed, sc, grads, at, region=None):
    left, right, gleft, vright, keys, dq, dkv_t, weights, slopes = sc[:9]
    q_t, do_t, dmix, s, dp, two_keys, two_values = sc[9:]
    proj = deep(layer[R_PROJ : R_PROJ + EMB, :])
    grads[at + R_PROJ : at + R_PROJ + EMB, :] = mm_tn(rows_t(mixed[...]), grad)[:EMB]
    grads[at + R_PROJB : at + R_PROJB + 1, :] = colsum(grad)
    d_mixed = mm_nt(grad, proj)
    dmix[...] = d_mixed * mixed[...]
    q, k, v = (save[:, i * WIDE : (i + 1) * WIDE] for i in range(3))
    for g, part in enumerate(as_left(q)):
        left[g] = part
    for g, part in enumerate(as_right(k)):
        right[g] = part
    for g, part in enumerate(as_left(d_mixed)):
        gleft[g] = part
    for g, part in enumerate(as_right(v)):
        vright[g] = part
    kk = pair(with_rows(k, KEYS))
    keys[0:KEYS, :] = kk
    keys[KEYS : 2 * KEYS, :] = kk
    weights[:, ROWS:, :] = jnp.zeros((2, KEYS - ROWS, 2 * KEYS), BF16)
    slopes[:, ROWS:, :] = jnp.zeros((2, KEYS - ROWS, 2 * KEYS), BF16)
    for ref, x in ((q_t, q), (do_t, d_mixed)):
        hi, lo = split(with_rows(x, KEYS).T)
        ref[0] = hi
        ref[1] = lo
    dq[...] = jnp.zeros_like(dq)
    dkv_t[...] = jnp.zeros_like(dkv_t)

    def per_pair(pair_of, carry):
        g = lax.div(pair_of, 2)
        heads = [2 * pair_of, 2 * pair_of + 1]
        both_heads(right[g], heads, two_keys)
        both_heads(vright[g], heads, two_values)
        s[...] = dot_nt(left[g], two_keys[...])
        dp[...] = dot_nt(gleft[g], two_values[...])
        for k in range(2):
            h = 2 * pair_of + k
            lanes = own_lanes(h)
            at_h = jnp.where(iota((1, WIDE), 1) == h, 1.0, 0.0)
            for block in BLOCKS:
                rows = slice(*block)
                level = jnp.sum(lse[rows, :] * at_h, 1, keepdims=True)
                delta = jnp.sum(dmix[rows, :] * lanes, 1, keepdims=True)
                at_k = k * KEYS
                tiles = score_tiles(s[rows, at_k : at_k + KEYS], rows, region)
                for i, t in enumerate(tiles):
                    p = jnp.exp2(t - level)
                    put_split(weights.at[k], rows, i, p)
                    low = at_k + i * WIDE
                    p = p * (dp[rows, low : low + WIDE] - delta)
                    put_split(slopes.at[k], rows, i, p)
        total = 0.0
        for k in range(2):
            out = fold(dot(slopes[k, 0:ROWS, :], keys[...]))
            total = total + out * own_lanes(2 * pair_of + k)
        dq[...] += total
        for k in range(2):
            here = pl.ds(pl.multiple_of((2 * pair_of + k) * HDIM, HDIM), HDIM)
            for i, (t, m) in enumerate(((q_t, slopes), (do_t, weights))):
                lhs = jnp.concatenate([t[0, here, :], t[1, here, :]], 0)
                dkv_t[i, here, :] = fold_rows(fold(dot(lhs, m[k])))
        return carry

    lax.fori_loop(0, HEADS // 2, per_pair, 0)
    d_q = dq[...] * HDIM**-0.5
    d_k = dkv_t[0].T[0:ROWS] * (1.0 / LOG2E)
    d_v = dkv_t[1].T[0:ROWS]
    x_t = rows_t(normed)
    d_normed = None
    for i, d in enumerate((d_q, d_k, d_v)):
        grads[pl.ds(at + R_QKV + i, EMB, stride=3), :] = mm_tn(x_t, d)[:EMB]
        grads[at + R_QKVB + i : at + R_QKVB + i + 1, :] = colsum(d)
        part = mm_nt(d, deep(layer[pl.ds(R_QKV + i, EMB, stride=3), :]))
        d_normed = part if d_normed is None else d_normed + part
    return d_normed


def mlp(middle, layer, hpre):
    normed = norm(middle, layer[2:3, :], layer[3:4, :])
    w = deep(hidden_rows(layer, R_HID, EMB))
    pre = mm(normed, w) + hidden_rows(layer, R_HIDB, 1)
    hpre[...] = pre
    out = mm(gelu(pre), layer[R_OUT : R_OUT + HID, :])
    return middle + out + layer[R_OUTB : R_OUTB + 1, :]


def mlp_back(grad, middle, hpre, layer, grads, at):
    hat, inv = norm_stats(middle)
    normed = hat * layer[2:3, :] + layer[3:4, :]
    act, slope = gelu_both(hpre[...])
    grads[at + R_OUTB : at + R_OUTB + 1, :] = colsum(grad)
    grads[at + R_OUT : at + R_OUT + HID, :] = mm_tn(rows_t(grad), act).T
    d_pre = mm_nt(grad, layer[R_OUT : R_OUT + HID, :]) * slope
    put_hidden_rows(grads, at + R_HIDB, 1, colsum(d_pre))
    put_hidden_rows(grads, at + R_HID, EMB, mm_tn(rows_t(normed), d_pre)[:EMB])
    d_normed = mm_nt(d_pre, deep(hidden_rows(layer, R_HID, EMB)))
    grads[at + 2 : at + 3, :] = colsum(d_normed * hat)
    grads[at + 3 : at + 4, :] = colsum(d_normed)
    return grad + norm_back(hat, inv, layer[2:3, :], d_normed)


def pre_norm_back(grad, tokens, layer, grads, at):
    hat, inv = norm_stats(tokens)
    grads[at : at + 1, :] = colsum(grad * hat)
    grads[at + 1 : at + 2, :] = colsum(grad)
    return norm_back(hat, inv, layer[0:1, :], grad)


def region_of(rows, sizes):
    d = lax.shift_right_logical(rows * 1338, 16)
    line = lax.shift_right_logical(rows * 9363, 16)
    places = (d, line - d * WIN, rows - line * WIN)
    starts = (lax.axis_index("slab") * WIN, lax.axis_index("mp") * WIN, 0)
    total = None
    for place, start, blocks in zip(places, starts, sizes + (1,)):
        turned = jnp.where(place < SHIFT, place + FAR, place - SHIFT) + start
        length = WIN * blocks
        part = jnp.where(turned < length - WIN, 0, jnp.where(turned < length - SHIFT, 1, 2))
        total = part if total is None else total * 3 + part
    return total


def put_region(region, sizes):
    rows = region_of(iota((ROWS, WIDE), 0), sizes)[:, 0:1]
    lanes = region_of(iota((8, KEYS), 1), sizes)[0:1, :]
    apart = jnp.where(rows == lanes, 0.0, -100.0 * LOG2E)
    region[...] = jnp.where(iota((ROWS, KEYS), 1) < VOX, apart, -1e30)


def send_parts(ref, a, b, c):
    far = FAR * WIN
    near = SHIFT * WIN
    for d in range(SHIFT):
        base = d * PLANE
        c[d * near : (d + 1) * near, :] = ref[base : base + near, :]
        a[d * far : (d + 1) * far, :] = ref[base + near : base + PLANE, :]
    for d in range(FAR):
        base = (d + SHIFT) * PLANE
        b[d * near : (d + 1) * near, :] = ref[base : base + near, :]


def take_parts(own, a, b, c, out):
    far = FAR * WIN
    near = SHIFT * WIN
    for d in range(WIN):
        base = d * PLANE
        if d < SHIFT:
            out[base : base + near, :] = c[d * near : (d + 1) * near, :]
            out[base + near : base + PLANE, :] = a[d * far : (d + 1) * far, :]
        else:
            e = d - SHIFT
            out[base : base + near, :] = b[e * near : (e + 1) * near, :]
            out[base + near : base + PLANE, :] = own[base + near : base + PLANE, :]
    out[VOX:, :] = jnp.zeros((ROWS - VOX, WIDE), F32)


def span_of(groups):
    low, high = groups
    first = 3 * low // 8 * 8
    last = -(-3 * high // 8) * 8
    return first, min(last, NPARAM // WIDE // 8 * 8) - first


def copied(params, groups, flat, sem):
    first, rows = span_of(groups)
    size = rows * WIDE
    return pltpu.make_async_copy(
        params.at[pl.ds(first * WIDE, size)], flat.at[pl.ds(0, size)], sem
    )


def relay(groups, flat, out, square, last=None):
    low, high = groups
    first, rows = span_of(groups)
    square[0:rows, :] = flat[0 : rows * WIDE].reshape(rows, WIDE)
    if last is not None:
        square[rows : rows + 24, :] = jnp.zeros((24, WIDE), F32)
        square[rows : rows + 1, 0 : last.shape[0]] = last[...].reshape(1, last.shape[0])
    skip = 3 * low - first
    n = high - low
    parts = three_to_four([square[pl.ds(skip + c, n, stride=3), :] for c in range(3)])
    for c in range(4):
        out[pl.ds(c, n, stride=4), :] = parts[c]


FIRST_SPANS = ((0, 98), (98, 392))
LAYER_SPANS = ((389, 681), (680, 972))
CONV_SPANS = ((971, 1620), (1620, GROUPS))


def prep_kernel(spans, params, *refs, last=None):
    outs, (flats, square, sems) = refs[: len(spans)], refs[-3:]
    for i, groups in enumerate(spans):
        copied(params, groups, flats[i], sems.at[i]).start()
    for i, groups in enumerate(spans):
        copied(params, groups, flats[i], sems.at[i]).wait()
        relay(groups, flats[i], outs[i], square, last if i == len(spans) - 1 else None)


def head_picks():
    width = HEAD_ROWS * WIDE
    place = iota((WIDE, width), 1) - HEAD_LANE
    row = iota((WIDE, width), 0)
    here = (place >= row * CLASSES) & (place < (row + 1) * CLASSES) & (row <= EMB)
    place = iota((width, WIDE), 0) - HEAD_LANE
    col = iota((width, WIDE), 1)
    row = lax.shift_right_logical(place * 4682, 16)
    there = (place - row * CLASSES == col) & (place >= 0)
    return jnp.where(here, 1.0, 0.0), jnp.where(there, 1.0, 0.0).astype(BF16)


def prep_conv0_kernel(params, conv0, weights0, bias, *scratch):
    prep_kernel(CONV_SPANS[:1], params, conv0, *scratch)
    tap_weights(conv0, 3, weights0)
    bias[0:1, :] = conv0[3 + TAP_ROWS : 4 + TAP_ROWS, :]
    bias[1:8, :] = jnp.zeros((7, WIDE), F32)


def prep_conv1_kernel(last, bias, params, conv1, head, weights1, vectors, *scratch):
    prep_kernel(CONV_SPANS[1:], params, conv1, *scratch, last=last)
    tap_weights(conv1, 0, weights1)
    vectors[0:1, :] = bias[0:1, :]
    vectors[1:4, :] = conv1[TAP_ROWS : TAP_ROWS + 3, :]
    vectors[4:8, :] = jnp.zeros((4, WIDE), F32)
    square = scratch[1]
    first, _ = span_of(CONV_SPANS[1])
    row = jnp.concatenate(
        [square[HEAD_ROW + i - first : HEAD_ROW + i - first + 1, :] for i in range(HEAD_ROWS)], 1
    )
    here, there = head_picks()
    hi, lo = split(here * row)
    head[...] = dot(hi, there) + dot(lo, there)


def head_rows(d_head, out, at):
    here, there = head_picks()
    hi, lo = split(d_head)
    spread = (dot_nt(hi, there) + dot_nt(lo, there)) * here
    row = colsum(spread)
    for i in range(HEAD_ROWS):
        out[at + i : at + i + 1, :] += row[:, i * WIDE : (i + 1) * WIDE]


class Rows:
    def __init__(self, ref, at):
        self.ref, self.at = ref, at

    def __getitem__(self, key):
        rows, lanes = key
        if isinstance(rows, slice):
            rows = slice(rows.start + self.at, rows.stop + self.at)
        else:
            rows = pl.ds(rows.start + self.at, rows.size, stride=rows.stride)
        return self.ref[rows, lanes]


def merged_norm(x):
    mean = jnp.sum(x, 1, keepdims=True) * (1.0 / MERGE)
    centred = x - mean
    var = jnp.sum(centred * centred, 1, keepdims=True) * (1.0 / MERGE)
    return centred * lax.rsqrt(var + eps_norm)


def first_kernel(
    feats, params,
    merge, lay0, dense, tok0, save, lse, mixed, middle, hpre, tok1, ahead, pa, pb, pc,
    *scratch,
):
    sc, prep = scratch[:-3], scratch[-3:]
    prep_kernel(FIRST_SPANS, params, merge, lay0, *prep)
    dense[VOX:, :] = jnp.zeros((ROWS - VOX, MERGE), F32)
    for line in range(PLANE):
        dense[line * WIN : (line + 1) * WIN, :] = feats[line]
    hat = merged_norm(dense[...])
    normed = hat * hidden_rows(merge, 0, 1) + hidden_rows(merge, 4, 1)
    tokens = mm(normed, merge[8 : 8 + MERGE, :])
    tok0[...] = tokens
    layer = Rows(lay0, 0)
    normed = norm(tokens, layer[0:1, :], layer[1:2, :])
    attended = attention(normed, layer, save, lse, mixed, sc)
    mid = tokens + attended
    middle[...] = mid
    tokens = mlp(mid, layer, hpre)
    tok1[...] = tokens
    ahead[...] = norm(tokens, layer[1165:1166, :], layer[1166:1167, :])
    send_parts(ahead, pa, pb, pc)


def shifted_kernel(
    sizes,
    own, pa, pb, pc, lay1, _,
    window, save, lse, mixed, out, qa, qb, qc,
    region, *sc,
):
    put_region(region, sizes)
    take_parts(own, pa, pb, pc, window)
    out[...] = attention(
        window[...], Rows(lay1, 1), save, lse, mixed, sc, region
    )
    send_parts(out, qa, qb, qc)


def to_lines(ref, out):
    for line in range(PLANE):
        out[line, 0:WIN, :] = ref[line * WIN : (line + 1) * WIN, :]
        out[line, WIN:8, :] = jnp.zeros((8 - WIN, WIDE), F32)


def from_lines(ref, out):
    out[VOX:, :] = jnp.zeros((ROWS - VOX, WIDE), F32)
    for line in range(PLANE):
        out[line * WIN : (line + 1) * WIN, :] = ref[line, 0:WIN, :]


def send_sides(lines, near_d, far_d, near_h, far_h):
    odd_d = jnp.bitwise_and(lax.axis_index("slab"), 1) == 1
    odd_h = jnp.bitwise_and(lax.axis_index("mp"), 1) == 1
    low, high = lines[0 : 2 * WIN], lines[(WIN - 2) * WIN : PLANE]
    near_d[...] = jnp.where(odd_d, low, high)
    far_d[...] = jnp.where(odd_d, high, low)
    for d in range(WIN):
        low = lines[d * WIN : d * WIN + 2]
        high = lines[d * WIN + WIN - 2 : (d + 1) * WIN]
        near_h[2 * d : 2 * d + 2] = jnp.where(odd_h, low, high)
        far_h[2 * d : 2 * d + 2] = jnp.where(odd_h, high, low)


def second_kernel(
    tok1, own, qa, qb, qc, lay1, lay2, _,
    mid1, hpre1, tok2, save, lse, mixed, mid2, hpre2, lines,
    s0, s1, s2, s3,
    attended, *sc,
):
    take_parts(own, qa, qb, qc, attended)
    mid = tok1[...] + attended[...]
    mid1[...] = mid
    tokens = mlp(mid, Rows(lay1, 1), hpre1)
    tok2[...] = tokens
    layer = Rows(lay2, 2)
    normed = norm(tokens, layer[0:1, :], layer[1:2, :])
    mid = tokens + attention(normed, layer, save, lse, mixed, sc)
    mid2[...] = mid
    attended[...] = mlp(mid, layer, hpre2)
    to_lines(attended, lines)
    send_sides(lines, s0, s1, s2, s3)


def grown_lines(sizes, own, near_d, far_d, near_h, far_h, out):
    slab, row = lax.axis_index("slab"), lax.axis_index("mp")
    odd_d = jnp.bitwise_and(slab, 1) == 1
    odd_h = jnp.bitwise_and(row, 1) == 1
    out[:, 11:12] = jnp.zeros((11, 1, 8, WIDE), F32)
    for d in range(WIN):
        out[d + 2, 2 : 2 + WIN] = own[d * WIN : (d + 1) * WIN]
    for d in range(2):
        near = near_d[d * WIN : (d + 1) * WIN]
        far = far_d[d * WIN : (d + 1) * WIN]
        out[d, 2 : 2 + WIN] = jnp.where(odd_d, near, jnp.where(slab == 0, 0.0, far))
        out[d + 9, 2 : 2 + WIN] = jnp.where(
            odd_d, jnp.where(slab == sizes[0] - 1, 0.0, far), near
        )
    for d in range(11):
        near = near_h[2 * d : 2 * d + 2]
        far = far_h[2 * d : 2 * d + 2]
        out[d, 0:2] = jnp.where(odd_h, near, jnp.where(row == 0, 0.0, far))
        out[d, 9:11] = jnp.where(odd_h, jnp.where(row == sizes[1] - 1, 0.0, far), near)


def put_marks(labels, valid, out):
    across = iota((8, WIN), 1) == iota((8, WIN), 0)
    classes = iota((8, WIDE), 1) - EMB
    for d in range(WIN):
        code = jnp.where(valid[d] == 1, labels[d], -1 - EMB - WIDE)
        code = code.astype(F32)
        for h in range(WIN):
            line = jnp.where(across, code[h : h + 1, :], 0.0)
            column = jnp.sum(line, 1, keepdims=True)
            mark = jnp.where(column == classes.astype(F32), 1.0, 0.0)
            out[d * WIN + h] = jnp.where(iota((8, WIDE), 0) < WIN, mark, 0.0)


def taps(source, first_plane, planes, first_line, lines, out):
    def per_plane(d, carry):
        for c in range(3):
            for b in range(3):
                x = source[d + first_plane, first_line + b : first_line + b + lines]
                if c != 1:
                    x = roll(x, 1 if c == 0 else 7, 1)
                x = pair(x.reshape(lines * 8, WIDE))
                at = pl.multiple_of(d * (lines * 8), lines * 8)
                t = b * 3 + c
                out[pl.ds(at, lines * 8), t * 256 : (t + 1) * 256] = x
        return carry

    lax.fori_loop(0, planes, per_plane, 0)


def tap_weights(ref, at, out):
    def per_tap(i, carry):
        w = deep(ref[pl.ds(i * EMB + at, EMB), :])
        out[pl.ds(pl.multiple_of(i * 256, 256), 256), :] = weight_nn(w)
        return carry

    lax.fori_loop(0, 27, per_tap, 0)


def tap_weights_back(ref, at, out):
    for i in range(27):
        w = deep(ref[(26 - i) * EMB + at : (27 - i) * EMB + at, :]).T
        out[i * 256 : (i + 1) * 256, :] = weight_nn(w)


def conv(side, weights, planes, pitch, at_once, put):
    rows = at_once * pitch
    for start in range(0, planes, at_once):
        total = None
        for a in range(3):
            low = (start + a) * pitch
            x = side[low : low + rows, :]
            part = dot(x, weights[a * 2304 : (a + 1) * 2304, :])
            total = part if total is None else total + part
        put(start, fold(total))


def conv_weight_grad(side, grad_rows, pitch, out, at):
    rows = 512
    g = jnp.concatenate([grad_rows, jnp.zeros((rows - grad_rows.shape[0], WIDE), F32)], 0)
    left = jnp.concatenate(split(g.T[:EMB]), 0)
    for a in range(3):
        for bc in range(9):
            y = dot(left, side[a * pitch : a * pitch + rows, bc * 256 : (bc + 1) * 256])
            y = deep(fold_rows(fold(y))).T
            t = a * 9 + bc
            out[at + t * EMB : at + (t + 1) * EMB, :] = y[:EMB]


def volume_mask(sizes, planes, lines, reach, real_lines):
    slab, row = lax.axis_index("slab"), lax.axis_index("mp")
    ends = (slab == 0, slab == sizes[0] - 1, row == 0, row == sizes[1] - 1)
    shape = (planes, lines, 8, WIDE)
    d, h, w = iota(shape, 0), iota(shape, 1), iota(shape, 2)
    low_d = jnp.where(ends[0], reach, 0)
    high_d = jnp.where(ends[1], planes - reach, planes)
    low_h = jnp.where(ends[2], reach, 0)
    high_h = jnp.where(ends[3], real_lines - reach, real_lines)
    inside = (d >= low_d) & (d < high_d) & (h >= low_h) & (h < high_h) & (w < WIN)
    return jnp.where(inside, 1.0, 0.0)


def conv_kernel(
    sizes,
    own, s0, s1, s2, s3, labels, valid, weights0, weights1, vectors, _,
    grown, pre, tok, stats, t0, t1, t2, t3,
    act, side, side_own, marks,
):
    grown_lines(sizes, own, s0, s1, s2, s3, grown)
    put_marks(labels, valid, marks)
    taps(grown, 0, 11, 0, 10, side)
    bias0 = vectors[0:1, :]
    inside = volume_mask(sizes, 9, 10, 1, 9)


    def put(start, y):
        z = (y + bias0).reshape(3, 10, 8, WIDE)
        pre[start : start + 3] = z
        act[start : start + 3] = gelu(z) * inside[start : start + 3]

    conv(side, weights0, 9, 80, 3, put)
    taps(act, 0, 9, 0, 8, side_own)
    bias1 = vectors[1:2, :]
    sums = []

    def put_own(start, y):
        y = (y + bias1).reshape(WIN, 8, 8, WIDE)[:, 0:WIN]
        y = y + own[...].reshape(WIN, WIN, 8, WIDE)
        y = jnp.where(iota(y.shape, 2) < WIN, y, 0.0).reshape(PLANE, 8, WIDE)
        tok[...] = y + marks[...]
        send_sides(tok, t0, t1, t2, t3)
        flat = y.reshape(PLANE * 8, WIDE)
        sums.append(colsum(flat))
        sums.append(colsum(flat * flat))

    conv(side_own, weights1, WIN, 64, WIN, put_own)
    count = jnp.sum(marks[...].reshape(PLANE * 8, WIDE))
    row = iota((8, WIDE), 0)
    stats[...] = (
        jnp.where(row == 0, sums[0], 0.0)
        + jnp.where(row == 1, sums[1], 0.0)
        + jnp.where(row == 2, count, 0.0)
    )


def head_kernel(
    sizes, voxels,
    own, s0, s1, s2, s3, sums, vectors, head_w,
    grown, slope_out, stats, d_head, d_rows,
):
    grown_lines(sizes, own, s0, s1, s2, s3, grown)
    rows = 11 * 12 * 8
    both = grown[...].reshape(rows, WIDE)
    lane = iota((rows, WIDE), 1)
    tokens = jnp.where(lane < EMB, both, 0.0)
    target = jnp.where(lane < CLASSES, roll(both, WIDE - EMB, 1), 0.0)
    live = jnp.sum(target, 1, keepdims=True)
    count = F32(voxels)
    average = sums[0:1, :] / count
    spread = sums[1:2, :] / count - average * average
    inv = lax.rsqrt(spread + eps_norm)
    gain = vectors[2:3, :]
    bias = vectors[3:4, :]
    hat = (tokens - average) * inv
    act, slope = gelu_both(hat * gain + bias)
    act = jnp.where(lane == EMB, 1.0, act)
    w = head_w[...]
    logits = mm(act, w)
    logits = jnp.where(lane < CLASSES, logits, -1e30)
    top = jnp.max(logits, 1, keepdims=True)
    e = jnp.exp(logits - top)
    total = jnp.sum(e, 1, keepdims=True)
    logp = logits - top - jnp.log(total)
    scale = 1.0 / sums[2:3, 0:1]
    d_logits = (e / total * live - target) * scale
    d_normed = jnp.where(lane < EMB, mm_nt(d_logits, w) * slope, 0.0)
    d_tokens = d_normed * gain * inv
    slope_out[...] = d_tokens.reshape(11, 12, 8, WIDE)

    def own_rows(x):
        x = x.reshape(11, 12, 8, WIDE)[2:9, 2:9]
        x = jnp.where(iota(x.shape, 2) < WIN, x, 0.0)
        return x.reshape(PLANE * 8, WIDE)

    loss = -jnp.sum(own_rows(target * jnp.where(lane < CLASSES, logp, 0.0)))
    own_d = own_rows(d_logits)
    own_n = own_rows(d_normed)
    own_hat = own_rows(hat)
    zeros = jnp.zeros((512 - PLANE * 8, WIDE), F32)
    left = rows_t(jnp.concatenate([own_d, zeros], 0))
    d_head[...] = mm_tn(left, jnp.concatenate([own_rows(act), zeros], 0)).T
    d_gain = colsum(own_n * own_hat)
    d_bias = colsum(own_n)
    d_average = -d_bias * gain * inv
    d_spread = d_gain * gain * inv * inv * -0.5
    d_two = d_spread / count
    d_one = (d_average - 2.0 * average * d_spread) / count
    row = iota((8, WIDE), 0)
    live_lane = iota((8, WIDE), 1) < EMB
    stats[...] = (
        jnp.where((row == 0) & live_lane, d_one, 0.0)
        + jnp.where((row == 1) & live_lane, d_two, 0.0)
        + jnp.where(row == 2, loss, 0.0)
    )
    d_rows[...] = (
        jnp.where(row == 0, d_gain, 0.0)
        + jnp.where(row == 1, d_bias, 0.0)
    )


def sides_back_kernel(sizes, grown, pre, side_act, side_grown, act):
    act[0:9] = gelu(pre[...]) * volume_mask(sizes, 9, 10, 1, 9)
    act[9:10] = jnp.zeros((1, 10, 8, WIDE), F32)
    taps(act, 0, 10, 0, 8, side_act)
    taps(grown, 1, 10, 1, 8, side_grown)


def weights_back_kernel(conv0, conv1, weights0, weights1):
    tap_weights_back(conv0, 3, weights0)
    tap_weights_back(conv1, 0, weights1)


def conv_back_kernel(
    sizes,
    tok, slope, sums, pre, side_act, side_grown, weights0, weights1, d_rows, d_head,
    d_own, keep, send, carry, seam,
    grads, dgrown, act, side, side_own, flat,
):
    lane = iota((11, 12, 8, WIDE), 3)
    inside = volume_mask(sizes, 11, 12, 2, 11)
    steady = sums[0:1, :].reshape(1, 1, 1, WIDE)
    rising = 2.0 * sums[1:2, :].reshape(1, 1, 1, WIDE)
    d_tok = slope[...] + jnp.where(lane < EMB, (steady + tok[...] * rising) * inside, 0.0)
    dgrown[...] = d_tok
    grads[5191:, :] = jnp.zeros((45, WIDE), F32)
    grads[0:8, :] = jnp.zeros((8, WIDE), F32)
    grads[5189:5191, :] = d_rows[0:2, :]
    own = dgrown[2:9, 2:10]
    line = iota(own.shape, 1)
    own = jnp.where(line < WIN, own, 0.0).reshape(WIN * 64, WIDE)
    grads[5188:5189, :] = colsum(own)

    near = volume_mask(sizes, 9, 10, 1, 9)
    conv_weight_grad(side_act, own, 64, grads, 2596)
    taps(dgrown, 0, 11, 0, 10, side)


    def put(start, y):
        _, s = gelu_both(pre[start : start + 3])
        act[start : start + 3] = y.reshape(3, 10, 8, WIDE) * s * near[start : start + 3]

    conv(side, weights1, 9, 80, 3, put)

    own = act[1:8, 1:9]
    line = iota(own.shape, 1)
    own = jnp.where(line < WIN, own, 0.0).reshape(WIN * 64, WIDE)
    grads[2595:2596, :] = colsum(own)
    conv_weight_grad(side_grown, own, 64, grads, 3)
    carry[...] = grads[0:24, :]
    flat[3 * (GROUPS - CUTS[3]) :, :] = jnp.zeros((flat.shape[0] - 3912, WIDE), F32)
    flatten(grads, 20, GROUPS - CUTS[3], flat)
    start = 3 * CUTS[3]
    head_rows(d_head[...], flat, HEAD_ROW - start)
    seam[...] = flat[0 : LATE_ROWS - start, :]
    scatter(sizes, flat, LATE_ROWS - start, keep, send)
    taps(act, 0, 9, 0, 8, side_own)

    def put_own(start, y):
        y = y.reshape(WIN, 8, 8, WIDE)[:, 0:WIN] + dgrown[2:9, 2:9]
        y = jnp.where(iota(y.shape, 2) < WIN, y, 0.0)
        d_own[...] = y.reshape(PLANE, 8, WIDE)

    conv(side_own, weights0, WIN, 64, WIN, put_own)


def back_mlp_kernel(d_own, lay2, mid2, hpre2, d_mid, grads, dense):
    from_lines(d_own, dense)
    grads[...] = jnp.zeros_like(grads)
    d_mid[...] = mlp_back(dense[...], mid2[...], hpre2, Rows(lay2, 2), grads, 2)


def back_two_kernel(
    d_mid2, grads2, carry, lay1, lay2, tok2, save, lse, mixed, mid1, hpre1,
    d_mid, grads1, flat, carry2, pa, pb, pc,
    grads, *sc,
):
    layer = Rows(lay2, 2)
    grads[0:1168, :] = grads2[...]
    d = d_mid2[...]
    tokens = tok2[...]
    normed = norm(tokens, layer[0:1, :], layer[1:2, :])
    d_normed = attention_back(d, normed, layer, save, lse, mixed, sc, grads, 2)
    d = d + pre_norm_back(d_normed, tokens, layer, grads, 2)
    grads[1167:1184, :] = carry[3:20, :]
    flatten(grads, 32, CUTS[3] - CUTS[2], flat)
    carry2[...] = grads[0:32, :]
    layer = Rows(lay1, 1)
    d = mlp_back(d, mid1[...], hpre1, layer, grads1, 1)
    d_mid[...] = d
    send_parts(d_mid, pa, pb, pc)


def back_shifted_kernel(
    sizes,
    own, pa, pb, pc, lay1, window, save, lse, mixed, grads1, carry2, _,
    d_window, flat, carry1, qa, qb, qc,
    region, grads, grad, *sc,
):
    put_region(region, sizes)
    take_parts(own, pa, pb, pc, grad)
    grads[0:1168, :] = grads1[...]
    grads[0:3, :] = jnp.zeros((3, WIDE), F32)
    d_window[...] = attention_back(
        grad[...], window[...], Rows(lay1, 1), save, lse, mixed, sc, grads, 1,
        region,
    )
    send_parts(d_window, qa, qb, qc)
    grads[1166:1196, :] = carry2[2:32, :]
    flatten(grads, 12, CUTS[2] - CUTS[1], flat)
    carry1[...] = grads[0:16, :]


def back_first_kernel(
    sizes,
    d_mid, own, qa, qb, qc, tok1, lay0, lay1, merge, dense, tok0, save, lse, mixed, middle, hpre,
    carry1, flat1, flat2, seam, _,
    keep, send,
    flat, grads, grad, *sc,
):
    take_parts(own, qa, qb, qc, grad)
    grads[1556:1572, :] = carry1[...]
    d = d_mid[...] + pre_norm_back(grad[...], tok1[...], Rows(lay1, 1), grads, 1557)
    layer = Rows(lay0, 0)
    at = MERGE_ROWS
    d = mlp_back(d, middle[...], hpre, layer, grads, at)
    tokens = tok0[...]
    normed = norm(tokens, layer[0:1, :], layer[1:2, :])
    d_normed = attention_back(d, normed, layer, save, lse, mixed, sc, grads, at)
    d = d + pre_norm_back(d_normed, tokens, layer, grads, at)
    live = iota((ROWS, WIDE), 0) < VOX
    d = jnp.where(live, d, 0.0)
    hat = merged_norm(dense[...])
    gain = hidden_rows(merge, 0, 1)
    bias = hidden_rows(merge, 4, 1)
    w = merge[8 : 8 + MERGE, :]
    put_hidden_rows(grads, 8 - 8, 1, jnp.zeros((1, MERGE), F32))
    grads[8 : 8 + MERGE, :] = mm_tn(rows_t(d), hat * gain + bias).T
    d_hat = mm_nt(d, w)
    put_hidden_rows(grads, 0, 1, colsum(d_hat * hat))
    put_hidden_rows(grads, 4, 1, colsum(d_hat))
    flatten(grads, 0, CUTS[1], flat)
    at = 0
    for cut, part in ((CUTS[1], flat1), (CUTS[2], flat2), (CUTS[3], seam)):
        at = 3 * cut
        flat[at : at + part.shape[0], :] = part[...]
    at += seam.shape[0]
    if flat.shape[0] > at:
        flat[at:, :] = jnp.zeros((flat.shape[0] - at, WIDE), F32)
    scatter(sizes, flat, 0, keep, send)


def radices(count):
    steps = [2]
    left = count // 2
    while left > 1:
        steps.append(4 if left >= 4 else 2)
        left //= steps[-1]
    return steps


def block_rows(rows, count):
    return -(-rows // (8 * count)) * 8


def own_number(sizes):
    return lax.axis_index("slab") * sizes[1] + lax.axis_index("mp")


def place_in_half(distance, count):
    place = 0
    shift = 1
    for radix in radices(count)[1:]:
        digit = jnp.bitwise_and(lax.shift_right_logical(distance, shift), radix - 1)
        place = place * radix + digit
        shift += radix.bit_length() - 1
    return place


def scatter(sizes, source, first, keep, send):
    count = sizes[0] * sizes[1]
    rows = keep.shape[0] * 2 // count
    me = own_number(sizes)
    odd = jnp.bitwise_and(me, 1)

    def per_pair(t, carry):
        for block, out in ((2 * t + odd, keep), (2 * t + 1 - odd, send)):
            place = place_in_half(jnp.bitwise_xor(block, me), count)
            at = pl.multiple_of(first + block * rows, 8)
            to = pl.multiple_of(place * rows, 8)
            out[pl.ds(to, rows), :] = source[pl.ds(at, rows), :]
        return carry

    lax.fori_loop(0, count // 2, per_pair, 0)


def traded(value, distance, count):
    pairs = [(i, i ^ distance) for i in range(count)]
    return lax.ppermute(value, ("slab", "mp"), pairs)


def later(got, after):
    return got if after is None else list(lax.optimization_barrier((*got, after)))[:-1]


def summing(keep, send, count):
    steps = radices(count)
    got = [keep, traded(send, 1, count)]
    shift = 1
    after = yield None
    for radix in steps[1:]:
        got = later(got, after)
        total = sum(got[1:], got[0])
        rows = total.shape[0] // radix
        parts = [total[k * rows : (k + 1) * rows] for k in range(radix)]
        got = parts[:1] + [traded(parts[k], k << shift, count) for k in range(1, radix)]
        shift += radix.bit_length() - 1
        after = yield parts[0]
    got = later(got, after)
    own = sum(got[1:], got[0])
    for radix in reversed(steps[1:]):
        shift -= radix.bit_length() - 1
        got = [own] + [traded(own, k << shift, count) for k in range(1, radix)]
        after = yield own
        own = jnp.concatenate(later(got, after), 0)
        yield own
    yield own, traded(own, 1, count)


def finished(chain, after=None):
    last = next(chain) if after is None else chain.send(after)
    while not isinstance(last, tuple):
        last = next(chain)
    return last


def exchanged_sum(value, count):
    shift = 0
    for radix in radices(count):
        got = [value] + [traded(value, k << shift, count) for k in range(1, radix)]
        while len(got) > 1:
            got = [got[i] + got[i + 1] for i in range(0, len(got), 2)]
        value = got[0]
        shift += radix.bit_length() - 1
    return value


PIECE = 294912


def place_blocks(sizes, own, other, out, size):
    count = sizes[0] * sizes[1]
    me = own_number(sizes)
    rows = own.shape[0] * 2 // count

    def per_block(block, carry):
        distance = jnp.bitwise_xor(block, me)
        at = pl.ds(pl.multiple_of(place_in_half(distance, count) * rows, 8), rows)
        near = jnp.bitwise_and(distance, 1) == 0
        to = pl.ds(pl.multiple_of(block * rows, 8), rows)
        out[to, :] = jnp.where(near, own[at, :], other[at, :])
        return carry

    lax.fori_loop(0, size // rows, per_block, 0)


def squares(*refs):
    total = jnp.zeros((8, WIDE), F32)
    for ref in refs:
        x = ref[...]
        total = total + jnp.sum((x * x).reshape(-1, 8, WIDE), 0)
    return total


def place_early_kernel(sizes, own, other, out, square):
    place_blocks(sizes, own, other, out, EARLY_ROWS)
    square[...] = squares(own, other)


def adamw_kernel(
    sizes,
    late, late_other, early, square, tail, sums, params, first, second,
    new_params, new_first, new_second, loss, valid, norm_out,
    grad, scale_ref,
):
    step = pl.program_id(0)

    @pl.when(step == 0)
    def gather():
        norm = jnp.sqrt(jnp.sum(squares(late, late_other) + square[...]))
        loss[0] = jnp.sum(tail[2:3, 0:1])
        valid[0] = jnp.sum(sums[2:3, 0:1])
        norm_out[0] = norm
        scale_ref[0] = jnp.minimum(1.0, clip_norm / (norm + 1e-06))
        place_blocks(sizes, late, late_other, grad, LATE_ROWS)
        grad[LATE_ROWS:, :] = early[...]

    def update(base, low, size):
        rows = -(-size // 1024) * 8
        at = pl.ds(pl.multiple_of(base // WIDE + low // WIDE, 8), rows)
        g = grad[at, :].reshape(rows * WIDE)[:size] * scale_ref[0]
        here = pl.ds(pl.multiple_of(base + low, 1024), size)
        one = beta_one * first[here] + (1.0 - beta_one) * g
        two = beta_two * second[here] + (1.0 - beta_two) * g * g
        there = pl.ds(low, size)
        new_first[there] = one
        new_second[there] = two
        two = two * (1.0 / (1.0 - beta_two**STEP))
        low_by = two * lax.rsqrt(jnp.maximum(two, 1e-37)) + adam_eps
        inverse = pl.reciprocal(low_by, approx=True)
        inverse = inverse * (2.0 - low_by * inverse)
        new_params[there] = params[here] * (1.0 - learn_rate * decay_rate) - (
            one * (learn_rate / (1.0 - beta_one**STEP))
        ) * inverse

    whole = NPARAM // PIECE

    @pl.when(step < whole)
    def full():
        def part(i, carry):
            low = pl.multiple_of(i * 16384, 16384)
            update(step * PIECE, low, 16384)
            return carry

        lax.fori_loop(0, PIECE // 16384, part, 0)

    @pl.when(step == whole)
    def last():
        rest = NPARAM - whole * PIECE
        main = rest // 1024 * 1024
        for low in range(0, main, 16384):
            update(whole * PIECE, low, min(16384, main - low))
        update(whole * PIECE, main, rest - main)


def adamw(sizes, parts, arrays):
    pieces = -(-NPARAM // PIECE)
    piece = pl.BlockSpec((PIECE,), lambda i: (i,))
    vmem = pl.BlockSpec(memory_space=pltpu.VMEM)
    smem = pl.BlockSpec(memory_space=pltpu.SMEM)
    return pl.pallas_call(
        functools.partial(adamw_kernel, sizes),
        grid=(pieces,),
        out_shape=[arr(NPARAM)] * 3 + [arr(1)] * 3,
        in_specs=[vmem] * (len(parts) + len(arrays)),
        out_specs=[piece] * 3 + [smem] * 3,
        scratch_shapes=[pltpu.VMEM((LATE_ROWS + EARLY_ROWS, WIDE), F32), pltpu.SMEM((1,), F32)],
        compiler_params=pltpu.CompilerParams(vmem_limit_bytes=16 * 1024 * 1024),
        cost_estimate=pl.CostEstimate(flops=6 * 10**9, bytes_accessed=0, transcendentals=0),
        name="adamw",
    )(*parts, *arrays)


def arr(*shape):
    return jax.ShapeDtypeStruct(shape, F32)


def call(kernel, outs, scratch, *args, name=None, us=1.0, far=(), mib=16):
    vmem = pl.BlockSpec(memory_space=pltpu.VMEM)
    smem = pl.BlockSpec(memory_space=pltpu.SMEM)
    return pl.pallas_call(
        kernel,
        out_shape=list(outs),
        in_specs=[vmem] * len(args) + [pl.BlockSpec(memory_space=pl.ANY)] * len(far),
        out_specs=[smem if o.shape == (1,) else vmem for o in outs],
        scratch_shapes=list(scratch),
        compiler_params=pltpu.CompilerParams(vmem_limit_bytes=mib * 1024 * 1024),
        cost_estimate=pl.CostEstimate(
            flops=int(us * 1.15e9), bytes_accessed=0, transcendentals=0
        ),
        name=name,
    )(*args, *far)


SQUARE = arr(ROWS, WIDE)
SAVE = arr(ROWS, 3 * WIDE)
FORWARD = [
    pltpu.VMEM((2, ROWS, 2 * WIDE), BF16),
    pltpu.VMEM((2, KEYS, 2 * WIDE), BF16),
    pltpu.VMEM((2 * KEYS, 2 * WIDE), BF16),
]
BACKWARD = [
    pltpu.VMEM((2, ROWS, 2 * WIDE), BF16),
    pltpu.VMEM((2, KEYS, 2 * WIDE), BF16),
    pltpu.VMEM((2, ROWS, 2 * WIDE), BF16),
    pltpu.VMEM((2, KEYS, 2 * WIDE), BF16),
    pltpu.VMEM((2 * KEYS, 2 * WIDE), BF16),
    pltpu.VMEM((ROWS, WIDE), F32),
    pltpu.VMEM((2, WIDE, KEYS), F32),
    pltpu.VMEM((2, KEYS, 2 * KEYS), BF16),
    pltpu.VMEM((2, KEYS, 2 * KEYS), BF16),
    pltpu.VMEM((2, WIDE, KEYS), BF16),
    pltpu.VMEM((2, WIDE, KEYS), BF16),
    pltpu.VMEM((ROWS, WIDE), F32),
    pltpu.VMEM((ROWS, 2 * KEYS), F32),
    pltpu.VMEM((ROWS, 2 * KEYS), F32),
    pltpu.VMEM((2 * KEYS, 2 * WIDE), BF16),
    pltpu.VMEM((2 * KEYS, 2 * WIDE), BF16),
]
PARTS = [arr(ROWS_A, WIDE), arr(ROWS_B, WIDE), arr(ROWS_C, WIDE)]


def passed(parts, steps, sizes):
    slabs, rows = sizes
    moved = []
    for part, (ds, dm) in zip(parts, ((1, 0), (0, 1), (1, 1))):
        pairs = []
        for s in range(slabs):
            for m in range(rows):
                target = ((s + steps * ds) % slabs) * rows + (m + steps * dm) % rows
                pairs.append((s * rows + m, target))
        moved.append(lax.ppermute(part, ("slab", "mp"), pairs))
    return moved


SIDES = [arr(2 * WIN, 8, WIDE)] * 4


def paired(axis, size):
    near = [(i, i ^ 1) for i in range(size)]
    far = [(i, (i + (1 if i % 2 else -1)) % size) for i in range(size)]
    return (
        lambda value: lax.ppermute(value, axis, near),
        lambda value: lax.ppermute(value, axis, far),
    )


def column_kernel(sizes, near_d, far_d, near_h, far_h, near_out, far_out):
    slab = lax.axis_index("slab")
    odd_d = jnp.bitwise_and(slab, 1) == 1
    odd_h = jnp.bitwise_and(lax.axis_index("mp"), 1) == 1
    at_low = slab == 0
    at_high = slab == sizes[0] - 1
    near_out[4:18] = near_h[...]
    far_out[4:18] = far_h[...]
    for d in range(2):
        near = near_d[d * WIN : (d + 1) * WIN]
        far = far_d[d * WIN : (d + 1) * WIN]
        before = jnp.where(odd_d, near, jnp.where(at_low, 0.0, far))
        after = jnp.where(odd_d, jnp.where(at_high, 0.0, far), near)
        for x, at in ((before, 2 * d), (after, 18 + 2 * d)):
            low, high = x[0:2], x[WIN - 2 : WIN]
            near_out[at : at + 2] = jnp.where(odd_h, low, high)
            far_out[at : at + 2] = jnp.where(odd_h, high, low)


def beside(sides, sizes):
    near, far = paired("slab", sizes[0])
    near_d, far_d = near(sides[0]), far(sides[1])
    near_h, far_h = call(
        functools.partial(column_kernel, sizes), [arr(22, 8, WIDE)] * 2, [],
        near_d, far_d, sides[2], sides[3],
        name="column", us=0.3,
    )
    near, far = paired("mp", sizes[1])
    return near_d, far_d, near(near_h), far(far_h)


REGION = [pltpu.VMEM((ROWS, KEYS), F32)]


def on_device(sizes, feats, labels, valid, params, moment_one, moment_two):
    slabs, rows = sizes
    count = slabs * rows

    def room(spans):
        sizes = [(span_of(groups)[1] + 8) * WIDE for groups in spans]
        return [
            [pltpu.VMEM((size,), F32) for size in sizes],
            pltpu.VMEM((2048, WIDE), F32),
            pltpu.SemaphoreType.DMA((len(spans),)),
        ]

    first_size = FIRST_SPANS[-1][1] * 384
    lay1, lay2 = call(
        functools.partial(prep_kernel, LAYER_SPANS),
        [arr(1168, WIDE)] * 2,
        room(LAYER_SPANS),
        name="prep_layers", us=2.0, far=(params,),
    )
    taps_shape = jax.ShapeDtypeStruct((27 * 256, 256), BF16)
    conv0, weights0, bias0 = call(
        prep_conv0_kernel,
        [arr(2596, WIDE), taps_shape, arr(8, WIDE)],
        room(CONV_SPANS[:1]),
        name="prep_conv0", us=1.5, far=(params,),
    )
    conv1, head_w, weights1, vectors = call(
        prep_conv1_kernel,
        [arr(2640, WIDE), arr(WIDE, WIDE), taps_shape, arr(8, WIDE)],
        room(CONV_SPANS[1:]),
        params[NPARAM // WIDE * WIDE :], bias0,
        name="prep_conv1", us=1.5, far=(params,),
    )

    merge, lay0, dense, tok0, save0, lse0, mixed0, mid0, hpre0, tok1, ahead, *parts = call(
        first_kernel,
        [arr(MERGE_ROWS, WIDE), arr(1176, WIDE)]
        + [arr(ROWS, MERGE), SQUARE, SAVE, SQUARE, SQUARE, SQUARE, arr(ROWS, HID), SQUARE, SQUARE]
        + PARTS,
        FORWARD + room(FIRST_SPANS),
        feats.reshape(PLANE, WIN, MERGE),
        name="first", us=6.5, far=(params[: FIRST_SPANS[-1][1] * 384],),
    )
    parts = passed(parts, -1, sizes)
    window, save1, lse1, mixed1, out1, *parts = call(
        functools.partial(shifted_kernel, sizes),
        [SQUARE, SAVE, SQUARE, SQUARE, SQUARE] + PARTS,
        REGION + FORWARD,
        ahead, *parts, lay1,
        name="shifted", us=4.5, far=(weights0,),
    )
    parts = passed(parts, 1, sizes)
    mid1, hpre1, tok2, save2, lse2, mixed2, mid2, hpre2, lines, *sides = call(
        second_kernel,
        [SQUARE, arr(ROWS, HID), SQUARE, SAVE, SQUARE, SQUARE, SQUARE, arr(ROWS, HID)]
        + [arr(PLANE, 8, WIDE)] + SIDES,
        [pltpu.VMEM((ROWS, WIDE), F32)] + FORWARD,
        tok1, out1, *parts, lay1, lay2,
        name="second", us=6.5, far=(weights1,),
    )
    sides = beside(sides, sizes)
    back0, back1 = call(
        weights_back_kernel,
        [taps_shape] * 2,
        [],
        conv0, conv1,
        name="weights_back", us=1.5,
    )
    grown, pre, tok3, sums, *tok_sides = call(
        functools.partial(conv_kernel, sizes),
        [arr(11, 12, 8, WIDE), arr(9, 10, 8, WIDE), arr(PLANE, 8, WIDE), arr(8, WIDE)] + SIDES,
        [
            pltpu.VMEM((9, 10, 8, WIDE), F32),
            pltpu.VMEM((880, 2304), BF16),
            pltpu.VMEM((576, 2304), BF16),
            pltpu.VMEM((PLANE, 8, WIDE), F32),
        ],
        lines, *sides, labels, valid, weights0, weights1, vectors,
        name="conv", us=8.0, mib=20, far=(back0,),
    )
    tok_sides = beside(tok_sides, sizes)
    side_act, side_grown = call(
        functools.partial(sides_back_kernel, sizes),
        [jax.ShapeDtypeStruct((640, 2304), BF16)] * 2,
        [pltpu.VMEM((10, 10, 8, WIDE), F32)],
        grown, pre,
        name="sides_back", us=2.0,
    )
    sums = exchanged_sum(sums, count)
    voxels = WIN * slabs * WIN * rows * WIN
    tok3, slope, tail, d_head, d_rows = call(
        functools.partial(head_kernel, sizes, voxels),
        [arr(11, 12, 8, WIDE), arr(11, 12, 8, WIDE), arr(8, WIDE), arr(WIDE, WIDE), arr(8, WIDE)],
        [],
        tok3, *tok_sides, sums, vectors, head_w,
        name="head", us=3.5,
    )
    tail = exchanged_sum(tail, count)
    late_rows = block_rows(LATE_ROWS, count) * count
    early_rows = block_rows(EARLY_ROWS, count) * count
    seam_rows = LATE_ROWS - 3 * CUTS[3]
    d_own, keep, send, carry3, seam = call(
        functools.partial(conv_back_kernel, sizes),
        [arr(PLANE, 8, WIDE)] + [arr(early_rows // 2, WIDE)] * 2
        + [arr(24, WIDE), arr(seam_rows, WIDE)],
        [
            pltpu.VMEM((5236, WIDE), F32),
            pltpu.VMEM((11, 12, 8, WIDE), F32),
            pltpu.VMEM((10, 10, 8, WIDE), F32),
            pltpu.VMEM((880, 2304), BF16),
            pltpu.VMEM((576, 2304), BF16),
            pltpu.VMEM((seam_rows + early_rows, WIDE), F32),
        ],
        tok3, slope, tail, pre, side_act, side_grown, back0, back1, d_rows, d_head,
        name="conv_back", us=14.0, mib=28,
    )
    early = summing(keep, send, count)
    next(early)
    d_mid2, grads2 = call(
        back_mlp_kernel,
        [SQUARE, arr(1168, WIDE)],
        [pltpu.VMEM((ROWS, WIDE), F32)],
        d_own, lay2, mid2, hpre2,
        name="back_mlp", us=3.0,
    )
    step = early.send(d_mid2)
    d_mid, grads1, flat2, carry2, *parts = call(
        back_two_kernel,
        [SQUARE, arr(1168, WIDE), arr(3 * (CUTS[3] - CUTS[2]), WIDE), arr(32, WIDE)] + PARTS,
        [pltpu.VMEM((1184, WIDE), F32)] + BACKWARD,
        d_mid2, grads2, carry3, lay1, lay2, tok2, save2, lse2, mixed2, mid1, hpre1,
        name="back_two", us=9.0,
    )
    parts = passed(parts, -1, sizes)
    step = early.send(d_mid)
    d_window, flat1, carry1, *parts = call(
        functools.partial(back_shifted_kernel, sizes),
        [SQUARE, arr(3 * (CUTS[2] - CUTS[1]), WIDE), arr(16, WIDE)] + PARTS,
        REGION + [pltpu.VMEM((1200, WIDE), F32), pltpu.VMEM((ROWS, WIDE), F32)] + BACKWARD,
        d_mid, *parts, lay1, window, save1, lse1, mixed1, grads1, carry2,
        name="back_shifted", us=10.5, far=(step,),
    )
    early.send(d_window)
    parts = passed(parts, 1, sizes)
    next(early)
    step = next(early)
    late = call(
        functools.partial(back_first_kernel, sizes),
        [arr(late_rows // 2, WIDE)] * 2,
        [
            pltpu.VMEM((late_rows, WIDE), F32),
            pltpu.VMEM((1572, WIDE), F32),
            pltpu.VMEM((ROWS, WIDE), F32),
        ]
        + BACKWARD,
        d_mid, d_window, *parts, tok1, lay0, lay1, merge, dense, tok0, save0, lse0, mixed0, mid0,
        hpre0, carry1, flat1, flat2, seam,
        name="back_first", us=13.5, far=(step,),
    )
    step = early.send(late[0])
    keep, send = later(list(late), step)
    late_sum = finished(summing(keep, send, count))
    early = finished(early)
    early = call(
        functools.partial(place_early_kernel, sizes),
        [arr(EARLY_ROWS, WIDE), arr(8, WIDE)],
        [],
        *early,
        name="place_early", us=0.6,
    )
    new_params, new_first, new_second, loss, valid_count, norm = adamw(
        sizes, (*late_sum, *early, tail, sums), (params, moment_one, moment_two)
    )
    return (
        loss.reshape(()), valid_count.reshape(()), norm.reshape(()),
        new_params, new_first, new_second,
    )


def solution(mesh):
    placed = (
        P("slab", "mp", None, None),
        P("slab", "mp", None),
        P("slab", "mp", None),
        P(),
        P(),
        P(),
    )
    sizes = (mesh.shape["slab"], mesh.shape["mp"])
    return jax.shard_map(
        functools.partial(on_device, sizes),
        mesh=mesh,
        in_specs=placed,
        out_specs=(P(), P(), P(), P(), P(), P()),
        check_vma=False,
    )
```

```python
import functools

import jax
import jax.numpy as jnp
from jax import lax
from jax.experimental import pallas as pl
from jax.experimental.pallas import tpu as pltpu
from jax.sharding import PartitionSpec as P

EMB = 96
HEADS = 6
HDIM = 16
HID = 384
MERGE = 384
CLASSES = 14
WIN = 7
SHIFT = 3
LAYERS = 3
STEP = 10

F32 = jnp.float32
BF16 = jnp.bfloat16
eps_norm = 1e-05
beta_one = 0.9
beta_two = 0.999
adam_eps = 1e-08
learn_rate = 0.05
decay_rate = 0.05
clip_norm = 0.01
LOG2E = 1.4426950408889634

VOX = WIN * WIN * WIN
ROWS = 352
KEYS = 384
BLOCKS = ((0, 128), (128, 256), (256, 352))
WIDE = 128
PLANE = WIN * WIN
FAR = WIN - SHIFT
ROWS_A = SHIFT * FAR * WIN
ROWS_B = FAR * SHIFT * WIN
ROWS_C = SHIFT * SHIFT * WIN

MERGE_ROWS = 392
LAYER_ROWS = 1165
TAP_ROWS = 27 * EMB
GROUPS = 2280
NPARAM = 872558
HEAD_ROW = 6806
HEAD_ROWS = 11
HEAD_LANE = 32
LATE_ROWS = 3072
EARLY_ROWS = 3840
LAYER_BASE = (98, 389, 680)
CONV_BASE = (971, 1620)
CUTS = (0, 392, 688, 976, 2280)

R_QKV, R_QKVB, R_PROJ, R_PROJB = 4, 292, 295, 391
R_HID, R_HIDB, R_OUT, R_OUTB = 392, 776, 780, 1164


def iota(shape, dim):
    return lax.broadcasted_iota(jnp.int32, shape, dim)


def split(x):
    hi = x.astype(BF16)
    return hi, (x - hi.astype(F32)).astype(BF16)


def pair(x):
    return jnp.concatenate(split(x), 1)


def fold(y):
    half = y.shape[1] // 2
    return y[:, :half] + y[:, half:]


def fold_rows(y):
    half = y.shape[0] // 2
    return y[:half] + y[half:]


def dot(a, b):
    return jnp.dot(a, b, preferred_element_type=F32)


def dot_nt(a, b):
    return lax.dot_general(a, b, (((1,), (1,)), ((), ())), preferred_element_type=F32)


def weight_nn(w):
    top = pair(w)
    return jnp.concatenate([top, top], 0)


def weight_nt(w):
    hi, lo = split(w)
    return jnp.concatenate(
        [jnp.concatenate([hi, hi], 1), jnp.concatenate([lo, lo], 1)], 0
    )


def mm(x, w):
    return fold(dot(pair(x), weight_nn(w)))


def mm_nt(x, w):
    return fold(dot_nt(pair(x), weight_nt(w)))


def with_rows(x, rows):
    if x.shape[0] == rows:
        return x
    return jnp.concatenate([x, jnp.zeros((rows - x.shape[0], x.shape[1]), F32)], 0)


def rows_t(x):
    return jnp.concatenate(split(with_rows(x, -(-x.shape[0] // WIDE) * WIDE).T), 0)


def mm_tn(xt, y):
    return fold_rows(fold(dot(xt, pair(with_rows(y, xt.shape[1])))))


def deep(w):
    return jnp.concatenate([w, jnp.zeros((WIDE - EMB, w.shape[1]), F32)], 0)


def roll(x, shift, axis):
    return pltpu.roll(x, shift, axis)


def four_to_three(y):
    lane = iota(y[0].shape, 1)
    a = jnp.where(lane < 96, y[0], roll(y[1], 96, 1))
    b = jnp.where(lane < 64, roll(y[1], 96, 1), roll(y[2], 64, 1))
    c = jnp.where(lane < 32, roll(y[2], 64, 1), roll(y[3], 32, 1))
    return a, b, c


def three_to_four(x):
    lane = iota(x[0].shape, 1)
    live = lane < EMB
    a = x[0]
    b = jnp.where(lane < 32, roll(x[0], 32, 1), roll(x[1], 32, 1))
    c = jnp.where(lane < 64, roll(x[1], 64, 1), roll(x[2], 64, 1))
    d = roll(x[2], 96, 1)
    return tuple(jnp.where(live, v, 0.0) for v in (a, b, c, d))


def hidden_rows(ref, start, count):
    return jnp.concatenate(
        four_to_three([ref[pl.ds(start + c, count, stride=4), :] for c in range(4)]), 1
    )


def put_hidden_rows(ref, start, count, x):
    parts = three_to_four([x[:, i * WIDE : (i + 1) * WIDE] for i in range(3)])
    for c in range(4):
        ref[pl.ds(start + c, count, stride=4), :] = parts[c]


def flatten(ref, start, groups, out):
    parts = four_to_three([ref[pl.ds(start + c, groups, stride=4), :] for c in range(4)])
    for c in range(3):
        out[pl.ds(c, groups, stride=3), :] = parts[c]


def norm_stats(x):
    live = iota(x.shape, 1) < EMB
    mean = jnp.sum(x, 1, keepdims=True) * (1.0 / EMB)
    centred = jnp.where(live, x - mean, 0.0)
    var = jnp.sum(centred * centred, 1, keepdims=True) * (1.0 / EMB)
    inv = lax.rsqrt(var + eps_norm)
    return centred * inv, inv


def norm(x, gain, bias):
    hat, _ = norm_stats(x)
    return hat * gain + bias


def norm_back(hat, inv, gain, grad):
    up = grad * gain
    one = jnp.sum(up, 1, keepdims=True) * (1.0 / EMB)
    two = jnp.sum(up * hat, 1, keepdims=True) * (1.0 / EMB)
    live = iota(hat.shape, 1) < EMB
    return jnp.where(live, inv * (up - one - hat * two), 0.0)


def colsum(x):
    return jnp.sum(x, 0, keepdims=True)


def gelu(x):
    return 0.5 * x * (1.0 + lax.erf(x * (0.5**0.5)))


def gelu_both(x):
    cdf = 0.5 * (1.0 + lax.erf(x * (0.5**0.5)))
    slope = cdf + x * (jnp.exp(x * x * -0.5) * 0.3989422804014327)
    return x * cdf, slope


def head_groups(x):
    lane = iota(x.shape, 1)
    swapped = roll(x, 64, 1)
    return jnp.where(lane < 64, x, swapped), jnp.where(lane < 64, swapped, x)


def as_left(x):
    both = []
    low = iota(x.shape, 1) < 64
    for part in head_groups(x):
        hi = part.astype(BF16).astype(F32)
        one = jnp.where(low, hi, part - hi).astype(BF16)
        both.append(jnp.concatenate([one, one], 1))
    return both


def as_right(x):
    return [pair(part) for part in head_groups(with_rows(x, KEYS))]


def head_mask(h, width):
    lane = iota((1, width), 1)
    lane = jnp.bitwise_and(lane, 63)
    low = jnp.bitwise_and(h, 3) * HDIM
    return jnp.where((lane >= low) & (lane < low + HDIM), 1.0, 0.0)


def own_lanes(h):
    lane = iota((1, WIDE), 1)
    return jnp.where((lane >= h * HDIM) & (lane < (h + 1) * HDIM), 1.0, 0.0)


def both_heads(right, heads, out):
    for k, h in enumerate(heads):
        out[k * KEYS : (k + 1) * KEYS, :] = right * head_mask(h, 2 * WIDE).astype(BF16)


def score_tiles(s, rows, region):
    tiles = [s[:, i * WIDE : (i + 1) * WIDE] for i in range(3)]
    if region is not None:
        return [t + region[rows, i * WIDE : (i + 1) * WIDE] for i, t in enumerate(tiles)]
    pad = jnp.where(iota((1, WIDE), 1) < VOX - 2 * WIDE, 0.0, -1e30)
    return tiles[:2] + [tiles[2] + pad]


def put_split(ref, rows, i, x):
    hi, lo = split(x)
    ref[rows, i * WIDE : (i + 1) * WIDE] = hi
    ref[rows, KEYS + i * WIDE : KEYS + (i + 1) * WIDE] = lo


def attention(normed, layer, save, lse, mixed, sc, region=None):
    left, right, values = sc
    x = pair(normed)
    qkv = []
    for i in range(3):
        w = deep(layer[pl.ds(R_QKV + i, EMB, stride=3), :])
        y = fold(dot(x, weight_nn(w))) + layer[R_QKVB + i : R_QKVB + i + 1, :]
        if i == 0:
            y = y * (HDIM**-0.5 * LOG2E)
        save[:, i * WIDE : (i + 1) * WIDE] = y
        qkv.append(y)
    for g, part in enumerate(as_left(qkv[0])):
        left[g] = part
    for g, part in enumerate(as_right(qkv[1])):
        right[g] = part
    v = jnp.where(iota((ROWS, WIDE), 1) == EMB, 1.0, qkv[2])
    v = pair(with_rows(v, KEYS))
    values[0:KEYS, :] = v
    values[KEYS : 2 * KEYS, :] = v
    mixed[...] = jnp.zeros_like(mixed)
    lse[...] = jnp.zeros_like(lse)

    def per_pair(pair_of, carry):
        heads = [2 * pair_of, 2 * pair_of + 1]
        masks = [head_mask(h, 2 * WIDE).astype(BF16) for h in heads]
        lanes = [own_lanes(h) for h in heads]
        spots = [jnp.where(iota((1, WIDE), 1) == h, 1.0, 0.0) for h in heads]
        g = lax.div(pair_of, 2)
        for block in BLOCKS:
            rows = slice(*block)
            out = level = 0.0
            for k in range(2):
                s = dot_nt(left[g, rows, :] * masks[k], right[g])
                tiles = score_tiles(s, rows, region)
                top = jnp.maximum(jnp.maximum(tiles[0], tiles[1]), tiles[2])
                top = jnp.max(top, 1, keepdims=True)
                parts = [split(jnp.exp2(t - top)) for t in tiles]
                e = jnp.concatenate([p[0] for p in parts] + [p[1] for p in parts], 1)
                o = fold(dot(e, values[...]))
                total = o[:, EMB : EMB + 1]
                out = out + o * (lanes[k] / total)
                level = level + (top + jnp.log(total) * LOG2E) * spots[k]
            mixed[rows, :] += out
            lse[rows, :] += level
        return carry

    lax.fori_loop(0, HEADS // 2, per_pair, 0)
    proj = deep(layer[R_PROJ : R_PROJ + EMB, :])
    return mm(mixed[...], proj) + layer[R_PROJB : R_PROJB + 1, :]


def attention_back(grad, normed, layer, save, lse, mixed, sc, grads, at, region=None):
    left, right, gleft, vright, keys, dq, dkv_t, weights, slopes = sc[:9]
    q_t, do_t, dmix, s, dp, two_keys, two_values = sc[9:]
    proj = deep(layer[R_PROJ : R_PROJ + EMB, :])
    grads[at + R_PROJ : at + R_PROJ + EMB, :] = mm_tn(rows_t(mixed[...]), grad)[:EMB]
    grads[at + R_PROJB : at + R_PROJB + 1, :] = colsum(grad)
    d_mixed = mm_nt(grad, proj)
    dmix[...] = d_mixed * mixed[...]
    q, k, v = (save[:, i * WIDE : (i + 1) * WIDE] for i in range(3))
    for g, part in enumerate(as_left(q)):
        left[g] = part
    for g, part in enumerate(as_right(k)):
        right[g] = part
    for g, part in enumerate(as_left(d_mixed)):
        gleft[g] = part
    for g, part in enumerate(as_right(v)):
        vright[g] = part
    kk = pair(with_rows(k, KEYS))
    keys[0:KEYS, :] = kk
    keys[KEYS : 2 * KEYS, :] = kk
    weights[:, ROWS:, :] = jnp.zeros((2, KEYS - ROWS, 2 * KEYS), BF16)
    slopes[:, ROWS:, :] = jnp.zeros((2, KEYS - ROWS, 2 * KEYS), BF16)
    for ref, x in ((q_t, q), (do_t, d_mixed)):
        hi, lo = split(with_rows(x, KEYS).T)
        ref[0] = hi
        ref[1] = lo
    dq[...] = jnp.zeros_like(dq)
    dkv_t[...] = jnp.zeros_like(dkv_t)

    def per_pair(pair_of, carry):
        g = lax.div(pair_of, 2)
        heads = [2 * pair_of, 2 * pair_of + 1]
        both_heads(right[g], heads, two_keys)
        both_heads(vright[g], heads, two_values)
        s[...] = dot_nt(left[g], two_keys[...])
        dp[...] = dot_nt(gleft[g], two_values[...])
        for k in range(2):
            h = 2 * pair_of + k
            lanes = own_lanes(h)
            at_h = jnp.where(iota((1, WIDE), 1) == h, 1.0, 0.0)
            for block in BLOCKS:
                rows = slice(*block)
                level = jnp.sum(lse[rows, :] * at_h, 1, keepdims=True)
                delta = jnp.sum(dmix[rows, :] * lanes, 1, keepdims=True)
                at_k = k * KEYS
                tiles = score_tiles(s[rows, at_k : at_k + KEYS], rows, region)
                for i, t in enumerate(tiles):
                    p = jnp.exp2(t - level)
                    put_split(weights.at[k], rows, i, p)
                    low = at_k + i * WIDE
                    p = p * (dp[rows, low : low + WIDE] - delta)
                    put_split(slopes.at[k], rows, i, p)
        total = 0.0
        for k in range(2):
            out = fold(dot(slopes[k, 0:ROWS, :], keys[...]))
            total = total + out * own_lanes(2 * pair_of + k)
        dq[...] += total
        for k in range(2):
            here = pl.ds(pl.multiple_of((2 * pair_of + k) * HDIM, HDIM), HDIM)
            for i, (t, m) in enumerate(((q_t, slopes), (do_t, weights))):
                lhs = jnp.concatenate([t[0, here, :], t[1, here, :]], 0)
                dkv_t[i, here, :] = fold_rows(fold(dot(lhs, m[k])))
        return carry

    lax.fori_loop(0, HEADS // 2, per_pair, 0)
    d_q = dq[...] * HDIM**-0.5
    d_k = dkv_t[0].T[0:ROWS] * (1.0 / LOG2E)
    d_v = dkv_t[1].T[0:ROWS]
    x_t = rows_t(normed)
    d_normed = None
    for i, d in enumerate((d_q, d_k, d_v)):
        grads[pl.ds(at + R_QKV + i, EMB, stride=3), :] = mm_tn(x_t, d)[:EMB]
        grads[at + R_QKVB + i : at + R_QKVB + i + 1, :] = colsum(d)
        part = mm_nt(d, deep(layer[pl.ds(R_QKV + i, EMB, stride=3), :]))
        d_normed = part if d_normed is None else d_normed + part
    return d_normed


def mlp(middle, layer, hpre):
    normed = norm(middle, layer[2:3, :], layer[3:4, :])
    w = deep(hidden_rows(layer, R_HID, EMB))
    pre = mm(normed, w) + hidden_rows(layer, R_HIDB, 1)
    hpre[...] = pre
    out = mm(gelu(pre), layer[R_OUT : R_OUT + HID, :])
    return middle + out + layer[R_OUTB : R_OUTB + 1, :]


def mlp_back(grad, middle, hpre, layer, grads, at):
    hat, inv = norm_stats(middle)
    normed = hat * layer[2:3, :] + layer[3:4, :]
    act, slope = gelu_both(hpre[...])
    grads[at + R_OUTB : at + R_OUTB + 1, :] = colsum(grad)
    grads[at + R_OUT : at + R_OUT + HID, :] = mm_tn(rows_t(grad), act).T
    d_pre = mm_nt(grad, layer[R_OUT : R_OUT + HID, :]) * slope
    put_hidden_rows(grads, at + R_HIDB, 1, colsum(d_pre))
    put_hidden_rows(grads, at + R_HID, EMB, mm_tn(rows_t(normed), d_pre)[:EMB])
    d_normed = mm_nt(d_pre, deep(hidden_rows(layer, R_HID, EMB)))
    grads[at + 2 : at + 3, :] = colsum(d_normed * hat)
    grads[at + 3 : at + 4, :] = colsum(d_normed)
    return grad + norm_back(hat, inv, layer[2:3, :], d_normed)


def pre_norm_back(grad, tokens, layer, grads, at):
    hat, inv = norm_stats(tokens)
    grads[at : at + 1, :] = colsum(grad * hat)
    grads[at + 1 : at + 2, :] = colsum(grad)
    return norm_back(hat, inv, layer[0:1, :], grad)


def region_of(rows, sizes):
    d = lax.shift_right_logical(rows * 1338, 16)
    line = lax.shift_right_logical(rows * 9363, 16)
    places = (d, line - d * WIN, rows - line * WIN)
    starts = (lax.axis_index("slab") * WIN, lax.axis_index("mp") * WIN, 0)
    total = None
    for place, start, blocks in zip(places, starts, sizes + (1,)):
        turned = jnp.where(place < SHIFT, place + FAR, place - SHIFT) + start
        length = WIN * blocks
        part = jnp.where(turned < length - WIN, 0, jnp.where(turned < length - SHIFT, 1, 2))
        total = part if total is None else total * 3 + part
    return total


def put_region(region, sizes):
    rows = region_of(iota((ROWS, WIDE), 0), sizes)[:, 0:1]
    lanes = region_of(iota((8, KEYS), 1), sizes)[0:1, :]
    apart = jnp.where(rows == lanes, 0.0, -100.0 * LOG2E)
    region[...] = jnp.where(iota((ROWS, KEYS), 1) < VOX, apart, -1e30)


def send_parts(ref, a, b, c):
    far = FAR * WIN
    near = SHIFT * WIN
    for d in range(SHIFT):
        base = d * PLANE
        c[d * near : (d + 1) * near, :] = ref[base : base + near, :]
        a[d * far : (d + 1) * far, :] = ref[base + near : base + PLANE, :]
    for d in range(FAR):
        base = (d + SHIFT) * PLANE
        b[d * near : (d + 1) * near, :] = ref[base : base + near, :]


def take_parts(own, a, b, c, out):
    far = FAR * WIN
    near = SHIFT * WIN
    for d in range(WIN):
        base = d * PLANE
        if d < SHIFT:
            out[base : base + near, :] = c[d * near : (d + 1) * near, :]
            out[base + near : base + PLANE, :] = a[d * far : (d + 1) * far, :]
        else:
            e = d - SHIFT
            out[base : base + near, :] = b[e * near : (e + 1) * near, :]
            out[base + near : base + PLANE, :] = own[base + near : base + PLANE, :]
    out[VOX:, :] = jnp.zeros((ROWS - VOX, WIDE), F32)


def span_of(groups):
    low, high = groups
    first = 3 * low // 8 * 8
    last = -(-3 * high // 8) * 8
    return first, min(last, NPARAM // WIDE // 8 * 8) - first


def copied(params, groups, flat, sem):
    first, rows = span_of(groups)
    size = rows * WIDE
    return pltpu.make_async_copy(
        params.at[pl.ds(first * WIDE, size)], flat.at[pl.ds(0, size)], sem
    )


def relay(groups, flat, out, square, last=None):
    low, high = groups
    first, rows = span_of(groups)
    square[0:rows, :] = flat[0 : rows * WIDE].reshape(rows, WIDE)
    if last is not None:
        square[rows : rows + 24, :] = jnp.zeros((24, WIDE), F32)
        square[rows : rows + 1, 0 : last.shape[0]] = last[...].reshape(1, last.shape[0])
    skip = 3 * low - first
    n = high - low
    parts = three_to_four([square[pl.ds(skip + c, n, stride=3), :] for c in range(3)])
    for c in range(4):
        out[pl.ds(c, n, stride=4), :] = parts[c]


FIRST_SPANS = ((0, 98), (98, 392))
LAYER_SPANS = ((389, 681), (680, 972))
CONV_SPANS = ((971, 1620), (1620, GROUPS))


def prep_kernel(spans, params, *refs, last=None):
    outs, (flats, square, sems) = refs[: len(spans)], refs[-3:]
    for i, groups in enumerate(spans):
        copied(params, groups, flats[i], sems.at[i]).start()
    for i, groups in enumerate(spans):
        copied(params, groups, flats[i], sems.at[i]).wait()
        relay(groups, flats[i], outs[i], square, last if i == len(spans) - 1 else None)


def head_picks():
    width = HEAD_ROWS * WIDE
    place = iota((WIDE, width), 1) - HEAD_LANE
    row = iota((WIDE, width), 0)
    here = (place >= row * CLASSES) & (place < (row + 1) * CLASSES) & (row <= EMB)
    place = iota((width, WIDE), 0) - HEAD_LANE
    col = iota((width, WIDE), 1)
    row = lax.shift_right_logical(place * 4682, 16)
    there = (place - row * CLASSES == col) & (place >= 0)
    return jnp.where(here, 1.0, 0.0), jnp.where(there, 1.0, 0.0).astype(BF16)


def prep_conv0_kernel(params, conv0, weights0, bias, *scratch):
    prep_kernel(CONV_SPANS[:1], params, conv0, *scratch)
    tap_weights(conv0, 3, weights0)
    bias[0:1, :] = conv0[3 + TAP_ROWS : 4 + TAP_ROWS, :]
    bias[1:8, :] = jnp.zeros((7, WIDE), F32)


def prep_conv1_kernel(last, bias, params, conv1, head, weights1, vectors, *scratch):
    prep_kernel(CONV_SPANS[1:], params, conv1, *scratch, last=last)
    tap_weights(conv1, 0, weights1)
    vectors[0:1, :] = bias[0:1, :]
    vectors[1:4, :] = conv1[TAP_ROWS : TAP_ROWS + 3, :]
    vectors[4:8, :] = jnp.zeros((4, WIDE), F32)
    square = scratch[1]
    first, _ = span_of(CONV_SPANS[1])
    row = jnp.concatenate(
        [square[HEAD_ROW + i - first : HEAD_ROW + i - first + 1, :] for i in range(HEAD_ROWS)], 1
    )
    here, there = head_picks()
    hi, lo = split(here * row)
    head[...] = dot(hi, there) + dot(lo, there)


def head_rows(d_head, out, at):
    here, there = head_picks()
    hi, lo = split(d_head)
    spread = (dot_nt(hi, there) + dot_nt(lo, there)) * here
    row = colsum(spread)
    for i in range(HEAD_ROWS):
        out[at + i : at + i + 1, :] += row[:, i * WIDE : (i + 1) * WIDE]


class Rows:
    def __init__(self, ref, at):
        self.ref, self.at = ref, at

    def __getitem__(self, key):
        rows, lanes = key
        if isinstance(rows, slice):
            rows = slice(rows.start + self.at, rows.stop + self.at)
        else:
            rows = pl.ds(rows.start + self.at, rows.size, stride=rows.stride)
        return self.ref[rows, lanes]


def merged_norm(x):
    mean = jnp.sum(x, 1, keepdims=True) * (1.0 / MERGE)
    centred = x - mean
    var = jnp.sum(centred * centred, 1, keepdims=True) * (1.0 / MERGE)
    return centred * lax.rsqrt(var + eps_norm)


def first_kernel(
    feats, merge, lay0,
    dense, tok0, save, lse, mixed, middle, hpre, tok1, ahead, pa, pb, pc,
    *sc,
):
    dense[VOX:, :] = jnp.zeros((ROWS - VOX, MERGE), F32)
    for line in range(PLANE):
        dense[line * WIN : (line + 1) * WIN, :] = feats[line]
    hat = merged_norm(dense[...])
    normed = hat * hidden_rows(merge, 0, 1) + hidden_rows(merge, 4, 1)
    tokens = mm(normed, merge[8 : 8 + MERGE, :])
    tok0[...] = tokens
    layer = Rows(lay0, 0)
    normed = norm(tokens, layer[0:1, :], layer[1:2, :])
    attended = attention(normed, layer, save, lse, mixed, sc)
    mid = tokens + attended
    middle[...] = mid
    tokens = mlp(mid, layer, hpre)
    tok1[...] = tokens
    ahead[...] = norm(tokens, layer[1165:1166, :], layer[1166:1167, :])
    send_parts(ahead, pa, pb, pc)


def shifted_kernel(
    sizes,
    own, pa, pb, pc, lay1, _,
    window, save, lse, mixed, out, qa, qb, qc,
    region, *sc,
):
    put_region(region, sizes)
    take_parts(own, pa, pb, pc, window)
    out[...] = attention(
        window[...], Rows(lay1, 1), save, lse, mixed, sc, region
    )
    send_parts(out, qa, qb, qc)


def to_lines(ref, out):
    for line in range(PLANE):
        out[line, 0:WIN, :] = ref[line * WIN : (line + 1) * WIN, :]
        out[line, WIN:8, :] = jnp.zeros((8 - WIN, WIDE), F32)


def from_lines(ref, out):
    out[VOX:, :] = jnp.zeros((ROWS - VOX, WIDE), F32)
    for line in range(PLANE):
        out[line * WIN : (line + 1) * WIN, :] = ref[line, 0:WIN, :]


def send_sides(lines, near_d, far_d, near_h, far_h):
    odd_d = jnp.bitwise_and(lax.axis_index("slab"), 1) == 1
    odd_h = jnp.bitwise_and(lax.axis_index("mp"), 1) == 1
    low, high = lines[0 : 2 * WIN], lines[(WIN - 2) * WIN : PLANE]
    near_d[...] = jnp.where(odd_d, low, high)
    far_d[...] = jnp.where(odd_d, high, low)
    for d in range(WIN):
        low = lines[d * WIN : d * WIN + 2]
        high = lines[d * WIN + WIN - 2 : (d + 1) * WIN]
        near_h[2 * d : 2 * d + 2] = jnp.where(odd_h, low, high)
        far_h[2 * d : 2 * d + 2] = jnp.where(odd_h, high, low)


def second_kernel(
    tok1, own, qa, qb, qc, lay1, lay2, _,
    mid1, hpre1, tok2, save, lse, mixed, mid2, hpre2, lines,
    s0, s1, s2, s3,
    attended, *sc,
):
    take_parts(own, qa, qb, qc, attended)
    mid = tok1[...] + attended[...]
    mid1[...] = mid
    tokens = mlp(mid, Rows(lay1, 1), hpre1)
    tok2[...] = tokens
    layer = Rows(lay2, 2)
    normed = norm(tokens, layer[0:1, :], layer[1:2, :])
    mid = tokens + attention(normed, layer, save, lse, mixed, sc)
    mid2[...] = mid
    attended[...] = mlp(mid, layer, hpre2)
    to_lines(attended, lines)
    send_sides(lines, s0, s1, s2, s3)


def grown_lines(sizes, own, near_d, far_d, near_h, far_h, out):
    slab, row = lax.axis_index("slab"), lax.axis_index("mp")
    odd_d = jnp.bitwise_and(slab, 1) == 1
    odd_h = jnp.bitwise_and(row, 1) == 1
    out[:, 11:12] = jnp.zeros((11, 1, 8, WIDE), F32)
    for d in range(WIN):
        out[d + 2, 2 : 2 + WIN] = own[d * WIN : (d + 1) * WIN]
    for d in range(2):
        near = near_d[d * WIN : (d + 1) * WIN]
        far = far_d[d * WIN : (d + 1) * WIN]
        out[d, 2 : 2 + WIN] = jnp.where(odd_d, near, jnp.where(slab == 0, 0.0, far))
        out[d + 9, 2 : 2 + WIN] = jnp.where(
            odd_d, jnp.where(slab == sizes[0] - 1, 0.0, far), near
        )
    for d in range(11):
        near = near_h[2 * d : 2 * d + 2]
        far = far_h[2 * d : 2 * d + 2]
        out[d, 0:2] = jnp.where(odd_h, near, jnp.where(row == 0, 0.0, far))
        out[d, 9:11] = jnp.where(odd_h, jnp.where(row == sizes[1] - 1, 0.0, far), near)


def put_marks(labels, valid, out):
    across = iota((8, WIN), 1) == iota((8, WIN), 0)
    classes = iota((8, WIDE), 1) - EMB
    for d in range(WIN):
        code = jnp.where(valid[d] == 1, labels[d], -1 - EMB - WIDE)
        code = code.astype(F32)
        for h in range(WIN):
            line = jnp.where(across, code[h : h + 1, :], 0.0)
            column = jnp.sum(line, 1, keepdims=True)
            mark = jnp.where(column == classes.astype(F32), 1.0, 0.0)
            out[d * WIN + h] = jnp.where(iota((8, WIDE), 0) < WIN, mark, 0.0)


def taps(source, first_plane, planes, first_line, lines, out):
    def per_plane(d, carry):
        for c in range(3):
            for b in range(3):
                x = source[d + first_plane, first_line + b : first_line + b + lines]
                if c != 1:
                    x = roll(x, 1 if c == 0 else 7, 1)
                x = pair(x.reshape(lines * 8, WIDE))
                at = pl.multiple_of(d * (lines * 8), lines * 8)
                t = b * 3 + c
                out[pl.ds(at, lines * 8), t * 256 : (t + 1) * 256] = x
        return carry

    lax.fori_loop(0, planes, per_plane, 0)


def tap_weights(ref, at, out):
    def per_tap(i, carry):
        w = deep(ref[pl.ds(i * EMB + at, EMB), :])
        out[pl.ds(pl.multiple_of(i * 256, 256), 256), :] = weight_nn(w)
        return carry

    lax.fori_loop(0, 27, per_tap, 0)


def tap_weights_back(ref, at, out):
    for i in range(27):
        w = deep(ref[(26 - i) * EMB + at : (27 - i) * EMB + at, :]).T
        out[i * 256 : (i + 1) * 256, :] = weight_nn(w)


def conv(side, weights, planes, pitch, at_once, put):
    rows = at_once * pitch
    for start in range(0, planes, at_once):
        total = None
        for a in range(3):
            low = (start + a) * pitch
            x = side[low : low + rows, :]
            part = dot(x, weights[a * 2304 : (a + 1) * 2304, :])
            total = part if total is None else total + part
        put(start, fold(total))


def conv_weight_grad(side, grad_rows, pitch, out, at):
    rows = 512
    g = jnp.concatenate([grad_rows, jnp.zeros((rows - grad_rows.shape[0], WIDE), F32)], 0)
    left = jnp.concatenate(split(g.T[:EMB]), 0)
    for a in range(3):
        for bc in range(9):
            y = dot(left, side[a * pitch : a * pitch + rows, bc * 256 : (bc + 1) * 256])
            y = deep(fold_rows(fold(y))).T
            t = a * 9 + bc
            out[at + t * EMB : at + (t + 1) * EMB, :] = y[:EMB]


def volume_mask(sizes, planes, lines, reach, real_lines):
    slab, row = lax.axis_index("slab"), lax.axis_index("mp")
    ends = (slab == 0, slab == sizes[0] - 1, row == 0, row == sizes[1] - 1)
    shape = (planes, lines, 8, WIDE)
    d, h, w = iota(shape, 0), iota(shape, 1), iota(shape, 2)
    low_d = jnp.where(ends[0], reach, 0)
    high_d = jnp.where(ends[1], planes - reach, planes)
    low_h = jnp.where(ends[2], reach, 0)
    high_h = jnp.where(ends[3], real_lines - reach, real_lines)
    inside = (d >= low_d) & (d < high_d) & (h >= low_h) & (h < high_h) & (w < WIN)
    return jnp.where(inside, 1.0, 0.0)


def conv_kernel(
    sizes,
    own, s0, s1, s2, s3, labels, valid, weights0, weights1, vectors, _,
    grown, pre, tok, stats, t0, t1, t2, t3,
    act, side, side_own, marks,
):
    grown_lines(sizes, own, s0, s1, s2, s3, grown)
    put_marks(labels, valid, marks)
    taps(grown, 0, 11, 0, 10, side)
    bias0 = vectors[0:1, :]
    inside = volume_mask(sizes, 9, 10, 1, 9)


    def put(start, y):
        z = (y + bias0).reshape(3, 10, 8, WIDE)
        pre[start : start + 3] = z
        act[start : start + 3] = gelu(z) * inside[start : start + 3]

    conv(side, weights0, 9, 80, 3, put)
    taps(act, 0, 9, 0, 8, side_own)
    bias1 = vectors[1:2, :]
    sums = []

    def put_own(start, y):
        y = (y + bias1).reshape(WIN, 8, 8, WIDE)[:, 0:WIN]
        y = y + own[...].reshape(WIN, WIN, 8, WIDE)
        y = jnp.where(iota(y.shape, 2) < WIN, y, 0.0).reshape(PLANE, 8, WIDE)
        tok[...] = y + marks[...]
        send_sides(tok, t0, t1, t2, t3)
        flat = y.reshape(PLANE * 8, WIDE)
        sums.append(colsum(flat))
        sums.append(colsum(flat * flat))

    conv(side_own, weights1, WIN, 64, WIN, put_own)
    count = jnp.sum(marks[...].reshape(PLANE * 8, WIDE))
    row = iota((8, WIDE), 0)
    stats[...] = (
        jnp.where(row == 0, sums[0], 0.0)
        + jnp.where(row == 1, sums[1], 0.0)
        + jnp.where(row == 2, count, 0.0)
    )


def head_kernel(
    sizes, voxels,
    own, s0, s1, s2, s3, sums, vectors, head_w,
    grown, slope_out, stats, d_head, d_rows,
):
    grown_lines(sizes, own, s0, s1, s2, s3, grown)
    rows = 11 * 12 * 8
    both = grown[...].reshape(rows, WIDE)
    lane = iota((rows, WIDE), 1)
    tokens = jnp.where(lane < EMB, both, 0.0)
    target = jnp.where(lane < CLASSES, roll(both, WIDE - EMB, 1), 0.0)
    live = jnp.sum(target, 1, keepdims=True)
    count = F32(voxels)
    average = sums[0:1, :] / count
    spread = sums[1:2, :] / count - average * average
    inv = lax.rsqrt(spread + eps_norm)
    gain = vectors[2:3, :]
    bias = vectors[3:4, :]
    hat = (tokens - average) * inv
    act, slope = gelu_both(hat * gain + bias)
    act = jnp.where(lane == EMB, 1.0, act)
    w = head_w[...]
    logits = mm(act, w)
    logits = jnp.where(lane < CLASSES, logits, -1e30)
    top = jnp.max(logits, 1, keepdims=True)
    e = jnp.exp(logits - top)
    total = jnp.sum(e, 1, keepdims=True)
    logp = logits - top - jnp.log(total)
    scale = 1.0 / sums[2:3, 0:1]
    d_logits = (e / total * live - target) * scale
    d_normed = jnp.where(lane < EMB, mm_nt(d_logits, w) * slope, 0.0)
    d_tokens = d_normed * gain * inv
    slope_out[...] = d_tokens.reshape(11, 12, 8, WIDE)

    def own_rows(x):
        x = x.reshape(11, 12, 8, WIDE)[2:9, 2:9]
        x = jnp.where(iota(x.shape, 2) < WIN, x, 0.0)
        return x.reshape(PLANE * 8, WIDE)

    loss = -jnp.sum(own_rows(target * jnp.where(lane < CLASSES, logp, 0.0)))
    own_d = own_rows(d_logits)
    own_n = own_rows(d_normed)
    own_hat = own_rows(hat)
    zeros = jnp.zeros((512 - PLANE * 8, WIDE), F32)
    left = rows_t(jnp.concatenate([own_d, zeros], 0))
    d_head[...] = mm_tn(left, jnp.concatenate([own_rows(act), zeros], 0)).T
    d_gain = colsum(own_n * own_hat)
    d_bias = colsum(own_n)
    d_average = -d_bias * gain * inv
    d_spread = d_gain * gain * inv * inv * -0.5
    d_two = d_spread / count
    d_one = (d_average - 2.0 * average * d_spread) / count
    row = iota((8, WIDE), 0)
    live_lane = iota((8, WIDE), 1) < EMB
    stats[...] = (
        jnp.where((row == 0) & live_lane, d_one, 0.0)
        + jnp.where((row == 1) & live_lane, d_two, 0.0)
        + jnp.where(row == 2, loss, 0.0)
    )
    d_rows[...] = (
        jnp.where(row == 0, d_gain, 0.0)
        + jnp.where(row == 1, d_bias, 0.0)
    )


def sides_back_kernel(sizes, grown, pre, side_act, side_grown, act):
    act[0:9] = gelu(pre[...]) * volume_mask(sizes, 9, 10, 1, 9)
    act[9:10] = jnp.zeros((1, 10, 8, WIDE), F32)
    taps(act, 0, 10, 0, 8, side_act)
    taps(grown, 1, 10, 1, 8, side_grown)


def weights_back_kernel(conv0, conv1, weights0, weights1):
    tap_weights_back(conv0, 3, weights0)
    tap_weights_back(conv1, 0, weights1)


def conv_back_kernel(
    sizes,
    tok, slope, sums, pre, side_act, side_grown, weights0, weights1, d_rows, d_head,
    d_own, keep, send, carry, seam,
    grads, dgrown, act, side, side_own, flat,
):
    lane = iota((11, 12, 8, WIDE), 3)
    inside = volume_mask(sizes, 11, 12, 2, 11)
    steady = sums[0:1, :].reshape(1, 1, 1, WIDE)
    rising = 2.0 * sums[1:2, :].reshape(1, 1, 1, WIDE)
    d_tok = slope[...] + jnp.where(lane < EMB, (steady + tok[...] * rising) * inside, 0.0)
    dgrown[...] = d_tok
    grads[5191:, :] = jnp.zeros((45, WIDE), F32)
    grads[0:8, :] = jnp.zeros((8, WIDE), F32)
    grads[5189:5191, :] = d_rows[0:2, :]
    own = dgrown[2:9, 2:10]
    line = iota(own.shape, 1)
    own = jnp.where(line < WIN, own, 0.0).reshape(WIN * 64, WIDE)
    grads[5188:5189, :] = colsum(own)

    near = volume_mask(sizes, 9, 10, 1, 9)
    conv_weight_grad(side_act, own, 64, grads, 2596)
    taps(dgrown, 0, 11, 0, 10, side)


    def put(start, y):
        _, s = gelu_both(pre[start : start + 3])
        act[start : start + 3] = y.reshape(3, 10, 8, WIDE) * s * near[start : start + 3]

    conv(side, weights1, 9, 80, 3, put)

    own = act[1:8, 1:9]
    line = iota(own.shape, 1)
    own = jnp.where(line < WIN, own, 0.0).reshape(WIN * 64, WIDE)
    grads[2595:2596, :] = colsum(own)
    conv_weight_grad(side_grown, own, 64, grads, 3)
    carry[...] = grads[0:24, :]
    flat[3 * (GROUPS - CUTS[3]) :, :] = jnp.zeros((flat.shape[0] - 3912, WIDE), F32)
    flatten(grads, 20, GROUPS - CUTS[3], flat)
    start = 3 * CUTS[3]
    head_rows(d_head[...], flat, HEAD_ROW - start)
    seam[...] = flat[0 : LATE_ROWS - start, :]
    scatter(sizes, flat, LATE_ROWS - start, keep, send)
    taps(act, 0, 9, 0, 8, side_own)

    def put_own(start, y):
        y = y.reshape(WIN, 8, 8, WIDE)[:, 0:WIN] + dgrown[2:9, 2:9]
        y = jnp.where(iota(y.shape, 2) < WIN, y, 0.0)
        d_own[...] = y.reshape(PLANE, 8, WIDE)

    conv(side_own, weights0, WIN, 64, WIN, put_own)


def back_mlp_kernel(d_own, lay2, mid2, hpre2, d_mid, grads, dense):
    from_lines(d_own, dense)
    grads[...] = jnp.zeros_like(grads)
    d_mid[...] = mlp_back(dense[...], mid2[...], hpre2, Rows(lay2, 2), grads, 2)


def back_two_kernel(
    d_mid2, grads2, carry, lay1, lay2, tok2, save, lse, mixed, mid1, hpre1,
    d_mid, grads1, flat, carry2, pa, pb, pc,
    grads, *sc,
):
    layer = Rows(lay2, 2)
    grads[0:1168, :] = grads2[...]
    d = d_mid2[...]
    tokens = tok2[...]
    normed = norm(tokens, layer[0:1, :], layer[1:2, :])
    d_normed = attention_back(d, normed, layer, save, lse, mixed, sc, grads, 2)
    d = d + pre_norm_back(d_normed, tokens, layer, grads, 2)
    grads[1167:1184, :] = carry[3:20, :]
    flatten(grads, 32, CUTS[3] - CUTS[2], flat)
    carry2[...] = grads[0:32, :]
    layer = Rows(lay1, 1)
    d = mlp_back(d, mid1[...], hpre1, layer, grads1, 1)
    d_mid[...] = d
    send_parts(d_mid, pa, pb, pc)


def back_shifted_kernel(
    sizes,
    own, pa, pb, pc, lay1, window, save, lse, mixed, grads1, carry2, _,
    d_window, flat, carry1, qa, qb, qc,
    region, grads, grad, *sc,
):
    put_region(region, sizes)
    take_parts(own, pa, pb, pc, grad)
    grads[0:1168, :] = grads1[...]
    grads[0:3, :] = jnp.zeros((3, WIDE), F32)
    d_window[...] = attention_back(
        grad[...], window[...], Rows(lay1, 1), save, lse, mixed, sc, grads, 1,
        region,
    )
    send_parts(d_window, qa, qb, qc)
    grads[1166:1196, :] = carry2[2:32, :]
    flatten(grads, 12, CUTS[2] - CUTS[1], flat)
    carry1[...] = grads[0:16, :]


def back_first_kernel(
    sizes,
    d_mid, own, qa, qb, qc, tok1, lay0, lay1, merge, dense, tok0, save, lse, mixed, middle, hpre,
    carry1, flat1, flat2, seam, _,
    keep, send,
    flat, grads, grad, *sc,
):
    take_parts(own, qa, qb, qc, grad)
    grads[1556:1572, :] = carry1[...]
    d = d_mid[...] + pre_norm_back(grad[...], tok1[...], Rows(lay1, 1), grads, 1557)
    layer = Rows(lay0, 0)
    at = MERGE_ROWS
    d = mlp_back(d, middle[...], hpre, layer, grads, at)
    tokens = tok0[...]
    normed = norm(tokens, layer[0:1, :], layer[1:2, :])
    d_normed = attention_back(d, normed, layer, save, lse, mixed, sc, grads, at)
    d = d + pre_norm_back(d_normed, tokens, layer, grads, at)
    live = iota((ROWS, WIDE), 0) < VOX
    d = jnp.where(live, d, 0.0)
    hat = merged_norm(dense[...])
    gain = hidden_rows(merge, 0, 1)
    bias = hidden_rows(merge, 4, 1)
    w = merge[8 : 8 + MERGE, :]
    put_hidden_rows(grads, 8 - 8, 1, jnp.zeros((1, MERGE), F32))
    grads[8 : 8 + MERGE, :] = mm_tn(rows_t(d), hat * gain + bias).T
    d_hat = mm_nt(d, w)
    put_hidden_rows(grads, 0, 1, colsum(d_hat * hat))
    put_hidden_rows(grads, 4, 1, colsum(d_hat))
    flatten(grads, 0, CUTS[1], flat)
    at = 0
    for cut, part in ((CUTS[1], flat1), (CUTS[2], flat2), (CUTS[3], seam)):
        at = 3 * cut
        flat[at : at + part.shape[0], :] = part[...]
    at += seam.shape[0]
    if flat.shape[0] > at:
        flat[at:, :] = jnp.zeros((flat.shape[0] - at, WIDE), F32)
    scatter(sizes, flat, 0, keep, send)


def radices(count):
    steps = [2]
    left = count // 2
    while left > 1:
        steps.append(4 if left >= 4 else 2)
        left //= steps[-1]
    return steps


def block_rows(rows, count):
    return -(-rows // (8 * count)) * 8


def own_number(sizes):
    return lax.axis_index("slab") * sizes[1] + lax.axis_index("mp")


def place_in_half(distance, count):
    place = 0
    shift = 1
    for radix in radices(count)[1:]:
        digit = jnp.bitwise_and(lax.shift_right_logical(distance, shift), radix - 1)
        place = place * radix + digit
        shift += radix.bit_length() - 1
    return place


def scatter(sizes, source, first, keep, send):
    count = sizes[0] * sizes[1]
    rows = keep.shape[0] * 2 // count
    me = own_number(sizes)
    odd = jnp.bitwise_and(me, 1)

    def per_pair(t, carry):
        for block, out in ((2 * t + odd, keep), (2 * t + 1 - odd, send)):
            place = place_in_half(jnp.bitwise_xor(block, me), count)
            at = pl.multiple_of(first + block * rows, 8)
            to = pl.multiple_of(place * rows, 8)
            out[pl.ds(to, rows), :] = source[pl.ds(at, rows), :]
        return carry

    lax.fori_loop(0, count // 2, per_pair, 0)


def traded(value, distance, count):
    pairs = [(i, i ^ distance) for i in range(count)]
    return lax.ppermute(value, ("slab", "mp"), pairs)


def later(got, after):
    return got if after is None else list(lax.optimization_barrier((*got, after)))[:-1]


def summing(keep, send, count):
    steps = radices(count)
    got = [keep, traded(send, 1, count)]
    shift = 1
    after = yield None
    for radix in steps[1:]:
        got = later(got, after)
        total = sum(got[1:], got[0])
        rows = total.shape[0] // radix
        parts = [total[k * rows : (k + 1) * rows] for k in range(radix)]
        got = parts[:1] + [traded(parts[k], k << shift, count) for k in range(1, radix)]
        shift += radix.bit_length() - 1
        after = yield parts[0]
    got = later(got, after)
    own = sum(got[1:], got[0])
    for radix in reversed(steps[1:]):
        shift -= radix.bit_length() - 1
        got = [own] + [traded(own, k << shift, count) for k in range(1, radix)]
        after = yield own
        own = jnp.concatenate(later(got, after), 0)
        yield own
    yield own, traded(own, 1, count)


def finished(chain, after=None):
    last = next(chain) if after is None else chain.send(after)
    while not isinstance(last, tuple):
        last = next(chain)
    return last


def exchanged_sum(value, count):
    shift = 0
    for radix in radices(count):
        got = [value] + [traded(value, k << shift, count) for k in range(1, radix)]
        while len(got) > 1:
            got = [got[i] + got[i + 1] for i in range(0, len(got), 2)]
        value = got[0]
        shift += radix.bit_length() - 1
    return value


PIECE = 294912


def place_blocks(sizes, own, other, out, size):
    count = sizes[0] * sizes[1]
    me = own_number(sizes)
    rows = own.shape[0] * 2 // count

    def per_block(block, carry):
        distance = jnp.bitwise_xor(block, me)
        at = pl.ds(pl.multiple_of(place_in_half(distance, count) * rows, 8), rows)
        near = jnp.bitwise_and(distance, 1) == 0
        to = pl.ds(pl.multiple_of(block * rows, 8), rows)
        out[to, :] = jnp.where(near, own[at, :], other[at, :])
        return carry

    lax.fori_loop(0, size // rows, per_block, 0)


def squares(*refs):
    total = jnp.zeros((8, WIDE), F32)
    for ref in refs:
        x = ref[...]
        total = total + jnp.sum((x * x).reshape(-1, 8, WIDE), 0)
    return total


def place_early_kernel(sizes, own, other, out, square):
    place_blocks(sizes, own, other, out, EARLY_ROWS)
    square[...] = squares(own, other)


def adamw_kernel(
    sizes,
    late, late_other, early, square, tail, sums, params, first, second,
    new_params, new_first, new_second, loss, valid, norm_out,
    grad, scale_ref,
):
    step = pl.program_id(0)

    @pl.when(step == 0)
    def gather():
        norm = jnp.sqrt(jnp.sum(squares(late, late_other) + square[...]))
        loss[0] = jnp.sum(tail[2:3, 0:1])
        valid[0] = jnp.sum(sums[2:3, 0:1])
        norm_out[0] = norm
        scale_ref[0] = jnp.minimum(1.0, clip_norm / (norm + 1e-06))
        place_blocks(sizes, late, late_other, grad, LATE_ROWS)
        grad[LATE_ROWS:, :] = early[...]

    def update(base, low, size):
        rows = -(-size // 1024) * 8
        at = pl.ds(pl.multiple_of(base // WIDE + low // WIDE, 8), rows)
        g = grad[at, :].reshape(rows * WIDE)[:size] * scale_ref[0]
        here = pl.ds(pl.multiple_of(base + low, 1024), size)
        one = beta_one * first[here] + (1.0 - beta_one) * g
        two = beta_two * second[here] + (1.0 - beta_two) * g * g
        there = pl.ds(low, size)
        new_first[there] = one
        new_second[there] = two
        two = two * (1.0 / (1.0 - beta_two**STEP))
        low_by = two * lax.rsqrt(jnp.maximum(two, 1e-37)) + adam_eps
        inverse = pl.reciprocal(low_by, approx=True)
        inverse = inverse * (2.0 - low_by * inverse)
        new_params[there] = params[here] * (1.0 - learn_rate * decay_rate) - (
            one * (learn_rate / (1.0 - beta_one**STEP))
        ) * inverse

    whole = NPARAM // PIECE

    @pl.when(step < whole)
    def full():
        def part(i, carry):
            low = pl.multiple_of(i * 16384, 16384)
            update(step * PIECE, low, 16384)
            return carry

        lax.fori_loop(0, PIECE // 16384, part, 0)

    @pl.when(step == whole)
    def last():
        rest = NPARAM - whole * PIECE
        main = rest // 1024 * 1024
        for low in range(0, main, 16384):
            update(whole * PIECE, low, min(16384, main - low))
        update(whole * PIECE, main, rest - main)


def adamw(sizes, parts, arrays):
    pieces = -(-NPARAM // PIECE)
    piece = pl.BlockSpec((PIECE,), lambda i: (i,))
    vmem = pl.BlockSpec(memory_space=pltpu.VMEM)
    smem = pl.BlockSpec(memory_space=pltpu.SMEM)
    return pl.pallas_call(
        functools.partial(adamw_kernel, sizes),
        grid=(pieces,),
        out_shape=[arr(NPARAM)] * 3 + [arr(1)] * 3,
        in_specs=[vmem] * (len(parts) + len(arrays)),
        out_specs=[piece] * 3 + [smem] * 3,
        scratch_shapes=[pltpu.VMEM((LATE_ROWS + EARLY_ROWS, WIDE), F32), pltpu.SMEM((1,), F32)],
        compiler_params=pltpu.CompilerParams(vmem_limit_bytes=16 * 1024 * 1024),
        cost_estimate=pl.CostEstimate(flops=6 * 10**9, bytes_accessed=0, transcendentals=0),
        name="adamw",
    )(*parts, *arrays)


def arr(*shape):
    return jax.ShapeDtypeStruct(shape, F32)


def call(kernel, outs, scratch, *args, name=None, us=1.0, far=(), mib=16):
    vmem = pl.BlockSpec(memory_space=pltpu.VMEM)
    smem = pl.BlockSpec(memory_space=pltpu.SMEM)
    return pl.pallas_call(
        kernel,
        out_shape=list(outs),
        in_specs=[vmem] * len(args) + [pl.BlockSpec(memory_space=pl.ANY)] * len(far),
        out_specs=[smem if o.shape == (1,) else vmem for o in outs],
        scratch_shapes=list(scratch),
        compiler_params=pltpu.CompilerParams(vmem_limit_bytes=mib * 1024 * 1024),
        cost_estimate=pl.CostEstimate(
            flops=int(us * 1.15e9), bytes_accessed=0, transcendentals=0
        ),
        name=name,
    )(*args, *far)


SQUARE = arr(ROWS, WIDE)
SAVE = arr(ROWS, 3 * WIDE)
FORWARD = [
    pltpu.VMEM((2, ROWS, 2 * WIDE), BF16),
    pltpu.VMEM((2, KEYS, 2 * WIDE), BF16),
    pltpu.VMEM((2 * KEYS, 2 * WIDE), BF16),
]
BACKWARD = [
    pltpu.VMEM((2, ROWS, 2 * WIDE), BF16),
    pltpu.VMEM((2, KEYS, 2 * WIDE), BF16),
    pltpu.VMEM((2, ROWS, 2 * WIDE), BF16),
    pltpu.VMEM((2, KEYS, 2 * WIDE), BF16),
    pltpu.VMEM((2 * KEYS, 2 * WIDE), BF16),
    pltpu.VMEM((ROWS, WIDE), F32),
    pltpu.VMEM((2, WIDE, KEYS), F32),
    pltpu.VMEM((2, KEYS, 2 * KEYS), BF16),
    pltpu.VMEM((2, KEYS, 2 * KEYS), BF16),
    pltpu.VMEM((2, WIDE, KEYS), BF16),
    pltpu.VMEM((2, WIDE, KEYS), BF16),
    pltpu.VMEM((ROWS, WIDE), F32),
    pltpu.VMEM((ROWS, 2 * KEYS), F32),
    pltpu.VMEM((ROWS, 2 * KEYS), F32),
    pltpu.VMEM((2 * KEYS, 2 * WIDE), BF16),
    pltpu.VMEM((2 * KEYS, 2 * WIDE), BF16),
]
PARTS = [arr(ROWS_A, WIDE), arr(ROWS_B, WIDE), arr(ROWS_C, WIDE)]


def passed(parts, steps, sizes):
    slabs, rows = sizes
    moved = []
    for part, (ds, dm) in zip(parts, ((1, 0), (0, 1), (1, 1))):
        pairs = []
        for s in range(slabs):
            for m in range(rows):
                target = ((s + steps * ds) % slabs) * rows + (m + steps * dm) % rows
                pairs.append((s * rows + m, target))
        moved.append(lax.ppermute(part, ("slab", "mp"), pairs))
    return moved


SIDES = [arr(2 * WIN, 8, WIDE)] * 4


def paired(axis, size):
    near = [(i, i ^ 1) for i in range(size)]
    far = [(i, (i + (1 if i % 2 else -1)) % size) for i in range(size)]
    return (
        lambda value: lax.ppermute(value, axis, near),
        lambda value: lax.ppermute(value, axis, far),
    )


def column_kernel(sizes, near_d, far_d, near_h, far_h, near_out, far_out):
    slab = lax.axis_index("slab")
    odd_d = jnp.bitwise_and(slab, 1) == 1
    odd_h = jnp.bitwise_and(lax.axis_index("mp"), 1) == 1
    at_low = slab == 0
    at_high = slab == sizes[0] - 1
    near_out[4:18] = near_h[...]
    far_out[4:18] = far_h[...]
    for d in range(2):
        near = near_d[d * WIN : (d + 1) * WIN]
        far = far_d[d * WIN : (d + 1) * WIN]
        before = jnp.where(odd_d, near, jnp.where(at_low, 0.0, far))
        after = jnp.where(odd_d, jnp.where(at_high, 0.0, far), near)
        for x, at in ((before, 2 * d), (after, 18 + 2 * d)):
            low, high = x[0:2], x[WIN - 2 : WIN]
            near_out[at : at + 2] = jnp.where(odd_h, low, high)
            far_out[at : at + 2] = jnp.where(odd_h, high, low)


def beside(sides, sizes):
    near, far = paired("slab", sizes[0])
    near_d, far_d = near(sides[0]), far(sides[1])
    near_h, far_h = call(
        functools.partial(column_kernel, sizes), [arr(22, 8, WIDE)] * 2, [],
        near_d, far_d, sides[2], sides[3],
        name="column", us=0.3,
    )
    near, far = paired("mp", sizes[1])
    return near_d, far_d, near(near_h), far(far_h)


REGION = [pltpu.VMEM((ROWS, KEYS), F32)]


def on_device(sizes, feats, labels, valid, params, moment_one, moment_two):
    slabs, rows = sizes
    count = slabs * rows

    def room(spans):
        sizes = [(span_of(groups)[1] + 8) * WIDE for groups in spans]
        return [
            [pltpu.VMEM((size,), F32) for size in sizes],
            pltpu.VMEM((2048, WIDE), F32),
            pltpu.SemaphoreType.DMA((len(spans),)),
        ]

    first_size = FIRST_SPANS[-1][1] * 384
    merge, lay0 = call(
        functools.partial(prep_kernel, FIRST_SPANS),
        [arr(MERGE_ROWS, WIDE), arr(1176, WIDE)],
        room(FIRST_SPANS),
        name="prep_first", us=2.0, far=(params[:first_size],),
    )
    lay1, lay2 = call(
        functools.partial(prep_kernel, LAYER_SPANS),
        [arr(1168, WIDE)] * 2,
        room(LAYER_SPANS),
        name="prep_layers", us=2.0, far=(params,),
    )
    taps_shape = jax.ShapeDtypeStruct((27 * 256, 256), BF16)
    conv0, weights0, bias0 = call(
        prep_conv0_kernel,
        [arr(2596, WIDE), taps_shape, arr(8, WIDE)],
        room(CONV_SPANS[:1]),
        name="prep_conv0", us=1.5, far=(params,),
    )
    conv1, head_w, weights1, vectors = call(
        prep_conv1_kernel,
        [arr(2640, WIDE), arr(WIDE, WIDE), taps_shape, arr(8, WIDE)],
        room(CONV_SPANS[1:]),
        params[NPARAM // WIDE * WIDE :], bias0,
        name="prep_conv1", us=1.5, far=(params,),
    )

    dense, tok0, save0, lse0, mixed0, mid0, hpre0, tok1, ahead, *parts = call(
        first_kernel,
        [arr(ROWS, MERGE), SQUARE, SAVE, SQUARE, SQUARE, SQUARE, arr(ROWS, HID), SQUARE, SQUARE]
        + PARTS,
        FORWARD,
        feats.reshape(PLANE, WIN, MERGE), merge, lay0,
        name="first", us=6.0,
    )
    parts = passed(parts, -1, sizes)
    window, save1, lse1, mixed1, out1, *parts = call(
        functools.partial(shifted_kernel, sizes),
        [SQUARE, SAVE, SQUARE, SQUARE, SQUARE] + PARTS,
        REGION + FORWARD,
        ahead, *parts, lay1,
        name="shifted", us=4.5, far=(weights0,),
    )
    parts = passed(parts, 1, sizes)
    mid1, hpre1, tok2, save2, lse2, mixed2, mid2, hpre2, lines, *sides = call(
        second_kernel,
        [SQUARE, arr(ROWS, HID), SQUARE, SAVE, SQUARE, SQUARE, SQUARE, arr(ROWS, HID)]
        + [arr(PLANE, 8, WIDE)] + SIDES,
        [pltpu.VMEM((ROWS, WIDE), F32)] + FORWARD,
        tok1, out1, *parts, lay1, lay2,
        name="second", us=6.5, far=(weights1,),
    )
    sides = beside(sides, sizes)
    back0, back1 = call(
        weights_back_kernel,
        [taps_shape] * 2,
        [],
        conv0, conv1,
        name="weights_back", us=1.5,
    )
    grown, pre, tok3, sums, *tok_sides = call(
        functools.partial(conv_kernel, sizes),
        [arr(11, 12, 8, WIDE), arr(9, 10, 8, WIDE), arr(PLANE, 8, WIDE), arr(8, WIDE)] + SIDES,
        [
            pltpu.VMEM((9, 10, 8, WIDE), F32),
            pltpu.VMEM((880, 2304), BF16),
            pltpu.VMEM((576, 2304), BF16),
            pltpu.VMEM((PLANE, 8, WIDE), F32),
        ],
        lines, *sides, labels, valid, weights0, weights1, vectors,
        name="conv", us=8.0, mib=20, far=(back0,),
    )
    tok_sides = beside(tok_sides, sizes)
    side_act, side_grown = call(
        functools.partial(sides_back_kernel, sizes),
        [jax.ShapeDtypeStruct((640, 2304), BF16)] * 2,
        [pltpu.VMEM((10, 10, 8, WIDE), F32)],
        grown, pre,
        name="sides_back", us=2.0,
    )
    sums = exchanged_sum(sums, count)
    voxels = WIN * slabs * WIN * rows * WIN
    tok3, slope, tail, d_head, d_rows = call(
        functools.partial(head_kernel, sizes, voxels),
        [arr(11, 12, 8, WIDE), arr(11, 12, 8, WIDE), arr(8, WIDE), arr(WIDE, WIDE), arr(8, WIDE)],
        [],
        tok3, *tok_sides, sums, vectors, head_w,
        name="head", us=3.5,
    )
    tail = exchanged_sum(tail, count)
    late_rows = block_rows(LATE_ROWS, count) * count
    early_rows = block_rows(EARLY_ROWS, count) * count
    seam_rows = LATE_ROWS - 3 * CUTS[3]
    d_own, keep, send, carry3, seam = call(
        functools.partial(conv_back_kernel, sizes),
        [arr(PLANE, 8, WIDE)] + [arr(early_rows // 2, WIDE)] * 2
        + [arr(24, WIDE), arr(seam_rows, WIDE)],
        [
            pltpu.VMEM((5236, WIDE), F32),
            pltpu.VMEM((11, 12, 8, WIDE), F32),
            pltpu.VMEM((10, 10, 8, WIDE), F32),
            pltpu.VMEM((880, 2304), BF16),
            pltpu.VMEM((576, 2304), BF16),
            pltpu.VMEM((seam_rows + early_rows, WIDE), F32),
        ],
        tok3, slope, tail, pre, side_act, side_grown, back0, back1, d_rows, d_head,
        name="conv_back", us=14.0, mib=28,
    )
    early = summing(keep, send, count)
    next(early)
    d_mid2, grads2 = call(
        back_mlp_kernel,
        [SQUARE, arr(1168, WIDE)],
        [pltpu.VMEM((ROWS, WIDE), F32)],
        d_own, lay2, mid2, hpre2,
        name="back_mlp", us=3.0,
    )
    step = early.send(d_mid2)
    d_mid, grads1, flat2, carry2, *parts = call(
        back_two_kernel,
        [SQUARE, arr(1168, WIDE), arr(3 * (CUTS[3] - CUTS[2]), WIDE), arr(32, WIDE)] + PARTS,
        [pltpu.VMEM((1184, WIDE), F32)] + BACKWARD,
        d_mid2, grads2, carry3, lay1, lay2, tok2, save2, lse2, mixed2, mid1, hpre1,
        name="back_two", us=9.0,
    )
    parts = passed(parts, -1, sizes)
    step = early.send(d_mid)
    d_window, flat1, carry1, *parts = call(
        functools.partial(back_shifted_kernel, sizes),
        [SQUARE, arr(3 * (CUTS[2] - CUTS[1]), WIDE), arr(16, WIDE)] + PARTS,
        REGION + [pltpu.VMEM((1200, WIDE), F32), pltpu.VMEM((ROWS, WIDE), F32)] + BACKWARD,
        d_mid, *parts, lay1, window, save1, lse1, mixed1, grads1, carry2,
        name="back_shifted", us=10.5, far=(step,),
    )
    early.send(d_window)
    parts = passed(parts, 1, sizes)
    next(early)
    step = next(early)
    late = call(
        functools.partial(back_first_kernel, sizes),
        [arr(late_rows // 2, WIDE)] * 2,
        [
            pltpu.VMEM((late_rows, WIDE), F32),
            pltpu.VMEM((1572, WIDE), F32),
            pltpu.VMEM((ROWS, WIDE), F32),
        ]
        + BACKWARD,
        d_mid, d_window, *parts, tok1, lay0, lay1, merge, dense, tok0, save0, lse0, mixed0, mid0,
        hpre0, carry1, flat1, flat2, seam,
        name="back_first", us=13.5, far=(step,),
    )
    step = early.send(late[0])
    keep, send = later(list(late), step)
    late_sum = finished(summing(keep, send, count))
    early = finished(early)
    early = call(
        functools.partial(place_early_kernel, sizes),
        [arr(EARLY_ROWS, WIDE), arr(8, WIDE)],
        [],
        *early,
        name="place_early", us=0.6,
    )
    new_params, new_first, new_second, loss, valid_count, norm = adamw(
        sizes, (*late_sum, *early, tail, sums), (params, moment_one, moment_two)
    )
    return (
        loss.reshape(()), valid_count.reshape(()), norm.reshape(()),
        new_params, new_first, new_second,
    )


def solution(mesh):
    placed = (
        P("slab", "mp", None, None),
        P("slab", "mp", None),
        P("slab", "mp", None),
        P(),
        P(),
        P(),
    )
    sizes = (mesh.shape["slab"], mesh.shape["mp"])
    return jax.shard_map(
        functools.partial(on_device, sizes),
        mesh=mesh,
        in_specs=placed,
        out_specs=(P(), P(), P(), P(), P(), P()),
        check_vma=False,
    )
```

```python
import functools

import jax
import jax.numpy as jnp
from jax import lax
from jax.experimental import pallas as pl
from jax.experimental.pallas import tpu as pltpu
from jax.sharding import PartitionSpec as P

EMB = 96
HEADS = 6
HDIM = 16
HID = 384
MERGE = 384
CLASSES = 14
WIN = 7
SHIFT = 3
LAYERS = 3
STEP = 10

F32 = jnp.float32
BF16 = jnp.bfloat16
eps_norm = 1e-05
beta_one = 0.9
beta_two = 0.999
adam_eps = 1e-08
learn_rate = 0.05
decay_rate = 0.05
clip_norm = 0.01
LOG2E = 1.4426950408889634

VOX = WIN * WIN * WIN
ROWS = 352
KEYS = 384
BLOCKS = ((0, 128), (128, 256), (256, 352))
WIDE = 128
PLANE = WIN * WIN
FAR = WIN - SHIFT
ROWS_A = SHIFT * FAR * WIN
ROWS_B = FAR * SHIFT * WIN
ROWS_C = SHIFT * SHIFT * WIN

MERGE_ROWS = 392
LAYER_ROWS = 1165
TAP_ROWS = 27 * EMB
GROUPS = 2280
NPARAM = 872558
HEAD_ROW = 6806
HEAD_ROWS = 11
HEAD_LANE = 32
LATE_ROWS = 3072
EARLY_ROWS = 3840
LAYER_BASE = (98, 389, 680)
CONV_BASE = (971, 1620)
CUTS = (0, 392, 688, 976, 2280)

R_QKV, R_QKVB, R_PROJ, R_PROJB = 4, 292, 295, 391
R_HID, R_HIDB, R_OUT, R_OUTB = 392, 776, 780, 1164


def iota(shape, dim):
    return lax.broadcasted_iota(jnp.int32, shape, dim)


def split(x):
    hi = x.astype(BF16)
    return hi, (x - hi.astype(F32)).astype(BF16)


def pair(x):
    return jnp.concatenate(split(x), 1)


def fold(y):
    half = y.shape[1] // 2
    return y[:, :half] + y[:, half:]


def fold_rows(y):
    half = y.shape[0] // 2
    return y[:half] + y[half:]


def dot(a, b):
    return jnp.dot(a, b, preferred_element_type=F32)


def dot_nt(a, b):
    return lax.dot_general(a, b, (((1,), (1,)), ((), ())), preferred_element_type=F32)


def weight_nn(w):
    top = pair(w)
    return jnp.concatenate([top, top], 0)


def weight_nt(w):
    hi, lo = split(w)
    return jnp.concatenate(
        [jnp.concatenate([hi, hi], 1), jnp.concatenate([lo, lo], 1)], 0
    )


def mm(x, w):
    return fold(dot(pair(x), weight_nn(w)))


def mm_nt(x, w):
    return fold(dot_nt(pair(x), weight_nt(w)))


def with_rows(x, rows):
    if x.shape[0] == rows:
        return x
    return jnp.concatenate([x, jnp.zeros((rows - x.shape[0], x.shape[1]), F32)], 0)


def rows_t(x):
    return jnp.concatenate(split(with_rows(x, -(-x.shape[0] // WIDE) * WIDE).T), 0)


def mm_tn(xt, y):
    return fold_rows(fold(dot(xt, pair(with_rows(y, xt.shape[1])))))


def deep(w):
    return jnp.concatenate([w, jnp.zeros((WIDE - EMB, w.shape[1]), F32)], 0)


def roll(x, shift, axis):
    return pltpu.roll(x, shift, axis)


def four_to_three(y):
    lane = iota(y[0].shape, 1)
    a = jnp.where(lane < 96, y[0], roll(y[1], 96, 1))
    b = jnp.where(lane < 64, roll(y[1], 96, 1), roll(y[2], 64, 1))
    c = jnp.where(lane < 32, roll(y[2], 64, 1), roll(y[3], 32, 1))
    return a, b, c


def three_to_four(x):
    lane = iota(x[0].shape, 1)
    live = lane < EMB
    a = x[0]
    b = jnp.where(lane < 32, roll(x[0], 32, 1), roll(x[1], 32, 1))
    c = jnp.where(lane < 64, roll(x[1], 64, 1), roll(x[2], 64, 1))
    d = roll(x[2], 96, 1)
    return tuple(jnp.where(live, v, 0.0) for v in (a, b, c, d))


def hidden_rows(ref, start, count):
    return jnp.concatenate(
        four_to_three([ref[pl.ds(start + c, count, stride=4), :] for c in range(4)]), 1
    )


def put_hidden_rows(ref, start, count, x):
    parts = three_to_four([x[:, i * WIDE : (i + 1) * WIDE] for i in range(3)])
    for c in range(4):
        ref[pl.ds(start + c, count, stride=4), :] = parts[c]


def flatten(ref, start, groups, out):
    parts = four_to_three([ref[pl.ds(start + c, groups, stride=4), :] for c in range(4)])
    for c in range(3):
        out[pl.ds(c, groups, stride=3), :] = parts[c]


def norm_stats(x):
    live = iota(x.shape, 1) < EMB
    mean = jnp.sum(x, 1, keepdims=True) * (1.0 / EMB)
    centred = jnp.where(live, x - mean, 0.0)
    var = jnp.sum(centred * centred, 1, keepdims=True) * (1.0 / EMB)
    inv = lax.rsqrt(var + eps_norm)
    return centred * inv, inv


def norm(x, gain, bias):
    hat, _ = norm_stats(x)
    return hat * gain + bias


def norm_back(hat, inv, gain, grad):
    up = grad * gain
    one = jnp.sum(up, 1, keepdims=True) * (1.0 / EMB)
    two = jnp.sum(up * hat, 1, keepdims=True) * (1.0 / EMB)
    live = iota(hat.shape, 1) < EMB
    return jnp.where(live, inv * (up - one - hat * two), 0.0)


def colsum(x):
    return jnp.sum(x, 0, keepdims=True)


def gelu(x):
    return 0.5 * x * (1.0 + lax.erf(x * (0.5**0.5)))


def gelu_both(x):
    cdf = 0.5 * (1.0 + lax.erf(x * (0.5**0.5)))
    slope = cdf + x * (jnp.exp(x * x * -0.5) * 0.3989422804014327)
    return x * cdf, slope


def head_groups(x):
    lane = iota(x.shape, 1)
    swapped = roll(x, 64, 1)
    return jnp.where(lane < 64, x, swapped), jnp.where(lane < 64, swapped, x)


def as_left(x):
    both = []
    low = iota(x.shape, 1) < 64
    for part in head_groups(x):
        hi = part.astype(BF16).astype(F32)
        one = jnp.where(low, hi, part - hi).astype(BF16)
        both.append(jnp.concatenate([one, one], 1))
    return both


def as_right(x):
    return [pair(part) for part in head_groups(with_rows(x, KEYS))]


def head_mask(h, width):
    lane = iota((1, width), 1)
    lane = jnp.bitwise_and(lane, 63)
    low = jnp.bitwise_and(h, 3) * HDIM
    return jnp.where((lane >= low) & (lane < low + HDIM), 1.0, 0.0)


def own_lanes(h):
    lane = iota((1, WIDE), 1)
    return jnp.where((lane >= h * HDIM) & (lane < (h + 1) * HDIM), 1.0, 0.0)


def both_heads(right, heads, out):
    for k, h in enumerate(heads):
        out[k * KEYS : (k + 1) * KEYS, :] = right * head_mask(h, 2 * WIDE).astype(BF16)


def score_tiles(s, rows, region):
    tiles = [s[:, i * WIDE : (i + 1) * WIDE] for i in range(3)]
    if region is not None:
        return [t + region[rows, i * WIDE : (i + 1) * WIDE] for i, t in enumerate(tiles)]
    pad = jnp.where(iota((1, WIDE), 1) < VOX - 2 * WIDE, 0.0, -1e30)
    return tiles[:2] + [tiles[2] + pad]


def put_split(ref, rows, i, x):
    hi, lo = split(x)
    ref[rows, i * WIDE : (i + 1) * WIDE] = hi
    ref[rows, KEYS + i * WIDE : KEYS + (i + 1) * WIDE] = lo


def attention(normed, layer, save, lse, mixed, sc, region=None):
    left, right, values = sc
    x = pair(normed)
    qkv = []
    for i in range(3):
        w = deep(layer[pl.ds(R_QKV + i, EMB, stride=3), :])
        y = fold(dot(x, weight_nn(w))) + layer[R_QKVB + i : R_QKVB + i + 1, :]
        if i == 0:
            y = y * (HDIM**-0.5 * LOG2E)
        save[:, i * WIDE : (i + 1) * WIDE] = y
        qkv.append(y)
    for g, part in enumerate(as_left(qkv[0])):
        left[g] = part
    for g, part in enumerate(as_right(qkv[1])):
        right[g] = part
    v = jnp.where(iota((ROWS, WIDE), 1) == EMB, 1.0, qkv[2])
    v = pair(with_rows(v, KEYS))
    values[0:KEYS, :] = v
    values[KEYS : 2 * KEYS, :] = v
    mixed[...] = jnp.zeros_like(mixed)
    lse[...] = jnp.zeros_like(lse)

    def per_pair(pair_of, carry):
        heads = [2 * pair_of, 2 * pair_of + 1]
        masks = [head_mask(h, 2 * WIDE).astype(BF16) for h in heads]
        lanes = [own_lanes(h) for h in heads]
        spots = [jnp.where(iota((1, WIDE), 1) == h, 1.0, 0.0) for h in heads]
        g = lax.div(pair_of, 2)
        for block in BLOCKS:
            rows = slice(*block)
            out = level = 0.0
            for k in range(2):
                s = dot_nt(left[g, rows, :] * masks[k], right[g])
                tiles = score_tiles(s, rows, region)
                top = jnp.maximum(jnp.maximum(tiles[0], tiles[1]), tiles[2])
                top = jnp.max(top, 1, keepdims=True)
                parts = [split(jnp.exp2(t - top)) for t in tiles]
                e = jnp.concatenate([p[0] for p in parts] + [p[1] for p in parts], 1)
                o = fold(dot(e, values[...]))
                total = o[:, EMB : EMB + 1]
                out = out + o * (lanes[k] / total)
                level = level + (top + jnp.log(total) * LOG2E) * spots[k]
            mixed[rows, :] += out
            lse[rows, :] += level
        return carry

    lax.fori_loop(0, HEADS // 2, per_pair, 0)
    proj = deep(layer[R_PROJ : R_PROJ + EMB, :])
    return mm(mixed[...], proj) + layer[R_PROJB : R_PROJB + 1, :]


def attention_back(grad, normed, layer, save, lse, mixed, sc, grads, at, region=None):
    left, right, gleft, vright, keys, dq, dkv_t, weights, slopes = sc[:9]
    q_t, do_t, dmix, s, dp, two_keys, two_values = sc[9:]
    proj = deep(layer[R_PROJ : R_PROJ + EMB, :])
    grads[at + R_PROJ : at + R_PROJ + EMB, :] = mm_tn(rows_t(mixed[...]), grad)[:EMB]
    grads[at + R_PROJB : at + R_PROJB + 1, :] = colsum(grad)
    d_mixed = mm_nt(grad, proj)
    dmix[...] = d_mixed * mixed[...]
    q, k, v = (save[:, i * WIDE : (i + 1) * WIDE] for i in range(3))
    for g, part in enumerate(as_left(q)):
        left[g] = part
    for g, part in enumerate(as_right(k)):
        right[g] = part
    for g, part in enumerate(as_left(d_mixed)):
        gleft[g] = part
    for g, part in enumerate(as_right(v)):
        vright[g] = part
    kk = pair(with_rows(k, KEYS))
    keys[0:KEYS, :] = kk
    keys[KEYS : 2 * KEYS, :] = kk
    weights[:, ROWS:, :] = jnp.zeros((2, KEYS - ROWS, 2 * KEYS), BF16)
    slopes[:, ROWS:, :] = jnp.zeros((2, KEYS - ROWS, 2 * KEYS), BF16)
    for ref, x in ((q_t, q), (do_t, d_mixed)):
        hi, lo = split(with_rows(x, KEYS).T)
        ref[0] = hi
        ref[1] = lo
    dq[...] = jnp.zeros_like(dq)
    dkv_t[...] = jnp.zeros_like(dkv_t)

    def per_pair(pair_of, carry):
        g = lax.div(pair_of, 2)
        heads = [2 * pair_of, 2 * pair_of + 1]
        both_heads(right[g], heads, two_keys)
        both_heads(vright[g], heads, two_values)
        s[...] = dot_nt(left[g], two_keys[...])
        dp[...] = dot_nt(gleft[g], two_values[...])
        for k in range(2):
            h = 2 * pair_of + k
            lanes = own_lanes(h)
            at_h = jnp.where(iota((1, WIDE), 1) == h, 1.0, 0.0)
            for block in BLOCKS:
                rows = slice(*block)
                level = jnp.sum(lse[rows, :] * at_h, 1, keepdims=True)
                delta = jnp.sum(dmix[rows, :] * lanes, 1, keepdims=True)
                at_k = k * KEYS
                tiles = score_tiles(s[rows, at_k : at_k + KEYS], rows, region)
                for i, t in enumerate(tiles):
                    p = jnp.exp2(t - level)
                    put_split(weights.at[k], rows, i, p)
                    low = at_k + i * WIDE
                    p = p * (dp[rows, low : low + WIDE] - delta)
                    put_split(slopes.at[k], rows, i, p)
        total = 0.0
        for k in range(2):
            out = fold(dot(slopes[k, 0:ROWS, :], keys[...]))
            total = total + out * own_lanes(2 * pair_of + k)
        dq[...] += total
        for k in range(2):
            here = pl.ds(pl.multiple_of((2 * pair_of + k) * HDIM, HDIM), HDIM)
            for i, (t, m) in enumerate(((q_t, slopes), (do_t, weights))):
                lhs = jnp.concatenate([t[0, here, :], t[1, here, :]], 0)
                dkv_t[i, here, :] = fold_rows(fold(dot(lhs, m[k])))
        return carry

    lax.fori_loop(0, HEADS // 2, per_pair, 0)
    d_q = dq[...] * HDIM**-0.5
    d_k = dkv_t[0].T[0:ROWS] * (1.0 / LOG2E)
    d_v = dkv_t[1].T[0:ROWS]
    x_t = rows_t(normed)
    d_normed = None
    for i, d in enumerate((d_q, d_k, d_v)):
        grads[pl.ds(at + R_QKV + i, EMB, stride=3), :] = mm_tn(x_t, d)[:EMB]
        grads[at + R_QKVB + i : at + R_QKVB + i + 1, :] = colsum(d)
        part = mm_nt(d, deep(layer[pl.ds(R_QKV + i, EMB, stride=3), :]))
        d_normed = part if d_normed is None else d_normed + part
    return d_normed


def mlp(middle, layer, hpre):
    normed = norm(middle, layer[2:3, :], layer[3:4, :])
    w = deep(hidden_rows(layer, R_HID, EMB))
    pre = mm(normed, w) + hidden_rows(layer, R_HIDB, 1)
    hpre[...] = pre
    out = mm(gelu(pre), layer[R_OUT : R_OUT + HID, :])
    return middle + out + layer[R_OUTB : R_OUTB + 1, :]


def mlp_back(grad, middle, hpre, layer, grads, at):
    hat, inv = norm_stats(middle)
    normed = hat * layer[2:3, :] + layer[3:4, :]
    act, slope = gelu_both(hpre[...])
    grads[at + R_OUTB : at + R_OUTB + 1, :] = colsum(grad)
    grads[at + R_OUT : at + R_OUT + HID, :] = mm_tn(rows_t(grad), act).T
    d_pre = mm_nt(grad, layer[R_OUT : R_OUT + HID, :]) * slope
    put_hidden_rows(grads, at + R_HIDB, 1, colsum(d_pre))
    put_hidden_rows(grads, at + R_HID, EMB, mm_tn(rows_t(normed), d_pre)[:EMB])
    d_normed = mm_nt(d_pre, deep(hidden_rows(layer, R_HID, EMB)))
    grads[at + 2 : at + 3, :] = colsum(d_normed * hat)
    grads[at + 3 : at + 4, :] = colsum(d_normed)
    return grad + norm_back(hat, inv, layer[2:3, :], d_normed)


def pre_norm_back(grad, tokens, layer, grads, at):
    hat, inv = norm_stats(tokens)
    grads[at : at + 1, :] = colsum(grad * hat)
    grads[at + 1 : at + 2, :] = colsum(grad)
    return norm_back(hat, inv, layer[0:1, :], grad)


def region_of(rows, sizes):
    d = lax.shift_right_logical(rows * 1338, 16)
    line = lax.shift_right_logical(rows * 9363, 16)
    places = (d, line - d * WIN, rows - line * WIN)
    starts = (lax.axis_index("slab") * WIN, lax.axis_index("mp") * WIN, 0)
    total = None
    for place, start, blocks in zip(places, starts, sizes + (1,)):
        turned = jnp.where(place < SHIFT, place + FAR, place - SHIFT) + start
        length = WIN * blocks
        part = jnp.where(turned < length - WIN, 0, jnp.where(turned < length - SHIFT, 1, 2))
        total = part if total is None else total * 3 + part
    return total


def put_region(region, sizes):
    rows = region_of(iota((ROWS, WIDE), 0), sizes)[:, 0:1]
    lanes = region_of(iota((8, KEYS), 1), sizes)[0:1, :]
    apart = jnp.where(rows == lanes, 0.0, -100.0 * LOG2E)
    region[...] = jnp.where(iota((ROWS, KEYS), 1) < VOX, apart, -1e30)


def send_parts(ref, a, b, c):
    far = FAR * WIN
    near = SHIFT * WIN
    for d in range(SHIFT):
        base = d * PLANE
        c[d * near : (d + 1) * near, :] = ref[base : base + near, :]
        a[d * far : (d + 1) * far, :] = ref[base + near : base + PLANE, :]
    for d in range(FAR):
        base = (d + SHIFT) * PLANE
        b[d * near : (d + 1) * near, :] = ref[base : base + near, :]


def take_parts(own, a, b, c, out):
    far = FAR * WIN
    near = SHIFT * WIN
    for d in range(WIN):
        base = d * PLANE
        if d < SHIFT:
            out[base : base + near, :] = c[d * near : (d + 1) * near, :]
            out[base + near : base + PLANE, :] = a[d * far : (d + 1) * far, :]
        else:
            e = d - SHIFT
            out[base : base + near, :] = b[e * near : (e + 1) * near, :]
            out[base + near : base + PLANE, :] = own[base + near : base + PLANE, :]
    out[VOX:, :] = jnp.zeros((ROWS - VOX, WIDE), F32)


def span_of(groups):
    low, high = groups
    first = 3 * low // 8 * 8
    last = -(-3 * high // 8) * 8
    return first, min(last, NPARAM // WIDE // 8 * 8) - first


def copied(params, groups, flat, sem):
    first, rows = span_of(groups)
    size = rows * WIDE
    return pltpu.make_async_copy(
        params.at[pl.ds(first * WIDE, size)], flat.at[pl.ds(0, size)], sem
    )


def relay(groups, flat, out, square, last=None):
    low, high = groups
    first, rows = span_of(groups)
    square[0:rows, :] = flat[0 : rows * WIDE].reshape(rows, WIDE)
    if last is not None:
        square[rows : rows + 24, :] = jnp.zeros((24, WIDE), F32)
        square[rows : rows + 1, 0 : last.shape[0]] = last[...].reshape(1, last.shape[0])
    skip = 3 * low - first
    n = high - low
    parts = three_to_four([square[pl.ds(skip + c, n, stride=3), :] for c in range(3)])
    for c in range(4):
        out[pl.ds(c, n, stride=4), :] = parts[c]


FIRST_SPANS = ((0, 98), (98, 392))
LAYER_SPANS = ((389, 681), (680, 972))
CONV_SPANS = ((971, 1620), (1620, GROUPS))


def prep_kernel(spans, params, *refs, last=None):
    outs, (flats, square, sems) = refs[: len(spans)], refs[-3:]
    for i, groups in enumerate(spans):
        copied(params, groups, flats[i], sems.at[i]).start()
    for i, groups in enumerate(spans):
        copied(params, groups, flats[i], sems.at[i]).wait()
        relay(groups, flats[i], outs[i], square, last if i == len(spans) - 1 else None)


def head_picks():
    width = HEAD_ROWS * WIDE
    place = iota((WIDE, width), 1) - HEAD_LANE
    row = iota((WIDE, width), 0)
    here = (place >= row * CLASSES) & (place < (row + 1) * CLASSES) & (row <= EMB)
    place = iota((width, WIDE), 0) - HEAD_LANE
    col = iota((width, WIDE), 1)
    row = lax.shift_right_logical(place * 4682, 16)
    there = (place - row * CLASSES == col) & (place >= 0)
    return jnp.where(here, 1.0, 0.0), jnp.where(there, 1.0, 0.0).astype(BF16)


def prep_conv0_kernel(params, conv0, weights0, bias, *scratch):
    prep_kernel(CONV_SPANS[:1], params, conv0, *scratch)
    tap_weights(conv0, 3, weights0)
    bias[0:1, :] = conv0[3 + TAP_ROWS : 4 + TAP_ROWS, :]
    bias[1:8, :] = jnp.zeros((7, WIDE), F32)


def prep_conv1_kernel(last, bias, params, conv1, head, weights1, vectors, *scratch):
    prep_kernel(CONV_SPANS[1:], params, conv1, *scratch, last=last)
    tap_weights(conv1, 0, weights1)
    vectors[0:1, :] = bias[0:1, :]
    vectors[1:4, :] = conv1[TAP_ROWS : TAP_ROWS + 3, :]
    vectors[4:8, :] = jnp.zeros((4, WIDE), F32)
    square = scratch[1]
    first, _ = span_of(CONV_SPANS[1])
    row = jnp.concatenate(
        [square[HEAD_ROW + i - first : HEAD_ROW + i - first + 1, :] for i in range(HEAD_ROWS)], 1
    )
    here, there = head_picks()
    hi, lo = split(here * row)
    head[...] = dot(hi, there) + dot(lo, there)


def head_rows(d_head, out, at):
    here, there = head_picks()
    hi, lo = split(d_head)
    spread = (dot_nt(hi, there) + dot_nt(lo, there)) * here
    row = colsum(spread)
    for i in range(HEAD_ROWS):
        out[at + i : at + i + 1, :] += row[:, i * WIDE : (i + 1) * WIDE]


class Rows:
    def __init__(self, ref, at):
        self.ref, self.at = ref, at

    def __getitem__(self, key):
        rows, lanes = key
        if isinstance(rows, slice):
            rows = slice(rows.start + self.at, rows.stop + self.at)
        else:
            rows = pl.ds(rows.start + self.at, rows.size, stride=rows.stride)
        return self.ref[rows, lanes]


def merged_norm(x):
    mean = jnp.sum(x, 1, keepdims=True) * (1.0 / MERGE)
    centred = x - mean
    var = jnp.sum(centred * centred, 1, keepdims=True) * (1.0 / MERGE)
    return centred * lax.rsqrt(var + eps_norm)


def first_kernel(
    feats, merge, lay0,
    dense, tok0, save, lse, mixed, middle, hpre, tok1, ahead, pa, pb, pc,
    *sc,
):
    dense[VOX:, :] = jnp.zeros((ROWS - VOX, MERGE), F32)
    for line in range(PLANE):
        dense[line * WIN : (line + 1) * WIN, :] = feats[line]
    hat = merged_norm(dense[...])
    normed = hat * hidden_rows(merge, 0, 1) + hidden_rows(merge, 4, 1)
    tokens = mm(normed, merge[8 : 8 + MERGE, :])
    tok0[...] = tokens
    layer = Rows(lay0, 0)
    normed = norm(tokens, layer[0:1, :], layer[1:2, :])
    attended = attention(normed, layer, save, lse, mixed, sc)
    mid = tokens + attended
    middle[...] = mid
    tokens = mlp(mid, layer, hpre)
    tok1[...] = tokens
    ahead[...] = norm(tokens, layer[1165:1166, :], layer[1166:1167, :])
    send_parts(ahead, pa, pb, pc)


def shifted_kernel(
    sizes,
    own, pa, pb, pc, lay1, _,
    window, save, lse, mixed, out, qa, qb, qc,
    region, *sc,
):
    put_region(region, sizes)
    take_parts(own, pa, pb, pc, window)
    out[...] = attention(
        window[...], Rows(lay1, 1), save, lse, mixed, sc, region
    )
    send_parts(out, qa, qb, qc)


def to_lines(ref, out):
    for line in range(PLANE):
        out[line, 0:WIN, :] = ref[line * WIN : (line + 1) * WIN, :]
        out[line, WIN:8, :] = jnp.zeros((8 - WIN, WIDE), F32)


def from_lines(ref, out):
    out[VOX:, :] = jnp.zeros((ROWS - VOX, WIDE), F32)
    for line in range(PLANE):
        out[line * WIN : (line + 1) * WIN, :] = ref[line, 0:WIN, :]


def send_sides(lines, near_d, far_d, near_h, far_h):
    odd_d = jnp.bitwise_and(lax.axis_index("slab"), 1) == 1
    odd_h = jnp.bitwise_and(lax.axis_index("mp"), 1) == 1
    low, high = lines[0 : 2 * WIN], lines[(WIN - 2) * WIN : PLANE]
    near_d[...] = jnp.where(odd_d, low, high)
    far_d[...] = jnp.where(odd_d, high, low)
    for d in range(WIN):
        low = lines[d * WIN : d * WIN + 2]
        high = lines[d * WIN + WIN - 2 : (d + 1) * WIN]
        near_h[2 * d : 2 * d + 2] = jnp.where(odd_h, low, high)
        far_h[2 * d : 2 * d + 2] = jnp.where(odd_h, high, low)


def second_kernel(
    tok1, own, qa, qb, qc, lay1, lay2, _,
    mid1, hpre1, tok2, save, lse, mixed, mid2, hpre2, lines,
    s0, s1, s2, s3,
    attended, *sc,
):
    take_parts(own, qa, qb, qc, attended)
    mid = tok1[...] + attended[...]
    mid1[...] = mid
    tokens = mlp(mid, Rows(lay1, 1), hpre1)
    tok2[...] = tokens
    layer = Rows(lay2, 2)
    normed = norm(tokens, layer[0:1, :], layer[1:2, :])
    mid = tokens + attention(normed, layer, save, lse, mixed, sc)
    mid2[...] = mid
    attended[...] = mlp(mid, layer, hpre2)
    to_lines(attended, lines)
    send_sides(lines, s0, s1, s2, s3)


def grown_lines(sizes, own, near_d, far_d, near_h, far_h, out):
    slab, row = lax.axis_index("slab"), lax.axis_index("mp")
    odd_d = jnp.bitwise_and(slab, 1) == 1
    odd_h = jnp.bitwise_and(row, 1) == 1
    out[:, 11:12] = jnp.zeros((11, 1, 8, WIDE), F32)
    for d in range(WIN):
        out[d + 2, 2 : 2 + WIN] = own[d * WIN : (d + 1) * WIN]
    for d in range(2):
        near = near_d[d * WIN : (d + 1) * WIN]
        far = far_d[d * WIN : (d + 1) * WIN]
        out[d, 2 : 2 + WIN] = jnp.where(odd_d, near, jnp.where(slab == 0, 0.0, far))
        out[d + 9, 2 : 2 + WIN] = jnp.where(
            odd_d, jnp.where(slab == sizes[0] - 1, 0.0, far), near
        )
    for d in range(11):
        near = near_h[2 * d : 2 * d + 2]
        far = far_h[2 * d : 2 * d + 2]
        out[d, 0:2] = jnp.where(odd_h, near, jnp.where(row == 0, 0.0, far))
        out[d, 9:11] = jnp.where(odd_h, jnp.where(row == sizes[1] - 1, 0.0, far), near)


def put_marks(labels, valid, out):
    across = iota((8, WIN), 1) == iota((8, WIN), 0)
    classes = iota((8, WIDE), 1) - EMB
    for d in range(WIN):
        code = jnp.where(valid[d] == 1, labels[d], -1 - EMB - WIDE)
        code = code.astype(F32)
        for h in range(WIN):
            line = jnp.where(across, code[h : h + 1, :], 0.0)
            column = jnp.sum(line, 1, keepdims=True)
            mark = jnp.where(column == classes.astype(F32), 1.0, 0.0)
            out[d * WIN + h] = jnp.where(iota((8, WIDE), 0) < WIN, mark, 0.0)


def taps(source, first_plane, planes, first_line, lines, out):
    def per_plane(d, carry):
        for c in range(3):
            for b in range(3):
                x = source[d + first_plane, first_line + b : first_line + b + lines]
                if c != 1:
                    x = roll(x, 1 if c == 0 else 7, 1)
                x = pair(x.reshape(lines * 8, WIDE))
                at = pl.multiple_of(d * (lines * 8), lines * 8)
                t = b * 3 + c
                out[pl.ds(at, lines * 8), t * 256 : (t + 1) * 256] = x
        return carry

    lax.fori_loop(0, planes, per_plane, 0)


def tap_weights(ref, at, out):
    def per_tap(i, carry):
        w = deep(ref[pl.ds(i * EMB + at, EMB), :])
        out[pl.ds(pl.multiple_of(i * 256, 256), 256), :] = weight_nn(w)
        return carry

    lax.fori_loop(0, 27, per_tap, 0)


def tap_weights_back(ref, at, out):
    for i in range(27):
        w = deep(ref[(26 - i) * EMB + at : (27 - i) * EMB + at, :]).T
        out[i * 256 : (i + 1) * 256, :] = weight_nn(w)


def conv(side, weights, cuts, pitch, out):
    for start, end in zip(cuts, cuts[1:]):
        total = None
        for a in range(3):
            x = side[(start + a) * pitch : (end + a) * pitch, :]
            part = dot(x, weights[a * 2304 : (a + 1) * 2304, :])
            total = part if total is None else total + part
        out[start * pitch : end * pitch, :] = fold(total)


def conv_weight_grad(side, grad_rows, pitch, out, at):
    rows = 512
    g = jnp.concatenate([grad_rows, jnp.zeros((rows - grad_rows.shape[0], WIDE), F32)], 0)
    left = jnp.concatenate(split(g.T[:EMB]), 0)
    for a in range(3):
        for bc in range(9):
            y = dot(left, side[a * pitch : a * pitch + rows, bc * 256 : (bc + 1) * 256])
            y = deep(fold_rows(fold(y))).T
            t = a * 9 + bc
            out[at + t * EMB : at + (t + 1) * EMB, :] = y[:EMB]


def volume_mask(sizes, planes, lines, reach, real_lines):
    slab, row = lax.axis_index("slab"), lax.axis_index("mp")
    ends = (slab == 0, slab == sizes[0] - 1, row == 0, row == sizes[1] - 1)
    shape = (planes, lines, 8, WIDE)
    d, h, w = iota(shape, 0), iota(shape, 1), iota(shape, 2)
    low_d = jnp.where(ends[0], reach, 0)
    high_d = jnp.where(ends[1], planes - reach, planes)
    low_h = jnp.where(ends[2], reach, 0)
    high_h = jnp.where(ends[3], real_lines - reach, real_lines)
    inside = (d >= low_d) & (d < high_d) & (h >= low_h) & (h < high_h) & (w < WIN)
    return jnp.where(inside, 1.0, 0.0)


def conv_kernel(
    sizes,
    own, s0, s1, s2, s3, labels, valid, weights0, weights1, vectors, _,
    grown, pre, tok, stats, t0, t1, t2, t3,
    act, side, side_own, marks, result,
):
    grown_lines(sizes, own, s0, s1, s2, s3, grown)
    put_marks(labels, valid, marks)
    taps(grown, 0, 11, 0, 10, side)
    bias0 = vectors[0:1, :]
    inside = volume_mask(sizes, 9, 10, 1, 9)

    conv(side, weights0, (0, 3, 6, 9), 80, result)
    z = (result[...] + bias0).reshape(9, 10, 8, WIDE)
    pre[...] = z
    act[...] = gelu(z) * inside
    taps(act, 0, 9, 0, 8, side_own)
    bias1 = vectors[1:2, :]
    conv(side_own, weights1, (0, 4, WIN), 64, result)
    y = (result[0 : WIN * 64, :] + bias1).reshape(WIN, 8, 8, WIDE)[:, 0:WIN]
    y = y + own[...].reshape(WIN, WIN, 8, WIDE)
    y = jnp.where(iota(y.shape, 2) < WIN, y, 0.0).reshape(PLANE, 8, WIDE)
    tok[...] = y + marks[...]
    send_sides(tok, t0, t1, t2, t3)
    flat = y.reshape(PLANE * 8, WIDE)
    count = jnp.sum(marks[...].reshape(PLANE * 8, WIDE))
    row = iota((8, WIDE), 0)
    stats[...] = (
        jnp.where(row == 0, colsum(flat), 0.0)
        + jnp.where(row == 1, colsum(flat * flat), 0.0)
        + jnp.where(row == 2, count, 0.0)
    )


def head_kernel(
    sizes, voxels,
    own, s0, s1, s2, s3, sums, vectors, head_w,
    grown, slope_out, stats, d_head, d_rows,
):
    grown_lines(sizes, own, s0, s1, s2, s3, grown)
    rows = 11 * 12 * 8
    both = grown[...].reshape(rows, WIDE)
    lane = iota((rows, WIDE), 1)
    tokens = jnp.where(lane < EMB, both, 0.0)
    target = jnp.where(lane < CLASSES, roll(both, WIDE - EMB, 1), 0.0)
    live = jnp.sum(target, 1, keepdims=True)
    count = F32(voxels)
    average = sums[0:1, :] / count
    spread = sums[1:2, :] / count - average * average
    inv = lax.rsqrt(spread + eps_norm)
    gain = vectors[2:3, :]
    bias = vectors[3:4, :]
    hat = (tokens - average) * inv
    act, slope = gelu_both(hat * gain + bias)
    act = jnp.where(lane == EMB, 1.0, act)
    w = head_w[...]
    logits = mm(act, w)
    logits = jnp.where(lane < CLASSES, logits, -1e30)
    top = jnp.max(logits, 1, keepdims=True)
    e = jnp.exp(logits - top)
    total = jnp.sum(e, 1, keepdims=True)
    logp = logits - top - jnp.log(total)
    scale = 1.0 / sums[2:3, 0:1]
    d_logits = (e / total * live - target) * scale
    d_normed = jnp.where(lane < EMB, mm_nt(d_logits, w) * slope, 0.0)
    d_tokens = d_normed * gain * inv
    slope_out[...] = d_tokens.reshape(11, 12, 8, WIDE)

    def own_rows(x):
        x = x.reshape(11, 12, 8, WIDE)[2:9, 2:9]
        x = jnp.where(iota(x.shape, 2) < WIN, x, 0.0)
        return x.reshape(PLANE * 8, WIDE)

    loss = -jnp.sum(own_rows(target * jnp.where(lane < CLASSES, logp, 0.0)))
    own_d = own_rows(d_logits)
    own_n = own_rows(d_normed)
    own_hat = own_rows(hat)
    zeros = jnp.zeros((512 - PLANE * 8, WIDE), F32)
    left = rows_t(jnp.concatenate([own_d, zeros], 0))
    d_head[...] = mm_tn(left, jnp.concatenate([own_rows(act), zeros], 0)).T
    d_gain = colsum(own_n * own_hat)
    d_bias = colsum(own_n)
    d_average = -d_bias * gain * inv
    d_spread = d_gain * gain * inv * inv * -0.5
    d_two = d_spread / count
    d_one = (d_average - 2.0 * average * d_spread) / count
    row = iota((8, WIDE), 0)
    live_lane = iota((8, WIDE), 1) < EMB
    stats[...] = (
        jnp.where((row == 0) & live_lane, d_one, 0.0)
        + jnp.where((row == 1) & live_lane, d_two, 0.0)
        + jnp.where(row == 2, loss, 0.0)
    )
    d_rows[...] = (
        jnp.where(row == 0, d_gain, 0.0)
        + jnp.where(row == 1, d_bias, 0.0)
    )


def sides_back_kernel(sizes, grown, pre, side_act, side_grown, act):
    act[0:9] = gelu(pre[...]) * volume_mask(sizes, 9, 10, 1, 9)
    act[9:10] = jnp.zeros((1, 10, 8, WIDE), F32)
    taps(act, 0, 10, 0, 8, side_act)
    taps(grown, 1, 10, 1, 8, side_grown)


def weights_back_kernel(conv0, conv1, weights0, weights1):
    tap_weights_back(conv0, 3, weights0)
    tap_weights_back(conv1, 0, weights1)


def conv_back_kernel(
    sizes,
    tok, slope, sums, pre, side_act, side_grown, weights0, weights1, d_rows, d_head,
    d_own, keep, send, carry, seam,
    grads, dgrown, act, side, side_own, flat, result,
):
    lane = iota((11, 12, 8, WIDE), 3)
    inside = volume_mask(sizes, 11, 12, 2, 11)
    steady = sums[0:1, :].reshape(1, 1, 1, WIDE)
    rising = 2.0 * sums[1:2, :].reshape(1, 1, 1, WIDE)
    d_tok = slope[...] + jnp.where(lane < EMB, (steady + tok[...] * rising) * inside, 0.0)
    dgrown[...] = d_tok
    grads[5191:, :] = jnp.zeros((45, WIDE), F32)
    grads[0:8, :] = jnp.zeros((8, WIDE), F32)
    grads[5189:5191, :] = d_rows[0:2, :]
    own = dgrown[2:9, 2:10]
    line = iota(own.shape, 1)
    own = jnp.where(line < WIN, own, 0.0).reshape(WIN * 64, WIDE)
    grads[5188:5189, :] = colsum(own)

    near = volume_mask(sizes, 9, 10, 1, 9)
    conv_weight_grad(side_act, own, 64, grads, 2596)
    taps(dgrown, 0, 11, 0, 10, side)

    conv(side, weights1, (0, 3, 6, 9), 80, result)
    act[0:9] = result[...].reshape(9, 10, 8, WIDE) * gelu_both(pre[...])[1] * near

    own = act[1:8, 1:9]
    line = iota(own.shape, 1)
    own = jnp.where(line < WIN, own, 0.0).reshape(WIN * 64, WIDE)
    grads[2595:2596, :] = colsum(own)
    conv_weight_grad(side_grown, own, 64, grads, 3)
    carry[...] = grads[0:24, :]
    flat[3 * (GROUPS - CUTS[3]) :, :] = jnp.zeros((flat.shape[0] - 3912, WIDE), F32)
    flatten(grads, 20, GROUPS - CUTS[3], flat)
    start = 3 * CUTS[3]
    head_rows(d_head[...], flat, HEAD_ROW - start)
    seam[...] = flat[0 : LATE_ROWS - start, :]
    scatter(sizes, flat, LATE_ROWS - start, keep, send)
    taps(act, 0, 9, 0, 8, side_own)
    conv(side_own, weights0, (0, 4, WIN), 64, result)
    y = result[0 : WIN * 64, :].reshape(WIN, 8, 8, WIDE)[:, 0:WIN] + dgrown[2:9, 2:9]
    y = jnp.where(iota(y.shape, 2) < WIN, y, 0.0)
    d_own[...] = y.reshape(PLANE, 8, WIDE)


def back_mlp_kernel(d_own, lay2, mid2, hpre2, d_mid, grads, dense):
    from_lines(d_own, dense)
    grads[...] = jnp.zeros_like(grads)
    d_mid[...] = mlp_back(dense[...], mid2[...], hpre2, Rows(lay2, 2), grads, 2)


def back_two_kernel(
    d_mid2, grads2, carry, lay1, lay2, tok2, save, lse, mixed, mid1, hpre1,
    d_mid, grads1, flat, carry2, pa, pb, pc,
    grads, *sc,
):
    layer = Rows(lay2, 2)
    grads[0:1168, :] = grads2[...]
    d = d_mid2[...]
    tokens = tok2[...]
    normed = norm(tokens, layer[0:1, :], layer[1:2, :])
    d_normed = attention_back(d, normed, layer, save, lse, mixed, sc, grads, 2)
    d = d + pre_norm_back(d_normed, tokens, layer, grads, 2)
    grads[1167:1184, :] = carry[3:20, :]
    flatten(grads, 32, CUTS[3] - CUTS[2], flat)
    carry2[...] = grads[0:32, :]
    layer = Rows(lay1, 1)
    d = mlp_back(d, mid1[...], hpre1, layer, grads1, 1)
    d_mid[...] = d
    send_parts(d_mid, pa, pb, pc)


def back_shifted_kernel(
    sizes,
    own, pa, pb, pc, lay1, window, save, lse, mixed, grads1, carry2, _,
    d_window, flat, carry1, qa, qb, qc,
    region, grads, grad, *sc,
):
    put_region(region, sizes)
    take_parts(own, pa, pb, pc, grad)
    grads[0:1168, :] = grads1[...]
    grads[0:3, :] = jnp.zeros((3, WIDE), F32)
    d_window[...] = attention_back(
        grad[...], window[...], Rows(lay1, 1), save, lse, mixed, sc, grads, 1,
        region,
    )
    send_parts(d_window, qa, qb, qc)
    grads[1166:1196, :] = carry2[2:32, :]
    flatten(grads, 12, CUTS[2] - CUTS[1], flat)
    carry1[...] = grads[0:16, :]


def back_first_kernel(
    sizes,
    d_mid, own, qa, qb, qc, tok1, lay0, lay1, merge, dense, tok0, save, lse, mixed, middle, hpre,
    carry1, flat1, flat2, seam, _,
    keep, send,
    flat, grads, grad, *sc,
):
    take_parts(own, qa, qb, qc, grad)
    grads[1556:1572, :] = carry1[...]
    d = d_mid[...] + pre_norm_back(grad[...], tok1[...], Rows(lay1, 1), grads, 1557)
    layer = Rows(lay0, 0)
    at = MERGE_ROWS
    d = mlp_back(d, middle[...], hpre, layer, grads, at)
    tokens = tok0[...]
    normed = norm(tokens, layer[0:1, :], layer[1:2, :])
    d_normed = attention_back(d, normed, layer, save, lse, mixed, sc, grads, at)
    d = d + pre_norm_back(d_normed, tokens, layer, grads, at)
    live = iota((ROWS, WIDE), 0) < VOX
    d = jnp.where(live, d, 0.0)
    hat = merged_norm(dense[...])
    gain = hidden_rows(merge, 0, 1)
    bias = hidden_rows(merge, 4, 1)
    w = merge[8 : 8 + MERGE, :]
    put_hidden_rows(grads, 8 - 8, 1, jnp.zeros((1, MERGE), F32))
    grads[8 : 8 + MERGE, :] = mm_tn(rows_t(d), hat * gain + bias).T
    d_hat = mm_nt(d, w)
    put_hidden_rows(grads, 0, 1, colsum(d_hat * hat))
    put_hidden_rows(grads, 4, 1, colsum(d_hat))
    flatten(grads, 0, CUTS[1], flat)
    at = 0
    for cut, part in ((CUTS[1], flat1), (CUTS[2], flat2), (CUTS[3], seam)):
        at = 3 * cut
        flat[at : at + part.shape[0], :] = part[...]
    at += seam.shape[0]
    if flat.shape[0] > at:
        flat[at:, :] = jnp.zeros((flat.shape[0] - at, WIDE), F32)
    scatter(sizes, flat, 0, keep, send)


def radices(count):
    steps = [2]
    left = count // 2
    while left > 1:
        steps.append(4 if left >= 4 else 2)
        left //= steps[-1]
    return steps


def block_rows(rows, count):
    return -(-rows // (8 * count)) * 8


def own_number(sizes):
    return lax.axis_index("slab") * sizes[1] + lax.axis_index("mp")


def place_in_half(distance, count):
    place = 0
    shift = 1
    for radix in radices(count)[1:]:
        digit = jnp.bitwise_and(lax.shift_right_logical(distance, shift), radix - 1)
        place = place * radix + digit
        shift += radix.bit_length() - 1
    return place


def scatter(sizes, source, first, keep, send):
    count = sizes[0] * sizes[1]
    rows = keep.shape[0] * 2 // count
    me = own_number(sizes)
    odd = jnp.bitwise_and(me, 1)

    def per_pair(t, carry):
        for block, out in ((2 * t + odd, keep), (2 * t + 1 - odd, send)):
            place = place_in_half(jnp.bitwise_xor(block, me), count)
            at = pl.multiple_of(first + block * rows, 8)
            to = pl.multiple_of(place * rows, 8)
            out[pl.ds(to, rows), :] = source[pl.ds(at, rows), :]
        return carry

    lax.fori_loop(0, count // 2, per_pair, 0)


def traded(value, distance, count):
    pairs = [(i, i ^ distance) for i in range(count)]
    return lax.ppermute(value, ("slab", "mp"), pairs)


def later(got, after):
    return got if after is None else list(lax.optimization_barrier((*got, after)))[:-1]


def summing(keep, send, count):
    steps = radices(count)
    got = [keep, traded(send, 1, count)]
    shift = 1
    after = yield None
    for radix in steps[1:]:
        got = later(got, after)
        total = sum(got[1:], got[0])
        rows = total.shape[0] // radix
        parts = [total[k * rows : (k + 1) * rows] for k in range(radix)]
        got = parts[:1] + [traded(parts[k], k << shift, count) for k in range(1, radix)]
        shift += radix.bit_length() - 1
        after = yield parts[0]
    got = later(got, after)
    own = sum(got[1:], got[0])
    for radix in reversed(steps[1:]):
        shift -= radix.bit_length() - 1
        got = [own] + [traded(own, k << shift, count) for k in range(1, radix)]
        after = yield own
        own = jnp.concatenate(later(got, after), 0)
        yield own
    yield own, traded(own, 1, count)


def finished(chain, after=None):
    last = next(chain) if after is None else chain.send(after)
    while not isinstance(last, tuple):
        last = next(chain)
    return last


def exchanged_sum(value, count):
    shift = 0
    for radix in radices(count):
        got = [value] + [traded(value, k << shift, count) for k in range(1, radix)]
        while len(got) > 1:
            got = [got[i] + got[i + 1] for i in range(0, len(got), 2)]
        value = got[0]
        shift += radix.bit_length() - 1
    return value


PIECE = 294912


def place_blocks(sizes, own, other, out, size):
    count = sizes[0] * sizes[1]
    me = own_number(sizes)
    rows = own.shape[0] * 2 // count

    def per_block(block, carry):
        distance = jnp.bitwise_xor(block, me)
        at = pl.ds(pl.multiple_of(place_in_half(distance, count) * rows, 8), rows)
        near = jnp.bitwise_and(distance, 1) == 0
        to = pl.ds(pl.multiple_of(block * rows, 8), rows)
        out[to, :] = jnp.where(near, own[at, :], other[at, :])
        return carry

    lax.fori_loop(0, size // rows, per_block, 0)


def squares(*refs):
    total = jnp.zeros((8, WIDE), F32)
    for ref in refs:
        x = ref[...]
        total = total + jnp.sum((x * x).reshape(-1, 8, WIDE), 0)
    return total


def place_early_kernel(sizes, own, other, out, square):
    place_blocks(sizes, own, other, out, EARLY_ROWS)
    square[...] = squares(own, other)


def adamw_kernel(
    sizes,
    late, late_other, early, square, tail, sums, params, first, second,
    new_params, new_first, new_second, loss, valid, norm_out,
    grad, scale_ref,
):
    step = pl.program_id(0)

    @pl.when(step == 0)
    def gather():
        norm = jnp.sqrt(jnp.sum(squares(late, late_other) + square[...]))
        loss[0] = jnp.sum(tail[2:3, 0:1])
        valid[0] = jnp.sum(sums[2:3, 0:1])
        norm_out[0] = norm
        scale_ref[0] = jnp.minimum(1.0, clip_norm / (norm + 1e-06))
        place_blocks(sizes, late, late_other, grad, LATE_ROWS)
        grad[LATE_ROWS:, :] = early[...]

    def update(base, low, size):
        rows = -(-size // 1024) * 8
        at = pl.ds(pl.multiple_of(base // WIDE + low // WIDE, 8), rows)
        g = grad[at, :].reshape(rows * WIDE)[:size] * scale_ref[0]
        here = pl.ds(pl.multiple_of(base + low, 1024), size)
        one = beta_one * first[here] + (1.0 - beta_one) * g
        two = beta_two * second[here] + (1.0 - beta_two) * g * g
        there = pl.ds(low, size)
        new_first[there] = one
        new_second[there] = two
        two = two * (1.0 / (1.0 - beta_two**STEP))
        low_by = two * lax.rsqrt(jnp.maximum(two, 1e-37)) + adam_eps
        inverse = pl.reciprocal(low_by, approx=True)
        inverse = inverse * (2.0 - low_by * inverse)
        new_params[there] = params[here] * (1.0 - learn_rate * decay_rate) - (
            one * (learn_rate / (1.0 - beta_one**STEP))
        ) * inverse

    whole = NPARAM // PIECE

    @pl.when(step < whole)
    def full():
        def part(i, carry):
            low = pl.multiple_of(i * 16384, 16384)
            update(step * PIECE, low, 16384)
            return carry

        lax.fori_loop(0, PIECE // 16384, part, 0)

    @pl.when(step == whole)
    def last():
        rest = NPARAM - whole * PIECE
        main = rest // 1024 * 1024
        for low in range(0, main, 16384):
            update(whole * PIECE, low, min(16384, main - low))
        update(whole * PIECE, main, rest - main)


def adamw(sizes, parts, arrays):
    pieces = -(-NPARAM // PIECE)
    piece = pl.BlockSpec((PIECE,), lambda i: (i,))
    vmem = pl.BlockSpec(memory_space=pltpu.VMEM)
    smem = pl.BlockSpec(memory_space=pltpu.SMEM)
    return pl.pallas_call(
        functools.partial(adamw_kernel, sizes),
        grid=(pieces,),
        out_shape=[arr(NPARAM)] * 3 + [arr(1)] * 3,
        in_specs=[vmem] * (len(parts) + len(arrays)),
        out_specs=[piece] * 3 + [smem] * 3,
        scratch_shapes=[pltpu.VMEM((LATE_ROWS + EARLY_ROWS, WIDE), F32), pltpu.SMEM((1,), F32)],
        compiler_params=pltpu.CompilerParams(vmem_limit_bytes=16 * 1024 * 1024),
        cost_estimate=pl.CostEstimate(flops=6 * 10**9, bytes_accessed=0, transcendentals=0),
        name="adamw",
    )(*parts, *arrays)


def arr(*shape):
    return jax.ShapeDtypeStruct(shape, F32)


def call(kernel, outs, scratch, *args, name=None, us=1.0, far=(), mib=16):
    vmem = pl.BlockSpec(memory_space=pltpu.VMEM)
    smem = pl.BlockSpec(memory_space=pltpu.SMEM)
    return pl.pallas_call(
        kernel,
        out_shape=list(outs),
        in_specs=[vmem] * len(args) + [pl.BlockSpec(memory_space=pl.ANY)] * len(far),
        out_specs=[smem if o.shape == (1,) else vmem for o in outs],
        scratch_shapes=list(scratch),
        compiler_params=pltpu.CompilerParams(vmem_limit_bytes=mib * 1024 * 1024),
        cost_estimate=pl.CostEstimate(
            flops=int(us * 1.15e9), bytes_accessed=0, transcendentals=0
        ),
        name=name,
    )(*args, *far)


SQUARE = arr(ROWS, WIDE)
SAVE = arr(ROWS, 3 * WIDE)
FORWARD = [
    pltpu.VMEM((2, ROWS, 2 * WIDE), BF16),
    pltpu.VMEM((2, KEYS, 2 * WIDE), BF16),
    pltpu.VMEM((2 * KEYS, 2 * WIDE), BF16),
]
BACKWARD = [
    pltpu.VMEM((2, ROWS, 2 * WIDE), BF16),
    pltpu.VMEM((2, KEYS, 2 * WIDE), BF16),
    pltpu.VMEM((2, ROWS, 2 * WIDE), BF16),
    pltpu.VMEM((2, KEYS, 2 * WIDE), BF16),
    pltpu.VMEM((2 * KEYS, 2 * WIDE), BF16),
    pltpu.VMEM((ROWS, WIDE), F32),
    pltpu.VMEM((2, WIDE, KEYS), F32),
    pltpu.VMEM((2, KEYS, 2 * KEYS), BF16),
    pltpu.VMEM((2, KEYS, 2 * KEYS), BF16),
    pltpu.VMEM((2, WIDE, KEYS), BF16),
    pltpu.VMEM((2, WIDE, KEYS), BF16),
    pltpu.VMEM((ROWS, WIDE), F32),
    pltpu.VMEM((ROWS, 2 * KEYS), F32),
    pltpu.VMEM((ROWS, 2 * KEYS), F32),
    pltpu.VMEM((2 * KEYS, 2 * WIDE), BF16),
    pltpu.VMEM((2 * KEYS, 2 * WIDE), BF16),
]
PARTS = [arr(ROWS_A, WIDE), arr(ROWS_B, WIDE), arr(ROWS_C, WIDE)]


def passed(parts, steps, sizes):
    slabs, rows = sizes
    moved = []
    for part, (ds, dm) in zip(parts, ((1, 0), (0, 1), (1, 1))):
        pairs = []
        for s in range(slabs):
            for m in range(rows):
                target = ((s + steps * ds) % slabs) * rows + (m + steps * dm) % rows
                pairs.append((s * rows + m, target))
        moved.append(lax.ppermute(part, ("slab", "mp"), pairs))
    return moved


SIDES = [arr(2 * WIN, 8, WIDE)] * 4


def paired(axis, size):
    near = [(i, i ^ 1) for i in range(size)]
    far = [(i, (i + (1 if i % 2 else -1)) % size) for i in range(size)]
    return (
        lambda value: lax.ppermute(value, axis, near),
        lambda value: lax.ppermute(value, axis, far),
    )


def column_kernel(sizes, near_d, far_d, near_h, far_h, near_out, far_out):
    slab = lax.axis_index("slab")
    odd_d = jnp.bitwise_and(slab, 1) == 1
    odd_h = jnp.bitwise_and(lax.axis_index("mp"), 1) == 1
    at_low = slab == 0
    at_high = slab == sizes[0] - 1
    near_out[4:18] = near_h[...]
    far_out[4:18] = far_h[...]
    for d in range(2):
        near = near_d[d * WIN : (d + 1) * WIN]
        far = far_d[d * WIN : (d + 1) * WIN]
        before = jnp.where(odd_d, near, jnp.where(at_low, 0.0, far))
        after = jnp.where(odd_d, jnp.where(at_high, 0.0, far), near)
        for x, at in ((before, 2 * d), (after, 18 + 2 * d)):
            low, high = x[0:2], x[WIN - 2 : WIN]
            near_out[at : at + 2] = jnp.where(odd_h, low, high)
            far_out[at : at + 2] = jnp.where(odd_h, high, low)


def beside(sides, sizes):
    near, far = paired("slab", sizes[0])
    near_d, far_d = near(sides[0]), far(sides[1])
    near_h, far_h = call(
        functools.partial(column_kernel, sizes), [arr(22, 8, WIDE)] * 2, [],
        near_d, far_d, sides[2], sides[3],
        name="column", us=0.3,
    )
    near, far = paired("mp", sizes[1])
    return near_d, far_d, near(near_h), far(far_h)


REGION = [pltpu.VMEM((ROWS, KEYS), F32)]


def on_device(sizes, feats, labels, valid, params, moment_one, moment_two):
    slabs, rows = sizes
    count = slabs * rows

    def room(spans):
        sizes = [(span_of(groups)[1] + 8) * WIDE for groups in spans]
        return [
            [pltpu.VMEM((size,), F32) for size in sizes],
            pltpu.VMEM((2048, WIDE), F32),
            pltpu.SemaphoreType.DMA((len(spans),)),
        ]

    first_size = FIRST_SPANS[-1][1] * 384
    merge, lay0 = call(
        functools.partial(prep_kernel, FIRST_SPANS),
        [arr(MERGE_ROWS, WIDE), arr(1176, WIDE)],
        room(FIRST_SPANS),
        name="prep_first", us=2.0, far=(params[:first_size],),
    )
    lay1, lay2 = call(
        functools.partial(prep_kernel, LAYER_SPANS),
        [arr(1168, WIDE)] * 2,
        room(LAYER_SPANS),
        name="prep_layers", us=2.0, far=(params,),
    )
    taps_shape = jax.ShapeDtypeStruct((27 * 256, 256), BF16)
    conv0, weights0, bias0 = call(
        prep_conv0_kernel,
        [arr(2596, WIDE), taps_shape, arr(8, WIDE)],
        room(CONV_SPANS[:1]),
        name="prep_conv0", us=1.5, far=(params,),
    )
    conv1, head_w, weights1, vectors = call(
        prep_conv1_kernel,
        [arr(2640, WIDE), arr(WIDE, WIDE), taps_shape, arr(8, WIDE)],
        room(CONV_SPANS[1:]),
        params[NPARAM // WIDE * WIDE :], bias0,
        name="prep_conv1", us=1.5, far=(params,),
    )

    dense, tok0, save0, lse0, mixed0, mid0, hpre0, tok1, ahead, *parts = call(
        first_kernel,
        [arr(ROWS, MERGE), SQUARE, SAVE, SQUARE, SQUARE, SQUARE, arr(ROWS, HID), SQUARE, SQUARE]
        + PARTS,
        FORWARD,
        feats.reshape(PLANE, WIN, MERGE), merge, lay0,
        name="first", us=6.0,
    )
    parts = passed(parts, -1, sizes)
    window, save1, lse1, mixed1, out1, *parts = call(
        functools.partial(shifted_kernel, sizes),
        [SQUARE, SAVE, SQUARE, SQUARE, SQUARE] + PARTS,
        REGION + FORWARD,
        ahead, *parts, lay1,
        name="shifted", us=4.5, far=(weights0,),
    )
    parts = passed(parts, 1, sizes)
    mid1, hpre1, tok2, save2, lse2, mixed2, mid2, hpre2, lines, *sides = call(
        second_kernel,
        [SQUARE, arr(ROWS, HID), SQUARE, SAVE, SQUARE, SQUARE, SQUARE, arr(ROWS, HID)]
        + [arr(PLANE, 8, WIDE)] + SIDES,
        [pltpu.VMEM((ROWS, WIDE), F32)] + FORWARD,
        tok1, out1, *parts, lay1, lay2,
        name="second", us=6.5, far=(weights1,),
    )
    sides = beside(sides, sizes)
    back0, back1 = call(
        weights_back_kernel,
        [taps_shape] * 2,
        [],
        conv0, conv1,
        name="weights_back", us=1.5,
    )
    grown, pre, tok3, sums, *tok_sides = call(
        functools.partial(conv_kernel, sizes),
        [arr(11, 12, 8, WIDE), arr(9, 10, 8, WIDE), arr(PLANE, 8, WIDE), arr(8, WIDE)] + SIDES,
        [
            pltpu.VMEM((9, 10, 8, WIDE), F32),
            pltpu.VMEM((880, 2304), BF16),
            pltpu.VMEM((576, 2304), BF16),
            pltpu.VMEM((PLANE, 8, WIDE), F32),
            pltpu.VMEM((720, WIDE), F32),
        ],
        lines, *sides, labels, valid, weights0, weights1, vectors,
        name="conv", us=8.0, mib=20, far=(back0,),
    )
    tok_sides = beside(tok_sides, sizes)
    side_act, side_grown = call(
        functools.partial(sides_back_kernel, sizes),
        [jax.ShapeDtypeStruct((640, 2304), BF16)] * 2,
        [pltpu.VMEM((10, 10, 8, WIDE), F32)],
        grown, pre,
        name="sides_back", us=2.0,
    )
    sums = exchanged_sum(sums, count)
    voxels = WIN * slabs * WIN * rows * WIN
    tok3, slope, tail, d_head, d_rows = call(
        functools.partial(head_kernel, sizes, voxels),
        [arr(11, 12, 8, WIDE), arr(11, 12, 8, WIDE), arr(8, WIDE), arr(WIDE, WIDE), arr(8, WIDE)],
        [],
        tok3, *tok_sides, sums, vectors, head_w,
        name="head", us=3.5,
    )
    tail = exchanged_sum(tail, count)
    late_rows = block_rows(LATE_ROWS, count) * count
    early_rows = block_rows(EARLY_ROWS, count) * count
    seam_rows = LATE_ROWS - 3 * CUTS[3]
    d_own, keep, send, carry3, seam = call(
        functools.partial(conv_back_kernel, sizes),
        [arr(PLANE, 8, WIDE)] + [arr(early_rows // 2, WIDE)] * 2
        + [arr(24, WIDE), arr(seam_rows, WIDE)],
        [
            pltpu.VMEM((5236, WIDE), F32),
            pltpu.VMEM((11, 12, 8, WIDE), F32),
            pltpu.VMEM((10, 10, 8, WIDE), F32),
            pltpu.VMEM((880, 2304), BF16),
            pltpu.VMEM((576, 2304), BF16),
            pltpu.VMEM((seam_rows + early_rows, WIDE), F32),
            pltpu.VMEM((720, WIDE), F32),
        ],
        tok3, slope, tail, pre, side_act, side_grown, back0, back1, d_rows, d_head,
        name="conv_back", us=14.0, mib=28,
    )
    early = summing(keep, send, count)
    next(early)
    d_mid2, grads2 = call(
        back_mlp_kernel,
        [SQUARE, arr(1168, WIDE)],
        [pltpu.VMEM((ROWS, WIDE), F32)],
        d_own, lay2, mid2, hpre2,
        name="back_mlp", us=3.0,
    )
    step = early.send(d_mid2)
    d_mid, grads1, flat2, carry2, *parts = call(
        back_two_kernel,
        [SQUARE, arr(1168, WIDE), arr(3 * (CUTS[3] - CUTS[2]), WIDE), arr(32, WIDE)] + PARTS,
        [pltpu.VMEM((1184, WIDE), F32)] + BACKWARD,
        d_mid2, grads2, carry3, lay1, lay2, tok2, save2, lse2, mixed2, mid1, hpre1,
        name="back_two", us=9.0,
    )
    parts = passed(parts, -1, sizes)
    step = early.send(d_mid)
    d_window, flat1, carry1, *parts = call(
        functools.partial(back_shifted_kernel, sizes),
        [SQUARE, arr(3 * (CUTS[2] - CUTS[1]), WIDE), arr(16, WIDE)] + PARTS,
        REGION + [pltpu.VMEM((1200, WIDE), F32), pltpu.VMEM((ROWS, WIDE), F32)] + BACKWARD,
        d_mid, *parts, lay1, window, save1, lse1, mixed1, grads1, carry2,
        name="back_shifted", us=10.5, far=(step,),
    )
    early.send(d_window)
    parts = passed(parts, 1, sizes)
    next(early)
    step = next(early)
    late = call(
        functools.partial(back_first_kernel, sizes),
        [arr(late_rows // 2, WIDE)] * 2,
        [
            pltpu.VMEM((late_rows, WIDE), F32),
            pltpu.VMEM((1572, WIDE), F32),
            pltpu.VMEM((ROWS, WIDE), F32),
        ]
        + BACKWARD,
        d_mid, d_window, *parts, tok1, lay0, lay1, merge, dense, tok0, save0, lse0, mixed0, mid0,
        hpre0, carry1, flat1, flat2, seam,
        name="back_first", us=13.5, far=(step,),
    )
    step = early.send(late[0])
    keep, send = later(list(late), step)
    late_sum = finished(summing(keep, send, count))
    early = finished(early)
    early = call(
        functools.partial(place_early_kernel, sizes),
        [arr(EARLY_ROWS, WIDE), arr(8, WIDE)],
        [],
        *early,
        name="place_early", us=0.6,
    )
    new_params, new_first, new_second, loss, valid_count, norm = adamw(
        sizes, (*late_sum, *early, tail, sums), (params, moment_one, moment_two)
    )
    return (
        loss.reshape(()), valid_count.reshape(()), norm.reshape(()),
        new_params, new_first, new_second,
    )


def solution(mesh):
    placed = (
        P("slab", "mp", None, None),
        P("slab", "mp", None),
        P("slab", "mp", None),
        P(),
        P(),
        P(),
    )
    sizes = (mesh.shape["slab"], mesh.shape["mp"])
    return jax.shard_map(
        functools.partial(on_device, sizes),
        mesh=mesh,
        in_specs=placed,
        out_specs=(P(), P(), P(), P(), P(), P()),
        check_vma=False,
    )
```

```python
import functools

import jax
import jax.numpy as jnp
from jax import lax
from jax.experimental import pallas as pl
from jax.experimental.pallas import tpu as pltpu
from jax.sharding import PartitionSpec as P

EMB = 96
HEADS = 6
HDIM = 16
HID = 384
MERGE = 384
CLASSES = 14
WIN = 7
SHIFT = 3
LAYERS = 3
STEP = 10

F32 = jnp.float32
BF16 = jnp.bfloat16
eps_norm = 1e-05
beta_one = 0.9
beta_two = 0.999
adam_eps = 1e-08
learn_rate = 0.05
decay_rate = 0.05
clip_norm = 0.01
LOG2E = 1.4426950408889634

VOX = WIN * WIN * WIN
ROWS = 352
KEYS = 384
BLOCKS = ((0, 128), (128, 256), (256, 352))
WIDE = 128
PLANE = WIN * WIN
FAR = WIN - SHIFT
ROWS_A = SHIFT * FAR * WIN
ROWS_B = FAR * SHIFT * WIN
ROWS_C = SHIFT * SHIFT * WIN

MERGE_ROWS = 392
LAYER_ROWS = 1165
TAP_ROWS = 27 * EMB
GROUPS = 2280
NPARAM = 872558
HEAD_ROW = 6806
HEAD_ROWS = 11
HEAD_LANE = 32
LATE_ROWS = 3072
EARLY_ROWS = 3840
LAYER_BASE = (98, 389, 680)
CONV_BASE = (971, 1620)
CUTS = (0, 392, 688, 976, 2280)

R_QKV, R_QKVB, R_PROJ, R_PROJB = 4, 292, 295, 391
R_HID, R_HIDB, R_OUT, R_OUTB = 392, 776, 780, 1164


def iota(shape, dim):
    return lax.broadcasted_iota(jnp.int32, shape, dim)


def split(x):
    hi = x.astype(BF16)
    return hi, (x - hi.astype(F32)).astype(BF16)


def pair(x):
    return jnp.concatenate(split(x), 1)


def fold(y):
    half = y.shape[1] // 2
    return y[:, :half] + y[:, half:]


def fold_rows(y):
    half = y.shape[0] // 2
    return y[:half] + y[half:]


def dot(a, b):
    return jnp.dot(a, b, preferred_element_type=F32)


def dot_nt(a, b):
    return lax.dot_general(a, b, (((1,), (1,)), ((), ())), preferred_element_type=F32)


def weight_nn(w):
    top = pair(w)
    return jnp.concatenate([top, top], 0)


def weight_nt(w):
    hi, lo = split(w)
    return jnp.concatenate(
        [jnp.concatenate([hi, hi], 1), jnp.concatenate([lo, lo], 1)], 0
    )


def mm(x, w):
    return fold(dot(pair(x), weight_nn(w)))


def mm_nt(x, w):
    return fold(dot_nt(pair(x), weight_nt(w)))


def with_rows(x, rows):
    if x.shape[0] == rows:
        return x
    return jnp.concatenate([x, jnp.zeros((rows - x.shape[0], x.shape[1]), F32)], 0)


def rows_t(x):
    return jnp.concatenate(split(with_rows(x, -(-x.shape[0] // WIDE) * WIDE).T), 0)


def mm_tn(xt, y):
    return fold_rows(fold(dot(xt, pair(with_rows(y, xt.shape[1])))))


def deep(w):
    return jnp.concatenate([w, jnp.zeros((WIDE - EMB, w.shape[1]), F32)], 0)


def roll(x, shift, axis):
    return pltpu.roll(x, shift, axis)


def four_to_three(y):
    lane = iota(y[0].shape, 1)
    a = jnp.where(lane < 96, y[0], roll(y[1], 96, 1))
    b = jnp.where(lane < 64, roll(y[1], 96, 1), roll(y[2], 64, 1))
    c = jnp.where(lane < 32, roll(y[2], 64, 1), roll(y[3], 32, 1))
    return a, b, c


def three_to_four(x):
    lane = iota(x[0].shape, 1)
    live = lane < EMB
    a = x[0]
    b = jnp.where(lane < 32, roll(x[0], 32, 1), roll(x[1], 32, 1))
    c = jnp.where(lane < 64, roll(x[1], 64, 1), roll(x[2], 64, 1))
    d = roll(x[2], 96, 1)
    return tuple(jnp.where(live, v, 0.0) for v in (a, b, c, d))


def hidden_rows(ref, start, count):
    return jnp.concatenate(
        four_to_three([ref[pl.ds(start + c, count, stride=4), :] for c in range(4)]), 1
    )


def put_hidden_rows(ref, start, count, x):
    parts = three_to_four([x[:, i * WIDE : (i + 1) * WIDE] for i in range(3)])
    for c in range(4):
        ref[pl.ds(start + c, count, stride=4), :] = parts[c]


def flatten(ref, start, groups, out):
    parts = four_to_three([ref[pl.ds(start + c, groups, stride=4), :] for c in range(4)])
    for c in range(3):
        out[pl.ds(c, groups, stride=3), :] = parts[c]


def norm_stats(x):
    live = iota(x.shape, 1) < EMB
    mean = jnp.sum(x, 1, keepdims=True) * (1.0 / EMB)
    centred = jnp.where(live, x - mean, 0.0)
    var = jnp.sum(centred * centred, 1, keepdims=True) * (1.0 / EMB)
    inv = lax.rsqrt(var + eps_norm)
    return centred * inv, inv


def norm(x, gain, bias):
    hat, _ = norm_stats(x)
    return hat * gain + bias


def norm_back(hat, inv, gain, grad):
    up = grad * gain
    one = jnp.sum(up, 1, keepdims=True) * (1.0 / EMB)
    two = jnp.sum(up * hat, 1, keepdims=True) * (1.0 / EMB)
    live = iota(hat.shape, 1) < EMB
    return jnp.where(live, inv * (up - one - hat * two), 0.0)


def colsum(x):
    return jnp.sum(x, 0, keepdims=True)


def gelu(x):
    return 0.5 * x * (1.0 + lax.erf(x * (0.5**0.5)))


def gelu_both(x):
    cdf = 0.5 * (1.0 + lax.erf(x * (0.5**0.5)))
    slope = cdf + x * (jnp.exp(x * x * -0.5) * 0.3989422804014327)
    return x * cdf, slope


def head_groups(x):
    lane = iota(x.shape, 1)
    swapped = roll(x, 64, 1)
    return jnp.where(lane < 64, x, swapped), jnp.where(lane < 64, swapped, x)


def as_left(x):
    both = []
    low = iota(x.shape, 1) < 64
    for part in head_groups(x):
        hi = part.astype(BF16).astype(F32)
        one = jnp.where(low, hi, part - hi).astype(BF16)
        both.append(jnp.concatenate([one, one], 1))
    return both


def as_right(x):
    return [pair(part) for part in head_groups(with_rows(x, KEYS))]


def head_mask(h, width):
    lane = iota((1, width), 1)
    lane = jnp.bitwise_and(lane, 63)
    low = jnp.bitwise_and(h, 3) * HDIM
    return jnp.where((lane >= low) & (lane < low + HDIM), 1.0, 0.0)


def own_lanes(h):
    lane = iota((1, WIDE), 1)
    return jnp.where((lane >= h * HDIM) & (lane < (h + 1) * HDIM), 1.0, 0.0)


def both_heads(right, heads, out):
    for k, h in enumerate(heads):
        out[k * KEYS : (k + 1) * KEYS, :] = right * head_mask(h, 2 * WIDE).astype(BF16)


def score_tiles(s, rows, region):
    tiles = [s[:, i * WIDE : (i + 1) * WIDE] for i in range(3)]
    if region is not None:
        return [t + region[rows, i * WIDE : (i + 1) * WIDE] for i, t in enumerate(tiles)]
    pad = jnp.where(iota((1, WIDE), 1) < VOX - 2 * WIDE, 0.0, -1e30)
    return tiles[:2] + [tiles[2] + pad]


def put_split(ref, rows, i, x):
    hi, lo = split(x)
    ref[rows, i * WIDE : (i + 1) * WIDE] = hi
    ref[rows, KEYS + i * WIDE : KEYS + (i + 1) * WIDE] = lo


def attention(normed, layer, save, lse, mixed, sc, region=None):
    left, right, values = sc
    x = pair(normed)
    qkv = []
    for i in range(3):
        w = deep(layer[pl.ds(R_QKV + i, EMB, stride=3), :])
        y = fold(dot(x, weight_nn(w))) + layer[R_QKVB + i : R_QKVB + i + 1, :]
        if i == 0:
            y = y * (HDIM**-0.5 * LOG2E)
        save[:, i * WIDE : (i + 1) * WIDE] = y
        qkv.append(y)
    for g, part in enumerate(as_left(qkv[0])):
        left[g] = part
    for g, part in enumerate(as_right(qkv[1])):
        right[g] = part
    v = jnp.where(iota((ROWS, WIDE), 1) == EMB, 1.0, qkv[2])
    v = pair(with_rows(v, KEYS))
    values[0:KEYS, :] = v
    values[KEYS : 2 * KEYS, :] = v
    mixed[...] = jnp.zeros_like(mixed)
    lse[...] = jnp.zeros_like(lse)

    def per_pair(pair_of, carry):
        heads = [2 * pair_of, 2 * pair_of + 1]
        masks = [head_mask(h, 2 * WIDE).astype(BF16) for h in heads]
        lanes = [own_lanes(h) for h in heads]
        spots = [jnp.where(iota((1, WIDE), 1) == h, 1.0, 0.0) for h in heads]
        g = lax.div(pair_of, 2)
        for block in BLOCKS:
            rows = slice(*block)
            out = level = 0.0
            for k in range(2):
                s = dot_nt(left[g, rows, :] * masks[k], right[g])
                tiles = score_tiles(s, rows, region)
                top = jnp.maximum(jnp.maximum(tiles[0], tiles[1]), tiles[2])
                top = jnp.max(top, 1, keepdims=True)
                parts = [split(jnp.exp2(t - top)) for t in tiles]
                e = jnp.concatenate([p[0] for p in parts] + [p[1] for p in parts], 1)
                o = fold(dot(e, values[...]))
                total = o[:, EMB : EMB + 1]
                out = out + o * (lanes[k] / total)
                level = level + (top + jnp.log(total) * LOG2E) * spots[k]
            mixed[rows, :] += out
            lse[rows, :] += level
        return carry

    lax.fori_loop(0, HEADS // 2, per_pair, 0)
    proj = deep(layer[R_PROJ : R_PROJ + EMB, :])
    return mm(mixed[...], proj) + layer[R_PROJB : R_PROJB + 1, :]


def attention_back(grad, normed, layer, save, lse, mixed, sc, grads, at, region=None):
    left, right, gleft, vright, keys, dq, dkv_t, weights, slopes = sc[:9]
    q_t, do_t, dmix, s, dp, two_keys, two_values = sc[9:]
    proj = deep(layer[R_PROJ : R_PROJ + EMB, :])
    grads[at + R_PROJ : at + R_PROJ + EMB, :] = mm_tn(rows_t(mixed[...]), grad)[:EMB]
    grads[at + R_PROJB : at + R_PROJB + 1, :] = colsum(grad)
    d_mixed = mm_nt(grad, proj)
    dmix[...] = d_mixed * mixed[...]
    q, k, v = (save[:, i * WIDE : (i + 1) * WIDE] for i in range(3))
    for g, part in enumerate(as_left(q)):
        left[g] = part
    for g, part in enumerate(as_right(k)):
        right[g] = part
    for g, part in enumerate(as_left(d_mixed)):
        gleft[g] = part
    for g, part in enumerate(as_right(v)):
        vright[g] = part
    kk = pair(with_rows(k, KEYS))
    keys[0:KEYS, :] = kk
    keys[KEYS : 2 * KEYS, :] = kk
    weights[:, ROWS:, :] = jnp.zeros((2, KEYS - ROWS, 2 * KEYS), BF16)
    slopes[:, ROWS:, :] = jnp.zeros((2, KEYS - ROWS, 2 * KEYS), BF16)
    for ref, x in ((q_t, q), (do_t, d_mixed)):
        hi, lo = split(with_rows(x, KEYS).T)
        ref[0] = hi
        ref[1] = lo
    dq[...] = jnp.zeros_like(dq)
    dkv_t[...] = jnp.zeros_like(dkv_t)

    def per_pair(pair_of, carry):
        g = lax.div(pair_of, 2)
        heads = [2 * pair_of, 2 * pair_of + 1]
        both_heads(right[g], heads, two_keys)
        both_heads(vright[g], heads, two_values)
        s[...] = dot_nt(left[g], two_keys[...])
        dp[...] = dot_nt(gleft[g], two_values[...])
        for k in range(2):
            h = 2 * pair_of + k
            lanes = own_lanes(h)
            at_h = jnp.where(iota((1, WIDE), 1) == h, 1.0, 0.0)
            for block in BLOCKS:
                rows = slice(*block)
                level = jnp.sum(lse[rows, :] * at_h, 1, keepdims=True)
                delta = jnp.sum(dmix[rows, :] * lanes, 1, keepdims=True)
                at_k = k * KEYS
                tiles = score_tiles(s[rows, at_k : at_k + KEYS], rows, region)
                for i, t in enumerate(tiles):
                    p = jnp.exp2(t - level)
                    put_split(weights.at[k], rows, i, p)
                    low = at_k + i * WIDE
                    p = p * (dp[rows, low : low + WIDE] - delta)
                    put_split(slopes.at[k], rows, i, p)
        total = 0.0
        for k in range(2):
            out = fold(dot(slopes[k, 0:ROWS, :], keys[...]))
            total = total + out * own_lanes(2 * pair_of + k)
        dq[...] += total
        for k in range(2):
            here = pl.ds(pl.multiple_of((2 * pair_of + k) * HDIM, HDIM), HDIM)
            for i, (t, m) in enumerate(((q_t, slopes), (do_t, weights))):
                lhs = jnp.concatenate([t[0, here, :], t[1, here, :]], 0)
                dkv_t[i, here, :] = fold_rows(fold(dot(lhs, m[k])))
        return carry

    lax.fori_loop(0, HEADS // 2, per_pair, 0)
    d_q = dq[...] * HDIM**-0.5
    d_k = dkv_t[0].T[0:ROWS] * (1.0 / LOG2E)
    d_v = dkv_t[1].T[0:ROWS]
    x_t = rows_t(normed)
    d_normed = None
    for i, d in enumerate((d_q, d_k, d_v)):
        grads[pl.ds(at + R_QKV + i, EMB, stride=3), :] = mm_tn(x_t, d)[:EMB]
        grads[at + R_QKVB + i : at + R_QKVB + i + 1, :] = colsum(d)
        part = mm_nt(d, deep(layer[pl.ds(R_QKV + i, EMB, stride=3), :]))
        d_normed = part if d_normed is None else d_normed + part
    return d_normed


def mlp(middle, layer, hpre):
    normed = norm(middle, layer[2:3, :], layer[3:4, :])
    w = deep(hidden_rows(layer, R_HID, EMB))
    pre = mm(normed, w) + hidden_rows(layer, R_HIDB, 1)
    hpre[...] = pre
    out = mm(gelu(pre), layer[R_OUT : R_OUT + HID, :])
    return middle + out + layer[R_OUTB : R_OUTB + 1, :]


def mlp_back(grad, middle, hpre, layer, grads, at):
    hat, inv = norm_stats(middle)
    normed = hat * layer[2:3, :] + layer[3:4, :]
    act, slope = gelu_both(hpre[...])
    grads[at + R_OUTB : at + R_OUTB + 1, :] = colsum(grad)
    grads[at + R_OUT : at + R_OUT + HID, :] = mm_tn(rows_t(grad), act).T
    d_pre = mm_nt(grad, layer[R_OUT : R_OUT + HID, :]) * slope
    put_hidden_rows(grads, at + R_HIDB, 1, colsum(d_pre))
    put_hidden_rows(grads, at + R_HID, EMB, mm_tn(rows_t(normed), d_pre)[:EMB])
    d_normed = mm_nt(d_pre, deep(hidden_rows(layer, R_HID, EMB)))
    grads[at + 2 : at + 3, :] = colsum(d_normed * hat)
    grads[at + 3 : at + 4, :] = colsum(d_normed)
    return grad + norm_back(hat, inv, layer[2:3, :], d_normed)


def pre_norm_back(grad, tokens, layer, grads, at):
    hat, inv = norm_stats(tokens)
    grads[at : at + 1, :] = colsum(grad * hat)
    grads[at + 1 : at + 2, :] = colsum(grad)
    return norm_back(hat, inv, layer[0:1, :], grad)


def region_of(rows, sizes):
    d = lax.shift_right_logical(rows * 1338, 16)
    line = lax.shift_right_logical(rows * 9363, 16)
    places = (d, line - d * WIN, rows - line * WIN)
    starts = (lax.axis_index("slab") * WIN, lax.axis_index("mp") * WIN, 0)
    total = None
    for place, start, blocks in zip(places, starts, sizes + (1,)):
        turned = jnp.where(place < SHIFT, place + FAR, place - SHIFT) + start
        length = WIN * blocks
        part = jnp.where(turned < length - WIN, 0, jnp.where(turned < length - SHIFT, 1, 2))
        total = part if total is None else total * 3 + part
    return total


def put_region(region, sizes):
    rows = region_of(iota((ROWS, WIDE), 0), sizes)[:, 0:1]
    lanes = region_of(iota((8, KEYS), 1), sizes)[0:1, :]
    apart = jnp.where(rows == lanes, 0.0, -100.0 * LOG2E)
    region[...] = jnp.where(iota((ROWS, KEYS), 1) < VOX, apart, -1e30)


def send_parts(ref, a, b, c):
    far = FAR * WIN
    near = SHIFT * WIN
    for d in range(SHIFT):
        base = d * PLANE
        c[d * near : (d + 1) * near, :] = ref[base : base + near, :]
        a[d * far : (d + 1) * far, :] = ref[base + near : base + PLANE, :]
    for d in range(FAR):
        base = (d + SHIFT) * PLANE
        b[d * near : (d + 1) * near, :] = ref[base : base + near, :]


def take_parts(own, a, b, c, out):
    far = FAR * WIN
    near = SHIFT * WIN
    for d in range(WIN):
        base = d * PLANE
        if d < SHIFT:
            out[base : base + near, :] = c[d * near : (d + 1) * near, :]
            out[base + near : base + PLANE, :] = a[d * far : (d + 1) * far, :]
        else:
            e = d - SHIFT
            out[base : base + near, :] = b[e * near : (e + 1) * near, :]
            out[base + near : base + PLANE, :] = own[base + near : base + PLANE, :]
    out[VOX:, :] = jnp.zeros((ROWS - VOX, WIDE), F32)


def span_of(groups):
    low, high = groups
    first = 3 * low // 8 * 8
    last = -(-3 * high // 8) * 8
    return first, min(last, NPARAM // WIDE // 8 * 8) - first


def copied(params, groups, flat, sem):
    first, rows = span_of(groups)
    size = rows * WIDE
    return pltpu.make_async_copy(
        params.at[pl.ds(first * WIDE, size)], flat.at[pl.ds(0, size)], sem
    )


def relay(groups, flat, out, square, last=None):
    low, high = groups
    first, rows = span_of(groups)
    square[0:rows, :] = flat[0 : rows * WIDE].reshape(rows, WIDE)
    if last is not None:
        square[rows : rows + 24, :] = jnp.zeros((24, WIDE), F32)
        square[rows : rows + 1, 0 : last.shape[0]] = last[...].reshape(1, last.shape[0])
    skip = 3 * low - first
    n = high - low
    parts = three_to_four([square[pl.ds(skip + c, n, stride=3), :] for c in range(3)])
    for c in range(4):
        out[pl.ds(c, n, stride=4), :] = parts[c]


FIRST_SPANS = ((0, 98), (98, 392))
LAYER_SPANS = ((389, 681), (680, 972))
CONV_SPANS = ((971, 1620), (1620, GROUPS))


def prep_kernel(spans, params, *refs, last=None):
    outs, (flats, square, sems) = refs[: len(spans)], refs[-3:]
    for i, groups in enumerate(spans):
        copied(params, groups, flats[i], sems.at[i]).start()
    for i, groups in enumerate(spans):
        copied(params, groups, flats[i], sems.at[i]).wait()
        relay(groups, flats[i], outs[i], square, last if i == len(spans) - 1 else None)


def head_picks():
    width = HEAD_ROWS * WIDE
    place = iota((WIDE, width), 1) - HEAD_LANE
    row = iota((WIDE, width), 0)
    here = (place >= row * CLASSES) & (place < (row + 1) * CLASSES) & (row <= EMB)
    place = iota((width, WIDE), 0) - HEAD_LANE
    col = iota((width, WIDE), 1)
    row = lax.shift_right_logical(place * 4682, 16)
    there = (place - row * CLASSES == col) & (place >= 0)
    return jnp.where(here, 1.0, 0.0), jnp.where(there, 1.0, 0.0).astype(BF16)


def prep_conv0_kernel(params, conv0, weights0, bias, *scratch):
    prep_kernel(CONV_SPANS[:1], params, conv0, *scratch)
    tap_weights(conv0, 3, weights0)
    bias[0:1, :] = conv0[3 + TAP_ROWS : 4 + TAP_ROWS, :]
    bias[1:8, :] = jnp.zeros((7, WIDE), F32)


def prep_conv1_kernel(last, bias, params, conv1, head, weights1, vectors, *scratch):
    prep_kernel(CONV_SPANS[1:], params, conv1, *scratch, last=last)
    tap_weights(conv1, 0, weights1)
    vectors[0:1, :] = bias[0:1, :]
    vectors[1:4, :] = conv1[TAP_ROWS : TAP_ROWS + 3, :]
    vectors[4:8, :] = jnp.zeros((4, WIDE), F32)
    square = scratch[1]
    first, _ = span_of(CONV_SPANS[1])
    row = jnp.concatenate(
        [square[HEAD_ROW + i - first : HEAD_ROW + i - first + 1, :] for i in range(HEAD_ROWS)], 1
    )
    here, there = head_picks()
    hi, lo = split(here * row)
    head[...] = dot(hi, there) + dot(lo, there)


def head_rows(d_head, out, at):
    here, there = head_picks()
    hi, lo = split(d_head)
    spread = (dot_nt(hi, there) + dot_nt(lo, there)) * here
    row = colsum(spread)
    for i in range(HEAD_ROWS):
        out[at + i : at + i + 1, :] += row[:, i * WIDE : (i + 1) * WIDE]


class Rows:
    def __init__(self, ref, at):
        self.ref, self.at = ref, at

    def __getitem__(self, key):
        rows, lanes = key
        if isinstance(rows, slice):
            rows = slice(rows.start + self.at, rows.stop + self.at)
        else:
            rows = pl.ds(rows.start + self.at, rows.size, stride=rows.stride)
        return self.ref[rows, lanes]


def merged_norm(x):
    mean = jnp.sum(x, 1, keepdims=True) * (1.0 / MERGE)
    centred = x - mean
    var = jnp.sum(centred * centred, 1, keepdims=True) * (1.0 / MERGE)
    return centred * lax.rsqrt(var + eps_norm)


def first_kernel(
    feats, merge, lay0,
    dense, tok0, save, lse, mixed, middle, hpre, tok1, ahead, pa, pb, pc,
    *sc,
):
    dense[VOX:, :] = jnp.zeros((ROWS - VOX, MERGE), F32)
    for line in range(PLANE):
        dense[line * WIN : (line + 1) * WIN, :] = feats[line]
    hat = merged_norm(dense[...])
    normed = hat * hidden_rows(merge, 0, 1) + hidden_rows(merge, 4, 1)
    tokens = mm(normed, merge[8 : 8 + MERGE, :])
    tok0[...] = tokens
    layer = Rows(lay0, 0)
    normed = norm(tokens, layer[0:1, :], layer[1:2, :])
    attended = attention(normed, layer, save, lse, mixed, sc)
    mid = tokens + attended
    middle[...] = mid
    tokens = mlp(mid, layer, hpre)
    tok1[...] = tokens
    ahead[...] = norm(tokens, layer[1165:1166, :], layer[1166:1167, :])
    send_parts(ahead, pa, pb, pc)


def shifted_kernel(
    sizes,
    own, pa, pb, pc, lay1, _,
    window, save, lse, mixed, out, qa, qb, qc,
    region, *sc,
):
    put_region(region, sizes)
    take_parts(own, pa, pb, pc, window)
    out[...] = attention(
        window[...], Rows(lay1, 1), save, lse, mixed, sc, region
    )
    send_parts(out, qa, qb, qc)


def to_lines(ref, out):
    for line in range(PLANE):
        out[line, 0:WIN, :] = ref[line * WIN : (line + 1) * WIN, :]
        out[line, WIN:8, :] = jnp.zeros((8 - WIN, WIDE), F32)


def from_lines(ref, out):
    out[VOX:, :] = jnp.zeros((ROWS - VOX, WIDE), F32)
    for line in range(PLANE):
        out[line * WIN : (line + 1) * WIN, :] = ref[line, 0:WIN, :]


def send_sides(lines, near_d, far_d, near_h, far_h):
    odd_d = jnp.bitwise_and(lax.axis_index("slab"), 1) == 1
    odd_h = jnp.bitwise_and(lax.axis_index("mp"), 1) == 1
    low, high = lines[0 : 2 * WIN], lines[(WIN - 2) * WIN : PLANE]
    near_d[...] = jnp.where(odd_d, low, high)
    far_d[...] = jnp.where(odd_d, high, low)
    for d in range(WIN):
        low = lines[d * WIN : d * WIN + 2]
        high = lines[d * WIN + WIN - 2 : (d + 1) * WIN]
        near_h[2 * d : 2 * d + 2] = jnp.where(odd_h, low, high)
        far_h[2 * d : 2 * d + 2] = jnp.where(odd_h, high, low)


def second_kernel(
    tok1, own, qa, qb, qc, lay1, lay2, _,
    mid1, hpre1, tok2, save, lse, mixed, mid2, hpre2, lines,
    s0, s1, s2, s3,
    attended, *sc,
):
    take_parts(own, qa, qb, qc, attended)
    mid = tok1[...] + attended[...]
    mid1[...] = mid
    tokens = mlp(mid, Rows(lay1, 1), hpre1)
    tok2[...] = tokens
    layer = Rows(lay2, 2)
    normed = norm(tokens, layer[0:1, :], layer[1:2, :])
    mid = tokens + attention(normed, layer, save, lse, mixed, sc)
    mid2[...] = mid
    attended[...] = mlp(mid, layer, hpre2)
    to_lines(attended, lines)
    send_sides(lines, s0, s1, s2, s3)


def grown_lines(sizes, own, near_d, far_d, near_h, far_h, out):
    slab, row = lax.axis_index("slab"), lax.axis_index("mp")
    odd_d = jnp.bitwise_and(slab, 1) == 1
    odd_h = jnp.bitwise_and(row, 1) == 1
    out[:, 11:12] = jnp.zeros((11, 1, 8, WIDE), F32)
    for d in range(WIN):
        out[d + 2, 2 : 2 + WIN] = own[d * WIN : (d + 1) * WIN]
    for d in range(2):
        near = near_d[d * WIN : (d + 1) * WIN]
        far = far_d[d * WIN : (d + 1) * WIN]
        out[d, 2 : 2 + WIN] = jnp.where(odd_d, near, jnp.where(slab == 0, 0.0, far))
        out[d + 9, 2 : 2 + WIN] = jnp.where(
            odd_d, jnp.where(slab == sizes[0] - 1, 0.0, far), near
        )
    for d in range(11):
        near = near_h[2 * d : 2 * d + 2]
        far = far_h[2 * d : 2 * d + 2]
        out[d, 0:2] = jnp.where(odd_h, near, jnp.where(row == 0, 0.0, far))
        out[d, 9:11] = jnp.where(odd_h, jnp.where(row == sizes[1] - 1, 0.0, far), near)


def put_marks(labels, valid, out):
    across = iota((8, WIN), 1) == iota((8, WIN), 0)
    classes = iota((8, WIDE), 1) - EMB
    for d in range(WIN):
        code = jnp.where(valid[d] == 1, labels[d], -1 - EMB - WIDE)
        code = code.astype(F32)
        for h in range(WIN):
            line = jnp.where(across, code[h : h + 1, :], 0.0)
            column = jnp.sum(line, 1, keepdims=True)
            mark = jnp.where(column == classes.astype(F32), 1.0, 0.0)
            out[d * WIN + h] = jnp.where(iota((8, WIDE), 0) < WIN, mark, 0.0)


def taps(source, first_plane, planes, first_line, lines, out):
    def per_plane(d, carry):
        for c in range(3):
            for b in range(3):
                x = source[d + first_plane, first_line + b : first_line + b + lines]
                if c != 1:
                    x = roll(x, 1 if c == 0 else 7, 1)
                x = pair(x.reshape(lines * 8, WIDE))
                at = pl.multiple_of(d * (lines * 8), lines * 8)
                t = b * 3 + c
                out[pl.ds(at, lines * 8), t * 256 : (t + 1) * 256] = x
        return carry

    lax.fori_loop(0, planes, per_plane, 0)


def tap_weights(ref, at, out):
    def per_tap(i, carry):
        w = deep(ref[pl.ds(i * EMB + at, EMB), :])
        out[pl.ds(pl.multiple_of(i * 256, 256), 256), :] = weight_nn(w)
        return carry

    lax.fori_loop(0, 27, per_tap, 0)


def tap_weights_back(ref, at, out):
    for i in range(27):
        w = deep(ref[(26 - i) * EMB + at : (27 - i) * EMB + at, :]).T
        out[i * 256 : (i + 1) * 256, :] = weight_nn(w)


def conv(side, weights, cuts, pitch, out):
    for start, end in zip(cuts, cuts[1:]):
        total = None
        for a in range(3):
            x = side[start + a * pitch : end + a * pitch, :]
            part = dot(x, weights[a * 2304 : (a + 1) * 2304, :])
            total = part if total is None else total + part
        out[start:end, :] = fold(total)


def conv_weight_grad(side, grad_rows, pitch, out, at):
    rows = 512
    g = jnp.concatenate([grad_rows, jnp.zeros((rows - grad_rows.shape[0], WIDE), F32)], 0)
    left = jnp.concatenate(split(g.T[:EMB]), 0)
    for a in range(3):
        for bc in range(9):
            y = dot(left, side[a * pitch : a * pitch + rows, bc * 256 : (bc + 1) * 256])
            y = deep(fold_rows(fold(y))).T
            t = a * 9 + bc
            out[at + t * EMB : at + (t + 1) * EMB, :] = y[:EMB]


def volume_mask(sizes, planes, lines, reach, real_lines):
    slab, row = lax.axis_index("slab"), lax.axis_index("mp")
    ends = (slab == 0, slab == sizes[0] - 1, row == 0, row == sizes[1] - 1)
    shape = (planes, lines, 8, WIDE)
    d, h, w = iota(shape, 0), iota(shape, 1), iota(shape, 2)
    low_d = jnp.where(ends[0], reach, 0)
    high_d = jnp.where(ends[1], planes - reach, planes)
    low_h = jnp.where(ends[2], reach, 0)
    high_h = jnp.where(ends[3], real_lines - reach, real_lines)
    inside = (d >= low_d) & (d < high_d) & (h >= low_h) & (h < high_h) & (w < WIN)
    return jnp.where(inside, 1.0, 0.0)


def conv_kernel(
    sizes,
    own, s0, s1, s2, s3, labels, valid, weights0, weights1, vectors, _,
    grown, pre, tok, stats, t0, t1, t2, t3,
    act, side, side_own, marks, result,
):
    grown_lines(sizes, own, s0, s1, s2, s3, grown)
    put_marks(labels, valid, marks)
    taps(grown, 0, 11, 0, 10, side)
    bias0 = vectors[0:1, :]
    inside = volume_mask(sizes, 9, 10, 1, 9)

    conv(side, weights0, (0, 176, 352, 528, 720), 80, result)
    z = (result[...] + bias0).reshape(9, 10, 8, WIDE)
    pre[...] = z
    act[...] = gelu(z) * inside
    taps(act, 0, 9, 0, 8, side_own)
    bias1 = vectors[1:2, :]
    conv(side_own, weights1, (0, 224, 448), 64, result)
    y = (result[0 : WIN * 64, :] + bias1).reshape(WIN, 8, 8, WIDE)[:, 0:WIN]
    y = y + own[...].reshape(WIN, WIN, 8, WIDE)
    y = jnp.where(iota(y.shape, 2) < WIN, y, 0.0).reshape(PLANE, 8, WIDE)
    tok[...] = y + marks[...]
    send_sides(tok, t0, t1, t2, t3)
    flat = y.reshape(PLANE * 8, WIDE)
    count = jnp.sum(marks[...].reshape(PLANE * 8, WIDE))
    row = iota((8, WIDE), 0)
    stats[...] = (
        jnp.where(row == 0, colsum(flat), 0.0)
        + jnp.where(row == 1, colsum(flat * flat), 0.0)
        + jnp.where(row == 2, count, 0.0)
    )


def head_kernel(
    sizes, voxels,
    own, s0, s1, s2, s3, sums, vectors, head_w,
    grown, slope_out, stats, d_head, d_rows,
):
    grown_lines(sizes, own, s0, s1, s2, s3, grown)
    rows = 11 * 12 * 8
    both = grown[...].reshape(rows, WIDE)
    lane = iota((rows, WIDE), 1)
    tokens = jnp.where(lane < EMB, both, 0.0)
    target = jnp.where(lane < CLASSES, roll(both, WIDE - EMB, 1), 0.0)
    live = jnp.sum(target, 1, keepdims=True)
    count = F32(voxels)
    average = sums[0:1, :] / count
    spread = sums[1:2, :] / count - average * average
    inv = lax.rsqrt(spread + eps_norm)
    gain = vectors[2:3, :]
    bias = vectors[3:4, :]
    hat = (tokens - average) * inv
    act, slope = gelu_both(hat * gain + bias)
    act = jnp.where(lane == EMB, 1.0, act)
    w = head_w[...]
    logits = mm(act, w)
    logits = jnp.where(lane < CLASSES, logits, -1e30)
    top = jnp.max(logits, 1, keepdims=True)
    e = jnp.exp(logits - top)
    total = jnp.sum(e, 1, keepdims=True)
    logp = logits - top - jnp.log(total)
    scale = 1.0 / sums[2:3, 0:1]
    d_logits = (e / total * live - target) * scale
    d_normed = jnp.where(lane < EMB, mm_nt(d_logits, w) * slope, 0.0)
    d_tokens = d_normed * gain * inv
    slope_out[...] = d_tokens.reshape(11, 12, 8, WIDE)

    def own_rows(x):
        x = x.reshape(11, 12, 8, WIDE)[2:9, 2:9]
        x = jnp.where(iota(x.shape, 2) < WIN, x, 0.0)
        return x.reshape(PLANE * 8, WIDE)

    loss = -jnp.sum(own_rows(target * jnp.where(lane < CLASSES, logp, 0.0)))
    own_d = own_rows(d_logits)
    own_n = own_rows(d_normed)
    own_hat = own_rows(hat)
    zeros = jnp.zeros((512 - PLANE * 8, WIDE), F32)
    left = rows_t(jnp.concatenate([own_d, zeros], 0))
    d_head[...] = mm_tn(left, jnp.concatenate([own_rows(act), zeros], 0)).T
    d_gain = colsum(own_n * own_hat)
    d_bias = colsum(own_n)
    d_average = -d_bias * gain * inv
    d_spread = d_gain * gain * inv * inv * -0.5
    d_two = d_spread / count
    d_one = (d_average - 2.0 * average * d_spread) / count
    row = iota((8, WIDE), 0)
    live_lane = iota((8, WIDE), 1) < EMB
    stats[...] = (
        jnp.where((row == 0) & live_lane, d_one, 0.0)
        + jnp.where((row == 1) & live_lane, d_two, 0.0)
        + jnp.where(row == 2, loss, 0.0)
    )
    d_rows[...] = (
        jnp.where(row == 0, d_gain, 0.0)
        + jnp.where(row == 1, d_bias, 0.0)
    )


def sides_back_kernel(sizes, grown, pre, side_act, side_grown, act):
    act[0:9] = gelu(pre[...]) * volume_mask(sizes, 9, 10, 1, 9)
    act[9:10] = jnp.zeros((1, 10, 8, WIDE), F32)
    taps(act, 0, 10, 0, 8, side_act)
    taps(grown, 1, 10, 1, 8, side_grown)


def weights_back_kernel(conv0, conv1, weights0, weights1):
    tap_weights_back(conv0, 3, weights0)
    tap_weights_back(conv1, 0, weights1)


def conv_back_kernel(
    sizes,
    tok, slope, sums, pre, side_act, side_grown, weights0, weights1, d_rows, d_head,
    d_own, keep, send, carry, seam,
    grads, dgrown, act, side, side_own, flat, result,
):
    lane = iota((11, 12, 8, WIDE), 3)
    inside = volume_mask(sizes, 11, 12, 2, 11)
    steady = sums[0:1, :].reshape(1, 1, 1, WIDE)
    rising = 2.0 * sums[1:2, :].reshape(1, 1, 1, WIDE)
    d_tok = slope[...] + jnp.where(lane < EMB, (steady + tok[...] * rising) * inside, 0.0)
    dgrown[...] = d_tok
    grads[5191:, :] = jnp.zeros((45, WIDE), F32)
    grads[0:8, :] = jnp.zeros((8, WIDE), F32)
    grads[5189:5191, :] = d_rows[0:2, :]
    own = dgrown[2:9, 2:10]
    line = iota(own.shape, 1)
    own = jnp.where(line < WIN, own, 0.0).reshape(WIN * 64, WIDE)
    grads[5188:5189, :] = colsum(own)

    near = volume_mask(sizes, 9, 10, 1, 9)
    conv_weight_grad(side_act, own, 64, grads, 2596)
    taps(dgrown, 0, 11, 0, 10, side)

    conv(side, weights1, (0, 176, 352, 528, 720), 80, result)
    act[0:9] = result[...].reshape(9, 10, 8, WIDE) * gelu_both(pre[...])[1] * near

    own = act[1:8, 1:9]
    line = iota(own.shape, 1)
    own = jnp.where(line < WIN, own, 0.0).reshape(WIN * 64, WIDE)
    grads[2595:2596, :] = colsum(own)
    conv_weight_grad(side_grown, own, 64, grads, 3)
    carry[...] = grads[0:24, :]
    flat[3 * (GROUPS - CUTS[3]) :, :] = jnp.zeros((flat.shape[0] - 3912, WIDE), F32)
    flatten(grads, 20, GROUPS - CUTS[3], flat)
    start = 3 * CUTS[3]
    head_rows(d_head[...], flat, HEAD_ROW - start)
    seam[...] = flat[0 : LATE_ROWS - start, :]
    scatter(sizes, flat, LATE_ROWS - start, keep, send)
    taps(act, 0, 9, 0, 8, side_own)
    conv(side_own, weights0, (0, 224, 448), 64, result)
    y = result[0 : WIN * 64, :].reshape(WIN, 8, 8, WIDE)[:, 0:WIN] + dgrown[2:9, 2:9]
    y = jnp.where(iota(y.shape, 2) < WIN, y, 0.0)
    d_own[...] = y.reshape(PLANE, 8, WIDE)


def back_mlp_kernel(d_own, lay2, mid2, hpre2, d_mid, grads, dense):
    from_lines(d_own, dense)
    grads[...] = jnp.zeros_like(grads)
    d_mid[...] = mlp_back(dense[...], mid2[...], hpre2, Rows(lay2, 2), grads, 2)


def back_two_kernel(
    d_mid2, grads2, carry, lay1, lay2, tok2, save, lse, mixed, mid1, hpre1,
    d_mid, grads1, flat, carry2, pa, pb, pc,
    grads, *sc,
):
    layer = Rows(lay2, 2)
    grads[0:1168, :] = grads2[...]
    d = d_mid2[...]
    tokens = tok2[...]
    normed = norm(tokens, layer[0:1, :], layer[1:2, :])
    d_normed = attention_back(d, normed, layer, save, lse, mixed, sc, grads, 2)
    d = d + pre_norm_back(d_normed, tokens, layer, grads, 2)
    grads[1167:1184, :] = carry[3:20, :]
    flatten(grads, 32, CUTS[3] - CUTS[2], flat)
    carry2[...] = grads[0:32, :]
    layer = Rows(lay1, 1)
    d = mlp_back(d, mid1[...], hpre1, layer, grads1, 1)
    d_mid[...] = d
    send_parts(d_mid, pa, pb, pc)


def back_shifted_kernel(
    sizes,
    own, pa, pb, pc, lay1, window, save, lse, mixed, grads1, carry2, _,
    d_window, flat, carry1, qa, qb, qc,
    region, grads, grad, *sc,
):
    put_region(region, sizes)
    take_parts(own, pa, pb, pc, grad)
    grads[0:1168, :] = grads1[...]
    grads[0:3, :] = jnp.zeros((3, WIDE), F32)
    d_window[...] = attention_back(
        grad[...], window[...], Rows(lay1, 1), save, lse, mixed, sc, grads, 1,
        region,
    )
    send_parts(d_window, qa, qb, qc)
    grads[1166:1196, :] = carry2[2:32, :]
    flatten(grads, 12, CUTS[2] - CUTS[1], flat)
    carry1[...] = grads[0:16, :]


def back_first_kernel(
    sizes,
    d_mid, own, qa, qb, qc, tok1, lay0, lay1, merge, dense, tok0, save, lse, mixed, middle, hpre,
    carry1, flat1, flat2, seam, _,
    keep, send,
    flat, grads, grad, *sc,
):
    take_parts(own, qa, qb, qc, grad)
    grads[1556:1572, :] = carry1[...]
    d = d_mid[...] + pre_norm_back(grad[...], tok1[...], Rows(lay1, 1), grads, 1557)
    layer = Rows(lay0, 0)
    at = MERGE_ROWS
    d = mlp_back(d, middle[...], hpre, layer, grads, at)
    tokens = tok0[...]
    normed = norm(tokens, layer[0:1, :], layer[1:2, :])
    d_normed = attention_back(d, normed, layer, save, lse, mixed, sc, grads, at)
    d = d + pre_norm_back(d_normed, tokens, layer, grads, at)
    live = iota((ROWS, WIDE), 0) < VOX
    d = jnp.where(live, d, 0.0)
    hat = merged_norm(dense[...])
    gain = hidden_rows(merge, 0, 1)
    bias = hidden_rows(merge, 4, 1)
    w = merge[8 : 8 + MERGE, :]
    put_hidden_rows(grads, 8 - 8, 1, jnp.zeros((1, MERGE), F32))
    grads[8 : 8 + MERGE, :] = mm_tn(rows_t(d), hat * gain + bias).T
    d_hat = mm_nt(d, w)
    put_hidden_rows(grads, 0, 1, colsum(d_hat * hat))
    put_hidden_rows(grads, 4, 1, colsum(d_hat))
    flatten(grads, 0, CUTS[1], flat)
    at = 0
    for cut, part in ((CUTS[1], flat1), (CUTS[2], flat2), (CUTS[3], seam)):
        at = 3 * cut
        flat[at : at + part.shape[0], :] = part[...]
    at += seam.shape[0]
    if flat.shape[0] > at:
        flat[at:, :] = jnp.zeros((flat.shape[0] - at, WIDE), F32)
    scatter(sizes, flat, 0, keep, send)


def radices(count):
    steps = [2]
    left = count // 2
    while left > 1:
        steps.append(4 if left >= 4 else 2)
        left //= steps[-1]
    return steps


def block_rows(rows, count):
    return -(-rows // (8 * count)) * 8


def own_number(sizes):
    return lax.axis_index("slab") * sizes[1] + lax.axis_index("mp")


def place_in_half(distance, count):
    place = 0
    shift = 1
    for radix in radices(count)[1:]:
        digit = jnp.bitwise_and(lax.shift_right_logical(distance, shift), radix - 1)
        place = place * radix + digit
        shift += radix.bit_length() - 1
    return place


def scatter(sizes, source, first, keep, send):
    count = sizes[0] * sizes[1]
    rows = keep.shape[0] * 2 // count
    me = own_number(sizes)
    odd = jnp.bitwise_and(me, 1)

    def per_pair(t, carry):
        for block, out in ((2 * t + odd, keep), (2 * t + 1 - odd, send)):
            place = place_in_half(jnp.bitwise_xor(block, me), count)
            at = pl.multiple_of(first + block * rows, 8)
            to = pl.multiple_of(place * rows, 8)
            out[pl.ds(to, rows), :] = source[pl.ds(at, rows), :]
        return carry

    lax.fori_loop(0, count // 2, per_pair, 0)


def traded(value, distance, count):
    pairs = [(i, i ^ distance) for i in range(count)]
    return lax.ppermute(value, ("slab", "mp"), pairs)


def later(got, after):
    return got if after is None else list(lax.optimization_barrier((*got, after)))[:-1]


def summing(keep, send, count):
    steps = radices(count)
    got = [keep, traded(send, 1, count)]
    shift = 1
    after = yield None
    for radix in steps[1:]:
        got = later(got, after)
        total = sum(got[1:], got[0])
        rows = total.shape[0] // radix
        parts = [total[k * rows : (k + 1) * rows] for k in range(radix)]
        got = parts[:1] + [traded(parts[k], k << shift, count) for k in range(1, radix)]
        shift += radix.bit_length() - 1
        after = yield parts[0]
    got = later(got, after)
    own = sum(got[1:], got[0])
    for radix in reversed(steps[1:]):
        shift -= radix.bit_length() - 1
        got = [own] + [traded(own, k << shift, count) for k in range(1, radix)]
        after = yield own
        own = jnp.concatenate(later(got, after), 0)
        yield own
    yield own, traded(own, 1, count)


def finished(chain, after=None):
    last = next(chain) if after is None else chain.send(after)
    while not isinstance(last, tuple):
        last = next(chain)
    return last


def exchanged_sum(value, count):
    shift = 0
    for radix in radices(count):
        got = [value] + [traded(value, k << shift, count) for k in range(1, radix)]
        while len(got) > 1:
            got = [got[i] + got[i + 1] for i in range(0, len(got), 2)]
        value = got[0]
        shift += radix.bit_length() - 1
    return value


PIECE = 294912


def place_blocks(sizes, own, other, out, size):
    count = sizes[0] * sizes[1]
    me = own_number(sizes)
    rows = own.shape[0] * 2 // count

    def per_block(block, carry):
        distance = jnp.bitwise_xor(block, me)
        at = pl.ds(pl.multiple_of(place_in_half(distance, count) * rows, 8), rows)
        near = jnp.bitwise_and(distance, 1) == 0
        to = pl.ds(pl.multiple_of(block * rows, 8), rows)
        out[to, :] = jnp.where(near, own[at, :], other[at, :])
        return carry

    lax.fori_loop(0, size // rows, per_block, 0)


def squares(*refs):
    total = jnp.zeros((8, WIDE), F32)
    for ref in refs:
        x = ref[...]
        total = total + jnp.sum((x * x).reshape(-1, 8, WIDE), 0)
    return total


def place_early_kernel(sizes, own, other, out, square):
    place_blocks(sizes, own, other, out, EARLY_ROWS)
    square[...] = squares(own, other)


def adamw_kernel(
    sizes,
    late, late_other, early, square, tail, sums, params, first, second,
    new_params, new_first, new_second, loss, valid, norm_out,
    grad, scale_ref,
):
    step = pl.program_id(0)

    @pl.when(step == 0)
    def gather():
        norm = jnp.sqrt(jnp.sum(squares(late, late_other) + square[...]))
        loss[0] = jnp.sum(tail[2:3, 0:1])
        valid[0] = jnp.sum(sums[2:3, 0:1])
        norm_out[0] = norm
        scale_ref[0] = jnp.minimum(1.0, clip_norm / (norm + 1e-06))
        place_blocks(sizes, late, late_other, grad, LATE_ROWS)
        grad[LATE_ROWS:, :] = early[...]

    def update(base, low, size):
        rows = -(-size // 1024) * 8
        at = pl.ds(pl.multiple_of(base // WIDE + low // WIDE, 8), rows)
        g = grad[at, :].reshape(rows * WIDE)[:size] * scale_ref[0]
        here = pl.ds(pl.multiple_of(base + low, 1024), size)
        one = beta_one * first[here] + (1.0 - beta_one) * g
        two = beta_two * second[here] + (1.0 - beta_two) * g * g
        there = pl.ds(low, size)
        new_first[there] = one
        new_second[there] = two
        two = two * (1.0 / (1.0 - beta_two**STEP))
        low_by = two * lax.rsqrt(jnp.maximum(two, 1e-37)) + adam_eps
        inverse = pl.reciprocal(low_by, approx=True)
        inverse = inverse * (2.0 - low_by * inverse)
        new_params[there] = params[here] * (1.0 - learn_rate * decay_rate) - (
            one * (learn_rate / (1.0 - beta_one**STEP))
        ) * inverse

    whole = NPARAM // PIECE

    @pl.when(step < whole)
    def full():
        def part(i, carry):
            low = pl.multiple_of(i * 16384, 16384)
            update(step * PIECE, low, 16384)
            return carry

        lax.fori_loop(0, PIECE // 16384, part, 0)

    @pl.when(step == whole)
    def last():
        rest = NPARAM - whole * PIECE
        main = rest // 1024 * 1024
        for low in range(0, main, 16384):
            update(whole * PIECE, low, min(16384, main - low))
        update(whole * PIECE, main, rest - main)


def adamw(sizes, parts, arrays):
    pieces = -(-NPARAM // PIECE)
    piece = pl.BlockSpec((PIECE,), lambda i: (i,))
    vmem = pl.BlockSpec(memory_space=pltpu.VMEM)
    smem = pl.BlockSpec(memory_space=pltpu.SMEM)
    return pl.pallas_call(
        functools.partial(adamw_kernel, sizes),
        grid=(pieces,),
        out_shape=[arr(NPARAM)] * 3 + [arr(1)] * 3,
        in_specs=[vmem] * (len(parts) + len(arrays)),
        out_specs=[piece] * 3 + [smem] * 3,
        scratch_shapes=[pltpu.VMEM((LATE_ROWS + EARLY_ROWS, WIDE), F32), pltpu.SMEM((1,), F32)],
        compiler_params=pltpu.CompilerParams(vmem_limit_bytes=16 * 1024 * 1024),
        cost_estimate=pl.CostEstimate(flops=6 * 10**9, bytes_accessed=0, transcendentals=0),
        name="adamw",
    )(*parts, *arrays)


def arr(*shape):
    return jax.ShapeDtypeStruct(shape, F32)


def call(kernel, outs, scratch, *args, name=None, us=1.0, far=(), mib=16):
    vmem = pl.BlockSpec(memory_space=pltpu.VMEM)
    smem = pl.BlockSpec(memory_space=pltpu.SMEM)
    return pl.pallas_call(
        kernel,
        out_shape=list(outs),
        in_specs=[vmem] * len(args) + [pl.BlockSpec(memory_space=pl.ANY)] * len(far),
        out_specs=[smem if o.shape == (1,) else vmem for o in outs],
        scratch_shapes=list(scratch),
        compiler_params=pltpu.CompilerParams(vmem_limit_bytes=mib * 1024 * 1024),
        cost_estimate=pl.CostEstimate(
            flops=int(us * 1.15e9), bytes_accessed=0, transcendentals=0
        ),
        name=name,
    )(*args, *far)


SQUARE = arr(ROWS, WIDE)
SAVE = arr(ROWS, 3 * WIDE)
FORWARD = [
    pltpu.VMEM((2, ROWS, 2 * WIDE), BF16),
    pltpu.VMEM((2, KEYS, 2 * WIDE), BF16),
    pltpu.VMEM((2 * KEYS, 2 * WIDE), BF16),
]
BACKWARD = [
    pltpu.VMEM((2, ROWS, 2 * WIDE), BF16),
    pltpu.VMEM((2, KEYS, 2 * WIDE), BF16),
    pltpu.VMEM((2, ROWS, 2 * WIDE), BF16),
    pltpu.VMEM((2, KEYS, 2 * WIDE), BF16),
    pltpu.VMEM((2 * KEYS, 2 * WIDE), BF16),
    pltpu.VMEM((ROWS, WIDE), F32),
    pltpu.VMEM((2, WIDE, KEYS), F32),
    pltpu.VMEM((2, KEYS, 2 * KEYS), BF16),
    pltpu.VMEM((2, KEYS, 2 * KEYS), BF16),
    pltpu.VMEM((2, WIDE, KEYS), BF16),
    pltpu.VMEM((2, WIDE, KEYS), BF16),
    pltpu.VMEM((ROWS, WIDE), F32),
    pltpu.VMEM((ROWS, 2 * KEYS), F32),
    pltpu.VMEM((ROWS, 2 * KEYS), F32),
    pltpu.VMEM((2 * KEYS, 2 * WIDE), BF16),
    pltpu.VMEM((2 * KEYS, 2 * WIDE), BF16),
]
PARTS = [arr(ROWS_A, WIDE), arr(ROWS_B, WIDE), arr(ROWS_C, WIDE)]


def passed(parts, steps, sizes):
    slabs, rows = sizes
    moved = []
    for part, (ds, dm) in zip(parts, ((1, 0), (0, 1), (1, 1))):
        pairs = []
        for s in range(slabs):
            for m in range(rows):
                target = ((s + steps * ds) % slabs) * rows + (m + steps * dm) % rows
                pairs.append((s * rows + m, target))
        moved.append(lax.ppermute(part, ("slab", "mp"), pairs))
    return moved


SIDES = [arr(2 * WIN, 8, WIDE)] * 4


def paired(axis, size):
    near = [(i, i ^ 1) for i in range(size)]
    far = [(i, (i + (1 if i % 2 else -1)) % size) for i in range(size)]
    return (
        lambda value: lax.ppermute(value, axis, near),
        lambda value: lax.ppermute(value, axis, far),
    )


def column_kernel(sizes, near_d, far_d, near_h, far_h, near_out, far_out):
    slab = lax.axis_index("slab")
    odd_d = jnp.bitwise_and(slab, 1) == 1
    odd_h = jnp.bitwise_and(lax.axis_index("mp"), 1) == 1
    at_low = slab == 0
    at_high = slab == sizes[0] - 1
    near_out[4:18] = near_h[...]
    far_out[4:18] = far_h[...]
    for d in range(2):
        near = near_d[d * WIN : (d + 1) * WIN]
        far = far_d[d * WIN : (d + 1) * WIN]
        before = jnp.where(odd_d, near, jnp.where(at_low, 0.0, far))
        after = jnp.where(odd_d, jnp.where(at_high, 0.0, far), near)
        for x, at in ((before, 2 * d), (after, 18 + 2 * d)):
            low, high = x[0:2], x[WIN - 2 : WIN]
            near_out[at : at + 2] = jnp.where(odd_h, low, high)
            far_out[at : at + 2] = jnp.where(odd_h, high, low)


def beside(sides, sizes):
    near, far = paired("slab", sizes[0])
    near_d, far_d = near(sides[0]), far(sides[1])
    near_h, far_h = call(
        functools.partial(column_kernel, sizes), [arr(22, 8, WIDE)] * 2, [],
        near_d, far_d, sides[2], sides[3],
        name="column", us=0.3,
    )
    near, far = paired("mp", sizes[1])
    return near_d, far_d, near(near_h), far(far_h)


REGION = [pltpu.VMEM((ROWS, KEYS), F32)]


def on_device(sizes, feats, labels, valid, params, moment_one, moment_two):
    slabs, rows = sizes
    count = slabs * rows

    def room(spans):
        sizes = [(span_of(groups)[1] + 8) * WIDE for groups in spans]
        return [
            [pltpu.VMEM((size,), F32) for size in sizes],
            pltpu.VMEM((2048, WIDE), F32),
            pltpu.SemaphoreType.DMA((len(spans),)),
        ]

    first_size = FIRST_SPANS[-1][1] * 384
    merge, lay0 = call(
        functools.partial(prep_kernel, FIRST_SPANS),
        [arr(MERGE_ROWS, WIDE), arr(1176, WIDE)],
        room(FIRST_SPANS),
        name="prep_first", us=2.0, far=(params[:first_size],),
    )
    lay1, lay2 = call(
        functools.partial(prep_kernel, LAYER_SPANS),
        [arr(1168, WIDE)] * 2,
        room(LAYER_SPANS),
        name="prep_layers", us=2.0, far=(params,),
    )
    taps_shape = jax.ShapeDtypeStruct((27 * 256, 256), BF16)
    conv0, weights0, bias0 = call(
        prep_conv0_kernel,
        [arr(2596, WIDE), taps_shape, arr(8, WIDE)],
        room(CONV_SPANS[:1]),
        name="prep_conv0", us=1.5, far=(params,),
    )
    conv1, head_w, weights1, vectors = call(
        prep_conv1_kernel,
        [arr(2640, WIDE), arr(WIDE, WIDE), taps_shape, arr(8, WIDE)],
        room(CONV_SPANS[1:]),
        params[NPARAM // WIDE * WIDE :], bias0,
        name="prep_conv1", us=1.5, far=(params,),
    )

    dense, tok0, save0, lse0, mixed0, mid0, hpre0, tok1, ahead, *parts = call(
        first_kernel,
        [arr(ROWS, MERGE), SQUARE, SAVE, SQUARE, SQUARE, SQUARE, arr(ROWS, HID), SQUARE, SQUARE]
        + PARTS,
        FORWARD,
        feats.reshape(PLANE, WIN, MERGE), merge, lay0,
        name="first", us=6.0,
    )
    parts = passed(parts, -1, sizes)
    window, save1, lse1, mixed1, out1, *parts = call(
        functools.partial(shifted_kernel, sizes),
        [SQUARE, SAVE, SQUARE, SQUARE, SQUARE] + PARTS,
        REGION + FORWARD,
        ahead, *parts, lay1,
        name="shifted", us=4.5, far=(weights0,),
    )
    parts = passed(parts, 1, sizes)
    mid1, hpre1, tok2, save2, lse2, mixed2, mid2, hpre2, lines, *sides = call(
        second_kernel,
        [SQUARE, arr(ROWS, HID), SQUARE, SAVE, SQUARE, SQUARE, SQUARE, arr(ROWS, HID)]
        + [arr(PLANE, 8, WIDE)] + SIDES,
        [pltpu.VMEM((ROWS, WIDE), F32)] + FORWARD,
        tok1, out1, *parts, lay1, lay2,
        name="second", us=6.5, far=(weights1,),
    )
    sides = beside(sides, sizes)
    back0, back1 = call(
        weights_back_kernel,
        [taps_shape] * 2,
        [],
        conv0, conv1,
        name="weights_back", us=1.5,
    )
    grown, pre, tok3, sums, *tok_sides = call(
        functools.partial(conv_kernel, sizes),
        [arr(11, 12, 8, WIDE), arr(9, 10, 8, WIDE), arr(PLANE, 8, WIDE), arr(8, WIDE)] + SIDES,
        [
            pltpu.VMEM((9, 10, 8, WIDE), F32),
            pltpu.VMEM((880, 2304), BF16),
            pltpu.VMEM((576, 2304), BF16),
            pltpu.VMEM((PLANE, 8, WIDE), F32),
            pltpu.VMEM((720, WIDE), F32),
        ],
        lines, *sides, labels, valid, weights0, weights1, vectors,
        name="conv", us=8.0, mib=20, far=(back0,),
    )
    tok_sides = beside(tok_sides, sizes)
    side_act, side_grown = call(
        functools.partial(sides_back_kernel, sizes),
        [jax.ShapeDtypeStruct((640, 2304), BF16)] * 2,
        [pltpu.VMEM((10, 10, 8, WIDE), F32)],
        grown, pre,
        name="sides_back", us=2.0,
    )
    sums = exchanged_sum(sums, count)
    voxels = WIN * slabs * WIN * rows * WIN
    tok3, slope, tail, d_head, d_rows = call(
        functools.partial(head_kernel, sizes, voxels),
        [arr(11, 12, 8, WIDE), arr(11, 12, 8, WIDE), arr(8, WIDE), arr(WIDE, WIDE), arr(8, WIDE)],
        [],
        tok3, *tok_sides, sums, vectors, head_w,
        name="head", us=3.5,
    )
    tail = exchanged_sum(tail, count)
    late_rows = block_rows(LATE_ROWS, count) * count
    early_rows = block_rows(EARLY_ROWS, count) * count
    seam_rows = LATE_ROWS - 3 * CUTS[3]
    d_own, keep, send, carry3, seam = call(
        functools.partial(conv_back_kernel, sizes),
        [arr(PLANE, 8, WIDE)] + [arr(early_rows // 2, WIDE)] * 2
        + [arr(24, WIDE), arr(seam_rows, WIDE)],
        [
            pltpu.VMEM((5236, WIDE), F32),
            pltpu.VMEM((11, 12, 8, WIDE), F32),
            pltpu.VMEM((10, 10, 8, WIDE), F32),
            pltpu.VMEM((880, 2304), BF16),
            pltpu.VMEM((576, 2304), BF16),
            pltpu.VMEM((seam_rows + early_rows, WIDE), F32),
            pltpu.VMEM((720, WIDE), F32),
        ],
        tok3, slope, tail, pre, side_act, side_grown, back0, back1, d_rows, d_head,
        name="conv_back", us=14.0, mib=28,
    )
    early = summing(keep, send, count)
    next(early)
    d_mid2, grads2 = call(
        back_mlp_kernel,
        [SQUARE, arr(1168, WIDE)],
        [pltpu.VMEM((ROWS, WIDE), F32)],
        d_own, lay2, mid2, hpre2,
        name="back_mlp", us=3.0,
    )
    step = early.send(d_mid2)
    d_mid, grads1, flat2, carry2, *parts = call(
        back_two_kernel,
        [SQUARE, arr(1168, WIDE), arr(3 * (CUTS[3] - CUTS[2]), WIDE), arr(32, WIDE)] + PARTS,
        [pltpu.VMEM((1184, WIDE), F32)] + BACKWARD,
        d_mid2, grads2, carry3, lay1, lay2, tok2, save2, lse2, mixed2, mid1, hpre1,
        name="back_two", us=9.0,
    )
    parts = passed(parts, -1, sizes)
    step = early.send(d_mid)
    d_window, flat1, carry1, *parts = call(
        functools.partial(back_shifted_kernel, sizes),
        [SQUARE, arr(3 * (CUTS[2] - CUTS[1]), WIDE), arr(16, WIDE)] + PARTS,
        REGION + [pltpu.VMEM((1200, WIDE), F32), pltpu.VMEM((ROWS, WIDE), F32)] + BACKWARD,
        d_mid, *parts, lay1, window, save1, lse1, mixed1, grads1, carry2,
        name="back_shifted", us=10.5, far=(step,),
    )
    early.send(d_window)
    parts = passed(parts, 1, sizes)
    next(early)
    step = next(early)
    late = call(
        functools.partial(back_first_kernel, sizes),
        [arr(late_rows // 2, WIDE)] * 2,
        [
            pltpu.VMEM((late_rows, WIDE), F32),
            pltpu.VMEM((1572, WIDE), F32),
            pltpu.VMEM((ROWS, WIDE), F32),
        ]
        + BACKWARD,
        d_mid, d_window, *parts, tok1, lay0, lay1, merge, dense, tok0, save0, lse0, mixed0, mid0,
        hpre0, carry1, flat1, flat2, seam,
        name="back_first", us=13.5, far=(step,),
    )
    step = early.send(late[0])
    keep, send = later(list(late), step)
    late_sum = finished(summing(keep, send, count))
    early = finished(early)
    early = call(
        functools.partial(place_early_kernel, sizes),
        [arr(EARLY_ROWS, WIDE), arr(8, WIDE)],
        [],
        *early,
        name="place_early", us=0.6,
    )
    new_params, new_first, new_second, loss, valid_count, norm = adamw(
        sizes, (*late_sum, *early, tail, sums), (params, moment_one, moment_two)
    )
    return (
        loss.reshape(()), valid_count.reshape(()), norm.reshape(()),
        new_params, new_first, new_second,
    )


def solution(mesh):
    placed = (
        P("slab", "mp", None, None),
        P("slab", "mp", None),
        P("slab", "mp", None),
        P(),
        P(),
        P(),
    )
    sizes = (mesh.shape["slab"], mesh.shape["mp"])
    return jax.shard_map(
        functools.partial(on_device, sizes),
        mesh=mesh,
        in_specs=placed,
        out_specs=(P(), P(), P(), P(), P(), P()),
        check_vma=False,
    )
```

```python
import functools

import jax
import jax.numpy as jnp
from jax import lax
from jax.experimental import pallas as pl
from jax.experimental.pallas import tpu as pltpu
from jax.sharding import PartitionSpec as P

EMB = 96
HEADS = 6
HDIM = 16
HID = 384
MERGE = 384
CLASSES = 14
WIN = 7
SHIFT = 3
LAYERS = 3
STEP = 10

F32 = jnp.float32
BF16 = jnp.bfloat16
eps_norm = 1e-05
beta_one = 0.9
beta_two = 0.999
adam_eps = 1e-08
learn_rate = 0.05
decay_rate = 0.05
clip_norm = 0.01
LOG2E = 1.4426950408889634

VOX = WIN * WIN * WIN
ROWS = 352
KEYS = 384
BLOCKS = ((0, 128), (128, 256), (256, 352))
WIDE = 128
PLANE = WIN * WIN
FAR = WIN - SHIFT
ROWS_A = SHIFT * FAR * WIN
ROWS_B = FAR * SHIFT * WIN
ROWS_C = SHIFT * SHIFT * WIN

MERGE_ROWS = 392
LAYER_ROWS = 1165
TAP_ROWS = 27 * EMB
GROUPS = 2280
NPARAM = 872558
HEAD_ROW = 6806
HEAD_ROWS = 11
HEAD_LANE = 32
LATE_ROWS = 3072
EARLY_ROWS = 3840
LAYER_BASE = (98, 389, 680)
CONV_BASE = (971, 1620)
CUTS = (0, 392, 688, 976, 2280)

R_QKV, R_QKVB, R_PROJ, R_PROJB = 4, 292, 295, 391
R_HID, R_HIDB, R_OUT, R_OUTB = 392, 776, 780, 1164


def iota(shape, dim):
    return lax.broadcasted_iota(jnp.int32, shape, dim)


def split(x):
    hi = x.astype(BF16)
    return hi, (x - hi.astype(F32)).astype(BF16)


def pair(x):
    return jnp.concatenate(split(x), 1)


def fold(y):
    half = y.shape[1] // 2
    return y[:, :half] + y[:, half:]


def fold_rows(y):
    half = y.shape[0] // 2
    return y[:half] + y[half:]


def dot(a, b):
    return jnp.dot(a, b, preferred_element_type=F32)


def dot_nt(a, b):
    return lax.dot_general(a, b, (((1,), (1,)), ((), ())), preferred_element_type=F32)


def weight_nn(w):
    top = pair(w)
    return jnp.concatenate([top, top], 0)


def weight_nt(w):
    hi, lo = split(w)
    return jnp.concatenate(
        [jnp.concatenate([hi, hi], 1), jnp.concatenate([lo, lo], 1)], 0
    )


def mm(x, w):
    return fold(dot(pair(x), weight_nn(w)))


def mm_nt(x, w):
    return fold(dot_nt(pair(x), weight_nt(w)))


def with_rows(x, rows):
    if x.shape[0] == rows:
        return x
    return jnp.concatenate([x, jnp.zeros((rows - x.shape[0], x.shape[1]), F32)], 0)


def rows_t(x):
    return jnp.concatenate(split(with_rows(x, -(-x.shape[0] // WIDE) * WIDE).T), 0)


def mm_tn(xt, y):
    return fold_rows(fold(dot(xt, pair(with_rows(y, xt.shape[1])))))


def deep(w):
    return jnp.concatenate([w, jnp.zeros((WIDE - EMB, w.shape[1]), F32)], 0)


def roll(x, shift, axis):
    return pltpu.roll(x, shift, axis)


def four_to_three(y):
    lane = iota(y[0].shape, 1)
    a = jnp.where(lane < 96, y[0], roll(y[1], 96, 1))
    b = jnp.where(lane < 64, roll(y[1], 96, 1), roll(y[2], 64, 1))
    c = jnp.where(lane < 32, roll(y[2], 64, 1), roll(y[3], 32, 1))
    return a, b, c


def three_to_four(x):
    lane = iota(x[0].shape, 1)
    live = lane < EMB
    a = x[0]
    b = jnp.where(lane < 32, roll(x[0], 32, 1), roll(x[1], 32, 1))
    c = jnp.where(lane < 64, roll(x[1], 64, 1), roll(x[2], 64, 1))
    d = roll(x[2], 96, 1)
    return tuple(jnp.where(live, v, 0.0) for v in (a, b, c, d))


def hidden_rows(ref, start, count):
    return jnp.concatenate(
        four_to_three([ref[pl.ds(start + c, count, stride=4), :] for c in range(4)]), 1
    )


def put_hidden_rows(ref, start, count, x):
    parts = three_to_four([x[:, i * WIDE : (i + 1) * WIDE] for i in range(3)])
    for c in range(4):
        ref[pl.ds(start + c, count, stride=4), :] = parts[c]


def flatten(ref, start, groups, out):
    parts = four_to_three([ref[pl.ds(start + c, groups, stride=4), :] for c in range(4)])
    for c in range(3):
        out[pl.ds(c, groups, stride=3), :] = parts[c]


def norm_stats(x):
    live = iota(x.shape, 1) < EMB
    mean = jnp.sum(x, 1, keepdims=True) * (1.0 / EMB)
    centred = jnp.where(live, x - mean, 0.0)
    var = jnp.sum(centred * centred, 1, keepdims=True) * (1.0 / EMB)
    inv = lax.rsqrt(var + eps_norm)
    return centred * inv, inv


def norm(x, gain, bias):
    hat, _ = norm_stats(x)
    return hat * gain + bias


def norm_back(hat, inv, gain, grad):
    up = grad * gain
    one = jnp.sum(up, 1, keepdims=True) * (1.0 / EMB)
    two = jnp.sum(up * hat, 1, keepdims=True) * (1.0 / EMB)
    live = iota(hat.shape, 1) < EMB
    return jnp.where(live, inv * (up - one - hat * two), 0.0)


def colsum(x):
    return jnp.sum(x, 0, keepdims=True)


def gelu(x):
    return 0.5 * x * (1.0 + lax.erf(x * (0.5**0.5)))


def gelu_both(x):
    cdf = 0.5 * (1.0 + lax.erf(x * (0.5**0.5)))
    slope = cdf + x * (jnp.exp(x * x * -0.5) * 0.3989422804014327)
    return x * cdf, slope


def head_groups(x):
    lane = iota(x.shape, 1)
    swapped = roll(x, 64, 1)
    return jnp.where(lane < 64, x, swapped), jnp.where(lane < 64, swapped, x)


def as_left(x):
    both = []
    low = iota(x.shape, 1) < 64
    for part in head_groups(x):
        hi = part.astype(BF16).astype(F32)
        one = jnp.where(low, hi, part - hi).astype(BF16)
        both.append(jnp.concatenate([one, one], 1))
    return both


def as_right(x):
    return [pair(part) for part in head_groups(with_rows(x, KEYS))]


def head_mask(h, width):
    lane = iota((1, width), 1)
    lane = jnp.bitwise_and(lane, 63)
    low = jnp.bitwise_and(h, 3) * HDIM
    return jnp.where((lane >= low) & (lane < low + HDIM), 1.0, 0.0)


def own_lanes(h):
    lane = iota((1, WIDE), 1)
    return jnp.where((lane >= h * HDIM) & (lane < (h + 1) * HDIM), 1.0, 0.0)


def both_heads(right, heads, out):
    for k, h in enumerate(heads):
        out[k * KEYS : (k + 1) * KEYS, :] = right * head_mask(h, 2 * WIDE).astype(BF16)


def score_tiles(s, rows, region):
    tiles = [s[:, i * WIDE : (i + 1) * WIDE] for i in range(3)]
    if region is not None:
        return [t + region[rows, i * WIDE : (i + 1) * WIDE] for i, t in enumerate(tiles)]
    pad = jnp.where(iota((1, WIDE), 1) < VOX - 2 * WIDE, 0.0, -1e30)
    return tiles[:2] + [tiles[2] + pad]


def put_split(ref, rows, i, x):
    hi, lo = split(x)
    ref[rows, i * WIDE : (i + 1) * WIDE] = hi
    ref[rows, KEYS + i * WIDE : KEYS + (i + 1) * WIDE] = lo


def attention(normed, layer, save, lse, mixed, sc, region=None):
    left, right, values = sc
    x = pair(normed)
    qkv = []
    for i in range(3):
        w = deep(layer[pl.ds(R_QKV + i, EMB, stride=3), :])
        y = fold(dot(x, weight_nn(w))) + layer[R_QKVB + i : R_QKVB + i + 1, :]
        if i == 0:
            y = y * (HDIM**-0.5 * LOG2E)
        save[:, i * WIDE : (i + 1) * WIDE] = y
        qkv.append(y)
    for g, part in enumerate(as_left(qkv[0])):
        left[g] = part
    for g, part in enumerate(as_right(qkv[1])):
        right[g] = part
    v = jnp.where(iota((ROWS, WIDE), 1) == EMB, 1.0, qkv[2])
    v = pair(with_rows(v, KEYS))
    values[0:KEYS, :] = v
    values[KEYS : 2 * KEYS, :] = v
    mixed[...] = jnp.zeros_like(mixed)
    lse[...] = jnp.zeros_like(lse)

    def per_pair(pair_of, carry):
        heads = [2 * pair_of, 2 * pair_of + 1]
        masks = [head_mask(h, 2 * WIDE).astype(BF16) for h in heads]
        lanes = [own_lanes(h) for h in heads]
        spots = [jnp.where(iota((1, WIDE), 1) == h, 1.0, 0.0) for h in heads]
        g = lax.div(pair_of, 2)
        for block in BLOCKS:
            rows = slice(*block)
            out = level = 0.0
            for k in range(2):
                s = dot_nt(left[g, rows, :] * masks[k], right[g])
                tiles = score_tiles(s, rows, region)
                top = jnp.maximum(jnp.maximum(tiles[0], tiles[1]), tiles[2])
                top = jnp.max(top, 1, keepdims=True)
                parts = [split(jnp.exp2(t - top)) for t in tiles]
                e = jnp.concatenate([p[0] for p in parts] + [p[1] for p in parts], 1)
                o = fold(dot(e, values[...]))
                total = o[:, EMB : EMB + 1]
                out = out + o * (lanes[k] / total)
                level = level + (top + jnp.log(total) * LOG2E) * spots[k]
            mixed[rows, :] += out
            lse[rows, :] += level
        return carry

    lax.fori_loop(0, HEADS // 2, per_pair, 0)
    proj = deep(layer[R_PROJ : R_PROJ + EMB, :])
    return mm(mixed[...], proj) + layer[R_PROJB : R_PROJB + 1, :]


def attention_back(grad, normed, layer, save, lse, mixed, sc, grads, at, region=None):
    left, right, gleft, vright, keys, dq, dkv_t, weights, slopes = sc[:9]
    q_t, do_t, dmix, s, dp, two_keys, two_values = sc[9:]
    proj = deep(layer[R_PROJ : R_PROJ + EMB, :])
    grads[at + R_PROJ : at + R_PROJ + EMB, :] = mm_tn(rows_t(mixed[...]), grad)[:EMB]
    grads[at + R_PROJB : at + R_PROJB + 1, :] = colsum(grad)
    d_mixed = mm_nt(grad, proj)
    dmix[...] = d_mixed * mixed[...]
    q, k, v = (save[:, i * WIDE : (i + 1) * WIDE] for i in range(3))
    for g, part in enumerate(as_left(q)):
        left[g] = part
    for g, part in enumerate(as_right(k)):
        right[g] = part
    for g, part in enumerate(as_left(d_mixed)):
        gleft[g] = part
    for g, part in enumerate(as_right(v)):
        vright[g] = part
    kk = pair(with_rows(k, KEYS))
    keys[0:KEYS, :] = kk
    keys[KEYS : 2 * KEYS, :] = kk
    weights[:, ROWS:, :] = jnp.zeros((2, KEYS - ROWS, 2 * KEYS), BF16)
    slopes[:, ROWS:, :] = jnp.zeros((2, KEYS - ROWS, 2 * KEYS), BF16)
    for ref, x in ((q_t, q), (do_t, d_mixed)):
        hi, lo = split(with_rows(x, KEYS).T)
        ref[0] = hi
        ref[1] = lo
    dq[...] = jnp.zeros_like(dq)
    dkv_t[...] = jnp.zeros_like(dkv_t)

    def per_pair(pair_of, carry):
        g = lax.div(pair_of, 2)
        heads = [2 * pair_of, 2 * pair_of + 1]
        both_heads(right[g], heads, two_keys)
        both_heads(vright[g], heads, two_values)
        s[...] = dot_nt(left[g], two_keys[...])
        dp[...] = dot_nt(gleft[g], two_values[...])
        for k in range(2):
            h = 2 * pair_of + k
            lanes = own_lanes(h)
            at_h = jnp.where(iota((1, WIDE), 1) == h, 1.0, 0.0)
            for block in BLOCKS:
                rows = slice(*block)
                level = jnp.sum(lse[rows, :] * at_h, 1, keepdims=True)
                delta = jnp.sum(dmix[rows, :] * lanes, 1, keepdims=True)
                at_k = k * KEYS
                tiles = score_tiles(s[rows, at_k : at_k + KEYS], rows, region)
                for i, t in enumerate(tiles):
                    p = jnp.exp2(t - level)
                    put_split(weights.at[k], rows, i, p)
                    low = at_k + i * WIDE
                    p = p * (dp[rows, low : low + WIDE] - delta)
                    put_split(slopes.at[k], rows, i, p)
        total = 0.0
        for k in range(2):
            out = fold(dot(slopes[k, 0:ROWS, :], keys[...]))
            total = total + out * own_lanes(2 * pair_of + k)
        dq[...] += total
        for k in range(2):
            here = pl.ds(pl.multiple_of((2 * pair_of + k) * HDIM, HDIM), HDIM)
            for i, (t, m) in enumerate(((q_t, slopes), (do_t, weights))):
                lhs = jnp.concatenate([t[0, here, :], t[1, here, :]], 0)
                dkv_t[i, here, :] = fold_rows(fold(dot(lhs, m[k])))
        return carry

    lax.fori_loop(0, HEADS // 2, per_pair, 0)
    d_q = dq[...] * HDIM**-0.5
    d_k = dkv_t[0].T[0:ROWS] * (1.0 / LOG2E)
    d_v = dkv_t[1].T[0:ROWS]
    x_t = rows_t(normed)
    d_normed = None
    for i, d in enumerate((d_q, d_k, d_v)):
        grads[pl.ds(at + R_QKV + i, EMB, stride=3), :] = mm_tn(x_t, d)[:EMB]
        grads[at + R_QKVB + i : at + R_QKVB + i + 1, :] = colsum(d)
        part = mm_nt(d, deep(layer[pl.ds(R_QKV + i, EMB, stride=3), :]))
        d_normed = part if d_normed is None else d_normed + part
    return d_normed


def mlp(middle, layer, hpre):
    normed = norm(middle, layer[2:3, :], layer[3:4, :])
    w = deep(hidden_rows(layer, R_HID, EMB))
    pre = mm(normed, w) + hidden_rows(layer, R_HIDB, 1)
    hpre[...] = pre
    out = mm(gelu(pre), layer[R_OUT : R_OUT + HID, :])
    return middle + out + layer[R_OUTB : R_OUTB + 1, :]


def mlp_back(grad, middle, hpre, layer, grads, at):
    hat, inv = norm_stats(middle)
    normed = hat * layer[2:3, :] + layer[3:4, :]
    act, slope = gelu_both(hpre[...])
    grads[at + R_OUTB : at + R_OUTB + 1, :] = colsum(grad)
    grads[at + R_OUT : at + R_OUT + HID, :] = mm_tn(rows_t(grad), act).T
    d_pre = mm_nt(grad, layer[R_OUT : R_OUT + HID, :]) * slope
    put_hidden_rows(grads, at + R_HIDB, 1, colsum(d_pre))
    put_hidden_rows(grads, at + R_HID, EMB, mm_tn(rows_t(normed), d_pre)[:EMB])
    d_normed = mm_nt(d_pre, deep(hidden_rows(layer, R_HID, EMB)))
    grads[at + 2 : at + 3, :] = colsum(d_normed * hat)
    grads[at + 3 : at + 4, :] = colsum(d_normed)
    return grad + norm_back(hat, inv, layer[2:3, :], d_normed)


def pre_norm_back(grad, tokens, layer, grads, at):
    hat, inv = norm_stats(tokens)
    grads[at : at + 1, :] = colsum(grad * hat)
    grads[at + 1 : at + 2, :] = colsum(grad)
    return norm_back(hat, inv, layer[0:1, :], grad)


def region_of(rows, sizes):
    d = lax.shift_right_logical(rows * 1338, 16)
    line = lax.shift_right_logical(rows * 9363, 16)
    places = (d, line - d * WIN, rows - line * WIN)
    starts = (lax.axis_index("slab") * WIN, lax.axis_index("mp") * WIN, 0)
    total = None
    for place, start, blocks in zip(places, starts, sizes + (1,)):
        turned = jnp.where(place < SHIFT, place + FAR, place - SHIFT) + start
        length = WIN * blocks
        part = jnp.where(turned < length - WIN, 0, jnp.where(turned < length - SHIFT, 1, 2))
        total = part if total is None else total * 3 + part
    return total


def put_region(region, sizes):
    rows = region_of(iota((ROWS, WIDE), 0), sizes)[:, 0:1]
    lanes = region_of(iota((8, KEYS), 1), sizes)[0:1, :]
    apart = jnp.where(rows == lanes, 0.0, -100.0 * LOG2E)
    region[...] = jnp.where(iota((ROWS, KEYS), 1) < VOX, apart, -1e30)


def send_parts(ref, a, b, c):
    far = FAR * WIN
    near = SHIFT * WIN
    for d in range(SHIFT):
        base = d * PLANE
        c[d * near : (d + 1) * near, :] = ref[base : base + near, :]
        a[d * far : (d + 1) * far, :] = ref[base + near : base + PLANE, :]
    for d in range(FAR):
        base = (d + SHIFT) * PLANE
        b[d * near : (d + 1) * near, :] = ref[base : base + near, :]


def take_parts(own, a, b, c, out):
    far = FAR * WIN
    near = SHIFT * WIN
    for d in range(WIN):
        base = d * PLANE
        if d < SHIFT:
            out[base : base + near, :] = c[d * near : (d + 1) * near, :]
            out[base + near : base + PLANE, :] = a[d * far : (d + 1) * far, :]
        else:
            e = d - SHIFT
            out[base : base + near, :] = b[e * near : (e + 1) * near, :]
            out[base + near : base + PLANE, :] = own[base + near : base + PLANE, :]
    out[VOX:, :] = jnp.zeros((ROWS - VOX, WIDE), F32)


def span_of(groups):
    low, high = groups
    first = 3 * low // 8 * 8
    last = -(-3 * high // 8) * 8
    return first, min(last, NPARAM // WIDE // 8 * 8) - first


def copied(params, groups, flat, sem):
    first, rows = span_of(groups)
    size = rows * WIDE
    return pltpu.make_async_copy(
        params.at[pl.ds(first * WIDE, size)], flat.at[pl.ds(0, size)], sem
    )


def relay(groups, flat, out, square, last=None):
    low, high = groups
    first, rows = span_of(groups)
    square[0:rows, :] = flat[0 : rows * WIDE].reshape(rows, WIDE)
    if last is not None:
        square[rows : rows + 24, :] = jnp.zeros((24, WIDE), F32)
        square[rows : rows + 1, 0 : last.shape[0]] = last[...].reshape(1, last.shape[0])
    skip = 3 * low - first
    n = high - low
    parts = three_to_four([square[pl.ds(skip + c, n, stride=3), :] for c in range(3)])
    for c in range(4):
        out[pl.ds(c, n, stride=4), :] = parts[c]


FIRST_SPANS = ((0, 98), (98, 392))
LAYER_SPANS = ((389, 681), (680, 972))
CONV_SPANS = ((971, 1620), (1620, GROUPS))


def prep_kernel(spans, params, *refs, last=None):
    outs, (flats, square, sems) = refs[: len(spans)], refs[-3:]
    for i, groups in enumerate(spans):
        copied(params, groups, flats[i], sems.at[i]).start()
    for i, groups in enumerate(spans):
        copied(params, groups, flats[i], sems.at[i]).wait()
        relay(groups, flats[i], outs[i], square, last if i == len(spans) - 1 else None)


def head_picks():
    width = HEAD_ROWS * WIDE
    place = iota((WIDE, width), 1) - HEAD_LANE
    row = iota((WIDE, width), 0)
    here = (place >= row * CLASSES) & (place < (row + 1) * CLASSES) & (row <= EMB)
    place = iota((width, WIDE), 0) - HEAD_LANE
    col = iota((width, WIDE), 1)
    row = lax.shift_right_logical(place * 4682, 16)
    there = (place - row * CLASSES == col) & (place >= 0)
    return jnp.where(here, 1.0, 0.0), jnp.where(there, 1.0, 0.0).astype(BF16)


def prep_conv0_kernel(params, conv0, weights0, bias, *scratch):
    prep_kernel(CONV_SPANS[:1], params, conv0, *scratch)
    tap_weights(conv0, 3, weights0)
    bias[0:1, :] = conv0[3 + TAP_ROWS : 4 + TAP_ROWS, :]
    bias[1:8, :] = jnp.zeros((7, WIDE), F32)


def prep_conv1_kernel(last, bias, params, conv1, head, weights1, vectors, *scratch):
    prep_kernel(CONV_SPANS[1:], params, conv1, *scratch, last=last)
    tap_weights(conv1, 0, weights1)
    vectors[0:1, :] = bias[0:1, :]
    vectors[1:4, :] = conv1[TAP_ROWS : TAP_ROWS + 3, :]
    vectors[4:8, :] = jnp.zeros((4, WIDE), F32)
    square = scratch[1]
    first, _ = span_of(CONV_SPANS[1])
    row = jnp.concatenate(
        [square[HEAD_ROW + i - first : HEAD_ROW + i - first + 1, :] for i in range(HEAD_ROWS)], 1
    )
    here, there = head_picks()
    hi, lo = split(here * row)
    head[...] = dot(hi, there) + dot(lo, there)


def head_rows(d_head, out, at):
    here, there = head_picks()
    hi, lo = split(d_head)
    spread = (dot_nt(hi, there) + dot_nt(lo, there)) * here
    row = colsum(spread)
    for i in range(HEAD_ROWS):
        out[at + i : at + i + 1, :] += row[:, i * WIDE : (i + 1) * WIDE]


class Rows:
    def __init__(self, ref, at):
        self.ref, self.at = ref, at

    def __getitem__(self, key):
        rows, lanes = key
        if isinstance(rows, slice):
            rows = slice(rows.start + self.at, rows.stop + self.at)
        else:
            rows = pl.ds(rows.start + self.at, rows.size, stride=rows.stride)
        return self.ref[rows, lanes]


def merged_norm(x):
    mean = jnp.sum(x, 1, keepdims=True) * (1.0 / MERGE)
    centred = x - mean
    var = jnp.sum(centred * centred, 1, keepdims=True) * (1.0 / MERGE)
    return centred * lax.rsqrt(var + eps_norm)


def first_kernel(
    feats, merge, lay0,
    dense, tok0, save, lse, mixed, middle, hpre, tok1, ahead, pa, pb, pc,
    *sc,
):
    dense[VOX:, :] = jnp.zeros((ROWS - VOX, MERGE), F32)
    for line in range(PLANE):
        dense[line * WIN : (line + 1) * WIN, :] = feats[line]
    hat = merged_norm(dense[...])
    normed = hat * hidden_rows(merge, 0, 1) + hidden_rows(merge, 4, 1)
    tokens = mm(normed, merge[8 : 8 + MERGE, :])
    tok0[...] = tokens
    layer = Rows(lay0, 0)
    normed = norm(tokens, layer[0:1, :], layer[1:2, :])
    attended = attention(normed, layer, save, lse, mixed, sc)
    mid = tokens + attended
    middle[...] = mid
    tokens = mlp(mid, layer, hpre)
    tok1[...] = tokens
    ahead[...] = norm(tokens, layer[1165:1166, :], layer[1166:1167, :])
    send_parts(ahead, pa, pb, pc)


def shifted_kernel(
    sizes,
    own, pa, pb, pc, lay1, _,
    window, save, lse, mixed, out, qa, qb, qc,
    region, *sc,
):
    put_region(region, sizes)
    take_parts(own, pa, pb, pc, window)
    out[...] = attention(
        window[...], Rows(lay1, 1), save, lse, mixed, sc, region
    )
    send_parts(out, qa, qb, qc)


def to_lines(ref, out):
    for line in range(PLANE):
        out[line, 0:WIN, :] = ref[line * WIN : (line + 1) * WIN, :]
        out[line, WIN:8, :] = jnp.zeros((8 - WIN, WIDE), F32)


def from_lines(ref, out):
    out[VOX:, :] = jnp.zeros((ROWS - VOX, WIDE), F32)
    for line in range(PLANE):
        out[line * WIN : (line + 1) * WIN, :] = ref[line, 0:WIN, :]


def send_sides(lines, near_d, far_d, near_h, far_h):
    odd_d = jnp.bitwise_and(lax.axis_index("slab"), 1) == 1
    odd_h = jnp.bitwise_and(lax.axis_index("mp"), 1) == 1
    low, high = lines[0 : 2 * WIN], lines[(WIN - 2) * WIN : PLANE]
    near_d[...] = jnp.where(odd_d, low, high)
    far_d[...] = jnp.where(odd_d, high, low)
    for d in range(WIN):
        low = lines[d * WIN : d * WIN + 2]
        high = lines[d * WIN + WIN - 2 : (d + 1) * WIN]
        near_h[2 * d : 2 * d + 2] = jnp.where(odd_h, low, high)
        far_h[2 * d : 2 * d + 2] = jnp.where(odd_h, high, low)


def second_kernel(
    tok1, own, qa, qb, qc, lay1, lay2, _,
    mid1, hpre1, tok2, save, lse, mixed, mid2, hpre2, lines,
    s0, s1, s2, s3,
    attended, *sc,
):
    take_parts(own, qa, qb, qc, attended)
    mid = tok1[...] + attended[...]
    mid1[...] = mid
    tokens = mlp(mid, Rows(lay1, 1), hpre1)
    tok2[...] = tokens
    layer = Rows(lay2, 2)
    normed = norm(tokens, layer[0:1, :], layer[1:2, :])
    mid = tokens + attention(normed, layer, save, lse, mixed, sc)
    mid2[...] = mid
    attended[...] = mlp(mid, layer, hpre2)
    to_lines(attended, lines)
    send_sides(lines, s0, s1, s2, s3)


def grown_lines(sizes, own, near_d, far_d, near_h, far_h, out):
    slab, row = lax.axis_index("slab"), lax.axis_index("mp")
    odd_d = jnp.bitwise_and(slab, 1) == 1
    odd_h = jnp.bitwise_and(row, 1) == 1
    out[:, 11:12] = jnp.zeros((11, 1, 8, WIDE), F32)
    for d in range(WIN):
        out[d + 2, 2 : 2 + WIN] = own[d * WIN : (d + 1) * WIN]
    for d in range(2):
        near = near_d[d * WIN : (d + 1) * WIN]
        far = far_d[d * WIN : (d + 1) * WIN]
        out[d, 2 : 2 + WIN] = jnp.where(odd_d, near, jnp.where(slab == 0, 0.0, far))
        out[d + 9, 2 : 2 + WIN] = jnp.where(
            odd_d, jnp.where(slab == sizes[0] - 1, 0.0, far), near
        )
    for d in range(11):
        near = near_h[2 * d : 2 * d + 2]
        far = far_h[2 * d : 2 * d + 2]
        out[d, 0:2] = jnp.where(odd_h, near, jnp.where(row == 0, 0.0, far))
        out[d, 9:11] = jnp.where(odd_h, jnp.where(row == sizes[1] - 1, 0.0, far), near)


def put_marks(labels, valid, out):
    across = iota((8, WIN), 1) == iota((8, WIN), 0)
    classes = iota((8, WIDE), 1) - EMB
    for d in range(WIN):
        code = jnp.where(valid[d] == 1, labels[d], -1 - EMB - WIDE)
        code = code.astype(F32)
        for h in range(WIN):
            line = jnp.where(across, code[h : h + 1, :], 0.0)
            column = jnp.sum(line, 1, keepdims=True)
            mark = jnp.where(column == classes.astype(F32), 1.0, 0.0)
            out[d * WIN + h] = jnp.where(iota((8, WIDE), 0) < WIN, mark, 0.0)


def taps(source, first_plane, planes, first_line, lines, out):
    def per_plane(d, carry):
        for c in range(3):
            for b in range(3):
                x = source[d + first_plane, first_line + b : first_line + b + lines]
                if c != 1:
                    x = roll(x, 1 if c == 0 else 7, 1)
                x = pair(x.reshape(lines * 8, WIDE))
                at = pl.multiple_of(d * (lines * 8), lines * 8)
                t = b * 3 + c
                out[pl.ds(at, lines * 8), t * 256 : (t + 1) * 256] = x
        return carry

    lax.fori_loop(0, planes, per_plane, 0)


def tap_weights(ref, at, out):
    def per_tap(i, carry):
        w = deep(ref[pl.ds(i * EMB + at, EMB), :])
        out[pl.ds(pl.multiple_of(i * 256, 256), 256), :] = weight_nn(w)
        return carry

    lax.fori_loop(0, 27, per_tap, 0)


def tap_weights_back(ref, at, out):
    for i in range(27):
        w = deep(ref[(26 - i) * EMB + at : (27 - i) * EMB + at, :]).T
        out[i * 256 : (i + 1) * 256, :] = weight_nn(w)


def conv(side, weights, cuts, pitch, out):
    for start, end in zip(cuts, cuts[1:]):
        total = None
        for a in range(3):
            x = side[start + a * pitch : end + a * pitch, :]
            part = dot(x, weights[a * 2304 : (a + 1) * 2304, :])
            total = part if total is None else total + part
        out[start:end, :] = fold(total)


def conv_weight_grad(side, grad_rows, pitch, out, at):
    rows = 512
    g = jnp.concatenate([grad_rows, jnp.zeros((rows - grad_rows.shape[0], WIDE), F32)], 0)
    left = jnp.concatenate(split(g.T[:EMB]), 0)
    for a in range(3):
        for bc in range(9):
            y = dot(left, side[a * pitch : a * pitch + rows, bc * 256 : (bc + 1) * 256])
            y = deep(fold_rows(fold(y))).T
            t = a * 9 + bc
            out[at + t * EMB : at + (t + 1) * EMB, :] = y[:EMB]


def volume_mask(sizes, planes, lines, reach, real_lines):
    slab, row = lax.axis_index("slab"), lax.axis_index("mp")
    ends = (slab == 0, slab == sizes[0] - 1, row == 0, row == sizes[1] - 1)
    shape = (planes, lines, 8, WIDE)
    d, h, w = iota(shape, 0), iota(shape, 1), iota(shape, 2)
    low_d = jnp.where(ends[0], reach, 0)
    high_d = jnp.where(ends[1], planes - reach, planes)
    low_h = jnp.where(ends[2], reach, 0)
    high_h = jnp.where(ends[3], real_lines - reach, real_lines)
    inside = (d >= low_d) & (d < high_d) & (h >= low_h) & (h < high_h) & (w < WIN)
    return jnp.where(inside, 1.0, 0.0)


def conv_kernel(
    sizes,
    own, s0, s1, s2, s3, labels, valid, weights0, weights1, vectors, _,
    grown, pre, tok, stats, t0, t1, t2, t3,
    act, side, side_own, marks, result,
):
    grown_lines(sizes, own, s0, s1, s2, s3, grown)
    put_marks(labels, valid, marks)
    taps(grown, 0, 11, 0, 10, side)
    bias0 = vectors[0:1, :]
    inside = volume_mask(sizes, 9, 10, 1, 9)

    conv(side, weights0, (0, 176, 352, 528, 720), 80, result)
    z = (result[...] + bias0).reshape(9, 10, 8, WIDE)
    pre[...] = z
    act[...] = gelu(z) * inside
    taps(act, 0, 9, 0, 8, side_own)
    bias1 = vectors[1:2, :]
    conv(side_own, weights1, (0, 160, 304, 448), 64, result)
    y = (result[0 : WIN * 64, :] + bias1).reshape(WIN, 8, 8, WIDE)[:, 0:WIN]
    y = y + own[...].reshape(WIN, WIN, 8, WIDE)
    y = jnp.where(iota(y.shape, 2) < WIN, y, 0.0).reshape(PLANE, 8, WIDE)
    tok[...] = y + marks[...]
    send_sides(tok, t0, t1, t2, t3)
    flat = y.reshape(PLANE * 8, WIDE)
    count = jnp.sum(marks[...].reshape(PLANE * 8, WIDE))
    row = iota((8, WIDE), 0)
    stats[...] = (
        jnp.where(row == 0, colsum(flat), 0.0)
        + jnp.where(row == 1, colsum(flat * flat), 0.0)
        + jnp.where(row == 2, count, 0.0)
    )


def head_kernel(
    sizes, voxels,
    own, s0, s1, s2, s3, sums, vectors, head_w,
    grown, slope_out, stats, d_head, d_rows,
):
    grown_lines(sizes, own, s0, s1, s2, s3, grown)
    rows = 11 * 12 * 8
    both = grown[...].reshape(rows, WIDE)
    lane = iota((rows, WIDE), 1)
    tokens = jnp.where(lane < EMB, both, 0.0)
    target = jnp.where(lane < CLASSES, roll(both, WIDE - EMB, 1), 0.0)
    live = jnp.sum(target, 1, keepdims=True)
    count = F32(voxels)
    average = sums[0:1, :] / count
    spread = sums[1:2, :] / count - average * average
    inv = lax.rsqrt(spread + eps_norm)
    gain = vectors[2:3, :]
    bias = vectors[3:4, :]
    hat = (tokens - average) * inv
    act, slope = gelu_both(hat * gain + bias)
    act = jnp.where(lane == EMB, 1.0, act)
    w = head_w[...]
    logits = mm(act, w)
    logits = jnp.where(lane < CLASSES, logits, -1e30)
    top = jnp.max(logits, 1, keepdims=True)
    e = jnp.exp(logits - top)
    total = jnp.sum(e, 1, keepdims=True)
    logp = logits - top - jnp.log(total)
    scale = 1.0 / sums[2:3, 0:1]
    d_logits = (e / total * live - target) * scale
    d_normed = jnp.where(lane < EMB, mm_nt(d_logits, w) * slope, 0.0)
    d_tokens = d_normed * gain * inv
    slope_out[...] = d_tokens.reshape(11, 12, 8, WIDE)

    def own_rows(x):
        x = x.reshape(11, 12, 8, WIDE)[2:9, 2:9]
        x = jnp.where(iota(x.shape, 2) < WIN, x, 0.0)
        return x.reshape(PLANE * 8, WIDE)

    loss = -jnp.sum(own_rows(target * jnp.where(lane < CLASSES, logp, 0.0)))
    own_d = own_rows(d_logits)
    own_n = own_rows(d_normed)
    own_hat = own_rows(hat)
    zeros = jnp.zeros((512 - PLANE * 8, WIDE), F32)
    left = rows_t(jnp.concatenate([own_d, zeros], 0))
    d_head[...] = mm_tn(left, jnp.concatenate([own_rows(act), zeros], 0)).T
    d_gain = colsum(own_n * own_hat)
    d_bias = colsum(own_n)
    d_average = -d_bias * gain * inv
    d_spread = d_gain * gain * inv * inv * -0.5
    d_two = d_spread / count
    d_one = (d_average - 2.0 * average * d_spread) / count
    row = iota((8, WIDE), 0)
    live_lane = iota((8, WIDE), 1) < EMB
    stats[...] = (
        jnp.where((row == 0) & live_lane, d_one, 0.0)
        + jnp.where((row == 1) & live_lane, d_two, 0.0)
        + jnp.where(row == 2, loss, 0.0)
    )
    d_rows[...] = (
        jnp.where(row == 0, d_gain, 0.0)
        + jnp.where(row == 1, d_bias, 0.0)
    )


def sides_back_kernel(sizes, grown, pre, side_act, side_grown, act):
    act[0:9] = gelu(pre[...]) * volume_mask(sizes, 9, 10, 1, 9)
    act[9:10] = jnp.zeros((1, 10, 8, WIDE), F32)
    taps(act, 0, 10, 0, 8, side_act)
    taps(grown, 1, 10, 1, 8, side_grown)


def weights_back_kernel(conv0, conv1, weights0, weights1):
    tap_weights_back(conv0, 3, weights0)
    tap_weights_back(conv1, 0, weights1)


def conv_back_kernel(
    sizes,
    tok, slope, sums, pre, side_act, side_grown, weights0, weights1, d_rows, d_head,
    d_own, keep, send, carry, seam,
    grads, dgrown, act, side, side_own, flat, result,
):
    lane = iota((11, 12, 8, WIDE), 3)
    inside = volume_mask(sizes, 11, 12, 2, 11)
    steady = sums[0:1, :].reshape(1, 1, 1, WIDE)
    rising = 2.0 * sums[1:2, :].reshape(1, 1, 1, WIDE)
    d_tok = slope[...] + jnp.where(lane < EMB, (steady + tok[...] * rising) * inside, 0.0)
    dgrown[...] = d_tok
    grads[5191:, :] = jnp.zeros((45, WIDE), F32)
    grads[0:8, :] = jnp.zeros((8, WIDE), F32)
    grads[5189:5191, :] = d_rows[0:2, :]
    own = dgrown[2:9, 2:10]
    line = iota(own.shape, 1)
    own = jnp.where(line < WIN, own, 0.0).reshape(WIN * 64, WIDE)
    grads[5188:5189, :] = colsum(own)

    near = volume_mask(sizes, 9, 10, 1, 9)
    conv_weight_grad(side_act, own, 64, grads, 2596)
    taps(dgrown, 0, 11, 0, 10, side)

    conv(side, weights1, (0, 176, 352, 528, 720), 80, result)
    act[0:9] = result[...].reshape(9, 10, 8, WIDE) * gelu_both(pre[...])[1] * near

    own = act[1:8, 1:9]
    line = iota(own.shape, 1)
    own = jnp.where(line < WIN, own, 0.0).reshape(WIN * 64, WIDE)
    grads[2595:2596, :] = colsum(own)
    conv_weight_grad(side_grown, own, 64, grads, 3)
    carry[...] = grads[0:24, :]
    flat[3 * (GROUPS - CUTS[3]) :, :] = jnp.zeros((flat.shape[0] - 3912, WIDE), F32)
    flatten(grads, 20, GROUPS - CUTS[3], flat)
    start = 3 * CUTS[3]
    head_rows(d_head[...], flat, HEAD_ROW - start)
    seam[...] = flat[0 : LATE_ROWS - start, :]
    scatter(sizes, flat, LATE_ROWS - start, keep, send)
    taps(act, 0, 9, 0, 8, side_own)
    conv(side_own, weights0, (0, 160, 304, 448), 64, result)
    y = result[0 : WIN * 64, :].reshape(WIN, 8, 8, WIDE)[:, 0:WIN] + dgrown[2:9, 2:9]
    y = jnp.where(iota(y.shape, 2) < WIN, y, 0.0)
    d_own[...] = y.reshape(PLANE, 8, WIDE)


def back_mlp_kernel(d_own, lay2, mid2, hpre2, d_mid, grads, dense):
    from_lines(d_own, dense)
    grads[...] = jnp.zeros_like(grads)
    d_mid[...] = mlp_back(dense[...], mid2[...], hpre2, Rows(lay2, 2), grads, 2)


def back_two_kernel(
    d_mid2, grads2, carry, lay1, lay2, tok2, save, lse, mixed, mid1, hpre1,
    d_mid, grads1, flat, carry2, pa, pb, pc,
    grads, *sc,
):
    layer = Rows(lay2, 2)
    grads[0:1168, :] = grads2[...]
    d = d_mid2[...]
    tokens = tok2[...]
    normed = norm(tokens, layer[0:1, :], layer[1:2, :])
    d_normed = attention_back(d, normed, layer, save, lse, mixed, sc, grads, 2)
    d = d + pre_norm_back(d_normed, tokens, layer, grads, 2)
    grads[1167:1184, :] = carry[3:20, :]
    flatten(grads, 32, CUTS[3] - CUTS[2], flat)
    carry2[...] = grads[0:32, :]
    layer = Rows(lay1, 1)
    d = mlp_back(d, mid1[...], hpre1, layer, grads1, 1)
    d_mid[...] = d
    send_parts(d_mid, pa, pb, pc)


def back_shifted_kernel(
    sizes,
    own, pa, pb, pc, lay1, window, save, lse, mixed, grads1, carry2, _,
    d_window, flat, carry1, qa, qb, qc,
    region, grads, grad, *sc,
):
    put_region(region, sizes)
    take_parts(own, pa, pb, pc, grad)
    grads[0:1168, :] = grads1[...]
    grads[0:3, :] = jnp.zeros((3, WIDE), F32)
    d_window[...] = attention_back(
        grad[...], window[...], Rows(lay1, 1), save, lse, mixed, sc, grads, 1,
        region,
    )
    send_parts(d_window, qa, qb, qc)
    grads[1166:1196, :] = carry2[2:32, :]
    flatten(grads, 12, CUTS[2] - CUTS[1], flat)
    carry1[...] = grads[0:16, :]


def back_first_kernel(
    sizes,
    d_mid, own, qa, qb, qc, tok1, lay0, lay1, merge, dense, tok0, save, lse, mixed, middle, hpre,
    carry1, flat1, flat2, seam, _,
    keep, send,
    flat, grads, grad, *sc,
):
    take_parts(own, qa, qb, qc, grad)
    grads[1556:1572, :] = carry1[...]
    d = d_mid[...] + pre_norm_back(grad[...], tok1[...], Rows(lay1, 1), grads, 1557)
    layer = Rows(lay0, 0)
    at = MERGE_ROWS
    d = mlp_back(d, middle[...], hpre, layer, grads, at)
    tokens = tok0[...]
    normed = norm(tokens, layer[0:1, :], layer[1:2, :])
    d_normed = attention_back(d, normed, layer, save, lse, mixed, sc, grads, at)
    d = d + pre_norm_back(d_normed, tokens, layer, grads, at)
    live = iota((ROWS, WIDE), 0) < VOX
    d = jnp.where(live, d, 0.0)
    hat = merged_norm(dense[...])
    gain = hidden_rows(merge, 0, 1)
    bias = hidden_rows(merge, 4, 1)
    w = merge[8 : 8 + MERGE, :]
    put_hidden_rows(grads, 8 - 8, 1, jnp.zeros((1, MERGE), F32))
    grads[8 : 8 + MERGE, :] = mm_tn(rows_t(d), hat * gain + bias).T
    d_hat = mm_nt(d, w)
    put_hidden_rows(grads, 0, 1, colsum(d_hat * hat))
    put_hidden_rows(grads, 4, 1, colsum(d_hat))
    flatten(grads, 0, CUTS[1], flat)
    at = 0
    for cut, part in ((CUTS[1], flat1), (CUTS[2], flat2), (CUTS[3], seam)):
        at = 3 * cut
        flat[at : at + part.shape[0], :] = part[...]
    at += seam.shape[0]
    if flat.shape[0] > at:
        flat[at:, :] = jnp.zeros((flat.shape[0] - at, WIDE), F32)
    scatter(sizes, flat, 0, keep, send)


def radices(count):
    steps = [2]
    left = count // 2
    while left > 1:
        steps.append(4 if left >= 4 else 2)
        left //= steps[-1]
    return steps


def block_rows(rows, count):
    return -(-rows // (8 * count)) * 8


def own_number(sizes):
    return lax.axis_index("slab") * sizes[1] + lax.axis_index("mp")


def place_in_half(distance, count):
    place = 0
    shift = 1
    for radix in radices(count)[1:]:
        digit = jnp.bitwise_and(lax.shift_right_logical(distance, shift), radix - 1)
        place = place * radix + digit
        shift += radix.bit_length() - 1
    return place


def scatter(sizes, source, first, keep, send):
    count = sizes[0] * sizes[1]
    rows = keep.shape[0] * 2 // count
    me = own_number(sizes)
    odd = jnp.bitwise_and(me, 1)

    def per_pair(t, carry):
        for block, out in ((2 * t + odd, keep), (2 * t + 1 - odd, send)):
            place = place_in_half(jnp.bitwise_xor(block, me), count)
            at = pl.multiple_of(first + block * rows, 8)
            to = pl.multiple_of(place * rows, 8)
            out[pl.ds(to, rows), :] = source[pl.ds(at, rows), :]
        return carry

    lax.fori_loop(0, count // 2, per_pair, 0)


def traded(value, distance, count):
    pairs = [(i, i ^ distance) for i in range(count)]
    return lax.ppermute(value, ("slab", "mp"), pairs)


def later(got, after):
    return got if after is None else list(lax.optimization_barrier((*got, after)))[:-1]


def summing(keep, send, count):
    steps = radices(count)
    got = [keep, traded(send, 1, count)]
    shift = 1
    after = yield None
    for radix in steps[1:]:
        got = later(got, after)
        total = sum(got[1:], got[0])
        rows = total.shape[0] // radix
        parts = [total[k * rows : (k + 1) * rows] for k in range(radix)]
        got = parts[:1] + [traded(parts[k], k << shift, count) for k in range(1, radix)]
        shift += radix.bit_length() - 1
        after = yield parts[0]
    got = later(got, after)
    own = sum(got[1:], got[0])
    for radix in reversed(steps[1:]):
        shift -= radix.bit_length() - 1
        got = [own] + [traded(own, k << shift, count) for k in range(1, radix)]
        after = yield own
        own = jnp.concatenate(later(got, after), 0)
        yield own
    yield own, traded(own, 1, count)


def finished(chain, after=None):
    last = next(chain) if after is None else chain.send(after)
    while not isinstance(last, tuple):
        last = next(chain)
    return last


def exchanged_sum(value, count):
    shift = 0
    for radix in radices(count):
        got = [value] + [traded(value, k << shift, count) for k in range(1, radix)]
        while len(got) > 1:
            got = [got[i] + got[i + 1] for i in range(0, len(got), 2)]
        value = got[0]
        shift += radix.bit_length() - 1
    return value


PIECE = 294912


def place_blocks(sizes, own, other, out, size):
    count = sizes[0] * sizes[1]
    me = own_number(sizes)
    rows = own.shape[0] * 2 // count

    def per_block(block, carry):
        distance = jnp.bitwise_xor(block, me)
        at = pl.ds(pl.multiple_of(place_in_half(distance, count) * rows, 8), rows)
        near = jnp.bitwise_and(distance, 1) == 0
        to = pl.ds(pl.multiple_of(block * rows, 8), rows)
        out[to, :] = jnp.where(near, own[at, :], other[at, :])
        return carry

    lax.fori_loop(0, size // rows, per_block, 0)


def squares(*refs):
    total = jnp.zeros((8, WIDE), F32)
    for ref in refs:
        x = ref[...]
        total = total + jnp.sum((x * x).reshape(-1, 8, WIDE), 0)
    return total


def place_early_kernel(sizes, own, other, out, square):
    place_blocks(sizes, own, other, out, EARLY_ROWS)
    square[...] = squares(own, other)


def adamw_kernel(
    sizes,
    late, late_other, early, square, tail, sums, params, first, second,
    new_params, new_first, new_second, loss, valid, norm_out,
    grad, scale_ref,
):
    step = pl.program_id(0)

    @pl.when(step == 0)
    def gather():
        norm = jnp.sqrt(jnp.sum(squares(late, late_other) + square[...]))
        loss[0] = jnp.sum(tail[2:3, 0:1])
        valid[0] = jnp.sum(sums[2:3, 0:1])
        norm_out[0] = norm
        scale_ref[0] = jnp.minimum(1.0, clip_norm / (norm + 1e-06))
        place_blocks(sizes, late, late_other, grad, LATE_ROWS)
        grad[LATE_ROWS:, :] = early[...]

    def update(base, low, size):
        rows = -(-size // 1024) * 8
        at = pl.ds(pl.multiple_of(base // WIDE + low // WIDE, 8), rows)
        g = grad[at, :].reshape(rows * WIDE)[:size] * scale_ref[0]
        here = pl.ds(pl.multiple_of(base + low, 1024), size)
        one = beta_one * first[here] + (1.0 - beta_one) * g
        two = beta_two * second[here] + (1.0 - beta_two) * g * g
        there = pl.ds(low, size)
        new_first[there] = one
        new_second[there] = two
        two = two * (1.0 / (1.0 - beta_two**STEP))
        low_by = two * lax.rsqrt(jnp.maximum(two, 1e-37)) + adam_eps
        inverse = pl.reciprocal(low_by, approx=True)
        inverse = inverse * (2.0 - low_by * inverse)
        new_params[there] = params[here] * (1.0 - learn_rate * decay_rate) - (
            one * (learn_rate / (1.0 - beta_one**STEP))
        ) * inverse

    whole = NPARAM // PIECE

    @pl.when(step < whole)
    def full():
        def part(i, carry):
            low = pl.multiple_of(i * 16384, 16384)
            update(step * PIECE, low, 16384)
            return carry

        lax.fori_loop(0, PIECE // 16384, part, 0)

    @pl.when(step == whole)
    def last():
        rest = NPARAM - whole * PIECE
        main = rest // 1024 * 1024
        for low in range(0, main, 16384):
            update(whole * PIECE, low, min(16384, main - low))
        update(whole * PIECE, main, rest - main)


def adamw(sizes, parts, arrays):
    pieces = -(-NPARAM // PIECE)
    piece = pl.BlockSpec((PIECE,), lambda i: (i,))
    vmem = pl.BlockSpec(memory_space=pltpu.VMEM)
    smem = pl.BlockSpec(memory_space=pltpu.SMEM)
    return pl.pallas_call(
        functools.partial(adamw_kernel, sizes),
        grid=(pieces,),
        out_shape=[arr(NPARAM)] * 3 + [arr(1)] * 3,
        in_specs=[vmem] * (len(parts) + len(arrays)),
        out_specs=[piece] * 3 + [smem] * 3,
        scratch_shapes=[pltpu.VMEM((LATE_ROWS + EARLY_ROWS, WIDE), F32), pltpu.SMEM((1,), F32)],
        compiler_params=pltpu.CompilerParams(vmem_limit_bytes=16 * 1024 * 1024),
        cost_estimate=pl.CostEstimate(flops=6 * 10**9, bytes_accessed=0, transcendentals=0),
        name="adamw",
    )(*parts, *arrays)


def arr(*shape):
    return jax.ShapeDtypeStruct(shape, F32)


def call(kernel, outs, scratch, *args, name=None, us=1.0, far=(), mib=16):
    vmem = pl.BlockSpec(memory_space=pltpu.VMEM)
    smem = pl.BlockSpec(memory_space=pltpu.SMEM)
    return pl.pallas_call(
        kernel,
        out_shape=list(outs),
        in_specs=[vmem] * len(args) + [pl.BlockSpec(memory_space=pl.ANY)] * len(far),
        out_specs=[smem if o.shape == (1,) else vmem for o in outs],
        scratch_shapes=list(scratch),
        compiler_params=pltpu.CompilerParams(vmem_limit_bytes=mib * 1024 * 1024),
        cost_estimate=pl.CostEstimate(
            flops=int(us * 1.15e9), bytes_accessed=0, transcendentals=0
        ),
        name=name,
    )(*args, *far)


SQUARE = arr(ROWS, WIDE)
SAVE = arr(ROWS, 3 * WIDE)
FORWARD = [
    pltpu.VMEM((2, ROWS, 2 * WIDE), BF16),
    pltpu.VMEM((2, KEYS, 2 * WIDE), BF16),
    pltpu.VMEM((2 * KEYS, 2 * WIDE), BF16),
]
BACKWARD = [
    pltpu.VMEM((2, ROWS, 2 * WIDE), BF16),
    pltpu.VMEM((2, KEYS, 2 * WIDE), BF16),
    pltpu.VMEM((2, ROWS, 2 * WIDE), BF16),
    pltpu.VMEM((2, KEYS, 2 * WIDE), BF16),
    pltpu.VMEM((2 * KEYS, 2 * WIDE), BF16),
    pltpu.VMEM((ROWS, WIDE), F32),
    pltpu.VMEM((2, WIDE, KEYS), F32),
    pltpu.VMEM((2, KEYS, 2 * KEYS), BF16),
    pltpu.VMEM((2, KEYS, 2 * KEYS), BF16),
    pltpu.VMEM((2, WIDE, KEYS), BF16),
    pltpu.VMEM((2, WIDE, KEYS), BF16),
    pltpu.VMEM((ROWS, WIDE), F32),
    pltpu.VMEM((ROWS, 2 * KEYS), F32),
    pltpu.VMEM((ROWS, 2 * KEYS), F32),
    pltpu.VMEM((2 * KEYS, 2 * WIDE), BF16),
    pltpu.VMEM((2 * KEYS, 2 * WIDE), BF16),
]
PARTS = [arr(ROWS_A, WIDE), arr(ROWS_B, WIDE), arr(ROWS_C, WIDE)]


def passed(parts, steps, sizes):
    slabs, rows = sizes
    moved = []
    for part, (ds, dm) in zip(parts, ((1, 0), (0, 1), (1, 1))):
        pairs = []
        for s in range(slabs):
            for m in range(rows):
                target = ((s + steps * ds) % slabs) * rows + (m + steps * dm) % rows
                pairs.append((s * rows + m, target))
        moved.append(lax.ppermute(part, ("slab", "mp"), pairs))
    return moved


SIDES = [arr(2 * WIN, 8, WIDE)] * 4


def paired(axis, size):
    near = [(i, i ^ 1) for i in range(size)]
    far = [(i, (i + (1 if i % 2 else -1)) % size) for i in range(size)]
    return (
        lambda value: lax.ppermute(value, axis, near),
        lambda value: lax.ppermute(value, axis, far),
    )


def column_kernel(sizes, near_d, far_d, near_h, far_h, near_out, far_out):
    slab = lax.axis_index("slab")
    odd_d = jnp.bitwise_and(slab, 1) == 1
    odd_h = jnp.bitwise_and(lax.axis_index("mp"), 1) == 1
    at_low = slab == 0
    at_high = slab == sizes[0] - 1
    near_out[4:18] = near_h[...]
    far_out[4:18] = far_h[...]
    for d in range(2):
        near = near_d[d * WIN : (d + 1) * WIN]
        far = far_d[d * WIN : (d + 1) * WIN]
        before = jnp.where(odd_d, near, jnp.where(at_low, 0.0, far))
        after = jnp.where(odd_d, jnp.where(at_high, 0.0, far), near)
        for x, at in ((before, 2 * d), (after, 18 + 2 * d)):
            low, high = x[0:2], x[WIN - 2 : WIN]
            near_out[at : at + 2] = jnp.where(odd_h, low, high)
            far_out[at : at + 2] = jnp.where(odd_h, high, low)


def beside(sides, sizes):
    near, far = paired("slab", sizes[0])
    near_d, far_d = near(sides[0]), far(sides[1])
    near_h, far_h = call(
        functools.partial(column_kernel, sizes), [arr(22, 8, WIDE)] * 2, [],
        near_d, far_d, sides[2], sides[3],
        name="column", us=0.3,
    )
    near, far = paired("mp", sizes[1])
    return near_d, far_d, near(near_h), far(far_h)


REGION = [pltpu.VMEM((ROWS, KEYS), F32)]


def on_device(sizes, feats, labels, valid, params, moment_one, moment_two):
    slabs, rows = sizes
    count = slabs * rows

    def room(spans):
        sizes = [(span_of(groups)[1] + 8) * WIDE for groups in spans]
        return [
            [pltpu.VMEM((size,), F32) for size in sizes],
            pltpu.VMEM((2048, WIDE), F32),
            pltpu.SemaphoreType.DMA((len(spans),)),
        ]

    first_size = FIRST_SPANS[-1][1] * 384
    merge, lay0 = call(
        functools.partial(prep_kernel, FIRST_SPANS),
        [arr(MERGE_ROWS, WIDE), arr(1176, WIDE)],
        room(FIRST_SPANS),
        name="prep_first", us=2.0, far=(params[:first_size],),
    )
    lay1, lay2 = call(
        functools.partial(prep_kernel, LAYER_SPANS),
        [arr(1168, WIDE)] * 2,
        room(LAYER_SPANS),
        name="prep_layers", us=2.0, far=(params,),
    )
    taps_shape = jax.ShapeDtypeStruct((27 * 256, 256), BF16)
    conv0, weights0, bias0 = call(
        prep_conv0_kernel,
        [arr(2596, WIDE), taps_shape, arr(8, WIDE)],
        room(CONV_SPANS[:1]),
        name="prep_conv0", us=1.5, far=(params,),
    )
    conv1, head_w, weights1, vectors = call(
        prep_conv1_kernel,
        [arr(2640, WIDE), arr(WIDE, WIDE), taps_shape, arr(8, WIDE)],
        room(CONV_SPANS[1:]),
        params[NPARAM // WIDE * WIDE :], bias0,
        name="prep_conv1", us=1.5, far=(params,),
    )

    dense, tok0, save0, lse0, mixed0, mid0, hpre0, tok1, ahead, *parts = call(
        first_kernel,
        [arr(ROWS, MERGE), SQUARE, SAVE, SQUARE, SQUARE, SQUARE, arr(ROWS, HID), SQUARE, SQUARE]
        + PARTS,
        FORWARD,
        feats.reshape(PLANE, WIN, MERGE), merge, lay0,
        name="first", us=6.0,
    )
    parts = passed(parts, -1, sizes)
    window, save1, lse1, mixed1, out1, *parts = call(
        functools.partial(shifted_kernel, sizes),
        [SQUARE, SAVE, SQUARE, SQUARE, SQUARE] + PARTS,
        REGION + FORWARD,
        ahead, *parts, lay1,
        name="shifted", us=4.5, far=(weights0,),
    )
    parts = passed(parts, 1, sizes)
    mid1, hpre1, tok2, save2, lse2, mixed2, mid2, hpre2, lines, *sides = call(
        second_kernel,
        [SQUARE, arr(ROWS, HID), SQUARE, SAVE, SQUARE, SQUARE, SQUARE, arr(ROWS, HID)]
        + [arr(PLANE, 8, WIDE)] + SIDES,
        [pltpu.VMEM((ROWS, WIDE), F32)] + FORWARD,
        tok1, out1, *parts, lay1, lay2,
        name="second", us=6.5, far=(weights1,),
    )
    sides = beside(sides, sizes)
    back0, back1 = call(
        weights_back_kernel,
        [taps_shape] * 2,
        [],
        conv0, conv1,
        name="weights_back", us=1.5,
    )
    grown, pre, tok3, sums, *tok_sides = call(
        functools.partial(conv_kernel, sizes),
        [arr(11, 12, 8, WIDE), arr(9, 10, 8, WIDE), arr(PLANE, 8, WIDE), arr(8, WIDE)] + SIDES,
        [
            pltpu.VMEM((9, 10, 8, WIDE), F32),
            pltpu.VMEM((880, 2304), BF16),
            pltpu.VMEM((576, 2304), BF16),
            pltpu.VMEM((PLANE, 8, WIDE), F32),
            pltpu.VMEM((720, WIDE), F32),
        ],
        lines, *sides, labels, valid, weights0, weights1, vectors,
        name="conv", us=8.0, mib=20, far=(back0,),
    )
    tok_sides = beside(tok_sides, sizes)
    side_act, side_grown = call(
        functools.partial(sides_back_kernel, sizes),
        [jax.ShapeDtypeStruct((640, 2304), BF16)] * 2,
        [pltpu.VMEM((10, 10, 8, WIDE), F32)],
        grown, pre,
        name="sides_back", us=2.0,
    )
    sums = exchanged_sum(sums, count)
    voxels = WIN * slabs * WIN * rows * WIN
    tok3, slope, tail, d_head, d_rows = call(
        functools.partial(head_kernel, sizes, voxels),
        [arr(11, 12, 8, WIDE), arr(11, 12, 8, WIDE), arr(8, WIDE), arr(WIDE, WIDE), arr(8, WIDE)],
        [],
        tok3, *tok_sides, sums, vectors, head_w,
        name="head", us=3.5,
    )
    tail = exchanged_sum(tail, count)
    late_rows = block_rows(LATE_ROWS, count) * count
    early_rows = block_rows(EARLY_ROWS, count) * count
    seam_rows = LATE_ROWS - 3 * CUTS[3]
    d_own, keep, send, carry3, seam = call(
        functools.partial(conv_back_kernel, sizes),
        [arr(PLANE, 8, WIDE)] + [arr(early_rows // 2, WIDE)] * 2
        + [arr(24, WIDE), arr(seam_rows, WIDE)],
        [
            pltpu.VMEM((5236, WIDE), F32),
            pltpu.VMEM((11, 12, 8, WIDE), F32),
            pltpu.VMEM((10, 10, 8, WIDE), F32),
            pltpu.VMEM((880, 2304), BF16),
            pltpu.VMEM((576, 2304), BF16),
            pltpu.VMEM((seam_rows + early_rows, WIDE), F32),
            pltpu.VMEM((720, WIDE), F32),
        ],
        tok3, slope, tail, pre, side_act, side_grown, back0, back1, d_rows, d_head,
        name="conv_back", us=14.0, mib=28,
    )
    early = summing(keep, send, count)
    next(early)
    d_mid2, grads2 = call(
        back_mlp_kernel,
        [SQUARE, arr(1168, WIDE)],
        [pltpu.VMEM((ROWS, WIDE), F32)],
        d_own, lay2, mid2, hpre2,
        name="back_mlp", us=3.0,
    )
    step = early.send(d_mid2)
    d_mid, grads1, flat2, carry2, *parts = call(
        back_two_kernel,
        [SQUARE, arr(1168, WIDE), arr(3 * (CUTS[3] - CUTS[2]), WIDE), arr(32, WIDE)] + PARTS,
        [pltpu.VMEM((1184, WIDE), F32)] + BACKWARD,
        d_mid2, grads2, carry3, lay1, lay2, tok2, save2, lse2, mixed2, mid1, hpre1,
        name="back_two", us=9.0,
    )
    parts = passed(parts, -1, sizes)
    step = early.send(d_mid)
    d_window, flat1, carry1, *parts = call(
        functools.partial(back_shifted_kernel, sizes),
        [SQUARE, arr(3 * (CUTS[2] - CUTS[1]), WIDE), arr(16, WIDE)] + PARTS,
        REGION + [pltpu.VMEM((1200, WIDE), F32), pltpu.VMEM((ROWS, WIDE), F32)] + BACKWARD,
        d_mid, *parts, lay1, window, save1, lse1, mixed1, grads1, carry2,
        name="back_shifted", us=10.5, far=(step,),
    )
    early.send(d_window)
    parts = passed(parts, 1, sizes)
    next(early)
    step = next(early)
    late = call(
        functools.partial(back_first_kernel, sizes),
        [arr(late_rows // 2, WIDE)] * 2,
        [
            pltpu.VMEM((late_rows, WIDE), F32),
            pltpu.VMEM((1572, WIDE), F32),
            pltpu.VMEM((ROWS, WIDE), F32),
        ]
        + BACKWARD,
        d_mid, d_window, *parts, tok1, lay0, lay1, merge, dense, tok0, save0, lse0, mixed0, mid0,
        hpre0, carry1, flat1, flat2, seam,
        name="back_first", us=13.5, far=(step,),
    )
    step = early.send(late[0])
    keep, send = later(list(late), step)
    late_sum = finished(summing(keep, send, count))
    early = finished(early)
    early = call(
        functools.partial(place_early_kernel, sizes),
        [arr(EARLY_ROWS, WIDE), arr(8, WIDE)],
        [],
        *early,
        name="place_early", us=0.6,
    )
    new_params, new_first, new_second, loss, valid_count, norm = adamw(
        sizes, (*late_sum, *early, tail, sums), (params, moment_one, moment_two)
    )
    return (
        loss.reshape(()), valid_count.reshape(()), norm.reshape(()),
        new_params, new_first, new_second,
    )


def solution(mesh):
    placed = (
        P("slab", "mp", None, None),
        P("slab", "mp", None),
        P("slab", "mp", None),
        P(),
        P(),
        P(),
    )
    sizes = (mesh.shape["slab"], mesh.shape["mp"])
    return jax.shard_map(
        functools.partial(on_device, sizes),
        mesh=mesh,
        in_specs=placed,
        out_specs=(P(), P(), P(), P(), P(), P()),
        check_vma=False,
    )
```
